32 devices in a mesh: fsdp: 8 (over z, y), dp: 4 (over x, core).
Axes of the slice: x: 2, y: 2, z: 4, core: 2. Of those that a mesh axis runs over, the one named last changes fastest.
Arguments:
- inputs: bfloat16 [2, 12288, 1024], P(None, ('fsdp', 'dp')), may hold values from -6 to 6
- cotangent: bfloat16 [2, 12288, 1024], P(None, ('fsdp', 'dp')), may hold values from -6 to 6
- lengths: int32 [2, 32], P(None, ('fsdp', 'dp')), may hold values from 96 to 384, as said below
- attention_weights: float32 [4, 1024, 1024], P(None, 'fsdp')
- attention_momentum: float32 [4, 1024, 1024], P(None, 'fsdp')
- attention_average: float32 [4, 1024, 1024], P(None, 'fsdp'), may hold values from -0.1875 to 0.1875
- ffn_inputs: float32 [2, 1024, 2816], P(None, 'fsdp'), may hold values from -0.1875 to 0.1875
- ffn_inputs_momentum: float32 [2, 1024, 2816], P(None, 'fsdp')
- ffn_inputs_average: float32 [2, 1024, 2816], P(None, 'fsdp'), may hold values from -0.1875 to 0.1875
- ffn_output: float32 [2816, 1024], P('fsdp'), may hold values from -0.109375 to 0.109375
- ffn_output_momentum: float32 [2816, 1024], P('fsdp')
- ffn_output_average: float32 [2816, 1024], P('fsdp'), may hold values from -0.109375 to 0.109375
- gains: float32 [3, 1024], P(None, 'fsdp'), may hold values from 0.5 to 1.5
- gains_momentum: float32 [3, 1024], P(None, 'fsdp')
- gains_average: float32 [3, 1024], P(None, 'fsdp'), may hold values from 0.5 to 1.5
Outputs:
- output: bfloat16 [2, 12288, 1024], P(None, ('fsdp', 'dp'))
- input_grad: float32 [2, 12288, 1024], P(None, ('fsdp', 'dp'))
- attention_momentum_new: float32 [4, 1024, 1024], P(None, 'fsdp')
- attention_average_new: float32 [4, 1024, 1024], P(None, 'fsdp')
- attention_weights_new: float32 [4, 1024, 1024], P(None, 'fsdp')
- ffn_inputs_momentum_new: float32 [2, 1024, 2816], P(None, 'fsdp')
- ffn_inputs_average_new: float32 [2, 1024, 2816], P(None, 'fsdp')
- ffn_inputs_new: float32 [2, 1024, 2816], P(None, 'fsdp')
- ffn_output_momentum_new: float32 [2816, 1024], P('fsdp')
- ffn_output_average_new: float32 [2816, 1024], P('fsdp')
- ffn_output_new: float32 [2816, 1024], P('fsdp')
- gains_momentum_new: float32 [3, 1024], P(None, 'fsdp')
- gains_average_new: float32 [3, 1024], P(None, 'fsdp')
- gains_new: float32 [3, 1024], P(None, 'fsdp')
The draws below stay inside these ranges and needn't reach their ends.
Inputs may be any that keep to these rules, and one draw needn't show every extreme that they name: `lengths`: in every micro-batch one sequence has exactly 384 valid positions.
All inputs are finite; a program needn't handle non-finite values.
Results may differ from the reference program's by a relative error of at most 0.013.
Values may be sent and summed in bfloat16 or wider, within the bound.
No kernel may reach another device: no remote copies, remote signals or barrier semaphores. Data moves between devices by JAX's collectives and lax.ppermute only.
A program may use at most 320 MiB of HBM per device.

```python
import math
import jax
import jax.numpy as jnp
from jax import lax

D = 1024
FF = 2816
HEAD_DIM = 128
SPAN = 64
MICRO = 2
SLOT = 384
SEQS = 32
ROWS = 12288
MIN_LEN = 96


def gradient_size():
    return math.sqrt(0.6 * MICRO * ROWS)


def draw_lengths(key, part):
    key = jax.random.fold_in(key, 5)
    first_key, second_key = jax.random.split(key)
    drawn = jax.random.randint(first_key, (MICRO, SEQS), MIN_LEN, SLOT + 1, dtype=jnp.int32)
    longest = jax.random.randint(second_key, (MICRO,), 0, SEQS, dtype=jnp.int32)
    columns = jnp.arange(SEQS, dtype=jnp.int32)
    return jnp.where(columns[None, :] == longest[:, None], SLOT, drawn).astype(jnp.int32)


def draw_attention_weights(key, part):
    key = jax.random.fold_in(key, 7)
    samples = jax.random.normal(key, (4, D, D), jnp.float32)
    factors = jnp.array([1.0, 3.0, 1.0, 1.0], jnp.float32)[:, None, None]
    return samples * factors / math.sqrt(D)


def draw_attention_momentum(key, part):
    key = jax.random.fold_in(key, 11)
    samples = jax.random.normal(key, (4, D, D), jnp.float32)
    factors = jnp.array([1.0, 0.1, 0.3, 1.2], jnp.float32)[:, None, None]
    return samples * factors * gradient_size()


def draw_ffn_inputs_momentum(key, part):
    key = jax.random.fold_in(key, 13)
    samples = jax.random.normal(key, (2, D, FF), jnp.float32)
    return samples * 0.36 * gradient_size()


def draw_ffn_output_momentum(key, part):
    key = jax.random.fold_in(key, 17)
    samples = jax.random.normal(key, (FF, D), jnp.float32)
    return samples * 0.6 * gradient_size()


def draw_gains_momentum(key, part):
    key = jax.random.fold_in(key, 19)
    samples = jax.random.normal(key, (3, D), jnp.float32)
    return samples * gradient_size()


def strengthened(values, stream_key, source, target, shards_of, factor):
    def block_of(axis_at):
        return (jnp.arange(values.shape[axis_at]) // (values.shape[axis_at] // shards_of)).reshape((-1,) + (1,) * (values.ndim - 1 - axis_at))

    near = jax.random.permutation(stream_key, shards_of)[block_of(target)]
    far = (block_of(target) + shards_of // 2) % shards_of
    return jnp.where((block_of(source) == near) | (block_of(source) == far), factor * values, values)


def steps_of(rng, dims, shards, least, top_value):
    loudness = 1.0
    for axis_at, shards_of in shards:
        draws = jax.random.uniform(jax.random.fold_in(jax.random.fold_in(rng, 6), axis_at), (shards_of,), jnp.float32, least / len(shards), top_value / len(shards))
        loudness = loudness * jnp.repeat(jnp.exp(draws), dims[axis_at] // shards_of).reshape((-1,) + (1,) * (len(dims) - 1 - axis_at))
    return loudness


def bell_draw(own_key, extent, scale, limit, cuts=(), held_as=jnp.bfloat16):
    values = jax.random.normal(own_key, extent, jnp.float32) * scale
    if len(cuts) > 0:
        values = steps_of(own_key, extent, cuts, -0.22, 0.18) * values
    return jnp.clip(values, min=-limit, max=limit).astype(held_as)


def bell_draw_with(key, extent, width, reach, cuts, heavy, kind=jnp.bfloat16):
    values = width * jax.random.normal(key, extent, jnp.float32)
    if cuts:
        values = values * steps_of(key, extent, cuts, -0.22, 0.18)
    return jnp.clip(strengthened(values, jax.random.fold_in(key, 3), *heavy), -reach, reach).astype(kind)


def setup_inputs(seed: int = 0) -> dict:
    arg_keys = jax.random.split(jax.random.key(seed), 16)
    inputs = bell_draw_with(arg_keys[0], (MICRO, ROWS, D), 1.0, 6.0, ((1, 32),), (1, 2, 32, 2.75))
    cotangent = bell_draw(arg_keys[1], (MICRO, ROWS, D), 1.0, 6.0, ((1, 32),))
    lengths = draw_lengths(jax.random.fold_in(arg_keys[15], 71), 0)
    attention_weights = draw_attention_weights(jax.random.fold_in(arg_keys[15], 71), 0)
    attention_momentum = draw_attention_momentum(jax.random.fold_in(arg_keys[15], 71), 0)
    attention_average = bell_draw(arg_keys[5], (4, D, D), D ** -0.5, 0.1875, ((1, 8),), jnp.float32)
    ffn_inputs = bell_draw(arg_keys[6], (2, D, FF), D ** -0.5, 0.1875, ((1, 8),), jnp.float32)
    ffn_inputs_momentum = draw_ffn_inputs_momentum(jax.random.fold_in(arg_keys[15], 71), 0)
    ffn_inputs_average = bell_draw(arg_keys[8], (2, D, FF), D ** -0.5, 0.1875, ((1, 8),), jnp.float32)
    ffn_output = bell_draw(arg_keys[9], (FF, D), FF ** -0.5, 0.109375, ((0, 8),), jnp.float32)
    ffn_output_momentum = draw_ffn_output_momentum(jax.random.fold_in(arg_keys[15], 71), 0)
    ffn_output_average = bell_draw(arg_keys[11], (FF, D), FF ** -0.5, 0.109375, ((0, 8),), jnp.float32)
    gains = jnp.clip(1.0 + 0.1 * jax.random.normal(arg_keys[12], (3, D), jnp.float32), 0.5, 1.5)
    gains_momentum = draw_gains_momentum(jax.random.fold_in(arg_keys[15], 71), 0)
    gains_average = jnp.clip(1.0 + 0.1 * jax.random.normal(arg_keys[14], (3, D), jnp.float32), 0.5, 1.5)
    return dict(inputs=inputs, cotangent=cotangent, lengths=lengths, attention_weights=attention_weights, attention_momentum=attention_momentum, attention_average=attention_average, ffn_inputs=ffn_inputs, ffn_inputs_momentum=ffn_inputs_momentum, ffn_inputs_average=ffn_inputs_average, ffn_output=ffn_output, ffn_output_momentum=ffn_output_momentum, ffn_output_average=ffn_output_average, gains=gains, gains_momentum=gains_momentum, gains_average=gains_average)


lower_bound = 0.9
momentum_decay = 0.9
average_decay = 0.7
weight_decay = 0.0005
matrix_rate = 0.03
gain_rate = 0.1
highest = lax.Precision.HIGHEST

@jax.custom_vjp
def low(v):
    return lax.optimization_barrier(v.astype(jnp.bfloat16)).astype(jnp.float32)

@jax.custom_vjp
def low_back(v):
    return v

def low_keep(v):
    return (low(v), None)

def low_pass(kept, grad):
    return (grad,)

def back_keep(v):
    return (v, None)

def back_low(kept, grad):
    return (low(grad),)
low.defvjp(low_keep, low_pass)
low_back.defvjp(back_keep, back_low)

def matmul(left_side, right_side):
    return jnp.dot(left_side, right_side, precision=highest, preferred_element_type=jnp.float32)

def rms_scale(tensor, epsilon):
    return lax.rsqrt(lax.optimization_barrier(jnp.mean(tensor * tensor, axis=-1, keepdims=True)) + epsilon)

def span_step(carried, pieces):
    queries, keys_in, values, log_gate = pieces
    cumulative = jnp.cumsum(log_gate, axis=1)
    decay_total = cumulative[:, -1, :]
    decayed_q = queries * jnp.exp(cumulative)
    grown_k = keys_in * jnp.exp(-cumulative)
    block_width = queries.shape[1]
    causal = jnp.arange(block_width)[:, None] >= jnp.arange(block_width)[None, :]
    scores = jnp.einsum('hcd,hsd->hcs', decayed_q, grown_k, precision=highest)
    scores = jnp.where(causal[None], scores, 0.0)
    outputs = jnp.einsum('hcs,hse->hce', scores, values, precision=highest)
    outputs = outputs + jnp.einsum('hcd,hde->hce', decayed_q, carried, precision=highest)
    added = jnp.einsum('hsd,hse->hde', grown_k, values, precision=highest)
    new_state = jnp.exp(decay_total)[:, :, None] * (carried + added)
    return (new_state, outputs)

def recurrence(queries, keys_in, values, log_gate):
    length, block_width = queries.shape
    head_count = block_width // HEAD_DIM

    def to_blocks(tensor):
        return tensor.reshape(length // SPAN, SPAN, head_count, HEAD_DIM).transpose(0, 2, 1, 3)
    start_state = jnp.zeros((head_count, HEAD_DIM, HEAD_DIM), jnp.float32)
    final_state, outputs = lax.scan(jax.checkpoint(span_step), start_state, (to_blocks(queries), to_blocks(keys_in), to_blocks(values), to_blocks(log_gate)))
    return outputs.transpose(0, 2, 1, 3).reshape(length, block_width)

def mixer(q_pre, f_pre, values, gain_o):
    queries = jax.nn.silu(q_pre)
    forget = lower_bound + (1.0 - lower_bound) * jax.nn.sigmoid(f_pre)
    keys_in = 1.0 - forget
    mixed_out = recurrence(queries, keys_in, values, jnp.log(forget))
    length, block_width = mixed_out.shape
    per_head = mixed_out.reshape(length, block_width // HEAD_DIM, HEAD_DIM)
    normed = per_head * rms_scale(per_head, 1e-05)
    return normed.reshape(length, block_width) * gain_o

def block(params, inputs_group, mask_group):
    attention, ffn_in, ffn_out, gain_rows = params
    attention = low(attention)
    ffn_in = low(ffn_in)
    ffn_out = low(ffn_out)
    gain_rows = low(gain_rows)
    group_size, length, block_width = inputs_group.shape
    rows_all = inputs_group.reshape(group_size * length, block_width)
    first_low = low(rows_all * rms_scale(rows_all, 1e-06) * gain_rows[0])
    q_pre = low_back(matmul(first_low, attention[0]))
    f_pre = low_back(matmul(first_low, attention[1]))
    v_pre = low_back(matmul(first_low, attention[2]))
    shaped = (group_size, length, block_width)
    mixed_out = jax.vmap(mixer, in_axes=(0, 0, 0, None))(q_pre.reshape(shaped), f_pre.reshape(shaped), v_pre.reshape(shaped), gain_rows[1])
    mixed_low = low(mixed_out.reshape(group_size * length, block_width))
    middle = rows_all + low_back(matmul(mixed_low, attention[3]))
    second_low = low(middle * rms_scale(middle, 1e-06) * gain_rows[2])
    gate_pre = low_back(matmul(second_low, ffn_in[0]))
    up_pre = low_back(matmul(second_low, ffn_in[1]))
    hidden_low = low(jax.nn.silu(gate_pre) * up_pre)
    block_out = middle + low_back(matmul(hidden_low, ffn_out))
    block_out = block_out * mask_group.reshape(group_size * length, 1)
    return block_out.reshape(shaped)

def update(weight, momentum, average, gradient, step_rate):
    new_momentum = momentum_decay * momentum + gradient
    direction = gradient + momentum_decay * new_momentum + weight_decay * weight
    new_weight = weight - step_rate * direction
    new_average = average_decay * average + (1.0 - average_decay) * new_weight
    return (new_momentum, new_average, new_weight)

def reference(inputs, cotangent, lengths, attention_weights, attention_momentum, attention_average, ffn_inputs, ffn_inputs_momentum, ffn_inputs_average, ffn_output, ffn_output_momentum, ffn_output_average, gains, gains_momentum, gains_average):
    params = (attention_weights.astype(jnp.float32), ffn_inputs.astype(jnp.float32), ffn_output.astype(jnp.float32), gains.astype(jnp.float32))
    positions = jnp.arange(SLOT, dtype=jnp.int32)
    valid_mask = (positions[None, None, :] < lengths[:, :, None]).astype(jnp.float32)
    total_seqs = MICRO * SEQS
    group_size = math.gcd(total_seqs, max(1, 4096 // SLOT))
    group_count = total_seqs // group_size
    inputs_f = inputs.astype(jnp.float32).reshape(group_count, group_size, SLOT, D)
    cotangent_f = cotangent.astype(jnp.float32).reshape(group_count, group_size, SLOT, D)
    mask_groups = valid_mask.reshape(group_count, group_size, SLOT)
    zero_grads = jax.tree.map(jnp.zeros_like, params)

    def visit_group(carried, pieces):
        inputs_group, cotangent_group, mask_group = pieces

        def forward_only(param_tree, inputs_tree):
            return block(param_tree, inputs_tree, mask_group)
        result, backward = jax.vjp(forward_only, params, inputs_group)
        grad_params, grad_inputs = backward(cotangent_group)
        return (jax.tree.map(jnp.add, carried, grad_params), (result.astype(jnp.bfloat16), grad_inputs))
    gradients, (outputs, input_grads) = lax.scan(visit_group, zero_grads, (inputs_f, cotangent_f, mask_groups))
    output = outputs.reshape(MICRO, ROWS, D)
    input_grad = input_grads.reshape(MICRO, ROWS, D)
    scale_rows = 1.0 / math.sqrt(MICRO * ROWS)
    attention_new = update(params[0], attention_momentum, attention_average, gradients[0], matrix_rate * scale_rows)
    ffn_in_new = update(params[1], ffn_inputs_momentum, ffn_inputs_average, gradients[1], matrix_rate * scale_rows)
    ffn_out_new = update(params[2], ffn_output_momentum, ffn_output_average, gradients[2], matrix_rate * scale_rows)
    gains_new = update(params[3], gains_momentum, gains_average, gradients[3], gain_rate * scale_rows)
    return (output, input_grad, attention_new[0], attention_new[1], attention_new[2], ffn_in_new[0], ffn_in_new[1], ffn_in_new[2], ffn_out_new[0], ffn_out_new[1], ffn_out_new[2], gains_new[0], gains_new[1], gains_new[2])
```

```python
import functools
import math

import jax
import jax.numpy as jnp
from jax import lax
from jax.experimental import pallas as pl
from jax.experimental.pallas import tpu as pltpu
from jax.sharding import PartitionSpec as P

HEAD_DIM = 128
PAIR = 2 * HEAD_DIM
TILE_F = 256

lower_bound = 0.9
momentum_decay = 0.9
average_decay = 0.7
weight_decay = 0.0005
matrix_rate = 0.03
gain_rate = 0.1
low = jnp.bfloat16
wide = jnp.float32
VMEM_BYTES = 60 * 1024 * 1024


def mm(left, right):
    return jnp.dot(left, right, preferred_element_type=wide)


def mm_nt(left, right):
    return lax.dot_general(left, right, (((1,), (1,)), ((), ())), preferred_element_type=wide)


def mm_tn(left, right):
    return lax.dot_general(left, right, (((0,), (0,)), ((), ())), preferred_element_type=wide)


def sigmoid(u):
    return 1.0 / (1.0 + jnp.exp(-u))


def whole(shape):
    return pl.BlockSpec(shape, lambda *_: (0,) * len(shape), pipeline_mode=pl.Buffered(1))


def split_sum(ones_matrix, tensor):
    high = tensor.astype(low)
    rest = (tensor - high.astype(wide)).astype(low)
    return mm(ones_matrix, high) + mm(ones_matrix, rest)


def triangle(length, lower):
    rows = lax.broadcasted_iota(jnp.int32, (length, length), 0)
    columns = lax.broadcasted_iota(jnp.int32, (length, length), 1)
    kept = rows >= columns if lower else rows <= columns
    return kept.astype(wide).astype(low)


def decay_parts(f_pre, lower_ones):
    share = sigmoid(f_pre)
    gate = lower_bound + (1.0 - lower_bound) * share
    keys_in = (1.0 - lower_bound) * (1.0 - share)
    cumulative = split_sum(lower_ones, jnp.log(gate))
    middle_row = cumulative.shape[0] // 2
    cumulative = cumulative - cumulative[middle_row : middle_row + 1, :]
    return share, gate, keys_in, cumulative


def first_norm(x_ref, gain_row):
    rows = x_ref[...].astype(wide)
    scale = lax.rsqrt(jnp.mean(rows * rows, axis=-1, keepdims=True) + 1e-06)
    return rows * scale, scale


def mixer_forward_kernel(slot, x_ref, w_ref, g_ref, on_ref, q_ref, f_ref, v_ref, o_ref, h_s):
    @pl.when(pl.program_id(0) == 0)
    def _():
        normed, _ = first_norm(x_ref, None)
        h_s[...] = (normed * g_ref[0:1, :]).astype(low)

    column = pl.multiple_of(pl.program_id(0) * PAIR, PAIR)
    gain_o = g_ref[1:2, pl.ds(column, PAIR)]
    pre = mm(h_s[...], w_ref[...])
    q_ref[...] = pre[:, :PAIR]
    f_ref[...] = pre[:, PAIR : 2 * PAIR]
    v_ref[...] = pre[:, 2 * PAIR :].astype(low)
    lower_ones = triangle(slot, True)
    block_rows = lax.broadcasted_iota(jnp.int32, (HEAD_DIM, HEAD_DIM), 0)
    block_columns = lax.broadcasted_iota(jnp.int32, (HEAD_DIM, HEAD_DIM), 1)
    causal = block_rows >= block_columns
    for sequence in range(x_ref.shape[0] // slot):
        rows = slice(sequence * slot, (sequence + 1) * slot)
        q_pre = q_ref[rows, :]
        _, _, keys_in, cumulative = decay_parts(f_ref[rows, :], lower_ones)
        grown = jnp.exp(-cumulative)
        decayed_q = (q_pre * sigmoid(q_pre) * jnp.exp(cumulative)).astype(low)
        grown_k = (keys_in * grown).astype(low)
        values = v_ref[rows, :]
        for head in range(2):
            lanes = slice(head * HEAD_DIM, (head + 1) * HEAD_DIM)
            for block in range(slot // HEAD_DIM):
                start, end = block * HEAD_DIM, (block + 1) * HEAD_DIM
                q_block = decayed_q[start:end, lanes]
                diagonal = mm_nt(q_block, grown_k[start:end, lanes])
                diagonal = jnp.where(causal, diagonal, 0.0).astype(low)
                out = mm(diagonal, values[start:end, lanes])
                if block > 0:
                    scores = mm_nt(q_block, grown_k[:start, lanes]).astype(low)
                    out = out + mm(scores, values[:start, lanes])
                scale = lax.rsqrt(jnp.mean(out * out, axis=-1, keepdims=True) + 1e-05)
                target = slice(sequence * slot + start, sequence * slot + end)
                o_ref[target, lanes] = out
                on_ref[target, lanes] = (out * scale * gain_o[:, lanes]).astype(low)


def mixer_forward(rows, weights, gains8, slot):
    count, width = rows.shape
    pairs = width // PAIR
    by_pair = pl.BlockSpec((count, PAIR), lambda j: (0, j))
    shape = lambda kind: jax.ShapeDtypeStruct((count, width), kind)
    return pl.pallas_call(
        functools.partial(mixer_forward_kernel, slot),
        grid=(pairs,),
        in_specs=[
            whole(rows.shape),
            pl.BlockSpec((width, 3 * PAIR), lambda j: (0, j)),
            whole(gains8.shape),
        ],
        out_specs=[by_pair] * 5,
        out_shape=[shape(low), shape(wide), shape(wide), shape(low), shape(wide)],
        scratch_shapes=[pltpu.VMEM((count, width), low)],
        compiler_params=pltpu.CompilerParams(vmem_limit_bytes=VMEM_BYTES),
        cost_estimate=pl.CostEstimate(
            flops=2 * count * width * 3 * width + 20 * count * slot * width,
            bytes_accessed=count * width * 18 + width * width * 6,
            transcendentals=count * width * 6,
        ),
        name="mixer_forward",
    )(rows, weights, gains8)


def ffn_kernel(
    tiles,
    x_ref,
    on_ref,
    e_ref,
    m_ref,
    g_ref,
    wo_ref,
    wg_ref,
    wu_ref,
    wd_ref,
    out_ref,
    dx1_ref,
    don_ref,
    go_ref,
    g2_ref,
    gg_ref,
    gu_ref,
    gd_ref,
    x1_s,
    acc_s,
    dh_s,
    h_s,
    ht_s,
):
    step = pl.program_id(0)

    @pl.when(step == 0)
    def _():
        x1 = x_ref[...].astype(wide) + mm(on_ref[...], wo_ref[...])
        scale = lax.rsqrt(jnp.mean(x1 * x1, axis=-1, keepdims=True) + 1e-06)
        normed = x1 * scale * g_ref[2:3, :]
        x1_s[...] = x1
        acc_s[...] = x1
        dh_s[...] = jnp.zeros_like(dh_s)
        h_s[...] = normed.astype(low)
        ht_s[...] = normed.T.astype(low)

    a = mm(h_s[...], wg_ref[...])
    b = mm(h_s[...], wu_ref[...])
    share = sigmoid(a)
    swish = a * share
    mid = (swish * b).astype(low)
    acc_s[...] += mm(mid, wd_ref[...])
    d_mid = mm_nt(e_ref[...], wd_ref[...])
    gd_ref[...] = mm_tn(mid, e_ref[...]).astype(low)
    d_a = (d_mid * b * share * (1.0 + a * (1.0 - share))).astype(low)
    d_b = (d_mid * swish).astype(low)
    gg_ref[...] = mm(ht_s[...], d_a).astype(low)
    gu_ref[...] = mm(ht_s[...], d_b).astype(low)
    dh_s[...] += mm_nt(d_a, wg_ref[...]) + mm_nt(d_b, wu_ref[...])

    @pl.when(step == tiles - 1)
    def _():
        mask = m_ref[...]
        out_ref[...] = (acc_s[...] * mask).astype(low)
        x1 = x1_s[...]
        scale = lax.rsqrt(jnp.mean(x1 * x1, axis=-1, keepdims=True) + 1e-06)
        normed = x1 * scale
        d_h2 = dh_s[...]
        scaled = d_h2 * g_ref[2:3, :]
        g2_ref[...] = jnp.sum(d_h2 * normed, axis=0, keepdims=True)
        d_x1 = e_ref[...].astype(wide) + scale * (
            scaled - normed * jnp.mean(scaled * normed, axis=-1, keepdims=True)
        )
        dx1_ref[...] = d_x1
        d_1 = d_x1.astype(low)
        don_ref[...] = mm_nt(d_1, wo_ref[...])
        go_ref[...] = mm_tn(on_ref[...], d_1).astype(low)


def ffn(rows, mixed, errors, mask, gains8, w_o, w_gu, w_d):
    count, width = rows.shape
    hidden = w_d.shape[0]
    tiles = hidden // TILE_F
    full = whole((count, width))
    in_tile = pl.BlockSpec((width, TILE_F), lambda j: (0, j))
    in_tile_up = pl.BlockSpec((width, TILE_F), lambda j: (0, j + tiles))
    out_tile = pl.BlockSpec((TILE_F, width), lambda j: (j, 0))
    struct = jax.ShapeDtypeStruct
    return pl.pallas_call(
        functools.partial(ffn_kernel, tiles),
        grid=(tiles,),
        in_specs=[
            full,
            full,
            full,
            whole((count, 1)),
            whole(gains8.shape),
            whole((width, width)),
            in_tile,
            in_tile_up,
            out_tile,
        ],
        out_specs=[
            full,
            full,
            full,
            whole((width, width)),
            whole((1, width)),
            in_tile,
            in_tile,
            out_tile,
        ],
        out_shape=[
            struct((count, width), low),
            struct((count, width), wide),
            struct((count, width), wide),
            struct((width, width), low),
            struct((1, width), wide),
            struct((width, hidden), low),
            struct((width, hidden), low),
            struct((hidden, width), low),
        ],
        scratch_shapes=[
            pltpu.VMEM((count, width), wide),
            pltpu.VMEM((count, width), wide),
            pltpu.VMEM((count, width), wide),
            pltpu.VMEM((count, width), low),
            pltpu.VMEM((width, count), low),
        ],
        compiler_params=pltpu.CompilerParams(vmem_limit_bytes=VMEM_BYTES),
        cost_estimate=pl.CostEstimate(
            flops=2 * count * width * (8 * hidden + 3 * width),
            bytes_accessed=count * width * 20 + width * hidden * 12 + width * width * 4,
            transcendentals=count * hidden,
        ),
        name="ffn",
    )(rows, mixed, errors, mask, gains8, w_o, w_gu, w_gu, w_d)


def mixer_backward_kernel(
    slot,
    pairs,
    x_ref,
    w_ref,
    g_ref,
    q_ref,
    f_ref,
    v_ref,
    o_ref,
    don_ref,
    dx1_ref,
    grad_ref,
    ggo_ref,
    g1_ref,
    dx_ref,
    ht_s,
    dh_s,
    pre_s,
):
    step = pl.program_id(0)

    @pl.when(step == 0)
    def _():
        normed, _ = first_norm(x_ref, None)
        ht_s[...] = (normed * g_ref[0:1, :]).T.astype(low)
        dh_s[...] = jnp.zeros_like(dh_s)

    column = pl.multiple_of(step * PAIR, PAIR)
    gain_o = g_ref[1:2, pl.ds(column, PAIR)]
    lower_ones = triangle(slot, True)
    upper_ones = triangle(slot, False)
    block_rows = lax.broadcasted_iota(jnp.int32, (HEAD_DIM, HEAD_DIM), 0)
    block_columns = lax.broadcasted_iota(jnp.int32, (HEAD_DIM, HEAD_DIM), 1)
    causal = block_rows >= block_columns
    causal_t = block_rows <= block_columns
    blocks = slot // HEAD_DIM
    ggo_total = jnp.zeros((1, PAIR), wide)
    for sequence in range(x_ref.shape[0] // slot):
        rows = slice(sequence * slot, (sequence + 1) * slot)
        d_on = don_ref[rows, :]
        out = o_ref[rows, :]
        d_out_parts = []
        ggo_parts = []
        for head in range(2):
            lanes = slice(head * HEAD_DIM, (head + 1) * HEAD_DIM)
            out_h, d_on_h = out[:, lanes], d_on[:, lanes]
            scale = lax.rsqrt(jnp.mean(out_h * out_h, axis=-1, keepdims=True) + 1e-05)
            normed = out_h * scale
            ggo_parts.append(jnp.sum(d_on_h * normed, axis=0, keepdims=True))
            scaled = d_on_h * gain_o[:, lanes]
            inner = jnp.mean(scaled * normed, axis=-1, keepdims=True)
            d_out_parts.append((scale * (scaled - normed * inner)).astype(low))
        ggo_total = ggo_total + jnp.concatenate(ggo_parts, axis=1)

        q_pre = q_ref[rows, :]
        share, gate, keys_in, cumulative = decay_parts(f_ref[rows, :], lower_ones)
        grown = jnp.exp(-cumulative)
        shrunk = jnp.exp(cumulative)
        q_share = sigmoid(q_pre)
        decayed_q = (q_pre * q_share * shrunk).astype(low)
        grown_k = (keys_in * grown).astype(low)
        values = v_ref[rows, :]
        dq_parts, dk_parts, dv_parts = [], [], []
        for head in range(2):
            lanes = slice(head * HEAD_DIM, (head + 1) * HEAD_DIM)
            q_h, k_h, v_h = decayed_q[:, lanes], grown_k[:, lanes], values[:, lanes]
            d_out = d_out_parts[head]
            dq_blocks, dk_blocks, dv_blocks = [], [], []
            for block in range(blocks):
                start, end = block * HEAD_DIM, (block + 1) * HEAD_DIM
                here = slice(start, end)
                d_scores = mm_nt(d_out[here], v_h[here])
                d_scores = jnp.where(causal, d_scores, 0.0).astype(low)
                d_q = mm(d_scores, k_h[here])
                if block > 0:
                    before = slice(0, start)
                    d_scores = mm_nt(d_out[here], v_h[before]).astype(low)
                    d_q = d_q + mm(d_scores, k_h[before])
                dq_blocks.append(d_q)
                scores = jnp.where(causal_t, mm_nt(k_h[here], q_h[here]), 0.0).astype(low)
                d_scores = jnp.where(causal_t, mm_nt(v_h[here], d_out[here]), 0.0).astype(low)
                d_v = mm(scores, d_out[here])
                d_k = mm(d_scores, q_h[here])
                if block < blocks - 1:
                    after = slice(end, slot)
                    scores = mm_nt(k_h[here], q_h[after]).astype(low)
                    d_scores = mm_nt(v_h[here], d_out[after]).astype(low)
                    d_v = d_v + mm(scores, d_out[after])
                    d_k = d_k + mm(d_scores, q_h[after])
                dk_blocks.append(d_k)
                dv_blocks.append(d_v)
            dq_parts.append(jnp.concatenate(dq_blocks, axis=0))
            dk_parts.append(jnp.concatenate(dk_blocks, axis=0))
            dv_parts.append(jnp.concatenate(dv_blocks, axis=0))
        d_decayed = jnp.concatenate(dq_parts, axis=1)
        d_grown = jnp.concatenate(dk_parts, axis=1)
        d_value = jnp.concatenate(dv_parts, axis=1)
        d_cumulative = decayed_q.astype(wide) * d_decayed - grown_k.astype(wide) * d_grown
        d_log = split_sum(upper_ones, d_cumulative)
        d_query = d_decayed * shrunk
        d_key = d_grown * grown
        d_q_pre = d_query * q_share * (1.0 + q_pre * (1.0 - q_share))
        d_f_pre = (1.0 - lower_bound) * (d_log / gate - d_key) * share * (1.0 - share)
        pre_s[rows, :PAIR] = d_q_pre.astype(low)
        pre_s[rows, PAIR : 2 * PAIR] = d_f_pre.astype(low)
        pre_s[rows, 2 * PAIR :] = d_value.astype(low)

    ggo_ref[...] = ggo_total
    grad_ref[...] = mm(ht_s[...], pre_s[...]).astype(low)
    dh_s[...] += mm_nt(pre_s[...], w_ref[...])

    @pl.when(step == pairs - 1)
    def _():
        normed, scale = first_norm(x_ref, None)
        d_h1 = dh_s[...]
        scaled = d_h1 * g_ref[0:1, :]
        g1_ref[...] = jnp.sum(d_h1 * normed, axis=0, keepdims=True)
        dx_ref[...] = dx1_ref[...] + scale * (
            scaled - normed * jnp.mean(scaled * normed, axis=-1, keepdims=True)
        )


def mixer_backward(rows, weights, gains8, kept, d_mixed, d_x1, slot):
    count, width = rows.shape
    pairs = width // PAIR
    full = whole((count, width))
    by_pair = pl.BlockSpec((count, PAIR), lambda j: (0, j))
    weight_tile = pl.BlockSpec((width, 3 * PAIR), lambda j: (0, j))
    struct = jax.ShapeDtypeStruct
    return pl.pallas_call(
        functools.partial(mixer_backward_kernel, slot, pairs),
        grid=(pairs,),
        in_specs=[full, weight_tile, whole(gains8.shape)] + [by_pair] * 5 + [full],
        out_specs=[
            weight_tile,
            pl.BlockSpec((1, PAIR), lambda j: (0, j)),
            whole((1, width)),
            full,
        ],
        out_shape=[
            struct((width, 3 * width), low),
            struct((1, width), wide),
            struct((1, width), wide),
            struct((count, width), wide),
        ],
        scratch_shapes=[
            pltpu.VMEM((width, count), low),
            pltpu.VMEM((count, width), wide),
            pltpu.VMEM((count, 3 * PAIR), low),
        ],
        compiler_params=pltpu.CompilerParams(vmem_limit_bytes=VMEM_BYTES),
        cost_estimate=pl.CostEstimate(
            flops=4 * count * width * 3 * width + 40 * count * slot * width,
            bytes_accessed=count * width * 26 + width * width * 12,
            transcendentals=count * width * 8,
        ),
        name="mixer_backward",
    )(rows, weights, gains8, *kept, d_mixed, d_x1)


def update(weight, momentum, average, gradient, step_rate):
    new_momentum = momentum_decay * momentum + gradient
    direction = gradient + momentum_decay * new_momentum + weight_decay * weight
    new_weight = weight - step_rate * direction
    new_average = average_decay * average + (1.0 - average_decay) * new_weight
    return (new_momentum, new_average, new_weight)


def gather_rows(shard):
    replicas = lax.axis_size("dp")
    part_rows = shard.shape[0] // replicas
    part = lax.dynamic_slice_in_dim(shard, lax.axis_index("dp") * part_rows, part_rows, 0)
    return lax.all_gather(part, ("fsdp", "dp"), axis=0, tiled=True)


def reduce_rows(partial_sums):
    part = lax.psum_scatter(partial_sums, ("fsdp", "dp"), scatter_dimension=0, tiled=True)
    return lax.all_gather(part, "dp", axis=0, tiled=True)


def on_device(
    inputs,
    cotangent,
    lengths,
    attention_weights,
    attention_momentum,
    attention_average,
    ffn_inputs,
    ffn_inputs_momentum,
    ffn_inputs_average,
    ffn_output,
    ffn_output_momentum,
    ffn_output_average,
    gains,
    gains_momentum,
    gains_average,
):
    micro_count, slot, width = inputs.shape
    shard = attention_weights.shape[1]
    fsdp_size = lax.axis_size("fsdp")
    replicas = lax.axis_size("dp")
    pairs = width // PAIR
    hidden = ffn_inputs.shape[2]
    count = micro_count * slot

    proj_shard = (
        attention_weights[:3].astype(low).reshape(3, shard, pairs, PAIR).transpose(1, 2, 0, 3)
    ).reshape(shard, 3 * width)
    gain_columns = jnp.pad(gains.astype(low).T, ((0, 0), (0, HEAD_DIM - 3)))
    w_qfv = gather_rows(jnp.concatenate([proj_shard, gain_columns], axis=1))
    w_o = gather_rows(attention_weights[3].astype(low))
    w_gu = gather_rows(
        jnp.concatenate([ffn_inputs[0], ffn_inputs[1]], axis=1).astype(low)
    )
    w_d = gather_rows(ffn_output.astype(low))
    gains8 = jnp.pad(w_qfv[:, 3 * width : 3 * width + 3].T.astype(wide), ((0, 5), (0, 0)))

    rows = inputs.reshape(count, width)
    positions = jnp.arange(slot, dtype=jnp.int32)
    valid = (positions[None, :] < lengths).astype(wide).reshape(count, 1)
    errors = (cotangent.reshape(count, width).astype(wide) * valid).astype(low)

    mixed, q_pre, f_pre, values, mixer_out = mixer_forward(rows, w_qfv, gains8, slot)
    output, d_x1, d_mixed, grad_o, grad_two, grad_g, grad_u, grad_d = ffn(
        rows, mixed, errors, valid, gains8, w_o, w_gu, w_d
    )
    grad_qfv, grad_go, grad_one, input_grad = mixer_backward(
        rows, w_qfv, gains8, (q_pre, f_pre, values, mixer_out), d_mixed, d_x1, slot
    )
    gain_grads = jnp.concatenate([grad_one, grad_go, grad_two], axis=0)
    grad_o_gains = jnp.concatenate(
        [grad_o, jnp.pad(gain_grads.astype(low).T, ((0, 0), (0, HEAD_DIM - 3)))], axis=1
    )
    sum_g = reduce_rows(grad_g).astype(wide)
    sum_u = reduce_rows(grad_u).astype(wide)
    sum_d = reduce_rows(grad_d).astype(wide)
    sum_qfv = reduce_rows(grad_qfv).astype(wide)
    sum_o_gains = reduce_rows(grad_o_gains).astype(wide)

    sum_proj = sum_qfv.reshape(shard, pairs, 3, PAIR).transpose(2, 0, 1, 3).reshape(3, shard, width)
    sums = (
        jnp.concatenate([sum_proj, sum_o_gains[None, :, :width]], axis=0),
        jnp.stack([sum_g, sum_u]),
        sum_d,
        sum_o_gains[:, width : width + 3].T,
    )
    scale_rows = 1.0 / math.sqrt(count * fsdp_size * replicas)
    rates = (
        matrix_rate * scale_rows,
        matrix_rate * scale_rows,
        matrix_rate * scale_rows,
        gain_rate * scale_rows,
    )
    masters = (attention_weights, ffn_inputs, ffn_output, gains)
    momenta = (attention_momentum, ffn_inputs_momentum, ffn_output_momentum, gains_momentum)
    averages = (attention_average, ffn_inputs_average, ffn_output_average, gains_average)
    results = []
    for which in range(4):
        results.extend(
            update(masters[which], momenta[which], averages[which], sums[which], rates[which])
        )
    return (
        output.reshape(micro_count, slot, width),
        input_grad.reshape(micro_count, slot, width),
        *results,
    )


def solution(mesh):
    rows_split = P(None, ("fsdp", "dp"), None)
    middle_split = P(None, "fsdp", None)
    first_split = P("fsdp", None)
    gains_split = P(None, "fsdp")
    in_specs = (
        (rows_split, rows_split, P(None, ("fsdp", "dp")))
        + (middle_split,) * 6
        + (first_split,) * 3
        + (gains_split,) * 3
    )
    out_specs = (
        (rows_split, rows_split)
        + (middle_split,) * 6
        + (first_split,) * 3
        + (gains_split,) * 3
    )
    return jax.shard_map(
        on_device, mesh=mesh, in_specs=in_specs, out_specs=out_specs, check_vma=False
    )
```

```python
import functools
import math

import jax
import jax.numpy as jnp
from jax import lax
from jax.experimental import pallas as pl
from jax.experimental.pallas import tpu as pltpu
from jax.sharding import PartitionSpec as P

HEAD_DIM = 128
PAIR = 2 * HEAD_DIM
TILE_F = 256

lower_bound = 0.9
momentum_decay = 0.9
average_decay = 0.7
weight_decay = 0.0005
matrix_rate = 0.03
gain_rate = 0.1
low = jnp.bfloat16
wide = jnp.float32
VMEM_BYTES = 60 * 1024 * 1024


def mm(left, right):
    return jnp.dot(left, right, preferred_element_type=wide)


def mm_nt(left, right):
    return lax.dot_general(left, right, (((1,), (1,)), ((), ())), preferred_element_type=wide)


def mm_tn(left, right):
    return lax.dot_general(left, right, (((0,), (0,)), ((), ())), preferred_element_type=wide)


def sigmoid(u):
    return 1.0 / (1.0 + jnp.exp(-u))


def whole(shape):
    return pl.BlockSpec(shape, lambda *_: (0,) * len(shape), pipeline_mode=pl.Buffered(1))


def split_sum(ones_matrix, tensor):
    high = tensor.astype(low)
    rest = (tensor - high.astype(wide)).astype(low)
    return mm(ones_matrix, high) + mm(ones_matrix, rest)


def triangle(length, lower):
    rows = lax.broadcasted_iota(jnp.int32, (length, length), 0)
    columns = lax.broadcasted_iota(jnp.int32, (length, length), 1)
    kept = rows >= columns if lower else rows <= columns
    return kept.astype(wide).astype(low)


def decay_parts(f_pre, lower_ones):
    share = sigmoid(f_pre)
    gate = lower_bound + (1.0 - lower_bound) * share
    keys_in = (1.0 - lower_bound) * (1.0 - share)
    cumulative = split_sum(lower_ones, jnp.log(gate))
    middle_row = cumulative.shape[0] // 2
    cumulative = cumulative - cumulative[middle_row : middle_row + 1, :]
    return share, gate, keys_in, cumulative


def first_norm(x_ref, gain_row):
    rows = x_ref[...].astype(wide)
    scale = lax.rsqrt(jnp.mean(rows * rows, axis=-1, keepdims=True) + 1e-06)
    return rows * scale, scale


def lanes_of(half, size):
    return pl.ds(pl.multiple_of(half * size, size), size)


def mixer_forward_kernel(
    slot, half_ref, x_ref, w_ref, g_ref, on_ref, q_ref, f_ref, v_ref, o_ref, h_s
):
    @pl.when(pl.program_id(0) == 0)
    def _():
        normed, _ = first_norm(x_ref, None)
        h_s[...] = (normed * g_ref[0:1, :]).astype(low)

    gain_o = g_ref[1:2, lanes_of(half_ref[0] * pl.num_programs(0) + pl.program_id(0), PAIR)]
    pre = mm(h_s[...], w_ref[...])
    q_ref[...] = pre[:, :PAIR]
    f_ref[...] = pre[:, PAIR : 2 * PAIR]
    v_ref[...] = pre[:, 2 * PAIR :].astype(low)
    lower_ones = triangle(slot, True)
    block_rows = lax.broadcasted_iota(jnp.int32, (HEAD_DIM, HEAD_DIM), 0)
    block_columns = lax.broadcasted_iota(jnp.int32, (HEAD_DIM, HEAD_DIM), 1)
    causal = block_rows >= block_columns
    for sequence in range(x_ref.shape[0] // slot):
        rows = slice(sequence * slot, (sequence + 1) * slot)
        q_pre = q_ref[rows, :]
        _, _, keys_in, cumulative = decay_parts(f_ref[rows, :], lower_ones)
        grown = jnp.exp(-cumulative)
        decayed_q = (q_pre * sigmoid(q_pre) * jnp.exp(cumulative)).astype(low)
        grown_k = (keys_in * grown).astype(low)
        values = v_ref[rows, :]
        for head in range(2):
            lanes = slice(head * HEAD_DIM, (head + 1) * HEAD_DIM)
            for block in range(slot // HEAD_DIM):
                start, end = block * HEAD_DIM, (block + 1) * HEAD_DIM
                q_block = decayed_q[start:end, lanes]
                diagonal = mm_nt(q_block, grown_k[start:end, lanes])
                diagonal = jnp.where(causal, diagonal, 0.0).astype(low)
                out = mm(diagonal, values[start:end, lanes])
                if block > 0:
                    scores = mm_nt(q_block, grown_k[:start, lanes]).astype(low)
                    out = out + mm(scores, values[:start, lanes])
                scale = lax.rsqrt(jnp.mean(out * out, axis=-1, keepdims=True) + 1e-05)
                target = slice(sequence * slot + start, sequence * slot + end)
                o_ref[target, lanes] = out
                on_ref[target, lanes] = (out * scale * gain_o[:, lanes]).astype(low)


def mixer_forward(half, rows, weights, gains8, slot):
    count, width = rows.shape
    pairs = width // PAIR // 2
    by_pair = pl.BlockSpec((count, PAIR), lambda j, _: (0, j))
    shape = lambda kind: jax.ShapeDtypeStruct((count, width // 2), kind)
    return pl.pallas_call(
        functools.partial(mixer_forward_kernel, slot),
        grid_spec=pltpu.PrefetchScalarGridSpec(
            num_scalar_prefetch=1,
            grid=(pairs,),
            in_specs=[
                whole(rows.shape),
                pl.BlockSpec((width, 3 * PAIR), lambda j, _: (0, j)),
                whole(gains8.shape),
            ],
            out_specs=[by_pair] * 5,
            scratch_shapes=[pltpu.VMEM((count, width), low)],
        ),
        out_shape=[shape(low), shape(wide), shape(wide), shape(low), shape(wide)],
        compiler_params=pltpu.CompilerParams(vmem_limit_bytes=VMEM_BYTES),
        cost_estimate=pl.CostEstimate(
            flops=count * width * 3 * width + 10 * count * slot * width,
            bytes_accessed=count * width * 9 + width * width * 3,
            transcendentals=count * width * 3,
        ),
        name="mixer_forward",
    )(half, rows, weights, gains8)


def ffn_kernel(
    tiles,
    core_ref,
    x_ref,
    onm_ref,
    ono_ref,
    e_ref,
    m_ref,
    g_ref,
    wom_ref,
    woo_ref,
    wm_ref,
    wu_ref,
    wdm_ref,
    wdo_ref,
    out_ref,
    dx1_ref,
    donm_ref,
    dono_ref,
    gom_ref,
    goo_ref,
    g2_ref,
    gm_ref,
    gu_ref,
    gdm_ref,
    gdo_ref,
    x1_s,
    acc_s,
    dh_s,
    h_s,
    ht_s,
    on_s,
):
    step = pl.program_id(0)
    half = onm_ref.shape[1]
    first = core_ref[0] == 0
    mine = lanes_of(core_ref[0], half)
    other = lanes_of(1 - core_ref[0], half)

    @pl.when(step == 0)
    def _():
        on_s[:, mine] = onm_ref[...]
        on_s[:, other] = ono_ref[...]
        x1_s[:, mine] = x_ref[:, mine].astype(wide) + mm(on_s[...], wom_ref[...])
        x1_s[:, other] = x_ref[:, other].astype(wide) + mm(on_s[...], woo_ref[...])
        x1 = x1_s[...]
        scale = lax.rsqrt(jnp.mean(x1 * x1, axis=-1, keepdims=True) + 1e-06)
        normed = x1 * scale * g_ref[2:3, :]
        acc_s[...] = x1
        dh_s[...] = jnp.zeros_like(dh_s)
        h_s[...] = normed.astype(low)
        ht_s[...] = normed.T.astype(low)

    own = mm(h_s[...], wm_ref[...])
    swapped = mm(h_s[...], wu_ref[...])
    a = jnp.where(first, own, swapped)
    b = jnp.where(first, swapped, own)
    share = sigmoid(a)
    swish = a * share
    mid = (swish * b).astype(low)
    acc_s[:, mine] += mm(mid, wdm_ref[...])
    acc_s[:, other] += mm(mid, wdo_ref[...])
    d_mid = mm_nt(e_ref[:, mine], wdm_ref[...]) + mm_nt(e_ref[:, other], wdo_ref[...])
    gdm_ref[...] = mm_tn(mid, e_ref[:, mine]).astype(low)
    gdo_ref[...] = mm_tn(mid, e_ref[:, other]).astype(low)
    d_a = (d_mid * b * share * (1.0 + a * (1.0 - share))).astype(low)
    d_b = (d_mid * swish).astype(low)
    d_own = jnp.where(first, d_a, d_b)
    d_swapped = jnp.where(first, d_b, d_a)
    gm_ref[...] = mm(ht_s[...], d_own).astype(low)
    gu_ref[...] = mm(ht_s[...], d_swapped).astype(low)
    dh_s[...] += mm_nt(d_own, wm_ref[...]) + mm_nt(d_swapped, wu_ref[...])

    @pl.when(step == tiles - 1)
    def _():
        mask = m_ref[...]
        out_ref[...] = (acc_s[...] * mask).astype(low)
        x1 = x1_s[...]
        scale = lax.rsqrt(jnp.mean(x1 * x1, axis=-1, keepdims=True) + 1e-06)
        normed = x1 * scale
        d_h2 = dh_s[...]
        scaled = d_h2 * g_ref[2:3, :]
        g2_ref[...] = jnp.sum(d_h2 * normed, axis=0, keepdims=True)
        d_x1 = e_ref[...].astype(wide) + scale * (
            scaled - normed * jnp.mean(scaled * normed, axis=-1, keepdims=True)
        )
        dx1_ref[...] = d_x1
        h_s[...] = d_x1.astype(low)
        dh_s[...] = mm_nt(h_s[:, mine], wom_ref[...]) + mm_nt(h_s[:, other], woo_ref[...])
        donm_ref[...] = dh_s[:, mine]
        dono_ref[...] = dh_s[:, other]
        gom_ref[...] = mm_tn(on_s[...], h_s[:, mine]).astype(low)
        goo_ref[...] = mm_tn(on_s[...], h_s[:, other]).astype(low)


def ffn(core, rows, mixed, errors, mask, gains8, w_o, w_gu, w_d):
    count, width = rows.shape
    half = width // 2
    hidden = w_d[0].shape[0]
    tiles = hidden // TILE_F
    full = whole((count, width))
    half_full = whole((count, half))
    in_tile = pl.BlockSpec((width, TILE_F), lambda j, _: (0, j))
    out_tile = pl.BlockSpec((TILE_F, half), lambda j, _: (j, 0))
    struct = jax.ShapeDtypeStruct
    return pl.pallas_call(
        functools.partial(ffn_kernel, tiles),
        grid_spec=pltpu.PrefetchScalarGridSpec(
            num_scalar_prefetch=1,
            grid=(tiles,),
            in_specs=[
                full,
                half_full,
                half_full,
                full,
                whole((count, 1)),
                whole(gains8.shape),
                whole((width, half)),
                whole((width, half)),
                in_tile,
                in_tile,
                out_tile,
                out_tile,
            ],
            out_specs=[
                full,
                full,
                half_full,
                half_full,
                whole((width, half)),
                whole((width, half)),
                whole((1, width)),
                in_tile,
                in_tile,
                out_tile,
                out_tile,
            ],
            scratch_shapes=[
                pltpu.VMEM((count, width), wide),
                pltpu.VMEM((count, width), wide),
                pltpu.VMEM((count, width), wide),
                pltpu.VMEM((count, width), low),
                pltpu.VMEM((width, count), low),
                pltpu.VMEM((count, width), low),
            ],
        ),
        out_shape=[
            struct((count, width), low),
            struct((count, width), wide),
            struct((count, half), wide),
            struct((count, half), wide),
            struct((width, half), low),
            struct((width, half), low),
            struct((1, width), wide),
            struct((width, hidden), low),
            struct((width, hidden), low),
            struct((hidden, half), low),
            struct((hidden, half), low),
        ],
        compiler_params=pltpu.CompilerParams(vmem_limit_bytes=VMEM_BYTES),
        cost_estimate=pl.CostEstimate(
            flops=2 * count * width * (8 * hidden + 3 * width),
            bytes_accessed=count * width * 20 + width * hidden * 12 + width * width * 4,
            transcendentals=count * hidden,
        ),
        name="ffn",
    )(core, rows, *mixed, errors, mask, gains8, *w_o, *w_gu, *w_d)


def mixer_backward_kernel(
    slot,
    pairs,
    last,
    half_ref,
    x_ref,
    w_ref,
    g_ref,
    q_ref,
    f_ref,
    v_ref,
    o_ref,
    don_ref,
    part_ref,
    dx1_ref,
    grad_ref,
    ggo_ref,
    g1_ref,
    dx_ref,
    ht_s,
    dh_s,
    pre_s,
):
    step = pl.program_id(0)

    @pl.when(step == 0)
    def _():
        normed, _ = first_norm(x_ref, None)
        ht_s[...] = (normed * g_ref[0:1, :]).T.astype(low)
        dh_s[...] = part_ref[...] if last else jnp.zeros_like(dh_s)

    gain_o = g_ref[1:2, lanes_of(half_ref[0] * pairs + step, PAIR)]
    lower_ones = triangle(slot, True)
    upper_ones = triangle(slot, False)
    block_rows = lax.broadcasted_iota(jnp.int32, (HEAD_DIM, HEAD_DIM), 0)
    block_columns = lax.broadcasted_iota(jnp.int32, (HEAD_DIM, HEAD_DIM), 1)
    causal = block_rows >= block_columns
    causal_t = block_rows <= block_columns
    blocks = slot // HEAD_DIM
    ggo_total = jnp.zeros((1, PAIR), wide)
    for sequence in range(x_ref.shape[0] // slot):
        rows = slice(sequence * slot, (sequence + 1) * slot)
        d_on = don_ref[rows, :]
        out = o_ref[rows, :]
        d_out_parts = []
        ggo_parts = []
        for head in range(2):
            lanes = slice(head * HEAD_DIM, (head + 1) * HEAD_DIM)
            out_h, d_on_h = out[:, lanes], d_on[:, lanes]
            scale = lax.rsqrt(jnp.mean(out_h * out_h, axis=-1, keepdims=True) + 1e-05)
            normed = out_h * scale
            ggo_parts.append(jnp.sum(d_on_h * normed, axis=0, keepdims=True))
            scaled = d_on_h * gain_o[:, lanes]
            inner = jnp.mean(scaled * normed, axis=-1, keepdims=True)
            d_out_parts.append((scale * (scaled - normed * inner)).astype(low))
        ggo_total = ggo_total + jnp.concatenate(ggo_parts, axis=1)

        q_pre = q_ref[rows, :]
        share, gate, keys_in, cumulative = decay_parts(f_ref[rows, :], lower_ones)
        grown = jnp.exp(-cumulative)
        shrunk = jnp.exp(cumulative)
        q_share = sigmoid(q_pre)
        decayed_q = (q_pre * q_share * shrunk).astype(low)
        grown_k = (keys_in * grown).astype(low)
        values = v_ref[rows, :]
        dq_parts, dk_parts, dv_parts = [], [], []
        for head in range(2):
            lanes = slice(head * HEAD_DIM, (head + 1) * HEAD_DIM)
            q_h, k_h, v_h = decayed_q[:, lanes], grown_k[:, lanes], values[:, lanes]
            d_out = d_out_parts[head]
            dq_blocks, dk_blocks, dv_blocks = [], [], []
            for block in range(blocks):
                start, end = block * HEAD_DIM, (block + 1) * HEAD_DIM
                here = slice(start, end)
                d_scores = mm_nt(d_out[here], v_h[here])
                d_scores = jnp.where(causal, d_scores, 0.0).astype(low)
                d_q = mm(d_scores, k_h[here])
                if block > 0:
                    before = slice(0, start)
                    d_scores = mm_nt(d_out[here], v_h[before]).astype(low)
                    d_q = d_q + mm(d_scores, k_h[before])
                dq_blocks.append(d_q)
                scores = jnp.where(causal_t, mm_nt(k_h[here], q_h[here]), 0.0).astype(low)
                d_scores = jnp.where(causal_t, mm_nt(v_h[here], d_out[here]), 0.0).astype(low)
                d_v = mm(scores, d_out[here])
                d_k = mm(d_scores, q_h[here])
                if block < blocks - 1:
                    after = slice(end, slot)
                    scores = mm_nt(k_h[here], q_h[after]).astype(low)
                    d_scores = mm_nt(v_h[here], d_out[after]).astype(low)
                    d_v = d_v + mm(scores, d_out[after])
                    d_k = d_k + mm(d_scores, q_h[after])
                dk_blocks.append(d_k)
                dv_blocks.append(d_v)
            dq_parts.append(jnp.concatenate(dq_blocks, axis=0))
            dk_parts.append(jnp.concatenate(dk_blocks, axis=0))
            dv_parts.append(jnp.concatenate(dv_blocks, axis=0))
        d_decayed = jnp.concatenate(dq_parts, axis=1)
        d_grown = jnp.concatenate(dk_parts, axis=1)
        d_value = jnp.concatenate(dv_parts, axis=1)
        d_cumulative = decayed_q.astype(wide) * d_decayed - grown_k.astype(wide) * d_grown
        d_log = split_sum(upper_ones, d_cumulative)
        d_query = d_decayed * shrunk
        d_key = d_grown * grown
        d_q_pre = d_query * q_share * (1.0 + q_pre * (1.0 - q_share))
        d_f_pre = (1.0 - lower_bound) * (d_log / gate - d_key) * share * (1.0 - share)
        pre_s[rows, :PAIR] = d_q_pre.astype(low)
        pre_s[rows, PAIR : 2 * PAIR] = d_f_pre.astype(low)
        pre_s[rows, 2 * PAIR :] = d_value.astype(low)

    ggo_ref[...] = ggo_total
    grad_ref[...] = mm(ht_s[...], pre_s[...]).astype(low)
    dh_s[...] += mm_nt(pre_s[...], w_ref[...])

    @pl.when(step == pairs - 1)
    def _():
        if not last:
            dx_ref[...] = dh_s[...]
            return
        normed, scale = first_norm(x_ref, None)
        d_h1 = dh_s[...]
        scaled = d_h1 * g_ref[0:1, :]
        g1_ref[...] = jnp.sum(d_h1 * normed, axis=0, keepdims=True)
        dx_ref[...] = dx1_ref[...] + scale * (
            scaled - normed * jnp.mean(scaled * normed, axis=-1, keepdims=True)
        )


def mixer_backward_first_kernel(
    slot, pairs, half_ref, x_ref, w_ref, g_ref, q_ref, f_ref, v_ref, o_ref, don_ref, *outs
):
    grad_ref, ggo_ref, dh_ref, ht_s, dh_s, pre_s = outs
    mixer_backward_kernel(
        slot,
        pairs,
        False,
        half_ref,
        x_ref,
        w_ref,
        g_ref,
        q_ref,
        f_ref,
        v_ref,
        o_ref,
        don_ref,
        None,
        None,
        grad_ref,
        ggo_ref,
        None,
        dh_ref,
        ht_s,
        dh_s,
        pre_s,
    )


def mixer_backward(half, rows, weights, gains8, kept, d_mixed, slot, ending=None):
    count, width = rows.shape
    pairs = width // PAIR // 2
    full = whole((count, width))
    by_pair = pl.BlockSpec((count, PAIR), lambda j, _: (0, j))
    weight_tile = pl.BlockSpec((width, 3 * PAIR), lambda j, _: (0, j))
    gain_tile = pl.BlockSpec((1, PAIR), lambda j, _: (0, j))
    struct = jax.ShapeDtypeStruct
    in_specs = [full, weight_tile, whole(gains8.shape)] + [by_pair] * 5
    out_specs = [weight_tile, gain_tile, full]
    out_shape = [
        struct((width, 3 * width // 2), low),
        struct((1, width // 2), wide),
        struct((count, width), wide),
    ]
    kernel = functools.partial(mixer_backward_first_kernel, slot, pairs)
    operands = [half, rows, weights, gains8, *kept, d_mixed]
    if ending is not None:
        kernel = functools.partial(mixer_backward_kernel, slot, pairs, True)
        in_specs += [full, full]
        operands += list(ending)
        out_specs.insert(2, whole((1, width)))
        out_shape.insert(2, struct((1, width), wide))
    return pl.pallas_call(
        kernel,
        grid_spec=pltpu.PrefetchScalarGridSpec(
            num_scalar_prefetch=1,
            grid=(pairs,),
            in_specs=in_specs,
            out_specs=out_specs,
            scratch_shapes=[
                pltpu.VMEM((width, count), low),
                pltpu.VMEM((count, width), wide),
                pltpu.VMEM((count, 3 * PAIR), low),
            ],
        ),
        out_shape=out_shape,
        compiler_params=pltpu.CompilerParams(vmem_limit_bytes=VMEM_BYTES),
        cost_estimate=pl.CostEstimate(
            flops=2 * count * width * 3 * width + 20 * count * slot * width,
            bytes_accessed=count * width * 17 + width * width * 6,
            transcendentals=count * width * 4,
        ),
        name="mixer_backward",
    )(*operands)


def update(weight, momentum, average, gradient, step_rate):
    new_momentum = momentum_decay * momentum + gradient
    direction = gradient + momentum_decay * new_momentum + weight_decay * weight
    new_weight = weight - step_rate * direction
    new_average = average_decay * average + (1.0 - average_decay) * new_weight
    return (new_momentum, new_average, new_weight)


def update_kernel(pick, step_rate, core_ref, w_ref, m_ref, a_ref, *refs):
    sums, outs = refs[:-3], refs[-3:]
    gradient = pick(core_ref[0], *[s[...] for s in sums]).astype(wide).reshape(w_ref.shape)
    results = update(w_ref[...], m_ref[...], a_ref[...], gradient, step_rate)
    for out, result in zip(outs, results):
        out[...] = result


def update_call(core, state, sums, grid, state_spec, sum_specs, pick, step_rate, name):
    struct = jax.ShapeDtypeStruct(state[0].shape, wide)
    size = math.prod(state[0].shape)
    return pl.pallas_call(
        functools.partial(update_kernel, pick, step_rate),
        grid_spec=pltpu.PrefetchScalarGridSpec(
            num_scalar_prefetch=1,
            grid=grid,
            in_specs=[state_spec] * 3 + sum_specs,
            out_specs=[state_spec] * 3,
        ),
        out_shape=[struct] * 3,
        compiler_params=pltpu.CompilerParams(vmem_limit_bytes=VMEM_BYTES),
        cost_estimate=pl.CostEstimate(flops=10 * size, bytes_accessed=26 * size, transcendentals=0),
        name=name,
    )(core, *state, *sums)


def update_attention(core, state, qfv, out, step_rate):
    _, shard, width = state[0].shape

    def pick(core_index, qfv_mine, qfv_other, out_mine, out_other):
        own = pl.program_id(1) // 2 == core_index
        proj = jnp.where(own, qfv_mine.astype(wide), qfv_other.astype(wide))
        last = jnp.where(own, out_mine.astype(wide), out_other.astype(wide))
        return jnp.where(pl.program_id(0) < 3, proj, last)

    proj_spec = pl.BlockSpec(
        (shard, PAIR), lambda kind, pair, _: (0, (pair % 2) * 3 + jnp.minimum(kind, 2))
    )
    out_spec = pl.BlockSpec((shard, PAIR), lambda kind, pair, _: (0, pair % 2))
    return update_call(
        core,
        state,
        (*qfv, *out),
        (4, width // PAIR),
        pl.BlockSpec((1, shard, PAIR), lambda kind, pair, _: (kind, 0, pair)),
        [proj_spec, proj_spec, out_spec, out_spec],
        pick,
        step_rate,
        "update_attention",
    )


def update_ffn_in(core, state, sums, step_rate):
    _, shard, hidden = state[0].shape
    tile = hidden // 2

    def pick(core_index, mine, other):
        own = pl.program_id(0) == core_index
        return jnp.where(own, mine.astype(wide), other.astype(wide))

    sum_spec = pl.BlockSpec((shard, tile), lambda kind, j, _: (0, j))
    return update_call(
        core,
        state,
        sums,
        (2, 2),
        pl.BlockSpec((1, shard, tile), lambda kind, j, _: (kind, 0, j)),
        [sum_spec, sum_spec],
        pick,
        step_rate,
        "update_ffn_in",
    )


def update_ffn_out(core, state, sums, step_rate):
    shard, width = state[0].shape

    def pick(core_index, mine, other):
        own = pl.program_id(0) // 2 == core_index
        return jnp.where(own, mine.astype(wide), other.astype(wide))

    sum_spec = pl.BlockSpec((shard, PAIR), lambda j, _: (0, j % 2))
    return update_call(
        core,
        state,
        sums,
        (width // PAIR,),
        pl.BlockSpec((shard, PAIR), lambda j, _: (0, j)),
        [sum_spec, sum_spec],
        pick,
        step_rate,
        "update_ffn_out",
    )


RING = 8


def ring_place(index):
    return jnp.where(index % 2 == 0, index // 2, RING - 1 - index // 2)


def ring_member(place):
    place = place % RING
    return jnp.where(place < RING // 2, 2 * place, 2 * RING - 1 - 2 * place)


def ring_next(tensor):
    cycle = [0, 2, 4, 6, 7, 5, 3, 1]
    replicas = lax.axis_size("dp")
    pairs = []
    for place, member in enumerate(cycle):
        for replica in range(replicas):
            target = cycle[(place + (1 if replica % 2 == 0 else -1)) % RING]
            pairs.append((member * replicas + replica, target * replicas + replica))
    return lax.ppermute(tensor, ("fsdp", "dp"), pairs)


def core_swap(tensor):
    return lax.ppermute(tensor, "dp", [(d, d ^ 1) for d in range(lax.axis_size("dp"))])


def column_swap(tensor):
    return lax.ppermute(tensor, "dp", [(d, d ^ 2) for d in range(lax.axis_size("dp"))])


def gather_rows(shard):
    if lax.axis_size("fsdp") != RING:
        mine = lax.all_gather(shard, "fsdp", axis=0, tiled=True)
        return mine, core_swap(mine)
    me = lax.axis_index("fsdp")
    way = 1 - 2 * (lax.axis_index("dp") % 2)
    rows = shard.shape[0]
    mine = jnp.zeros((RING * rows, shard.shape[1]), shard.dtype)
    mine = lax.dynamic_update_slice_in_dim(mine, shard, me * rows, 0)
    piece = shard
    for step in range(1, RING):
        piece = ring_next(piece)
        origin = ring_member(ring_place(me) - way * step + RING)
        mine = lax.dynamic_update_slice_in_dim(mine, piece, origin * rows, 0)
    return mine, core_swap(mine)


def reduce_rows(mine, other):
    arrived = core_swap(other)
    if lax.axis_size("fsdp") != RING:
        both = (mine.astype(wide) + arrived.astype(wide)).astype(low)
        total = lax.psum_scatter(both, "fsdp", scatter_dimension=0, tiled=True)
    else:
        me = lax.axis_index("fsdp")
        way = 1 - 2 * (lax.axis_index("dp") % 2)
        rows = mine.shape[0] // RING
        total = None
        for step in range(RING):
            owner = ring_member(ring_place(me) - way * (step + 1) + 2 * RING)
            term = lax.dynamic_slice_in_dim(mine, owner * rows, rows, 0).astype(wide)
            term = term + lax.dynamic_slice_in_dim(arrived, owner * rows, rows, 0).astype(wide)
            if total is not None:
                term = term + ring_next(total).astype(wide)
            total = term.astype(low)
    total = (total.astype(wide) + column_swap(total).astype(wide)).astype(low)
    return total, core_swap(total)


def on_device(
    inputs,
    cotangent,
    lengths,
    attention_weights,
    attention_momentum,
    attention_average,
    ffn_inputs,
    ffn_inputs_momentum,
    ffn_inputs_average,
    ffn_output,
    ffn_output_momentum,
    ffn_output_average,
    gains,
    gains_momentum,
    gains_average,
):
    micro_count, slot, width = inputs.shape
    shard = attention_weights.shape[1]
    fsdp_size = lax.axis_size("fsdp")
    replicas = lax.axis_size("dp")
    core = lax.axis_index("dp") % 2
    halves = width // PAIR // 2
    count = micro_count * slot

    proj = lax.dynamic_slice_in_dim(attention_weights[:3], core * (width // 2), width // 2, 2)
    proj = proj.astype(low).reshape(3, shard, halves, PAIR).transpose(1, 2, 0, 3)
    proj = proj.reshape(shard, 3 * width // 2)
    gain_columns = jnp.pad(gains.astype(low).T, ((0, 0), (0, HEAD_DIM - 3)))
    w_qfv = gather_rows(jnp.concatenate([proj, gain_columns], axis=1))
    out_half = lax.dynamic_slice_in_dim(attention_weights[3], core * (width // 2), width // 2, 1)
    w_o = gather_rows(out_half.astype(low))
    w_gu = gather_rows(
        lax.dynamic_index_in_dim(ffn_inputs, core, 0, keepdims=False).astype(low)
    )
    down_half = lax.dynamic_slice_in_dim(ffn_output, core * (width // 2), width // 2, 1)
    w_d = gather_rows(down_half.astype(low))
    gain_rows = w_qfv[0][:, 3 * width // 2 : 3 * width // 2 + 3].T.astype(wide)
    gains8 = jnp.pad(gain_rows, ((0, 5), (0, 0)))

    rows = inputs.reshape(count, width)
    positions = jnp.arange(slot, dtype=jnp.int32)
    valid = (positions[None, :] < lengths).astype(wide).reshape(count, 1)
    errors = (cotangent.reshape(count, width).astype(wide) * valid).astype(low)
    core_ref = core.astype(jnp.int32).reshape(1)
    other_ref = 1 - core_ref

    mixed_mine, *kept_mine = mixer_forward(core_ref, rows, w_qfv[0], gains8, slot)
    mixed_other, *kept_other = mixer_forward(other_ref, rows, w_qfv[1], gains8, slot)
    output, d_x1, don_mine, don_other, go_mine, go_other, grad_two, *grad_ffn = ffn(
        core_ref, rows, (mixed_mine, mixed_other), errors, valid, gains8, w_o, w_gu, w_d
    )
    sum_gu = reduce_rows(*grad_ffn[:2])
    sum_d = reduce_rows(*grad_ffn[2:])
    gqfv_other, ggo_other, d_h1 = mixer_backward(
        other_ref, rows, w_qfv[1], gains8, kept_other, don_other, slot
    )
    gqfv_mine, ggo_mine, grad_one, input_grad = mixer_backward(
        core_ref, rows, w_qfv[0], gains8, kept_mine, don_mine, slot, (d_h1, d_x1)
    )
    sum_qfv = reduce_rows(gqfv_mine, gqfv_other)
    is_first = core == 0
    grad_go = jnp.concatenate(
        [jnp.where(is_first, ggo_mine, ggo_other), jnp.where(is_first, ggo_other, ggo_mine)], axis=1
    )
    gain_grads = jnp.concatenate([grad_one, grad_go, grad_two], axis=0).astype(low).T
    gain_grads = jnp.pad(gain_grads, ((0, 0), (0, HEAD_DIM - 3)))
    sum_o = reduce_rows(
        jnp.concatenate([go_mine, gain_grads], axis=1),
        jnp.concatenate([go_other, gain_grads], axis=1),
    )
    sum_gains = sum_o[0][:, width // 2 : width // 2 + 3].T.astype(wide)

    scale_rows = 1.0 / math.sqrt(count * fsdp_size * replicas)
    attention_state = (attention_weights, attention_momentum, attention_average)
    ffn_in_state = (ffn_inputs, ffn_inputs_momentum, ffn_inputs_average)
    ffn_out_state = (ffn_output, ffn_output_momentum, ffn_output_average)
    return (
        output.reshape(micro_count, slot, width),
        input_grad.reshape(micro_count, slot, width),
        *update_attention(core_ref, attention_state, sum_qfv, sum_o, matrix_rate * scale_rows),
        *update_ffn_in(core_ref, ffn_in_state, sum_gu, matrix_rate * scale_rows),
        *update_ffn_out(core_ref, ffn_out_state, sum_d, matrix_rate * scale_rows),
        *update(gains, gains_momentum, gains_average, sum_gains, gain_rate * scale_rows),
    )


def solution(mesh):
    rows_split = P(None, ("fsdp", "dp"), None)
    middle_split = P(None, "fsdp", None)
    first_split = P("fsdp", None)
    gains_split = P(None, "fsdp")
    in_specs = (
        (rows_split, rows_split, P(None, ("fsdp", "dp")))
        + (middle_split,) * 6
        + (first_split,) * 3
        + (gains_split,) * 3
    )
    out_specs = (
        (rows_split, rows_split)
        + (middle_split,) * 6
        + (first_split,) * 3
        + (gains_split,) * 3
    )
    return jax.shard_map(
        on_device, mesh=mesh, in_specs=in_specs, out_specs=out_specs, check_vma=False
    )
```

```python
import functools
import math

import jax
import jax.numpy as jnp
from jax import lax
from jax.experimental import pallas as pl
from jax.experimental.pallas import tpu as pltpu
from jax.sharding import PartitionSpec as P

HEAD_DIM = 128
PAIR = 2 * HEAD_DIM

lower_bound = 0.9
momentum_decay = 0.9
average_decay = 0.7
weight_decay = 0.0005
matrix_rate = 0.03
gain_rate = 0.1
low = jnp.bfloat16
wide = jnp.float32
VMEM_BYTES = 60 * 1024 * 1024


def mm(left, right):
    return jnp.dot(left, right, preferred_element_type=wide)


def mm_nt(left, right):
    return lax.dot_general(left, right, (((1,), (1,)), ((), ())), preferred_element_type=wide)


def mm_tn(left, right):
    return lax.dot_general(left, right, (((0,), (0,)), ((), ())), preferred_element_type=wide)


def sigmoid(u):
    return 1.0 / (1.0 + jnp.exp(-u))


def whole(shape):
    return pl.BlockSpec(shape, lambda *_: (0,) * len(shape), pipeline_mode=pl.Buffered(1))


def split_sum(ones_matrix, tensor):
    high = tensor.astype(low)
    rest = (tensor - high.astype(wide)).astype(low)
    return mm(ones_matrix, high) + mm(ones_matrix, rest)


def triangle(length, lower):
    rows = lax.broadcasted_iota(jnp.int32, (length, length), 0)
    columns = lax.broadcasted_iota(jnp.int32, (length, length), 1)
    kept = rows >= columns if lower else rows <= columns
    return kept.astype(wide).astype(low)


def decay_parts(f_pre, lower_ones):
    share = sigmoid(f_pre)
    gate = lower_bound + (1.0 - lower_bound) * share
    keys_in = (1.0 - lower_bound) * (1.0 - share)
    cumulative = split_sum(lower_ones, jnp.log(gate))
    middle_row = cumulative.shape[0] // 2
    cumulative = cumulative - cumulative[middle_row : middle_row + 1, :]
    return share, gate, keys_in, cumulative


def first_norm(x_ref, gain_row):
    rows = x_ref[...].astype(wide)
    scale = lax.rsqrt(jnp.mean(rows * rows, axis=-1, keepdims=True) + 1e-06)
    return rows * scale, scale


def lanes_of(half, size):
    return pl.ds(pl.multiple_of(half * size, size), size)


def mixer_forward_kernel(
    slot, half_ref, x_ref, w_ref, g_ref, on_ref, q_ref, f_ref, v_ref, o_ref, h_s
):
    @pl.when(pl.program_id(0) == 0)
    def _():
        normed, _ = first_norm(x_ref, None)
        h_s[...] = (normed * g_ref[0:1, :]).astype(low)

    gain_o = g_ref[1:2, lanes_of(half_ref[0] * pl.num_programs(0) + pl.program_id(0), PAIR)]
    pre = mm(h_s[...], w_ref[...])
    q_ref[...] = pre[:, :PAIR]
    f_ref[...] = pre[:, PAIR : 2 * PAIR]
    v_ref[...] = pre[:, 2 * PAIR :].astype(low)
    lower_ones = triangle(slot, True)
    block_rows = lax.broadcasted_iota(jnp.int32, (HEAD_DIM, HEAD_DIM), 0)
    block_columns = lax.broadcasted_iota(jnp.int32, (HEAD_DIM, HEAD_DIM), 1)
    causal = block_rows >= block_columns
    for sequence in range(x_ref.shape[0] // slot):
        rows = slice(sequence * slot, (sequence + 1) * slot)
        q_pre = q_ref[rows, :]
        _, _, keys_in, cumulative = decay_parts(f_ref[rows, :], lower_ones)
        grown = jnp.exp(-cumulative)
        decayed_q = (q_pre * sigmoid(q_pre) * jnp.exp(cumulative)).astype(low)
        grown_k = (keys_in * grown).astype(low)
        values = v_ref[rows, :]
        for head in range(2):
            lanes = slice(head * HEAD_DIM, (head + 1) * HEAD_DIM)
            for block in range(slot // HEAD_DIM):
                start, end = block * HEAD_DIM, (block + 1) * HEAD_DIM
                q_block = decayed_q[start:end, lanes]
                diagonal = mm_nt(q_block, grown_k[start:end, lanes])
                diagonal = jnp.where(causal, diagonal, 0.0).astype(low)
                out = mm(diagonal, values[start:end, lanes])
                if block > 0:
                    scores = mm_nt(q_block, grown_k[:start, lanes]).astype(low)
                    out = out + mm(scores, values[:start, lanes])
                scale = lax.rsqrt(jnp.mean(out * out, axis=-1, keepdims=True) + 1e-05)
                target = slice(sequence * slot + start, sequence * slot + end)
                o_ref[target, lanes] = out
                on_ref[target, lanes] = (out * scale * gain_o[:, lanes]).astype(low)


def mixer_forward_last_kernel(
    slot,
    half_ref,
    x_ref,
    w_ref,
    g_ref,
    before_ref,
    woo_ref,
    wom_ref,
    on_ref,
    q_ref,
    f_ref,
    v_ref,
    o_ref,
    x1_ref,
    h2_ref,
    h2t_ref,
    h_s,
    on_s,
):
    step = pl.program_id(0)
    half = before_ref.shape[1]
    mixer_forward_kernel(
        slot, half_ref, x_ref, w_ref, g_ref, on_ref, q_ref, f_ref, v_ref, o_ref, h_s
    )
    on_s[:, lanes_of(half_ref[0] * pl.num_programs(0) + step, PAIR)] = on_ref[...]

    @pl.when(step == pl.num_programs(0) - 1)
    def _():
        here = lanes_of(half_ref[0], half)
        there = lanes_of(1 - half_ref[0], half)
        on_s[:, there] = before_ref[...]
        x1_ref[:, here] = x_ref[:, here].astype(wide) + mm(on_s[...], woo_ref[...])
        x1_ref[:, there] = x_ref[:, there].astype(wide) + mm(on_s[...], wom_ref[...])
        x1 = x1_ref[...]
        scale = lax.rsqrt(jnp.mean(x1 * x1, axis=-1, keepdims=True) + 1e-06)
        normed = x1 * scale * g_ref[2:3, :]
        h2_ref[...] = normed.astype(low)
        h2t_ref[...] = normed.T.astype(low)


def mixer_forward(half, rows, weights, gains8, slot, ending=None):
    count, width = rows.shape
    pairs = width // PAIR // 2
    by_pair = pl.BlockSpec((count, PAIR), lambda j, _: (0, j))
    struct = jax.ShapeDtypeStruct
    shape = lambda kind: struct((count, width // 2), kind)
    kernel = mixer_forward_kernel
    in_specs = [
        whole(rows.shape),
        pl.BlockSpec((width, 3 * PAIR), lambda j, _: (0, j)),
        whole(gains8.shape),
    ]
    operands = [half, rows, weights, gains8]
    out_specs = [by_pair] * 5
    out_shape = [shape(low), shape(wide), shape(wide), shape(low), shape(wide)]
    scratch = [pltpu.VMEM((count, width), low)]
    if ending is not None:
        kernel = mixer_forward_last_kernel
        out_weights = pl.BlockSpec((width, width // 2), lambda j, _: (0, 3))
        in_specs += [whole((count, width // 2)), out_weights, out_weights]
        operands += [ending[0], weights, ending[1]]
        out_specs += [whole((count, width)), whole((count, width)), whole((width, count))]
        out_shape += [
            struct((count, width), wide),
            struct((count, width), low),
            struct((width, count), low),
        ]
        scratch += [pltpu.VMEM((count, width), low)]
    return pl.pallas_call(
        functools.partial(kernel, slot),
        grid_spec=pltpu.PrefetchScalarGridSpec(
            num_scalar_prefetch=1,
            grid=(pairs,),
            in_specs=in_specs,
            out_specs=out_specs,
            scratch_shapes=scratch,
        ),
        out_shape=out_shape,
        compiler_params=pltpu.CompilerParams(vmem_limit_bytes=VMEM_BYTES),
        cost_estimate=pl.CostEstimate(
            flops=count * width * 4 * width + 10 * count * slot * width,
            bytes_accessed=count * width * 12 + width * width * 4,
            transcendentals=count * width * 3,
        ),
        name="mixer_forward",
    )(*operands)


def ffn_tile(
    core_ref, h_ref, ht_ref, e_ref, wm_ref, wu_ref, wdm_ref, wdo_ref, grads, acc_ref, dh_ref
):
    gm_ref, gu_ref, gdm_ref, gdo_ref = grads
    half = wdm_ref.shape[1]
    first = core_ref[0] == 0
    mine = lanes_of(core_ref[0], half)
    other = lanes_of(1 - core_ref[0], half)
    own = mm(h_ref[...], wm_ref[...])
    swapped = mm(h_ref[...], wu_ref[...])
    a = jnp.where(first, own, swapped)
    b = jnp.where(first, swapped, own)
    share = sigmoid(a)
    swish = a * share
    mid = (swish * b).astype(low)
    acc_ref[:, mine] += mm(mid, wdm_ref[...])
    acc_ref[:, other] += mm(mid, wdo_ref[...])
    d_mid = mm_nt(e_ref[:, mine], wdm_ref[...]) + mm_nt(e_ref[:, other], wdo_ref[...])
    gdm_ref[...] = mm_tn(mid, e_ref[:, mine]).astype(low)
    gdo_ref[...] = mm_tn(mid, e_ref[:, other]).astype(low)
    d_a = (d_mid * b * share * (1.0 + a * (1.0 - share))).astype(low)
    d_b = (d_mid * swish).astype(low)
    d_own = jnp.where(first, d_a, d_b)
    d_swapped = jnp.where(first, d_b, d_a)
    gm_ref[...] = mm(ht_ref[...], d_own).astype(low)
    gu_ref[...] = mm(ht_ref[...], d_swapped).astype(low)
    dh_ref[...] += mm_nt(d_own, wm_ref[...]) + mm_nt(d_swapped, wu_ref[...])


def ffn_first_kernel(
    core_ref,
    h_ref,
    ht_ref,
    e_ref,
    wm_ref,
    wu_ref,
    wdm_ref,
    wdo_ref,
    x1_ref,
    gm_ref,
    gu_ref,
    gdm_ref,
    gdo_ref,
    acc_ref,
    dh_ref,
):
    @pl.when(pl.program_id(0) == 0)
    def _():
        acc_ref[...] = x1_ref[...]
        dh_ref[...] = jnp.zeros_like(dh_ref)

    grads = (gm_ref, gu_ref, gdm_ref, gdo_ref)
    ffn_tile(
        core_ref, h_ref, ht_ref, e_ref, wm_ref, wu_ref, wdm_ref, wdo_ref, grads, acc_ref, dh_ref
    )


def ffn_middle_kernel(
    core_ref,
    h_ref,
    ht_ref,
    e_ref,
    wm_ref,
    wu_ref,
    wdm_ref,
    wdo_ref,
    acc_in_ref,
    dh_in_ref,
    gdm_in_ref,
    gdo_in_ref,
    gm_ref,
    gu_ref,
    gdm_ref,
    gdo_ref,
    acc_ref,
    dh_ref,
):
    @pl.when(pl.program_id(0) == 0)
    def _():
        acc_ref[...] = acc_in_ref[...]
        dh_ref[...] = dh_in_ref[...]

    grads = (gm_ref, gu_ref, gdm_ref, gdo_ref)
    ffn_tile(
        core_ref, h_ref, ht_ref, e_ref, wm_ref, wu_ref, wdm_ref, wdo_ref, grads, acc_ref, dh_ref
    )


def ffn_last_kernel(
    core_ref,
    h_ref,
    ht_ref,
    e_ref,
    wm_ref,
    wu_ref,
    wdm_ref,
    wdo_ref,
    acc_in_ref,
    dh_in_ref,
    gdm_in_ref,
    gdo_in_ref,
    x1_ref,
    onm_ref,
    ono_ref,
    wom_ref,
    woo_ref,
    m_ref,
    g_ref,
    gm_ref,
    gu_ref,
    gdm_ref,
    gdo_ref,
    out_ref,
    dh_s,
    acc_s,
    gom_ref,
    goo_ref,
    g2_ref,
    on_s,
):
    @pl.when(pl.program_id(0) == 0)
    def _():
        acc_s[...] = acc_in_ref[...]
        dh_s[...] = dh_in_ref[...]

    grads = (gm_ref, gu_ref, gdm_ref, gdo_ref)
    ffn_tile(
        core_ref, h_ref, ht_ref, e_ref, wm_ref, wu_ref, wdm_ref, wdo_ref, grads, acc_s, dh_s
    )

    @pl.when(pl.program_id(0) == pl.num_programs(0) - 1)
    def _():
        half = onm_ref.shape[1]
        mine = lanes_of(core_ref[0], half)
        other = lanes_of(1 - core_ref[0], half)
        out_ref[...] = (acc_s[...] * m_ref[...]).astype(low)
        x1 = x1_ref[...]
        scale = lax.rsqrt(jnp.mean(x1 * x1, axis=-1, keepdims=True) + 1e-06)
        normed = x1 * scale
        d_h2 = dh_s[...]
        scaled = d_h2 * g_ref[2:3, :]
        g2_ref[...] = jnp.sum(d_h2 * normed, axis=0, keepdims=True)
        d_x1 = e_ref[...].astype(wide) + scale * (
            scaled - normed * jnp.mean(scaled * normed, axis=-1, keepdims=True)
        )
        dh_s[...] = d_x1
        on_s[...] = d_x1.astype(low)
        acc_s[...] = mm_nt(on_s[:, mine], wom_ref[...]) + mm_nt(on_s[:, other], woo_ref[...])
        onm, ono = onm_ref[...], ono_ref[...]
        d_mine, d_other = on_s[:, mine], on_s[:, other]
        here = pl.ds(pl.multiple_of(core_ref[0] * half, half), half)
        there = pl.ds(pl.multiple_of((1 - core_ref[0]) * half, half), half)
        gom_ref[here, :] = mm_tn(onm, d_mine).astype(low)
        gom_ref[there, :] = mm_tn(ono, d_mine).astype(low)
        goo_ref[here, :] = mm_tn(onm, d_other).astype(low)
        goo_ref[there, :] = mm_tn(ono, d_other).astype(low)


def ffn(core, h2, h2t, errors, w_gu, w_d, start, tile, before, ending=None):
    count, width = h2.shape
    half = width // 2
    hidden = w_gu[0].shape[1]
    full = whole((count, width))
    half_full = whole((count, half))
    square = whole((width, half))
    in_tile = pl.BlockSpec((width, tile), lambda j, _: (0, j))
    out_tile = pl.BlockSpec(
        (pl.Element(tile), pl.Element(half)),
        lambda j, _: (pl.multiple_of(start + j * tile, HEAD_DIM), 0),
    )
    anywhere = pl.BlockSpec(memory_space=pl.ANY)
    out_weights = pl.BlockSpec((width, half), lambda j, _: (0, 3))
    struct = jax.ShapeDtypeStruct
    in_specs = [full, whole(h2t.shape), full, in_tile, in_tile, out_tile, out_tile]
    operands = [core, h2, h2t, errors, *w_gu, *w_d, *before]
    out_specs = [in_tile, in_tile, out_tile, out_tile, full, full]
    out_shape = [struct(w_gu[0].shape, low)] * 2 + [struct(w_d[0].shape, low)] * 2
    aliases = {}
    scratch = []
    kernel = ffn_first_kernel
    if len(before) == 1:
        in_specs += [full]
    else:
        kernel = ffn_middle_kernel
        in_specs += [full, full, anywhere, anywhere]
        aliases = {len(operands) - 2: 2, len(operands) - 1: 3}
    if ending is None:
        out_shape += [struct((count, width), wide)] * 2
    else:
        kernel = ffn_last_kernel
        in_specs += [full, half_full, half_full, out_weights, out_weights]
        in_specs += [whole((count, 1)), whole((8, width))]
        operands += list(ending)
        out_specs += [full, square, square, whole((1, width))]
        out_shape += [
            struct((count, width), low),
            struct((count, width), wide),
            struct((count, width), wide),
            struct((width, half), low),
            struct((width, half), low),
            struct((1, width), wide),
        ]
        scratch = [pltpu.VMEM((count, width), low)]
    return pl.pallas_call(
        kernel,
        grid_spec=pltpu.PrefetchScalarGridSpec(
            num_scalar_prefetch=1,
            grid=(hidden // tile,),
            in_specs=in_specs,
            out_specs=out_specs,
            scratch_shapes=scratch,
        ),
        out_shape=out_shape,
        input_output_aliases=aliases,
        compiler_params=pltpu.CompilerParams(vmem_limit_bytes=VMEM_BYTES),
        cost_estimate=pl.CostEstimate(
            flops=16 * count * width * hidden,
            bytes_accessed=count * width * 20 + width * hidden * 12,
            transcendentals=count * hidden,
        ),
        name="ffn",
    )(*operands)


def mixer_backward_kernel(
    slot,
    pairs,
    last,
    half_ref,
    x_ref,
    w_ref,
    g_ref,
    q_ref,
    f_ref,
    v_ref,
    o_ref,
    don_ref,
    part_ref,
    dx1_ref,
    ggo_in_ref,
    g2_ref,
    grad_ref,
    ggo_ref,
    dx_ref,
    ht_s,
    dh_s,
    pre_s,
):
    step = pl.program_id(0)

    @pl.when(step == 0)
    def _():
        normed, _ = first_norm(x_ref, None)
        ht_s[...] = (normed * g_ref[0:1, :]).T.astype(low)
        dh_s[...] = part_ref[...] if last else jnp.zeros_like(dh_s)

    gain_o = g_ref[1:2, lanes_of(half_ref[0] * pairs + step, PAIR)]
    lower_ones = triangle(slot, True)
    upper_ones = triangle(slot, False)
    block_rows = lax.broadcasted_iota(jnp.int32, (HEAD_DIM, HEAD_DIM), 0)
    block_columns = lax.broadcasted_iota(jnp.int32, (HEAD_DIM, HEAD_DIM), 1)
    causal = block_rows >= block_columns
    causal_t = block_rows <= block_columns
    blocks = slot // HEAD_DIM
    ggo_total = jnp.zeros((1, PAIR), wide)
    for sequence in range(x_ref.shape[0] // slot):
        rows = slice(sequence * slot, (sequence + 1) * slot)
        d_on = don_ref[rows, :]
        out = o_ref[rows, :]
        d_out_parts = []
        ggo_parts = []
        for head in range(2):
            lanes = slice(head * HEAD_DIM, (head + 1) * HEAD_DIM)
            out_h, d_on_h = out[:, lanes], d_on[:, lanes]
            scale = lax.rsqrt(jnp.mean(out_h * out_h, axis=-1, keepdims=True) + 1e-05)
            normed = out_h * scale
            ggo_parts.append(jnp.sum(d_on_h * normed, axis=0, keepdims=True))
            scaled = d_on_h * gain_o[:, lanes]
            inner = jnp.mean(scaled * normed, axis=-1, keepdims=True)
            d_out_parts.append((scale * (scaled - normed * inner)).astype(low))
        ggo_total = ggo_total + jnp.concatenate(ggo_parts, axis=1)

        q_pre = q_ref[rows, :]
        share, gate, keys_in, cumulative = decay_parts(f_ref[rows, :], lower_ones)
        grown = jnp.exp(-cumulative)
        shrunk = jnp.exp(cumulative)
        q_share = sigmoid(q_pre)
        decayed_q = (q_pre * q_share * shrunk).astype(low)
        grown_k = (keys_in * grown).astype(low)
        values = v_ref[rows, :]
        dq_parts, dk_parts, dv_parts = [], [], []
        for head in range(2):
            lanes = slice(head * HEAD_DIM, (head + 1) * HEAD_DIM)
            q_h, k_h, v_h = decayed_q[:, lanes], grown_k[:, lanes], values[:, lanes]
            d_out = d_out_parts[head]
            dq_blocks, dk_blocks, dv_blocks = [], [], []
            for block in range(blocks):
                start, end = block * HEAD_DIM, (block + 1) * HEAD_DIM
                here = slice(start, end)
                d_scores = mm_nt(d_out[here], v_h[here])
                d_scores = jnp.where(causal, d_scores, 0.0).astype(low)
                d_q = mm(d_scores, k_h[here])
                if block > 0:
                    before = slice(0, start)
                    d_scores = mm_nt(d_out[here], v_h[before]).astype(low)
                    d_q = d_q + mm(d_scores, k_h[before])
                dq_blocks.append(d_q)
                scores = jnp.where(causal_t, mm_nt(k_h[here], q_h[here]), 0.0).astype(low)
                d_scores = jnp.where(causal_t, mm_nt(v_h[here], d_out[here]), 0.0).astype(low)
                d_v = mm(scores, d_out[here])
                d_k = mm(d_scores, q_h[here])
                if block < blocks - 1:
                    after = slice(end, slot)
                    scores = mm_nt(k_h[here], q_h[after]).astype(low)
                    d_scores = mm_nt(v_h[here], d_out[after]).astype(low)
                    d_v = d_v + mm(scores, d_out[after])
                    d_k = d_k + mm(d_scores, q_h[after])
                dk_blocks.append(d_k)
                dv_blocks.append(d_v)
            dq_parts.append(jnp.concatenate(dq_blocks, axis=0))
            dk_parts.append(jnp.concatenate(dk_blocks, axis=0))
            dv_parts.append(jnp.concatenate(dv_blocks, axis=0))
        d_decayed = jnp.concatenate(dq_parts, axis=1)
        d_grown = jnp.concatenate(dk_parts, axis=1)
        d_value = jnp.concatenate(dv_parts, axis=1)
        d_cumulative = decayed_q.astype(wide) * d_decayed - grown_k.astype(wide) * d_grown
        d_log = split_sum(upper_ones, d_cumulative)
        d_query = d_decayed * shrunk
        d_key = d_grown * grown
        d_q_pre = d_query * q_share * (1.0 + q_pre * (1.0 - q_share))
        d_f_pre = (1.0 - lower_bound) * (d_log / gate - d_key) * share * (1.0 - share)
        pre_s[rows, :PAIR] = d_q_pre.astype(low)
        pre_s[rows, PAIR : 2 * PAIR] = d_f_pre.astype(low)
        pre_s[rows, 2 * PAIR :] = d_value.astype(low)

    ggo_ref[:, lanes_of(step, PAIR)] = ggo_total
    grad_ref[:, lanes_of(step, 3 * PAIR)] = mm(ht_s[...], pre_s[...]).astype(low)
    dh_s[...] += mm_nt(pre_s[...], w_ref[...])

    @pl.when(step == pairs - 1)
    def _():
        gain_lanes = slice(3 * PAIR * pairs, 3 * PAIR * pairs + HEAD_DIM)
        if not last:
            dx_ref[...] = dh_s[...]
            grad_ref[:, gain_lanes] = jnp.zeros((x_ref.shape[1], HEAD_DIM), low)
            return
        normed, scale = first_norm(x_ref, None)
        d_h1 = dh_s[...]
        scaled = d_h1 * g_ref[0:1, :]
        grad_one = jnp.sum(d_h1 * normed, axis=0, keepdims=True)
        here, there = ggo_ref[...], ggo_in_ref[...]
        first = half_ref[0] == 0
        left = jnp.where(first, here, there)
        right = jnp.where(first, there, here)
        grad_go = jnp.concatenate([left, right], axis=1)
        rows = lax.broadcasted_iota(jnp.int32, (HEAD_DIM, x_ref.shape[1]), 0)
        packed = jnp.where(rows == 0, grad_one, jnp.where(rows == 1, grad_go, g2_ref[...]))
        grad_ref[:, gain_lanes] = jnp.where(rows < 3, packed, 0.0).T.astype(low)
        dx_ref[...] = dx1_ref[...] + scale * (
            scaled - normed * jnp.mean(scaled * normed, axis=-1, keepdims=True)
        )


def mixer_backward_first_kernel(
    slot, pairs, half_ref, x_ref, w_ref, g_ref, q_ref, f_ref, v_ref, o_ref, don_ref, *outs
):
    grad_ref, ggo_ref, dh_ref, ht_s, dh_s, pre_s = outs
    mixer_backward_kernel(
        slot,
        pairs,
        False,
        half_ref,
        x_ref,
        w_ref,
        g_ref,
        q_ref,
        f_ref,
        v_ref,
        o_ref,
        don_ref,
        None,
        None,
        None,
        None,
        grad_ref,
        ggo_ref,
        dh_ref,
        ht_s,
        dh_s,
        pre_s,
    )


def mixer_backward(half, rows, weights, gains8, kept, d_mixed, slot, ending=None):
    count, width = rows.shape
    pairs = width // PAIR // 2
    full = whole((count, width))
    by_pair = pl.BlockSpec((count, PAIR), lambda j, _: (0, j))
    weight_tile = pl.BlockSpec((width, 3 * PAIR), lambda j, _: (0, j))
    struct = jax.ShapeDtypeStruct
    grad_shape = (width, 3 * width // 2 + HEAD_DIM)
    from_half = pl.BlockSpec((count, PAIR), lambda j, half: (0, half[0] * pairs + j))
    in_specs = [full, weight_tile, whole(gains8.shape)] + [by_pair] * 4 + [from_half]
    out_specs = [whole(grad_shape), whole((1, width // 2)), full]
    out_shape = [
        struct(grad_shape, low),
        struct((1, width // 2), wide),
        struct((count, width), wide),
    ]
    kernel = functools.partial(mixer_backward_first_kernel, slot, pairs)
    operands = [half, rows, weights, gains8, *kept, d_mixed]
    if ending is not None:
        kernel = functools.partial(mixer_backward_kernel, slot, pairs, True)
        in_specs += [full, full, whole((1, width // 2)), whole((1, width))]
        operands += list(ending)
    return pl.pallas_call(
        kernel,
        grid_spec=pltpu.PrefetchScalarGridSpec(
            num_scalar_prefetch=1,
            grid=(pairs,),
            in_specs=in_specs,
            out_specs=out_specs,
            scratch_shapes=[
                pltpu.VMEM((width, count), low),
                pltpu.VMEM((count, width), wide),
                pltpu.VMEM((count, 3 * PAIR), low),
            ],
        ),
        out_shape=out_shape,
        compiler_params=pltpu.CompilerParams(vmem_limit_bytes=VMEM_BYTES),
        cost_estimate=pl.CostEstimate(
            flops=2 * count * width * 3 * width + 20 * count * slot * width,
            bytes_accessed=count * width * 17 + width * width * 6,
            transcendentals=count * width * 4,
        ),
        name="mixer_backward",
    )(*operands)


def update(weight, momentum, average, gradient, step_rate):
    new_momentum = momentum_decay * momentum + gradient
    direction = gradient + momentum_decay * new_momentum + weight_decay * weight
    new_weight = weight - step_rate * direction
    new_average = average_decay * average + (1.0 - average_decay) * new_weight
    return (new_momentum, new_average, new_weight)


def update_kernel(pick, step_rate, core_ref, w_ref, m_ref, a_ref, *refs):
    sums, outs = refs[:-3], refs[-3:]
    gradient = pick(core_ref[0], *[s[...] for s in sums]).astype(wide).reshape(w_ref.shape)
    results = update(w_ref[...], m_ref[...], a_ref[...], gradient, step_rate)
    for out, result in zip(outs, results):
        out[...] = result


def update_call(core, state, sums, grid, state_spec, sum_specs, pick, step_rate, name):
    struct = jax.ShapeDtypeStruct(state[0].shape, wide)
    size = math.prod(state[0].shape)
    return pl.pallas_call(
        functools.partial(update_kernel, pick, step_rate),
        grid_spec=pltpu.PrefetchScalarGridSpec(
            num_scalar_prefetch=1,
            grid=grid,
            in_specs=[state_spec] * 3 + sum_specs,
            out_specs=[state_spec] * 3,
        ),
        out_shape=[struct] * 3,
        compiler_params=pltpu.CompilerParams(vmem_limit_bytes=VMEM_BYTES),
        cost_estimate=pl.CostEstimate(flops=10 * size, bytes_accessed=26 * size, transcendentals=0),
        name=name,
    )(core, *state, *sums)


def update_attention(core, state, qfv, out, step_rate):
    _, shard, width = state[0].shape

    def pick(core_index, qfv_mine, qfv_other, out_mine, out_other):
        own = pl.program_id(1) // 2 == core_index
        proj = jnp.where(own, qfv_mine.astype(wide), qfv_other.astype(wide))
        last = jnp.where(own, out_mine.astype(wide), out_other.astype(wide))
        return jnp.where(pl.program_id(0) < 3, proj, last)

    proj_spec = pl.BlockSpec(
        (shard, PAIR), lambda kind, pair, _: (0, (pair % 2) * 3 + jnp.minimum(kind, 2))
    )
    out_spec = pl.BlockSpec((shard, PAIR), lambda kind, pair, _: (0, pair % 2))
    return update_call(
        core,
        state,
        (*qfv, *out),
        (4, width // PAIR),
        pl.BlockSpec((1, shard, PAIR), lambda kind, pair, _: (kind, 0, pair)),
        [proj_spec, proj_spec, out_spec, out_spec],
        pick,
        step_rate,
        "update_attention",
    )


def update_ffn_in(core, state, sums, step_rate):
    _, shard, hidden = state[0].shape

    def pick(core_index, *totals):
        own = pl.program_id(0) == core_index
        parts = [
            jnp.where(own, mine.astype(wide), other.astype(wide))
            for mine, other in zip(totals[::2], totals[1::2])
        ]
        return jnp.concatenate(parts, axis=1)

    flat = [total for pair in sums for total in pair]
    return update_call(
        core,
        state,
        flat,
        (2,),
        pl.BlockSpec((1, shard, hidden), lambda kind, _: (kind, 0, 0)),
        [whole(total.shape) for total in flat],
        pick,
        step_rate,
        "update_ffn_in",
    )


def update_ffn_out(core, state, sums, step_rate):
    shard, width = state[0].shape

    def pick(core_index, mine, other):
        own = pl.program_id(0) // 2 == core_index
        return jnp.where(own, mine.astype(wide), other.astype(wide))

    sum_spec = pl.BlockSpec((shard, PAIR), lambda j, _: (0, j % 2))
    return update_call(
        core,
        state,
        sums,
        (width // PAIR,),
        pl.BlockSpec((shard, PAIR), lambda j, _: (0, j)),
        [sum_spec, sum_spec],
        pick,
        step_rate,
        "update_ffn_out",
    )


def pack_kernel(core_ref, w_ref, g_ref, out_ref):
    pairs = w_ref.shape[2] // PAIR
    for pair in range(pairs):
        for kind in range(3):
            start = (pair * 3 + kind) * PAIR
            piece = w_ref[kind, :, pair * PAIR : (pair + 1) * PAIR]
            out_ref[:, start : start + PAIR] = piece.astype(low)
    start = 3 * pairs * PAIR
    out_ref[:, start : start + pairs * PAIR] = w_ref[3].astype(low)
    start += pairs * PAIR
    out_ref[:, start:] = g_ref[...].astype(low)


def pack_attention(core, weights, gains):
    _, shard, width = weights.shape
    half = width // 2
    gain_columns = jnp.pad(gains.T, ((0, 0), (0, HEAD_DIM - 3)))
    columns = 4 * half + HEAD_DIM
    return pl.pallas_call(
        pack_kernel,
        grid_spec=pltpu.PrefetchScalarGridSpec(
            num_scalar_prefetch=1,
            grid=(1,),
            in_specs=[
                pl.BlockSpec((4, shard, half), lambda j, core: (0, 0, core[0])),
                whole((shard, HEAD_DIM)),
            ],
            out_specs=whole((shard, columns)),
        ),
        out_shape=jax.ShapeDtypeStruct((shard, columns), low),
        name="pack_attention",
    )(core, weights, gain_columns)


RING = 8


def ring_place(index):
    return jnp.where(index % 2 == 0, index // 2, RING - 1 - index // 2)


def ring_member(place):
    place = place % RING
    return jnp.where(place < RING // 2, 2 * place, 2 * RING - 1 - 2 * place)


def ring_next(tensor):
    cycle = [0, 2, 4, 6, 7, 5, 3, 1]
    replicas = lax.axis_size("dp")
    pairs = []
    for place, member in enumerate(cycle):
        for replica in range(replicas):
            target = cycle[(place + (1 if replica % 2 == 0 else -1)) % RING]
            pairs.append((member * replicas + replica, target * replicas + replica))
    return lax.ppermute(tensor, ("fsdp", "dp"), pairs)


def core_swap(tensor):
    return lax.ppermute(tensor, "dp", [(d, d ^ 1) for d in range(lax.axis_size("dp"))])


def column_swap(tensor):
    return lax.ppermute(tensor, "dp", [(d, d ^ 2) for d in range(lax.axis_size("dp"))])


def assemble_kernel(origin_ref, *refs):
    pieces, out_ref, semaphores = refs[:RING], refs[RING], refs[RING + 1]
    rows = pieces[0].shape[0]
    copies = []
    for step, piece in enumerate(pieces):
        start = pl.multiple_of(origin_ref[step] * rows, 16)
        copies.append(
            pltpu.make_async_copy(piece, out_ref.at[pl.ds(start, rows), :], semaphores.at[step])
        )
    for copy in copies:
        copy.start()
    for copy in copies:
        copy.wait()


def assemble(origins, pieces):
    rows, columns = pieces[0].shape
    anywhere = pl.BlockSpec(memory_space=pl.ANY)
    return pl.pallas_call(
        assemble_kernel,
        grid_spec=pltpu.PrefetchScalarGridSpec(
            num_scalar_prefetch=1,
            grid=(1,),
            in_specs=[anywhere] * RING,
            out_specs=anywhere,
            scratch_shapes=[pltpu.SemaphoreType.DMA((RING,))],
        ),
        out_shape=jax.ShapeDtypeStruct((RING * rows, columns), pieces[0].dtype),
        cost_estimate=pl.CostEstimate(
            flops=0, bytes_accessed=4 * RING * rows * columns, transcendentals=0
        ),
        name="assemble",
    )(origins, *pieces)


def after(tensor, *others):
    return lax.optimization_barrier((tensor, *others))[0]


def gather_rows(shard):
    return lax.all_gather(shard, "fsdp", axis=0, tiled=True)


def ring_gather_rows(first, second):
    if lax.axis_size("fsdp") != RING:
        return gather_rows(first), gather_rows(second)
    place = ring_place(lax.axis_index("fsdp"))
    way = 1 - 2 * (lax.axis_index("dp") % 2)
    origins = ring_member(place - way * jnp.arange(RING, dtype=jnp.int32) + RING).astype(jnp.int32)
    firsts, seconds = [first], [second]
    for step in range(1, RING):
        source = firsts[-1] if step == 1 else after(firsts[-1], seconds[-2])
        firsts.append(ring_next(source))
        source = seconds[-1] if step == 1 else after(seconds[-1], firsts[-2])
        seconds.append(ring_next(source))
    return assemble(origins, firsts), assemble(origins, seconds)


def core_sum(mine, other):
    return (mine.astype(wide) + core_swap(other).astype(wide)).astype(low)


def reduce_rows(both):
    total = lax.psum_scatter(both, "fsdp", scatter_dimension=0, tiled=True)
    total = (total.astype(wide) + column_swap(total).astype(wide)).astype(low)
    return total, core_swap(total)


def on_device(
    inputs,
    cotangent,
    lengths,
    attention_weights,
    attention_momentum,
    attention_average,
    ffn_inputs,
    ffn_inputs_momentum,
    ffn_inputs_average,
    ffn_output,
    ffn_output_momentum,
    ffn_output_average,
    gains,
    gains_momentum,
    gains_average,
):
    micro_count, slot, width = inputs.shape
    hidden = ffn_inputs.shape[2]
    fsdp_size = lax.axis_size("fsdp")
    replicas = lax.axis_size("dp")
    core = lax.axis_index("dp") % 2
    count = micro_count * slot
    half = width // 2
    core_ref = core.astype(jnp.int32).reshape(1)
    other_ref = 1 - core_ref
    cuts = [(0, 1024, 512), (1024, 1024, 512), (2048, hidden - 2048, 384)]

    up_half = lax.dynamic_index_in_dim(ffn_inputs, core, 0, keepdims=False).astype(low)
    up_parts = [up_half[:, start : start + size] for start, size, _ in cuts]
    packed = pack_attention(core_ref, attention_weights, gains)
    down_half = lax.dynamic_slice_in_dim(ffn_output, core * half, half, 1).astype(low)
    packed = after(packed, *up_parts, down_half)
    w_up = [gather_rows(part) for part in up_parts]
    w_a_mine, w_d_mine = ring_gather_rows(packed, down_half)
    w_a = (w_a_mine, core_swap(w_a_mine))
    w_d = (w_d_mine, core_swap(w_d_mine))
    gain_rows = w_a_mine[:, 4 * half : 4 * half + 3].T.astype(wide)
    gains8 = jnp.pad(gain_rows, ((0, 5), (0, 0)))

    rows = inputs.reshape(count, width)
    positions = jnp.arange(slot, dtype=jnp.int32)
    valid = (positions[None, :] < lengths).astype(wide).reshape(count, 1)
    errors = (cotangent.reshape(count, width).astype(wide) * valid).astype(low)

    mixed_mine, *kept_mine = mixer_forward(core_ref, rows, w_a[0], gains8, slot)
    mixed_other, *rest = mixer_forward(
        other_ref, rows, w_a[1], gains8, slot, (mixed_mine, w_a[0])
    )
    kept_other, (x1, h2, h2t) = rest[:4], rest[4:]
    w_gu = [(part, core_swap(part)) for part in w_up]
    state = (x1,)
    sums = []
    for which, (start, size, tile) in enumerate(cuts):
        ending = None
        if which == len(cuts) - 1:
            ending = (x1, mixed_mine, mixed_other, *w_a, valid, gains8)
        if which == 2:
            state = (after(state[0], sums[0]), *state[1:])
        gm, gu, gd_mine, gd_other, *rest = ffn(
            core_ref, h2, h2t, errors, w_gu[which], w_d, start, tile, state, ending
        )
        state = (*rest[:2], gd_mine, gd_other)
        sums.append(core_sum(gm, gu))
    output, d_x1, d_mixed, go_mine, go_other, grad_two = rest
    sums.append(core_sum(gd_mine, gd_other))
    sums.append(core_sum(go_mine, go_other))
    gqfv_other, ggo_other, d_h1 = mixer_backward(
        other_ref, after(rows, sums[1]), w_a[1], gains8, kept_other, d_mixed, slot
    )
    gqfv_mine, _, input_grad = mixer_backward(
        core_ref,
        after(rows, *sums),
        w_a[0],
        gains8,
        kept_mine,
        d_mixed,
        slot,
        (d_h1, d_x1, ggo_other, grad_two),
    )
    sums.append(core_sum(gqfv_mine, gqfv_other))
    totals = [reduce_rows(both) for both in sums]
    sum_gu, (sum_d, sum_o, sum_qfv) = totals[:3], totals[3:]
    gain_sums = [total[:, 3 * half : 3 * half + 3].T.astype(wide) for total in sum_qfv]
    sum_gains = gain_sums[0] + gain_sums[1]

    scale_rows = 1.0 / math.sqrt(count * fsdp_size * replicas)
    attention_state = (attention_weights, attention_momentum, attention_average)
    ffn_in_state = (ffn_inputs, ffn_inputs_momentum, ffn_inputs_average)
    ffn_out_state = (ffn_output, ffn_output_momentum, ffn_output_average)
    return (
        output.reshape(micro_count, slot, width),
        input_grad.reshape(micro_count, slot, width),
        *update_attention(core_ref, attention_state, sum_qfv, sum_o, matrix_rate * scale_rows),
        *update_ffn_in(core_ref, ffn_in_state, sum_gu, matrix_rate * scale_rows),
        *update_ffn_out(core_ref, ffn_out_state, sum_d, matrix_rate * scale_rows),
        *update(gains, gains_momentum, gains_average, sum_gains, gain_rate * scale_rows),
    )


def solution(mesh):
    rows_split = P(None, ("fsdp", "dp"), None)
    middle_split = P(None, "fsdp", None)
    first_split = P("fsdp", None)
    gains_split = P(None, "fsdp")
    in_specs = (
        (rows_split, rows_split, P(None, ("fsdp", "dp")))
        + (middle_split,) * 6
        + (first_split,) * 3
        + (gains_split,) * 3
    )
    out_specs = (
        (rows_split, rows_split)
        + (middle_split,) * 6
        + (first_split,) * 3
        + (gains_split,) * 3
    )
    return jax.shard_map(
        on_device, mesh=mesh, in_specs=in_specs, out_specs=out_specs, check_vma=False
    )
```

```python
import functools
import math

import jax
import jax.numpy as jnp
from jax import lax
from jax.experimental import pallas as pl
from jax.experimental.pallas import tpu as pltpu
from jax.sharding import PartitionSpec as P

HEAD_DIM = 128
PAIR = 2 * HEAD_DIM

lower_bound = 0.9
momentum_decay = 0.9
average_decay = 0.7
weight_decay = 0.0005
matrix_rate = 0.03
gain_rate = 0.1
low = jnp.bfloat16
wide = jnp.float32
TILE_F = 256
VMEM_BYTES = 60 * 1024 * 1024


def mm(left, right):
    return jnp.dot(left, right, preferred_element_type=wide)


def mm_nt(left, right):
    return lax.dot_general(left, right, (((1,), (1,)), ((), ())), preferred_element_type=wide)


def mm_tn(left, right):
    return lax.dot_general(left, right, (((0,), (0,)), ((), ())), preferred_element_type=wide)


def sigmoid(u):
    return 1.0 / (1.0 + jnp.exp(-u))


def whole(shape):
    return pl.BlockSpec(shape, lambda *_: (0,) * len(shape), pipeline_mode=pl.Buffered(1))


def split_sum(ones_matrix, tensor):
    high = tensor.astype(low)
    rest = (tensor - high.astype(wide)).astype(low)
    return mm(ones_matrix, high) + mm(ones_matrix, rest)


def triangle(length, lower):
    rows = lax.broadcasted_iota(jnp.int32, (length, length), 0)
    columns = lax.broadcasted_iota(jnp.int32, (length, length), 1)
    kept = rows >= columns if lower else rows <= columns
    return kept.astype(wide).astype(low)


def decay_parts(f_pre, lower_ones):
    share = sigmoid(f_pre)
    gate = lower_bound + (1.0 - lower_bound) * share
    keys_in = (1.0 - lower_bound) * (1.0 - share)
    cumulative = split_sum(lower_ones, jnp.log(gate))
    middle_row = cumulative.shape[0] // 2
    cumulative = cumulative - cumulative[middle_row : middle_row + 1, :]
    return share, gate, keys_in, cumulative


def first_norm(x_ref, gain_row):
    rows = x_ref[...].astype(wide)
    scale = lax.rsqrt(jnp.mean(rows * rows, axis=-1, keepdims=True) + 1e-06)
    return rows * scale, scale


def lanes_of(half, size):
    return pl.ds(pl.multiple_of(half * size, size), size)


def mixer_forward_kernel(
    slot, half_ref, x_ref, w_ref, g_ref, on_ref, q_ref, f_ref, v_ref, o_ref, h_s
):
    @pl.when(pl.program_id(0) == 0)
    def _():
        normed, _ = first_norm(x_ref, None)
        h_s[...] = (normed * g_ref[0:1, :]).astype(low)

    gain_o = g_ref[1:2, lanes_of(half_ref[0] * pl.num_programs(0) + pl.program_id(0), PAIR)]
    pre = mm(h_s[...], w_ref[...])
    q_ref[...] = pre[:, :PAIR]
    f_ref[...] = pre[:, PAIR : 2 * PAIR]
    v_ref[...] = pre[:, 2 * PAIR :].astype(low)
    lower_ones = triangle(slot, True)
    block_rows = lax.broadcasted_iota(jnp.int32, (HEAD_DIM, HEAD_DIM), 0)
    block_columns = lax.broadcasted_iota(jnp.int32, (HEAD_DIM, HEAD_DIM), 1)
    causal = block_rows >= block_columns
    for sequence in range(x_ref.shape[0] // slot):
        rows = slice(sequence * slot, (sequence + 1) * slot)
        q_pre = q_ref[rows, :]
        _, _, keys_in, cumulative = decay_parts(f_ref[rows, :], lower_ones)
        grown = jnp.exp(-cumulative)
        decayed_q = (q_pre * sigmoid(q_pre) * jnp.exp(cumulative)).astype(low)
        grown_k = (keys_in * grown).astype(low)
        values = v_ref[rows, :]
        for head in range(2):
            lanes = slice(head * HEAD_DIM, (head + 1) * HEAD_DIM)
            for block in range(slot // HEAD_DIM):
                start, end = block * HEAD_DIM, (block + 1) * HEAD_DIM
                q_block = decayed_q[start:end, lanes]
                diagonal = mm_nt(q_block, grown_k[start:end, lanes])
                diagonal = jnp.where(causal, diagonal, 0.0).astype(low)
                out = mm(diagonal, values[start:end, lanes])
                if block > 0:
                    scores = mm_nt(q_block, grown_k[:start, lanes]).astype(low)
                    out = out + mm(scores, values[:start, lanes])
                scale = lax.rsqrt(jnp.mean(out * out, axis=-1, keepdims=True) + 1e-05)
                target = slice(sequence * slot + start, sequence * slot + end)
                o_ref[target, lanes] = out
                on_ref[target, lanes] = (out * scale * gain_o[:, lanes]).astype(low)


def mixer_forward_last_kernel(
    slot,
    half_ref,
    x_ref,
    w_ref,
    g_ref,
    before_ref,
    woo_ref,
    wom_ref,
    on_ref,
    q_ref,
    f_ref,
    v_ref,
    o_ref,
    x1_ref,
    h2_ref,
    h2t_ref,
    h1t_ref,
    h_s,
    on_s,
):
    step = pl.program_id(0)
    half = before_ref.shape[1]
    mixer_forward_kernel(
        slot, half_ref, x_ref, w_ref, g_ref, on_ref, q_ref, f_ref, v_ref, o_ref, h_s
    )
    on_s[:, lanes_of(half_ref[0] * pl.num_programs(0) + step, PAIR)] = on_ref[...]

    @pl.when(step == pl.num_programs(0) - 1)
    def _():
        here = lanes_of(half_ref[0], half)
        there = lanes_of(1 - half_ref[0], half)
        on_s[:, there] = before_ref[...]
        h1t_ref[...] = h_s[...].astype(wide).T.astype(low)
        x1_ref[:, here] = x_ref[:, here].astype(wide) + mm(on_s[...], woo_ref[...])
        x1_ref[:, there] = x_ref[:, there].astype(wide) + mm(on_s[...], wom_ref[...])
        x1 = x1_ref[...]
        scale = lax.rsqrt(jnp.mean(x1 * x1, axis=-1, keepdims=True) + 1e-06)
        normed = x1 * scale * g_ref[2:3, :]
        h2_ref[...] = normed.astype(low)
        h2t_ref[...] = normed.T.astype(low)


def mixer_forward(half, rows, weights, gains8, slot, ending=None):
    count, width = rows.shape
    pairs = width // PAIR // 2
    by_pair = pl.BlockSpec((count, PAIR), lambda j, _: (0, j))
    struct = jax.ShapeDtypeStruct
    shape = lambda kind: struct((count, width // 2), kind)
    kernel = mixer_forward_kernel
    in_specs = [
        whole(rows.shape),
        pl.BlockSpec((width, 3 * PAIR), lambda j, _: (0, j)),
        whole(gains8.shape),
    ]
    operands = [half, rows, weights, gains8]
    out_specs = [by_pair] * 5
    out_shape = [shape(low), shape(wide), shape(wide), shape(low), shape(wide)]
    scratch = [pltpu.VMEM((count, width), low)]
    if ending is not None:
        kernel = mixer_forward_last_kernel
        out_weights = pl.BlockSpec((width, width // 2), lambda j, _: (0, 3))
        in_specs += [whole((count, width // 2)), out_weights, out_weights]
        operands += [ending[0], weights, ending[1]]
        out_specs += [whole((count, width))] * 2 + [whole((width, count))] * 2
        out_shape += [
            struct((count, width), wide),
            struct((count, width), low),
            struct((width, count), low),
            struct((width, count), low),
        ]
        scratch += [pltpu.VMEM((count, width), low)]
    return pl.pallas_call(
        functools.partial(kernel, slot),
        grid_spec=pltpu.PrefetchScalarGridSpec(
            num_scalar_prefetch=1,
            grid=(pairs,),
            in_specs=in_specs,
            out_specs=out_specs,
            scratch_shapes=scratch,
        ),
        out_shape=out_shape,
        compiler_params=pltpu.CompilerParams(vmem_limit_bytes=VMEM_BYTES),
        cost_estimate=pl.CostEstimate(
            flops=count * width * 4 * width + 10 * count * slot * width,
            bytes_accessed=count * width * 12 + width * width * 4,
            transcendentals=count * width * 3,
        ),
        name="mixer_forward",
    )(*operands)


def ffn_tile(
    core_ref, h_ref, ht_ref, e_ref, wm_ref, wu_ref, wdm_ref, wdo_ref, grads, acc_ref, dh_ref
):
    gm_ref, gu_ref, gdm_ref, gdo_ref = grads
    half = wdm_ref.shape[1]
    first = core_ref[0] == 0
    mine = lanes_of(core_ref[0], half)
    other = lanes_of(1 - core_ref[0], half)
    own = mm(h_ref[...], wm_ref[...])
    swapped = mm(h_ref[...], wu_ref[...])
    a = jnp.where(first, own, swapped)
    b = jnp.where(first, swapped, own)
    share = sigmoid(a)
    swish = a * share
    mid = (swish * b).astype(low)
    acc_ref[:, mine] += mm(mid, wdm_ref[...])
    acc_ref[:, other] += mm(mid, wdo_ref[...])
    d_mid = mm_nt(e_ref[:, mine], wdm_ref[...]) + mm_nt(e_ref[:, other], wdo_ref[...])
    gdm_ref[...] = mm_tn(mid, e_ref[:, mine]).astype(low)
    gdo_ref[...] = mm_tn(mid, e_ref[:, other]).astype(low)
    d_a = (d_mid * b * share * (1.0 + a * (1.0 - share))).astype(low)
    d_b = (d_mid * swish).astype(low)
    d_own = jnp.where(first, d_a, d_b)
    d_swapped = jnp.where(first, d_b, d_a)
    gm_ref[...] = mm(ht_ref[...], d_own).astype(low)
    gu_ref[...] = mm(ht_ref[...], d_swapped).astype(low)
    dh_ref[...] += mm_nt(d_own, wm_ref[...]) + mm_nt(d_swapped, wu_ref[...])


def ffn_kernel(
    core_ref,
    h_ref,
    ht_ref,
    e_ref,
    wm_ref,
    wu_ref,
    wdm_ref,
    wdo_ref,
    x1_ref,
    onm_ref,
    ono_ref,
    wom_ref,
    woo_ref,
    m_ref,
    g_ref,
    gm_ref,
    gu_ref,
    gdm_ref,
    gdo_ref,
    out_ref,
    dh_s,
    acc_s,
    gom_ref,
    goo_ref,
    g2_ref,
    on_s,
):
    @pl.when(pl.program_id(0) == 0)
    def _():
        acc_s[...] = x1_ref[...]
        dh_s[...] = jnp.zeros_like(dh_s)

    grads = (gm_ref, gu_ref, gdm_ref, gdo_ref)
    ffn_tile(
        core_ref, h_ref, ht_ref, e_ref, wm_ref, wu_ref, wdm_ref, wdo_ref, grads, acc_s, dh_s
    )

    @pl.when(pl.program_id(0) == pl.num_programs(0) - 1)
    def _():
        half = onm_ref.shape[1]
        mine = lanes_of(core_ref[0], half)
        other = lanes_of(1 - core_ref[0], half)
        out_ref[...] = (acc_s[...] * m_ref[...]).astype(low)
        x1 = x1_ref[...]
        scale = lax.rsqrt(jnp.mean(x1 * x1, axis=-1, keepdims=True) + 1e-06)
        normed = x1 * scale
        d_h2 = dh_s[...]
        scaled = d_h2 * g_ref[2:3, :]
        g2_ref[...] = jnp.sum(d_h2 * normed, axis=0, keepdims=True)
        d_x1 = e_ref[...].astype(wide) + scale * (
            scaled - normed * jnp.mean(scaled * normed, axis=-1, keepdims=True)
        )
        dh_s[...] = d_x1
        on_s[...] = d_x1.astype(low)
        acc_s[...] = mm_nt(on_s[:, mine], wom_ref[...]) + mm_nt(on_s[:, other], woo_ref[...])
        onm, ono = onm_ref[...], ono_ref[...]
        d_mine, d_other = on_s[:, mine], on_s[:, other]
        here = pl.ds(pl.multiple_of(core_ref[0] * half, half), half)
        there = pl.ds(pl.multiple_of((1 - core_ref[0]) * half, half), half)
        gom_ref[here, :] = mm_tn(onm, d_mine).astype(low)
        gom_ref[there, :] = mm_tn(ono, d_mine).astype(low)
        goo_ref[here, :] = mm_tn(onm, d_other).astype(low)
        goo_ref[there, :] = mm_tn(ono, d_other).astype(low)


def ffn(core, h2, h2t, errors, w_gu, w_d, x1, mixed, w_a, mask, gains8):
    count, width = h2.shape
    half = width // 2
    hidden = w_gu[0].shape[1]
    full = whole((count, width))
    half_full = whole((count, half))
    square = whole((width, half))
    in_tile = pl.BlockSpec((width, TILE_F), lambda j, _: (0, j))
    out_tile = pl.BlockSpec((TILE_F, half), lambda j, _: (j, 0))
    out_weights = pl.BlockSpec((width, half), lambda j, _: (0, 3), pipeline_mode=pl.Buffered(1))
    struct = jax.ShapeDtypeStruct
    return pl.pallas_call(
        ffn_kernel,
        grid_spec=pltpu.PrefetchScalarGridSpec(
            num_scalar_prefetch=1,
            grid=(hidden // TILE_F,),
            in_specs=[full, whole(h2t.shape), full, in_tile, in_tile, out_tile, out_tile]
            + [full, half_full, half_full, out_weights, out_weights]
            + [whole((count, 1)), whole((8, width))],
            out_specs=[in_tile, in_tile, out_tile, out_tile]
            + [full, full, full, square, square, whole((1, width))],
            scratch_shapes=[pltpu.VMEM((count, width), low)],
        ),
        out_shape=[struct((width, hidden), low)] * 2
        + [struct((hidden, half), low)] * 2
        + [
            struct((count, width), low),
            struct((count, width), wide),
            struct((count, width), wide),
            struct((width, half), low),
            struct((width, half), low),
            struct((1, width), wide),
        ],
        compiler_params=pltpu.CompilerParams(vmem_limit_bytes=VMEM_BYTES),
        cost_estimate=pl.CostEstimate(
            flops=16 * count * width * hidden,
            bytes_accessed=count * width * 20 + width * hidden * 12,
            transcendentals=count * hidden,
        ),
        name="ffn",
    )(core, h2, h2t, errors, *w_gu, *w_d, x1, *mixed, *w_a, mask, gains8)


def mixer_backward_kernel(
    slot,
    half_ref,
    ht_ref,
    g_ref,
    q_ref,
    f_ref,
    v_ref,
    o_ref,
    don_ref,
    grad_ref,
    ggo_ref,
    dpre_ref,
):
    gain_o = g_ref[1:2, lanes_of(half_ref[0] * pl.num_programs(0) + pl.program_id(0), PAIR)]
    lower_ones = triangle(slot, True)
    upper_ones = triangle(slot, False)
    block_rows = lax.broadcasted_iota(jnp.int32, (HEAD_DIM, HEAD_DIM), 0)
    block_columns = lax.broadcasted_iota(jnp.int32, (HEAD_DIM, HEAD_DIM), 1)
    causal = block_rows >= block_columns
    causal_t = block_rows <= block_columns
    blocks = slot // HEAD_DIM
    ggo_total = jnp.zeros((1, PAIR), wide)
    for sequence in range(q_ref.shape[0] // slot):
        rows = slice(sequence * slot, (sequence + 1) * slot)
        d_on = don_ref[rows, :]
        out = o_ref[rows, :]
        d_out_parts = []
        ggo_parts = []
        for head in range(2):
            lanes = slice(head * HEAD_DIM, (head + 1) * HEAD_DIM)
            out_h, d_on_h = out[:, lanes], d_on[:, lanes]
            scale = lax.rsqrt(jnp.mean(out_h * out_h, axis=-1, keepdims=True) + 1e-05)
            normed = out_h * scale
            ggo_parts.append(jnp.sum(d_on_h * normed, axis=0, keepdims=True))
            scaled = d_on_h * gain_o[:, lanes]
            inner = jnp.mean(scaled * normed, axis=-1, keepdims=True)
            d_out_parts.append((scale * (scaled - normed * inner)).astype(low))
        ggo_total = ggo_total + jnp.concatenate(ggo_parts, axis=1)

        q_pre = q_ref[rows, :]
        share, gate, keys_in, cumulative = decay_parts(f_ref[rows, :], lower_ones)
        grown = jnp.exp(-cumulative)
        shrunk = jnp.exp(cumulative)
        q_share = sigmoid(q_pre)
        decayed_q = (q_pre * q_share * shrunk).astype(low)
        grown_k = (keys_in * grown).astype(low)
        values = v_ref[rows, :]
        dq_parts, dk_parts, dv_parts = [], [], []
        for head in range(2):
            lanes = slice(head * HEAD_DIM, (head + 1) * HEAD_DIM)
            q_h, k_h, v_h = decayed_q[:, lanes], grown_k[:, lanes], values[:, lanes]
            d_out = d_out_parts[head]
            dq_blocks, dk_blocks, dv_blocks = [], [], []
            for block in range(blocks):
                start, end = block * HEAD_DIM, (block + 1) * HEAD_DIM
                here = slice(start, end)
                d_scores = mm_nt(d_out[here], v_h[here])
                d_scores = jnp.where(causal, d_scores, 0.0).astype(low)
                d_q = mm(d_scores, k_h[here])
                if block > 0:
                    before = slice(0, start)
                    d_scores = mm_nt(d_out[here], v_h[before]).astype(low)
                    d_q = d_q + mm(d_scores, k_h[before])
                dq_blocks.append(d_q)
                scores = jnp.where(causal_t, mm_nt(k_h[here], q_h[here]), 0.0).astype(low)
                d_scores = jnp.where(causal_t, mm_nt(v_h[here], d_out[here]), 0.0).astype(low)
                d_v = mm(scores, d_out[here])
                d_k = mm(d_scores, q_h[here])
                if block < blocks - 1:
                    after = slice(end, slot)
                    scores = mm_nt(k_h[here], q_h[after]).astype(low)
                    d_scores = mm_nt(v_h[here], d_out[after]).astype(low)
                    d_v = d_v + mm(scores, d_out[after])
                    d_k = d_k + mm(d_scores, q_h[after])
                dk_blocks.append(d_k)
                dv_blocks.append(d_v)
            dq_parts.append(jnp.concatenate(dq_blocks, axis=0))
            dk_parts.append(jnp.concatenate(dk_blocks, axis=0))
            dv_parts.append(jnp.concatenate(dv_blocks, axis=0))
        d_decayed = jnp.concatenate(dq_parts, axis=1)
        d_grown = jnp.concatenate(dk_parts, axis=1)
        d_value = jnp.concatenate(dv_parts, axis=1)
        d_cumulative = decayed_q.astype(wide) * d_decayed - grown_k.astype(wide) * d_grown
        d_log = split_sum(upper_ones, d_cumulative)
        d_query = d_decayed * shrunk
        d_key = d_grown * grown
        d_q_pre = d_query * q_share * (1.0 + q_pre * (1.0 - q_share))
        d_f_pre = (1.0 - lower_bound) * (d_log / gate - d_key) * share * (1.0 - share)
        dpre_ref[rows, :PAIR] = d_q_pre.astype(low)
        dpre_ref[rows, PAIR : 2 * PAIR] = d_f_pre.astype(low)
        dpre_ref[rows, 2 * PAIR :] = d_value.astype(low)

    ggo_ref[...] = ggo_total
    grad_ref[...] = mm(ht_ref[...], dpre_ref[...]).astype(low)


def mixer_backward(half, h1t, gains8, kept, d_mixed, slot):
    width, count = h1t.shape
    pairs = width // PAIR // 2
    by_pair = pl.BlockSpec((count, PAIR), lambda j, _: (0, j))
    from_half = pl.BlockSpec((count, PAIR), lambda j, half: (0, half[0] * pairs + j))
    struct = jax.ShapeDtypeStruct
    return pl.pallas_call(
        functools.partial(mixer_backward_kernel, slot),
        grid_spec=pltpu.PrefetchScalarGridSpec(
            num_scalar_prefetch=1,
            grid=(pairs,),
            in_specs=[whole((width, count)), whole(gains8.shape)] + [by_pair] * 4 + [from_half],
            out_specs=[
                pl.BlockSpec((width, 3 * PAIR), lambda j, _: (0, j)),
                pl.BlockSpec((1, PAIR), lambda j, _: (0, j)),
                pl.BlockSpec((count, 3 * PAIR), lambda j, _: (0, j)),
            ],
        ),
        out_shape=[
            struct((width, 3 * width // 2), low),
            struct((1, width // 2), wide),
            struct((count, 3 * width // 2), low),
        ],
        compiler_params=pltpu.CompilerParams(vmem_limit_bytes=VMEM_BYTES),
        cost_estimate=pl.CostEstimate(
            flops=count * width * 3 * width + 20 * count * slot * width,
            bytes_accessed=count * width * 12 + width * width * 3,
            transcendentals=count * width * 4,
        ),
        name="mixer_backward",
    )(half, h1t, gains8, *kept, d_mixed)


def input_gradient_kernel(x_ref, g_ref, dm_ref, do_ref, wm_ref, wo_ref, dx1_ref, dx_ref, g1_ref, dh_s):
    step = pl.program_id(0)
    pairs = pl.num_programs(0) // 2

    @pl.when(step == 0)
    def _():
        dh_s[...] = mm_nt(do_ref[...], wo_ref[...])

    @pl.when(jnp.logical_and(step > 0, step < pairs))
    def _():
        dh_s[...] += mm_nt(do_ref[...], wo_ref[...])

    @pl.when(step >= pairs)
    def _():
        dh_s[...] += mm_nt(dm_ref[...], wm_ref[...])

    @pl.when(step == 2 * pairs - 1)
    def _():
        normed, scale = first_norm(x_ref, None)
        d_h1 = dh_s[...]
        scaled = d_h1 * g_ref[0:1, :]
        g1_ref[...] = jnp.sum(d_h1 * normed, axis=0, keepdims=True)
        dx_ref[...] = dx1_ref[...] + scale * (
            scaled - normed * jnp.mean(scaled * normed, axis=-1, keepdims=True)
        )


def input_gradient(rows, gains8, d_pre, weights, d_x1):
    count, width = rows.shape
    pairs = width // PAIR // 2
    full = whole((count, width))
    first = lambda j: (0, jnp.maximum(j - pairs, 0))
    second = lambda j: (0, jnp.minimum(j, pairs - 1))
    struct = jax.ShapeDtypeStruct
    return pl.pallas_call(
        input_gradient_kernel,
        grid=(2 * pairs,),
        in_specs=[
            full,
            whole(gains8.shape),
            pl.BlockSpec((count, 3 * PAIR), first),
            pl.BlockSpec((count, 3 * PAIR), second),
            pl.BlockSpec((width, 3 * PAIR), first),
            pl.BlockSpec((width, 3 * PAIR), second),
            full,
        ],
        out_specs=[full, whole((1, width))],
        out_shape=[struct((count, width), wide), struct((1, width), wide)],
        scratch_shapes=[pltpu.VMEM((count, width), wide)],
        compiler_params=pltpu.CompilerParams(vmem_limit_bytes=VMEM_BYTES),
        cost_estimate=pl.CostEstimate(
            flops=6 * count * width * width,
            bytes_accessed=count * width * 16 + width * width * 6,
            transcendentals=0,
        ),
        name="input_gradient",
    )(rows, gains8, *d_pre, *weights, d_x1)


def update(weight, momentum, average, gradient, step_rate):
    new_momentum = momentum_decay * momentum + gradient
    direction = gradient + momentum_decay * new_momentum + weight_decay * weight
    new_weight = weight - step_rate * direction
    new_average = average_decay * average + (1.0 - average_decay) * new_weight
    return (new_momentum, new_average, new_weight)


def update_kernel(pick, step_rate, core_ref, w_ref, m_ref, a_ref, *refs):
    sums, outs = refs[:-3], refs[-3:]
    gradient = pick(core_ref[0], *[s[...] for s in sums]).astype(wide).reshape(w_ref.shape)
    results = update(w_ref[...], m_ref[...], a_ref[...], gradient, step_rate)
    for out, result in zip(outs, results):
        out[...] = result


def update_call(core, state, sums, grid, state_spec, sum_specs, pick, step_rate, name):
    struct = jax.ShapeDtypeStruct(state[0].shape, wide)
    size = math.prod(state[0].shape)
    return pl.pallas_call(
        functools.partial(update_kernel, pick, step_rate),
        grid_spec=pltpu.PrefetchScalarGridSpec(
            num_scalar_prefetch=1,
            grid=grid,
            in_specs=[state_spec] * 3 + sum_specs,
            out_specs=[state_spec] * 3,
        ),
        out_shape=[struct] * 3,
        compiler_params=pltpu.CompilerParams(vmem_limit_bytes=VMEM_BYTES),
        cost_estimate=pl.CostEstimate(flops=10 * size, bytes_accessed=26 * size, transcendentals=0),
        name=name,
    )(core, *state, *sums)


def update_attention(core, state, qfv, out, step_rate):
    _, shard, width = state[0].shape

    def pick(core_index, qfv_mine, qfv_other, out_mine, out_other):
        own = pl.program_id(1) // 2 == core_index
        proj = jnp.where(own, qfv_mine.astype(wide), qfv_other.astype(wide))
        last = jnp.where(own, out_mine.astype(wide), out_other.astype(wide))
        return jnp.where(pl.program_id(0) < 3, proj, last)

    proj_spec = pl.BlockSpec(
        (shard, PAIR), lambda kind, pair, _: (0, (pair % 2) * 3 + jnp.minimum(kind, 2))
    )
    out_spec = pl.BlockSpec((shard, PAIR), lambda kind, pair, _: (0, pair % 2))
    return update_call(
        core,
        state,
        (*qfv, *out),
        (4, width // PAIR),
        pl.BlockSpec((1, shard, PAIR), lambda kind, pair, _: (kind, 0, pair)),
        [proj_spec, proj_spec, out_spec, out_spec],
        pick,
        step_rate,
        "update_attention",
    )


def update_ffn_in(core, state, sums, step_rate):
    _, shard, hidden = state[0].shape

    def pick(core_index, *totals):
        own = pl.program_id(0) == core_index
        parts = [
            jnp.where(own, mine.astype(wide), other.astype(wide))
            for mine, other in zip(totals[::2], totals[1::2])
        ]
        return jnp.concatenate(parts, axis=1)

    flat = [total for pair in sums for total in pair]
    return update_call(
        core,
        state,
        flat,
        (2,),
        pl.BlockSpec((1, shard, hidden), lambda kind, _: (kind, 0, 0)),
        [whole(total.shape) for total in flat],
        pick,
        step_rate,
        "update_ffn_in",
    )


def update_ffn_out(core, state, sums, step_rate):
    shard, width = state[0].shape

    def pick(core_index, mine, other):
        own = pl.program_id(0) // 2 == core_index
        return jnp.where(own, mine.astype(wide), other.astype(wide))

    sum_spec = pl.BlockSpec((shard, PAIR), lambda j, _: (0, j % 2))
    return update_call(
        core,
        state,
        sums,
        (width // PAIR,),
        pl.BlockSpec((shard, PAIR), lambda j, _: (0, j)),
        [sum_spec, sum_spec],
        pick,
        step_rate,
        "update_ffn_out",
    )


def pack_kernel(core_ref, w_ref, g_ref, out_ref):
    pairs = w_ref.shape[2] // PAIR
    for pair in range(pairs):
        for kind in range(3):
            start = (pair * 3 + kind) * PAIR
            piece = w_ref[kind, :, pair * PAIR : (pair + 1) * PAIR]
            out_ref[:, start : start + PAIR] = piece.astype(low)
    start = 3 * pairs * PAIR
    out_ref[:, start : start + pairs * PAIR] = w_ref[3].astype(low)
    start += pairs * PAIR
    out_ref[:, start:] = g_ref[...].astype(low)


def pack_attention(core, weights, gains):
    _, shard, width = weights.shape
    half = width // 2
    gain_columns = jnp.pad(gains.T, ((0, 0), (0, HEAD_DIM - 3)))
    columns = 4 * half + HEAD_DIM
    return pl.pallas_call(
        pack_kernel,
        grid_spec=pltpu.PrefetchScalarGridSpec(
            num_scalar_prefetch=1,
            grid=(1,),
            in_specs=[
                pl.BlockSpec((4, shard, half), lambda j, core: (0, 0, core[0])),
                whole((shard, HEAD_DIM)),
            ],
            out_specs=whole((shard, columns)),
        ),
        out_shape=jax.ShapeDtypeStruct((shard, columns), low),
        name="pack_attention",
    )(core, weights, gain_columns)


RING = 8


def ring_place(index):
    return jnp.where(index % 2 == 0, index // 2, RING - 1 - index // 2)


def ring_member(place):
    place = place % RING
    return jnp.where(place < RING // 2, 2 * place, 2 * RING - 1 - 2 * place)


def ring_next(tensor):
    cycle = [0, 2, 4, 6, 7, 5, 3, 1]
    replicas = lax.axis_size("dp")
    pairs = []
    for place, member in enumerate(cycle):
        for replica in range(replicas):
            target = cycle[(place + (1 if replica % 2 == 0 else -1)) % RING]
            pairs.append((member * replicas + replica, target * replicas + replica))
    return lax.ppermute(tensor, ("fsdp", "dp"), pairs)


def core_swap(tensor):
    return lax.ppermute(tensor, "dp", [(d, d ^ 1) for d in range(lax.axis_size("dp"))])


def column_swap(tensor):
    return lax.ppermute(tensor, "dp", [(d, d ^ 2) for d in range(lax.axis_size("dp"))])


def assemble_kernel(origin_ref, *refs):
    pieces, out_ref = refs[:RING], refs[RING]
    rows = pieces[0].shape[0]
    for step, piece in enumerate(pieces):
        start = pl.multiple_of(origin_ref[step] * rows, 16)
        out_ref[pl.ds(start, rows), :] = piece[...]


def assemble(origins, pieces):
    rows, columns = pieces[0].shape
    return pl.pallas_call(
        assemble_kernel,
        grid_spec=pltpu.PrefetchScalarGridSpec(
            num_scalar_prefetch=1,
            grid=(1,),
            in_specs=[whole((rows, columns))] * RING,
            out_specs=whole((RING * rows, columns)),
        ),
        out_shape=jax.ShapeDtypeStruct((RING * rows, columns), pieces[0].dtype),
        compiler_params=pltpu.CompilerParams(vmem_limit_bytes=VMEM_BYTES),
        cost_estimate=pl.CostEstimate(
            flops=0, bytes_accessed=4 * RING * rows * columns, transcendentals=0
        ),
        name="assemble",
    )(origins, *pieces)


def after(tensor, *others):
    return lax.optimization_barrier((tensor, *others))[0]


def core_way():
    return 1 - 2 * (lax.axis_index("dp") % 2)


def ring_origins():
    place = ring_place(lax.axis_index("fsdp"))
    return ring_member(
        place - core_way() * jnp.arange(RING, dtype=jnp.int32) + RING
    ).astype(jnp.int32)


class RingGather:
    def __init__(self, shard):
        self.pieces = [shard]

    def step(self, *others):
        source = after(self.pieces[-1], *others) if others else self.pieces[-1]
        self.pieces.append(ring_next(source))

    def last(self, back=1):
        return self.pieces[-back]


class RingSum:
    def __init__(self, mine, other):
        self.mine = mine
        self.arrived = [core_swap(part) for part in other]
        place = ring_place(lax.axis_index("fsdp"))
        self.owners = [ring_member(place - core_way() * (s + 1) + 2 * RING) for s in range(RING)]
        self.totals = []

    def term(self):
        parts = []
        for own, arrived in zip(self.mine, self.arrived):
            rows = own.shape[0] // RING
            start = self.owners[len(self.totals)] * rows
            part = lax.dynamic_slice_in_dim(own, start, rows, 0).astype(wide)
            parts.append(part + lax.dynamic_slice_in_dim(arrived, start, rows, 0).astype(wide))
        return parts[0] if len(parts) == 1 else jnp.concatenate(parts, axis=0)

    def step(self, *others):
        if not self.totals:
            self.totals.append(self.term().astype(low))
        total = self.totals[-1]
        moved = ring_next(after(total, *others) if others else total)
        self.totals.append((moved.astype(wide) + self.term()).astype(low))

    def last(self, back=1):
        return self.totals[-back]

    def finish(self):
        total = self.totals[-1]
        total = (total.astype(wide) + column_swap(total).astype(wide)).astype(low)
        return total, core_swap(total)


def gather_rows(shard):
    mine = lax.all_gather(shard, "fsdp", axis=0, tiled=True)
    return mine, core_swap(mine)


def reduce_rows(mine, other):
    totals = []
    for own, theirs in zip(mine, other):
        both = (own.astype(wide) + core_swap(theirs).astype(wide)).astype(low)
        totals.append(lax.psum_scatter(both, "fsdp", scatter_dimension=0, tiled=True))
    total = jnp.concatenate(totals, axis=0)
    total = (total.astype(wide) + column_swap(total).astype(wide)).astype(low)
    return total, core_swap(total)


def on_device(
    inputs,
    cotangent,
    lengths,
    attention_weights,
    attention_momentum,
    attention_average,
    ffn_inputs,
    ffn_inputs_momentum,
    ffn_inputs_average,
    ffn_output,
    ffn_output_momentum,
    ffn_output_average,
    gains,
    gains_momentum,
    gains_average,
):
    micro_count, slot, width = inputs.shape
    hidden = ffn_inputs.shape[2]
    fsdp_size = lax.axis_size("fsdp")
    replicas = lax.axis_size("dp")
    core = lax.axis_index("dp") % 2
    count = micro_count * slot
    half = width // 2
    core_ref = core.astype(jnp.int32).reshape(1)
    other_ref = 1 - core_ref
    ringed = fsdp_size == RING
    cut = (hidden // PAIR + 1) // 2 * PAIR
    me = lax.axis_index("fsdp")

    packed = pack_attention(core_ref, attention_weights, gains)
    up_half = lax.dynamic_index_in_dim(ffn_inputs, core, 0, keepdims=False).astype(low)
    down_half = lax.dynamic_slice_in_dim(ffn_output, core * half, half, 1).astype(low)

    rows = inputs.reshape(count, width)
    positions = jnp.arange(slot, dtype=jnp.int32)
    valid = (positions[None, :] < lengths).astype(wide).reshape(count, 1)
    errors = (cotangent.reshape(count, width).astype(wide) * valid).astype(low)

    def gains_of(weights):
        gain_rows = weights[:, 4 * half : 4 * half + 3].T.astype(wide)
        return jnp.pad(gain_rows, ((0, 5), (0, 0)))

    if ringed:
        origins = ring_origins()
        ring_a, ring_d = RingGather(packed), RingGather(down_half)
        ring_left, ring_right = RingGather(up_half[:, :cut]), RingGather(up_half[:, cut:])
        for step in range(1, RING):
            ring_a.step(*([] if step == 1 else [ring_left.last(2)]))
            ring_left.step(*([] if step == 1 else [ring_a.last(2)]))
        w_a_mine = assemble(origins, ring_a.pieces)
        w_a = (w_a_mine, core_swap(w_a_mine))
        gains8 = gains_of(w_a_mine)
        ring_d.step(ring_left.last(2), ring_a.last())
        ring_right.step(ring_left.last())
        left_mine = assemble(origins, ring_left.pieces)
        w_left = (left_mine, core_swap(left_mine))
        ring_d.step(ring_right.last(2))
        ring_right.step(ring_d.last(2))
        mixed_mine, *kept_mine = mixer_forward(
            core_ref, after(rows, ring_d.last(2), ring_right.last(2)), w_a[0], gains8, slot
        )
        ring_d.step(mixed_mine)
        ring_right.step(mixed_mine)
        mixed_other, *rest = mixer_forward(
            other_ref,
            after(rows, ring_d.last(2), ring_right.last(2)),
            w_a[1],
            gains8,
            slot,
            (mixed_mine, w_a[0]),
        )
        ring_d.step(mixed_other)
        ring_right.step(mixed_other)
        for step in range(3):
            ring_d.step(ring_right.last(2))
            ring_right.step(ring_d.last(2))
        d_mine, right_mine = assemble(origins, ring_d.pieces), assemble(origins, ring_right.pieces)
        w_d = (d_mine, core_swap(d_mine))
        w_right = (right_mine, core_swap(right_mine))
        w_gu = [jnp.concatenate([left, right], axis=1) for left, right in zip(w_left, w_right)]
    else:
        w_a, w_d, w_gu = gather_rows(packed), gather_rows(down_half), gather_rows(up_half)
        gains8 = gains_of(w_a[0])
        mixed_mine, *kept_mine = mixer_forward(core_ref, rows, w_a[0], gains8, slot)
        mixed_other, *rest = mixer_forward(
            other_ref, rows, w_a[1], gains8, slot, (mixed_mine, w_a[0])
        )
    kept_other, (x1, h2, h2t, h1t) = rest[:4], rest[4:]
    gm, gu, gd_mine, gd_other, output, d_x1, d_mixed, go_mine, go_other, grad_two = ffn(
        core_ref, h2, h2t, errors, w_gu, w_d, x1, (mixed_mine, mixed_other), w_a, valid, gains8
    )
    if ringed:
        sum_gu = RingSum([gm], [gu])
        sum_do = RingSum([gd_mine, go_mine], [gd_other, go_other])
    grad_other, ggo_other, dpre_other = mixer_backward(
        other_ref, h1t, gains8, kept_other, d_mixed, slot
    )
    if ringed:
        sum_gu.step(dpre_other)
        sum_do.step(dpre_other)
        tie = (sum_gu.mine[0], sum_gu.arrived[0], *sum_do.arrived)
    else:
        tie = ()
    grad_mine, ggo_mine, dpre_mine = mixer_backward(
        core_ref, after(h1t, *tie) if tie else h1t, gains8, kept_mine, d_mixed, slot
    )
    is_first = core == 0
    ggo_left = jnp.where(is_first, ggo_mine, ggo_other)
    ggo_right = jnp.where(is_first, ggo_other, ggo_mine)
    grad_go = jnp.concatenate([ggo_left, ggo_right], axis=1)

    def gains_sum(grad_one):
        stacked = jnp.concatenate([grad_one, grad_go, grad_two], axis=0)
        return lax.psum(stacked, ("fsdp", "dp"))

    if ringed:
        sum_qfv = RingSum([grad_mine], [grad_other])
        sum_gu.step(grad_mine)
        sum_do.step(grad_mine)
        turns = [sum_gu, sum_do]
        for step in range(6):
            turns.append(sum_qfv)
            if step < 5:
                turns += [sum_gu, sum_do]
        turns.append(sum_qfv)
        results = [sum_gu.last(), sum_do.last()]
        for place, ring in enumerate(turns[2:]):
            others = [results[-2]]
            if place == 6:
                input_grad, grad_one = input_gradient(
                    rows, gains8, (after(dpre_mine, results[-2]), dpre_other), w_a, d_x1
                )
                gain_grads = gains_sum(grad_one)
            if place == 10:
                others.append(gain_grads)
            ring.step(*others)
            results.append(ring.last())
        sum_gu, sum_do, sum_qfv = sum_gu.finish(), sum_do.finish(), sum_qfv.finish()
    else:
        sum_gu = reduce_rows([gm], [gu])
        sum_do = reduce_rows([gd_mine, go_mine], [gd_other, go_other])
        sum_qfv = reduce_rows([grad_mine], [grad_other])
        input_grad, grad_one = input_gradient(rows, gains8, (dpre_mine, dpre_other), w_a, d_x1)
        gain_grads = gains_sum(grad_one)
    sum_gains = lax.dynamic_slice_in_dim(gain_grads, me * gains.shape[1], gains.shape[1], 1)
    down_rows = ffn_output.shape[0]
    sum_d = [total[:down_rows] for total in sum_do]
    sum_o = [total[down_rows:] for total in sum_do]

    scale_rows = 1.0 / math.sqrt(count * fsdp_size * replicas)
    attention_state = (attention_weights, attention_momentum, attention_average)
    ffn_in_state = (ffn_inputs, ffn_inputs_momentum, ffn_inputs_average)
    ffn_out_state = (ffn_output, ffn_output_momentum, ffn_output_average)
    return (
        output.reshape(micro_count, slot, width),
        input_grad.reshape(micro_count, slot, width),
        *update_attention(core_ref, attention_state, sum_qfv, sum_o, matrix_rate * scale_rows),
        *update_ffn_in(core_ref, ffn_in_state, [sum_gu], matrix_rate * scale_rows),
        *update_ffn_out(core_ref, ffn_out_state, sum_d, matrix_rate * scale_rows),
        *update(gains, gains_momentum, gains_average, sum_gains, gain_rate * scale_rows),
    )


def solution(mesh):
    rows_split = P(None, ("fsdp", "dp"), None)
    middle_split = P(None, "fsdp", None)
    first_split = P("fsdp", None)
    gains_split = P(None, "fsdp")
    in_specs = (
        (rows_split, rows_split, P(None, ("fsdp", "dp")))
        + (middle_split,) * 6
        + (first_split,) * 3
        + (gains_split,) * 3
    )
    out_specs = (
        (rows_split, rows_split)
        + (middle_split,) * 6
        + (first_split,) * 3
        + (gains_split,) * 3
    )
    return jax.shard_map(
        on_device, mesh=mesh, in_specs=in_specs, out_specs=out_specs, check_vma=False
    )
```

```python
import functools
import math

import jax
import jax.numpy as jnp
from jax import lax
from jax.experimental import pallas as pl
from jax.experimental.pallas import tpu as pltpu
from jax.sharding import PartitionSpec as P

HEAD_DIM = 128
PAIR = 2 * HEAD_DIM

lower_bound = 0.9
momentum_decay = 0.9
average_decay = 0.7
weight_decay = 0.0005
matrix_rate = 0.03
gain_rate = 0.1
low = jnp.bfloat16
wide = jnp.float32
VMEM_BYTES = 60 * 1024 * 1024


def mm(left, right):
    return jnp.dot(left, right, preferred_element_type=wide)


def mm_nt(left, right):
    return lax.dot_general(left, right, (((1,), (1,)), ((), ())), preferred_element_type=wide)


def mm_tn(left, right):
    return lax.dot_general(left, right, (((0,), (0,)), ((), ())), preferred_element_type=wide)


def sigmoid(u):
    return 1.0 / (1.0 + jnp.exp(-u))


def whole(shape):
    return pl.BlockSpec(shape, lambda *_: (0,) * len(shape), pipeline_mode=pl.Buffered(1))


def split_sum(ones_matrix, tensor):
    high = tensor.astype(low)
    rest = (tensor - high.astype(wide)).astype(low)
    return mm(ones_matrix, high) + mm(ones_matrix, rest)


def triangle(length, lower):
    rows = lax.broadcasted_iota(jnp.int32, (length, length), 0)
    columns = lax.broadcasted_iota(jnp.int32, (length, length), 1)
    kept = rows >= columns if lower else rows <= columns
    return kept.astype(wide).astype(low)


def decay_parts(f_pre, lower_ones):
    share = sigmoid(f_pre)
    gate = lower_bound + (1.0 - lower_bound) * share
    keys_in = (1.0 - lower_bound) * (1.0 - share)
    cumulative = split_sum(lower_ones, jnp.log(gate))
    middle_row = cumulative.shape[0] // 2
    cumulative = cumulative - cumulative[middle_row : middle_row + 1, :]
    return share, gate, keys_in, cumulative


def first_norm(x_ref, gain_row):
    rows = x_ref[...].astype(wide)
    scale = lax.rsqrt(jnp.mean(rows * rows, axis=-1, keepdims=True) + 1e-06)
    return rows * scale, scale


def lanes_of(half, size):
    return pl.ds(pl.multiple_of(half * size, size), size)


def mixer_forward_kernel(
    slot, half_ref, x_ref, w_ref, g_ref, on_ref, q_ref, f_ref, v_ref, o_ref, h_s
):
    @pl.when(pl.program_id(0) == 0)
    def _():
        normed, _ = first_norm(x_ref, None)
        h_s[...] = (normed * g_ref[0:1, :]).astype(low)

    gain_o = g_ref[1:2, lanes_of(half_ref[0] * pl.num_programs(0) + pl.program_id(0), PAIR)]
    pre = mm(h_s[...], w_ref[...])
    q_ref[...] = pre[:, :PAIR]
    f_ref[...] = pre[:, PAIR : 2 * PAIR]
    v_ref[...] = pre[:, 2 * PAIR :].astype(low)
    lower_ones = triangle(slot, True)
    block_rows = lax.broadcasted_iota(jnp.int32, (HEAD_DIM, HEAD_DIM), 0)
    block_columns = lax.broadcasted_iota(jnp.int32, (HEAD_DIM, HEAD_DIM), 1)
    causal = block_rows >= block_columns
    for sequence in range(x_ref.shape[0] // slot):
        rows = slice(sequence * slot, (sequence + 1) * slot)
        q_pre = q_ref[rows, :]
        _, _, keys_in, cumulative = decay_parts(f_ref[rows, :], lower_ones)
        grown = jnp.exp(-cumulative)
        decayed_q = (q_pre * sigmoid(q_pre) * jnp.exp(cumulative)).astype(low)
        grown_k = (keys_in * grown).astype(low)
        values = v_ref[rows, :]
        for head in range(2):
            lanes = slice(head * HEAD_DIM, (head + 1) * HEAD_DIM)
            for block in range(slot // HEAD_DIM):
                start, end = block * HEAD_DIM, (block + 1) * HEAD_DIM
                q_block = decayed_q[start:end, lanes]
                diagonal = mm_nt(q_block, grown_k[start:end, lanes])
                diagonal = jnp.where(causal, diagonal, 0.0).astype(low)
                out = mm(diagonal, values[start:end, lanes])
                if block > 0:
                    scores = mm_nt(q_block, grown_k[:start, lanes]).astype(low)
                    out = out + mm(scores, values[:start, lanes])
                scale = lax.rsqrt(jnp.mean(out * out, axis=-1, keepdims=True) + 1e-05)
                target = slice(sequence * slot + start, sequence * slot + end)
                o_ref[target, lanes] = out
                on_ref[target, lanes] = (out * scale * gain_o[:, lanes]).astype(low)


def mixer_forward_last_kernel(
    slot,
    half_ref,
    x_ref,
    w_ref,
    g_ref,
    before_ref,
    woo_ref,
    wom_ref,
    on_ref,
    q_ref,
    f_ref,
    v_ref,
    o_ref,
    x1_ref,
    h2_ref,
    h1t_ref,
    h_s,
    on_s,
):
    step = pl.program_id(0)
    half = before_ref.shape[1]
    mixer_forward_kernel(
        slot, half_ref, x_ref, w_ref, g_ref, on_ref, q_ref, f_ref, v_ref, o_ref, h_s
    )
    on_s[:, lanes_of(half_ref[0] * pl.num_programs(0) + step, PAIR)] = on_ref[...]

    @pl.when(step == pl.num_programs(0) - 1)
    def _():
        here = lanes_of(half_ref[0], half)
        there = lanes_of(1 - half_ref[0], half)
        on_s[:, there] = before_ref[...]
        h1t_ref[...] = h_s[...].astype(wide).T.astype(low)
        x1_ref[:, here] = x_ref[:, here].astype(wide) + mm(on_s[...], woo_ref[...])
        x1_ref[:, there] = x_ref[:, there].astype(wide) + mm(on_s[...], wom_ref[...])
        x1 = x1_ref[...]
        scale = lax.rsqrt(jnp.mean(x1 * x1, axis=-1, keepdims=True) + 1e-06)
        normed = x1 * scale * g_ref[2:3, :]
        h2_ref[...] = normed.astype(low)


def mixer_forward(half, rows, weights, gains8, slot, ending=None):
    count, width = rows.shape
    pairs = width // PAIR // 2
    by_pair = pl.BlockSpec((count, PAIR), lambda j, _: (0, j))
    struct = jax.ShapeDtypeStruct
    shape = lambda kind: struct((count, width // 2), kind)
    kernel = mixer_forward_kernel
    in_specs = [
        whole(rows.shape),
        pl.BlockSpec((width, 3 * PAIR), lambda j, _: (0, j)),
        whole(gains8.shape),
    ]
    operands = [half, rows, weights, gains8]
    out_specs = [by_pair] * 5
    out_shape = [shape(low), shape(wide), shape(wide), shape(low), shape(wide)]
    scratch = [pltpu.VMEM((count, width), low)]
    if ending is not None:
        kernel = mixer_forward_last_kernel
        out_weights = pl.BlockSpec((width, width // 2), lambda j, _: (0, 3))
        in_specs += [whole((count, width // 2)), out_weights, out_weights]
        operands += [ending[0], weights, ending[1]]
        out_specs += [whole((count, width))] * 2 + [whole((width, count))]
        out_shape += [
            struct((count, width), wide),
            struct((count, width), low),
            struct((width, count), low),
        ]
        scratch += [pltpu.VMEM((count, width), low)]
    return pl.pallas_call(
        functools.partial(kernel, slot),
        grid_spec=pltpu.PrefetchScalarGridSpec(
            num_scalar_prefetch=1,
            grid=(pairs,),
            in_specs=in_specs,
            out_specs=out_specs,
            scratch_shapes=scratch,
        ),
        out_shape=out_shape,
        compiler_params=pltpu.CompilerParams(vmem_limit_bytes=VMEM_BYTES),
        cost_estimate=pl.CostEstimate(
            flops=count * width * 4 * width + 10 * count * slot * width,
            bytes_accessed=count * width * 12 + width * width * 4,
            transcendentals=count * width * 3,
        ),
        name="mixer_forward",
    )(*operands)


def ffn_rows_kernel(
    core_ref,
    h_ref,
    e_ref,
    wm_ref,
    wu_ref,
    wdm_ref,
    wdo_ref,
    mid_ref,
    down_ref,
    dswap_ref,
    x2_ref,
    dh_ref,
):
    half = wdm_ref.shape[1]
    first = core_ref[0] == 0
    mine = lanes_of(core_ref[0], half)
    other = lanes_of(1 - core_ref[0], half)
    own = mm(h_ref[...], wm_ref[...])
    swapped = mm(h_ref[...], wu_ref[...])
    a = jnp.where(first, own, swapped)
    b = jnp.where(first, swapped, own)
    share = sigmoid(a)
    swish = a * share
    mid = (swish * b).astype(low)
    mid_ref[...] = mid
    d_mid = mm_nt(e_ref[:, mine], wdm_ref[...]) + mm_nt(e_ref[:, other], wdo_ref[...])
    d_a = (d_mid * b * share * (1.0 + a * (1.0 - share))).astype(low)
    d_b = (d_mid * swish).astype(low)
    d_own = jnp.where(first, d_a, d_b)
    d_swapped = jnp.where(first, d_b, d_a)
    down_ref[...] = d_own
    dswap_ref[...] = d_swapped
    d_h2 = mm_nt(d_own, wm_ref[...]) + mm_nt(d_swapped, wu_ref[...])
    dh_ref[...] = d_h2.astype(dh_ref.dtype)
    x2_ref[:, mine] = mm(mid, wdm_ref[...]).astype(x2_ref.dtype)
    x2_ref[:, other] = mm(mid, wdo_ref[...]).astype(x2_ref.dtype)


def ffn_rows(core, h2, errors, block, first_block, blocks, w_gu, w_d, kind):
    width = h2.shape[1]
    hidden = w_gu[0].shape[1]
    rows = blocks * block
    by_rows = lambda columns: pl.BlockSpec((block, columns), lambda j, _: (j, 0))
    errors_spec = pl.BlockSpec((block, width), lambda j, _: (first_block + j, 0))
    struct = jax.ShapeDtypeStruct
    return pl.pallas_call(
        ffn_rows_kernel,
        grid_spec=pltpu.PrefetchScalarGridSpec(
            num_scalar_prefetch=1,
            grid=(blocks,),
            in_specs=[by_rows(width), errors_spec]
            + [whole(w.shape) for w in (*w_gu, *w_d)],
            out_specs=[by_rows(hidden)] * 3 + [by_rows(width)] * 2,
        ),
        out_shape=[struct((rows, hidden), low)] * 3 + [struct((rows, width), kind)] * 2,
        compiler_params=pltpu.CompilerParams(vmem_limit_bytes=VMEM_BYTES),
        cost_estimate=pl.CostEstimate(
            flops=10 * rows * width * hidden,
            bytes_accessed=rows * (width * 12 + hidden * 6) + width * hidden * 6,
            transcendentals=rows * hidden,
        ),
        name="ffn_rows",
    )(core, h2, errors, *w_gu, *w_d)


def ffn_weights_kernel(groups, core_ref, *refs):
    h_refs, e_refs = refs[:groups], refs[groups : groups + 2]
    mids = refs[groups + 2 : 2 * groups + 2]
    owns = refs[2 * groups + 2 : 3 * groups + 2]
    swaps = refs[3 * groups + 2 : 4 * groups + 2]
    gm_ref, gu_ref, gdm_ref, gdo_ref, ht_s, e_s = refs[4 * groups + 2 :]
    half = gdm_ref.shape[1]

    @pl.when(pl.program_id(0) == 0)
    def _():
        start = 0
        for h_ref in h_refs:
            end = start + h_ref.shape[0]
            ht_s[:, start:end] = h_ref[...].astype(wide).T.astype(low)
            start = end
        start = 0
        for e_ref in e_refs:
            end = start + e_ref.shape[0]
            e_s[start:end, :] = e_ref[...]
            start = end

    own = jnp.concatenate([ref[...] for ref in owns], axis=0)
    swapped = jnp.concatenate([ref[...] for ref in swaps], axis=0)
    grads = mm(ht_s[...], jnp.concatenate([own, swapped], axis=1)).astype(low)
    gm_ref[...] = grads[:, :HEAD_DIM]
    gu_ref[...] = grads[:, HEAD_DIM:]
    mid = jnp.concatenate([ref[...] for ref in mids], axis=0)
    gdm_ref[...] = mm_tn(mid, e_s[:, lanes_of(core_ref[0], half)]).astype(low)
    gdo_ref[...] = mm_tn(mid, e_s[:, lanes_of(1 - core_ref[0], half)]).astype(low)


def ffn_weights(core, h2_parts, errors, mids, owns, swaps):
    width = h2_parts[0].shape[1]
    half = width // 2
    hidden = mids[0].shape[1]
    count = sum(part.shape[0] for part in h2_parts)
    tiles = [pl.BlockSpec((part.shape[0], HEAD_DIM), lambda j, _: (0, j)) for part in h2_parts]
    by_columns = pl.BlockSpec((width, HEAD_DIM), lambda j, _: (0, j))
    by_rows = pl.BlockSpec((HEAD_DIM, half), lambda j, _: (j, 0))
    struct = jax.ShapeDtypeStruct
    return pl.pallas_call(
        functools.partial(ffn_weights_kernel, len(h2_parts)),
        grid_spec=pltpu.PrefetchScalarGridSpec(
            num_scalar_prefetch=1,
            grid=(hidden // HEAD_DIM,),
            in_specs=[whole(part.shape) for part in (*h2_parts, *errors)] + tiles * 3,
            out_specs=[by_columns] * 2 + [by_rows] * 2,
            scratch_shapes=[pltpu.VMEM((width, count), low), pltpu.VMEM((count, width), low)],
        ),
        out_shape=[struct((width, hidden), low)] * 2 + [struct((hidden, half), low)] * 2,
        compiler_params=pltpu.CompilerParams(vmem_limit_bytes=VMEM_BYTES),
        cost_estimate=pl.CostEstimate(
            flops=6 * count * width * hidden,
            bytes_accessed=count * (width * 4 + hidden * 6) + width * hidden * 6,
            transcendentals=0,
        ),
        name="ffn_weights",
    )(core, *h2_parts, *errors, *mids, *owns, *swaps)


def middle_backward_kernel(
    core_ref,
    x1_ref,
    e_ref,
    dh_ref,
    dha_ref,
    dhb_ref,
    onm_ref,
    ono_ref,
    wom_ref,
    woo_ref,
    g_ref,
    dx1_ref,
    don_ref,
    gom_ref,
    goo_ref,
    g2_ref,
    d1_s,
):
    half = onm_ref.shape[1]
    mine = lanes_of(core_ref[0], half)
    other = lanes_of(1 - core_ref[0], half)
    x1 = x1_ref[...]
    scale = lax.rsqrt(jnp.mean(x1 * x1, axis=-1, keepdims=True) + 1e-06)
    normed = x1 * scale
    arrived = jnp.concatenate([dha_ref[...], dhb_ref[...]], axis=0)
    d_h2 = dh_ref[...] + arrived.astype(wide)
    scaled = d_h2 * g_ref[2:3, :]
    g2_ref[...] = jnp.sum(d_h2 * normed, axis=0, keepdims=True)
    d_x1 = e_ref[...].astype(wide) + scale * (
        scaled - normed * jnp.mean(scaled * normed, axis=-1, keepdims=True)
    )
    dx1_ref[...] = d_x1
    d1_s[...] = d_x1.astype(low)
    don_ref[...] = mm_nt(d1_s[:, mine], wom_ref[...]) + mm_nt(d1_s[:, other], woo_ref[...])
    onm, ono = onm_ref[...], ono_ref[...]
    here = pl.ds(pl.multiple_of(core_ref[0] * half, half), half)
    there = pl.ds(pl.multiple_of((1 - core_ref[0]) * half, half), half)
    for out_ref, columns in ((gom_ref, mine), (goo_ref, other)):
        d_1 = d1_s[:, columns]
        out_ref[here, :] = mm_tn(onm, d_1).astype(low)
        out_ref[there, :] = mm_tn(ono, d_1).astype(low)


def middle_backward(core, x1, errors, d_h2, arrived, mixed, w_a, gains8):
    count, width = x1.shape
    half = width // 2
    full = whole((count, width))
    out_weights = pl.BlockSpec((width, half), lambda j, _: (0, 3), pipeline_mode=pl.Buffered(1))
    square = whole((width, half))
    struct = jax.ShapeDtypeStruct
    return pl.pallas_call(
        middle_backward_kernel,
        grid_spec=pltpu.PrefetchScalarGridSpec(
            num_scalar_prefetch=1,
            grid=(1,),
            in_specs=[full, full, full]
            + [whole(part.shape) for part in (*arrived, *mixed)]
            + [out_weights, out_weights, whole(gains8.shape)],
            out_specs=[full, full, square, square, whole((1, width))],
            scratch_shapes=[pltpu.VMEM((count, width), low)],
        ),
        out_shape=[struct((count, width), wide)] * 2
        + [struct((width, half), low)] * 2
        + [struct((1, width), wide)],
        compiler_params=pltpu.CompilerParams(vmem_limit_bytes=VMEM_BYTES),
        cost_estimate=pl.CostEstimate(
            flops=4 * count * width * width,
            bytes_accessed=count * width * 24 + width * width * 4,
            transcendentals=0,
        ),
        name="middle_backward",
    )(core, x1, errors, d_h2, *arrived, *mixed, *w_a, gains8)


def mixer_backward_kernel(
    slot,
    half_ref,
    ht_ref,
    g_ref,
    q_ref,
    f_ref,
    v_ref,
    o_ref,
    don_ref,
    grad_ref,
    ggo_ref,
    dpre_ref,
):
    gain_o = g_ref[1:2, lanes_of(half_ref[0] * pl.num_programs(0) + pl.program_id(0), PAIR)]
    lower_ones = triangle(slot, True)
    upper_ones = triangle(slot, False)
    block_rows = lax.broadcasted_iota(jnp.int32, (HEAD_DIM, HEAD_DIM), 0)
    block_columns = lax.broadcasted_iota(jnp.int32, (HEAD_DIM, HEAD_DIM), 1)
    causal = block_rows >= block_columns
    causal_t = block_rows <= block_columns
    blocks = slot // HEAD_DIM
    ggo_total = jnp.zeros((1, PAIR), wide)
    for sequence in range(q_ref.shape[0] // slot):
        rows = slice(sequence * slot, (sequence + 1) * slot)
        d_on = don_ref[rows, :]
        out = o_ref[rows, :]
        d_out_parts = []
        ggo_parts = []
        for head in range(2):
            lanes = slice(head * HEAD_DIM, (head + 1) * HEAD_DIM)
            out_h, d_on_h = out[:, lanes], d_on[:, lanes]
            scale = lax.rsqrt(jnp.mean(out_h * out_h, axis=-1, keepdims=True) + 1e-05)
            normed = out_h * scale
            ggo_parts.append(jnp.sum(d_on_h * normed, axis=0, keepdims=True))
            scaled = d_on_h * gain_o[:, lanes]
            inner = jnp.mean(scaled * normed, axis=-1, keepdims=True)
            d_out_parts.append((scale * (scaled - normed * inner)).astype(low))
        ggo_total = ggo_total + jnp.concatenate(ggo_parts, axis=1)

        q_pre = q_ref[rows, :]
        share, gate, keys_in, cumulative = decay_parts(f_ref[rows, :], lower_ones)
        grown = jnp.exp(-cumulative)
        shrunk = jnp.exp(cumulative)
        q_share = sigmoid(q_pre)
        decayed_q = (q_pre * q_share * shrunk).astype(low)
        grown_k = (keys_in * grown).astype(low)
        values = v_ref[rows, :]
        dq_parts, dk_parts, dv_parts = [], [], []
        for head in range(2):
            lanes = slice(head * HEAD_DIM, (head + 1) * HEAD_DIM)
            q_h, k_h, v_h = decayed_q[:, lanes], grown_k[:, lanes], values[:, lanes]
            d_out = d_out_parts[head]
            dq_blocks, dk_blocks, dv_blocks = [], [], []
            for block in range(blocks):
                start, end = block * HEAD_DIM, (block + 1) * HEAD_DIM
                here = slice(start, end)
                d_scores = mm_nt(d_out[here], v_h[here])
                d_scores = jnp.where(causal, d_scores, 0.0).astype(low)
                d_q = mm(d_scores, k_h[here])
                if block > 0:
                    before = slice(0, start)
                    d_scores = mm_nt(d_out[here], v_h[before]).astype(low)
                    d_q = d_q + mm(d_scores, k_h[before])
                dq_blocks.append(d_q)
                scores = jnp.where(causal_t, mm_nt(k_h[here], q_h[here]), 0.0).astype(low)
                d_scores = jnp.where(causal_t, mm_nt(v_h[here], d_out[here]), 0.0).astype(low)
                d_v = mm(scores, d_out[here])
                d_k = mm(d_scores, q_h[here])
                if block < blocks - 1:
                    after = slice(end, slot)
                    scores = mm_nt(k_h[here], q_h[after]).astype(low)
                    d_scores = mm_nt(v_h[here], d_out[after]).astype(low)
                    d_v = d_v + mm(scores, d_out[after])
                    d_k = d_k + mm(d_scores, q_h[after])
                dk_blocks.append(d_k)
                dv_blocks.append(d_v)
            dq_parts.append(jnp.concatenate(dq_blocks, axis=0))
            dk_parts.append(jnp.concatenate(dk_blocks, axis=0))
            dv_parts.append(jnp.concatenate(dv_blocks, axis=0))
        d_decayed = jnp.concatenate(dq_parts, axis=1)
        d_grown = jnp.concatenate(dk_parts, axis=1)
        d_value = jnp.concatenate(dv_parts, axis=1)
        d_cumulative = decayed_q.astype(wide) * d_decayed - grown_k.astype(wide) * d_grown
        d_log = split_sum(upper_ones, d_cumulative)
        d_query = d_decayed * shrunk
        d_key = d_grown * grown
        d_q_pre = d_query * q_share * (1.0 + q_pre * (1.0 - q_share))
        d_f_pre = (1.0 - lower_bound) * (d_log / gate - d_key) * share * (1.0 - share)
        dpre_ref[rows, :PAIR] = d_q_pre.astype(low)
        dpre_ref[rows, PAIR : 2 * PAIR] = d_f_pre.astype(low)
        dpre_ref[rows, 2 * PAIR :] = d_value.astype(low)

    ggo_ref[...] = ggo_total
    grad_ref[...] = mm(ht_ref[...], dpre_ref[...]).astype(low)


def mixer_backward(half, h1t, gains8, kept, d_mixed, slot):
    width, count = h1t.shape
    pairs = width // PAIR // 2
    by_pair = pl.BlockSpec((count, PAIR), lambda j, _: (0, j))
    from_half = pl.BlockSpec((count, PAIR), lambda j, half: (0, half[0] * pairs + j))
    struct = jax.ShapeDtypeStruct
    return pl.pallas_call(
        functools.partial(mixer_backward_kernel, slot),
        grid_spec=pltpu.PrefetchScalarGridSpec(
            num_scalar_prefetch=1,
            grid=(pairs,),
            in_specs=[whole((width, count)), whole(gains8.shape)] + [by_pair] * 4 + [from_half],
            out_specs=[
                pl.BlockSpec((width, 3 * PAIR), lambda j, _: (0, j)),
                pl.BlockSpec((1, PAIR), lambda j, _: (0, j)),
                pl.BlockSpec((count, 3 * PAIR), lambda j, _: (0, j)),
            ],
        ),
        out_shape=[
            struct((width, 3 * width // 2), low),
            struct((1, width // 2), wide),
            struct((count, 3 * width // 2), low),
        ],
        compiler_params=pltpu.CompilerParams(vmem_limit_bytes=VMEM_BYTES),
        cost_estimate=pl.CostEstimate(
            flops=count * width * 3 * width + 20 * count * slot * width,
            bytes_accessed=count * width * 12 + width * width * 3,
            transcendentals=count * width * 4,
        ),
        name="mixer_backward",
    )(half, h1t, gains8, *kept, d_mixed)


def input_gradient_kernel(x_ref, g_ref, dm_ref, do_ref, wm_ref, wo_ref, dx1_ref, dx_ref, g1_ref, dh_s):
    step = pl.program_id(0)
    pairs = pl.num_programs(0) // 2

    @pl.when(step == 0)
    def _():
        dh_s[...] = mm_nt(do_ref[...], wo_ref[...])

    @pl.when(jnp.logical_and(step > 0, step < pairs))
    def _():
        dh_s[...] += mm_nt(do_ref[...], wo_ref[...])

    @pl.when(step >= pairs)
    def _():
        dh_s[...] += mm_nt(dm_ref[...], wm_ref[...])

    @pl.when(step == 2 * pairs - 1)
    def _():
        normed, scale = first_norm(x_ref, None)
        d_h1 = dh_s[...]
        scaled = d_h1 * g_ref[0:1, :]
        g1_ref[...] = jnp.sum(d_h1 * normed, axis=0, keepdims=True)
        dx_ref[...] = dx1_ref[...] + scale * (
            scaled - normed * jnp.mean(scaled * normed, axis=-1, keepdims=True)
        )


def input_gradient(rows, gains8, d_pre, weights, d_x1):
    count, width = rows.shape
    pairs = width // PAIR // 2
    full = whole((count, width))
    first = lambda j: (0, jnp.maximum(j - pairs, 0))
    second = lambda j: (0, jnp.minimum(j, pairs - 1))
    struct = jax.ShapeDtypeStruct
    return pl.pallas_call(
        input_gradient_kernel,
        grid=(2 * pairs,),
        in_specs=[
            full,
            whole(gains8.shape),
            pl.BlockSpec((count, 3 * PAIR), first),
            pl.BlockSpec((count, 3 * PAIR), second),
            pl.BlockSpec((width, 3 * PAIR), first),
            pl.BlockSpec((width, 3 * PAIR), second),
            full,
        ],
        out_specs=[full, whole((1, width))],
        out_shape=[struct((count, width), wide), struct((1, width), wide)],
        scratch_shapes=[pltpu.VMEM((count, width), wide)],
        compiler_params=pltpu.CompilerParams(vmem_limit_bytes=VMEM_BYTES),
        cost_estimate=pl.CostEstimate(
            flops=6 * count * width * width,
            bytes_accessed=count * width * 16 + width * width * 6,
            transcendentals=0,
        ),
        name="input_gradient",
    )(rows, gains8, *d_pre, *weights, d_x1)


def update(weight, momentum, average, gradient, step_rate):
    new_momentum = momentum_decay * momentum + gradient
    direction = gradient + momentum_decay * new_momentum + weight_decay * weight
    new_weight = weight - step_rate * direction
    new_average = average_decay * average + (1.0 - average_decay) * new_weight
    return (new_momentum, new_average, new_weight)


def update_kernel(pick, step_rate, core_ref, w_ref, m_ref, a_ref, *refs):
    sums, outs = refs[:-3], refs[-3:]
    gradient = pick(core_ref[0], *[s[...] for s in sums]).astype(wide).reshape(w_ref.shape)
    results = update(w_ref[...], m_ref[...], a_ref[...], gradient, step_rate)
    for out, result in zip(outs, results):
        out[...] = result


def update_call(core, state, sums, grid, state_spec, sum_specs, pick, step_rate, name):
    struct = jax.ShapeDtypeStruct(state[0].shape, wide)
    size = math.prod(state[0].shape)
    return pl.pallas_call(
        functools.partial(update_kernel, pick, step_rate),
        grid_spec=pltpu.PrefetchScalarGridSpec(
            num_scalar_prefetch=1,
            grid=grid,
            in_specs=[state_spec] * 3 + sum_specs,
            out_specs=[state_spec] * 3,
        ),
        out_shape=[struct] * 3,
        compiler_params=pltpu.CompilerParams(vmem_limit_bytes=VMEM_BYTES),
        cost_estimate=pl.CostEstimate(flops=10 * size, bytes_accessed=26 * size, transcendentals=0),
        name=name,
    )(core, *state, *sums)


def update_attention(core, state, qfv, out, step_rate):
    _, shard, width = state[0].shape

    def pick(core_index, qfv_mine, qfv_other, out_mine, out_other):
        own = pl.program_id(1) == core_index
        proj = jnp.where(own, qfv_mine.astype(wide), qfv_other.astype(wide))
        last = jnp.where(own, out_mine.astype(wide), out_other.astype(wide))
        for kind in range(3):
            parts = [proj[:, (3 * pair + kind) * PAIR :][:, :PAIR] for pair in range(2)]
            chosen = jnp.concatenate(parts, axis=1)
            last = jnp.where(pl.program_id(0) == kind, chosen, last)
        return last

    return update_call(
        core,
        state,
        (*qfv, *out),
        (4, 2),
        pl.BlockSpec((1, shard, width // 2), lambda kind, half, _: (kind, 0, half)),
        [whole(total.shape) for total in (*qfv, *out)],
        pick,
        step_rate,
        "update_attention",
    )


def update_ffn_in(core, state, sums, step_rate):
    _, shard, hidden = state[0].shape

    def pick(core_index, mine, other):
        own = pl.program_id(0) == core_index
        return jnp.where(own, mine.astype(wide), other.astype(wide))

    return update_call(
        core,
        state,
        sums,
        (2,),
        pl.BlockSpec((1, shard, hidden), lambda kind, _: (kind, 0, 0)),
        [whole(total.shape) for total in sums],
        pick,
        step_rate,
        "update_ffn_in",
    )


def update_ffn_out(core, state, sums, step_rate):
    shard, width = state[0].shape

    def pick(core_index, mine, other):
        own = pl.program_id(0) == core_index
        return jnp.where(own, mine.astype(wide), other.astype(wide))

    return update_call(
        core,
        state,
        sums,
        (2,),
        pl.BlockSpec((shard, width // 2), lambda j, _: (0, j)),
        [whole(total.shape) for total in sums],
        pick,
        step_rate,
        "update_ffn_out",
    )


def pack_kernel(core_ref, w_ref, g_ref, out_ref):
    pairs = w_ref.shape[2] // PAIR
    for pair in range(pairs):
        for kind in range(3):
            start = (pair * 3 + kind) * PAIR
            piece = w_ref[kind, :, pair * PAIR : (pair + 1) * PAIR]
            out_ref[:, start : start + PAIR] = piece.astype(low)
    start = 3 * pairs * PAIR
    out_ref[:, start : start + pairs * PAIR] = w_ref[3].astype(low)
    start += pairs * PAIR
    out_ref[:, start:] = g_ref[...].astype(low)


def pack_attention(core, weights, gains):
    _, shard, width = weights.shape
    half = width // 2
    gain_columns = jnp.pad(gains.T, ((0, 0), (0, HEAD_DIM - 3)))
    columns = 4 * half + HEAD_DIM
    return pl.pallas_call(
        pack_kernel,
        grid_spec=pltpu.PrefetchScalarGridSpec(
            num_scalar_prefetch=1,
            grid=(1,),
            in_specs=[
                pl.BlockSpec((4, shard, half), lambda j, core: (0, 0, core[0])),
                whole((shard, HEAD_DIM)),
            ],
            out_specs=whole((shard, columns)),
        ),
        out_shape=jax.ShapeDtypeStruct((shard, columns), low),
        name="pack_attention",
    )(core, weights, gain_columns)


RING = 8


def ring_place(index):
    return jnp.where(index % 2 == 0, index // 2, RING - 1 - index // 2)


def ring_member(place):
    place = place % RING
    return jnp.where(place < RING // 2, 2 * place, 2 * RING - 1 - 2 * place)


def ring_next(tensor):
    cycle = [0, 2, 4, 6, 7, 5, 3, 1]
    replicas = lax.axis_size("dp")
    pairs = []
    for place, member in enumerate(cycle):
        for replica in range(replicas):
            target = cycle[(place + (1 if replica % 2 == 0 else -1)) % RING]
            pairs.append((member * replicas + replica, target * replicas + replica))
    return lax.ppermute(tensor, ("fsdp", "dp"), pairs)


def core_swap(tensor):
    return lax.ppermute(tensor, "dp", [(d, d ^ 1) for d in range(lax.axis_size("dp"))])


def column_swap(tensor):
    return lax.ppermute(tensor, "dp", [(d, d ^ 2) for d in range(lax.axis_size("dp"))])


def assemble_kernel(origin_ref, *refs):
    pieces, out_ref = refs[:RING], refs[RING]
    rows = pieces[0].shape[0]
    for step, piece in enumerate(pieces):
        start = pl.multiple_of(origin_ref[step] * rows, 16)
        out_ref[pl.ds(start, rows), :] = piece[...]


def assemble(origins, pieces):
    rows, columns = pieces[0].shape
    return pl.pallas_call(
        assemble_kernel,
        grid_spec=pltpu.PrefetchScalarGridSpec(
            num_scalar_prefetch=1,
            grid=(1,),
            in_specs=[whole((rows, columns))] * RING,
            out_specs=whole((RING * rows, columns)),
        ),
        out_shape=jax.ShapeDtypeStruct((RING * rows, columns), pieces[0].dtype),
        compiler_params=pltpu.CompilerParams(vmem_limit_bytes=VMEM_BYTES),
        cost_estimate=pl.CostEstimate(
            flops=0, bytes_accessed=4 * RING * rows * columns, transcendentals=0
        ),
        name="assemble",
    )(origins, *pieces)


def after(tensor, *others):
    return lax.optimization_barrier((tensor, *others))[0]


def core_way():
    return 1 - 2 * (lax.axis_index("dp") % 2)


def ring_origins():
    place = ring_place(lax.axis_index("fsdp"))
    return ring_member(
        place - core_way() * jnp.arange(RING, dtype=jnp.int32) + RING
    ).astype(jnp.int32)


class RingGather:
    def __init__(self, shard):
        self.pieces = [shard]

    def step(self, *others):
        source = after(self.pieces[-1], *others) if others else self.pieces[-1]
        self.pieces.append(ring_next(source))

    def last(self):
        return self.pieces[-1]


class RingSum:
    def __init__(self, mine, arrived):
        self.mine, self.arrived = mine, arrived
        place = ring_place(lax.axis_index("fsdp"))
        self.owners = [ring_member(place - core_way() * (s + 1) + 2 * RING) for s in range(RING)]
        self.totals = []

    def term(self):
        parts = []
        for own, arrived in zip(self.mine, self.arrived):
            rows = own.shape[0] // RING
            start = self.owners[len(self.totals)] * rows
            part = lax.dynamic_slice_in_dim(own, start, rows, 0).astype(wide)
            parts.append(part + lax.dynamic_slice_in_dim(arrived, start, rows, 0).astype(wide))
        return parts[0] if len(parts) == 1 else jnp.concatenate(parts, axis=0)

    def step(self, *others):
        if not self.totals:
            self.totals.append(self.term().astype(low))
        total = self.totals[-1]
        moved = ring_next(after(total, *others) if others else total)
        self.totals.append((moved.astype(wide) + self.term()).astype(low))

    def last(self):
        return self.totals[-1]


class Turns:
    def __init__(self):
        self.results = []

    def step(self, ring, *others):
        ring.step(*self.results[-2:-1], *others)
        self.results.append(ring.last())


def gather_rows(shard):
    mine = lax.all_gather(shard, "fsdp", axis=0, tiled=True)
    return mine, core_swap(mine)


def reduce_rows(mine, arrived):
    totals = []
    for own, theirs in zip(mine, arrived):
        both = (own.astype(wide) + theirs.astype(wide)).astype(low)
        totals.append(lax.psum_scatter(both, "fsdp", scatter_dimension=0, tiled=True))
    return totals[0] if len(totals) == 1 else jnp.concatenate(totals, axis=0)


def sum_everywhere(tensor):
    distance = 1
    while distance < lax.axis_size("dp"):
        pairs = [(d, d ^ distance) for d in range(lax.axis_size("dp"))]
        tensor = tensor + lax.ppermute(tensor, "dp", pairs)
        distance *= 2
    distance = 1
    while distance < lax.axis_size("fsdp"):
        pairs = [(f, f ^ distance) for f in range(lax.axis_size("fsdp"))]
        tensor = tensor + lax.ppermute(tensor, "fsdp", pairs)
        distance *= 2
    return tensor


def on_device(
    inputs,
    cotangent,
    lengths,
    attention_weights,
    attention_momentum,
    attention_average,
    ffn_inputs,
    ffn_inputs_momentum,
    ffn_inputs_average,
    ffn_output,
    ffn_output_momentum,
    ffn_output_average,
    gains,
    gains_momentum,
    gains_average,
):
    micro_count, slot, width = inputs.shape
    hidden = ffn_inputs.shape[2]
    shard = ffn_inputs.shape[1]
    down_rows = ffn_output.shape[0]
    fsdp_size = lax.axis_size("fsdp")
    replicas = lax.axis_size("dp")
    ringed = fsdp_size == RING
    core = lax.axis_index("dp") % 2
    column = lax.axis_index("dp") // 2
    me = lax.axis_index("fsdp")
    count = micro_count * slot
    half = width // 2
    core_ref = core.astype(jnp.int32).reshape(1)
    other_ref = 1 - core_ref
    is_first = core == 0

    packed = pack_attention(core_ref, attention_weights, gains)
    up_half = lax.dynamic_index_in_dim(ffn_inputs, core, 0, keepdims=False).astype(low)
    up_half = up_half.reshape(shard, fsdp_size, 2, down_rows // 2)
    up_half = lax.dynamic_index_in_dim(up_half, column, 2, keepdims=False)
    up_half = up_half.reshape(shard, hidden // 2)
    down_half = lax.dynamic_slice(
        ffn_output, (column * (down_rows // 2), core * half), (down_rows // 2, half)
    ).astype(low)

    rows = inputs.reshape(count, width)
    positions = jnp.arange(slot, dtype=jnp.int32)
    valid = (positions[None, :] < lengths).astype(wide).reshape(count, 1)
    errors = (cotangent.reshape(count, width).astype(wide) * valid).astype(low)
    errors_there = column_swap(errors)

    def gains_of(weights):
        gain_rows = weights[:, 4 * half : 4 * half + 3].T.astype(wide)
        return jnp.pad(gain_rows, ((0, 5), (0, 0)))

    if ringed:
        origins = ring_origins()
        rings = [RingGather(packed), RingGather(up_half), RingGather(down_half)]
        turns = Turns()
        for step in range(1, RING):
            for ring in rings:
                turns.step(ring)
        mine = [assemble(origins, ring.pieces) for ring in rings]
        w_a, w_gu, w_d = [(part, core_swap(part)) for part in mine]
        rows = after(rows, errors_there, w_gu[0], w_d[0])
    else:
        w_a, w_gu, w_d = gather_rows(packed), gather_rows(up_half), gather_rows(down_half)
    gains8 = gains_of(w_a[0])
    mixed_mine, *kept_mine = mixer_forward(core_ref, rows, w_a[0], gains8, slot)
    mixed_other, *rest = mixer_forward(
        other_ref, rows, w_a[1], gains8, slot, (mixed_mine, w_a[0])
    )
    kept_other, (x1, h2, h1t) = rest[:4], rest[4:]
    mixed = (mixed_mine, mixed_other)

    h2_there = [column_swap(h2[m * slot : (m + 1) * slot]) for m in range(micro_count)]
    products = [ffn_rows(core_ref, h2, errors, slot, 0, micro_count, w_gu, w_d, wide)]
    x2_there, dh_back = [], []
    for m in range(micro_count):
        part = ffn_rows(core_ref, h2_there[m], errors_there, slot, m, 1, w_gu, w_d, low)
        dh_back.append(column_swap(part[4]))
        x2_there.append(part[3])
        products.append(part)
    mids, owns, swaps = [[part[which] for part in products] for which in range(3)]
    grad_ffn = ffn_weights(
        core_ref, (h2, *h2_there), (errors, errors_there), mids, owns, swaps
    )
    x2_back = [column_swap(part) for part in x2_there]
    d_x1, d_mixed, go_mine, go_other, grad_two = middle_backward(
        core_ref, after(x1, grad_ffn[0]), errors, products[0][4], dh_back, mixed, w_a, gains8
    )
    block_out = x1 + products[0][3] + jnp.concatenate(x2_back, axis=0).astype(wide)
    output = (block_out * valid).astype(low)

    gm, gu, gd_mine, gd_other = grad_ffn
    mine_gu, arrived_gu = [gm], [core_swap(gu)]
    mine_do, arrived_do = [gd_mine, go_mine], [core_swap(gd_other), core_swap(go_other)]
    grad_other, ggo_other, dpre_other = mixer_backward(
        other_ref, h1t, gains8, kept_other, d_mixed, slot
    )
    arrived_qfv = [core_swap(grad_other)]
    if ringed:
        sum_gu = RingSum(mine_gu, arrived_gu)
        sum_do = RingSum(mine_do, arrived_do)
        turns = Turns()
        turns.step(sum_gu, dpre_other)
        turns.step(sum_do, dpre_other)
        h1t = after(h1t, sum_gu.totals[0], sum_do.totals[0])
    grad_mine, ggo_mine, dpre_mine = mixer_backward(
        core_ref, h1t, gains8, kept_mine, d_mixed, slot
    )
    ggo_left = jnp.where(is_first, ggo_mine, ggo_other)
    ggo_right = jnp.where(is_first, ggo_other, ggo_mine)
    grad_go = jnp.concatenate([ggo_left, ggo_right], axis=1)

    def finish_input(d_pre):
        gradient, grad_one = input_gradient(rows, gains8, (d_pre, dpre_other), w_a, d_x1)
        stacked = jnp.concatenate([grad_one, grad_go, grad_two], axis=0)
        return gradient, sum_everywhere(stacked)

    mine_qfv = [grad_mine]
    if ringed:
        sum_qfv = RingSum(mine_qfv, arrived_qfv)
        order = [sum_gu, sum_do, sum_qfv] * 6 + [sum_qfv]
        for place, ring in enumerate(order):
            if place == 8:
                late = after(dpre_mine, turns.results[-2])
                input_grad, gain_grads = finish_input(late)
            others = [gain_grads] if place == 16 else []
            if place == 2:
                others.append(grad_mine)
            turns.step(ring, *others)
        total_gu, total_do, total_qfv = sum_gu.last(), sum_do.last(), sum_qfv.last()
    else:
        total_gu = reduce_rows(mine_gu, arrived_gu)
        total_do = reduce_rows(mine_do, arrived_do)
        total_qfv = reduce_rows(mine_qfv, arrived_qfv)
        input_grad, gain_grads = finish_input(dpre_mine)

    def by_column(own, there):
        return jnp.where(column == 0, own, there), jnp.where(column == 0, there, own)

    parts = by_column(total_gu, column_swap(total_gu))
    parts = [part.reshape(shard, fsdp_size, 1, down_rows // 2) for part in parts]
    sum_gu = jnp.concatenate(parts, axis=2).reshape(shard, hidden)
    sum_gu = (sum_gu, core_swap(sum_gu))
    there_do = column_swap(total_do)
    cut = down_rows // 2
    parts = by_column(total_do[:cut], there_do[:cut])
    sum_o = (total_do[cut:].astype(wide) + there_do[cut:].astype(wide)).astype(low)
    sum_d = jnp.concatenate(parts, axis=0)
    sum_d, sum_o = (sum_d, core_swap(sum_d)), (sum_o, core_swap(sum_o))
    sum_qfv = (total_qfv.astype(wide) + column_swap(total_qfv).astype(wide)).astype(low)
    sum_qfv = (sum_qfv, core_swap(sum_qfv))
    sum_gains = lax.dynamic_slice_in_dim(gain_grads, me * gains.shape[1], gains.shape[1], 1)

    scale_rows = 1.0 / math.sqrt(count * fsdp_size * replicas)
    attention_state = (attention_weights, attention_momentum, attention_average)
    ffn_in_state = (ffn_inputs, ffn_inputs_momentum, ffn_inputs_average)
    ffn_out_state = (ffn_output, ffn_output_momentum, ffn_output_average)
    return (
        output.reshape(micro_count, slot, width),
        input_grad.reshape(micro_count, slot, width),
        *update_attention(core_ref, attention_state, sum_qfv, sum_o, matrix_rate * scale_rows),
        *update_ffn_in(core_ref, ffn_in_state, sum_gu, matrix_rate * scale_rows),
        *update_ffn_out(core_ref, ffn_out_state, sum_d, matrix_rate * scale_rows),
        *update(gains, gains_momentum, gains_average, sum_gains, gain_rate * scale_rows),
    )


def solution(mesh):
    rows_split = P(None, ("fsdp", "dp"), None)
    middle_split = P(None, "fsdp", None)
    first_split = P("fsdp", None)
    gains_split = P(None, "fsdp")
    in_specs = (
        (rows_split, rows_split, P(None, ("fsdp", "dp")))
        + (middle_split,) * 6
        + (first_split,) * 3
        + (gains_split,) * 3
    )
    out_specs = (
        (rows_split, rows_split)
        + (middle_split,) * 6
        + (first_split,) * 3
        + (gains_split,) * 3
    )
    return jax.shard_map(
        on_device, mesh=mesh, in_specs=in_specs, out_specs=out_specs, check_vma=False
    )
```

```python
import functools
import math

import jax
import jax.numpy as jnp
from jax import lax
from jax.experimental import pallas as pl
from jax.experimental.pallas import tpu as pltpu
from jax.sharding import PartitionSpec as P

HEAD_DIM = 128
PAIR = 2 * HEAD_DIM

lower_bound = 0.9
momentum_decay = 0.9
average_decay = 0.7
weight_decay = 0.0005
matrix_rate = 0.03
gain_rate = 0.1
low = jnp.bfloat16
wide = jnp.float32
TILE_F = 256
VMEM_BYTES = 60 * 1024 * 1024


def mm(left, right):
    return jnp.dot(left, right, preferred_element_type=wide)


def mm_nt(left, right):
    return lax.dot_general(left, right, (((1,), (1,)), ((), ())), preferred_element_type=wide)


def mm_tn(left, right):
    return lax.dot_general(left, right, (((0,), (0,)), ((), ())), preferred_element_type=wide)


def sigmoid(u):
    return 0.5 * jnp.tanh(0.5 * u) + 0.5


def whole(shape):
    return pl.BlockSpec(shape, lambda *_: (0,) * len(shape), pipeline_mode=pl.Buffered(1))


def split_sum(ones_matrix, tensor):
    high = tensor.astype(low)
    rest = (tensor - high.astype(wide)).astype(low)
    return mm(ones_matrix, high) + mm(ones_matrix, rest)


def triangle(length, lower):
    rows = lax.broadcasted_iota(jnp.int32, (length, length), 0)
    columns = lax.broadcasted_iota(jnp.int32, (length, length), 1)
    kept = rows >= columns if lower else rows <= columns
    return kept.astype(wide).astype(low)


def decay_parts(f_pre, lower_ones):
    share = sigmoid(f_pre)
    gate = lower_bound + (1.0 - lower_bound) * share
    keys_in = (1.0 - lower_bound) * (1.0 - share)
    cumulative = split_sum(lower_ones, jnp.log(gate))
    middle_row = cumulative.shape[0] // 2
    cumulative = cumulative - cumulative[middle_row : middle_row + 1, :]
    return share, gate, keys_in, cumulative


def first_norm(x_ref, gain_row):
    rows = x_ref[...].astype(wide)
    scale = lax.rsqrt(jnp.mean(rows * rows, axis=-1, keepdims=True) + 1e-06)
    return rows * scale, scale


def lanes_of(half, size):
    return pl.ds(pl.multiple_of(half * size, size), size)


def mixer_forward_kernel(
    slot, half_ref, x_ref, w_ref, g_ref, on_ref, q_ref, f_ref, v_ref, o_ref, h_s
):
    @pl.when(pl.program_id(0) == 0)
    def _():
        normed, _ = first_norm(x_ref, None)
        h_s[...] = (normed * g_ref[0:1, :]).astype(low)

    gain_o = g_ref[1:2, lanes_of(half_ref[0] * pl.num_programs(0) + pl.program_id(0), PAIR)]
    pre = mm(h_s[...], w_ref[...])
    q_ref[...] = pre[:, :PAIR]
    f_ref[...] = pre[:, PAIR : 2 * PAIR]
    v_ref[...] = pre[:, 2 * PAIR :].astype(low)
    lower_ones = triangle(slot, True)
    block_rows = lax.broadcasted_iota(jnp.int32, (HEAD_DIM, HEAD_DIM), 0)
    block_columns = lax.broadcasted_iota(jnp.int32, (HEAD_DIM, HEAD_DIM), 1)
    causal = block_rows >= block_columns
    for sequence in range(x_ref.shape[0] // slot):
        rows = slice(sequence * slot, (sequence + 1) * slot)
        q_pre = q_ref[rows, :]
        _, _, keys_in, cumulative = decay_parts(f_ref[rows, :], lower_ones)
        grown = jnp.exp(-cumulative)
        decayed_q = (q_pre * sigmoid(q_pre) * jnp.exp(cumulative)).astype(low)
        grown_k = (keys_in * grown).astype(low)
        values = v_ref[rows, :]
        for head in range(2):
            lanes = slice(head * HEAD_DIM, (head + 1) * HEAD_DIM)
            for block in range(slot // HEAD_DIM):
                start, end = block * HEAD_DIM, (block + 1) * HEAD_DIM
                q_block = decayed_q[start:end, lanes]
                diagonal = mm_nt(q_block, grown_k[start:end, lanes])
                diagonal = jnp.where(causal, diagonal, 0.0).astype(low)
                out = mm(diagonal, values[start:end, lanes])
                if block > 0:
                    scores = mm_nt(q_block, grown_k[:start, lanes]).astype(low)
                    out = out + mm(scores, values[:start, lanes])
                scale = lax.rsqrt(jnp.mean(out * out, axis=-1, keepdims=True) + 1e-05)
                target = slice(sequence * slot + start, sequence * slot + end)
                o_ref[target, lanes] = out
                on_ref[target, lanes] = (out * scale * gain_o[:, lanes]).astype(low)


def mixer_forward_last_kernel(
    slot,
    half_ref,
    x_ref,
    w_ref,
    g_ref,
    before_ref,
    woo_ref,
    wom_ref,
    on_ref,
    q_ref,
    f_ref,
    v_ref,
    o_ref,
    x1_ref,
    h2_ref,
    h2t_ref,
    h1t_ref,
    h_s,
    on_s,
):
    step = pl.program_id(0)
    half = before_ref.shape[1]
    mixer_forward_kernel(
        slot, half_ref, x_ref, w_ref, g_ref, on_ref, q_ref, f_ref, v_ref, o_ref, h_s
    )
    on_s[:, lanes_of(half_ref[0] * pl.num_programs(0) + step, PAIR)] = on_ref[...]

    @pl.when(step == pl.num_programs(0) - 1)
    def _():
        here = lanes_of(half_ref[0], half)
        there = lanes_of(1 - half_ref[0], half)
        on_s[:, there] = before_ref[...]
        h1t_ref[...] = h_s[...].astype(wide).T.astype(low)
        x1_ref[:, here] = x_ref[:, here].astype(wide) + mm(on_s[...], woo_ref[...])
        x1_ref[:, there] = x_ref[:, there].astype(wide) + mm(on_s[...], wom_ref[...])
        x1 = x1_ref[...]
        scale = lax.rsqrt(jnp.mean(x1 * x1, axis=-1, keepdims=True) + 1e-06)
        normed = x1 * scale * g_ref[2:3, :]
        h2_ref[...] = normed.astype(low)
        h2t_ref[...] = normed.T.astype(low)


def mixer_forward(half, rows, weights, gains8, slot, ending=None):
    count, width = rows.shape
    pairs = width // PAIR // 2
    by_pair = pl.BlockSpec((count, PAIR), lambda j, _: (0, j))
    struct = jax.ShapeDtypeStruct
    shape = lambda kind: struct((count, width // 2), kind)
    kernel = mixer_forward_kernel
    in_specs = [
        whole(rows.shape),
        pl.BlockSpec((width, 3 * PAIR), lambda j, _: (0, j)),
        whole(gains8.shape),
    ]
    operands = [half, rows, weights, gains8]
    out_specs = [by_pair] * 5
    out_shape = [shape(low), shape(wide), shape(wide), shape(low), shape(wide)]
    scratch = [pltpu.VMEM((count, width), low)]
    if ending is not None:
        kernel = mixer_forward_last_kernel
        out_weights = pl.BlockSpec((width, width // 2), lambda j, _: (0, 3))
        in_specs += [whole((count, width // 2)), out_weights, out_weights]
        operands += [ending[0], weights, ending[1]]
        out_specs += [whole((count, width))] * 2 + [whole((width, count))] * 2
        out_shape += [
            struct((count, width), wide),
            struct((count, width), low),
            struct((width, count), low),
            struct((width, count), low),
        ]
        scratch += [pltpu.VMEM((count, width), low)]
    return pl.pallas_call(
        functools.partial(kernel, slot),
        grid_spec=pltpu.PrefetchScalarGridSpec(
            num_scalar_prefetch=1,
            grid=(pairs,),
            in_specs=in_specs,
            out_specs=out_specs,
            scratch_shapes=scratch,
        ),
        out_shape=out_shape,
        compiler_params=pltpu.CompilerParams(vmem_limit_bytes=VMEM_BYTES),
        cost_estimate=pl.CostEstimate(
            flops=count * width * 4 * width + 10 * count * slot * width,
            bytes_accessed=count * width * 12 + width * width * 4,
            transcendentals=count * width * 3,
        ),
        name="mixer_forward",
    )(*operands)


def ffn_tile(
    core_ref, h_ref, ht_ref, e_ref, wm_ref, wu_ref, wdm_ref, wdo_ref, grads, acc_ref, dh_ref
):
    gm_ref, gu_ref, gdm_ref, gdo_ref = grads
    half = wdm_ref.shape[1]
    first = core_ref[0] == 0
    mine = lanes_of(core_ref[0], half)
    other = lanes_of(1 - core_ref[0], half)
    own = mm(h_ref[...], wm_ref[...])
    swapped = mm(h_ref[...], wu_ref[...])
    a = jnp.where(first, own, swapped)
    b = jnp.where(first, swapped, own)
    share = sigmoid(a)
    swish = a * share
    mid = (swish * b).astype(low)
    acc_ref[:, mine] += mm(mid, wdm_ref[...])
    acc_ref[:, other] += mm(mid, wdo_ref[...])
    d_mid = mm_nt(e_ref[:, mine], wdm_ref[...]) + mm_nt(e_ref[:, other], wdo_ref[...])
    gdm_ref[...] = mm_tn(mid, e_ref[:, mine]).astype(low)
    gdo_ref[...] = mm_tn(mid, e_ref[:, other]).astype(low)
    d_a = (d_mid * b * share * (1.0 + a * (1.0 - share))).astype(low)
    d_b = (d_mid * swish).astype(low)
    d_own = jnp.where(first, d_a, d_b)
    d_swapped = jnp.where(first, d_b, d_a)
    gm_ref[...] = mm(ht_ref[...], d_own).astype(low)
    gu_ref[...] = mm(ht_ref[...], d_swapped).astype(low)
    dh_ref[...] += mm_nt(d_own, wm_ref[...]) + mm_nt(d_swapped, wu_ref[...])


def ffn_kernel(
    core_ref,
    h_ref,
    ht_ref,
    e_ref,
    wm_ref,
    wu_ref,
    wdm_ref,
    wdo_ref,
    x1_ref,
    onm_ref,
    ono_ref,
    wom_ref,
    woo_ref,
    m_ref,
    g_ref,
    gm_ref,
    gu_ref,
    gdm_ref,
    gdo_ref,
    out_ref,
    dh_s,
    acc_s,
    gom_ref,
    goo_ref,
    g2_ref,
    on_s,
):
    @pl.when(pl.program_id(0) == 0)
    def _():
        acc_s[...] = x1_ref[...]
        dh_s[...] = jnp.zeros_like(dh_s)

    grads = (gm_ref, gu_ref, gdm_ref, gdo_ref)
    ffn_tile(
        core_ref, h_ref, ht_ref, e_ref, wm_ref, wu_ref, wdm_ref, wdo_ref, grads, acc_s, dh_s
    )

    @pl.when(pl.program_id(0) == pl.num_programs(0) - 1)
    def _():
        half = onm_ref.shape[1]
        mine = lanes_of(core_ref[0], half)
        other = lanes_of(1 - core_ref[0], half)
        out_ref[...] = (acc_s[...] * m_ref[...]).astype(low)
        x1 = x1_ref[...]
        scale = lax.rsqrt(jnp.mean(x1 * x1, axis=-1, keepdims=True) + 1e-06)
        normed = x1 * scale
        d_h2 = dh_s[...]
        scaled = d_h2 * g_ref[2:3, :]
        g2_ref[...] = jnp.sum(d_h2 * normed, axis=0, keepdims=True)
        d_x1 = e_ref[...].astype(wide) + scale * (
            scaled - normed * jnp.mean(scaled * normed, axis=-1, keepdims=True)
        )
        dh_s[...] = d_x1
        on_s[...] = d_x1.astype(low)
        acc_s[...] = mm_nt(on_s[:, mine], wom_ref[...]) + mm_nt(on_s[:, other], woo_ref[...])
        onm, ono = onm_ref[...], ono_ref[...]
        d_mine, d_other = on_s[:, mine], on_s[:, other]
        here = pl.ds(pl.multiple_of(core_ref[0] * half, half), half)
        there = pl.ds(pl.multiple_of((1 - core_ref[0]) * half, half), half)
        gom_ref[here, :] = mm_tn(onm, d_mine).astype(low)
        gom_ref[there, :] = mm_tn(ono, d_mine).astype(low)
        goo_ref[here, :] = mm_tn(onm, d_other).astype(low)
        goo_ref[there, :] = mm_tn(ono, d_other).astype(low)


def ffn(core, h2, h2t, errors, w_gu, w_d, x1, mixed, w_a, mask, gains8):
    count, width = h2.shape
    half = width // 2
    hidden = w_gu[0].shape[1]
    full = whole((count, width))
    half_full = whole((count, half))
    square = whole((width, half))
    in_tile = pl.BlockSpec((width, TILE_F), lambda j, _: (0, j))
    out_tile = pl.BlockSpec((TILE_F, half), lambda j, _: (j, 0))
    out_weights = pl.BlockSpec((width, half), lambda j, _: (0, 3), pipeline_mode=pl.Buffered(1))
    struct = jax.ShapeDtypeStruct
    return pl.pallas_call(
        ffn_kernel,
        grid_spec=pltpu.PrefetchScalarGridSpec(
            num_scalar_prefetch=1,
            grid=(hidden // TILE_F,),
            in_specs=[full, whole(h2t.shape), full, in_tile, in_tile, out_tile, out_tile]
            + [full, half_full, half_full, out_weights, out_weights]
            + [whole((count, 1)), whole((8, width))],
            out_specs=[in_tile, in_tile, out_tile, out_tile]
            + [full, full, full, square, square, whole((1, width))],
            scratch_shapes=[pltpu.VMEM((count, width), low)],
        ),
        out_shape=[struct((width, hidden), low)] * 2
        + [struct((hidden, half), low)] * 2
        + [
            struct((count, width), low),
            struct((count, width), wide),
            struct((count, width), wide),
            struct((width, half), low),
            struct((width, half), low),
            struct((1, width), wide),
        ],
        compiler_params=pltpu.CompilerParams(vmem_limit_bytes=VMEM_BYTES),
        cost_estimate=pl.CostEstimate(
            flops=16 * count * width * hidden,
            bytes_accessed=count * width * 20 + width * hidden * 12,
            transcendentals=count * hidden,
        ),
        name="ffn",
    )(core, h2, h2t, errors, *w_gu, *w_d, x1, *mixed, *w_a, mask, gains8)


def mixer_backward_kernel(
    slot,
    half_ref,
    ht_ref,
    g_ref,
    q_ref,
    f_ref,
    v_ref,
    o_ref,
    don_ref,
    grad_ref,
    ggo_ref,
    dpre_ref,
):
    gain_o = g_ref[1:2, lanes_of(half_ref[0] * pl.num_programs(0) + pl.program_id(0), PAIR)]
    lower_ones = triangle(slot, True)
    upper_ones = triangle(slot, False)
    block_rows = lax.broadcasted_iota(jnp.int32, (HEAD_DIM, HEAD_DIM), 0)
    block_columns = lax.broadcasted_iota(jnp.int32, (HEAD_DIM, HEAD_DIM), 1)
    causal = block_rows >= block_columns
    causal_t = block_rows <= block_columns
    blocks = slot // HEAD_DIM
    ggo_total = jnp.zeros((1, PAIR), wide)
    for sequence in range(q_ref.shape[0] // slot):
        rows = slice(sequence * slot, (sequence + 1) * slot)
        d_on = don_ref[rows, :]
        out = o_ref[rows, :]
        d_out_parts = []
        ggo_parts = []
        for head in range(2):
            lanes = slice(head * HEAD_DIM, (head + 1) * HEAD_DIM)
            out_h, d_on_h = out[:, lanes], d_on[:, lanes]
            scale = lax.rsqrt(jnp.mean(out_h * out_h, axis=-1, keepdims=True) + 1e-05)
            normed = out_h * scale
            ggo_parts.append(jnp.sum(d_on_h * normed, axis=0, keepdims=True))
            scaled = d_on_h * gain_o[:, lanes]
            inner = jnp.mean(scaled * normed, axis=-1, keepdims=True)
            d_out_parts.append((scale * (scaled - normed * inner)).astype(low))
        ggo_total = ggo_total + jnp.concatenate(ggo_parts, axis=1)

        q_pre = q_ref[rows, :]
        share, gate, keys_in, cumulative = decay_parts(f_ref[rows, :], lower_ones)
        grown = jnp.exp(-cumulative)
        shrunk = jnp.exp(cumulative)
        q_share = sigmoid(q_pre)
        decayed_q = (q_pre * q_share * shrunk).astype(low)
        grown_k = (keys_in * grown).astype(low)
        values = v_ref[rows, :]
        dq_parts, dk_parts, dv_parts = [], [], []
        for head in range(2):
            lanes = slice(head * HEAD_DIM, (head + 1) * HEAD_DIM)
            q_h, k_h, v_h = decayed_q[:, lanes], grown_k[:, lanes], values[:, lanes]
            d_out = d_out_parts[head]
            dq_blocks, dk_blocks, dv_blocks = [], [], []
            for block in range(blocks):
                start, end = block * HEAD_DIM, (block + 1) * HEAD_DIM
                here = slice(start, end)
                d_scores = mm_nt(d_out[here], v_h[here])
                d_scores = jnp.where(causal, d_scores, 0.0).astype(low)
                d_q = mm(d_scores, k_h[here])
                if block > 0:
                    before = slice(0, start)
                    d_scores = mm_nt(d_out[here], v_h[before]).astype(low)
                    d_q = d_q + mm(d_scores, k_h[before])
                dq_blocks.append(d_q)
                scores = jnp.where(causal_t, mm_nt(k_h[here], q_h[here]), 0.0).astype(low)
                d_scores = jnp.where(causal_t, mm_nt(v_h[here], d_out[here]), 0.0).astype(low)
                d_v = mm(scores, d_out[here])
                d_k = mm(d_scores, q_h[here])
                if block < blocks - 1:
                    after = slice(end, slot)
                    scores = mm_nt(k_h[here], q_h[after]).astype(low)
                    d_scores = mm_nt(v_h[here], d_out[after]).astype(low)
                    d_v = d_v + mm(scores, d_out[after])
                    d_k = d_k + mm(d_scores, q_h[after])
                dk_blocks.append(d_k)
                dv_blocks.append(d_v)
            dq_parts.append(jnp.concatenate(dq_blocks, axis=0))
            dk_parts.append(jnp.concatenate(dk_blocks, axis=0))
            dv_parts.append(jnp.concatenate(dv_blocks, axis=0))
        d_decayed = jnp.concatenate(dq_parts, axis=1)
        d_grown = jnp.concatenate(dk_parts, axis=1)
        d_value = jnp.concatenate(dv_parts, axis=1)
        d_cumulative = decayed_q.astype(wide) * d_decayed - grown_k.astype(wide) * d_grown
        d_log = split_sum(upper_ones, d_cumulative)
        d_query = d_decayed * shrunk
        d_key = d_grown * grown
        d_q_pre = d_query * q_share * (1.0 + q_pre * (1.0 - q_share))
        d_f_pre = (1.0 - lower_bound) * (d_log / gate - d_key) * share * (1.0 - share)
        dpre_ref[rows, :PAIR] = d_q_pre.astype(low)
        dpre_ref[rows, PAIR : 2 * PAIR] = d_f_pre.astype(low)
        dpre_ref[rows, 2 * PAIR :] = d_value.astype(low)

    ggo_ref[...] = ggo_total
    grad_ref[...] = mm(ht_ref[...], dpre_ref[...]).astype(low)


def mixer_backward(half, h1t, gains8, kept, d_mixed, slot):
    width, count = h1t.shape
    pairs = width // PAIR // 2
    by_pair = pl.BlockSpec((count, PAIR), lambda j, _: (0, j))
    from_half = pl.BlockSpec((count, PAIR), lambda j, half: (0, half[0] * pairs + j))
    struct = jax.ShapeDtypeStruct
    return pl.pallas_call(
        functools.partial(mixer_backward_kernel, slot),
        grid_spec=pltpu.PrefetchScalarGridSpec(
            num_scalar_prefetch=1,
            grid=(pairs,),
            in_specs=[whole((width, count)), whole(gains8.shape)] + [by_pair] * 4 + [from_half],
            out_specs=[
                pl.BlockSpec((width, 3 * PAIR), lambda j, _: (0, j)),
                pl.BlockSpec((1, PAIR), lambda j, _: (0, j)),
                pl.BlockSpec((count, 3 * PAIR), lambda j, _: (0, j)),
            ],
        ),
        out_shape=[
            struct((width, 3 * width // 2), low),
            struct((1, width // 2), wide),
            struct((count, 3 * width // 2), low),
        ],
        compiler_params=pltpu.CompilerParams(vmem_limit_bytes=VMEM_BYTES),
        cost_estimate=pl.CostEstimate(
            flops=count * width * 3 * width + 20 * count * slot * width,
            bytes_accessed=count * width * 12 + width * width * 3,
            transcendentals=count * width * 4,
        ),
        name="mixer_backward",
    )(half, h1t, gains8, *kept, d_mixed)


def input_gradient_kernel(x_ref, g_ref, dm_ref, do_ref, wm_ref, wo_ref, dx1_ref, dx_ref, g1_ref, dh_s):
    step = pl.program_id(0)
    pairs = pl.num_programs(0) // 2

    @pl.when(step == 0)
    def _():
        dh_s[...] = mm_nt(do_ref[...], wo_ref[...])

    @pl.when(jnp.logical_and(step > 0, step < pairs))
    def _():
        dh_s[...] += mm_nt(do_ref[...], wo_ref[...])

    @pl.when(step >= pairs)
    def _():
        dh_s[...] += mm_nt(dm_ref[...], wm_ref[...])

    @pl.when(step == 2 * pairs - 1)
    def _():
        normed, scale = first_norm(x_ref, None)
        d_h1 = dh_s[...]
        scaled = d_h1 * g_ref[0:1, :]
        g1_ref[...] = jnp.sum(d_h1 * normed, axis=0, keepdims=True)
        dx_ref[...] = dx1_ref[...] + scale * (
            scaled - normed * jnp.mean(scaled * normed, axis=-1, keepdims=True)
        )


def input_gradient(rows, gains8, d_pre, weights, d_x1):
    count, width = rows.shape
    pairs = width // PAIR // 2
    full = whole((count, width))
    first = lambda j: (0, jnp.maximum(j - pairs, 0))
    second = lambda j: (0, jnp.minimum(j, pairs - 1))
    struct = jax.ShapeDtypeStruct
    return pl.pallas_call(
        input_gradient_kernel,
        grid=(2 * pairs,),
        in_specs=[
            full,
            whole(gains8.shape),
            pl.BlockSpec((count, 3 * PAIR), first),
            pl.BlockSpec((count, 3 * PAIR), second),
            pl.BlockSpec((width, 3 * PAIR), first),
            pl.BlockSpec((width, 3 * PAIR), second),
            full,
        ],
        out_specs=[full, whole((1, width))],
        out_shape=[struct((count, width), wide), struct((1, width), wide)],
        scratch_shapes=[pltpu.VMEM((count, width), wide)],
        compiler_params=pltpu.CompilerParams(vmem_limit_bytes=VMEM_BYTES),
        cost_estimate=pl.CostEstimate(
            flops=6 * count * width * width,
            bytes_accessed=count * width * 16 + width * width * 6,
            transcendentals=0,
        ),
        name="input_gradient",
    )(rows, gains8, *d_pre, *weights, d_x1)


def update(weight, momentum, average, gradient, step_rate):
    new_momentum = momentum_decay * momentum + gradient
    direction = gradient + momentum_decay * new_momentum + weight_decay * weight
    new_weight = weight - step_rate * direction
    new_average = average_decay * average + (1.0 - average_decay) * new_weight
    return (new_momentum, new_average, new_weight)


def update_kernel(pick, step_rate, core_ref, w_ref, m_ref, a_ref, *refs):
    sums, outs = refs[:-3], refs[-3:]
    gradient = pick(core_ref[0], *[s[...] for s in sums]).astype(wide).reshape(w_ref.shape)
    results = update(w_ref[...], m_ref[...], a_ref[...], gradient, step_rate)
    for out, result in zip(outs, results):
        out[...] = result


def update_call(core, state, sums, grid, state_spec, sum_specs, pick, step_rate, name):
    struct = jax.ShapeDtypeStruct(state[0].shape, wide)
    size = math.prod(state[0].shape)
    return pl.pallas_call(
        functools.partial(update_kernel, pick, step_rate),
        grid_spec=pltpu.PrefetchScalarGridSpec(
            num_scalar_prefetch=1,
            grid=grid,
            in_specs=[state_spec] * 3 + sum_specs,
            out_specs=[state_spec] * 3,
        ),
        out_shape=[struct] * 3,
        compiler_params=pltpu.CompilerParams(vmem_limit_bytes=VMEM_BYTES),
        cost_estimate=pl.CostEstimate(flops=10 * size, bytes_accessed=26 * size, transcendentals=0),
        name=name,
    )(core, *state, *sums)


def update_attention(core, state, qfv, out, step_rate):
    _, shard, width = state[0].shape

    def pick(core_index, qfv_mine, qfv_other, out_mine, out_other):
        own = pl.program_id(1) == core_index
        proj = jnp.where(own, qfv_mine.astype(wide), qfv_other.astype(wide))
        last = jnp.where(own, out_mine.astype(wide), out_other.astype(wide))
        for kind in range(3):
            parts = [proj[:, (3 * pair + kind) * PAIR :][:, :PAIR] for pair in range(2)]
            chosen = jnp.concatenate(parts, axis=1)
            last = jnp.where(pl.program_id(0) == kind, chosen, last)
        return last

    return update_call(
        core,
        state,
        (*qfv, *out),
        (4, 2),
        pl.BlockSpec((1, shard, width // 2), lambda kind, half, _: (kind, 0, half)),
        [whole(total.shape) for total in (*qfv, *out)],
        pick,
        step_rate,
        "update_attention",
    )


def update_ffn_in(core, state, sums, step_rate):
    _, shard, hidden = state[0].shape

    def pick(core_index, mine, other):
        own = pl.program_id(0) == core_index
        return jnp.where(own, mine.astype(wide), other.astype(wide))

    return update_call(
        core,
        state,
        sums,
        (2,),
        pl.BlockSpec((1, shard, hidden), lambda kind, _: (kind, 0, 0)),
        [whole(total.shape) for total in sums],
        pick,
        step_rate,
        "update_ffn_in",
    )


def update_ffn_out(core, state, sums, step_rate):
    shard, width = state[0].shape

    def pick(core_index, mine, other):
        own = pl.program_id(0) == core_index
        return jnp.where(own, mine.astype(wide), other.astype(wide))

    return update_call(
        core,
        state,
        sums,
        (2,),
        pl.BlockSpec((shard, width // 2), lambda j, _: (0, j)),
        [whole(total.shape) for total in sums],
        pick,
        step_rate,
        "update_ffn_out",
    )


def pack_kernel(core_ref, w_ref, g_ref, out_ref):
    pairs = w_ref.shape[2] // PAIR
    for pair in range(pairs):
        for kind in range(3):
            start = (pair * 3 + kind) * PAIR
            piece = w_ref[kind, :, pair * PAIR : (pair + 1) * PAIR]
            out_ref[:, start : start + PAIR] = piece.astype(low)
    start = 3 * pairs * PAIR
    out_ref[:, start : start + pairs * PAIR] = w_ref[3].astype(low)
    start += pairs * PAIR
    out_ref[:, start:] = g_ref[...].astype(low)


def pack_attention(core, weights, gains):
    _, shard, width = weights.shape
    half = width // 2
    gain_columns = jnp.pad(gains.T, ((0, 0), (0, HEAD_DIM - 3)))
    columns = 4 * half + HEAD_DIM
    return pl.pallas_call(
        pack_kernel,
        grid_spec=pltpu.PrefetchScalarGridSpec(
            num_scalar_prefetch=1,
            grid=(1,),
            in_specs=[
                pl.BlockSpec((4, shard, half), lambda j, core: (0, 0, core[0])),
                whole((shard, HEAD_DIM)),
            ],
            out_specs=whole((shard, columns)),
        ),
        out_shape=jax.ShapeDtypeStruct((shard, columns), low),
        name="pack_attention",
    )(core, weights, gain_columns)


RING = 8


def ring_place(index):
    return jnp.where(index % 2 == 0, index // 2, RING - 1 - index // 2)


def ring_member(place):
    place = place % RING
    return jnp.where(place < RING // 2, 2 * place, 2 * RING - 1 - 2 * place)


def ring_next(tensor):
    cycle = [0, 2, 4, 6, 7, 5, 3, 1]
    replicas = lax.axis_size("dp")
    pairs = []
    for place, member in enumerate(cycle):
        for replica in range(replicas):
            target = cycle[(place + (1 if replica % 2 == 0 else -1)) % RING]
            pairs.append((member * replicas + replica, target * replicas + replica))
    return lax.ppermute(tensor, ("fsdp", "dp"), pairs)


def core_swap(tensor):
    return lax.ppermute(tensor, "dp", [(d, d ^ 1) for d in range(lax.axis_size("dp"))])


def column_swap(tensor):
    return lax.ppermute(tensor, "dp", [(d, d ^ 2) for d in range(lax.axis_size("dp"))])


def assemble_kernel(origin_ref, *refs):
    pieces, out_ref = refs[:RING], refs[RING]
    rows = pieces[0].shape[0]
    for step, piece in enumerate(pieces):
        start = pl.multiple_of(origin_ref[step] * rows, 16)
        out_ref[pl.ds(start, rows), :] = piece[...]


def assemble(origins, pieces):
    rows, columns = pieces[0].shape
    return pl.pallas_call(
        assemble_kernel,
        grid_spec=pltpu.PrefetchScalarGridSpec(
            num_scalar_prefetch=1,
            grid=(1,),
            in_specs=[whole((rows, columns))] * RING,
            out_specs=whole((RING * rows, columns)),
        ),
        out_shape=jax.ShapeDtypeStruct((RING * rows, columns), pieces[0].dtype),
        compiler_params=pltpu.CompilerParams(vmem_limit_bytes=VMEM_BYTES),
        cost_estimate=pl.CostEstimate(
            flops=0, bytes_accessed=4 * RING * rows * columns, transcendentals=0
        ),
        name="assemble",
    )(origins, *pieces)


def after(tensor, *others):
    return lax.optimization_barrier((tensor, *others))[0]


def core_way():
    return 1 - 2 * (lax.axis_index("dp") % 2)


def ring_origins():
    place = ring_place(lax.axis_index("fsdp"))
    return ring_member(
        place - core_way() * jnp.arange(RING, dtype=jnp.int32) + RING
    ).astype(jnp.int32)


class RingGather:
    def __init__(self, shard):
        self.pieces = [shard]

    def step(self, *others):
        source = after(self.pieces[-1], *others) if others else self.pieces[-1]
        self.pieces.append(ring_next(source))

    def last(self):
        return self.pieces[-1]


class RingSum:
    def __init__(self, *arrays):
        self.arrays = arrays
        place = ring_place(lax.axis_index("fsdp"))
        self.owners = [ring_member(place - core_way() * (s + 1) + 2 * RING) for s in range(RING)]
        self.totals = []

    def term(self):
        parts = []
        for array in self.arrays:
            rows = array.shape[0] // RING
            start = self.owners[len(self.totals)] * rows
            parts.append(lax.dynamic_slice_in_dim(array, start, rows, 0))
        return parts[0] if len(parts) == 1 else jnp.concatenate(parts, axis=0)

    def step(self, *others):
        if not self.totals:
            self.totals.append(self.term())
        total = self.totals[-1]
        moved = ring_next(after(total, *others) if others else total)
        self.totals.append((moved.astype(wide) + self.term().astype(wide)).astype(low))

    def last(self):
        return self.totals[-1]


class Turns:
    def __init__(self):
        self.results = []

    def step(self, ring, *others):
        ring.step(*self.results[-2:-1], *others)
        self.results.append(ring.last())


def gather_rows(shard, *others):
    mine = lax.all_gather(shard, "fsdp", axis=0, tiled=True)
    mine = after(mine, *others) if others else mine
    return mine, core_swap(mine)


def core_sum(mine, other):
    return (mine.astype(wide) + core_swap(other).astype(wide)).astype(low)


def scatter_rows(both):
    return lax.psum_scatter(both, "fsdp", scatter_dimension=0, tiled=True)


def over_columns(total):
    total = (total.astype(wide) + column_swap(total).astype(wide)).astype(low)
    return total, core_swap(total)


def sum_everywhere(tensor):
    distance = 1
    while distance < lax.axis_size("dp"):
        pairs = [(d, d ^ distance) for d in range(lax.axis_size("dp"))]
        tensor = tensor + lax.ppermute(tensor, "dp", pairs)
        distance *= 2
    distance = 1
    while distance < lax.axis_size("fsdp"):
        pairs = [(f, f ^ distance) for f in range(lax.axis_size("fsdp"))]
        tensor = tensor + lax.ppermute(tensor, "fsdp", pairs)
        distance *= 2
    return tensor


def on_device(
    inputs,
    cotangent,
    lengths,
    attention_weights,
    attention_momentum,
    attention_average,
    ffn_inputs,
    ffn_inputs_momentum,
    ffn_inputs_average,
    ffn_output,
    ffn_output_momentum,
    ffn_output_average,
    gains,
    gains_momentum,
    gains_average,
):
    micro_count, slot, width = inputs.shape
    down_rows = ffn_output.shape[0]
    fsdp_size = lax.axis_size("fsdp")
    replicas = lax.axis_size("dp")
    ringed = fsdp_size == RING
    core = lax.axis_index("dp") % 2
    me = lax.axis_index("fsdp")
    count = micro_count * slot
    half = width // 2
    core_ref = core.astype(jnp.int32).reshape(1)
    other_ref = 1 - core_ref
    is_first = core == 0

    up_half = lax.dynamic_index_in_dim(ffn_inputs, core, 0, keepdims=False).astype(low)
    packed = after(pack_attention(core_ref, attention_weights, gains), up_half)
    down_half = lax.dynamic_slice_in_dim(ffn_output, core * half, half, 1).astype(low)

    rows = inputs.reshape(count, width)
    positions = jnp.arange(slot, dtype=jnp.int32)
    valid = (positions[None, :] < lengths).astype(wide).reshape(count, 1)
    errors = (cotangent.reshape(count, width).astype(wide) * valid).astype(low)

    def gains_of(weights):
        gain_rows = weights[:, 4 * half : 4 * half + 3].T.astype(wide)
        return jnp.pad(gain_rows, ((0, 5), (0, 0)))

    if ringed:
        origins = ring_origins()
        ring_a, ring_d = RingGather(packed), RingGather(down_half)
        for step in range(1, RING):
            extra = [errors, valid] if step == 3 else []
            before = ring_a.pieces[-2:-1]
            ring_a.step(*ring_d.pieces[-2:-1], *extra)
            ring_d.step(*before)
        mine = [assemble(origins, ring.pieces) for ring in (ring_a, ring_d)]
        w_a, w_d = [(part, core_swap(part)) for part in mine]
        rows = after(rows, w_a[1], w_d[0])
    else:
        w_a, w_d, w_gu = gather_rows(packed), gather_rows(down_half), gather_rows(up_half)
    gains8 = gains_of(w_a[0])
    mixed_mine, *kept_mine = mixer_forward(core_ref, rows, w_a[0], gains8, slot)
    if ringed:
        w_gu = gather_rows(up_half, mixed_mine)
    mixed_other, *rest = mixer_forward(
        other_ref, rows, w_a[1], gains8, slot, (mixed_mine, w_a[0])
    )
    kept_other, (x1, h2, h2t, h1t) = rest[:4], rest[4:]
    gm, gu, gd_mine, gd_other, output, d_x1, d_mixed, go_mine, go_other, grad_two = ffn(
        core_ref, h2, h2t, errors, w_gu, w_d, x1, (mixed_mine, mixed_other), w_a, valid, gains8
    )
    grad_other, ggo_other, dpre_other = mixer_backward(
        other_ref, h1t, gains8, kept_other, d_mixed, slot
    )
    sum_gu = core_sum(after(gm, dpre_other), gu)
    total_gu = scatter_rows(sum_gu)
    sum_d = core_sum(after(gd_mine, dpre_other), gd_other)
    sum_o = core_sum(after(go_mine, dpre_other), go_other)
    if ringed:
        ring_do = RingSum(sum_d, sum_o)
        turns = Turns()
        turns.step(ring_do)
        h1t = after(h1t, sum_gu, ring_do.totals[0])
    grad_mine, ggo_mine, dpre_mine = mixer_backward(
        core_ref, h1t, gains8, kept_mine, d_mixed, slot
    )
    ggo_left = jnp.where(is_first, ggo_mine, ggo_other)
    ggo_right = jnp.where(is_first, ggo_other, ggo_mine)
    grad_go = jnp.concatenate([ggo_left, ggo_right], axis=1)
    sum_qfv = core_sum(grad_mine, grad_other)

    def finish_input(d_pre):
        gradient, grad_one = input_gradient(rows, gains8, (d_pre, dpre_other), w_a, d_x1)
        stacked = jnp.concatenate([grad_one, grad_go, grad_two], axis=0)
        return gradient, sum_everywhere(stacked)

    if ringed:
        ring_qfv = RingSum(sum_qfv)
        turns.step(ring_do, grad_mine)
        order = [ring_qfv, ring_do] * 5 + [ring_qfv] * 2
        for place_of, ring in enumerate(order):
            if place_of == 4:
                late = after(dpre_mine, turns.results[-2])
                input_grad, gain_grads = finish_input(late)
            turns.step(ring, *([gain_grads] if place_of == 10 else []))
        total_do, total_qfv = ring_do.last(), ring_qfv.last()
    else:
        total_do = jnp.concatenate([scatter_rows(sum_d), scatter_rows(sum_o)], axis=0)
        total_qfv = scatter_rows(sum_qfv)
        input_grad, gain_grads = finish_input(dpre_mine)
    sum_do = over_columns(total_do)
    sum_gu = over_columns(total_gu)
    sum_qfv = over_columns(total_qfv)
    sum_d = [total[:down_rows] for total in sum_do]
    sum_o = [total[down_rows:] for total in sum_do]
    sum_gains = lax.dynamic_slice_in_dim(gain_grads, me * gains.shape[1], gains.shape[1], 1)

    scale_rows = 1.0 / math.sqrt(count * fsdp_size * replicas)
    attention_state = (attention_weights, attention_momentum, attention_average)
    ffn_in_state = (ffn_inputs, ffn_inputs_momentum, ffn_inputs_average)
    ffn_out_state = (ffn_output, ffn_output_momentum, ffn_output_average)
    return (
        output.reshape(micro_count, slot, width),
        input_grad.reshape(micro_count, slot, width),
        *update_attention(core_ref, attention_state, sum_qfv, sum_o, matrix_rate * scale_rows),
        *update_ffn_in(core_ref, ffn_in_state, sum_gu, matrix_rate * scale_rows),
        *update_ffn_out(core_ref, ffn_out_state, sum_d, matrix_rate * scale_rows),
        *update(gains, gains_momentum, gains_average, sum_gains, gain_rate * scale_rows),
    )


def solution(mesh):
    rows_split = P(None, ("fsdp", "dp"), None)
    middle_split = P(None, "fsdp", None)
    first_split = P("fsdp", None)
    gains_split = P(None, "fsdp")
    in_specs = (
        (rows_split, rows_split, P(None, ("fsdp", "dp")))
        + (middle_split,) * 6
        + (first_split,) * 3
        + (gains_split,) * 3
    )
    out_specs = (
        (rows_split, rows_split)
        + (middle_split,) * 6
        + (first_split,) * 3
        + (gains_split,) * 3
    )
    return jax.shard_map(
        on_device, mesh=mesh, in_specs=in_specs, out_specs=out_specs, check_vma=False
    )
```

```python
import functools
import math

import jax
import jax.numpy as jnp
from jax import lax
from jax.experimental import pallas as pl
from jax.experimental.pallas import tpu as pltpu
from jax.sharding import PartitionSpec as P

HEAD_DIM = 128
PAIR = 2 * HEAD_DIM

lower_bound = 0.9
momentum_decay = 0.9
average_decay = 0.7
weight_decay = 0.0005
matrix_rate = 0.03
gain_rate = 0.1
low = jnp.bfloat16
wide = jnp.float32
TILE_F = 256
VMEM_BYTES = 60 * 1024 * 1024


def mm(left, right):
    return jnp.dot(left, right, preferred_element_type=wide)


def mm_nt(left, right):
    return lax.dot_general(left, right, (((1,), (1,)), ((), ())), preferred_element_type=wide)


def mm_tn(left, right):
    return lax.dot_general(left, right, (((0,), (0,)), ((), ())), preferred_element_type=wide)


def sigmoid(u):
    return 0.5 * jnp.tanh(0.5 * u) + 0.5


def whole(shape):
    return pl.BlockSpec(shape, lambda *_: (0,) * len(shape), pipeline_mode=pl.Buffered(1))


def split_sum(ones_matrix, tensor):
    high = tensor.astype(low)
    rest = (tensor - high.astype(wide)).astype(low)
    return mm(ones_matrix, high) + mm(ones_matrix, rest)


def triangle(length, lower):
    rows = lax.broadcasted_iota(jnp.int32, (length, length), 0)
    columns = lax.broadcasted_iota(jnp.int32, (length, length), 1)
    kept = rows >= columns if lower else rows <= columns
    return kept.astype(wide).astype(low)


def decay_parts(f_pre, lower_ones):
    share = sigmoid(f_pre)
    gate = lower_bound + (1.0 - lower_bound) * share
    keys_in = (1.0 - lower_bound) * (1.0 - share)
    cumulative = split_sum(lower_ones, jnp.log(gate))
    middle_row = cumulative.shape[0] // 2
    cumulative = cumulative - cumulative[middle_row : middle_row + 1, :]
    return share, gate, keys_in, cumulative


def first_norm(x_ref, gain_row):
    rows = x_ref[...].astype(wide)
    scale = lax.rsqrt(jnp.mean(rows * rows, axis=-1, keepdims=True) + 1e-06)
    return rows * scale, scale


def lanes_of(half, size):
    return pl.ds(pl.multiple_of(half * size, size), size)


def mixer_forward_kernel(
    slot, half_ref, x_ref, w_ref, g_ref, on_ref, q_ref, f_ref, v_ref, o_ref, h_s
):
    @pl.when(pl.program_id(0) == 0)
    def _():
        normed, _ = first_norm(x_ref, None)
        h_s[...] = (normed * g_ref[0:1, :]).astype(low)

    gain_o = g_ref[1:2, lanes_of(half_ref[0] * pl.num_programs(0) + pl.program_id(0), PAIR)]
    pre = mm(h_s[...], w_ref[...])
    q_ref[...] = pre[:, :PAIR]
    f_ref[...] = pre[:, PAIR : 2 * PAIR]
    v_ref[...] = pre[:, 2 * PAIR :].astype(low)
    lower_ones = triangle(slot, True)
    block_rows = lax.broadcasted_iota(jnp.int32, (HEAD_DIM, HEAD_DIM), 0)
    block_columns = lax.broadcasted_iota(jnp.int32, (HEAD_DIM, HEAD_DIM), 1)
    causal = block_rows >= block_columns
    for sequence in range(x_ref.shape[0] // slot):
        rows = slice(sequence * slot, (sequence + 1) * slot)
        q_pre = q_ref[rows, :]
        _, _, keys_in, cumulative = decay_parts(f_ref[rows, :], lower_ones)
        grown = jnp.exp(-cumulative)
        decayed_q = (q_pre * sigmoid(q_pre) * jnp.exp(cumulative)).astype(low)
        grown_k = (keys_in * grown).astype(low)
        values = v_ref[rows, :]
        for head in range(2):
            lanes = slice(head * HEAD_DIM, (head + 1) * HEAD_DIM)
            for block in range(slot // HEAD_DIM):
                start, end = block * HEAD_DIM, (block + 1) * HEAD_DIM
                q_block = decayed_q[start:end, lanes]
                diagonal = mm_nt(q_block, grown_k[start:end, lanes])
                diagonal = jnp.where(causal, diagonal, 0.0).astype(low)
                out = mm(diagonal, values[start:end, lanes])
                if block > 0:
                    scores = mm_nt(q_block, grown_k[:start, lanes]).astype(low)
                    out = out + mm(scores, values[:start, lanes])
                scale = lax.rsqrt(jnp.mean(out * out, axis=-1, keepdims=True) + 1e-05)
                target = slice(sequence * slot + start, sequence * slot + end)
                o_ref[target, lanes] = out
                on_ref[target, lanes] = (out * scale * gain_o[:, lanes]).astype(low)


def mixer_forward_last_kernel(
    slot,
    half_ref,
    x_ref,
    w_ref,
    g_ref,
    before_ref,
    woo_ref,
    wom_ref,
    on_ref,
    q_ref,
    f_ref,
    v_ref,
    o_ref,
    x1_ref,
    h2_ref,
    h2t_ref,
    h1t_ref,
    h_s,
    on_s,
):
    step = pl.program_id(0)
    half = before_ref.shape[1]
    mixer_forward_kernel(
        slot, half_ref, x_ref, w_ref, g_ref, on_ref, q_ref, f_ref, v_ref, o_ref, h_s
    )
    on_s[:, lanes_of(half_ref[0] * pl.num_programs(0) + step, PAIR)] = on_ref[...]

    @pl.when(step == pl.num_programs(0) - 1)
    def _():
        here = lanes_of(half_ref[0], half)
        there = lanes_of(1 - half_ref[0], half)
        on_s[:, there] = before_ref[...]
        h1t_ref[...] = h_s[...].astype(wide).T.astype(low)
        x1_ref[:, here] = x_ref[:, here].astype(wide) + mm(on_s[...], woo_ref[...])
        x1_ref[:, there] = x_ref[:, there].astype(wide) + mm(on_s[...], wom_ref[...])
        x1 = x1_ref[...]
        scale = lax.rsqrt(jnp.mean(x1 * x1, axis=-1, keepdims=True) + 1e-06)
        normed = x1 * scale * g_ref[2:3, :]
        h2_ref[...] = normed.astype(low)
        h2t_ref[...] = normed.T.astype(low)


def mixer_forward(half, rows, weights, gains8, slot, ending=None):
    count, width = rows.shape
    pairs = width // PAIR // 2
    by_pair = pl.BlockSpec((count, PAIR), lambda j, _: (0, j))
    struct = jax.ShapeDtypeStruct
    shape = lambda kind: struct((count, width // 2), kind)
    kernel = mixer_forward_kernel
    in_specs = [
        whole(rows.shape),
        pl.BlockSpec((width, 3 * PAIR), lambda j, _: (0, j)),
        whole(gains8.shape),
    ]
    operands = [half, rows, weights, gains8]
    out_specs = [by_pair] * 5
    out_shape = [shape(low), shape(wide), shape(wide), shape(low), shape(wide)]
    scratch = [pltpu.VMEM((count, width), low)]
    if ending is not None:
        kernel = mixer_forward_last_kernel
        out_weights = pl.BlockSpec((width, width // 2), lambda j, _: (0, 3))
        in_specs += [whole((count, width // 2)), out_weights, out_weights]
        operands += [ending[0], weights, ending[1]]
        out_specs += [whole((count, width))] * 2 + [whole((width, count))] * 2
        out_shape += [
            struct((count, width), wide),
            struct((count, width), low),
            struct((width, count), low),
            struct((width, count), low),
        ]
        scratch += [pltpu.VMEM((count, width), low)]
    return pl.pallas_call(
        functools.partial(kernel, slot),
        grid_spec=pltpu.PrefetchScalarGridSpec(
            num_scalar_prefetch=1,
            grid=(pairs,),
            in_specs=in_specs,
            out_specs=out_specs,
            scratch_shapes=scratch,
        ),
        out_shape=out_shape,
        compiler_params=pltpu.CompilerParams(vmem_limit_bytes=VMEM_BYTES),
        cost_estimate=pl.CostEstimate(
            flops=count * width * 4 * width + 10 * count * slot * width,
            bytes_accessed=count * width * 12 + width * width * 4,
            transcendentals=count * width * 3,
        ),
        name="mixer_forward",
    )(*operands)


def ffn_tile(
    core_ref, h_ref, ht_ref, e_ref, wm_ref, wu_ref, wdm_ref, wdo_ref, grads, acc_ref, dh_ref
):
    gm_ref, gu_ref, gdm_ref, gdo_ref = grads
    half = wdm_ref.shape[1]
    first = core_ref[0] == 0
    mine = lanes_of(core_ref[0], half)
    other = lanes_of(1 - core_ref[0], half)
    own = mm(h_ref[...], wm_ref[...])
    swapped = mm(h_ref[...], wu_ref[...])
    a = jnp.where(first, own, swapped)
    b = jnp.where(first, swapped, own)
    share = sigmoid(a)
    swish = a * share
    mid = (swish * b).astype(low)
    acc_ref[:, mine] += mm(mid, wdm_ref[...])
    acc_ref[:, other] += mm(mid, wdo_ref[...])
    d_mid = mm_nt(e_ref[:, mine], wdm_ref[...]) + mm_nt(e_ref[:, other], wdo_ref[...])
    gdm_ref[...] = mm_tn(mid, e_ref[:, mine]).astype(low)
    gdo_ref[...] = mm_tn(mid, e_ref[:, other]).astype(low)
    d_a = (d_mid * b * share * (1.0 + a * (1.0 - share))).astype(low)
    d_b = (d_mid * swish).astype(low)
    d_own = jnp.where(first, d_a, d_b)
    d_swapped = jnp.where(first, d_b, d_a)
    gm_ref[...] = mm(ht_ref[...], d_own).astype(low)
    gu_ref[...] = mm(ht_ref[...], d_swapped).astype(low)
    dh_ref[...] += mm_nt(d_own, wm_ref[...]) + mm_nt(d_swapped, wu_ref[...])


def ffn_kernel(
    core_ref,
    h_ref,
    ht_ref,
    e_ref,
    wm_ref,
    wu_ref,
    wdm_ref,
    wdo_ref,
    x1_ref,
    onm_ref,
    ono_ref,
    wom_ref,
    woo_ref,
    m_ref,
    g_ref,
    gm_ref,
    gu_ref,
    gdm_ref,
    gdo_ref,
    out_ref,
    dh_s,
    acc_s,
    gom_ref,
    goo_ref,
    g2_ref,
    on_s,
):
    @pl.when(pl.program_id(0) == 0)
    def _():
        acc_s[...] = x1_ref[...]
        dh_s[...] = jnp.zeros_like(dh_s)

    grads = (gm_ref, gu_ref, gdm_ref, gdo_ref)
    ffn_tile(
        core_ref, h_ref, ht_ref, e_ref, wm_ref, wu_ref, wdm_ref, wdo_ref, grads, acc_s, dh_s
    )

    @pl.when(pl.program_id(0) == pl.num_programs(0) - 1)
    def _():
        half = onm_ref.shape[1]
        mine = lanes_of(core_ref[0], half)
        other = lanes_of(1 - core_ref[0], half)
        out_ref[...] = (acc_s[...] * m_ref[...]).astype(low)
        x1 = x1_ref[...]
        scale = lax.rsqrt(jnp.mean(x1 * x1, axis=-1, keepdims=True) + 1e-06)
        normed = x1 * scale
        d_h2 = dh_s[...]
        scaled = d_h2 * g_ref[2:3, :]
        g2_ref[...] = jnp.sum(d_h2 * normed, axis=0, keepdims=True)
        d_x1 = e_ref[...].astype(wide) + scale * (
            scaled - normed * jnp.mean(scaled * normed, axis=-1, keepdims=True)
        )
        dh_s[...] = d_x1
        on_s[...] = d_x1.astype(low)
        acc_s[...] = mm_nt(on_s[:, mine], wom_ref[...]) + mm_nt(on_s[:, other], woo_ref[...])
        onm, ono = onm_ref[...], ono_ref[...]
        d_mine, d_other = on_s[:, mine], on_s[:, other]
        here = pl.ds(pl.multiple_of(core_ref[0] * half, half), half)
        there = pl.ds(pl.multiple_of((1 - core_ref[0]) * half, half), half)
        gom_ref[here, :] = mm_tn(onm, d_mine).astype(low)
        gom_ref[there, :] = mm_tn(ono, d_mine).astype(low)
        goo_ref[here, :] = mm_tn(onm, d_other).astype(low)
        goo_ref[there, :] = mm_tn(ono, d_other).astype(low)


def ffn(core, h2, h2t, errors, w_gu, w_d, x1, mixed, w_a, mask, gains8):
    count, width = h2.shape
    half = width // 2
    hidden = w_gu[0].shape[1]
    full = whole((count, width))
    half_full = whole((count, half))
    square = whole((width, half))
    in_tile = pl.BlockSpec((width, TILE_F), lambda j, _: (0, j))
    out_tile = pl.BlockSpec((TILE_F, half), lambda j, _: (j, 0))
    out_weights = pl.BlockSpec((width, half), lambda j, _: (0, 3), pipeline_mode=pl.Buffered(1))
    struct = jax.ShapeDtypeStruct
    return pl.pallas_call(
        ffn_kernel,
        grid_spec=pltpu.PrefetchScalarGridSpec(
            num_scalar_prefetch=1,
            grid=(hidden // TILE_F,),
            in_specs=[full, whole(h2t.shape), full, in_tile, in_tile, out_tile, out_tile]
            + [full, half_full, half_full, out_weights, out_weights]
            + [whole((count, 1)), whole((8, width))],
            out_specs=[in_tile, in_tile, out_tile, out_tile]
            + [full, full, full, square, square, whole((1, width))],
            scratch_shapes=[pltpu.VMEM((count, width), low)],
        ),
        out_shape=[struct((width, hidden), low)] * 2
        + [struct((hidden, half), low)] * 2
        + [
            struct((count, width), low),
            struct((count, width), wide),
            struct((count, width), wide),
            struct((width, half), low),
            struct((width, half), low),
            struct((1, width), wide),
        ],
        compiler_params=pltpu.CompilerParams(vmem_limit_bytes=VMEM_BYTES),
        cost_estimate=pl.CostEstimate(
            flops=16 * count * width * hidden,
            bytes_accessed=count * width * 20 + width * hidden * 12,
            transcendentals=count * hidden,
        ),
        name="ffn",
    )(core, h2, h2t, errors, *w_gu, *w_d, x1, *mixed, *w_a, mask, gains8)


def mixer_backward_kernel(
    slot,
    half_ref,
    ht_ref,
    g_ref,
    q_ref,
    f_ref,
    v_ref,
    o_ref,
    don_ref,
    grad_ref,
    ggo_ref,
    dpre_ref,
):
    gain_o = g_ref[1:2, lanes_of(half_ref[0], PAIR)]
    lower_ones = triangle(slot, True)
    upper_ones = triangle(slot, False)
    block_rows = lax.broadcasted_iota(jnp.int32, (HEAD_DIM, HEAD_DIM), 0)
    block_columns = lax.broadcasted_iota(jnp.int32, (HEAD_DIM, HEAD_DIM), 1)
    causal = block_rows >= block_columns
    causal_t = block_rows <= block_columns
    blocks = slot // HEAD_DIM
    ggo_total = jnp.zeros((1, PAIR), wide)
    for sequence in range(q_ref.shape[0] // slot):
        rows = slice(sequence * slot, (sequence + 1) * slot)
        d_on = don_ref[rows, :]
        out = o_ref[rows, :]
        d_out_parts = []
        ggo_parts = []
        for head in range(2):
            lanes = slice(head * HEAD_DIM, (head + 1) * HEAD_DIM)
            out_h, d_on_h = out[:, lanes], d_on[:, lanes]
            scale = lax.rsqrt(jnp.mean(out_h * out_h, axis=-1, keepdims=True) + 1e-05)
            normed = out_h * scale
            ggo_parts.append(jnp.sum(d_on_h * normed, axis=0, keepdims=True))
            scaled = d_on_h * gain_o[:, lanes]
            inner = jnp.mean(scaled * normed, axis=-1, keepdims=True)
            d_out_parts.append((scale * (scaled - normed * inner)).astype(low))
        ggo_total = ggo_total + jnp.concatenate(ggo_parts, axis=1)

        q_pre = q_ref[rows, :]
        share, gate, keys_in, cumulative = decay_parts(f_ref[rows, :], lower_ones)
        grown = jnp.exp(-cumulative)
        shrunk = jnp.exp(cumulative)
        q_share = sigmoid(q_pre)
        decayed_q = (q_pre * q_share * shrunk).astype(low)
        grown_k = (keys_in * grown).astype(low)
        values = v_ref[rows, :]
        dq_parts, dk_parts, dv_parts = [], [], []
        for head in range(2):
            lanes = slice(head * HEAD_DIM, (head + 1) * HEAD_DIM)
            q_h, k_h, v_h = decayed_q[:, lanes], grown_k[:, lanes], values[:, lanes]
            d_out = d_out_parts[head]
            dq_blocks, dk_blocks, dv_blocks = [], [], []
            for block in range(blocks):
                start, end = block * HEAD_DIM, (block + 1) * HEAD_DIM
                here = slice(start, end)
                d_scores = mm_nt(d_out[here], v_h[here])
                d_scores = jnp.where(causal, d_scores, 0.0).astype(low)
                d_q = mm(d_scores, k_h[here])
                if block > 0:
                    before = slice(0, start)
                    d_scores = mm_nt(d_out[here], v_h[before]).astype(low)
                    d_q = d_q + mm(d_scores, k_h[before])
                dq_blocks.append(d_q)
                scores = jnp.where(causal_t, mm_nt(k_h[here], q_h[here]), 0.0).astype(low)
                d_scores = jnp.where(causal_t, mm_nt(v_h[here], d_out[here]), 0.0).astype(low)
                d_v = mm(scores, d_out[here])
                d_k = mm(d_scores, q_h[here])
                if block < blocks - 1:
                    after = slice(end, slot)
                    scores = mm_nt(k_h[here], q_h[after]).astype(low)
                    d_scores = mm_nt(v_h[here], d_out[after]).astype(low)
                    d_v = d_v + mm(scores, d_out[after])
                    d_k = d_k + mm(d_scores, q_h[after])
                dk_blocks.append(d_k)
                dv_blocks.append(d_v)
            dq_parts.append(jnp.concatenate(dq_blocks, axis=0))
            dk_parts.append(jnp.concatenate(dk_blocks, axis=0))
            dv_parts.append(jnp.concatenate(dv_blocks, axis=0))
        d_decayed = jnp.concatenate(dq_parts, axis=1)
        d_grown = jnp.concatenate(dk_parts, axis=1)
        d_value = jnp.concatenate(dv_parts, axis=1)
        d_cumulative = decayed_q.astype(wide) * d_decayed - grown_k.astype(wide) * d_grown
        d_log = split_sum(upper_ones, d_cumulative)
        d_query = d_decayed * shrunk
        d_key = d_grown * grown
        d_q_pre = d_query * q_share * (1.0 + q_pre * (1.0 - q_share))
        d_f_pre = (1.0 - lower_bound) * (d_log / gate - d_key) * share * (1.0 - share)
        dpre_ref[rows, :PAIR] = d_q_pre.astype(low)
        dpre_ref[rows, PAIR : 2 * PAIR] = d_f_pre.astype(low)
        dpre_ref[rows, 2 * PAIR :] = d_value.astype(low)

    ggo_ref[...] = ggo_total
    grad_ref[...] = mm(ht_ref[...], dpre_ref[...]).astype(low)


def mixer_backward(which, h1t, gains8, kept, d_mixed, pair, slot):
    width, count = h1t.shape
    by_pair = pl.BlockSpec((count, PAIR), lambda j, _: (0, pair))
    from_whole = pl.BlockSpec((count, PAIR), lambda j, which: (0, which[0]))
    struct = jax.ShapeDtypeStruct
    return pl.pallas_call(
        functools.partial(mixer_backward_kernel, slot),
        grid_spec=pltpu.PrefetchScalarGridSpec(
            num_scalar_prefetch=1,
            grid=(1,),
            in_specs=[whole((width, count)), whole(gains8.shape)] + [by_pair] * 4 + [from_whole],
            out_specs=[whole((width, 3 * PAIR)), whole((1, PAIR)), whole((count, 3 * PAIR))],
        ),
        out_shape=[
            struct((width, 3 * PAIR), low),
            struct((1, PAIR), wide),
            struct((count, 3 * PAIR), low),
        ],
        compiler_params=pltpu.CompilerParams(vmem_limit_bytes=VMEM_BYTES),
        cost_estimate=pl.CostEstimate(
            flops=count * width * 6 * PAIR + 20 * count * slot * PAIR,
            bytes_accessed=count * width * 5 + width * PAIR * 6,
            transcendentals=count * PAIR * 6,
        ),
        name="mixer_backward",
    )(which, h1t, gains8, *kept, d_mixed)


def input_gradient_rows_kernel(x_ref, g_ref, *refs):
    pre_refs, weight_refs = refs[:4], refs[4:8]
    dx1_ref, dx_ref, g1_ref = refs[8:]
    d_h1 = mm_nt(pre_refs[0][...], weight_refs[0][...])
    for pre_ref, weight_ref in zip(pre_refs[1:], weight_refs[1:]):
        d_h1 = d_h1 + mm_nt(pre_ref[...], weight_ref[...])
    normed, scale = first_norm(x_ref, None)
    scaled = d_h1 * g_ref[0:1, :]
    grad_one = jnp.sum(d_h1 * normed, axis=0, keepdims=True)

    @pl.when(pl.program_id(0) == 0)
    def _():
        g1_ref[...] = grad_one

    @pl.when(pl.program_id(0) > 0)
    def _():
        g1_ref[...] += grad_one

    dx_ref[...] = dx1_ref[...] + scale * (
        scaled - normed * jnp.mean(scaled * normed, axis=-1, keepdims=True)
    )


def input_gradient(rows, gains8, d_pre, weights, d_x1):
    count, width = rows.shape
    block = count // 2
    by_rows = lambda columns: pl.BlockSpec((block, columns), lambda j: (j, 0))
    weight_specs = [
        pl.BlockSpec((width, 3 * PAIR), lambda j, p=p: (0, p), pipeline_mode=pl.Buffered(1))
        for p in (0, 1, 0, 1)
    ]
    struct = jax.ShapeDtypeStruct
    return pl.pallas_call(
        input_gradient_rows_kernel,
        grid=(count // block,),
        in_specs=[by_rows(width), whole(gains8.shape)]
        + [by_rows(3 * PAIR)] * 4
        + weight_specs
        + [by_rows(width)],
        out_specs=[by_rows(width), whole((1, width))],
        out_shape=[struct((count, width), wide), struct((1, width), wide)],
        compiler_params=pltpu.CompilerParams(vmem_limit_bytes=VMEM_BYTES),
        cost_estimate=pl.CostEstimate(
            flops=6 * count * width * width,
            bytes_accessed=count * width * 16 + width * width * 6,
            transcendentals=0,
        ),
        name="input_gradient",
    )(rows, gains8, *d_pre, weights[0], weights[0], weights[1], weights[1], d_x1)


def update(weight, momentum, average, gradient, step_rate):
    new_momentum = momentum_decay * momentum + gradient
    direction = gradient + momentum_decay * new_momentum + weight_decay * weight
    new_weight = weight - step_rate * direction
    new_average = average_decay * average + (1.0 - average_decay) * new_weight
    return (new_momentum, new_average, new_weight)


def update_kernel(pick, step_rate, core_ref, w_ref, m_ref, a_ref, *refs):
    sums, outs = refs[:-3], refs[-3:]
    gradient = pick(core_ref[0], *[s[...] for s in sums]).astype(wide).reshape(w_ref.shape)
    results = update(w_ref[...], m_ref[...], a_ref[...], gradient, step_rate)
    for out, result in zip(outs, results):
        out[...] = result


def update_call(core, state, sums, grid, state_spec, sum_specs, pick, step_rate, name):
    struct = jax.ShapeDtypeStruct(state[0].shape, wide)
    size = math.prod(state[0].shape)
    return pl.pallas_call(
        functools.partial(update_kernel, pick, step_rate),
        grid_spec=pltpu.PrefetchScalarGridSpec(
            num_scalar_prefetch=1,
            grid=grid,
            in_specs=[state_spec] * 3 + sum_specs,
            out_specs=[state_spec] * 3,
        ),
        out_shape=[struct] * 3,
        compiler_params=pltpu.CompilerParams(vmem_limit_bytes=VMEM_BYTES),
        cost_estimate=pl.CostEstimate(flops=10 * size, bytes_accessed=26 * size, transcendentals=0),
        name=name,
    )(core, *state, *sums)


def update_attention(core, state, qfv, out, step_rate):
    _, shard, width = state[0].shape

    def pick(core_index, qfv_mine, qfv_other, out_mine, out_other):
        own = pl.program_id(1) == core_index
        proj = jnp.where(own, qfv_mine.astype(wide), qfv_other.astype(wide))
        last = jnp.where(own, out_mine.astype(wide), out_other.astype(wide))
        for kind in range(3):
            parts = [proj[pair * shard :, kind * PAIR :][:shard, :PAIR] for pair in range(2)]
            chosen = jnp.concatenate(parts, axis=1)
            last = jnp.where(pl.program_id(0) == kind, chosen, last)
        return last

    return update_call(
        core,
        state,
        (*qfv, *out),
        (4, 2),
        pl.BlockSpec((1, shard, width // 2), lambda kind, half, _: (kind, 0, half)),
        [whole(total.shape) for total in (*qfv, *out)],
        pick,
        step_rate,
        "update_attention",
    )


def update_ffn_in(core, state, sums, step_rate):
    _, shard, hidden = state[0].shape

    def pick(core_index, mine, other):
        own = pl.program_id(0) == core_index
        return jnp.where(own, mine.astype(wide), other.astype(wide))

    return update_call(
        core,
        state,
        sums,
        (2,),
        pl.BlockSpec((1, shard, hidden), lambda kind, _: (kind, 0, 0)),
        [whole(total.shape) for total in sums],
        pick,
        step_rate,
        "update_ffn_in",
    )


def update_ffn_out(core, state, sums, step_rate):
    shard, width = state[0].shape

    def pick(core_index, mine, other):
        own = pl.program_id(0) == core_index
        return jnp.where(own, mine.astype(wide), other.astype(wide))

    return update_call(
        core,
        state,
        sums,
        (2,),
        pl.BlockSpec((shard, width // 2), lambda j, _: (0, j)),
        [whole(total.shape) for total in sums],
        pick,
        step_rate,
        "update_ffn_out",
    )


def pack_kernel(core_ref, w_ref, g_ref, out_ref):
    pairs = w_ref.shape[2] // PAIR
    for pair in range(pairs):
        for kind in range(3):
            start = (pair * 3 + kind) * PAIR
            piece = w_ref[kind, :, pair * PAIR : (pair + 1) * PAIR]
            out_ref[:, start : start + PAIR] = piece.astype(low)
    start = 3 * pairs * PAIR
    out_ref[:, start : start + pairs * PAIR] = w_ref[3].astype(low)
    start += pairs * PAIR
    out_ref[:, start:] = g_ref[...].astype(low)


def pack_attention(core, weights, gains):
    _, shard, width = weights.shape
    half = width // 2
    gain_columns = jnp.pad(gains.T, ((0, 0), (0, HEAD_DIM - 3)))
    columns = 4 * half + HEAD_DIM
    return pl.pallas_call(
        pack_kernel,
        grid_spec=pltpu.PrefetchScalarGridSpec(
            num_scalar_prefetch=1,
            grid=(1,),
            in_specs=[
                pl.BlockSpec((4, shard, half), lambda j, core: (0, 0, core[0])),
                whole((shard, HEAD_DIM)),
            ],
            out_specs=whole((shard, columns)),
        ),
        out_shape=jax.ShapeDtypeStruct((shard, columns), low),
        name="pack_attention",
    )(core, weights, gain_columns)


RING = 8


def ring_place(index):
    return jnp.where(index % 2 == 0, index // 2, RING - 1 - index // 2)


def ring_member(place):
    place = place % RING
    return jnp.where(place < RING // 2, 2 * place, 2 * RING - 1 - 2 * place)


def ring_next(tensor):
    cycle = [0, 2, 4, 6, 7, 5, 3, 1]
    replicas = lax.axis_size("dp")
    pairs = []
    for place, member in enumerate(cycle):
        for replica in range(replicas):
            target = cycle[(place + (1 if replica % 2 == 0 else -1)) % RING]
            pairs.append((member * replicas + replica, target * replicas + replica))
    return lax.ppermute(tensor, ("fsdp", "dp"), pairs)


def core_swap(tensor):
    return lax.ppermute(tensor, "dp", [(d, d ^ 1) for d in range(lax.axis_size("dp"))])


def column_swap(tensor):
    return lax.ppermute(tensor, "dp", [(d, d ^ 2) for d in range(lax.axis_size("dp"))])


def assemble_kernel(origin_ref, column_ref, *refs):
    pieces, there, out_ref = refs[:RING], refs[RING:-1], refs[-1]
    rows, columns = pieces[0].shape
    for step, piece in enumerate(pieces):
        here = pl.ds(pl.multiple_of(origin_ref[step] * rows, 16), rows)
        if there:
            out_ref[here, lanes_of(column_ref[0], columns)] = piece[...]
            out_ref[here, lanes_of(1 - column_ref[0], columns)] = there[step][...]
        else:
            out_ref[here, :] = piece[...]


def assemble(origins, column, pieces, there=()):
    rows, columns = pieces[0].shape
    shape = (RING * rows, columns * (2 if there else 1))
    return pl.pallas_call(
        assemble_kernel,
        grid_spec=pltpu.PrefetchScalarGridSpec(
            num_scalar_prefetch=2,
            grid=(1,),
            in_specs=[whole((rows, columns))] * (len(pieces) + len(there)),
            out_specs=whole(shape),
        ),
        out_shape=jax.ShapeDtypeStruct(shape, pieces[0].dtype),
        compiler_params=pltpu.CompilerParams(vmem_limit_bytes=VMEM_BYTES),
        cost_estimate=pl.CostEstimate(
            flops=0, bytes_accessed=4 * shape[0] * shape[1], transcendentals=0
        ),
        name="assemble",
    )(origins, column, *pieces, *there)


def after(tensor, *others):
    return lax.optimization_barrier((tensor, *others))[0]


def core_way():
    return 1 - 2 * (lax.axis_index("dp") % 2)


def ring_origins():
    place = ring_place(lax.axis_index("fsdp"))
    return ring_member(
        place - core_way() * jnp.arange(RING, dtype=jnp.int32) + RING
    ).astype(jnp.int32)


class RingSum:
    def __init__(self, mine, arrived):
        self.mine, self.arrived = mine, arrived
        place = ring_place(lax.axis_index("fsdp"))
        self.owners = [ring_member(place - core_way() * (s + 1) + 2 * RING) for s in range(RING)]
        self.totals = []

    def term(self):
        parts = []
        for own, arrived in zip(self.mine, self.arrived):
            rows = own.shape[0] // RING
            start = self.owners[len(self.totals)] * rows
            part = lax.dynamic_slice_in_dim(own, start, rows, 0).astype(wide)
            parts.append(part + lax.dynamic_slice_in_dim(arrived, start, rows, 0).astype(wide))
        return parts[0] if len(parts) == 1 else jnp.concatenate(parts, axis=0)

    def begin(self, *others):
        if others:
            self.mine = [after(self.mine[0], *others), *self.mine[1:]]
        self.totals.append(self.term().astype(low))

    def step(self, *others):
        total = self.totals[-1]
        moved = ring_next(after(total, *others) if others else total)
        self.totals.append((moved.astype(wide) + self.term()).astype(low))

    def last(self):
        return self.totals[-1]


class Turns:
    def __init__(self):
        self.results = []

    def step(self, ring, *others):
        ring.step(*self.results[-2:-1], *others)
        self.results.append(ring.last())


def gather_rows(shard):
    mine = lax.all_gather(shard, "fsdp", axis=0, tiled=True)
    return mine, core_swap(mine)


def core_sum(mine, other):
    return (mine.astype(wide) + core_swap(other).astype(wide)).astype(low)


def scatter_rows(both):
    return lax.psum_scatter(both, "fsdp", scatter_dimension=0, tiled=True)


def over_columns(total, *others):
    total = after(total, *others) if others else total
    total = (total.astype(wide) + column_swap(total).astype(wide)).astype(low)
    return total, core_swap(total)


def sum_everywhere(tensor):
    distance = 1
    while distance < lax.axis_size("dp"):
        pairs = [(d, d ^ distance) for d in range(lax.axis_size("dp"))]
        tensor = tensor + lax.ppermute(tensor, "dp", pairs)
        distance *= 2
    distance = 1
    while distance < lax.axis_size("fsdp"):
        pairs = [(f, f ^ distance) for f in range(lax.axis_size("fsdp"))]
        tensor = tensor + lax.ppermute(tensor, "fsdp", pairs)
        distance *= 2
    return tensor


def on_device(
    inputs,
    cotangent,
    lengths,
    attention_weights,
    attention_momentum,
    attention_average,
    ffn_inputs,
    ffn_inputs_momentum,
    ffn_inputs_average,
    ffn_output,
    ffn_output_momentum,
    ffn_output_average,
    gains,
    gains_momentum,
    gains_average,
):
    micro_count, slot, width = inputs.shape
    hidden = ffn_inputs.shape[2]
    shard, down_rows = ffn_inputs.shape[1], ffn_output.shape[0]
    fsdp_size = lax.axis_size("fsdp")
    replicas = lax.axis_size("dp")
    ringed = fsdp_size == RING
    core = lax.axis_index("dp") % 2
    column = lax.axis_index("dp") // 2
    me = lax.axis_index("fsdp")
    count = micro_count * slot
    half = width // 2
    core_ref = core.astype(jnp.int32).reshape(1)
    other_ref = 1 - core_ref
    column_ref = column.astype(jnp.int32).reshape(1)
    is_first = core == 0

    packed = pack_attention(core_ref, attention_weights, gains)

    def gains_of(weights):
        gain_rows = weights[:, 4 * half : 4 * half + 3].T.astype(wide)
        return jnp.pad(gain_rows, ((0, 5), (0, 0)))

    rows = inputs.reshape(count, width)
    positions = jnp.arange(slot, dtype=jnp.int32)
    valid = (positions[None, :] < lengths).astype(wide).reshape(count, 1)
    errors = (cotangent.reshape(count, width).astype(wide) * valid).astype(low)

    if ringed:
        origins = ring_origins()
        up_part = lax.dynamic_slice(
            ffn_inputs, (core, 0, column * (hidden // 2)), (1, shard, hidden // 2)
        )[0].astype(low)
        down_part = lax.dynamic_slice(
            ffn_output, (0, core * half + column * (half // 2)), (down_rows, half // 2)
        ).astype(low)
        rounds = [(packed, up_part, down_part)]
        swapped = []
        for step in range(1, RING):
            here = rounds[-1]
            extra = list(swapped[-1]) if swapped else []
            if step == 3:
                extra += [errors, valid]
            here = lax.optimization_barrier((*here, *extra))[:3]
            rounds.append(tuple(ring_next(piece) for piece in here))
            swapped.append(tuple(column_swap(piece) for piece in here[1:]))
        rounds[-1] = lax.optimization_barrier(rounds[-1])
        swapped.append(tuple(column_swap(piece) for piece in rounds[-1][1:]))
        w_a_mine = assemble(origins, column_ref, [pieces[0] for pieces in rounds])
        w_a = (w_a_mine, core_swap(w_a_mine))
    else:
        w_a = gather_rows(packed)
        w_gu = gather_rows(
            lax.dynamic_index_in_dim(ffn_inputs, core, 0, keepdims=False).astype(low)
        )
        w_d = gather_rows(lax.dynamic_slice_in_dim(ffn_output, core * half, half, 1).astype(low))
    gains8 = gains_of(w_a[0])
    mixed_mine, *kept_mine = mixer_forward(core_ref, rows, w_a[0], gains8, slot)
    if ringed:
        flat = [*swapped[-1], *swapped[-2], mixed_mine, w_a[1]]
        flat = lax.optimization_barrier(tuple(flat))
        swapped[-2:] = [flat[2:4], flat[:2]]
        w_gu, w_d = [
            assemble(
                origins,
                column_ref,
                [pieces[which + 1] for pieces in rounds],
                [pieces[which] for pieces in swapped],
            )
            for which in range(2)
        ]
        rows = after(rows, w_gu, w_d)
        w_gu, w_d = (w_gu, core_swap(w_gu)), (w_d, core_swap(w_d))
    mixed_other, *rest = mixer_forward(
        other_ref, rows, w_a[1], gains8, slot, (mixed_mine, w_a[0])
    )
    kept_other, (x1, h2, h2t, h1t) = rest[:4], rest[4:]
    gm, gu, gd_mine, gd_other, output, d_x1, d_mixed, go_mine, go_other, grad_two = ffn(
        core_ref, h2, h2t, errors, w_gu, w_d, x1, (mixed_mine, mixed_other), w_a, valid, gains8
    )

    mine_gu, arrived_gu = [gm], [core_swap(gu)]
    mine_do, arrived_do = [gd_mine, go_mine], [core_swap(gd_other), core_swap(go_other)]
    turns = Turns()
    backs = []
    for place in range(4):
        pair = place % 2
        from_half, kept = (other_ref, kept_other) if place < 2 else (core_ref, kept_mine)
        if ringed and place > 0:
            h1t = after(h1t, sum_gu.last(), sum_do.last())
        backs.append(
            mixer_backward(2 * from_half + pair, h1t, gains8, kept, d_mixed, pair, slot)
        )
        if ringed:
            if place == 0:
                sum_gu, sum_do = RingSum(mine_gu, arrived_gu), RingSum(mine_do, arrived_do)
                sum_gu.begin(backs[0][2])
                sum_do.begin(backs[0][2])
            else:
                turns.step(sum_gu, backs[-1][2])
                turns.step(sum_do, backs[-1][2])
    grads, ggo, d_pre = [[back[which] for back in backs] for which in range(3)]
    ggo_mine, ggo_other = jnp.concatenate(ggo[2:], axis=1), jnp.concatenate(ggo[:2], axis=1)
    ggo_left = jnp.where(is_first, ggo_mine, ggo_other)
    ggo_right = jnp.where(is_first, ggo_other, ggo_mine)
    grad_go = jnp.concatenate([ggo_left, ggo_right], axis=1)
    mine_qfv, arrived_qfv = grads[2:], [core_swap(grad) for grad in grads[:2]]

    def finish_input(last):
        parts = [after(d_pre[2], last) if last is not None else d_pre[2], d_pre[3], *d_pre[:2]]
        gradient, grad_one = input_gradient(rows, gains8, parts, w_a, d_x1)
        stacked = jnp.concatenate([grad_one, grad_go, grad_two], axis=0)
        return gradient, sum_everywhere(stacked)

    if ringed:
        sum_qfv = RingSum(mine_qfv, arrived_qfv)
        sum_qfv.begin()
        order = [sum_qfv, sum_gu, sum_do] * 4 + [sum_qfv] * 3
        for step, ring in enumerate(order):
            if step == 5:
                input_grad, gain_grads = finish_input(turns.results[-2])
            turns.step(ring)
        total_gu, total_do, total_qfv = sum_gu.last(), sum_do.last(), sum_qfv.last()
    else:
        total_gu, total_do, total_qfv = [
            jnp.concatenate(
                [
                    scatter_rows((own.astype(wide) + there.astype(wide)).astype(low))
                    for own, there in zip(mine, arrived)
                ],
                axis=0,
            )
            for mine, arrived in (
                (mine_gu, arrived_gu),
                (mine_do, arrived_do),
                (mine_qfv, arrived_qfv),
            )
        ]
        input_grad, gain_grads = finish_input(None)
    sum_gu = over_columns(total_gu)
    sum_do = over_columns(total_do)
    sum_qfv = over_columns(total_qfv, gain_grads)
    sum_d = [total[:down_rows] for total in sum_do]
    sum_o = [total[down_rows:] for total in sum_do]
    sum_gains = lax.dynamic_slice_in_dim(gain_grads, me * gains.shape[1], gains.shape[1], 1)

    scale_rows = 1.0 / math.sqrt(count * fsdp_size * replicas)
    attention_state = (attention_weights, attention_momentum, attention_average)
    ffn_in_state = (ffn_inputs, ffn_inputs_momentum, ffn_inputs_average)
    ffn_out_state = (ffn_output, ffn_output_momentum, ffn_output_average)
    return (
        output.reshape(micro_count, slot, width),
        input_grad.reshape(micro_count, slot, width),
        *update_attention(core_ref, attention_state, sum_qfv, sum_o, matrix_rate * scale_rows),
        *update_ffn_in(core_ref, ffn_in_state, sum_gu, matrix_rate * scale_rows),
        *update_ffn_out(core_ref, ffn_out_state, sum_d, matrix_rate * scale_rows),
        *update(gains, gains_momentum, gains_average, sum_gains, gain_rate * scale_rows),
    )


def solution(mesh):
    rows_split = P(None, ("fsdp", "dp"), None)
    middle_split = P(None, "fsdp", None)
    first_split = P("fsdp", None)
    gains_split = P(None, "fsdp")
    in_specs = (
        (rows_split, rows_split, P(None, ("fsdp", "dp")))
        + (middle_split,) * 6
        + (first_split,) * 3
        + (gains_split,) * 3
    )
    out_specs = (
        (rows_split, rows_split)
        + (middle_split,) * 6
        + (first_split,) * 3
        + (gains_split,) * 3
    )
    return jax.shard_map(
        on_device, mesh=mesh, in_specs=in_specs, out_specs=out_specs, check_vma=False
    )
```

```python
import functools
import math

import jax
import jax.numpy as jnp
from jax import lax
from jax.experimental import pallas as pl
from jax.experimental.pallas import tpu as pltpu
from jax.sharding import PartitionSpec as P

HEAD_DIM = 128
PAIR = 2 * HEAD_DIM

lower_bound = 0.9
momentum_decay = 0.9
average_decay = 0.7
weight_decay = 0.0005
matrix_rate = 0.03
gain_rate = 0.1
low = jnp.bfloat16
wide = jnp.float32
TILE_F = 256
VMEM_BYTES = 60 * 1024 * 1024


def mm(left, right):
    return jnp.dot(left, right, preferred_element_type=wide)


def mm_nt(left, right):
    return lax.dot_general(left, right, (((1,), (1,)), ((), ())), preferred_element_type=wide)


def mm_tn(left, right):
    return lax.dot_general(left, right, (((0,), (0,)), ((), ())), preferred_element_type=wide)


def sigmoid(u):
    return 0.5 * jnp.tanh(0.5 * u) + 0.5


def whole(shape):
    return pl.BlockSpec(shape, lambda *_: (0,) * len(shape), pipeline_mode=pl.Buffered(1))


def split_sum(ones_matrix, tensor):
    high = tensor.astype(low)
    rest = (tensor - high.astype(wide)).astype(low)
    return mm(ones_matrix, high) + mm(ones_matrix, rest)


def triangle(length, lower):
    rows = lax.broadcasted_iota(jnp.int32, (length, length), 0)
    columns = lax.broadcasted_iota(jnp.int32, (length, length), 1)
    kept = rows >= columns if lower else rows <= columns
    return kept.astype(wide).astype(low)


def decay_parts(f_pre, lower_ones):
    share = sigmoid(f_pre)
    gate = lower_bound + (1.0 - lower_bound) * share
    keys_in = (1.0 - lower_bound) * (1.0 - share)
    cumulative = split_sum(lower_ones, jnp.log(gate))
    middle_row = cumulative.shape[0] // 2
    cumulative = cumulative - cumulative[middle_row : middle_row + 1, :]
    return share, gate, keys_in, cumulative


def first_norm(x_ref, gain_row):
    rows = x_ref[...].astype(wide)
    scale = lax.rsqrt(jnp.mean(rows * rows, axis=-1, keepdims=True) + 1e-06)
    return rows * scale, scale


def lanes_of(half, size):
    return pl.ds(pl.multiple_of(half * size, size), size)


def mixer_forward_kernel(
    slot, half_ref, x_ref, w_ref, g_ref, on_ref, q_ref, f_ref, v_ref, o_ref, h_s
):
    @pl.when(pl.program_id(0) == 0)
    def _():
        normed, _ = first_norm(x_ref, None)
        h_s[...] = (normed * g_ref[0:1, :]).astype(low)

    gain_o = g_ref[1:2, lanes_of(half_ref[0] * pl.num_programs(0) + pl.program_id(0), PAIR)]
    pre = mm(h_s[...], w_ref[...])
    q_ref[...] = pre[:, :PAIR]
    f_ref[...] = pre[:, PAIR : 2 * PAIR]
    v_ref[...] = pre[:, 2 * PAIR :].astype(low)
    lower_ones = triangle(slot, True)
    block_rows = lax.broadcasted_iota(jnp.int32, (HEAD_DIM, HEAD_DIM), 0)
    block_columns = lax.broadcasted_iota(jnp.int32, (HEAD_DIM, HEAD_DIM), 1)
    causal = block_rows >= block_columns
    for sequence in range(x_ref.shape[0] // slot):
        rows = slice(sequence * slot, (sequence + 1) * slot)
        q_pre = q_ref[rows, :]
        _, _, keys_in, cumulative = decay_parts(f_ref[rows, :], lower_ones)
        grown = jnp.exp(-cumulative)
        decayed_q = (q_pre * sigmoid(q_pre) * jnp.exp(cumulative)).astype(low)
        grown_k = (keys_in * grown).astype(low)
        values = v_ref[rows, :]
        for head in range(2):
            lanes = slice(head * HEAD_DIM, (head + 1) * HEAD_DIM)
            for block in range(slot // HEAD_DIM):
                start, end = block * HEAD_DIM, (block + 1) * HEAD_DIM
                q_block = decayed_q[start:end, lanes]
                diagonal = mm_nt(q_block, grown_k[start:end, lanes])
                diagonal = jnp.where(causal, diagonal, 0.0).astype(low)
                out = mm(diagonal, values[start:end, lanes])
                if block > 0:
                    scores = mm_nt(q_block, grown_k[:start, lanes]).astype(low)
                    out = out + mm(scores, values[:start, lanes])
                scale = lax.rsqrt(jnp.mean(out * out, axis=-1, keepdims=True) + 1e-05)
                target = slice(sequence * slot + start, sequence * slot + end)
                o_ref[target, lanes] = out
                on_ref[target, lanes] = (out * scale * gain_o[:, lanes]).astype(low)


def mixer_forward_last_kernel(
    slot,
    half_ref,
    x_ref,
    w_ref,
    g_ref,
    before_ref,
    woo_ref,
    wom_ref,
    on_ref,
    q_ref,
    f_ref,
    v_ref,
    o_ref,
    x1_ref,
    h2_ref,
    h2t_ref,
    h1t_ref,
    h_s,
    on_s,
):
    step = pl.program_id(0)
    half = before_ref.shape[1]
    mixer_forward_kernel(
        slot, half_ref, x_ref, w_ref, g_ref, on_ref, q_ref, f_ref, v_ref, o_ref, h_s
    )
    on_s[:, lanes_of(half_ref[0] * pl.num_programs(0) + step, PAIR)] = on_ref[...]

    @pl.when(step == pl.num_programs(0) - 1)
    def _():
        here = lanes_of(half_ref[0], half)
        there = lanes_of(1 - half_ref[0], half)
        on_s[:, there] = before_ref[...]
        h1t_ref[...] = h_s[...].astype(wide).T.astype(low)
        x1_ref[:, here] = x_ref[:, here].astype(wide) + mm(on_s[...], woo_ref[...])
        x1_ref[:, there] = x_ref[:, there].astype(wide) + mm(on_s[...], wom_ref[...])
        x1 = x1_ref[...]
        scale = lax.rsqrt(jnp.mean(x1 * x1, axis=-1, keepdims=True) + 1e-06)
        normed = x1 * scale * g_ref[2:3, :]
        h2_ref[...] = normed.astype(low)
        h2t_ref[...] = normed.T.astype(low)


def mixer_forward(half, rows, weights, gains8, slot, ending=None):
    count, width = rows.shape
    pairs = width // PAIR // 2
    by_pair = pl.BlockSpec((count, PAIR), lambda j, _: (0, j))
    struct = jax.ShapeDtypeStruct
    shape = lambda kind: struct((count, width // 2), kind)
    kernel = mixer_forward_kernel
    in_specs = [
        whole(rows.shape),
        pl.BlockSpec((width, 3 * PAIR), lambda j, _: (0, j)),
        whole(gains8.shape),
    ]
    operands = [half, rows, weights, gains8]
    out_specs = [by_pair] * 5
    out_shape = [shape(low), shape(wide), shape(wide), shape(low), shape(wide)]
    scratch = [pltpu.VMEM((count, width), low)]
    if ending is not None:
        kernel = mixer_forward_last_kernel
        out_weights = pl.BlockSpec((width, width // 2), lambda j, _: (0, 3))
        in_specs += [whole((count, width // 2)), out_weights, out_weights]
        operands += [ending[0], weights, ending[1]]
        out_specs += [whole((count, width))] * 2 + [whole((width, count))] * 2
        out_shape += [
            struct((count, width), wide),
            struct((count, width), low),
            struct((width, count), low),
            struct((width, count), low),
        ]
        scratch += [pltpu.VMEM((count, width), low)]
    return pl.pallas_call(
        functools.partial(kernel, slot),
        grid_spec=pltpu.PrefetchScalarGridSpec(
            num_scalar_prefetch=1,
            grid=(pairs,),
            in_specs=in_specs,
            out_specs=out_specs,
            scratch_shapes=scratch,
        ),
        out_shape=out_shape,
        compiler_params=pltpu.CompilerParams(vmem_limit_bytes=VMEM_BYTES),
        cost_estimate=pl.CostEstimate(
            flops=count * width * 4 * width + 10 * count * slot * width,
            bytes_accessed=count * width * 12 + width * width * 4,
            transcendentals=count * width * 3,
        ),
        name="mixer_forward",
    )(*operands)


def store_down(out_ref, tile, owners):
    if owners is None:
        out_ref[...] = tile
        return
    _, stride, down_rows = owners
    block = math.gcd(down_rows, tile.shape[0])
    first = pl.program_id(0) * (tile.shape[0] // block)
    for part in range(tile.shape[0] // block):
        owner = (first + part) // (down_rows // block)
        inside = (first + part) % (down_rows // block)
        start = pl.multiple_of(owner * stride + inside * block, block)
        out_ref[pl.ds(start, block), :] = tile[part * block : (part + 1) * block, :]


def ffn_tile(
    owners, core_ref, h_ref, ht_ref, e_ref, wm_ref, wu_ref, wdm_ref, wdo_ref, grads, acc_ref, dh_ref
):
    gm_ref, gu_ref, gdm_ref, gdo_ref = grads
    half = wdm_ref.shape[1]
    first = core_ref[0] == 0
    mine = lanes_of(core_ref[0], half)
    other = lanes_of(1 - core_ref[0], half)
    own = mm(h_ref[...], wm_ref[...])
    swapped = mm(h_ref[...], wu_ref[...])
    a = jnp.where(first, own, swapped)
    b = jnp.where(first, swapped, own)
    share = sigmoid(a)
    swish = a * share
    mid = (swish * b).astype(low)
    acc_ref[:, mine] += mm(mid, wdm_ref[...])
    acc_ref[:, other] += mm(mid, wdo_ref[...])
    d_mid = mm_nt(e_ref[:, mine], wdm_ref[...]) + mm_nt(e_ref[:, other], wdo_ref[...])
    for out_ref, columns in ((gdm_ref, mine), (gdo_ref, other)):
        store_down(out_ref, mm_tn(mid, e_ref[:, columns]).astype(low), owners)
    d_a = (d_mid * b * share * (1.0 + a * (1.0 - share))).astype(low)
    d_b = (d_mid * swish).astype(low)
    d_own = jnp.where(first, d_a, d_b)
    d_swapped = jnp.where(first, d_b, d_a)
    gm_ref[...] = mm(ht_ref[...], d_own).astype(low)
    gu_ref[...] = mm(ht_ref[...], d_swapped).astype(low)
    dh_ref[...] += mm_nt(d_own, wm_ref[...]) + mm_nt(d_swapped, wu_ref[...])


def ffn_kernel(
    owners,
    core_ref,
    h_ref,
    ht_ref,
    e_ref,
    wm_ref,
    wu_ref,
    wdm_ref,
    wdo_ref,
    x1_ref,
    onm_ref,
    ono_ref,
    wom_ref,
    woo_ref,
    m_ref,
    g_ref,
    gm_ref,
    gu_ref,
    gdm_ref,
    gdo_ref,
    out_ref,
    dh_s,
    acc_s,
    gom_ref,
    goo_ref,
    g2_ref,
    on_s,
):
    @pl.when(pl.program_id(0) == 0)
    def _():
        acc_s[...] = x1_ref[...]
        dh_s[...] = jnp.zeros_like(dh_s)

    grads = (gm_ref, gu_ref, gdm_ref, gdo_ref)
    ffn_tile(
        owners, core_ref, h_ref, ht_ref, e_ref, wm_ref, wu_ref, wdm_ref, wdo_ref, grads, acc_s, dh_s
    )

    @pl.when(pl.program_id(0) == pl.num_programs(0) - 1)
    def _():
        half = onm_ref.shape[1]
        mine = lanes_of(core_ref[0], half)
        other = lanes_of(1 - core_ref[0], half)
        out_ref[...] = (acc_s[...] * m_ref[...]).astype(low)
        x1 = x1_ref[...]
        scale = lax.rsqrt(jnp.mean(x1 * x1, axis=-1, keepdims=True) + 1e-06)
        normed = x1 * scale
        d_h2 = dh_s[...]
        scaled = d_h2 * g_ref[2:3, :]
        g2_ref[...] = jnp.sum(d_h2 * normed, axis=0, keepdims=True)
        d_x1 = e_ref[...].astype(wide) + scale * (
            scaled - normed * jnp.mean(scaled * normed, axis=-1, keepdims=True)
        )
        dh_s[...] = d_x1
        on_s[...] = d_x1.astype(low)
        acc_s[...] = mm_nt(on_s[:, mine], wom_ref[...]) + mm_nt(on_s[:, other], woo_ref[...])
        for columns, g_down_ref, g_ref_o in ((mine, gdm_ref, gom_ref), (other, gdo_ref, goo_ref)):
            d_1 = on_s[:, columns]
            for which, on_ref in ((core_ref[0], onm_ref), (1 - core_ref[0], ono_ref)):
                grad_o = mm_tn(on_ref[...], d_1).astype(low)
                if owners is None:
                    g_ref_o[pl.ds(pl.multiple_of(which * half, half), half), :] = grad_o
                    continue
                count, stride, down_rows = owners
                rows = stride - down_rows
                for part in range(half // rows):
                    owner = which * (count // 2) + part
                    start = pl.multiple_of(owner * stride + down_rows, math.gcd(stride, down_rows))
                    g_down_ref[pl.ds(start, rows), :] = grad_o[part * rows : (part + 1) * rows, :]


def ffn(core, h2, h2t, errors, w_gu, w_d, x1, mixed, w_a, mask, gains8, owners):
    count, width = h2.shape
    half = width // 2
    hidden = w_gu[0].shape[1]
    full = whole((count, width))
    half_full = whole((count, half))
    square = whole((width, half))
    in_tile = pl.BlockSpec((width, TILE_F), lambda j, _: (0, j))
    out_tile = pl.BlockSpec((TILE_F, half), lambda j, _: (j, 0))
    out_weights = pl.BlockSpec((width, half), lambda j, _: (0, 3), pipeline_mode=pl.Buffered(1))
    down_spec, down_shape, out_spec, out_shape = out_tile, (hidden, half), square, (width, half)
    if owners is not None:
        down_shape, out_shape = (owners[0] * owners[1], half), (16, half)
        down_spec, out_spec = whole(down_shape), whole(out_shape)
    struct = jax.ShapeDtypeStruct
    return pl.pallas_call(
        functools.partial(ffn_kernel, owners),
        grid_spec=pltpu.PrefetchScalarGridSpec(
            num_scalar_prefetch=1,
            grid=(hidden // TILE_F,),
            in_specs=[full, whole(h2t.shape), full, in_tile, in_tile, out_tile, out_tile]
            + [full, half_full, half_full, out_weights, out_weights]
            + [whole((count, 1)), whole((8, width))],
            out_specs=[in_tile, in_tile, down_spec, down_spec]
            + [full, full, full, out_spec, out_spec, whole((1, width))],
            scratch_shapes=[pltpu.VMEM((count, width), low)],
        ),
        out_shape=[struct((width, hidden), low)] * 2
        + [struct(down_shape, low)] * 2
        + [
            struct((count, width), low),
            struct((count, width), wide),
            struct((count, width), wide),
            struct(out_shape, low),
            struct(out_shape, low),
            struct((1, width), wide),
        ],
        compiler_params=pltpu.CompilerParams(vmem_limit_bytes=VMEM_BYTES),
        cost_estimate=pl.CostEstimate(
            flops=16 * count * width * hidden,
            bytes_accessed=count * width * 20 + width * hidden * 12,
            transcendentals=count * hidden,
        ),
        name="ffn",
    )(core, h2, h2t, errors, *w_gu, *w_d, x1, *mixed, *w_a, mask, gains8)


def mixer_backward_kernel(
    slot,
    half_ref,
    ht_ref,
    g_ref,
    q_ref,
    f_ref,
    v_ref,
    o_ref,
    don_ref,
    grad_ref,
    ggo_ref,
    dpre_ref,
):
    gain_o = g_ref[1:2, lanes_of(half_ref[0], PAIR)]
    lower_ones = triangle(slot, True)
    upper_ones = triangle(slot, False)
    block_rows = lax.broadcasted_iota(jnp.int32, (HEAD_DIM, HEAD_DIM), 0)
    block_columns = lax.broadcasted_iota(jnp.int32, (HEAD_DIM, HEAD_DIM), 1)
    causal = block_rows >= block_columns
    causal_t = block_rows <= block_columns
    blocks = slot // HEAD_DIM
    ggo_total = jnp.zeros((1, PAIR), wide)
    for sequence in range(q_ref.shape[0] // slot):
        rows = slice(sequence * slot, (sequence + 1) * slot)
        d_on = don_ref[rows, :]
        out = o_ref[rows, :]
        d_out_parts = []
        ggo_parts = []
        for head in range(2):
            lanes = slice(head * HEAD_DIM, (head + 1) * HEAD_DIM)
            out_h, d_on_h = out[:, lanes], d_on[:, lanes]
            scale = lax.rsqrt(jnp.mean(out_h * out_h, axis=-1, keepdims=True) + 1e-05)
            normed = out_h * scale
            ggo_parts.append(jnp.sum(d_on_h * normed, axis=0, keepdims=True))
            scaled = d_on_h * gain_o[:, lanes]
            inner = jnp.mean(scaled * normed, axis=-1, keepdims=True)
            d_out_parts.append((scale * (scaled - normed * inner)).astype(low))
        ggo_total = ggo_total + jnp.concatenate(ggo_parts, axis=1)

        q_pre = q_ref[rows, :]
        share, gate, keys_in, cumulative = decay_parts(f_ref[rows, :], lower_ones)
        grown = jnp.exp(-cumulative)
        shrunk = jnp.exp(cumulative)
        q_share = sigmoid(q_pre)
        decayed_q = (q_pre * q_share * shrunk).astype(low)
        grown_k = (keys_in * grown).astype(low)
        values = v_ref[rows, :]
        dq_parts, dk_parts, dv_parts = [], [], []
        for head in range(2):
            lanes = slice(head * HEAD_DIM, (head + 1) * HEAD_DIM)
            q_h, k_h, v_h = decayed_q[:, lanes], grown_k[:, lanes], values[:, lanes]
            d_out = d_out_parts[head]
            dq_blocks, dk_blocks, dv_blocks = [], [], []
            for block in range(blocks):
                start, end = block * HEAD_DIM, (block + 1) * HEAD_DIM
                here = slice(start, end)
                d_scores = mm_nt(d_out[here], v_h[here])
                d_scores = jnp.where(causal, d_scores, 0.0).astype(low)
                d_q = mm(d_scores, k_h[here])
                if block > 0:
                    before = slice(0, start)
                    d_scores = mm_nt(d_out[here], v_h[before]).astype(low)
                    d_q = d_q + mm(d_scores, k_h[before])
                dq_blocks.append(d_q)
                scores = jnp.where(causal_t, mm_nt(k_h[here], q_h[here]), 0.0).astype(low)
                d_scores = jnp.where(causal_t, mm_nt(v_h[here], d_out[here]), 0.0).astype(low)
                d_v = mm(scores, d_out[here])
                d_k = mm(d_scores, q_h[here])
                if block < blocks - 1:
                    after = slice(end, slot)
                    scores = mm_nt(k_h[here], q_h[after]).astype(low)
                    d_scores = mm_nt(v_h[here], d_out[after]).astype(low)
                    d_v = d_v + mm(scores, d_out[after])
                    d_k = d_k + mm(d_scores, q_h[after])
                dk_blocks.append(d_k)
                dv_blocks.append(d_v)
            dq_parts.append(jnp.concatenate(dq_blocks, axis=0))
            dk_parts.append(jnp.concatenate(dk_blocks, axis=0))
            dv_parts.append(jnp.concatenate(dv_blocks, axis=0))
        d_decayed = jnp.concatenate(dq_parts, axis=1)
        d_grown = jnp.concatenate(dk_parts, axis=1)
        d_value = jnp.concatenate(dv_parts, axis=1)
        d_cumulative = decayed_q.astype(wide) * d_decayed - grown_k.astype(wide) * d_grown
        d_log = split_sum(upper_ones, d_cumulative)
        d_query = d_decayed * shrunk
        d_key = d_grown * grown
        d_q_pre = d_query * q_share * (1.0 + q_pre * (1.0 - q_share))
        d_f_pre = (1.0 - lower_bound) * (d_log / gate - d_key) * share * (1.0 - share)
        dpre_ref[rows, :PAIR] = d_q_pre.astype(low)
        dpre_ref[rows, PAIR : 2 * PAIR] = d_f_pre.astype(low)
        dpre_ref[rows, 2 * PAIR :] = d_value.astype(low)

    ggo_ref[...] = ggo_total
    grad_ref[...] = mm(ht_ref[...], dpre_ref[...]).astype(low)


def mixer_backward(which, h1t, gains8, kept, d_mixed, pair, slot):
    width, count = h1t.shape
    by_pair = pl.BlockSpec((count, PAIR), lambda j, _: (0, pair))
    from_whole = pl.BlockSpec((count, PAIR), lambda j, which: (0, which[0]))
    struct = jax.ShapeDtypeStruct
    return pl.pallas_call(
        functools.partial(mixer_backward_kernel, slot),
        grid_spec=pltpu.PrefetchScalarGridSpec(
            num_scalar_prefetch=1,
            grid=(1,),
            in_specs=[whole((width, count)), whole(gains8.shape)] + [by_pair] * 4 + [from_whole],
            out_specs=[whole((width, 3 * PAIR)), whole((1, PAIR)), whole((count, 3 * PAIR))],
        ),
        out_shape=[
            struct((width, 3 * PAIR), low),
            struct((1, PAIR), wide),
            struct((count, 3 * PAIR), low),
        ],
        compiler_params=pltpu.CompilerParams(vmem_limit_bytes=VMEM_BYTES),
        cost_estimate=pl.CostEstimate(
            flops=count * width * 6 * PAIR + 20 * count * slot * PAIR,
            bytes_accessed=count * width * 5 + width * PAIR * 6,
            transcendentals=count * PAIR * 6,
        ),
        name="mixer_backward",
    )(which, h1t, gains8, *kept, d_mixed)


def input_gradient_rows_kernel(x_ref, g_ref, *refs):
    pre_refs, weight_refs = refs[:4], refs[4:8]
    dx1_ref, dx_ref, g1_ref = refs[8:]
    d_h1 = mm_nt(pre_refs[0][...], weight_refs[0][...])
    for pre_ref, weight_ref in zip(pre_refs[1:], weight_refs[1:]):
        d_h1 = d_h1 + mm_nt(pre_ref[...], weight_ref[...])
    normed, scale = first_norm(x_ref, None)
    scaled = d_h1 * g_ref[0:1, :]
    grad_one = jnp.sum(d_h1 * normed, axis=0, keepdims=True)

    @pl.when(pl.program_id(0) == 0)
    def _():
        g1_ref[...] = grad_one

    @pl.when(pl.program_id(0) > 0)
    def _():
        g1_ref[...] += grad_one

    dx_ref[...] = dx1_ref[...] + scale * (
        scaled - normed * jnp.mean(scaled * normed, axis=-1, keepdims=True)
    )


def input_gradient(rows, gains8, d_pre, weights, d_x1):
    count, width = rows.shape
    block = count // 2
    by_rows = lambda columns: pl.BlockSpec((block, columns), lambda j: (j, 0))
    weight_specs = [
        pl.BlockSpec((width, 3 * PAIR), lambda j, p=p: (0, p), pipeline_mode=pl.Buffered(1))
        for p in (0, 1, 0, 1)
    ]
    struct = jax.ShapeDtypeStruct
    return pl.pallas_call(
        input_gradient_rows_kernel,
        grid=(count // block,),
        in_specs=[by_rows(width), whole(gains8.shape)]
        + [by_rows(3 * PAIR)] * 4
        + weight_specs
        + [by_rows(width)],
        out_specs=[by_rows(width), whole((1, width))],
        out_shape=[struct((count, width), wide), struct((1, width), wide)],
        compiler_params=pltpu.CompilerParams(vmem_limit_bytes=VMEM_BYTES),
        cost_estimate=pl.CostEstimate(
            flops=6 * count * width * width,
            bytes_accessed=count * width * 16 + width * width * 6,
            transcendentals=0,
        ),
        name="input_gradient",
    )(rows, gains8, *d_pre, weights[0], weights[0], weights[1], weights[1], d_x1)


def update(weight, momentum, average, gradient, step_rate):
    new_momentum = momentum_decay * momentum + gradient
    direction = gradient + momentum_decay * new_momentum + weight_decay * weight
    new_weight = weight - step_rate * direction
    new_average = average_decay * average + (1.0 - average_decay) * new_weight
    return (new_momentum, new_average, new_weight)


def update_kernel(pick, step_rate, core_ref, w_ref, m_ref, a_ref, *refs):
    sums, outs = refs[:-3], refs[-3:]
    gradient = pick(core_ref[0], *[s[...] for s in sums]).astype(wide).reshape(w_ref.shape)
    results = update(w_ref[...], m_ref[...], a_ref[...], gradient, step_rate)
    for out, result in zip(outs, results):
        out[...] = result


def update_call(core, state, sums, grid, state_spec, sum_specs, pick, step_rate, name):
    struct = jax.ShapeDtypeStruct(state[0].shape, wide)
    size = math.prod(state[0].shape)
    return pl.pallas_call(
        functools.partial(update_kernel, pick, step_rate),
        grid_spec=pltpu.PrefetchScalarGridSpec(
            num_scalar_prefetch=1,
            grid=grid,
            in_specs=[state_spec] * 3 + sum_specs,
            out_specs=[state_spec] * 3,
        ),
        out_shape=[struct] * 3,
        compiler_params=pltpu.CompilerParams(vmem_limit_bytes=VMEM_BYTES),
        cost_estimate=pl.CostEstimate(flops=10 * size, bytes_accessed=26 * size, transcendentals=0),
        name=name,
    )(core, *state, *sums)


def update_attention(core, state, qfv, out, step_rate):
    _, shard, width = state[0].shape
    down_rows = out[0].shape[0] - shard

    def pick(core_index, qfv_mine, qfv_other, out_mine, out_other):
        own = pl.program_id(1) == core_index
        proj = jnp.where(own, qfv_mine.astype(wide), qfv_other.astype(wide))
        last = jnp.where(own, out_mine[down_rows:].astype(wide), out_other[down_rows:].astype(wide))
        for kind in range(3):
            parts = [proj[pair * shard :, kind * PAIR :][:shard, :PAIR] for pair in range(2)]
            chosen = jnp.concatenate(parts, axis=1)
            last = jnp.where(pl.program_id(0) == kind, chosen, last)
        return last

    return update_call(
        core,
        state,
        (*qfv, *out),
        (4, 2),
        pl.BlockSpec((1, shard, width // 2), lambda kind, half, _: (kind, 0, half)),
        [whole(total.shape) for total in (*qfv, *out)],
        pick,
        step_rate,
        "update_attention",
    )


def update_ffn_in(core, state, sums, step_rate):
    _, shard, hidden = state[0].shape

    def pick(core_index, mine, other):
        own = pl.program_id(0) == core_index
        return jnp.where(own, mine.astype(wide), other.astype(wide))

    return update_call(
        core,
        state,
        sums,
        (2,),
        pl.BlockSpec((1, shard, hidden), lambda kind, _: (kind, 0, 0)),
        [whole(total.shape) for total in sums],
        pick,
        step_rate,
        "update_ffn_in",
    )


def update_ffn_out(core, state, sums, step_rate):
    shard, width = state[0].shape

    def pick(core_index, mine, other):
        own = pl.program_id(0) == core_index
        return jnp.where(own, mine[:shard].astype(wide), other[:shard].astype(wide))

    return update_call(
        core,
        state,
        sums,
        (2,),
        pl.BlockSpec((shard, width // 2), lambda j, _: (0, j)),
        [whole(total.shape) for total in sums],
        pick,
        step_rate,
        "update_ffn_out",
    )


def pack_kernel(core_ref, w_ref, g_ref, out_ref):
    pairs = w_ref.shape[2] // PAIR
    for pair in range(pairs):
        for kind in range(3):
            start = (pair * 3 + kind) * PAIR
            piece = w_ref[kind, :, pair * PAIR : (pair + 1) * PAIR]
            out_ref[:, start : start + PAIR] = piece.astype(low)
    start = 3 * pairs * PAIR
    out_ref[:, start : start + pairs * PAIR] = w_ref[3].astype(low)
    start += pairs * PAIR
    out_ref[:, start:] = g_ref[...].astype(low)


def pack_attention(core, weights, gains):
    _, shard, width = weights.shape
    half = width // 2
    gain_columns = jnp.pad(gains.T, ((0, 0), (0, HEAD_DIM - 3)))
    columns = 4 * half + HEAD_DIM
    return pl.pallas_call(
        pack_kernel,
        grid_spec=pltpu.PrefetchScalarGridSpec(
            num_scalar_prefetch=1,
            grid=(1,),
            in_specs=[
                pl.BlockSpec((4, shard, half), lambda j, core: (0, 0, core[0])),
                whole((shard, HEAD_DIM)),
            ],
            out_specs=whole((shard, columns)),
        ),
        out_shape=jax.ShapeDtypeStruct((shard, columns), low),
        name="pack_attention",
    )(core, weights, gain_columns)


RING = 8


def ring_place(index):
    return jnp.where(index % 2 == 0, index // 2, RING - 1 - index // 2)


def ring_member(place):
    place = place % RING
    return jnp.where(place < RING // 2, 2 * place, 2 * RING - 1 - 2 * place)


def ring_next(tensor):
    cycle = [0, 2, 4, 6, 7, 5, 3, 1]
    replicas = lax.axis_size("dp")
    pairs = []
    for place, member in enumerate(cycle):
        for replica in range(replicas):
            target = cycle[(place + (1 if replica % 2 == 0 else -1)) % RING]
            pairs.append((member * replicas + replica, target * replicas + replica))
    return lax.ppermute(tensor, ("fsdp", "dp"), pairs)


def core_swap(tensor):
    return lax.ppermute(tensor, "dp", [(d, d ^ 1) for d in range(lax.axis_size("dp"))])


def column_swap(tensor):
    return lax.ppermute(tensor, "dp", [(d, d ^ 2) for d in range(lax.axis_size("dp"))])


def place_kernel(step, side, origin_ref, column_ref, piece_ref, *refs):
    out_ref, semaphore = refs[-2:]
    rows, columns = piece_ref.shape
    lane = (0, column_ref[0], 1 - column_ref[0])[side]
    here = pl.ds(pl.multiple_of(origin_ref[step] * rows, 16), rows)
    target = out_ref.at[here, lanes_of(lane, columns)]
    copy = pltpu.make_async_copy(piece_ref, target, semaphore)
    copy.start()
    copy.wait()


def place(origins, column, step, side, piece, before):
    parts = 2 if side else 1
    rows, columns = piece.shape
    anywhere = pl.BlockSpec(memory_space=pl.ANY)
    held = [] if before is None else [before]
    return pl.pallas_call(
        functools.partial(place_kernel, step, side),
        grid_spec=pltpu.PrefetchScalarGridSpec(
            num_scalar_prefetch=2,
            grid=(1,),
            in_specs=[whole((rows, columns))] + [anywhere] * len(held),
            out_specs=anywhere,
            scratch_shapes=[pltpu.SemaphoreType.DMA(())],
        ),
        out_shape=jax.ShapeDtypeStruct((RING * rows, columns * parts), piece.dtype),
        input_output_aliases={3: 0} if held else {},
        cost_estimate=pl.CostEstimate(
            flops=0, bytes_accessed=4 * rows * columns, transcendentals=0
        ),
        name="place",
    )(origins, column, piece, *held)


def after(tensor, *others):
    return lax.optimization_barrier((tensor, *others))[0]


def core_way():
    return 1 - 2 * (lax.axis_index("dp") % 2)


def ring_origins():
    place = ring_place(lax.axis_index("fsdp"))
    return ring_member(
        place - core_way() * jnp.arange(RING, dtype=jnp.int32) + RING
    ).astype(jnp.int32)


class RingSum:
    def __init__(self, mine, arrived):
        self.mine, self.arrived = mine, arrived
        place = ring_place(lax.axis_index("fsdp"))
        self.owners = [ring_member(place - core_way() * (s + 1) + 2 * RING) for s in range(RING)]
        self.totals = []

    def term(self):
        parts = []
        for own, arrived in zip(self.mine, self.arrived):
            rows = own.shape[0] // RING
            start = self.owners[len(self.totals)] * rows
            part = lax.dynamic_slice_in_dim(own, start, rows, 0).astype(wide)
            parts.append(part + lax.dynamic_slice_in_dim(arrived, start, rows, 0).astype(wide))
        return parts[0] if len(parts) == 1 else jnp.concatenate(parts, axis=0)

    def begin(self, *others):
        if others:
            self.mine = [after(self.mine[0], *others), *self.mine[1:]]
        self.totals.append(self.term().astype(low))

    def step(self, *before, arriving=()):
        total = self.totals[-1]
        moved = ring_next(after(total, *before) if before else total)
        moved = after(moved, *arriving) if arriving else moved
        self.totals.append((moved.astype(wide) + self.term().astype(wide)).astype(low))

    def last(self):
        return self.totals[-1]


def gather_rows(shard):
    mine = lax.all_gather(shard, "fsdp", axis=0, tiled=True)
    return mine, core_swap(mine)


def core_sum(mine, other):
    return (mine.astype(wide) + core_swap(other).astype(wide)).astype(low)


def scatter_rows(both):
    return lax.psum_scatter(both, "fsdp", scatter_dimension=0, tiled=True)


def over_columns(total):
    total = (total.astype(wide) + column_swap(total).astype(wide)).astype(low)
    return total, core_swap(total)


def exchanges():
    for axis in ("dp", "fsdp"):
        distance = 1
        while distance < lax.axis_size(axis):
            yield axis, [(d, d ^ distance) for d in range(lax.axis_size(axis))]
            distance *= 2


def on_device(
    inputs,
    cotangent,
    lengths,
    attention_weights,
    attention_momentum,
    attention_average,
    ffn_inputs,
    ffn_inputs_momentum,
    ffn_inputs_average,
    ffn_output,
    ffn_output_momentum,
    ffn_output_average,
    gains,
    gains_momentum,
    gains_average,
):
    micro_count, slot, width = inputs.shape
    hidden = ffn_inputs.shape[2]
    shard, down_rows = ffn_inputs.shape[1], ffn_output.shape[0]
    fsdp_size = lax.axis_size("fsdp")
    replicas = lax.axis_size("dp")
    ringed = fsdp_size == RING
    core = lax.axis_index("dp") % 2
    column = lax.axis_index("dp") // 2
    me = lax.axis_index("fsdp")
    count = micro_count * slot
    half = width // 2
    core_ref = core.astype(jnp.int32).reshape(1)
    other_ref = 1 - core_ref
    column_ref = column.astype(jnp.int32).reshape(1)
    is_first = core == 0

    packed = pack_attention(core_ref, attention_weights, gains)

    def gains_of(weights):
        gain_rows = weights[:, 4 * half : 4 * half + 3].T.astype(wide)
        return jnp.pad(gain_rows, ((0, 5), (0, 0)))

    rows = inputs.reshape(count, width)
    positions = jnp.arange(slot, dtype=jnp.int32)
    valid = (positions[None, :] < lengths).astype(wide).reshape(count, 1)
    errors = (cotangent.reshape(count, width).astype(wide) * valid).astype(low)

    if ringed:
        origins = ring_origins()
        up_part = lax.dynamic_slice(
            ffn_inputs, (core, 0, column * (hidden // 2)), (1, shard, hidden // 2)
        )[0].astype(low)
        down_part = lax.dynamic_slice(
            ffn_output, (0, core * half + column * (half // 2)), (down_rows, half // 2)
        ).astype(low)
        wholes = [None] * 3

        def put(step, which, piece, other=False):
            side = 0 if which == 0 else 1 + other
            wholes[which] = place(origins, column_ref, step, side, piece, wholes[which])

        here, there = (packed, up_part, down_part), None
        for step in range(RING):
            if step < RING - 1:
                onward = tuple(ring_next(piece) for piece in here)
            across = tuple(column_swap(piece) for piece in here[1:])
            for which, piece in enumerate(here):
                put(step, which, piece)
            if there is not None:
                for which, piece in enumerate(there):
                    put(step - 1, which + 1, piece, True)
            extra = [errors, valid] if step == 2 else []
            if step < RING - 1:
                tied = lax.optimization_barrier((*onward, *across, *wholes, *extra))
                here, there, wholes = tied[:3], tied[3:5], list(tied[5:8])
        w_a = (wholes[0], core_swap(wholes[0]))
    else:
        w_a = gather_rows(packed)
        w_gu = gather_rows(
            lax.dynamic_index_in_dim(ffn_inputs, core, 0, keepdims=False).astype(low)
        )
        w_d = gather_rows(lax.dynamic_slice_in_dim(ffn_output, core * half, half, 1).astype(low))
    gains8 = gains_of(w_a[0])
    mixed_mine, *kept_mine = mixer_forward(core_ref, rows, w_a[0], gains8, slot)
    if ringed:
        across = lax.optimization_barrier((*across, mixed_mine, w_a[1]))[:2]
        for which, piece in enumerate(across):
            put(RING - 1, which + 1, piece, True)
        rows = after(rows, *wholes[1:])
        w_gu, w_d = [(array, core_swap(array)) for array in wholes[1:]]
    mixed_other, *rest = mixer_forward(
        other_ref, rows, w_a[1], gains8, slot, (mixed_mine, w_a[0])
    )
    kept_other, (x1, h2, h2t, h1t) = rest[:4], rest[4:]
    owners = (fsdp_size, down_rows + shard, down_rows) if ringed else None
    gm, gu, gd_mine, gd_other, output, d_x1, d_mixed, go_mine, go_other, grad_two = ffn(
        core_ref, h2, h2t, errors, w_gu, w_d, x1, (mixed_mine, mixed_other), w_a, valid, gains8, owners
    )

    mine_gu, arrived_gu = [gm], [core_swap(gu)]
    if ringed:
        mine_do, arrived_do = [gd_mine], [core_swap(gd_other)]
    else:
        mine_do, arrived_do = [gd_mine, go_mine], [core_swap(gd_other), core_swap(go_other)]
    backs = []
    for place_of in range(4):
        pair = place_of % 2
        from_half, kept = (other_ref, kept_other) if place_of < 2 else (core_ref, kept_mine)
        if ringed and place_of > 0:
            h1t = after(h1t, sum_gu.last(), sum_do.last())
        backs.append(
            mixer_backward(2 * from_half + pair, h1t, gains8, kept, d_mixed, pair, slot)
        )
        if ringed and place_of == 0:
            sum_gu, sum_do = RingSum(mine_gu, arrived_gu), RingSum(mine_do, arrived_do)
            sum_do.begin(backs[0][2])
            sum_gu.begin(backs[0][2])
        elif ringed:
            sum_do.step(arriving=(backs[-1][2],))
            sum_gu.step(arriving=(backs[-1][2],))
    grads, ggo, d_pre = [[back[which] for back in backs] for which in range(3)]
    ggo_mine, ggo_other = jnp.concatenate(ggo[2:], axis=1), jnp.concatenate(ggo[:2], axis=1)
    ggo_left = jnp.where(is_first, ggo_mine, ggo_other)
    ggo_right = jnp.where(is_first, ggo_other, ggo_mine)
    grad_go = jnp.concatenate([ggo_left, ggo_right], axis=1)
    mine_qfv, arrived_qfv = grads[2:], [core_swap(grad) for grad in grads[:2]]

    def finish_input(*others):
        last = after(d_pre[2], *others) if others else d_pre[2]
        gradient, grad_one = input_gradient(
            rows, gains8, [last, d_pre[3], *d_pre[:2]], w_a, d_x1
        )
        return gradient, jnp.concatenate([grad_one, grad_go, grad_two], axis=0)

    if ringed:
        sum_qfv = RingSum(mine_qfv, arrived_qfv)
        sum_qfv.begin()
        pending = exchanges()
        before = []
        for step in range(1, RING):
            sum_qfv.step(*before)
            if step <= 4:
                sum_do.step()
                sum_gu.step()
            if step == 2:
                input_grad, gain_grads = finish_input(sum_qfv.last())
                before = [gain_grads]
            elif step > 2:
                axis, pairs = next(pending)
                gain_grads = gain_grads + lax.ppermute(gain_grads, axis, pairs)
                before = [gain_grads]
        total_gu, total_do, total_qfv = sum_gu.last(), sum_do.last(), sum_qfv.last()
    else:
        total_gu, total_do, total_qfv = [
            jnp.concatenate(
                [
                    scatter_rows((own.astype(wide) + there.astype(wide)).astype(low))
                    for own, there in zip(mine, arrived)
                ],
                axis=0,
            )
            for mine, arrived in (
                (mine_gu, arrived_gu),
                (mine_do, arrived_do),
                (mine_qfv, arrived_qfv),
            )
        ]
        input_grad, gain_grads = finish_input()
        pending = exchanges()
    sum_gu = over_columns(total_gu)
    sum_do = over_columns(total_do)
    for axis, pairs in pending:
        gain_grads = gain_grads + lax.ppermute(gain_grads, axis, pairs)
    sum_gains = lax.dynamic_slice_in_dim(gain_grads, me * gains.shape[1], gains.shape[1], 1)

    scale_rows = 1.0 / math.sqrt(count * fsdp_size * replicas)
    attention_state = (attention_weights, attention_momentum, attention_average)
    ffn_in_state = (ffn_inputs, ffn_inputs_momentum, ffn_inputs_average)
    ffn_out_state = (ffn_output, ffn_output_momentum, ffn_output_average)
    new_in = update_ffn_in(core_ref, ffn_in_state, sum_gu, matrix_rate * scale_rows)
    new_out = update_ffn_out(core_ref, ffn_out_state, sum_do, matrix_rate * scale_rows)
    there = after(column_swap(total_qfv), new_in[0], new_out[0])
    sum_qfv = (total_qfv.astype(wide) + there.astype(wide)).astype(low)
    sum_qfv = (sum_qfv, core_swap(sum_qfv))
    return (
        output.reshape(micro_count, slot, width),
        input_grad.reshape(micro_count, slot, width),
        *update_attention(core_ref, attention_state, sum_qfv, sum_do, matrix_rate * scale_rows),
        *new_in,
        *new_out,
        *update(gains, gains_momentum, gains_average, sum_gains, gain_rate * scale_rows),
    )


def solution(mesh):
    rows_split = P(None, ("fsdp", "dp"), None)
    middle_split = P(None, "fsdp", None)
    first_split = P("fsdp", None)
    gains_split = P(None, "fsdp")
    in_specs = (
        (rows_split, rows_split, P(None, ("fsdp", "dp")))
        + (middle_split,) * 6
        + (first_split,) * 3
        + (gains_split,) * 3
    )
    out_specs = (
        (rows_split, rows_split)
        + (middle_split,) * 6
        + (first_split,) * 3
        + (gains_split,) * 3
    )
    return jax.shard_map(
        on_device, mesh=mesh, in_specs=in_specs, out_specs=out_specs, check_vma=False
    )
```

```python
import functools
import math

import jax
import jax.numpy as jnp
from jax import lax
from jax.experimental import pallas as pl
from jax.experimental.pallas import tpu as pltpu
from jax.sharding import PartitionSpec as P

HEAD_DIM = 128
PAIR = 2 * HEAD_DIM

lower_bound = 0.9
momentum_decay = 0.9
average_decay = 0.7
weight_decay = 0.0005
matrix_rate = 0.03
gain_rate = 0.1
low = jnp.bfloat16
wide = jnp.float32
TILE_F = 256
VMEM_BYTES = 60 * 1024 * 1024


def mm(left, right):
    return jnp.dot(left, right, preferred_element_type=wide)


def mm_nt(left, right):
    return lax.dot_general(left, right, (((1,), (1,)), ((), ())), preferred_element_type=wide)


def mm_tn(left, right):
    return lax.dot_general(left, right, (((0,), (0,)), ((), ())), preferred_element_type=wide)


def sigmoid(u):
    return 0.5 * jnp.tanh(0.5 * u) + 0.5


def whole(shape):
    return pl.BlockSpec(shape, lambda *_: (0,) * len(shape), pipeline_mode=pl.Buffered(1))


def split_sum(ones_matrix, tensor):
    high = tensor.astype(low)
    rest = (tensor - high.astype(wide)).astype(low)
    return mm(ones_matrix, high) + mm(ones_matrix, rest)


def triangle(length, lower):
    rows = lax.broadcasted_iota(jnp.int32, (length, length), 0)
    columns = lax.broadcasted_iota(jnp.int32, (length, length), 1)
    kept = rows >= columns if lower else rows <= columns
    return kept.astype(wide).astype(low)


def decay_parts(f_pre, lower_ones):
    share = sigmoid(f_pre)
    gate = lower_bound + (1.0 - lower_bound) * share
    keys_in = (1.0 - lower_bound) * (1.0 - share)
    cumulative = split_sum(lower_ones, jnp.log(gate))
    middle_row = cumulative.shape[0] // 2
    cumulative = cumulative - cumulative[middle_row : middle_row + 1, :]
    return share, gate, keys_in, cumulative


def first_norm(x_ref, gain_row):
    rows = x_ref[...].astype(wide)
    scale = lax.rsqrt(jnp.mean(rows * rows, axis=-1, keepdims=True) + 1e-06)
    return rows * scale, scale


def lanes_of(half, size):
    return pl.ds(pl.multiple_of(half * size, size), size)


def mixer_forward_kernel(
    slot, half_ref, x_ref, w_ref, g_ref, on_ref, q_ref, f_ref, v_ref, o_ref, h_s
):
    @pl.when(pl.program_id(0) == 0)
    def _():
        normed, _ = first_norm(x_ref, None)
        h_s[...] = (normed * g_ref[0:1, :]).astype(low)

    gain_o = g_ref[1:2, lanes_of(half_ref[0] * pl.num_programs(0) + pl.program_id(0), PAIR)]
    pre = mm(h_s[...], w_ref[...])
    q_ref[...] = pre[:, :PAIR]
    f_ref[...] = pre[:, PAIR : 2 * PAIR]
    v_ref[...] = pre[:, 2 * PAIR :].astype(low)
    lower_ones = triangle(slot, True)
    block_rows = lax.broadcasted_iota(jnp.int32, (HEAD_DIM, HEAD_DIM), 0)
    block_columns = lax.broadcasted_iota(jnp.int32, (HEAD_DIM, HEAD_DIM), 1)
    causal = block_rows >= block_columns
    for sequence in range(x_ref.shape[0] // slot):
        rows = slice(sequence * slot, (sequence + 1) * slot)
        q_pre = q_ref[rows, :]
        _, _, keys_in, cumulative = decay_parts(f_ref[rows, :], lower_ones)
        grown = jnp.exp(-cumulative)
        decayed_q = (q_pre * sigmoid(q_pre) * jnp.exp(cumulative)).astype(low)
        grown_k = (keys_in * grown).astype(low)
        values = v_ref[rows, :]
        for head in range(2):
            lanes = slice(head * HEAD_DIM, (head + 1) * HEAD_DIM)
            for block in range(slot // HEAD_DIM):
                start, end = block * HEAD_DIM, (block + 1) * HEAD_DIM
                q_block = decayed_q[start:end, lanes]
                diagonal = mm_nt(q_block, grown_k[start:end, lanes])
                diagonal = jnp.where(causal, diagonal, 0.0).astype(low)
                out = mm(diagonal, values[start:end, lanes])
                if block > 0:
                    scores = mm_nt(q_block, grown_k[:start, lanes]).astype(low)
                    out = out + mm(scores, values[:start, lanes])
                scale = lax.rsqrt(jnp.mean(out * out, axis=-1, keepdims=True) + 1e-05)
                target = slice(sequence * slot + start, sequence * slot + end)
                o_ref[target, lanes] = out
                on_ref[target, lanes] = (out * scale * gain_o[:, lanes]).astype(low)


def mixer_forward_last_kernel(
    slot,
    half_ref,
    x_ref,
    w_ref,
    g_ref,
    before_ref,
    woo_ref,
    wom_ref,
    on_ref,
    q_ref,
    f_ref,
    v_ref,
    o_ref,
    x1_ref,
    h2_ref,
    h2t_ref,
    h1t_ref,
    h_s,
    on_s,
):
    step = pl.program_id(0)
    half = before_ref.shape[1]
    mixer_forward_kernel(
        slot, half_ref, x_ref, w_ref, g_ref, on_ref, q_ref, f_ref, v_ref, o_ref, h_s
    )
    on_s[:, lanes_of(half_ref[0] * pl.num_programs(0) + step, PAIR)] = on_ref[...]

    @pl.when(step == pl.num_programs(0) - 1)
    def _():
        here = lanes_of(half_ref[0], half)
        there = lanes_of(1 - half_ref[0], half)
        on_s[:, there] = before_ref[...]
        h1t_ref[...] = h_s[...].astype(wide).T.astype(low)
        x1_ref[:, here] = x_ref[:, here].astype(wide) + mm(on_s[...], woo_ref[...])
        x1_ref[:, there] = x_ref[:, there].astype(wide) + mm(on_s[...], wom_ref[...])
        x1 = x1_ref[...]
        scale = lax.rsqrt(jnp.mean(x1 * x1, axis=-1, keepdims=True) + 1e-06)
        normed = x1 * scale * g_ref[2:3, :]
        h2_ref[...] = normed.astype(low)
        h2t_ref[...] = normed.T.astype(low)


def mixer_forward(half, rows, weights, gains8, slot, ending=None):
    count, width = rows.shape
    pairs = width // PAIR // 2
    by_pair = pl.BlockSpec((count, PAIR), lambda j, _: (0, j))
    struct = jax.ShapeDtypeStruct
    shape = lambda kind: struct((count, width // 2), kind)
    kernel = mixer_forward_kernel
    in_specs = [
        whole(rows.shape),
        pl.BlockSpec((width, 3 * PAIR), lambda j, _: (0, j)),
        whole(gains8.shape),
    ]
    operands = [half, rows, weights, gains8]
    out_specs = [by_pair] * 5
    out_shape = [shape(low), shape(wide), shape(wide), shape(low), shape(wide)]
    scratch = [pltpu.VMEM((count, width), low)]
    if ending is not None:
        kernel = mixer_forward_last_kernel
        out_weights = pl.BlockSpec((width, width // 2), lambda j, _: (0, 3))
        in_specs += [whole((count, width // 2)), out_weights, out_weights]
        operands += [ending[0], weights, ending[1]]
        out_specs += [whole((count, width))] * 2 + [whole((width, count))] * 2
        out_shape += [
            struct((count, width), wide),
            struct((count, width), low),
            struct((width, count), low),
            struct((width, count), low),
        ]
        scratch += [pltpu.VMEM((count, width), low)]
    return pl.pallas_call(
        functools.partial(kernel, slot),
        grid_spec=pltpu.PrefetchScalarGridSpec(
            num_scalar_prefetch=1,
            grid=(pairs,),
            in_specs=in_specs,
            out_specs=out_specs,
            scratch_shapes=scratch,
        ),
        out_shape=out_shape,
        compiler_params=pltpu.CompilerParams(vmem_limit_bytes=VMEM_BYTES),
        cost_estimate=pl.CostEstimate(
            flops=count * width * 4 * width + 10 * count * slot * width,
            bytes_accessed=count * width * 12 + width * width * 4,
            transcendentals=count * width * 3,
        ),
        name="mixer_forward",
    )(*operands)


def store_down(out_ref, tile, owners):
    if owners is None:
        out_ref[...] = tile
        return
    _, stride, down_rows = owners
    block = math.gcd(down_rows, tile.shape[0])
    first = pl.program_id(0) * (tile.shape[0] // block)
    for part in range(tile.shape[0] // block):
        owner = (first + part) // (down_rows // block)
        inside = (first + part) % (down_rows // block)
        start = pl.multiple_of(owner * stride + inside * block, block)
        out_ref[pl.ds(start, block), :] = tile[part * block : (part + 1) * block, :]


def ffn_tile(owners, core_ref, refs, grads, acc_ref, dh_ref, scratch):
    h_ref, ht_ref, e_ref, wm_ref, wu_ref, wdm_ref, wdo_ref = refs
    gm_ref, gu_ref, gdm_ref, gdo_ref = grads
    gu_w, down_w, gu_g, down_g = scratch
    half, tile = wdm_ref.shape[1], wm_ref.shape[1]
    mine, other = lanes_of(core_ref[0], half), lanes_of(1 - core_ref[0], half)
    kind, kind_other = lanes_of(core_ref[0], tile), lanes_of(1 - core_ref[0], tile)
    gu_w[:, kind] = wm_ref[...]
    gu_w[:, kind_other] = wu_ref[...]
    down_w[:, mine] = wdm_ref[...]
    down_w[:, other] = wdo_ref[...]
    pre = mm(h_ref[...], gu_w[...])
    a, b = pre[:, :tile], pre[:, tile:]
    share = sigmoid(a)
    swish = a * share
    mid = (swish * b).astype(low)
    d_mid = mm_nt(e_ref[...], down_w[...])
    down_g[...] = mm_tn(mid, e_ref[...]).astype(low)
    d_a = (d_mid * b * (share + swish * (1.0 - share))).astype(low)
    d_b = (d_mid * swish).astype(low)
    d_pre = jnp.concatenate([d_a, d_b], axis=1)
    acc_ref[...] += mm(mid, down_w[...])
    dh_ref[...] += mm_nt(d_pre, gu_w[...])
    gu_g[...] = mm(ht_ref[...], d_pre).astype(low)
    gm_ref[...] = gu_g[:, kind]
    gu_ref[...] = gu_g[:, kind_other]
    store_down(gdm_ref, down_g[:, mine], owners)
    store_down(gdo_ref, down_g[:, other], owners)


def ffn_kernel(
    owners,
    core_ref,
    h_ref,
    ht_ref,
    e_ref,
    wm_ref,
    wu_ref,
    wdm_ref,
    wdo_ref,
    x1_ref,
    onm_ref,
    ono_ref,
    wom_ref,
    woo_ref,
    m_ref,
    g_ref,
    gm_ref,
    gu_ref,
    gdm_ref,
    gdo_ref,
    out_ref,
    dh_s,
    acc_s,
    gom_ref,
    goo_ref,
    g2_ref,
    on_s,
    *scratch,
):
    @pl.when(pl.program_id(0) == 0)
    def _():
        acc_s[...] = x1_ref[...]
        dh_s[...] = jnp.zeros_like(dh_s)

    grads = (gm_ref, gu_ref, gdm_ref, gdo_ref)
    refs = (h_ref, ht_ref, e_ref, wm_ref, wu_ref, wdm_ref, wdo_ref)
    ffn_tile(owners, core_ref, refs, grads, acc_s, dh_s, scratch)

    @pl.when(pl.program_id(0) == pl.num_programs(0) - 1)
    def _():
        half = onm_ref.shape[1]
        mine = lanes_of(core_ref[0], half)
        other = lanes_of(1 - core_ref[0], half)
        out_ref[...] = (acc_s[...] * m_ref[...]).astype(low)
        x1 = x1_ref[...]
        scale = lax.rsqrt(jnp.mean(x1 * x1, axis=-1, keepdims=True) + 1e-06)
        normed = x1 * scale
        d_h2 = dh_s[...]
        scaled = d_h2 * g_ref[2:3, :]
        g2_ref[...] = jnp.sum(d_h2 * normed, axis=0, keepdims=True)
        d_x1 = e_ref[...].astype(wide) + scale * (
            scaled - normed * jnp.mean(scaled * normed, axis=-1, keepdims=True)
        )
        dh_s[...] = d_x1
        on_s[...] = d_x1.astype(low)
        acc_s[...] = mm_nt(on_s[:, mine], wom_ref[...]) + mm_nt(on_s[:, other], woo_ref[...])
        for columns, g_down_ref, g_ref_o in ((mine, gdm_ref, gom_ref), (other, gdo_ref, goo_ref)):
            d_1 = on_s[:, columns]
            for which, on_ref in ((core_ref[0], onm_ref), (1 - core_ref[0], ono_ref)):
                grad_o = mm_tn(on_ref[...], d_1).astype(low)
                if owners is None:
                    g_ref_o[pl.ds(pl.multiple_of(which * half, half), half), :] = grad_o
                    continue
                count, stride, down_rows = owners
                rows = stride - down_rows
                for part in range(half // rows):
                    owner = which * (count // 2) + part
                    start = pl.multiple_of(owner * stride + down_rows, math.gcd(stride, down_rows))
                    g_down_ref[pl.ds(start, rows), :] = grad_o[part * rows : (part + 1) * rows, :]


def ffn(core, h2, h2t, errors, w_gu, w_d, x1, mixed, w_a, mask, gains8, owners):
    count, width = h2.shape
    half = width // 2
    hidden = w_gu[0].shape[1]
    full = whole((count, width))
    half_full = whole((count, half))
    square = whole((width, half))
    in_tile = pl.BlockSpec((width, TILE_F), lambda j, _: (0, j))
    out_tile = pl.BlockSpec((TILE_F, half), lambda j, _: (j, 0))
    out_weights = pl.BlockSpec((width, half), lambda j, _: (0, 3), pipeline_mode=pl.Buffered(1))
    down_spec, down_shape, out_spec, out_shape = out_tile, (hidden, half), square, (width, half)
    if owners is not None:
        down_shape, out_shape = (owners[0] * owners[1], half), (16, half)
        down_spec, out_spec = whole(down_shape), whole(out_shape)
    struct = jax.ShapeDtypeStruct
    return pl.pallas_call(
        functools.partial(ffn_kernel, owners),
        grid_spec=pltpu.PrefetchScalarGridSpec(
            num_scalar_prefetch=1,
            grid=(hidden // TILE_F,),
            in_specs=[full, whole(h2t.shape), full, in_tile, in_tile, out_tile, out_tile]
            + [full, half_full, half_full, out_weights, out_weights]
            + [whole((count, 1)), whole((8, width))],
            out_specs=[in_tile, in_tile, down_spec, down_spec]
            + [full, full, full, out_spec, out_spec, whole((1, width))],
            scratch_shapes=[
                pltpu.VMEM((count, width), low),
                pltpu.VMEM((width, 2 * TILE_F), low),
                pltpu.VMEM((TILE_F, width), low),
                pltpu.VMEM((width, 2 * TILE_F), low),
                pltpu.VMEM((TILE_F, width), low),
            ],
        ),
        out_shape=[struct((width, hidden), low)] * 2
        + [struct(down_shape, low)] * 2
        + [
            struct((count, width), low),
            struct((count, width), wide),
            struct((count, width), wide),
            struct(out_shape, low),
            struct(out_shape, low),
            struct((1, width), wide),
        ],
        compiler_params=pltpu.CompilerParams(vmem_limit_bytes=VMEM_BYTES),
        cost_estimate=pl.CostEstimate(
            flops=16 * count * width * hidden,
            bytes_accessed=count * width * 20 + width * hidden * 12,
            transcendentals=count * hidden,
        ),
        name="ffn",
    )(core, h2, h2t, errors, *w_gu, *w_d, x1, *mixed, *w_a, mask, gains8)


def mixer_backward_kernel(
    slot,
    half_ref,
    ht_ref,
    g_ref,
    q_ref,
    f_ref,
    v_ref,
    o_ref,
    don_ref,
    *outs,
):
    grad_ref, ggo_ref, dpre_ref = outs[-3:]
    gain_o = g_ref[1:2, lanes_of(half_ref[0], PAIR)]
    lower_ones = triangle(slot, True)
    upper_ones = triangle(slot, False)
    block_rows = lax.broadcasted_iota(jnp.int32, (HEAD_DIM, HEAD_DIM), 0)
    block_columns = lax.broadcasted_iota(jnp.int32, (HEAD_DIM, HEAD_DIM), 1)
    causal = block_rows >= block_columns
    causal_t = block_rows <= block_columns
    blocks = slot // HEAD_DIM
    ggo_total = jnp.zeros((1, PAIR), wide)
    for sequence in range(q_ref.shape[0] // slot):
        rows = slice(sequence * slot, (sequence + 1) * slot)
        d_on = don_ref[rows, :]
        out = o_ref[rows, :]
        d_out_parts = []
        ggo_parts = []
        for head in range(2):
            lanes = slice(head * HEAD_DIM, (head + 1) * HEAD_DIM)
            out_h, d_on_h = out[:, lanes], d_on[:, lanes]
            scale = lax.rsqrt(jnp.mean(out_h * out_h, axis=-1, keepdims=True) + 1e-05)
            normed = out_h * scale
            ggo_parts.append(jnp.sum(d_on_h * normed, axis=0, keepdims=True))
            scaled = d_on_h * gain_o[:, lanes]
            inner = jnp.mean(scaled * normed, axis=-1, keepdims=True)
            d_out_parts.append((scale * (scaled - normed * inner)).astype(low))
        ggo_total = ggo_total + jnp.concatenate(ggo_parts, axis=1)

        q_pre = q_ref[rows, :]
        share, gate, keys_in, cumulative = decay_parts(f_ref[rows, :], lower_ones)
        grown = jnp.exp(-cumulative)
        shrunk = jnp.exp(cumulative)
        q_share = sigmoid(q_pre)
        decayed_q = (q_pre * q_share * shrunk).astype(low)
        grown_k = (keys_in * grown).astype(low)
        values = v_ref[rows, :]
        dq_parts, dk_parts, dv_parts = [], [], []
        for head in range(2):
            lanes = slice(head * HEAD_DIM, (head + 1) * HEAD_DIM)
            q_h, k_h, v_h = decayed_q[:, lanes], grown_k[:, lanes], values[:, lanes]
            d_out = d_out_parts[head]
            dq_blocks, dk_blocks, dv_blocks = [], [], []
            for block in range(blocks):
                start, end = block * HEAD_DIM, (block + 1) * HEAD_DIM
                here = slice(start, end)
                d_scores = mm_nt(d_out[here], v_h[here])
                d_scores = jnp.where(causal, d_scores, 0.0).astype(low)
                d_q = mm(d_scores, k_h[here])
                if block > 0:
                    before = slice(0, start)
                    d_scores = mm_nt(d_out[here], v_h[before]).astype(low)
                    d_q = d_q + mm(d_scores, k_h[before])
                dq_blocks.append(d_q)
                scores = jnp.where(causal_t, mm_nt(k_h[here], q_h[here]), 0.0).astype(low)
                d_scores = jnp.where(causal_t, mm_nt(v_h[here], d_out[here]), 0.0).astype(low)
                d_v = mm(scores, d_out[here])
                d_k = mm(d_scores, q_h[here])
                if block < blocks - 1:
                    after = slice(end, slot)
                    scores = mm_nt(k_h[here], q_h[after]).astype(low)
                    d_scores = mm_nt(v_h[here], d_out[after]).astype(low)
                    d_v = d_v + mm(scores, d_out[after])
                    d_k = d_k + mm(d_scores, q_h[after])
                dk_blocks.append(d_k)
                dv_blocks.append(d_v)
            dq_parts.append(jnp.concatenate(dq_blocks, axis=0))
            dk_parts.append(jnp.concatenate(dk_blocks, axis=0))
            dv_parts.append(jnp.concatenate(dv_blocks, axis=0))
        d_decayed = jnp.concatenate(dq_parts, axis=1)
        d_grown = jnp.concatenate(dk_parts, axis=1)
        d_value = jnp.concatenate(dv_parts, axis=1)
        d_cumulative = decayed_q.astype(wide) * d_decayed - grown_k.astype(wide) * d_grown
        d_log = split_sum(upper_ones, d_cumulative)
        d_query = d_decayed * shrunk
        d_key = d_grown * grown
        d_q_pre = d_query * q_share * (1.0 + q_pre * (1.0 - q_share))
        d_f_pre = (1.0 - lower_bound) * (d_log / gate - d_key) * share * (1.0 - share)
        dpre_ref[rows, :PAIR] = d_q_pre.astype(low)
        dpre_ref[rows, PAIR : 2 * PAIR] = d_f_pre.astype(low)
        dpre_ref[rows, 2 * PAIR :] = d_value.astype(low)

    ggo_ref[...] = ggo_total
    grad = mm(ht_ref[...], dpre_ref[...]).astype(low)
    grad_ref[...] = grad.reshape(grad_ref.shape)


def mixer_backward(which, h1t, gains8, kept, d_mixed, pair, slot, shard, grads):
    width, count = h1t.shape
    by_pair = pl.BlockSpec((count, PAIR), lambda j, _: (0, pair))
    from_whole = pl.BlockSpec((count, PAIR), lambda j, which: (0, which[0]))
    struct = jax.ShapeDtypeStruct
    shape = (width // shard, 2, shard, 3 * PAIR)
    grad_block = (width // shard, 1, shard, 3 * PAIR)
    held = [] if grads is None else [grads]
    return pl.pallas_call(
        functools.partial(mixer_backward_kernel, slot),
        grid_spec=pltpu.PrefetchScalarGridSpec(
            num_scalar_prefetch=1,
            grid=(1,),
            in_specs=[whole((width, count)), whole(gains8.shape)]
            + [by_pair] * 4
            + [from_whole]
            + [pl.BlockSpec(memory_space=pl.ANY)] * len(held),
            out_specs=[
                pl.BlockSpec(grad_block, lambda j, _: (0, pair, 0, 0)),
                whole((1, PAIR)),
                whole((count, 3 * PAIR)),
            ],
        ),
        out_shape=[
            struct(shape, low),
            struct((1, PAIR), wide),
            struct((count, 3 * PAIR), low),
        ],
        input_output_aliases={8: 0} if held else {},
        compiler_params=pltpu.CompilerParams(vmem_limit_bytes=VMEM_BYTES),
        cost_estimate=pl.CostEstimate(
            flops=count * width * 6 * PAIR + 20 * count * slot * PAIR,
            bytes_accessed=count * width * 5 + width * PAIR * 6,
            transcendentals=count * PAIR * 6,
        ),
        name="mixer_backward",
    )(which, h1t, gains8, *kept, d_mixed, *held)


def input_gradient_rows_kernel(x_ref, g_ref, *refs):
    pre_refs, weight_refs = refs[:4], refs[4:8]
    dx1_ref, dx_ref, g1_ref = refs[8:]
    d_h1 = mm_nt(pre_refs[0][...], weight_refs[0][...])
    for pre_ref, weight_ref in zip(pre_refs[1:], weight_refs[1:]):
        d_h1 = d_h1 + mm_nt(pre_ref[...], weight_ref[...])
    normed, scale = first_norm(x_ref, None)
    scaled = d_h1 * g_ref[0:1, :]
    grad_one = jnp.sum(d_h1 * normed, axis=0, keepdims=True)

    @pl.when(pl.program_id(0) == 0)
    def _():
        g1_ref[...] = grad_one

    @pl.when(pl.program_id(0) > 0)
    def _():
        g1_ref[...] += grad_one

    dx_ref[...] = dx1_ref[...] + scale * (
        scaled - normed * jnp.mean(scaled * normed, axis=-1, keepdims=True)
    )


def input_gradient(rows, gains8, d_pre, weights, d_x1):
    count, width = rows.shape
    block = count // 2
    by_rows = lambda columns: pl.BlockSpec((block, columns), lambda j: (j, 0))
    weight_specs = [
        pl.BlockSpec((width, 3 * PAIR), lambda j, p=p: (0, p), pipeline_mode=pl.Buffered(1))
        for p in (0, 1, 0, 1)
    ]
    struct = jax.ShapeDtypeStruct
    return pl.pallas_call(
        input_gradient_rows_kernel,
        grid=(count // block,),
        in_specs=[by_rows(width), whole(gains8.shape)]
        + [by_rows(3 * PAIR)] * 4
        + weight_specs
        + [by_rows(width)],
        out_specs=[by_rows(width), whole((1, width))],
        out_shape=[struct((count, width), wide), struct((1, width), wide)],
        compiler_params=pltpu.CompilerParams(vmem_limit_bytes=VMEM_BYTES),
        cost_estimate=pl.CostEstimate(
            flops=6 * count * width * width,
            bytes_accessed=count * width * 16 + width * width * 6,
            transcendentals=0,
        ),
        name="input_gradient",
    )(rows, gains8, *d_pre, weights[0], weights[0], weights[1], weights[1], d_x1)


def update(weight, momentum, average, gradient, step_rate):
    new_momentum = momentum_decay * momentum + gradient
    direction = gradient + momentum_decay * new_momentum + weight_decay * weight
    new_weight = weight - step_rate * direction
    new_average = average_decay * average + (1.0 - average_decay) * new_weight
    return (new_momentum, new_average, new_weight)


def update_kernel(pick, step_rate, sum_count, core_ref, w_ref, m_ref, a_ref, *refs):
    sums, outs = refs[:sum_count], refs[-3:]
    gradient = pick(core_ref[0], *[s[...] for s in sums]).astype(wide).reshape(w_ref.shape)
    results = update(w_ref[...], m_ref[...], a_ref[...], gradient, step_rate)
    for out, result in zip(outs, results):
        out[...] = result


def update_call(
    core, state, sums, grid, state_spec, sum_specs, pick, step_rate, name, before=()
):
    struct = jax.ShapeDtypeStruct(state[0].shape, wide)
    size = math.prod(state[0].shape)
    return pl.pallas_call(
        functools.partial(update_kernel, pick, step_rate, len(sums)),
        grid_spec=pltpu.PrefetchScalarGridSpec(
            num_scalar_prefetch=1,
            grid=grid,
            in_specs=[state_spec] * 3
            + sum_specs
            + [pl.BlockSpec(memory_space=pl.ANY)] * len(before),
            out_specs=[state_spec] * 3,
        ),
        out_shape=[struct] * 3,
        input_output_aliases={4 + len(sums) + k: k for k in range(len(before))},
        compiler_params=pltpu.CompilerParams(vmem_limit_bytes=VMEM_BYTES),
        cost_estimate=pl.CostEstimate(flops=10 * size, bytes_accessed=26 * size, transcendentals=0),
        name=name,
    )(core, *state, *sums, *before)


def update_attention(core, half_ref, state, qfv, out, step_rate, before):
    _, shard, width = state[0].shape
    down_rows = out.shape[0] - shard

    def pick(core_index, proj, last):
        gradient = last[down_rows:].astype(wide)
        for kind in range(3):
            parts = [proj[pair * shard :, kind * PAIR :][:shard, :PAIR] for pair in range(2)]
            chosen = jnp.concatenate(parts, axis=1).astype(wide)
            gradient = jnp.where(pl.program_id(0) == kind, chosen, gradient)
        return gradient

    return update_call(
        half_ref,
        state,
        (qfv, out),
        (4,),
        pl.BlockSpec((1, shard, width // 2), lambda kind, half: (kind, 0, half[0])),
        [whole(qfv.shape), whole(out.shape)],
        pick,
        step_rate,
        "update_attention",
        before,
    )


def update_ffn_in(core, state, sums, step_rate):
    _, shard, hidden = state[0].shape
    tile = hidden // 2

    def pick(core_index, mine, other):
        own = pl.program_id(0) == core_index
        return jnp.where(own, mine.astype(wide), other.astype(wide))

    sum_spec = pl.BlockSpec((shard, tile), lambda kind, j, _: (0, j))
    return update_call(
        core,
        state,
        sums,
        (2, 2),
        pl.BlockSpec((1, shard, tile), lambda kind, j, _: (kind, 0, j)),
        [sum_spec, sum_spec],
        pick,
        step_rate,
        "update_ffn_in",
    )


def update_ffn_out(core, state, sums, step_rate):
    shard, width = state[0].shape

    def pick(core_index, mine, other):
        own = pl.program_id(0) == core_index
        return jnp.where(own, mine[:shard].astype(wide), other[:shard].astype(wide))

    return update_call(
        core,
        state,
        sums,
        (2,),
        pl.BlockSpec((shard, width // 2), lambda j, _: (0, j)),
        [whole(total.shape) for total in sums],
        pick,
        step_rate,
        "update_ffn_out",
    )


def pack_kernel(core_ref, w_ref, g_ref, out_ref):
    pairs = w_ref.shape[2] // PAIR
    for pair in range(pairs):
        for kind in range(3):
            start = (pair * 3 + kind) * PAIR
            piece = w_ref[kind, :, pair * PAIR : (pair + 1) * PAIR]
            out_ref[:, start : start + PAIR] = piece.astype(low)
    start = 3 * pairs * PAIR
    out_ref[:, start : start + pairs * PAIR] = w_ref[3].astype(low)
    start += pairs * PAIR
    out_ref[:, start:] = g_ref[...].astype(low)


def pack_attention(core, weights, gains):
    _, shard, width = weights.shape
    half = width // 2
    gain_columns = jnp.pad(gains.T, ((0, 0), (0, HEAD_DIM - 3)))
    columns = 4 * half + HEAD_DIM
    return pl.pallas_call(
        pack_kernel,
        grid_spec=pltpu.PrefetchScalarGridSpec(
            num_scalar_prefetch=1,
            grid=(1,),
            in_specs=[
                pl.BlockSpec((4, shard, half), lambda j, core: (0, 0, core[0])),
                whole((shard, HEAD_DIM)),
            ],
            out_specs=whole((shard, columns)),
        ),
        out_shape=jax.ShapeDtypeStruct((shard, columns), low),
        name="pack_attention",
    )(core, weights, gain_columns)


RING = 8


def ring_place(index):
    return jnp.where(index % 2 == 0, index // 2, RING - 1 - index // 2)


def ring_member(place):
    place = place % RING
    return jnp.where(place < RING // 2, 2 * place, 2 * RING - 1 - 2 * place)


def ring_next(tensor):
    cycle = [0, 2, 4, 6, 7, 5, 3, 1]
    replicas = lax.axis_size("dp")
    pairs = []
    for place, member in enumerate(cycle):
        for replica in range(replicas):
            target = cycle[(place + (1 if replica % 2 == 0 else -1)) % RING]
            pairs.append((member * replicas + replica, target * replicas + replica))
    return lax.ppermute(tensor, ("fsdp", "dp"), pairs)


def core_swap(tensor):
    return lax.ppermute(tensor, "dp", [(d, d ^ 1) for d in range(lax.axis_size("dp"))])


def column_swap(tensor):
    return lax.ppermute(tensor, "dp", [(d, d ^ 2) for d in range(lax.axis_size("dp"))])


def place_kernel(which, origin_ref, column_ref, *refs):
    pieces, (semaphores,) = refs[: len(which)], refs[-1:]
    outs = refs[-4:-1]
    copies = []
    for number, (array, step, side) in enumerate(which):
        rows, columns = pieces[number].shape
        lane = (0, column_ref[0], 1 - column_ref[0])[side]
        here = pl.ds(pl.multiple_of(origin_ref[step] * rows, 16), rows)
        target = outs[array].at[here, lanes_of(lane, columns)]
        copies.append(pltpu.make_async_copy(pieces[number], target, semaphores.at[number]))
    for copy in copies:
        copy.start()
    for copy in copies:
        copy.wait()


def place(origins, column, which, pieces, arrays):
    anywhere = pl.BlockSpec(memory_space=pl.ANY)
    held = arrays is not None and list(arrays) or []
    shapes = [array.shape for array in held]
    if not held:
        shapes = [
            (RING * piece.shape[0], piece.shape[1] * (2 if side else 1))
            for piece, (_, _, side) in zip(pieces, which)
        ]
    size = sum(math.prod(piece.shape) for piece in pieces)
    first = 2 + len(pieces)
    return pl.pallas_call(
        functools.partial(place_kernel, which),
        grid_spec=pltpu.PrefetchScalarGridSpec(
            num_scalar_prefetch=2,
            grid=(1,),
            in_specs=[whole(piece.shape) for piece in pieces] + [anywhere] * len(held),
            out_specs=[anywhere] * 3,
            scratch_shapes=[pltpu.SemaphoreType.DMA((len(pieces),))],
        ),
        out_shape=[jax.ShapeDtypeStruct(shape, pieces[0].dtype) for shape in shapes],
        input_output_aliases={first + k: k for k in range(len(held))},
        cost_estimate=pl.CostEstimate(flops=0, bytes_accessed=8 * size, transcendentals=0),
        name="place",
    )(origins, column, *pieces, *held)


def after(tensor, *others):
    return lax.optimization_barrier((tensor, *others))[0]


def core_way():
    return 1 - 2 * (lax.axis_index("dp") % 2)


def ring_origins():
    place = ring_place(lax.axis_index("fsdp"))
    return ring_member(
        place - core_way() * jnp.arange(RING, dtype=jnp.int32) + RING
    ).astype(jnp.int32)


class RingSum:
    def __init__(self, mine, arrived):
        self.mine, self.arrived = mine, arrived
        place = ring_place(lax.axis_index("fsdp"))
        self.owners = [ring_member(place - core_way() * (s + 1) + 2 * RING) for s in range(RING)]
        self.totals = []

    def term(self):
        parts = []
        for own, arrived in zip(self.mine, self.arrived):
            rows = own.shape[0] // RING
            start = self.owners[len(self.totals)] * rows
            part = lax.dynamic_slice_in_dim(own, start, rows, 0).astype(wide)
            parts.append(part + lax.dynamic_slice_in_dim(arrived, start, rows, 0).astype(wide))
        return parts[0] if len(parts) == 1 else jnp.concatenate(parts, axis=0)

    def begin(self, *others):
        if others:
            self.mine = [after(self.mine[0], *others), *self.mine[1:]]
        self.totals.append(self.term().astype(low))

    def step(self, *before, arriving=()):
        total = self.totals[-1]
        moved = ring_next(after(total, *before) if before else total)
        moved = after(moved, *arriving) if arriving else moved
        self.totals.append((moved.astype(wide) + self.term().astype(wide)).astype(low))

    def last(self):
        return self.totals[-1]


def gather_rows(shard):
    mine = lax.all_gather(shard, "fsdp", axis=0, tiled=True)
    return mine, core_swap(mine)


def core_sum(mine, other):
    return (mine.astype(wide) + core_swap(other).astype(wide)).astype(low)


def scatter_rows(both):
    return lax.psum_scatter(both, "fsdp", scatter_dimension=0, tiled=True)


def over_columns(total):
    total = (total.astype(wide) + column_swap(total).astype(wide)).astype(low)
    return total, core_swap(total)


def exchanges():
    for axis in ("dp", "fsdp"):
        distance = 1
        while distance < lax.axis_size(axis):
            yield axis, [(d, d ^ distance) for d in range(lax.axis_size(axis))]
            distance *= 2


def on_device(
    inputs,
    cotangent,
    lengths,
    attention_weights,
    attention_momentum,
    attention_average,
    ffn_inputs,
    ffn_inputs_momentum,
    ffn_inputs_average,
    ffn_output,
    ffn_output_momentum,
    ffn_output_average,
    gains,
    gains_momentum,
    gains_average,
):
    micro_count, slot, width = inputs.shape
    hidden = ffn_inputs.shape[2]
    shard, down_rows = ffn_inputs.shape[1], ffn_output.shape[0]
    fsdp_size = lax.axis_size("fsdp")
    replicas = lax.axis_size("dp")
    ringed = fsdp_size == RING
    core = lax.axis_index("dp") % 2
    column = lax.axis_index("dp") // 2
    me = lax.axis_index("fsdp")
    count = micro_count * slot
    half = width // 2
    core_ref = core.astype(jnp.int32).reshape(1)
    other_ref = 1 - core_ref
    column_ref = column.astype(jnp.int32).reshape(1)
    is_first = core == 0

    packed = pack_attention(core_ref, attention_weights, gains)

    def gains_of(weights):
        gain_rows = weights[:, 4 * half : 4 * half + 3].T.astype(wide)
        return jnp.pad(gain_rows, ((0, 5), (0, 0)))

    rows = inputs.reshape(count, width)
    positions = jnp.arange(slot, dtype=jnp.int32)
    valid = (positions[None, :] < lengths).astype(wide).reshape(count, 1)
    errors = (cotangent.reshape(count, width).astype(wide) * valid).astype(low)

    if ringed:
        origins = ring_origins()
        up_part = lax.dynamic_slice(
            ffn_inputs, (core, 0, column * (hidden // 2)), (1, shard, hidden // 2)
        )[0].astype(low)
        down_part = lax.dynamic_slice(
            ffn_output, (0, core * half + column * (half // 2)), (down_rows, half // 2)
        ).astype(low)
        wholes, here, there = None, (packed, up_part, down_part), ()
        for step in range(RING):
            if step < RING - 1:
                onward = tuple(ring_next(piece) for piece in here)
            across = tuple(column_swap(piece) for piece in here[1:])
            which = [(array, step, min(array, 1)) for array in range(3)]
            which += [(array + 1, step - 1, 2) for array in range(len(there))]
            wholes = place(origins, column_ref, which, (*here, *there), wholes)
            extra = [errors, valid] if step == 2 else []
            if step < RING - 1:
                tied = lax.optimization_barrier((*onward, *across, *wholes, *extra))
                here, there, wholes = tied[:3], tied[3:5], tied[5:8]
        w_a = (wholes[0], core_swap(wholes[0]))
    else:
        w_a = gather_rows(packed)
        w_gu = gather_rows(
            lax.dynamic_index_in_dim(ffn_inputs, core, 0, keepdims=False).astype(low)
        )
        w_d = gather_rows(lax.dynamic_slice_in_dim(ffn_output, core * half, half, 1).astype(low))
    gains8 = gains_of(w_a[0])
    mixed_mine, *kept_mine = mixer_forward(core_ref, rows, w_a[0], gains8, slot)
    if ringed:
        across = lax.optimization_barrier((*across, mixed_mine, w_a[1]))[:2]
        which = [(array + 1, RING - 1, 2) for array in range(2)]
        wholes = place(origins, column_ref, which, across, wholes)
        rows = after(rows, *wholes[1:])
        w_gu, w_d = [(array, core_swap(array)) for array in wholes[1:]]
    mixed_other, *rest = mixer_forward(
        other_ref, rows, w_a[1], gains8, slot, (mixed_mine, w_a[0])
    )
    kept_other, (x1, h2, h2t, h1t) = rest[:4], rest[4:]
    owners = (fsdp_size, down_rows + shard, down_rows) if ringed else None
    gm, gu, gd_mine, gd_other, output, d_x1, d_mixed, go_mine, go_other, grad_two = ffn(
        core_ref, h2, h2t, errors, w_gu, w_d, x1, (mixed_mine, mixed_other), w_a, valid, gains8, owners
    )

    mine_gu, arrived_gu = [gm], [core_swap(gu)]
    if ringed:
        mine_do, arrived_do = [gd_mine], [core_swap(gd_other)]
    else:
        mine_do, arrived_do = [gd_mine, go_mine], [core_swap(gd_other), core_swap(go_other)]
    backs = []
    for place_of in range(4):
        pair = place_of % 2
        from_half, kept = (other_ref, kept_other) if place_of < 2 else (core_ref, kept_mine)
        if ringed and place_of > 0:
            h1t = after(h1t, sum_gu.last(), sum_do.last())
        backs.append(
            mixer_backward(
                2 * from_half + pair,
                h1t,
                gains8,
                kept,
                d_mixed,
                pair,
                slot,
                shard,
                backs[-1][0] if pair else None,
            )
        )
        if ringed and place_of == 0:
            sum_gu, sum_do = RingSum(mine_gu, arrived_gu), RingSum(mine_do, arrived_do)
            sum_do.begin(backs[0][2])
            sum_gu.begin(backs[0][2])
        elif ringed:
            sum_do.step(arriving=(backs[-1][2],))
            sum_gu.step(arriving=(backs[-1][2],))
    grads, ggo, d_pre = [[back[which] for back in backs] for which in range(3)]
    ggo_mine, ggo_other = jnp.concatenate(ggo[2:], axis=1), jnp.concatenate(ggo[:2], axis=1)
    ggo_left = jnp.where(is_first, ggo_mine, ggo_other)
    ggo_right = jnp.where(is_first, ggo_other, ggo_mine)
    grad_go = jnp.concatenate([ggo_left, ggo_right], axis=1)
    by_owner = (fsdp_size * 2 * shard, 3 * PAIR)
    mine_qfv, arrived_qfv = [grads[3].reshape(by_owner)], [core_swap(grads[1].reshape(by_owner))]

    def finish_input(*others):
        last = after(d_pre[2], *others) if others else d_pre[2]
        gradient, grad_one = input_gradient(
            rows, gains8, [last, d_pre[3], *d_pre[:2]], w_a, d_x1
        )
        return gradient, jnp.concatenate([grad_one, grad_go, grad_two], axis=0)

    if ringed:
        sum_qfv = RingSum(mine_qfv, arrived_qfv)
        sum_qfv.begin()
        pending = exchanges()
        before = []
        for step in range(1, RING):
            sum_qfv.step(*before)
            if step <= 4:
                sum_do.step()
                sum_gu.step()
            if step == 2:
                input_grad, gain_grads = finish_input(sum_qfv.last())
                before = [gain_grads]
            elif step > 2:
                axis, pairs = next(pending)
                gain_grads = gain_grads + lax.ppermute(gain_grads, axis, pairs)
                before = [gain_grads]
        total_gu, total_do, total_qfv = sum_gu.last(), sum_do.last(), sum_qfv.last()
    else:
        total_gu, total_do, total_qfv = [
            jnp.concatenate(
                [
                    scatter_rows((own.astype(wide) + there.astype(wide)).astype(low))
                    for own, there in zip(mine, arrived)
                ],
                axis=0,
            )
            for mine, arrived in (
                (mine_gu, arrived_gu),
                (mine_do, arrived_do),
                (mine_qfv, arrived_qfv),
            )
        ]
        input_grad, gain_grads = finish_input()
        pending = exchanges()
    sum_gu = over_columns(total_gu)
    sum_do = over_columns(total_do)
    for axis, pairs in pending:
        gain_grads = gain_grads + lax.ppermute(gain_grads, axis, pairs)
    sum_gains = lax.dynamic_slice_in_dim(gain_grads, me * gains.shape[1], gains.shape[1], 1)

    scale_rows = 1.0 / math.sqrt(count * fsdp_size * replicas)
    attention_state = (attention_weights, attention_momentum, attention_average)
    ffn_in_state = (ffn_inputs, ffn_inputs_momentum, ffn_inputs_average)
    ffn_out_state = (ffn_output, ffn_output_momentum, ffn_output_average)
    new_in = update_ffn_in(core_ref, ffn_in_state, sum_gu, matrix_rate * scale_rows)
    new_out = update_ffn_out(core_ref, ffn_out_state, sum_do, matrix_rate * scale_rows)
    there = after(column_swap(total_qfv), new_in[0], new_out[0])
    sum_qfv = (total_qfv.astype(wide) + there.astype(wide)).astype(low)
    own = update_attention(
        core_ref, core_ref, attention_state, sum_qfv, sum_do[0], matrix_rate * scale_rows, ()
    )
    theirs = after(core_swap(sum_qfv), own[0])
    new_attention = update_attention(
        core_ref, other_ref, attention_state, theirs, sum_do[1], matrix_rate * scale_rows, own
    )
    return (
        output.reshape(micro_count, slot, width),
        input_grad.reshape(micro_count, slot, width),
        *new_attention,
        *new_in,
        *new_out,
        *update(gains, gains_momentum, gains_average, sum_gains, gain_rate * scale_rows),
    )


def solution(mesh):
    rows_split = P(None, ("fsdp", "dp"), None)
    middle_split = P(None, "fsdp", None)
    first_split = P("fsdp", None)
    gains_split = P(None, "fsdp")
    in_specs = (
        (rows_split, rows_split, P(None, ("fsdp", "dp")))
        + (middle_split,) * 6
        + (first_split,) * 3
        + (gains_split,) * 3
    )
    out_specs = (
        (rows_split, rows_split)
        + (middle_split,) * 6
        + (first_split,) * 3
        + (gains_split,) * 3
    )
    return jax.shard_map(
        on_device, mesh=mesh, in_specs=in_specs, out_specs=out_specs, check_vma=False
    )
```

```python
import functools
import math

import jax
import jax.numpy as jnp
from jax import lax
from jax.experimental import pallas as pl
from jax.experimental.pallas import tpu as pltpu
from jax.sharding import PartitionSpec as P

HEAD_DIM = 128
PAIR = 2 * HEAD_DIM

lower_bound = 0.9
momentum_decay = 0.9
average_decay = 0.7
weight_decay = 0.0005
matrix_rate = 0.03
gain_rate = 0.1
low = jnp.bfloat16
wide = jnp.float32
TILE_F = 256
VMEM_BYTES = 60 * 1024 * 1024


def mm(left, right):
    return jnp.dot(left, right, preferred_element_type=wide)


def mm_nt(left, right):
    return lax.dot_general(left, right, (((1,), (1,)), ((), ())), preferred_element_type=wide)


def mm_tn(left, right):
    return lax.dot_general(left, right, (((0,), (0,)), ((), ())), preferred_element_type=wide)


def sigmoid(u):
    return 0.5 * jnp.tanh(0.5 * u) + 0.5


def whole(shape):
    return pl.BlockSpec(shape, lambda *_: (0,) * len(shape), pipeline_mode=pl.Buffered(1))


def split_sum(ones_matrix, tensor):
    high = tensor.astype(low)
    rest = (tensor - high.astype(wide)).astype(low)
    return mm(ones_matrix, high) + mm(ones_matrix, rest)


def triangle(length, lower):
    rows = lax.broadcasted_iota(jnp.int32, (length, length), 0)
    columns = lax.broadcasted_iota(jnp.int32, (length, length), 1)
    kept = rows >= columns if lower else rows <= columns
    return kept.astype(wide).astype(low)


def decay_parts(f_pre, lower_ones):
    share = sigmoid(f_pre)
    gate = lower_bound + (1.0 - lower_bound) * share
    keys_in = (1.0 - lower_bound) * (1.0 - share)
    cumulative = split_sum(lower_ones, jnp.log(gate))
    middle_row = cumulative.shape[0] // 2
    cumulative = cumulative - cumulative[middle_row : middle_row + 1, :]
    return share, gate, keys_in, cumulative


def first_norm(x_ref, gain_row):
    rows = x_ref[...].astype(wide)
    scale = lax.rsqrt(jnp.mean(rows * rows, axis=-1, keepdims=True) + 1e-06)
    return rows * scale, scale


def lanes_of(half, size):
    return pl.ds(pl.multiple_of(half * size, size), size)


def mixer_forward_kernel(
    slot, half_ref, x_ref, w_ref, g_ref, on_ref, q_ref, f_ref, v_ref, o_ref, h_s
):
    @pl.when(pl.program_id(0) == 0)
    def _():
        normed, _ = first_norm(x_ref, None)
        h_s[...] = (normed * g_ref[0:1, :]).astype(low)

    gain_o = g_ref[1:2, lanes_of(half_ref[0] * pl.num_programs(0) + pl.program_id(0), PAIR)]
    pre = mm(h_s[...], w_ref[...])
    q_ref[...] = pre[:, :PAIR]
    f_ref[...] = pre[:, PAIR : 2 * PAIR]
    v_ref[...] = pre[:, 2 * PAIR :].astype(low)
    lower_ones = triangle(slot, True)
    block_rows = lax.broadcasted_iota(jnp.int32, (HEAD_DIM, HEAD_DIM), 0)
    block_columns = lax.broadcasted_iota(jnp.int32, (HEAD_DIM, HEAD_DIM), 1)
    causal = block_rows >= block_columns
    for sequence in range(x_ref.shape[0] // slot):
        rows = slice(sequence * slot, (sequence + 1) * slot)
        q_pre = q_ref[rows, :]
        _, _, keys_in, cumulative = decay_parts(f_ref[rows, :], lower_ones)
        grown = jnp.exp(-cumulative)
        decayed_q = (q_pre * sigmoid(q_pre) * jnp.exp(cumulative)).astype(low)
        grown_k = (keys_in * grown).astype(low)
        values = v_ref[rows, :]
        for head in range(2):
            lanes = slice(head * HEAD_DIM, (head + 1) * HEAD_DIM)
            for block in range(slot // HEAD_DIM):
                start, end = block * HEAD_DIM, (block + 1) * HEAD_DIM
                q_block = decayed_q[start:end, lanes]
                diagonal = mm_nt(q_block, grown_k[start:end, lanes])
                diagonal = jnp.where(causal, diagonal, 0.0).astype(low)
                out = mm(diagonal, values[start:end, lanes])
                if block > 0:
                    scores = mm_nt(q_block, grown_k[:start, lanes]).astype(low)
                    out = out + mm(scores, values[:start, lanes])
                scale = lax.rsqrt(jnp.mean(out * out, axis=-1, keepdims=True) + 1e-05)
                target = slice(sequence * slot + start, sequence * slot + end)
                o_ref[target, lanes] = out
                on_ref[target, lanes] = (out * scale * gain_o[:, lanes]).astype(low)


def mixer_forward_last_kernel(
    slot,
    half_ref,
    x_ref,
    w_ref,
    g_ref,
    before_ref,
    woo_ref,
    wom_ref,
    on_ref,
    q_ref,
    f_ref,
    v_ref,
    o_ref,
    x1_ref,
    h2_ref,
    h2t_ref,
    h1t_ref,
    h_s,
    on_s,
):
    step = pl.program_id(0)
    half = before_ref.shape[1]
    mixer_forward_kernel(
        slot, half_ref, x_ref, w_ref, g_ref, on_ref, q_ref, f_ref, v_ref, o_ref, h_s
    )
    on_s[:, lanes_of(half_ref[0] * pl.num_programs(0) + step, PAIR)] = on_ref[...]

    @pl.when(step == pl.num_programs(0) - 1)
    def _():
        here = lanes_of(half_ref[0], half)
        there = lanes_of(1 - half_ref[0], half)
        on_s[:, there] = before_ref[...]
        h1t_ref[...] = h_s[...].astype(wide).T.astype(low)
        x1_ref[:, here] = x_ref[:, here].astype(wide) + mm(on_s[...], woo_ref[...])
        x1_ref[:, there] = x_ref[:, there].astype(wide) + mm(on_s[...], wom_ref[...])
        x1 = x1_ref[...]
        scale = lax.rsqrt(jnp.mean(x1 * x1, axis=-1, keepdims=True) + 1e-06)
        normed = x1 * scale * g_ref[2:3, :]
        h2_ref[...] = normed.astype(low)
        h2t_ref[...] = normed.T.astype(low)


def mixer_forward(half, rows, weights, gains8, slot, ending=None):
    count, width = rows.shape
    pairs = width // PAIR // 2
    by_pair = pl.BlockSpec((count, PAIR), lambda j, _: (0, j))
    struct = jax.ShapeDtypeStruct
    shape = lambda kind: struct((count, width // 2), kind)
    kernel = mixer_forward_kernel
    in_specs = [
        whole(rows.shape),
        pl.BlockSpec((width, 3 * PAIR), lambda j, _: (0, j)),
        whole(gains8.shape),
    ]
    operands = [half, rows, weights, gains8]
    out_specs = [by_pair] * 5
    out_shape = [shape(low), shape(wide), shape(wide), shape(low), shape(wide)]
    scratch = [pltpu.VMEM((count, width), low)]
    if ending is not None:
        kernel = mixer_forward_last_kernel
        out_weights = pl.BlockSpec((width, width // 2), lambda j, _: (0, 3))
        in_specs += [whole((count, width // 2)), out_weights, out_weights]
        operands += [ending[0], weights, ending[1]]
        out_specs += [whole((count, width))] * 2 + [whole((width, count))] * 2
        out_shape += [
            struct((count, width), wide),
            struct((count, width), low),
            struct((width, count), low),
            struct((width, count), low),
        ]
        scratch += [pltpu.VMEM((count, width), low)]
    return pl.pallas_call(
        functools.partial(kernel, slot),
        grid_spec=pltpu.PrefetchScalarGridSpec(
            num_scalar_prefetch=1,
            grid=(pairs,),
            in_specs=in_specs,
            out_specs=out_specs,
            scratch_shapes=scratch,
        ),
        out_shape=out_shape,
        compiler_params=pltpu.CompilerParams(vmem_limit_bytes=VMEM_BYTES),
        cost_estimate=pl.CostEstimate(
            flops=count * width * 4 * width + 10 * count * slot * width,
            bytes_accessed=count * width * 12 + width * width * 4,
            transcendentals=count * width * 3,
        ),
        name="mixer_forward",
    )(*operands)


def store_down(out_ref, tile, owners):
    if owners is None:
        out_ref[...] = tile
        return
    _, stride, down_rows = owners
    block = math.gcd(down_rows, tile.shape[0])
    first = pl.program_id(0) * (tile.shape[0] // block)
    for part in range(tile.shape[0] // block):
        owner = (first + part) // (down_rows // block)
        inside = (first + part) % (down_rows // block)
        start = pl.multiple_of(owner * stride + inside * block, block)
        out_ref[pl.ds(start, block), :] = tile[part * block : (part + 1) * block, :]


def ffn_tile(owners, core_ref, refs, grads, acc_ref, dh_ref, scratch):
    h_ref, ht_ref, e_ref, wm_ref, wu_ref, wdm_ref, wdo_ref = refs
    gm_ref, gu_ref, gdm_ref, gdo_ref = grads
    gu_w, down_w, gu_g, down_g = scratch
    half, tile = wdm_ref.shape[1], wm_ref.shape[1]
    mine, other = lanes_of(core_ref[0], half), lanes_of(1 - core_ref[0], half)
    kind, kind_other = lanes_of(core_ref[0], tile), lanes_of(1 - core_ref[0], tile)
    gu_w[:, kind] = wm_ref[...]
    gu_w[:, kind_other] = wu_ref[...]
    down_w[:, mine] = wdm_ref[...]
    down_w[:, other] = wdo_ref[...]
    pre = mm(h_ref[...], gu_w[...])
    a, b = pre[:, :tile], pre[:, tile:]
    share = sigmoid(a)
    swish = a * share
    mid = (swish * b).astype(low)
    d_mid = mm_nt(e_ref[...], down_w[...])
    down_g[...] = mm_tn(mid, e_ref[...]).astype(low)
    d_a = (d_mid * b * (share + swish * (1.0 - share))).astype(low)
    d_b = (d_mid * swish).astype(low)
    d_pre = jnp.concatenate([d_a, d_b], axis=1)
    acc_ref[...] += mm(mid, down_w[...])
    dh_ref[...] += mm_nt(d_pre, gu_w[...])
    gu_g[...] = mm(ht_ref[...], d_pre).astype(low)
    gm_ref[...] = gu_g[:, kind]
    gu_ref[...] = gu_g[:, kind_other]
    store_down(gdm_ref, down_g[:, mine], owners)
    store_down(gdo_ref, down_g[:, other], owners)


def ffn_kernel(
    owners,
    core_ref,
    h_ref,
    ht_ref,
    e_ref,
    wm_ref,
    wu_ref,
    wdm_ref,
    wdo_ref,
    x1_ref,
    onm_ref,
    ono_ref,
    wom_ref,
    woo_ref,
    m_ref,
    g_ref,
    gm_ref,
    gu_ref,
    gdm_ref,
    gdo_ref,
    out_ref,
    dh_s,
    acc_s,
    gom_ref,
    goo_ref,
    on_s,
    *scratch,
):
    @pl.when(pl.program_id(0) == 0)
    def _():
        acc_s[...] = x1_ref[...]
        dh_s[...] = jnp.zeros_like(dh_s)

    grads = (gm_ref, gu_ref, gdm_ref, gdo_ref)
    refs = (h_ref, ht_ref, e_ref, wm_ref, wu_ref, wdm_ref, wdo_ref)
    ffn_tile(owners, core_ref, refs, grads, acc_s, dh_s, scratch)

    @pl.when(pl.program_id(0) == pl.num_programs(0) - 1)
    def _():
        half = onm_ref.shape[1]
        mine = lanes_of(core_ref[0], half)
        other = lanes_of(1 - core_ref[0], half)
        out_ref[...] = (acc_s[...] * m_ref[...]).astype(low)
        x1 = x1_ref[...]
        scale = lax.rsqrt(jnp.mean(x1 * x1, axis=-1, keepdims=True) + 1e-06)
        normed = x1 * scale
        d_h2 = dh_s[...]
        scaled = d_h2 * g_ref[2:3, :]
        d_x1 = e_ref[...].astype(wide) + scale * (
            scaled - normed * jnp.mean(scaled * normed, axis=-1, keepdims=True)
        )
        dh_s[...] = d_x1
        on_s[...] = d_x1.astype(low)
        acc_s[...] = mm_nt(on_s[:, mine], wom_ref[...]) + mm_nt(on_s[:, other], woo_ref[...])
        for columns, g_down_ref, g_ref_o in ((mine, gdm_ref, gom_ref), (other, gdo_ref, goo_ref)):
            d_1 = on_s[:, columns]
            for which, on_ref in ((core_ref[0], onm_ref), (1 - core_ref[0], ono_ref)):
                grad_o = mm_tn(on_ref[...], d_1).astype(low)
                if owners is None:
                    g_ref_o[pl.ds(pl.multiple_of(which * half, half), half), :] = grad_o
                    continue
                count, stride, down_rows = owners
                rows = stride - down_rows
                for part in range(half // rows):
                    owner = which * (count // 2) + part
                    start = pl.multiple_of(owner * stride + down_rows, math.gcd(stride, down_rows))
                    g_down_ref[pl.ds(start, rows), :] = grad_o[part * rows : (part + 1) * rows, :]


def ffn(core, h2, h2t, errors, w_gu, w_d, x1, mixed, w_a, mask, gains8, owners):
    count, width = h2.shape
    half = width // 2
    hidden = w_gu[0].shape[1]
    full = whole((count, width))
    half_full = whole((count, half))
    square = whole((width, half))
    in_tile = pl.BlockSpec((width, TILE_F), lambda j, _: (0, j))
    out_tile = pl.BlockSpec((TILE_F, half), lambda j, _: (j, 0))
    out_weights = pl.BlockSpec((width, half), lambda j, _: (0, 3), pipeline_mode=pl.Buffered(1))
    down_spec, down_shape, out_spec, out_shape = out_tile, (hidden, half), square, (width, half)
    if owners is not None:
        down_shape, out_shape = (owners[0] * owners[1], half), (16, half)
        down_spec, out_spec = whole(down_shape), whole(out_shape)
    struct = jax.ShapeDtypeStruct
    return pl.pallas_call(
        functools.partial(ffn_kernel, owners),
        grid_spec=pltpu.PrefetchScalarGridSpec(
            num_scalar_prefetch=1,
            grid=(hidden // TILE_F,),
            in_specs=[full, whole(h2t.shape), full, in_tile, in_tile, out_tile, out_tile]
            + [full, half_full, half_full, out_weights, out_weights]
            + [whole((count, 1)), whole((8, width))],
            out_specs=[in_tile, in_tile, down_spec, down_spec]
            + [full, full, full, out_spec, out_spec],
            scratch_shapes=[
                pltpu.VMEM((count, width), low),
                pltpu.VMEM((width, 2 * TILE_F), low),
                pltpu.VMEM((TILE_F, width), low),
                pltpu.VMEM((width, 2 * TILE_F), low),
                pltpu.VMEM((TILE_F, width), low),
            ],
        ),
        out_shape=[struct((width, hidden), low)] * 2
        + [struct(down_shape, low)] * 2
        + [
            struct((count, width), low),
            struct((count, width), wide),
            struct((count, width), wide),
            struct(out_shape, low),
            struct(out_shape, low),
        ],
        compiler_params=pltpu.CompilerParams(vmem_limit_bytes=VMEM_BYTES),
        cost_estimate=pl.CostEstimate(
            flops=16 * count * width * hidden,
            bytes_accessed=count * width * 20 + width * hidden * 12,
            transcendentals=count * hidden,
        ),
        name="ffn",
    )(core, h2, h2t, errors, *w_gu, *w_d, x1, *mixed, *w_a, mask, gains8)


def mixer_backward_kernel(
    slot,
    half_ref,
    ht_ref,
    g_ref,
    q_ref,
    f_ref,
    v_ref,
    o_ref,
    don_ref,
    *outs,
):
    grad_ref, dpre_ref = outs[-2:]
    gain_o = g_ref[1:2, lanes_of(half_ref[0], PAIR)]
    lower_ones = triangle(slot, True)
    upper_ones = triangle(slot, False)
    block_rows = lax.broadcasted_iota(jnp.int32, (HEAD_DIM, HEAD_DIM), 0)
    block_columns = lax.broadcasted_iota(jnp.int32, (HEAD_DIM, HEAD_DIM), 1)
    causal = block_rows >= block_columns
    causal_t = block_rows <= block_columns
    blocks = slot // HEAD_DIM
    for sequence in range(q_ref.shape[0] // slot):
        rows = slice(sequence * slot, (sequence + 1) * slot)
        d_on = don_ref[rows, :]
        out = o_ref[rows, :]
        d_out_parts = []
        for head in range(2):
            lanes = slice(head * HEAD_DIM, (head + 1) * HEAD_DIM)
            out_h, d_on_h = out[:, lanes], d_on[:, lanes]
            scale = lax.rsqrt(jnp.mean(out_h * out_h, axis=-1, keepdims=True) + 1e-05)
            normed = out_h * scale
            scaled = d_on_h * gain_o[:, lanes]
            inner = jnp.mean(scaled * normed, axis=-1, keepdims=True)
            d_out_parts.append((scale * (scaled - normed * inner)).astype(low))

        q_pre = q_ref[rows, :]
        share, gate, keys_in, cumulative = decay_parts(f_ref[rows, :], lower_ones)
        grown = jnp.exp(-cumulative)
        shrunk = jnp.exp(cumulative)
        q_share = sigmoid(q_pre)
        decayed_q = (q_pre * q_share * shrunk).astype(low)
        grown_k = (keys_in * grown).astype(low)
        values = v_ref[rows, :]
        dq_parts, dk_parts, dv_parts = [], [], []
        for head in range(2):
            lanes = slice(head * HEAD_DIM, (head + 1) * HEAD_DIM)
            q_h, k_h, v_h = decayed_q[:, lanes], grown_k[:, lanes], values[:, lanes]
            d_out = d_out_parts[head]
            dq_blocks, dk_blocks, dv_blocks = [], [], []
            for block in range(blocks):
                start, end = block * HEAD_DIM, (block + 1) * HEAD_DIM
                here = slice(start, end)
                d_scores = mm_nt(d_out[here], v_h[here])
                d_scores = jnp.where(causal, d_scores, 0.0).astype(low)
                d_q = mm(d_scores, k_h[here])
                if block > 0:
                    before = slice(0, start)
                    d_scores = mm_nt(d_out[here], v_h[before]).astype(low)
                    d_q = d_q + mm(d_scores, k_h[before])
                dq_blocks.append(d_q)
                scores = jnp.where(causal_t, mm_nt(k_h[here], q_h[here]), 0.0).astype(low)
                d_scores = jnp.where(causal_t, mm_nt(v_h[here], d_out[here]), 0.0).astype(low)
                d_v = mm(scores, d_out[here])
                d_k = mm(d_scores, q_h[here])
                if block < blocks - 1:
                    after = slice(end, slot)
                    scores = mm_nt(k_h[here], q_h[after]).astype(low)
                    d_scores = mm_nt(v_h[here], d_out[after]).astype(low)
                    d_v = d_v + mm(scores, d_out[after])
                    d_k = d_k + mm(d_scores, q_h[after])
                dk_blocks.append(d_k)
                dv_blocks.append(d_v)
            dq_parts.append(jnp.concatenate(dq_blocks, axis=0))
            dk_parts.append(jnp.concatenate(dk_blocks, axis=0))
            dv_parts.append(jnp.concatenate(dv_blocks, axis=0))
        d_decayed = jnp.concatenate(dq_parts, axis=1)
        d_grown = jnp.concatenate(dk_parts, axis=1)
        d_value = jnp.concatenate(dv_parts, axis=1)
        d_cumulative = decayed_q.astype(wide) * d_decayed - grown_k.astype(wide) * d_grown
        d_log = split_sum(upper_ones, d_cumulative)
        d_query = d_decayed * shrunk
        d_key = d_grown * grown
        d_q_pre = d_query * q_share * (1.0 + q_pre * (1.0 - q_share))
        d_f_pre = (1.0 - lower_bound) * (d_log / gate - d_key) * share * (1.0 - share)
        dpre_ref[rows, :PAIR] = d_q_pre.astype(low)
        dpre_ref[rows, PAIR : 2 * PAIR] = d_f_pre.astype(low)
        dpre_ref[rows, 2 * PAIR :] = d_value.astype(low)

    grad = mm(ht_ref[...], dpre_ref[...]).astype(low)
    grad_ref[...] = grad.reshape(grad_ref.shape)


def mixer_backward(which, h1t, gains8, kept, d_mixed, pair, slot, shard, grads):
    width, count = h1t.shape
    by_pair = pl.BlockSpec((count, PAIR), lambda j, _: (0, pair))
    from_whole = pl.BlockSpec((count, PAIR), lambda j, which: (0, which[0]))
    struct = jax.ShapeDtypeStruct
    shape = (width // shard, 2, shard, 3 * PAIR)
    grad_block = (width // shard, 1, shard, 3 * PAIR)
    held = [] if grads is None else [grads]
    return pl.pallas_call(
        functools.partial(mixer_backward_kernel, slot),
        grid_spec=pltpu.PrefetchScalarGridSpec(
            num_scalar_prefetch=1,
            grid=(1,),
            in_specs=[whole((width, count)), whole(gains8.shape)]
            + [by_pair] * 4
            + [from_whole]
            + [pl.BlockSpec(memory_space=pl.ANY)] * len(held),
            out_specs=[
                pl.BlockSpec(grad_block, lambda j, _: (0, pair, 0, 0)),
                whole((count, 3 * PAIR)),
            ],
        ),
        out_shape=[
            struct(shape, low),
            struct((count, 3 * PAIR), low),
        ],
        input_output_aliases={8: 0} if held else {},
        compiler_params=pltpu.CompilerParams(vmem_limit_bytes=VMEM_BYTES),
        cost_estimate=pl.CostEstimate(
            flops=count * width * 6 * PAIR + 20 * count * slot * PAIR,
            bytes_accessed=count * width * 5 + width * PAIR * 6,
            transcendentals=count * PAIR * 6,
        ),
        name="mixer_backward",
    )(which, h1t, gains8, *kept, d_mixed, *held)


def input_gradient_rows_kernel(x_ref, g_ref, *refs):
    pre_refs, weight_refs = refs[:4], refs[4:8]
    dx1_ref, dx_ref = refs[8:]
    d_h1 = mm_nt(pre_refs[0][...], weight_refs[0][...])
    for pre_ref, weight_ref in zip(pre_refs[1:], weight_refs[1:]):
        d_h1 = d_h1 + mm_nt(pre_ref[...], weight_ref[...])
    normed, scale = first_norm(x_ref, None)
    scaled = d_h1 * g_ref[0:1, :]
    dx_ref[...] = dx1_ref[...] + scale * (
        scaled - normed * jnp.mean(scaled * normed, axis=-1, keepdims=True)
    )


def input_gradient(rows, gains8, d_pre, weights, d_x1):
    count, width = rows.shape
    block = count // 2
    by_rows = lambda columns: pl.BlockSpec((block, columns), lambda j: (j, 0))
    weight_specs = [
        pl.BlockSpec((width, 3 * PAIR), lambda j, p=p: (0, p), pipeline_mode=pl.Buffered(1))
        for p in (0, 1, 0, 1)
    ]
    struct = jax.ShapeDtypeStruct
    return pl.pallas_call(
        input_gradient_rows_kernel,
        grid=(count // block,),
        in_specs=[by_rows(width), whole(gains8.shape)]
        + [by_rows(3 * PAIR)] * 4
        + weight_specs
        + [by_rows(width)],
        out_specs=by_rows(width),
        out_shape=struct((count, width), wide),
        compiler_params=pltpu.CompilerParams(vmem_limit_bytes=VMEM_BYTES),
        cost_estimate=pl.CostEstimate(
            flops=6 * count * width * width,
            bytes_accessed=count * width * 16 + width * width * 6,
            transcendentals=0,
        ),
        name="input_gradient",
    )(rows, gains8, *d_pre, weights[0], weights[0], weights[1], weights[1], d_x1)


def update(weight, momentum, average, gradient, step_rate):
    new_momentum = momentum_decay * momentum + gradient
    direction = gradient + momentum_decay * new_momentum + weight_decay * weight
    new_weight = weight - step_rate * direction
    new_average = average_decay * average + (1.0 - average_decay) * new_weight
    return (new_momentum, new_average, new_weight)


def update_kernel(pick, step_rate, sum_count, core_ref, w_ref, m_ref, a_ref, *refs):
    sums, outs, dots_ref = refs[:sum_count], refs[-4:-1], refs[-1]
    weight = w_ref[...]
    gradient = pick(core_ref[0], *[s[...] for s in sums]).astype(wide).reshape(weight.shape)
    results = update(weight, m_ref[...], a_ref[...], gradient, step_rate)
    for out, result in zip(outs, results):
        out[...] = result
    product = weight.astype(low).astype(wide) * gradient
    total = product[..., :HEAD_DIM]
    for start in range(HEAD_DIM, product.shape[-1], HEAD_DIM):
        total = total + product[..., start : start + HEAD_DIM]
    dots_ref[...] = total.reshape(dots_ref.shape)


def update_call(
    core, state, sums, grid, state_spec, sum_specs, pick, step_rate, name, before=()
):
    struct = jax.ShapeDtypeStruct(state[0].shape, wide)
    size = math.prod(state[0].shape)
    rows = state_spec.block_shape[-2]
    steps = math.prod(grid)
    tail = grid[1:]

    def dots_index(*indices):
        place = indices[0]
        for length, index in zip(tail, indices[1:]):
            place = place * length + index
        return (place, 0, 0)

    return pl.pallas_call(
        functools.partial(update_kernel, pick, step_rate, len(sums)),
        grid_spec=pltpu.PrefetchScalarGridSpec(
            num_scalar_prefetch=1,
            grid=grid,
            in_specs=[state_spec] * 3
            + sum_specs
            + [pl.BlockSpec(memory_space=pl.ANY)] * len(before),
            out_specs=[state_spec] * 3 + [pl.BlockSpec((1, rows, HEAD_DIM), dots_index)],
        ),
        out_shape=[struct] * 3 + [jax.ShapeDtypeStruct((steps, rows, HEAD_DIM), wide)],
        input_output_aliases={4 + len(sums) + k: k for k in range(len(before))},
        compiler_params=pltpu.CompilerParams(vmem_limit_bytes=VMEM_BYTES),
        cost_estimate=pl.CostEstimate(flops=12 * size, bytes_accessed=26 * size, transcendentals=0),
        name=name,
    )(core, *state, *sums, *before)


def update_attention(core, half_ref, state, qfv, out, step_rate, before):
    _, shard, width = state[0].shape
    down_rows = out.shape[0] - shard

    def pick(core_index, proj, last):
        gradient = last[down_rows:].astype(wide)
        for kind in range(3):
            parts = [proj[pair * shard :, kind * PAIR :][:shard, :PAIR] for pair in range(2)]
            chosen = jnp.concatenate(parts, axis=1).astype(wide)
            gradient = jnp.where(pl.program_id(0) == kind, chosen, gradient)
        return gradient

    return update_call(
        half_ref,
        state,
        (qfv, out),
        (4,),
        pl.BlockSpec((1, shard, width // 2), lambda kind, half: (kind, 0, half[0])),
        [whole(qfv.shape), whole(out.shape)],
        pick,
        step_rate,
        "update_attention",
        before,
    )


def update_ffn_in(core, state, sums, step_rate):
    _, shard, hidden = state[0].shape
    tile = hidden // 2

    def pick(core_index, mine, other):
        own = pl.program_id(0) == core_index
        return jnp.where(own, mine.astype(wide), other.astype(wide))

    sum_spec = pl.BlockSpec((shard, tile), lambda kind, j, _: (0, j))
    return update_call(
        core,
        state,
        sums,
        (2, 2),
        pl.BlockSpec((1, shard, tile), lambda kind, j, _: (kind, 0, j)),
        [sum_spec, sum_spec],
        pick,
        step_rate,
        "update_ffn_in",
    )


def update_ffn_out(core, state, sums, step_rate):
    shard, width = state[0].shape

    def pick(core_index, mine, other):
        own = pl.program_id(0) == core_index
        return jnp.where(own, mine[:shard].astype(wide), other[:shard].astype(wide))

    return update_call(
        core,
        state,
        sums,
        (2,),
        pl.BlockSpec((shard, width // 2), lambda j, _: (0, j)),
        [whole(total.shape) for total in sums],
        pick,
        step_rate,
        "update_ffn_out",
    )


def pack_kernel(core_ref, w_ref, g_ref, out_ref):
    pairs = w_ref.shape[2] // PAIR
    for pair in range(pairs):
        for kind in range(3):
            start = (pair * 3 + kind) * PAIR
            piece = w_ref[kind, :, pair * PAIR : (pair + 1) * PAIR]
            out_ref[:, start : start + PAIR] = piece.astype(low)
    start = 3 * pairs * PAIR
    out_ref[:, start : start + pairs * PAIR] = w_ref[3].astype(low)
    start += pairs * PAIR
    out_ref[:, start:] = g_ref[...].astype(low)


def pack_attention(core, weights, gains):
    _, shard, width = weights.shape
    half = width // 2
    gain_columns = jnp.pad(gains.T, ((0, 0), (0, HEAD_DIM - 3)))
    columns = 4 * half + HEAD_DIM
    return pl.pallas_call(
        pack_kernel,
        grid_spec=pltpu.PrefetchScalarGridSpec(
            num_scalar_prefetch=1,
            grid=(1,),
            in_specs=[
                pl.BlockSpec((4, shard, half), lambda j, core: (0, 0, core[0])),
                whole((shard, HEAD_DIM)),
            ],
            out_specs=whole((shard, columns)),
        ),
        out_shape=jax.ShapeDtypeStruct((shard, columns), low),
        name="pack_attention",
    )(core, weights, gain_columns)


RING = 8


def ring_place(index):
    return jnp.where(index % 2 == 0, index // 2, RING - 1 - index // 2)


def ring_member(place):
    place = place % RING
    return jnp.where(place < RING // 2, 2 * place, 2 * RING - 1 - 2 * place)


CYCLE = (0, 2, 4, 6, 7, 5, 3, 1)


def ring_next(tensor):
    replicas = lax.axis_size("dp")
    pairs = []
    for place_of, member in enumerate(CYCLE):
        for replica in range(replicas):
            target = CYCLE[(place_of + (1 if replica % 2 == 0 else -1)) % RING]
            pairs.append((member * replicas + replica, target * replicas + replica))
    return lax.ppermute(tensor, ("fsdp", "dp"), pairs)


def ring_shift(tensor, way):
    pairs = [(member, CYCLE[(at + way) % RING]) for at, member in enumerate(CYCLE)]
    return lax.ppermute(tensor, "fsdp", pairs)


def core_swap(tensor):
    return lax.ppermute(tensor, "dp", [(d, d ^ 1) for d in range(lax.axis_size("dp"))])


def column_swap(tensor):
    return lax.ppermute(tensor, "dp", [(d, d ^ 2) for d in range(lax.axis_size("dp"))])


def place_kernel(which, array_count, origin_ref, column_ref, *refs):
    pieces, outs, semaphores = refs[: len(which)], refs[-1 - array_count : -1], refs[-1]
    copies = []
    for number, (array, origin, side) in enumerate(which):
        rows, columns = pieces[number].shape
        lane = (0, column_ref[0], 1 - column_ref[0])[side]
        here = pl.ds(pl.multiple_of(origin_ref[origin] * rows, 16), rows)
        target = outs[array].at[here, lanes_of(lane, columns)]
        copies.append(pltpu.make_async_copy(pieces[number], target, semaphores.at[number]))
    for copy in copies:
        copy.start()
    for copy in copies:
        copy.wait()


def place(origins, column, which, pieces, arrays):
    anywhere = pl.BlockSpec(memory_space=pl.ANY)
    held = [] if arrays is None else list(arrays)
    shapes = [array.shape for array in held]
    if arrays is None:
        shapes = [
            (RING * piece.shape[0], piece.shape[1] * (2 if side else 1))
            for piece, (_, _, side) in zip(pieces, which)
        ]
    size = sum(math.prod(piece.shape) for piece in pieces)
    first = 2 + len(pieces)
    return pl.pallas_call(
        functools.partial(place_kernel, which, len(shapes)),
        grid_spec=pltpu.PrefetchScalarGridSpec(
            num_scalar_prefetch=2,
            grid=(1,),
            in_specs=[whole(piece.shape) for piece in pieces] + [anywhere] * len(held),
            out_specs=[anywhere] * len(shapes),
            scratch_shapes=[pltpu.SemaphoreType.DMA((len(pieces),))],
        ),
        out_shape=[jax.ShapeDtypeStruct(shape, pieces[0].dtype) for shape in shapes],
        input_output_aliases={first + k: k for k in range(len(held))},
        compiler_params=pltpu.CompilerParams(vmem_limit_bytes=VMEM_BYTES),
        cost_estimate=pl.CostEstimate(flops=0, bytes_accessed=8 * size, transcendentals=0),
        name="place",
    )(origins, column, *pieces, *held)


def after(tensor, *others):
    return lax.optimization_barrier((tensor, *others))[0]


def core_way():
    return 1 - 2 * (lax.axis_index("dp") % 2)


def ring_origins():
    steps = jnp.array((0, -1, -2, -3, -4, 1, 2, 3), jnp.int32)
    return ring_member(ring_place(lax.axis_index("fsdp")) + steps + RING).astype(jnp.int32)


class RingSum:
    def __init__(self, mine, arrived):
        self.mine, self.arrived = mine, arrived
        place = ring_place(lax.axis_index("fsdp"))
        self.owners = [ring_member(place - core_way() * (s + 1) + 2 * RING) for s in range(RING)]
        self.totals = []

    def term(self):
        parts = []
        for own, arrived in zip(self.mine, self.arrived):
            rows = own.shape[0] // RING
            start = self.owners[len(self.totals)] * rows
            part = lax.dynamic_slice_in_dim(own, start, rows, 0).astype(wide)
            parts.append(part + lax.dynamic_slice_in_dim(arrived, start, rows, 0).astype(wide))
        return parts[0] if len(parts) == 1 else jnp.concatenate(parts, axis=0)

    def begin(self, *others):
        if others:
            self.mine = [after(self.mine[0], *others), *self.mine[1:]]
        self.totals.append(self.term().astype(low))

    def step(self, *before, arriving=()):
        total = self.totals[-1]
        moved = ring_next(after(total, *before) if before else total)
        moved = after(moved, *arriving) if arriving else moved
        self.totals.append((moved.astype(wide) + self.term().astype(wide)).astype(low))

    def last(self):
        return self.totals[-1]


def gather_rows(shard):
    mine = lax.all_gather(shard, "fsdp", axis=0, tiled=True)
    return mine, core_swap(mine)


def core_sum(mine, other):
    return (mine.astype(wide) + core_swap(other).astype(wide)).astype(low)


def scatter_rows(both):
    return lax.psum_scatter(both, "fsdp", scatter_dimension=0, tiled=True)


def over_columns(total):
    total = (total.astype(wide) + column_swap(total).astype(wide)).astype(low)
    return total, core_swap(total)


def on_device(
    inputs,
    cotangent,
    lengths,
    attention_weights,
    attention_momentum,
    attention_average,
    ffn_inputs,
    ffn_inputs_momentum,
    ffn_inputs_average,
    ffn_output,
    ffn_output_momentum,
    ffn_output_average,
    gains,
    gains_momentum,
    gains_average,
):
    micro_count, slot, width = inputs.shape
    hidden = ffn_inputs.shape[2]
    shard, down_rows = ffn_inputs.shape[1], ffn_output.shape[0]
    fsdp_size = lax.axis_size("fsdp")
    replicas = lax.axis_size("dp")
    ringed = fsdp_size == RING
    core = lax.axis_index("dp") % 2
    column = lax.axis_index("dp") // 2
    count = micro_count * slot
    half = width // 2
    core_ref = core.astype(jnp.int32).reshape(1)
    other_ref = 1 - core_ref
    column_ref = column.astype(jnp.int32).reshape(1)
    is_first = core == 0

    packed = pack_attention(core_ref, attention_weights, gains)

    def gains_of(weights):
        gain_rows = weights[:, 4 * half : 4 * half + 3].T.astype(wide)
        return jnp.pad(gain_rows, ((0, 5), (0, 0)))

    rows = inputs.reshape(count, width)
    positions = jnp.arange(slot, dtype=jnp.int32)
    valid = (positions[None, :] < lengths).astype(wide).reshape(count, 1)
    errors = (cotangent.reshape(count, width).astype(wide) * valid).astype(low)

    if ringed:
        origins = ring_origins()
        up_part = lax.dynamic_slice(
            ffn_inputs, (core, 0, column * (hidden // 2)), (1, shard, hidden // 2)
        )[0].astype(low)
        down_part = lax.dynamic_slice(
            ffn_output, (0, core * half + column * (half // 2)), (down_rows, half // 2)
        ).astype(low)
        wholes, there = None, ()
        here = [(packed, up_part, down_part)]
        which = [(array, 0, min(array, 1)) for array in range(3)]
        which_there = []
        for step in range(1, 6):
            if step <= 3:
                onward = [
                    tuple(ring_shift(piece, way) for piece in here[-1 if way < 0 else 0])
                    for way in (1, -1)
                ]
            elif step == 4:
                onward = [
                    tuple(
                        ring_next(jnp.where(is_first, ahead, back)) for ahead, back in zip(*here)
                    )
                ]
            across = [tuple(column_swap(piece) for piece in pieces[1:]) for pieces in here]
            flat = [piece for pieces in (*here, *there) for piece in pieces]
            wholes = place(origins, column_ref, which + which_there, flat, wholes)
            if step == 5:
                break
            which_there = [(array, origin, 2) for array, origin, _ in which if array]
            ways = [step, step + 4][: len(onward)]
            which = [(array, origin, min(array, 1)) for origin in ways for array in range(3)]
            extra = [errors, valid] if step == 2 else []
            flat = [piece for pieces in (*onward, *across) for piece in pieces]
            tied = lax.optimization_barrier((*flat, *wholes, *extra))
            here = [tied[3 * k : 3 * k + 3] for k in range(len(onward))]
            rest = tied[3 * len(onward) :]
            there = [rest[2 * k : 2 * k + 2] for k in range(len(across))]
            wholes = rest[2 * len(across) : 2 * len(across) + 3]
        across = across[0]
        w_a = (wholes[0], core_swap(wholes[0]))
    else:
        w_a = gather_rows(packed)
        w_gu = gather_rows(
            lax.dynamic_index_in_dim(ffn_inputs, core, 0, keepdims=False).astype(low)
        )
        w_d = gather_rows(lax.dynamic_slice_in_dim(ffn_output, core * half, half, 1).astype(low))
    gains8 = gains_of(w_a[0])
    mixed_mine, *kept_mine = mixer_forward(core_ref, rows, w_a[0], gains8, slot)
    if ringed:
        across = lax.optimization_barrier((*across, mixed_mine, w_a[1]))[:2]
        which = [(array, 4, 2) for array in range(2)]
        wholes = [wholes[0], *place(origins, column_ref, which, across, wholes[1:])]
        rows = after(rows, *wholes[1:])
        w_gu, w_d = [(array, core_swap(array)) for array in wholes[1:]]
    mixed_other, *rest = mixer_forward(
        other_ref, rows, w_a[1], gains8, slot, (mixed_mine, w_a[0])
    )
    kept_other, (x1, h2, h2t, h1t) = rest[:4], rest[4:]
    owners = (fsdp_size, down_rows + shard, down_rows) if ringed else None
    gm, gu, gd_mine, gd_other, output, d_x1, d_mixed, go_mine, go_other = ffn(
        core_ref, h2, h2t, errors, w_gu, w_d, x1, (mixed_mine, mixed_other), w_a, valid, gains8, owners
    )

    mine_gu, arrived_gu = [gm], [core_swap(gu)]
    if ringed:
        mine_do, arrived_do = [gd_mine], [core_swap(gd_other)]
    else:
        mine_do, arrived_do = [gd_mine, go_mine], [core_swap(gd_other), core_swap(go_other)]
    backs = []
    for place_of in range(4):
        pair = place_of % 2
        from_half, kept = (other_ref, kept_other) if place_of < 2 else (core_ref, kept_mine)
        if ringed and place_of > 0:
            h1t = after(h1t, sum_gu.last(), sum_do.last())
        backs.append(
            mixer_backward(
                2 * from_half + pair,
                h1t,
                gains8,
                kept,
                d_mixed,
                pair,
                slot,
                shard,
                backs[-1][0] if pair else None,
            )
        )
        if ringed and place_of == 0:
            sum_gu, sum_do = RingSum(mine_gu, arrived_gu), RingSum(mine_do, arrived_do)
            sum_do.begin(backs[0][1])
            sum_gu.begin(backs[0][1])
        elif ringed:
            sum_do.step(arriving=(backs[-1][1],))
            sum_gu.step(arriving=(backs[-1][1],))
    grads, d_pre = [[back[which] for back in backs] for which in range(2)]
    by_owner = (fsdp_size * 2 * shard, 3 * PAIR)
    mine_qfv, arrived_qfv = [grads[3].reshape(by_owner)], [core_swap(grads[1].reshape(by_owner))]

    def finish_input(*others):
        last = after(d_pre[2], *others) if others else d_pre[2]
        return input_gradient(rows, gains8, [last, d_pre[3], *d_pre[:2]], w_a, d_x1)

    if ringed:
        sum_qfv = RingSum(mine_qfv, arrived_qfv)
        sum_qfv.begin()
        for step in range(1, RING):
            sum_qfv.step(*([input_grad] if step == 4 else []))
            if step <= 4:
                sum_do.step()
                sum_gu.step()
            if step == 2:
                input_grad = finish_input(sum_qfv.last())
        total_gu, total_do, total_qfv = sum_gu.last(), sum_do.last(), sum_qfv.last()
    else:
        total_gu, total_do, total_qfv = [
            jnp.concatenate(
                [
                    scatter_rows((own.astype(wide) + there.astype(wide)).astype(low))
                    for own, there in zip(mine, arrived)
                ],
                axis=0,
            )
            for mine, arrived in (
                (mine_gu, arrived_gu),
                (mine_do, arrived_do),
                (mine_qfv, arrived_qfv),
            )
        ]
        input_grad = finish_input()
    sum_gu = over_columns(total_gu)
    sum_do = over_columns(total_do)

    scale_rows = 1.0 / math.sqrt(count * fsdp_size * replicas)
    attention_state = (attention_weights, attention_momentum, attention_average)
    ffn_in_state = (ffn_inputs, ffn_inputs_momentum, ffn_inputs_average)
    ffn_out_state = (ffn_output, ffn_output_momentum, ffn_output_average)
    *new_in, dots_two = update_ffn_in(core_ref, ffn_in_state, sum_gu, matrix_rate * scale_rows)
    *new_out, _ = update_ffn_out(core_ref, ffn_out_state, sum_do, matrix_rate * scale_rows)
    there = after(column_swap(total_qfv), new_in[0], new_out[0])
    sum_qfv = (total_qfv.astype(wide) + there.astype(wide)).astype(low)
    *own, dots_own = update_attention(
        core_ref, core_ref, attention_state, sum_qfv, sum_do[0], matrix_rate * scale_rows, ()
    )
    theirs = after(core_swap(sum_qfv), own[0])
    *new_attention, dots_theirs = update_attention(
        core_ref, other_ref, attention_state, theirs, sum_do[1], matrix_rate * scale_rows, own
    )
    dots = jnp.sum(dots_own + dots_theirs, axis=2)
    row_sums = jnp.stack([dots[0] + dots[1] + dots[2], dots[3], jnp.sum(dots_two, axis=(0, 2))])
    sum_gains = row_sums / gains.astype(low).astype(wide)
    return (
        output.reshape(micro_count, slot, width),
        input_grad.reshape(micro_count, slot, width),
        *new_attention,
        *new_in,
        *new_out,
        *update(gains, gains_momentum, gains_average, sum_gains, gain_rate * scale_rows),
    )


def solution(mesh):
    rows_split = P(None, ("fsdp", "dp"), None)
    middle_split = P(None, "fsdp", None)
    first_split = P("fsdp", None)
    gains_split = P(None, "fsdp")
    in_specs = (
        (rows_split, rows_split, P(None, ("fsdp", "dp")))
        + (middle_split,) * 6
        + (first_split,) * 3
        + (gains_split,) * 3
    )
    out_specs = (
        (rows_split, rows_split)
        + (middle_split,) * 6
        + (first_split,) * 3
        + (gains_split,) * 3
    )
    return jax.shard_map(
        on_device, mesh=mesh, in_specs=in_specs, out_specs=out_specs, check_vma=False
    )
```

```python
import functools
import math

import jax
import jax.numpy as jnp
from jax import lax
from jax.experimental import pallas as pl
from jax.experimental.pallas import tpu as pltpu
from jax.sharding import PartitionSpec as P

HEAD_DIM = 128
PAIR = 2 * HEAD_DIM

lower_bound = 0.9
momentum_decay = 0.9
average_decay = 0.7
weight_decay = 0.0005
matrix_rate = 0.03
gain_rate = 0.1
low = jnp.bfloat16
wide = jnp.float32
TILE_F = 256
VMEM_BYTES = 60 * 1024 * 1024


def mm(left, right):
    return jnp.dot(left, right, preferred_element_type=wide)


def mm_nt(left, right):
    return lax.dot_general(left, right, (((1,), (1,)), ((), ())), preferred_element_type=wide)


def mm_tn(left, right):
    return lax.dot_general(left, right, (((0,), (0,)), ((), ())), preferred_element_type=wide)


def sigmoid(u):
    return 0.5 * jnp.tanh(0.5 * u) + 0.5


def whole(shape):
    return pl.BlockSpec(shape, lambda *_: (0,) * len(shape), pipeline_mode=pl.Buffered(1))


def split_sum(ones_matrix, tensor):
    high = tensor.astype(low)
    rest = (tensor - high.astype(wide)).astype(low)
    return mm(ones_matrix, high) + mm(ones_matrix, rest)


def triangle(length, lower):
    rows = lax.broadcasted_iota(jnp.int32, (length, length), 0)
    columns = lax.broadcasted_iota(jnp.int32, (length, length), 1)
    kept = rows >= columns if lower else rows <= columns
    return kept.astype(wide).astype(low)


def decay_parts(f_pre, lower_ones):
    share = sigmoid(f_pre)
    gate = lower_bound + (1.0 - lower_bound) * share
    keys_in = (1.0 - lower_bound) * (1.0 - share)
    cumulative = split_sum(lower_ones, jnp.log(gate))
    middle_row = cumulative.shape[0] // 2
    cumulative = cumulative - cumulative[middle_row : middle_row + 1, :]
    return share, gate, keys_in, cumulative


def first_norm(x_ref, gain_row):
    rows = x_ref[...].astype(wide)
    scale = lax.rsqrt(jnp.mean(rows * rows, axis=-1, keepdims=True) + 1e-06)
    return rows * scale, scale


def lanes_of(half, size):
    return pl.ds(pl.multiple_of(half * size, size), size)


def mixer_forward_first_kernel(
    slot, half_ref, x_ref, w_ref, columns_ref, on_ref, q_ref, f_ref, v_ref, o_ref, g_ref, h_s
):
    @pl.when(pl.program_id(0) == 0)
    def _():
        g_ref[...] = columns_ref[...].astype(wide).T[: g_ref.shape[0], :]

    mixer_forward_kernel(
        slot, half_ref, x_ref, w_ref, g_ref, on_ref, q_ref, f_ref, v_ref, o_ref, h_s
    )


def mixer_forward_kernel(
    slot, half_ref, x_ref, w_ref, g_ref, on_ref, q_ref, f_ref, v_ref, o_ref, h_s
):
    @pl.when(pl.program_id(0) == 0)
    def _():
        normed, _ = first_norm(x_ref, None)
        h_s[...] = (normed * g_ref[0:1, :]).astype(low)

    gain_o = g_ref[1:2, lanes_of(half_ref[0] * pl.num_programs(0) + pl.program_id(0), PAIR)]
    pre = mm(h_s[...], w_ref[...])
    q_ref[...] = pre[:, :PAIR]
    f_ref[...] = pre[:, PAIR : 2 * PAIR]
    v_ref[...] = pre[:, 2 * PAIR :].astype(low)
    lower_ones = triangle(slot, True)
    block_rows = lax.broadcasted_iota(jnp.int32, (HEAD_DIM, HEAD_DIM), 0)
    block_columns = lax.broadcasted_iota(jnp.int32, (HEAD_DIM, HEAD_DIM), 1)
    causal = block_rows >= block_columns
    for sequence in range(x_ref.shape[0] // slot):
        rows = slice(sequence * slot, (sequence + 1) * slot)
        q_pre = q_ref[rows, :]
        _, _, keys_in, cumulative = decay_parts(f_ref[rows, :], lower_ones)
        grown = jnp.exp(-cumulative)
        decayed_q = (q_pre * sigmoid(q_pre) * jnp.exp(cumulative)).astype(low)
        grown_k = (keys_in * grown).astype(low)
        values = v_ref[rows, :]
        for head in range(2):
            lanes = slice(head * HEAD_DIM, (head + 1) * HEAD_DIM)
            for block in range(slot // HEAD_DIM):
                start, end = block * HEAD_DIM, (block + 1) * HEAD_DIM
                q_block = decayed_q[start:end, lanes]
                diagonal = mm_nt(q_block, grown_k[start:end, lanes])
                diagonal = jnp.where(causal, diagonal, 0.0).astype(low)
                out = mm(diagonal, values[start:end, lanes])
                if block > 0:
                    scores = mm_nt(q_block, grown_k[:start, lanes]).astype(low)
                    out = out + mm(scores, values[:start, lanes])
                scale = lax.rsqrt(jnp.mean(out * out, axis=-1, keepdims=True) + 1e-05)
                target = slice(sequence * slot + start, sequence * slot + end)
                o_ref[target, lanes] = out.astype(low)
                on_ref[target, lanes] = (out * scale * gain_o[:, lanes]).astype(low)


def mixer_forward_last_kernel(
    slot,
    half_ref,
    x_ref,
    w_ref,
    g_ref,
    before_ref,
    woo_ref,
    wom_ref,
    on_ref,
    q_ref,
    f_ref,
    v_ref,
    o_ref,
    x1_ref,
    h2_ref,
    h2t_ref,
    h1t_ref,
    h_s,
    on_s,
):
    step = pl.program_id(0)
    half = before_ref.shape[1]
    mixer_forward_kernel(
        slot, half_ref, x_ref, w_ref, g_ref, on_ref, q_ref, f_ref, v_ref, o_ref, h_s
    )
    on_s[:, lanes_of(half_ref[0] * pl.num_programs(0) + step, PAIR)] = on_ref[...]

    @pl.when(step == pl.num_programs(0) - 1)
    def _():
        here = lanes_of(half_ref[0], half)
        there = lanes_of(1 - half_ref[0], half)
        on_s[:, there] = before_ref[...]
        h1t_ref[...] = h_s[...].astype(wide).T.astype(low)
        x1_ref[:, here] = x_ref[:, here].astype(wide) + mm(on_s[...], woo_ref[...])
        x1_ref[:, there] = x_ref[:, there].astype(wide) + mm(on_s[...], wom_ref[...])
        x1 = x1_ref[...]
        scale = lax.rsqrt(jnp.mean(x1 * x1, axis=-1, keepdims=True) + 1e-06)
        normed = x1 * scale * g_ref[2:3, :]
        h2_ref[...] = normed.astype(low)
        h2t_ref[...] = normed.T.astype(low)


def mixer_forward(half, rows, weights, slot, ending=None):
    count, width = rows.shape
    pairs = width // PAIR // 2
    by_pair = pl.BlockSpec((count, PAIR), lambda j, _: (0, j))
    struct = jax.ShapeDtypeStruct
    shape = lambda kind: struct((count, width // 2), kind)
    in_specs = [whole(rows.shape), pl.BlockSpec((width, 3 * PAIR), lambda j, _: (0, j))]
    operands = [half, rows, weights]
    out_specs = [by_pair] * 5
    out_shape = [shape(low), shape(wide), shape(wide), shape(low), shape(low)]
    scratch = [pltpu.VMEM((count, width), low)]
    if ending is None:
        kernel = mixer_forward_first_kernel
        last = weights.shape[1] // HEAD_DIM - 1
        in_specs += [pl.BlockSpec((width, HEAD_DIM), lambda j, _: (0, last))]
        operands += [weights]
        out_specs += [whole((8, width))]
        out_shape += [struct((8, width), wide)]
    if ending is not None:
        kernel = mixer_forward_last_kernel
        out_weights = pl.BlockSpec((width, width // 2), lambda j, _: (0, 3))
        in_specs += [whole(ending[0].shape), whole((count, width // 2)), out_weights, out_weights]
        operands += [ending[0], ending[1], weights, ending[2]]
        out_specs += [whole((count, width))] * 2 + [whole((width, count))] * 2
        out_shape += [
            struct((count, width), wide),
            struct((count, width), low),
            struct((width, count), low),
            struct((width, count), low),
        ]
        scratch += [pltpu.VMEM((count, width), low)]
    return pl.pallas_call(
        functools.partial(kernel, slot),
        grid_spec=pltpu.PrefetchScalarGridSpec(
            num_scalar_prefetch=1,
            grid=(pairs,),
            in_specs=in_specs,
            out_specs=out_specs,
            scratch_shapes=scratch,
        ),
        out_shape=out_shape,
        compiler_params=pltpu.CompilerParams(vmem_limit_bytes=VMEM_BYTES),
        cost_estimate=pl.CostEstimate(
            flops=count * width * 4 * width + 10 * count * slot * width,
            bytes_accessed=count * width * 12 + width * width * 4,
            transcendentals=count * width * 3,
        ),
        name="mixer_forward",
    )(*operands)


def store_down(out_ref, tile, owners):
    if owners is None:
        out_ref[...] = tile
        return
    _, stride, down_rows = owners
    block = math.gcd(down_rows, tile.shape[0])
    first = pl.program_id(0) * (tile.shape[0] // block)
    for part in range(tile.shape[0] // block):
        owner = (first + part) // (down_rows // block)
        inside = (first + part) % (down_rows // block)
        start = pl.multiple_of(owner * stride + inside * block, block)
        out_ref[pl.ds(start, block), :] = tile[part * block : (part + 1) * block, :]


def ffn_tile(owners, core_ref, refs, grads, acc_ref, dh_ref, scratch):
    h_ref, ht_ref, e_ref, wm_ref, wu_ref, wdm_ref, wdo_ref = refs
    gm_ref, gu_ref, gdm_ref, gdo_ref = grads
    gu_w, down_w, gu_g, down_g = scratch
    half, tile = wdm_ref.shape[1], wm_ref.shape[1]
    mine, other = lanes_of(core_ref[0], half), lanes_of(1 - core_ref[0], half)
    kind, kind_other = lanes_of(core_ref[0], tile), lanes_of(1 - core_ref[0], tile)
    gu_w[:, kind] = wm_ref[...]
    gu_w[:, kind_other] = wu_ref[...]
    down_w[:, mine] = wdm_ref[...]
    down_w[:, other] = wdo_ref[...]
    pre = mm(h_ref[...], gu_w[...])
    a, b = pre[:, :tile], pre[:, tile:]
    share = sigmoid(a)
    swish = a * share
    mid = (swish * b).astype(low)
    d_mid = mm_nt(e_ref[...], down_w[...])
    down_g[...] = mm_tn(mid, e_ref[...]).astype(low)
    d_a = (d_mid * b * (share + swish * (1.0 - share))).astype(low)
    d_b = (d_mid * swish).astype(low)
    d_pre = jnp.concatenate([d_a, d_b], axis=1)
    acc_ref[...] += mm(mid, down_w[...])
    dh_ref[...] += mm_nt(d_pre, gu_w[...])
    gu_g[...] = mm(ht_ref[...], d_pre).astype(low)
    gm_ref[...] = gu_g[:, kind]
    gu_ref[...] = gu_g[:, kind_other]
    store_down(gdm_ref, down_g[:, mine], owners)
    store_down(gdo_ref, down_g[:, other], owners)


def ffn_kernel(
    owners,
    core_ref,
    h_ref,
    ht_ref,
    e_ref,
    wm_ref,
    wu_ref,
    wdm_ref,
    wdo_ref,
    x1_ref,
    onm_ref,
    ono_ref,
    wom_ref,
    woo_ref,
    m_ref,
    g_ref,
    gm_ref,
    gu_ref,
    gdm_ref,
    gdo_ref,
    out_ref,
    dh_s,
    don_ref,
    gom_ref,
    goo_ref,
    on_s,
    acc_s,
    *scratch,
):
    @pl.when(pl.program_id(0) == 0)
    def _():
        acc_s[...] = x1_ref[...]
        dh_s[...] = jnp.zeros_like(dh_s)

    grads = (gm_ref, gu_ref, gdm_ref, gdo_ref)
    refs = (h_ref, ht_ref, e_ref, wm_ref, wu_ref, wdm_ref, wdo_ref)
    ffn_tile(owners, core_ref, refs, grads, acc_s, dh_s, scratch)

    @pl.when(pl.program_id(0) == pl.num_programs(0) - 1)
    def _():
        half = onm_ref.shape[1]
        mine = lanes_of(core_ref[0], half)
        other = lanes_of(1 - core_ref[0], half)
        out_ref[...] = (acc_s[...] * m_ref[...]).astype(low)
        x1 = x1_ref[...]
        scale = lax.rsqrt(jnp.mean(x1 * x1, axis=-1, keepdims=True) + 1e-06)
        normed = x1 * scale
        d_h2 = dh_s[...]
        scaled = d_h2 * g_ref[2:3, :]
        d_x1 = e_ref[...].astype(wide) + scale * (
            scaled - normed * jnp.mean(scaled * normed, axis=-1, keepdims=True)
        )
        dh_s[...] = d_x1
        on_s[...] = d_x1.astype(low)
        d_mixed = mm_nt(on_s[:, mine], wom_ref[...]) + mm_nt(on_s[:, other], woo_ref[...])
        don_ref[...] = d_mixed.astype(low)
        for columns, g_down_ref, g_ref_o in ((mine, gdm_ref, gom_ref), (other, gdo_ref, goo_ref)):
            d_1 = on_s[:, columns]
            for which, on_ref in ((core_ref[0], onm_ref), (1 - core_ref[0], ono_ref)):
                grad_o = mm_tn(on_ref[...], d_1).astype(low)
                if owners is None:
                    g_ref_o[pl.ds(pl.multiple_of(which * half, half), half), :] = grad_o
                    continue
                count, stride, down_rows = owners
                rows = stride - down_rows
                for part in range(half // rows):
                    owner = which * (count // 2) + part
                    start = pl.multiple_of(owner * stride + down_rows, math.gcd(stride, down_rows))
                    g_down_ref[pl.ds(start, rows), :] = grad_o[part * rows : (part + 1) * rows, :]


def ffn(core, h2, h2t, errors, w_gu, w_d, x1, mixed, w_a, mask, gains8, owners):
    count, width = h2.shape
    half = width // 2
    hidden = w_gu[0].shape[1]
    full = whole((count, width))
    half_full = whole((count, half))
    square = whole((width, half))
    in_tile = pl.BlockSpec((width, TILE_F), lambda j, _: (0, j))
    out_tile = pl.BlockSpec((TILE_F, half), lambda j, _: (j, 0))
    out_weights = pl.BlockSpec((width, half), lambda j, _: (0, 3), pipeline_mode=pl.Buffered(1))
    down_spec, down_shape, out_spec, out_shape = out_tile, (hidden, half), square, (width, half)
    if owners is not None:
        down_shape, out_shape = (owners[0] * owners[1], half), (16, half)
        down_spec, out_spec = whole(down_shape), whole(out_shape)
    struct = jax.ShapeDtypeStruct
    return pl.pallas_call(
        functools.partial(ffn_kernel, owners),
        grid_spec=pltpu.PrefetchScalarGridSpec(
            num_scalar_prefetch=1,
            grid=(hidden // TILE_F,),
            in_specs=[full, whole(h2t.shape), full, in_tile, in_tile, out_tile, out_tile]
            + [full, half_full, half_full, out_weights, out_weights]
            + [whole((count, 1)), whole((8, width))],
            out_specs=[in_tile, in_tile, down_spec, down_spec]
            + [full, full, full, out_spec, out_spec],
            scratch_shapes=[
                pltpu.VMEM((count, width), low),
                pltpu.VMEM((count, width), wide),
                pltpu.VMEM((width, 2 * TILE_F), low),
                pltpu.VMEM((TILE_F, width), low),
                pltpu.VMEM((width, 2 * TILE_F), low),
                pltpu.VMEM((TILE_F, width), low),
            ],
        ),
        out_shape=[struct((width, hidden), low)] * 2
        + [struct(down_shape, low)] * 2
        + [
            struct((count, width), low),
            struct((count, width), wide),
            struct((count, width), low),
            struct(out_shape, low),
            struct(out_shape, low),
        ],
        compiler_params=pltpu.CompilerParams(vmem_limit_bytes=VMEM_BYTES),
        cost_estimate=pl.CostEstimate(
            flops=16 * count * width * hidden,
            bytes_accessed=count * width * 20 + width * hidden * 12,
            transcendentals=count * hidden,
        ),
        name="ffn",
    )(core, h2, h2t, errors, *w_gu, *w_d, x1, *mixed, *w_a, mask, gains8)


def mixer_backward_kernel(
    slot,
    half_ref,
    ht_ref,
    g_ref,
    q_ref,
    f_ref,
    v_ref,
    o_ref,
    don_ref,
    *outs,
):
    grad_ref, dpre_ref = outs[-2:]
    gain_o = g_ref[1:2, lanes_of(half_ref[0], PAIR)]
    lower_ones = triangle(slot, True)
    upper_ones = triangle(slot, False)
    block_rows = lax.broadcasted_iota(jnp.int32, (HEAD_DIM, HEAD_DIM), 0)
    block_columns = lax.broadcasted_iota(jnp.int32, (HEAD_DIM, HEAD_DIM), 1)
    causal = block_rows >= block_columns
    causal_t = block_rows <= block_columns
    blocks = slot // HEAD_DIM
    for sequence in range(q_ref.shape[0] // slot):
        rows = slice(sequence * slot, (sequence + 1) * slot)
        d_on = don_ref[rows, :].astype(wide)
        out = o_ref[rows, :].astype(wide)
        d_out_parts = []
        for head in range(2):
            lanes = slice(head * HEAD_DIM, (head + 1) * HEAD_DIM)
            out_h, d_on_h = out[:, lanes], d_on[:, lanes]
            scale = lax.rsqrt(jnp.mean(out_h * out_h, axis=-1, keepdims=True) + 1e-05)
            normed = out_h * scale
            scaled = d_on_h * gain_o[:, lanes]
            inner = jnp.mean(scaled * normed, axis=-1, keepdims=True)
            d_out_parts.append((scale * (scaled - normed * inner)).astype(low))

        q_pre = q_ref[rows, :]
        share, gate, keys_in, cumulative = decay_parts(f_ref[rows, :], lower_ones)
        grown = jnp.exp(-cumulative)
        shrunk = jnp.exp(cumulative)
        q_share = sigmoid(q_pre)
        decayed_q = (q_pre * q_share * shrunk).astype(low)
        grown_k = (keys_in * grown).astype(low)
        values = v_ref[rows, :]
        dq_parts, dk_parts, dv_parts = [], [], []
        for head in range(2):
            lanes = slice(head * HEAD_DIM, (head + 1) * HEAD_DIM)
            q_h, k_h, v_h = decayed_q[:, lanes], grown_k[:, lanes], values[:, lanes]
            d_out = d_out_parts[head]
            dq_blocks, dk_blocks, dv_blocks = [], [], []
            for block in range(blocks):
                start, end = block * HEAD_DIM, (block + 1) * HEAD_DIM
                here = slice(start, end)
                d_scores = mm_nt(d_out[here], v_h[here])
                d_scores = jnp.where(causal, d_scores, 0.0).astype(low)
                d_q = mm(d_scores, k_h[here])
                if block > 0:
                    before = slice(0, start)
                    d_scores = mm_nt(d_out[here], v_h[before]).astype(low)
                    d_q = d_q + mm(d_scores, k_h[before])
                dq_blocks.append(d_q)
                scores = jnp.where(causal_t, mm_nt(k_h[here], q_h[here]), 0.0).astype(low)
                d_scores = jnp.where(causal_t, mm_nt(v_h[here], d_out[here]), 0.0).astype(low)
                d_v = mm(scores, d_out[here])
                d_k = mm(d_scores, q_h[here])
                if block < blocks - 1:
                    after = slice(end, slot)
                    scores = mm_nt(k_h[here], q_h[after]).astype(low)
                    d_scores = mm_nt(v_h[here], d_out[after]).astype(low)
                    d_v = d_v + mm(scores, d_out[after])
                    d_k = d_k + mm(d_scores, q_h[after])
                dk_blocks.append(d_k)
                dv_blocks.append(d_v)
            dq_parts.append(jnp.concatenate(dq_blocks, axis=0))
            dk_parts.append(jnp.concatenate(dk_blocks, axis=0))
            dv_parts.append(jnp.concatenate(dv_blocks, axis=0))
        d_decayed = jnp.concatenate(dq_parts, axis=1)
        d_grown = jnp.concatenate(dk_parts, axis=1)
        d_value = jnp.concatenate(dv_parts, axis=1)
        d_cumulative = decayed_q.astype(wide) * d_decayed - grown_k.astype(wide) * d_grown
        d_log = split_sum(upper_ones, d_cumulative)
        d_query = d_decayed * shrunk
        d_key = d_grown * grown
        d_q_pre = d_query * q_share * (1.0 + q_pre * (1.0 - q_share))
        d_f_pre = (1.0 - lower_bound) * (d_log / gate - d_key) * share * (1.0 - share)
        dpre_ref[rows, :PAIR] = d_q_pre.astype(low)
        dpre_ref[rows, PAIR : 2 * PAIR] = d_f_pre.astype(low)
        dpre_ref[rows, 2 * PAIR :] = d_value.astype(low)

    grad = mm(ht_ref[...], dpre_ref[...]).astype(low)
    grad_ref[...] = grad.reshape(grad_ref.shape)


def mixer_backward(which, h1t, gains8, kept, d_mixed, pair, slot, shard, grads):
    width, count = h1t.shape
    by_pair = pl.BlockSpec((count, PAIR), lambda j, _: (0, pair))
    from_whole = pl.BlockSpec((count, PAIR), lambda j, which: (0, which[0]))
    struct = jax.ShapeDtypeStruct
    shape = (width // shard, 2, shard, 3 * PAIR)
    grad_block = (width // shard, 1, shard, 3 * PAIR)
    held = [] if grads is None else [grads]
    return pl.pallas_call(
        functools.partial(mixer_backward_kernel, slot),
        grid_spec=pltpu.PrefetchScalarGridSpec(
            num_scalar_prefetch=1,
            grid=(1,),
            in_specs=[whole((width, count)), whole(gains8.shape)]
            + [by_pair] * 4
            + [from_whole]
            + [pl.BlockSpec(memory_space=pl.ANY)] * len(held),
            out_specs=[
                pl.BlockSpec(grad_block, lambda j, _: (0, pair, 0, 0)),
                whole((count, 3 * PAIR)),
            ],
        ),
        out_shape=[
            struct(shape, low),
            struct((count, 3 * PAIR), low),
        ],
        input_output_aliases={8: 0} if held else {},
        compiler_params=pltpu.CompilerParams(vmem_limit_bytes=VMEM_BYTES),
        cost_estimate=pl.CostEstimate(
            flops=count * width * 6 * PAIR + 20 * count * slot * PAIR,
            bytes_accessed=count * width * 5 + width * PAIR * 6,
            transcendentals=count * PAIR * 6,
        ),
        name="mixer_backward",
    )(which, h1t, gains8, *kept, d_mixed, *held)


def input_gradient_rows_kernel(x_ref, g_ref, *refs):
    pre_refs, weight_refs = refs[:4], refs[4:8]
    dx1_ref, dx_ref = refs[8:]
    d_h1 = mm_nt(pre_refs[0][...], weight_refs[0][...])
    for pre_ref, weight_ref in zip(pre_refs[1:], weight_refs[1:]):
        d_h1 = d_h1 + mm_nt(pre_ref[...], weight_ref[...])
    normed, scale = first_norm(x_ref, None)
    scaled = d_h1 * g_ref[0:1, :]
    dx_ref[...] = dx1_ref[...] + scale * (
        scaled - normed * jnp.mean(scaled * normed, axis=-1, keepdims=True)
    )


def input_gradient(rows, gains8, d_pre, weights, d_x1):
    count, width = rows.shape
    block = count // 2
    by_rows = lambda columns: pl.BlockSpec((block, columns), lambda j: (j, 0))
    weight_specs = [
        pl.BlockSpec((width, 3 * PAIR), lambda j, p=p: (0, p), pipeline_mode=pl.Buffered(1))
        for p in (0, 1, 0, 1)
    ]
    struct = jax.ShapeDtypeStruct
    return pl.pallas_call(
        input_gradient_rows_kernel,
        grid=(count // block,),
        in_specs=[by_rows(width), whole(gains8.shape)]
        + [by_rows(3 * PAIR)] * 4
        + weight_specs
        + [by_rows(width)],
        out_specs=by_rows(width),
        out_shape=struct((count, width), wide),
        compiler_params=pltpu.CompilerParams(vmem_limit_bytes=VMEM_BYTES),
        cost_estimate=pl.CostEstimate(
            flops=6 * count * width * width,
            bytes_accessed=count * width * 16 + width * width * 6,
            transcendentals=0,
        ),
        name="input_gradient",
    )(rows, gains8, *d_pre, weights[0], weights[0], weights[1], weights[1], d_x1)


def update(weight, momentum, average, gradient, step_rate):
    new_momentum = momentum_decay * momentum + gradient
    direction = gradient + momentum_decay * new_momentum + weight_decay * weight
    new_weight = weight - step_rate * direction
    new_average = average_decay * average + (1.0 - average_decay) * new_weight
    return (new_momentum, new_average, new_weight)


def update_kernel(pick, step_rate, sum_count, core_ref, w_ref, m_ref, a_ref, *refs):
    sums, outs, dots_ref = refs[:sum_count], refs[-4:-1], refs[-1]
    weight = w_ref[...]
    gradient = pick(core_ref[0], *[s[...] for s in sums]).astype(wide).reshape(weight.shape)
    results = update(weight, m_ref[...], a_ref[...], gradient, step_rate)
    for out, result in zip(outs, results):
        out[...] = result
    product = weight.astype(low).astype(wide) * gradient
    total = product[..., :HEAD_DIM]
    for start in range(HEAD_DIM, product.shape[-1], HEAD_DIM):
        total = total + product[..., start : start + HEAD_DIM]
    dots_ref[...] = total.reshape(dots_ref.shape)


def update_call(
    core, state, sums, grid, state_spec, sum_specs, pick, step_rate, name, before=()
):
    struct = jax.ShapeDtypeStruct(state[0].shape, wide)
    size = math.prod(state[0].shape)
    rows = state_spec.block_shape[-2]
    steps = math.prod(grid)
    tail = grid[1:]

    def dots_index(*indices):
        place = indices[0]
        for length, index in zip(tail, indices[1:]):
            place = place * length + index
        return (place, 0, 0)

    return pl.pallas_call(
        functools.partial(update_kernel, pick, step_rate, len(sums)),
        grid_spec=pltpu.PrefetchScalarGridSpec(
            num_scalar_prefetch=1,
            grid=grid,
            in_specs=[state_spec] * 3
            + sum_specs
            + [pl.BlockSpec(memory_space=pl.ANY)] * len(before),
            out_specs=[state_spec] * 3 + [pl.BlockSpec((1, rows, HEAD_DIM), dots_index)],
        ),
        out_shape=[struct] * 3 + [jax.ShapeDtypeStruct((steps, rows, HEAD_DIM), wide)],
        input_output_aliases={4 + len(sums) + k: k for k in range(len(before))},
        compiler_params=pltpu.CompilerParams(vmem_limit_bytes=VMEM_BYTES),
        cost_estimate=pl.CostEstimate(flops=12 * size, bytes_accessed=26 * size, transcendentals=0),
        name=name,
    )(core, *state, *sums, *before)


def update_attention(core, half_ref, state, qfv, out, step_rate, before):
    _, shard, width = state[0].shape
    down_rows = out.shape[0] - shard

    def pick(core_index, proj, last):
        gradient = last[down_rows:].astype(wide)
        for kind in range(3):
            parts = [proj[pair * shard :, kind * PAIR :][:shard, :PAIR] for pair in range(2)]
            chosen = jnp.concatenate(parts, axis=1).astype(wide)
            gradient = jnp.where(pl.program_id(0) == kind, chosen, gradient)
        return gradient

    return update_call(
        half_ref,
        state,
        (qfv, out),
        (4,),
        pl.BlockSpec((1, shard, width // 2), lambda kind, half: (kind, 0, half[0])),
        [whole(qfv.shape), whole(out.shape)],
        pick,
        step_rate,
        "update_attention",
        before,
    )


def update_ffn_in(core, state, sums, step_rate):
    _, shard, hidden = state[0].shape
    tile = hidden // 2

    def pick(core_index, mine, other):
        own = pl.program_id(0) == core_index
        return jnp.where(own, mine.astype(wide), other.astype(wide))

    sum_spec = pl.BlockSpec((shard, tile), lambda kind, j, _: (0, j))
    return update_call(
        core,
        state,
        sums,
        (2, 2),
        pl.BlockSpec((1, shard, tile), lambda kind, j, _: (kind, 0, j)),
        [sum_spec, sum_spec],
        pick,
        step_rate,
        "update_ffn_in",
    )


def update_ffn_out(core, state, sums, step_rate):
    shard, width = state[0].shape

    def pick(core_index, mine, other):
        own = pl.program_id(0) == core_index
        return jnp.where(own, mine[:shard].astype(wide), other[:shard].astype(wide))

    return update_call(
        core,
        state,
        sums,
        (2,),
        pl.BlockSpec((shard, width // 2), lambda j, _: (0, j)),
        [whole(total.shape) for total in sums],
        pick,
        step_rate,
        "update_ffn_out",
    )


def pack_kernel(core_ref, w_ref, g_ref, out_ref):
    pairs = w_ref.shape[2] // PAIR
    for pair in range(pairs):
        for kind in range(3):
            start = (pair * 3 + kind) * PAIR
            piece = w_ref[kind, :, pair * PAIR : (pair + 1) * PAIR]
            out_ref[:, start : start + PAIR] = piece.astype(low)
    start = 3 * pairs * PAIR
    out_ref[:, start : start + pairs * PAIR] = w_ref[3].astype(low)
    start += pairs * PAIR
    out_ref[:, start:] = g_ref[...].astype(low)


def pack_attention(core, weights, gains):
    _, shard, width = weights.shape
    half = width // 2
    gain_columns = jnp.pad(gains.T, ((0, 0), (0, HEAD_DIM - 3)))
    columns = 4 * half + HEAD_DIM
    return pl.pallas_call(
        pack_kernel,
        grid_spec=pltpu.PrefetchScalarGridSpec(
            num_scalar_prefetch=1,
            grid=(1,),
            in_specs=[
                pl.BlockSpec((4, shard, half), lambda j, core: (0, 0, core[0])),
                whole((shard, HEAD_DIM)),
            ],
            out_specs=whole((shard, columns)),
        ),
        out_shape=jax.ShapeDtypeStruct((shard, columns), low),
        name="pack_attention",
    )(core, weights, gain_columns)


RING = 8


def ring_place(index):
    return jnp.where(index % 2 == 0, index // 2, RING - 1 - index // 2)


def ring_member(place):
    place = place % RING
    return jnp.where(place < RING // 2, 2 * place, 2 * RING - 1 - 2 * place)


CYCLE = (0, 2, 4, 6, 7, 5, 3, 1)


def ring_next(tensor):
    replicas = lax.axis_size("dp")
    pairs = []
    for place_of, member in enumerate(CYCLE):
        for replica in range(replicas):
            target = CYCLE[(place_of + (1 if replica % 2 == 0 else -1)) % RING]
            pairs.append((member * replicas + replica, target * replicas + replica))
    return lax.ppermute(tensor, ("fsdp", "dp"), pairs)


def ring_shift(tensor, way):
    pairs = [(member, CYCLE[(at + way) % RING]) for at, member in enumerate(CYCLE)]
    return lax.ppermute(tensor, "fsdp", pairs)


def core_swap(tensor):
    return lax.ppermute(tensor, "dp", [(d, d ^ 1) for d in range(lax.axis_size("dp"))])


def column_swap(tensor):
    return lax.ppermute(tensor, "dp", [(d, d ^ 2) for d in range(lax.axis_size("dp"))])


def pack_all_kernel(core_ref, column_ref, w_ref, up_ref, down_ref, g_ref, out_ref):
    shard = w_ref.shape[1]
    pairs = w_ref.shape[2] // PAIR
    start = 0
    for pair in range(pairs):
        for kind in range(3):
            piece = w_ref[kind, :, pair * PAIR : (pair + 1) * PAIR]
            out_ref[0, :, start : start + PAIR] = piece.astype(low)
            start += PAIR
    out_ref[0, :, start : start + pairs * PAIR] = w_ref[3].astype(low)
    start += pairs * PAIR
    rows = lax.broadcasted_iota(jnp.int32, (HEAD_DIM, shard), 0)
    gains = jnp.where(rows == 0, g_ref[0:1, :], jnp.where(rows == 1, g_ref[1:2, :], g_ref[2:3, :]))
    out_ref[0, :, start:] = jnp.where(rows < 3, gains, 0.0).T.astype(low)
    up_columns = up_ref.shape[2]
    out_ref[1, :, :up_columns] = up_ref[0].astype(low)
    for part, (start, count) in enumerate(down_parts(down_ref.shape[0], shard)):
        lanes = slice(up_columns + part * PAIR, up_columns + (part + 1) * PAIR)
        out_ref[1, :count, lanes] = down_ref[start : start + count, :].astype(low)
        if count < shard:
            out_ref[1, count:, lanes] = jnp.zeros((shard - count, PAIR), low)


def down_parts(down_rows, shard):
    return [(start, min(shard, down_rows - start)) for start in range(0, down_rows, shard)]


def pack_all(core, column, weights, up, down, gains):
    _, shard, width = weights.shape
    half = width // 2
    columns = 4 * half + HEAD_DIM
    return pl.pallas_call(
        pack_all_kernel,
        grid_spec=pltpu.PrefetchScalarGridSpec(
            num_scalar_prefetch=2,
            grid=(1,),
            in_specs=[
                pl.BlockSpec((4, shard, half), lambda j, core, column: (0, 0, core[0])),
                pl.BlockSpec(
                    (1, shard, up.shape[2] // 2), lambda j, core, column: (core[0], 0, column[0])
                ),
                pl.BlockSpec(
                    (down.shape[0], PAIR), lambda j, core, column: (0, 2 * core[0] + column[0])
                ),
                whole(gains.shape),
            ],
            out_specs=whole((2, shard, columns)),
        ),
        out_shape=jax.ShapeDtypeStruct((2, shard, columns), low),
        compiler_params=pltpu.CompilerParams(vmem_limit_bytes=VMEM_BYTES),
        name="pack_all",
    )(core, column, weights, up, down, gains)


def place_kernel(which, kept, shapes, origin_ref, column_ref, *refs):
    pieces, outs, semaphores = refs[: len(which)], refs[-1 - len(kept) : -1], refs[-1]
    targets = dict(zip(kept, outs))
    (shard, up_columns), down_rows = shapes
    copies = []

    def copy(source, target):
        copies.append(pltpu.make_async_copy(source, target, semaphores.at[len(copies)]))

    for piece, (origin, other) in zip(pieces, which):
        owner = origin_ref[origin]
        lane = 1 - column_ref[0] if other else column_ref[0]
        rows = pl.ds(pl.multiple_of(owner * shard, 16), shard)
        if not other:
            copy(piece.at[0], targets[0].at[rows, :])
        ffn = piece if other else piece.at[1]
        copy(ffn.at[:, pl.ds(0, up_columns)], targets[1].at[rows, lanes_of(lane, up_columns)])
        for part, (start, count) in enumerate(down_parts(down_rows, shard)):
            source = ffn.at[pl.ds(0, count), pl.ds(up_columns + part * PAIR, PAIR)]
            target = pl.ds(pl.multiple_of(owner * down_rows + start, 16), count)
            copy(source, targets[2].at[target, lanes_of(lane, PAIR)])
    for one in copies:
        one.start()
    for one in copies:
        one.wait()


def place(origins, column, which, pieces, arrays, shapes):
    anywhere = pl.BlockSpec(memory_space=pl.ANY)
    (shard, up_columns), down_rows = shapes
    kinds = [
        (RING * shard, pieces[0].shape[-1]),
        (RING * shard, 2 * up_columns),
        (RING * down_rows, 2 * PAIR),
    ]
    held = [] if arrays is None else list(arrays)
    kept = (1, 2) if len(held) == 2 else (0, 1, 2)
    size = sum(math.prod(piece.shape) for piece in pieces)
    first = 2 + len(pieces)
    return pl.pallas_call(
        functools.partial(place_kernel, which, kept, shapes),
        grid_spec=pltpu.PrefetchScalarGridSpec(
            num_scalar_prefetch=2,
            grid=(1,),
            in_specs=[whole(piece.shape) for piece in pieces] + [anywhere] * len(held),
            out_specs=[anywhere] * len(kept),
            scratch_shapes=[pltpu.SemaphoreType.DMA((8 * len(pieces),))],
        ),
        out_shape=[jax.ShapeDtypeStruct(kinds[k], pieces[0].dtype) for k in kept],
        input_output_aliases={first + k: k for k in range(len(held))},
        compiler_params=pltpu.CompilerParams(vmem_limit_bytes=VMEM_BYTES),
        cost_estimate=pl.CostEstimate(flops=0, bytes_accessed=8 * size, transcendentals=0),
        name="place",
    )(origins, column, *pieces, *held)


def after(tensor, *others):
    return lax.optimization_barrier((tensor, *others))[0]


def core_way():
    return 1 - 2 * (lax.axis_index("dp") % 2)


def ring_origins():
    steps = jnp.array((0, -1, -2, -3, -4, 1, 2, 3), jnp.int32)
    return ring_member(ring_place(lax.axis_index("fsdp")) + steps + RING).astype(jnp.int32)


class RingSum:
    def __init__(self, mine, arrived):
        self.mine, self.arrived = mine, arrived
        place = ring_place(lax.axis_index("fsdp"))
        self.owners = [ring_member(place - core_way() * (s + 1) + 2 * RING) for s in range(RING)]
        self.totals = []

    def term(self):
        parts = []
        for own, arrived in zip(self.mine, self.arrived):
            rows = own.shape[0] // RING
            start = self.owners[len(self.totals)] * rows
            part = lax.dynamic_slice_in_dim(own, start, rows, 0).astype(wide)
            parts.append(part + lax.dynamic_slice_in_dim(arrived, start, rows, 0).astype(wide))
        return parts[0] if len(parts) == 1 else jnp.concatenate(parts, axis=0)

    def begin(self, *others):
        if others:
            self.mine = [after(self.mine[0], *others), *self.mine[1:]]
        self.totals.append(self.term().astype(low))

    def step(self, *before, arriving=()):
        total = self.totals[-1]
        moved = ring_next(after(total, *before) if before else total)
        moved = after(moved, *arriving) if arriving else moved
        self.totals.append((moved.astype(wide) + self.term().astype(wide)).astype(low))

    def last(self):
        return self.totals[-1]


def gather_rows(shard):
    mine = lax.all_gather(shard, "fsdp", axis=0, tiled=True)
    return mine, core_swap(mine)


def core_sum(mine, other):
    return (mine.astype(wide) + core_swap(other).astype(wide)).astype(low)


def scatter_rows(both):
    return lax.psum_scatter(both, "fsdp", scatter_dimension=0, tiled=True)


def over_columns(total):
    total = (total.astype(wide) + column_swap(total).astype(wide)).astype(low)
    return total, core_swap(total)


def on_device(
    inputs,
    cotangent,
    lengths,
    attention_weights,
    attention_momentum,
    attention_average,
    ffn_inputs,
    ffn_inputs_momentum,
    ffn_inputs_average,
    ffn_output,
    ffn_output_momentum,
    ffn_output_average,
    gains,
    gains_momentum,
    gains_average,
):
    micro_count, slot, width = inputs.shape
    hidden = ffn_inputs.shape[2]
    shard, down_rows = ffn_inputs.shape[1], ffn_output.shape[0]
    fsdp_size = lax.axis_size("fsdp")
    replicas = lax.axis_size("dp")
    ringed = fsdp_size == RING
    core = lax.axis_index("dp") % 2
    column = lax.axis_index("dp") // 2
    count = micro_count * slot
    half = width // 2
    core_ref = core.astype(jnp.int32).reshape(1)
    other_ref = 1 - core_ref
    column_ref = column.astype(jnp.int32).reshape(1)
    is_first = core == 0

    rows = inputs.reshape(count, width)
    positions = jnp.arange(slot, dtype=jnp.int32)
    valid = (positions[None, :] < lengths).astype(wide).reshape(count, 1)
    errors = (cotangent.reshape(count, width).astype(wide) * valid).astype(low)

    if ringed:
        origins = ring_origins()
        shapes = ((shard, hidden // 2), down_rows)
        packed = pack_all(
            core_ref, column_ref, attention_weights, ffn_inputs, ffn_output, gains
        )
        wholes, there, which_there = None, [], []
        here, which = [packed], [(0, False)]
        for step in range(1, 6):
            if step <= 3:
                onward = [ring_shift(here[0], 1), ring_shift(here[-1], -1)]
            elif step == 4:
                onward = [ring_next(jnp.where(is_first, *here))]
            across = [column_swap(piece[1]) for piece in here]
            wholes = place(
                origins, column_ref, which + which_there, here + there, wholes, shapes
            )
            if step == 5:
                break
            which_there = [(origin, True) for origin, _ in which]
            which = [(origin, False) for origin in [step, step + 4][: len(onward)]]
            extra = [errors, valid] if step == 2 else []
            tied = list(lax.optimization_barrier((*onward, *across, *wholes, *extra)))
            here, rest = tied[: len(onward)], tied[len(onward) :]
            there, wholes = rest[: len(across)], rest[len(across) : len(across) + 3]
        w_a = (wholes[0], core_swap(wholes[0]))
    else:
        w_a = gather_rows(pack_attention(core_ref, attention_weights, gains))
        w_gu = gather_rows(
            lax.dynamic_index_in_dim(ffn_inputs, core, 0, keepdims=False).astype(low)
        )
        w_d = gather_rows(lax.dynamic_slice_in_dim(ffn_output, core * half, half, 1).astype(low))
    mixed_mine, *kept_mine, gains8 = mixer_forward(core_ref, rows, w_a[0], slot)
    if ringed:
        across = list(lax.optimization_barrier((*across, mixed_mine, w_a[1]))[:1])
        last = place(origins, column_ref, [(4, True)], across, wholes[1:], shapes)
        wholes = [wholes[0], *last]
        rows = after(rows, *wholes[1:])
        w_gu, w_d = [(array, core_swap(array)) for array in wholes[1:]]
    mixed_other, *rest = mixer_forward(
        other_ref, rows, w_a[1], slot, (gains8, mixed_mine, w_a[0])
    )
    kept_other, (x1, h2, h2t, h1t) = rest[:4], rest[4:]
    owners = (fsdp_size, down_rows + shard, down_rows) if ringed else None
    gm, gu, gd_mine, gd_other, output, d_x1, d_mixed, go_mine, go_other = ffn(
        core_ref, h2, h2t, errors, w_gu, w_d, x1, (mixed_mine, mixed_other), w_a, valid, gains8, owners
    )

    mine_gu, arrived_gu = [gm], [core_swap(gu)]
    if ringed:
        mine_do, arrived_do = [gd_mine], [core_swap(gd_other)]
    else:
        mine_do, arrived_do = [gd_mine, go_mine], [core_swap(gd_other), core_swap(go_other)]
    backs = []
    for place_of in range(4):
        pair = place_of % 2
        from_half, kept = (other_ref, kept_other) if place_of < 2 else (core_ref, kept_mine)
        if ringed and place_of > 0:
            h1t = after(h1t, sum_gu.last(), sum_do.last())
        backs.append(
            mixer_backward(
                2 * from_half + pair,
                h1t,
                gains8,
                kept,
                d_mixed,
                pair,
                slot,
                shard,
                backs[-1][0] if pair else None,
            )
        )
        if ringed and place_of == 0:
            sum_gu, sum_do = RingSum(mine_gu, arrived_gu), RingSum(mine_do, arrived_do)
            sum_do.begin(backs[0][1])
            sum_gu.begin(backs[0][1])
        elif ringed:
            sum_do.step(arriving=(backs[-1][1],))
            sum_gu.step(arriving=(backs[-1][1],))
    grads, d_pre = [[back[which] for back in backs] for which in range(2)]
    by_owner = (fsdp_size * 2 * shard, 3 * PAIR)
    mine_qfv, arrived_qfv = [grads[3].reshape(by_owner)], [core_swap(grads[1].reshape(by_owner))]

    def finish_input(*others):
        last = after(d_pre[2], *others) if others else d_pre[2]
        return input_gradient(rows, gains8, [last, d_pre[3], *d_pre[:2]], w_a, d_x1)

    if ringed:
        sum_qfv = RingSum(mine_qfv, arrived_qfv)
        sum_qfv.begin()
        order = [sum_qfv]
        for ring in (sum_gu, sum_do) * 4:
            order += [ring, sum_qfv] if len(order) < 13 else [ring]
        results = []
        for at, ring in enumerate(order):
            before = [results[-3]] if at > 2 and ring is not sum_qfv else []
            if at == 7:
                before.append(input_grad)
            ring.step(*before)
            results.append(ring.last())
            if at == 2:
                input_grad = finish_input(results[0])
        total_gu, total_do, total_qfv = sum_gu.last(), sum_do.last(), sum_qfv.last()
    else:
        total_gu, total_do, total_qfv = [
            jnp.concatenate(
                [
                    scatter_rows((own.astype(wide) + there.astype(wide)).astype(low))
                    for own, there in zip(mine, arrived)
                ],
                axis=0,
            )
            for mine, arrived in (
                (mine_gu, arrived_gu),
                (mine_do, arrived_do),
                (mine_qfv, arrived_qfv),
            )
        ]
        input_grad = finish_input()
    sum_gu = over_columns(total_gu)
    sum_do = over_columns(total_do)

    scale_rows = 1.0 / math.sqrt(count * fsdp_size * replicas)
    attention_state = (attention_weights, attention_momentum, attention_average)
    ffn_in_state = (ffn_inputs, ffn_inputs_momentum, ffn_inputs_average)
    ffn_out_state = (ffn_output, ffn_output_momentum, ffn_output_average)
    *new_in, dots_two = update_ffn_in(core_ref, ffn_in_state, sum_gu, matrix_rate * scale_rows)
    *new_out, _ = update_ffn_out(core_ref, ffn_out_state, sum_do, matrix_rate * scale_rows)
    there = after(column_swap(total_qfv), new_in[0], new_out[0])
    sum_qfv = (total_qfv.astype(wide) + there.astype(wide)).astype(low)
    *own, dots_own = update_attention(
        core_ref, core_ref, attention_state, sum_qfv, sum_do[0], matrix_rate * scale_rows, ()
    )
    theirs = after(core_swap(sum_qfv), own[0])
    *new_attention, dots_theirs = update_attention(
        core_ref, other_ref, attention_state, theirs, sum_do[1], matrix_rate * scale_rows, own
    )
    dots = jnp.sum(dots_own + dots_theirs, axis=2)
    row_sums = jnp.stack([dots[0] + dots[1] + dots[2], dots[3], jnp.sum(dots_two, axis=(0, 2))])
    sum_gains = row_sums / gains.astype(low).astype(wide)
    return (
        output.reshape(micro_count, slot, width),
        input_grad.reshape(micro_count, slot, width),
        *new_attention,
        *new_in,
        *new_out,
        *update(gains, gains_momentum, gains_average, sum_gains, gain_rate * scale_rows),
    )


def solution(mesh):
    rows_split = P(None, ("fsdp", "dp"), None)
    middle_split = P(None, "fsdp", None)
    first_split = P("fsdp", None)
    gains_split = P(None, "fsdp")
    in_specs = (
        (rows_split, rows_split, P(None, ("fsdp", "dp")))
        + (middle_split,) * 6
        + (first_split,) * 3
        + (gains_split,) * 3
    )
    out_specs = (
        (rows_split, rows_split)
        + (middle_split,) * 6
        + (first_split,) * 3
        + (gains_split,) * 3
    )
    return jax.shard_map(
        on_device, mesh=mesh, in_specs=in_specs, out_specs=out_specs, check_vma=False
    )
```

```python
import functools
import math

import jax
import jax.numpy as jnp
from jax import lax
from jax.experimental import pallas as pl
from jax.experimental.pallas import tpu as pltpu
from jax.sharding import PartitionSpec as P

HEAD_DIM = 128
PAIR = 2 * HEAD_DIM
HEAD = 3 * HEAD_DIM

lower_bound = 0.9
momentum_decay = 0.9
average_decay = 0.7
weight_decay = 0.0005
matrix_rate = 0.03
gain_rate = 0.1
low = jnp.bfloat16
wide = jnp.float32
TILE_F = 256
VMEM_BYTES = 60 * 1024 * 1024


def mm(left, right):
    return jnp.dot(left, right, preferred_element_type=wide)


def mm_nt(left, right):
    return lax.dot_general(left, right, (((1,), (1,)), ((), ())), preferred_element_type=wide)


def mm_tn(left, right):
    return lax.dot_general(left, right, (((0,), (0,)), ((), ())), preferred_element_type=wide)


def sigmoid(u):
    return 0.5 * jnp.tanh(0.5 * u) + 0.5


def whole(shape):
    return pl.BlockSpec(shape, lambda *_: (0,) * len(shape), pipeline_mode=pl.Buffered(1))


def split_sum(ones_matrix, tensor):
    high = tensor.astype(low)
    rest = (tensor - high.astype(wide)).astype(low)
    return mm(ones_matrix, high) + mm(ones_matrix, rest)


def triangle(length, lower):
    rows = lax.broadcasted_iota(jnp.int32, (length, length), 0)
    columns = lax.broadcasted_iota(jnp.int32, (length, length), 1)
    kept = rows >= columns if lower else rows <= columns
    return kept.astype(wide).astype(low)


def decay_parts(f_pre, lower_ones):
    share = sigmoid(f_pre)
    gate = lower_bound + (1.0 - lower_bound) * share
    keys_in = (1.0 - lower_bound) * (1.0 - share)
    cumulative = split_sum(lower_ones, jnp.log(gate))
    middle_row = cumulative.shape[0] // 2
    cumulative = cumulative - cumulative[middle_row : middle_row + 1, :]
    return share, gate, keys_in, cumulative


def first_norm(x_ref, gain_row):
    rows = x_ref[...].astype(wide)
    scale = lax.rsqrt(jnp.mean(rows * rows, axis=-1, keepdims=True) + 1e-06)
    return rows * scale, scale


def lanes_of(half, size):
    return pl.ds(pl.multiple_of(half * size, size), size)


def mixer_forward_first_kernel(
    slot, half_ref, x_ref, w_ref, columns_ref, on_ref, q_ref, f_ref, v_ref, o_ref, g_ref, h_s
):
    @pl.when(pl.program_id(0) == 0)
    def _():
        g_ref[...] = columns_ref[...].astype(wide).T[: g_ref.shape[0], :]

    mixer_forward_kernel(
        slot, half_ref, x_ref, w_ref, g_ref, on_ref, q_ref, f_ref, v_ref, o_ref, h_s
    )


def mixer_forward_kernel(
    slot, half_ref, x_ref, w_ref, g_ref, on_ref, q_ref, f_ref, v_ref, o_ref, h_s
):
    @pl.when(pl.program_id(0) == 0)
    def _():
        normed, _ = first_norm(x_ref, None)
        h_s[...] = (normed * g_ref[0:1, :]).astype(low)

    gain_o = g_ref[1:2, lanes_of(half_ref[0] * pl.num_programs(0) + pl.program_id(0), PAIR)]
    pre = mm(h_s[...], w_ref[...])
    for head in range(2):
        lanes = slice(head * HEAD_DIM, (head + 1) * HEAD_DIM)
        start = head * HEAD
        q_ref[:, lanes] = pre[:, start : start + HEAD_DIM]
        f_ref[:, lanes] = pre[:, start + HEAD_DIM : start + 2 * HEAD_DIM]
        v_ref[:, lanes] = pre[:, start + 2 * HEAD_DIM : start + HEAD].astype(low)
    lower_ones = triangle(slot, True)
    block_rows = lax.broadcasted_iota(jnp.int32, (HEAD_DIM, HEAD_DIM), 0)
    block_columns = lax.broadcasted_iota(jnp.int32, (HEAD_DIM, HEAD_DIM), 1)
    causal = block_rows >= block_columns
    for sequence in range(x_ref.shape[0] // slot):
        rows = slice(sequence * slot, (sequence + 1) * slot)
        q_pre = q_ref[rows, :]
        _, _, keys_in, cumulative = decay_parts(f_ref[rows, :], lower_ones)
        grown = jnp.exp(-cumulative)
        decayed_q = (q_pre * sigmoid(q_pre) * jnp.exp(cumulative)).astype(low)
        grown_k = (keys_in * grown).astype(low)
        values = v_ref[rows, :]
        for head in range(2):
            lanes = slice(head * HEAD_DIM, (head + 1) * HEAD_DIM)
            for block in range(slot // HEAD_DIM):
                start, end = block * HEAD_DIM, (block + 1) * HEAD_DIM
                q_block = decayed_q[start:end, lanes]
                diagonal = mm_nt(q_block, grown_k[start:end, lanes])
                diagonal = jnp.where(causal, diagonal, 0.0).astype(low)
                out = mm(diagonal, values[start:end, lanes])
                if block > 0:
                    scores = mm_nt(q_block, grown_k[:start, lanes]).astype(low)
                    out = out + mm(scores, values[:start, lanes])
                scale = lax.rsqrt(jnp.mean(out * out, axis=-1, keepdims=True) + 1e-05)
                target = slice(sequence * slot + start, sequence * slot + end)
                o_ref[target, lanes] = out.astype(low)
                on_ref[target, lanes] = (out * scale * gain_o[:, lanes]).astype(low)


def mixer_forward_last_kernel(
    slot,
    half_ref,
    x_ref,
    w_ref,
    g_ref,
    before_ref,
    woo_ref,
    wom_ref,
    on_ref,
    q_ref,
    f_ref,
    v_ref,
    o_ref,
    x1_ref,
    h2_ref,
    h2t_ref,
    h1t_ref,
    h_s,
    on_s,
):
    step = pl.program_id(0)
    half = before_ref.shape[1]
    mixer_forward_kernel(
        slot, half_ref, x_ref, w_ref, g_ref, on_ref, q_ref, f_ref, v_ref, o_ref, h_s
    )
    on_s[:, lanes_of(half_ref[0] * pl.num_programs(0) + step, PAIR)] = on_ref[...]

    @pl.when(step == pl.num_programs(0) - 1)
    def _():
        here = lanes_of(half_ref[0], half)
        there = lanes_of(1 - half_ref[0], half)
        on_s[:, there] = before_ref[...]
        h1t_ref[...] = h_s[...].astype(wide).T.astype(low)
        x1_ref[:, here] = x_ref[:, here].astype(wide) + mm(on_s[...], woo_ref[...])
        x1_ref[:, there] = x_ref[:, there].astype(wide) + mm(on_s[...], wom_ref[...])
        x1 = x1_ref[...]
        scale = lax.rsqrt(jnp.mean(x1 * x1, axis=-1, keepdims=True) + 1e-06)
        normed = x1 * scale * g_ref[2:3, :]
        h2_ref[...] = normed.astype(low)
        h2t_ref[...] = normed.T.astype(low)


def mixer_forward(half, rows, weights, slot, ending=None):
    count, width = rows.shape
    pairs = width // PAIR // 2
    by_pair = pl.BlockSpec((count, PAIR), lambda j, _: (0, j))
    struct = jax.ShapeDtypeStruct
    shape = lambda kind: struct((count, width // 2), kind)
    in_specs = [whole(rows.shape), pl.BlockSpec((width, 3 * PAIR), lambda j, _: (0, j))]
    operands = [half, rows, weights]
    out_specs = [by_pair] * 5
    out_shape = [shape(low), shape(wide), shape(wide), shape(low), shape(low)]
    scratch = [pltpu.VMEM((count, width), low)]
    if ending is None:
        kernel = mixer_forward_first_kernel
        last = weights.shape[1] // HEAD_DIM - 1
        in_specs += [pl.BlockSpec((width, HEAD_DIM), lambda j, _: (0, last))]
        operands += [weights]
        out_specs += [whole((8, width))]
        out_shape += [struct((8, width), wide)]
    if ending is not None:
        kernel = mixer_forward_last_kernel
        out_weights = pl.BlockSpec((width, width // 2), lambda j, _: (0, 3))
        in_specs += [whole(ending[0].shape), whole((count, width // 2)), out_weights, out_weights]
        operands += [ending[0], ending[1], weights, ending[2]]
        out_specs += [whole((count, width))] * 2 + [whole((width, count))] * 2
        out_shape += [
            struct((count, width), wide),
            struct((count, width), low),
            struct((width, count), low),
            struct((width, count), low),
        ]
        scratch += [pltpu.VMEM((count, width), low)]
    return pl.pallas_call(
        functools.partial(kernel, slot),
        grid_spec=pltpu.PrefetchScalarGridSpec(
            num_scalar_prefetch=1,
            grid=(pairs,),
            in_specs=in_specs,
            out_specs=out_specs,
            scratch_shapes=scratch,
        ),
        out_shape=out_shape,
        compiler_params=pltpu.CompilerParams(vmem_limit_bytes=VMEM_BYTES),
        cost_estimate=pl.CostEstimate(
            flops=count * width * 4 * width + 10 * count * slot * width,
            bytes_accessed=count * width * 12 + width * width * 4,
            transcendentals=count * width * 3,
        ),
        name="mixer_forward",
    )(*operands)


def store_down(out_ref, tile, owners):
    if owners is None:
        out_ref[...] = tile
        return
    _, stride, down_rows = owners
    block = math.gcd(down_rows, tile.shape[0])
    first = pl.program_id(0) * (tile.shape[0] // block)
    for part in range(tile.shape[0] // block):
        owner = (first + part) // (down_rows // block)
        inside = (first + part) % (down_rows // block)
        start = pl.multiple_of(owner * stride + inside * block, block)
        out_ref[pl.ds(start, block), :] = tile[part * block : (part + 1) * block, :]


def ffn_tile(owners, core_ref, refs, grads, acc_ref, dh_ref, scratch):
    h_ref, ht_ref, e_ref, wm_ref, wu_ref, wdm_ref, wdo_ref = refs
    gm_ref, gu_ref, gdm_ref, gdo_ref = grads
    gu_w, down_w, gu_g, down_g = scratch
    half, tile = wdm_ref.shape[1], wm_ref.shape[1]
    mine, other = lanes_of(core_ref[0], half), lanes_of(1 - core_ref[0], half)
    kind, kind_other = lanes_of(core_ref[0], tile), lanes_of(1 - core_ref[0], tile)
    gu_w[:, kind] = wm_ref[...]
    gu_w[:, kind_other] = wu_ref[...]
    down_w[:, mine] = wdm_ref[...]
    down_w[:, other] = wdo_ref[...]
    pre = mm(h_ref[...], gu_w[...])
    a, b = pre[:, :tile], pre[:, tile:]
    share = sigmoid(a)
    swish = a * share
    mid = (swish * b).astype(low)
    d_mid = mm_nt(e_ref[...], down_w[...])
    down_g[...] = mm_tn(mid, e_ref[...]).astype(low)
    d_a = (d_mid * b * (share + swish * (1.0 - share))).astype(low)
    d_b = (d_mid * swish).astype(low)
    d_pre = jnp.concatenate([d_a, d_b], axis=1)
    acc_ref[...] += mm(mid, down_w[...])
    dh_ref[...] += mm_nt(d_pre, gu_w[...])
    gu_g[...] = mm(ht_ref[...], d_pre).astype(low)
    gm_ref[...] = gu_g[:, kind]
    gu_ref[...] = gu_g[:, kind_other]
    store_down(gdm_ref, down_g[:, mine], owners)
    store_down(gdo_ref, down_g[:, other], owners)


def ffn_kernel(
    owners,
    core_ref,
    h_ref,
    ht_ref,
    e_ref,
    wm_ref,
    wu_ref,
    wdm_ref,
    wdo_ref,
    x1_ref,
    onm_ref,
    ono_ref,
    wom_ref,
    woo_ref,
    m_ref,
    g_ref,
    gm_ref,
    gu_ref,
    gdm_ref,
    gdo_ref,
    out_ref,
    dh_s,
    don_ref,
    gom_ref,
    goo_ref,
    on_s,
    acc_s,
    *scratch,
):
    @pl.when(pl.program_id(0) == 0)
    def _():
        acc_s[...] = x1_ref[...]
        dh_s[...] = jnp.zeros_like(dh_s)

    grads = (gm_ref, gu_ref, gdm_ref, gdo_ref)
    refs = (h_ref, ht_ref, e_ref, wm_ref, wu_ref, wdm_ref, wdo_ref)
    ffn_tile(owners, core_ref, refs, grads, acc_s, dh_s, scratch)

    @pl.when(pl.program_id(0) == pl.num_programs(0) - 1)
    def _():
        half = onm_ref.shape[1]
        mine = lanes_of(core_ref[0], half)
        other = lanes_of(1 - core_ref[0], half)
        out_ref[...] = (acc_s[...] * m_ref[...]).astype(low)
        x1 = x1_ref[...]
        scale = lax.rsqrt(jnp.mean(x1 * x1, axis=-1, keepdims=True) + 1e-06)
        normed = x1 * scale
        d_h2 = dh_s[...]
        scaled = d_h2 * g_ref[2:3, :]
        d_x1 = e_ref[...].astype(wide) + scale * (
            scaled - normed * jnp.mean(scaled * normed, axis=-1, keepdims=True)
        )
        dh_s[...] = d_x1
        on_s[...] = d_x1.astype(low)
        d_mixed = mm_nt(on_s[:, mine], wom_ref[...]) + mm_nt(on_s[:, other], woo_ref[...])
        don_ref[...] = d_mixed.astype(low)
        for columns, g_down_ref, g_ref_o in ((mine, gdm_ref, gom_ref), (other, gdo_ref, goo_ref)):
            d_1 = on_s[:, columns]
            for which, on_ref in ((core_ref[0], onm_ref), (1 - core_ref[0], ono_ref)):
                grad_o = mm_tn(on_ref[...], d_1).astype(low)
                if owners is None:
                    g_ref_o[pl.ds(pl.multiple_of(which * half, half), half), :] = grad_o
                    continue
                count, stride, down_rows = owners
                rows = stride - down_rows
                for part in range(half // rows):
                    owner = which * (count // 2) + part
                    start = pl.multiple_of(owner * stride + down_rows, math.gcd(stride, down_rows))
                    g_down_ref[pl.ds(start, rows), :] = grad_o[part * rows : (part + 1) * rows, :]


def ffn(core, h2, h2t, errors, w_gu, w_d, x1, mixed, w_a, mask, gains8, owners):
    count, width = h2.shape
    half = width // 2
    hidden = w_gu[0].shape[1]
    full = whole((count, width))
    half_full = whole((count, half))
    square = whole((width, half))
    in_tile = pl.BlockSpec((width, TILE_F), lambda j, _: (0, j))
    out_tile = pl.BlockSpec((TILE_F, half), lambda j, _: (j, 0))
    out_weights = pl.BlockSpec((width, half), lambda j, _: (0, 3), pipeline_mode=pl.Buffered(1))
    down_spec, down_shape, out_spec, out_shape = out_tile, (hidden, half), square, (width, half)
    if owners is not None:
        down_shape, out_shape = (owners[0] * owners[1], half), (16, half)
        down_spec, out_spec = whole(down_shape), whole(out_shape)
    struct = jax.ShapeDtypeStruct
    return pl.pallas_call(
        functools.partial(ffn_kernel, owners),
        grid_spec=pltpu.PrefetchScalarGridSpec(
            num_scalar_prefetch=1,
            grid=(hidden // TILE_F,),
            in_specs=[full, whole(h2t.shape), full, in_tile, in_tile, out_tile, out_tile]
            + [full, half_full, half_full, out_weights, out_weights]
            + [whole((count, 1)), whole((8, width))],
            out_specs=[in_tile, in_tile, down_spec, down_spec]
            + [full, full, full, out_spec, out_spec],
            scratch_shapes=[
                pltpu.VMEM((count, width), low),
                pltpu.VMEM((count, width), wide),
                pltpu.VMEM((width, 2 * TILE_F), low),
                pltpu.VMEM((TILE_F, width), low),
                pltpu.VMEM((width, 2 * TILE_F), low),
                pltpu.VMEM((TILE_F, width), low),
            ],
        ),
        out_shape=[struct((width, hidden), low)] * 2
        + [struct(down_shape, low)] * 2
        + [
            struct((count, width), low),
            struct((count, width), wide),
            struct((count, width), low),
            struct(out_shape, low),
            struct(out_shape, low),
        ],
        compiler_params=pltpu.CompilerParams(vmem_limit_bytes=VMEM_BYTES),
        cost_estimate=pl.CostEstimate(
            flops=16 * count * width * hidden,
            bytes_accessed=count * width * 20 + width * hidden * 12,
            transcendentals=count * hidden,
        ),
        name="ffn",
    )(core, h2, h2t, errors, *w_gu, *w_d, x1, *mixed, *w_a, mask, gains8)


def mixer_backward_kernel(
    slot,
    head_ref,
    ht_ref,
    g_ref,
    q_ref,
    f_ref,
    v_ref,
    o_ref,
    don_ref,
    *outs,
):
    grad_ref, dpre_ref = outs[-2:]
    gain_o = g_ref[1:2, lanes_of(head_ref[0], HEAD_DIM)]
    lower_ones = triangle(slot, True)
    upper_ones = triangle(slot, False)
    block_rows = lax.broadcasted_iota(jnp.int32, (HEAD_DIM, HEAD_DIM), 0)
    block_columns = lax.broadcasted_iota(jnp.int32, (HEAD_DIM, HEAD_DIM), 1)
    causal = block_rows >= block_columns
    causal_t = block_rows <= block_columns
    blocks = slot // HEAD_DIM
    for sequence in range(q_ref.shape[0] // slot):
        rows = slice(sequence * slot, (sequence + 1) * slot)
        d_on = don_ref[rows, :].astype(wide)
        out = o_ref[rows, :].astype(wide)
        scale = lax.rsqrt(jnp.mean(out * out, axis=-1, keepdims=True) + 1e-05)
        normed = out * scale
        scaled = d_on * gain_o
        inner = jnp.mean(scaled * normed, axis=-1, keepdims=True)
        d_out = (scale * (scaled - normed * inner)).astype(low)

        q_pre = q_ref[rows, :]
        share, gate, keys_in, cumulative = decay_parts(f_ref[rows, :], lower_ones)
        grown = jnp.exp(-cumulative)
        shrunk = jnp.exp(cumulative)
        q_share = sigmoid(q_pre)
        q_h = (q_pre * q_share * shrunk).astype(low)
        k_h = (keys_in * grown).astype(low)
        v_h = v_ref[rows, :]
        dq_blocks, dk_blocks, dv_blocks = [], [], []
        for block in range(blocks):
            start, end = block * HEAD_DIM, (block + 1) * HEAD_DIM
            here = slice(start, end)
            d_scores = mm_nt(d_out[here], v_h[here])
            d_scores = jnp.where(causal, d_scores, 0.0).astype(low)
            d_q = mm(d_scores, k_h[here])
            if block > 0:
                before = slice(0, start)
                d_scores = mm_nt(d_out[here], v_h[before]).astype(low)
                d_q = d_q + mm(d_scores, k_h[before])
            dq_blocks.append(d_q)
            scores = jnp.where(causal_t, mm_nt(k_h[here], q_h[here]), 0.0).astype(low)
            d_scores = jnp.where(causal_t, mm_nt(v_h[here], d_out[here]), 0.0).astype(low)
            d_v = mm(scores, d_out[here])
            d_k = mm(d_scores, q_h[here])
            if block < blocks - 1:
                after_it = slice(end, slot)
                scores = mm_nt(k_h[here], q_h[after_it]).astype(low)
                d_scores = mm_nt(v_h[here], d_out[after_it]).astype(low)
                d_v = d_v + mm(scores, d_out[after_it])
                d_k = d_k + mm(d_scores, q_h[after_it])
            dk_blocks.append(d_k)
            dv_blocks.append(d_v)
        d_decayed = jnp.concatenate(dq_blocks, axis=0)
        d_grown = jnp.concatenate(dk_blocks, axis=0)
        d_value = jnp.concatenate(dv_blocks, axis=0)
        d_cumulative = q_h.astype(wide) * d_decayed - k_h.astype(wide) * d_grown
        d_log = split_sum(upper_ones, d_cumulative)
        d_query = d_decayed * shrunk
        d_key = d_grown * grown
        d_q_pre = d_query * q_share * (1.0 + q_pre * (1.0 - q_share))
        d_f_pre = (1.0 - lower_bound) * (d_log / gate - d_key) * share * (1.0 - share)
        dpre_ref[rows, :HEAD_DIM] = d_q_pre.astype(low)
        dpre_ref[rows, HEAD_DIM : 2 * HEAD_DIM] = d_f_pre.astype(low)
        dpre_ref[rows, 2 * HEAD_DIM :] = d_value.astype(low)

    grad = mm(ht_ref[...], dpre_ref[...]).astype(low)
    grad_ref[...] = grad.reshape(grad_ref.shape)


def mixer_backward(which, h1t, gains8, kept, d_mixed, head, slot, shard, before):
    width, count = h1t.shape
    heads = kept[0].shape[1] // HEAD_DIM
    by_head = pl.BlockSpec((count, HEAD_DIM), lambda j, _: (0, head))
    from_whole = pl.BlockSpec((count, HEAD_DIM), lambda j, which: (0, which[0]))
    struct = jax.ShapeDtypeStruct
    return pl.pallas_call(
        functools.partial(mixer_backward_kernel, slot),
        grid_spec=pltpu.PrefetchScalarGridSpec(
            num_scalar_prefetch=1,
            grid=(1,),
            in_specs=[whole((width, count)), whole(gains8.shape)]
            + [by_head] * 4
            + [from_whole]
            + [pl.BlockSpec(memory_space=pl.ANY)] * len(before),
            out_specs=[
                pl.BlockSpec((width // shard, 1, shard, HEAD), lambda j, _: (0, head, 0, 0)),
                pl.BlockSpec((count, HEAD), lambda j, _: (0, head)),
            ],
        ),
        out_shape=[
            struct((width // shard, heads, shard, HEAD), low),
            struct((count, heads * HEAD), low),
        ],
        input_output_aliases={8 + k: k for k in range(len(before))},
        compiler_params=pltpu.CompilerParams(vmem_limit_bytes=VMEM_BYTES),
        cost_estimate=pl.CostEstimate(
            flops=count * width * 3 * PAIR + 20 * count * slot * HEAD_DIM,
            bytes_accessed=count * width * 3 + width * PAIR * 3,
            transcendentals=count * HEAD_DIM * 6,
        ),
        name="mixer_backward",
    )(which, h1t, gains8, *kept, d_mixed, *before)


def input_gradient_rows_kernel(
    x_ref, g_ref, dm_ref, do_ref, wm_ref, wo_ref, dx1_ref, dx_ref
):
    d_h1 = mm_nt(dm_ref[...], wm_ref[...]) + mm_nt(do_ref[...], wo_ref[...])
    normed, scale = first_norm(x_ref, None)
    scaled = d_h1 * g_ref[0:1, :]
    dx_ref[...] = dx1_ref[...] + scale * (
        scaled - normed * jnp.mean(scaled * normed, axis=-1, keepdims=True)
    )


def input_gradient(rows, gains8, d_pre, weights, d_x1):
    count, width = rows.shape
    block = count // 2
    columns = d_pre[0].shape[1]
    by_rows = lambda columns: pl.BlockSpec((block, columns), lambda j: (j, 0))
    weight_spec = pl.BlockSpec((width, columns), lambda j: (0, 0), pipeline_mode=pl.Buffered(1))
    return pl.pallas_call(
        input_gradient_rows_kernel,
        grid=(count // block,),
        in_specs=[by_rows(width), whole(gains8.shape)]
        + [by_rows(columns)] * 2
        + [weight_spec] * 2
        + [by_rows(width)],
        out_specs=by_rows(width),
        out_shape=jax.ShapeDtypeStruct((count, width), wide),
        compiler_params=pltpu.CompilerParams(vmem_limit_bytes=VMEM_BYTES),
        cost_estimate=pl.CostEstimate(
            flops=6 * count * width * width,
            bytes_accessed=count * width * 16 + width * width * 6,
            transcendentals=0,
        ),
        name="input_gradient",
    )(rows, gains8, *d_pre, *weights, d_x1)


def update(weight, momentum, average, gradient, step_rate):
    new_momentum = momentum_decay * momentum + gradient
    direction = gradient + momentum_decay * new_momentum + weight_decay * weight
    new_weight = weight - step_rate * direction
    new_average = average_decay * average + (1.0 - average_decay) * new_weight
    return (new_momentum, new_average, new_weight)


def update_kernel(pick, step_rate, sum_count, core_ref, w_ref, m_ref, a_ref, *refs):
    sums, outs, dots_ref = refs[:sum_count], refs[-4:-1], refs[-1]
    weight = w_ref[...]
    gradient = pick(core_ref[0], *[s[...] for s in sums]).astype(wide).reshape(weight.shape)
    results = update(weight, m_ref[...], a_ref[...], gradient, step_rate)
    for out, result in zip(outs, results):
        out[...] = result
    product = weight.astype(low).astype(wide) * gradient
    total = product[..., :HEAD_DIM]
    for start in range(HEAD_DIM, product.shape[-1], HEAD_DIM):
        total = total + product[..., start : start + HEAD_DIM]
    dots_ref[...] = total.reshape(dots_ref.shape)


def update_call(
    core, state, sums, grid, state_spec, sum_specs, pick, step_rate, name, before=()
):
    struct = jax.ShapeDtypeStruct(state[0].shape, wide)
    size = math.prod(state[0].shape)
    rows = state_spec.block_shape[-2]
    steps = math.prod(grid)
    tail = grid[1:]

    def dots_index(*indices):
        place = indices[0]
        for length, index in zip(tail, indices[1:]):
            place = place * length + index
        return (place, 0, 0)

    return pl.pallas_call(
        functools.partial(update_kernel, pick, step_rate, len(sums)),
        grid_spec=pltpu.PrefetchScalarGridSpec(
            num_scalar_prefetch=1,
            grid=grid,
            in_specs=[state_spec] * 3
            + sum_specs
            + [pl.BlockSpec(memory_space=pl.ANY)] * len(before),
            out_specs=[state_spec] * 3 + [pl.BlockSpec((1, rows, HEAD_DIM), dots_index)],
        ),
        out_shape=[struct] * 3 + [jax.ShapeDtypeStruct((steps, rows, HEAD_DIM), wide)],
        input_output_aliases={4 + len(sums) + k: k for k in range(len(before))},
        compiler_params=pltpu.CompilerParams(vmem_limit_bytes=VMEM_BYTES),
        cost_estimate=pl.CostEstimate(flops=12 * size, bytes_accessed=26 * size, transcendentals=0),
        name=name,
    )(core, *state, *sums, *before)


def update_attention(core, half_ref, state, qfv, out, step_rate, before):
    _, shard, width = state[0].shape
    down_rows = out.shape[0] - shard

    def pick(core_index, proj, last):
        gradient = last[down_rows:].astype(wide)
        for kind in range(3):
            lanes = slice(kind * HEAD_DIM, (kind + 1) * HEAD_DIM)
            parts = [proj[start : start + shard, lanes] for start in range(0, proj.shape[0], shard)]
            chosen = jnp.concatenate(parts, axis=1).astype(wide)
            gradient = jnp.where(pl.program_id(0) == kind, chosen, gradient)
        return gradient

    return update_call(
        half_ref,
        state,
        (qfv, out),
        (4,),
        pl.BlockSpec((1, shard, width // 2), lambda kind, half: (kind, 0, half[0])),
        [whole(qfv.shape), whole(out.shape)],
        pick,
        step_rate,
        "update_attention",
        before,
    )


def update_ffn_in(kind_ref, state, total, step_rate, before):
    _, shard, hidden = state[0].shape
    tile = hidden // 2
    return update_call(
        kind_ref,
        state,
        (total,),
        (2,),
        pl.BlockSpec((1, shard, tile), lambda j, kind: (kind[0], 0, j)),
        [pl.BlockSpec((shard, tile), lambda j, _: (0, j))],
        lambda _, gradient: gradient,
        step_rate,
        "update_ffn_in",
        before,
    )


def update_ffn_out(core, state, sums, step_rate):
    shard, width = state[0].shape

    def pick(core_index, mine, other):
        own = pl.program_id(0) == core_index
        return jnp.where(own, mine[:shard].astype(wide), other[:shard].astype(wide))

    return update_call(
        core,
        state,
        sums,
        (2,),
        pl.BlockSpec((shard, width // 2), lambda j, _: (0, j)),
        [whole(total.shape) for total in sums],
        pick,
        step_rate,
        "update_ffn_out",
    )


def pack_kernel(core_ref, w_ref, g_ref, out_ref):
    half = w_ref.shape[2]
    for head in range(half // HEAD_DIM):
        for kind in range(3):
            start = head * HEAD + kind * HEAD_DIM
            piece = w_ref[kind, :, head * HEAD_DIM : (head + 1) * HEAD_DIM]
            out_ref[:, start : start + HEAD_DIM] = piece.astype(low)
    out_ref[:, 3 * half : 4 * half] = w_ref[3].astype(low)
    out_ref[:, 4 * half :] = g_ref[...].astype(low)


def pack_attention(core, weights, gains):
    _, shard, width = weights.shape
    half = width // 2
    gain_columns = jnp.pad(gains.T, ((0, 0), (0, HEAD_DIM - 3)))
    columns = 4 * half + HEAD_DIM
    return pl.pallas_call(
        pack_kernel,
        grid_spec=pltpu.PrefetchScalarGridSpec(
            num_scalar_prefetch=1,
            grid=(1,),
            in_specs=[
                pl.BlockSpec((4, shard, half), lambda j, core: (0, 0, core[0])),
                whole((shard, HEAD_DIM)),
            ],
            out_specs=whole((shard, columns)),
        ),
        out_shape=jax.ShapeDtypeStruct((shard, columns), low),
        name="pack_attention",
    )(core, weights, gain_columns)


RING = 8


def ring_place(index):
    return jnp.where(index % 2 == 0, index // 2, RING - 1 - index // 2)


def ring_member(place):
    place = place % RING
    return jnp.where(place < RING // 2, 2 * place, 2 * RING - 1 - 2 * place)


CYCLE = (0, 2, 4, 6, 7, 5, 3, 1)


def ring_next(tensor):
    replicas = lax.axis_size("dp")
    pairs = []
    for place_of, member in enumerate(CYCLE):
        for replica in range(replicas):
            target = CYCLE[(place_of + (1 if replica % 2 == 0 else -1)) % RING]
            pairs.append((member * replicas + replica, target * replicas + replica))
    return lax.ppermute(tensor, ("fsdp", "dp"), pairs)


def ring_shift(tensor, way):
    pairs = [(member, CYCLE[(at + way) % RING]) for at, member in enumerate(CYCLE)]
    return lax.ppermute(tensor, "fsdp", pairs)


def core_swap(tensor):
    return lax.ppermute(tensor, "dp", [(d, d ^ 1) for d in range(lax.axis_size("dp"))])


def column_swap(tensor):
    return lax.ppermute(tensor, "dp", [(d, d ^ 2) for d in range(lax.axis_size("dp"))])


def pack_all_kernel(core_ref, column_ref, w_ref, up_ref, down_ref, g_ref, out_ref):
    shard = w_ref.shape[1]
    half = w_ref.shape[2]
    for head in range(half // HEAD_DIM):
        for kind in range(3):
            start = head * HEAD + kind * HEAD_DIM
            piece = w_ref[kind, :, head * HEAD_DIM : (head + 1) * HEAD_DIM]
            out_ref[0, :, start : start + HEAD_DIM] = piece.astype(low)
    out_ref[0, :, 3 * half : 4 * half] = w_ref[3].astype(low)
    start = 4 * half
    rows = lax.broadcasted_iota(jnp.int32, (HEAD_DIM, shard), 0)
    gains = jnp.where(rows == 0, g_ref[0:1, :], jnp.where(rows == 1, g_ref[1:2, :], g_ref[2:3, :]))
    out_ref[0, :, start:] = jnp.where(rows < 3, gains, 0.0).T.astype(low)
    up_columns = up_ref.shape[2]
    out_ref[1, :, :up_columns] = up_ref[0].astype(low)
    for part, (start, count) in enumerate(down_parts(down_ref.shape[0], shard)):
        lanes = slice(up_columns + part * PAIR, up_columns + (part + 1) * PAIR)
        out_ref[1, :count, lanes] = down_ref[start : start + count, :].astype(low)
        if count < shard:
            out_ref[1, count:, lanes] = jnp.zeros((shard - count, PAIR), low)


def down_parts(down_rows, shard):
    return [(start, min(shard, down_rows - start)) for start in range(0, down_rows, shard)]


def pack_all(core, column, weights, up, down, gains):
    _, shard, width = weights.shape
    half = width // 2
    columns = 4 * half + HEAD_DIM
    return pl.pallas_call(
        pack_all_kernel,
        grid_spec=pltpu.PrefetchScalarGridSpec(
            num_scalar_prefetch=2,
            grid=(1,),
            in_specs=[
                pl.BlockSpec((4, shard, half), lambda j, core, column: (0, 0, core[0])),
                pl.BlockSpec(
                    (1, shard, up.shape[2] // 2), lambda j, core, column: (core[0], 0, column[0])
                ),
                pl.BlockSpec(
                    (down.shape[0], PAIR), lambda j, core, column: (0, 2 * core[0] + column[0])
                ),
                whole(gains.shape),
            ],
            out_specs=whole((2, shard, columns)),
        ),
        out_shape=jax.ShapeDtypeStruct((2, shard, columns), low),
        compiler_params=pltpu.CompilerParams(vmem_limit_bytes=VMEM_BYTES),
        name="pack_all",
    )(core, column, weights, up, down, gains)


def place_kernel(which, kept, shapes, origin_ref, column_ref, *refs):
    pieces, outs, semaphores = refs[: len(which)], refs[-1 - len(kept) : -1], refs[-1]
    targets = dict(zip(kept, outs))
    (shard, up_columns), down_rows = shapes
    copies = []

    def copy(source, target):
        copies.append(pltpu.make_async_copy(source, target, semaphores.at[len(copies)]))

    for piece, (origin, other) in zip(pieces, which):
        owner = origin_ref[origin]
        lane = 1 - column_ref[0] if other else column_ref[0]
        rows = pl.ds(pl.multiple_of(owner * shard, 16), shard)
        if not other:
            copy(piece.at[0], targets[0].at[rows, :])
        ffn = piece if other else piece.at[1]
        copy(ffn.at[:, pl.ds(0, up_columns)], targets[1].at[rows, lanes_of(lane, up_columns)])
        for part, (start, count) in enumerate(down_parts(down_rows, shard)):
            source = ffn.at[pl.ds(0, count), pl.ds(up_columns + part * PAIR, PAIR)]
            target = pl.ds(pl.multiple_of(owner * down_rows + start, 16), count)
            copy(source, targets[2].at[target, lanes_of(lane, PAIR)])
    for one in copies:
        one.start()
    for one in copies:
        one.wait()


def place(origins, column, which, pieces, arrays, shapes):
    anywhere = pl.BlockSpec(memory_space=pl.ANY)
    (shard, up_columns), down_rows = shapes
    kinds = [
        (RING * shard, pieces[0].shape[-1]),
        (RING * shard, 2 * up_columns),
        (RING * down_rows, 2 * PAIR),
    ]
    held = [] if arrays is None else list(arrays)
    kept = (1, 2) if len(held) == 2 else (0, 1, 2)
    size = sum(math.prod(piece.shape) for piece in pieces)
    first = 2 + len(pieces)
    return pl.pallas_call(
        functools.partial(place_kernel, which, kept, shapes),
        grid_spec=pltpu.PrefetchScalarGridSpec(
            num_scalar_prefetch=2,
            grid=(1,),
            in_specs=[whole(piece.shape) for piece in pieces] + [anywhere] * len(held),
            out_specs=[anywhere] * len(kept),
            scratch_shapes=[pltpu.SemaphoreType.DMA((8 * len(pieces),))],
        ),
        out_shape=[jax.ShapeDtypeStruct(kinds[k], pieces[0].dtype) for k in kept],
        input_output_aliases={first + k: k for k in range(len(held))},
        compiler_params=pltpu.CompilerParams(vmem_limit_bytes=VMEM_BYTES),
        cost_estimate=pl.CostEstimate(flops=0, bytes_accessed=8 * size, transcendentals=0),
        name="place",
    )(origins, column, *pieces, *held)


def after(tensor, *others):
    return lax.optimization_barrier((tensor, *others))[0]


def core_way():
    return 1 - 2 * (lax.axis_index("dp") % 2)


def ring_origins():
    steps = jnp.array((0, -1, -2, -3, -4, 1, 2, 3), jnp.int32)
    return ring_member(ring_place(lax.axis_index("fsdp")) + steps + RING).astype(jnp.int32)


class RingSum:
    def __init__(self, mine, arrived):
        self.mine, self.arrived = mine, arrived
        place = ring_place(lax.axis_index("fsdp"))
        self.owners = [ring_member(place - core_way() * (s + 1) + 2 * RING) for s in range(RING)]
        self.totals = []

    def term(self):
        parts = []
        for own, arrived in zip(self.mine, self.arrived):
            rows = own.shape[0] // RING
            start = self.owners[len(self.totals)] * rows
            part = lax.dynamic_slice_in_dim(own, start, rows, 0).astype(wide)
            parts.append(part + lax.dynamic_slice_in_dim(arrived, start, rows, 0).astype(wide))
        return parts[0] if len(parts) == 1 else jnp.concatenate(parts, axis=0)

    def begin(self, *others):
        if others:
            self.mine = [after(self.mine[0], *others), *self.mine[1:]]
        self.totals.append(self.term().astype(low))

    def step(self, *before, arriving=()):
        total = self.totals[-1]
        moved = ring_next(after(total, *before) if before else total)
        moved = after(moved, *arriving) if arriving else moved
        self.totals.append((moved.astype(wide) + self.term().astype(wide)).astype(low))

    def last(self):
        return self.totals[-1]


def gather_rows(shard):
    mine = lax.all_gather(shard, "fsdp", axis=0, tiled=True)
    return mine, core_swap(mine)


def core_sum(mine, other):
    return (mine.astype(wide) + core_swap(other).astype(wide)).astype(low)


def scatter_rows(both):
    return lax.psum_scatter(both, "fsdp", scatter_dimension=0, tiled=True)


def over_columns(total):
    total = (total.astype(wide) + column_swap(total).astype(wide)).astype(low)
    return total, core_swap(total)


def on_device(
    inputs,
    cotangent,
    lengths,
    attention_weights,
    attention_momentum,
    attention_average,
    ffn_inputs,
    ffn_inputs_momentum,
    ffn_inputs_average,
    ffn_output,
    ffn_output_momentum,
    ffn_output_average,
    gains,
    gains_momentum,
    gains_average,
):
    micro_count, slot, width = inputs.shape
    hidden = ffn_inputs.shape[2]
    shard, down_rows = ffn_inputs.shape[1], ffn_output.shape[0]
    fsdp_size = lax.axis_size("fsdp")
    replicas = lax.axis_size("dp")
    ringed = fsdp_size == RING
    core = lax.axis_index("dp") % 2
    column = lax.axis_index("dp") // 2
    count = micro_count * slot
    half = width // 2
    core_ref = core.astype(jnp.int32).reshape(1)
    other_ref = 1 - core_ref
    column_ref = column.astype(jnp.int32).reshape(1)
    is_first = core == 0

    rows = inputs.reshape(count, width)
    positions = jnp.arange(slot, dtype=jnp.int32)
    valid = (positions[None, :] < lengths).astype(wide).reshape(count, 1)
    errors = (cotangent.reshape(count, width).astype(wide) * valid).astype(low)

    if ringed:
        origins = ring_origins()
        shapes = ((shard, hidden // 2), down_rows)
        packed = pack_all(
            core_ref, column_ref, attention_weights, ffn_inputs, ffn_output, gains
        )
        wholes, there, which_there = None, [], []
        here, which = [packed], [(0, False)]
        for step in range(1, 6):
            if step <= 3:
                onward = [ring_shift(here[0], 1), ring_shift(here[-1], -1)]
            elif step == 4:
                onward = [ring_next(jnp.where(is_first, *here))]
            across = [column_swap(piece[1]) for piece in here]
            wholes = place(
                origins, column_ref, which + which_there, here + there, wholes, shapes
            )
            if step == 5:
                break
            which_there = [(origin, True) for origin, _ in which]
            which = [(origin, False) for origin in [step, step + 4][: len(onward)]]
            extra = [errors, valid] if step == 2 else []
            if step == 4:
                late, across = across[1], across[:1]
                late_which, which_there = which_there[1:], which_there[:1]
            tied = list(lax.optimization_barrier((*onward, *across, *wholes, *extra)))
            here, rest = tied[: len(onward)], tied[len(onward) :]
            there, wholes = rest[: len(across)], rest[len(across) : len(across) + 3]
        w_a = (wholes[0], core_swap(wholes[0]))
    else:
        w_a = gather_rows(pack_attention(core_ref, attention_weights, gains))
        w_gu = gather_rows(
            lax.dynamic_index_in_dim(ffn_inputs, core, 0, keepdims=False).astype(low)
        )
        w_d = gather_rows(lax.dynamic_slice_in_dim(ffn_output, core * half, half, 1).astype(low))
    mixed_mine, *kept_mine, gains8 = mixer_forward(core_ref, rows, w_a[0], slot)
    if ringed:
        across = list(lax.optimization_barrier((late, *across, mixed_mine, w_a[1]))[:2])
        last = place(
            origins, column_ref, late_which + [(4, True)], across, wholes[1:], shapes
        )
        wholes = [wholes[0], *last]
        rows = after(rows, *wholes[1:])
        w_gu, w_d = [(array, core_swap(array)) for array in wholes[1:]]
    mixed_other, *rest = mixer_forward(
        other_ref, rows, w_a[1], slot, (gains8, mixed_mine, w_a[0])
    )
    kept_other, (x1, h2, h2t, h1t) = rest[:4], rest[4:]
    owners = (fsdp_size, down_rows + shard, down_rows) if ringed else None
    gm, gu, gd_mine, gd_other, output, d_x1, d_mixed, go_mine, go_other = ffn(
        core_ref, h2, h2t, errors, w_gu, w_d, x1, (mixed_mine, mixed_other), w_a, valid, gains8, owners
    )

    mine_gu, arrived_gu = [gm], [core_swap(gu)]
    if ringed:
        mine_do, arrived_do = [gd_mine], [core_swap(gd_other)]
    else:
        mine_do, arrived_do = [gd_mine, go_mine], [core_swap(gd_other), core_swap(go_other)]
    backs = []
    heads = half // HEAD_DIM
    for place_of in range(2 * heads):
        head = place_of % heads
        from_half, kept = (other_ref, kept_other) if place_of < heads else (core_ref, kept_mine)
        if ringed and place_of > 1:
            h1t = after(h1t, sum_gu.last(), sum_do.last())
        backs.append(
            mixer_backward(
                heads * from_half + head,
                h1t,
                gains8,
                kept,
                d_mixed,
                head,
                slot,
                shard,
                backs[-1] if head else (),
            )
        )
        if ringed and place_of == 1:
            sum_gu, sum_do = RingSum(mine_gu, arrived_gu), RingSum(mine_do, arrived_do)
            sum_do.begin(backs[-1][1])
            sum_gu.begin(backs[-1][1])
        elif ringed and place_of > 1:
            sum_do.step(arriving=(backs[-1][1],))
            sum_gu.step(arriving=(backs[-1][1],))
    d_pre = [backs[-1][1], backs[heads - 1][1]]
    by_owner = (fsdp_size * heads * shard, HEAD)
    mine_qfv = [backs[-1][0].reshape(by_owner)]
    arrived_qfv = [core_swap(backs[heads - 1][0].reshape(by_owner))]

    if ringed:
        sum_qfv = RingSum(mine_qfv, arrived_qfv)
        sum_qfv.begin()
        sum_qfv.step()
        while len(sum_gu.totals) < RING:
            sum_do.step()
            sum_gu.step()
        total_gu, total_do = sum_gu.last(), sum_do.last()
    else:
        total_gu, total_do, total_qfv = [
            jnp.concatenate(
                [
                    scatter_rows((own.astype(wide) + there.astype(wide)).astype(low))
                    for own, there in zip(mine, arrived)
                ],
                axis=0,
            )
            for mine, arrived in (
                (mine_gu, arrived_gu),
                (mine_do, arrived_do),
                (mine_qfv, arrived_qfv),
            )
        ]
    scale_rows = 1.0 / math.sqrt(count * fsdp_size * replicas)
    matrix_step = matrix_rate * scale_rows
    attention_state = (attention_weights, attention_momentum, attention_average)
    ffn_in_state = (ffn_inputs, ffn_inputs_momentum, ffn_inputs_average)
    ffn_out_state = (ffn_output, ffn_output_momentum, ffn_output_average)
    sum_do = over_columns(total_do)
    sum_gu = over_columns(total_gu)
    *new_out, _ = update_ffn_out(core_ref, ffn_out_state, sum_do, matrix_step)
    *new_in, dots_up = update_ffn_in(core_ref, ffn_in_state, sum_gu[0], matrix_step, ())
    *new_in, dots_gate = update_ffn_in(other_ref, ffn_in_state, sum_gu[1], matrix_step, new_in)
    if ringed:
        for beside in ([], [], [new_out[0]], [dots_up], [dots_gate], []):
            sum_qfv.step(*beside)
        total_qfv = sum_qfv.last()
    input_grad = input_gradient(rows, gains8, (after(d_pre[0], total_qfv), d_pre[1]), w_a, d_x1)
    there = after(column_swap(total_qfv), input_grad)
    sum_qfv = (total_qfv.astype(wide) + there.astype(wide)).astype(low)
    *own, dots_own = update_attention(
        core_ref, core_ref, attention_state, sum_qfv, sum_do[0], matrix_step, ()
    )
    theirs = after(core_swap(sum_qfv), own[0])
    *new_attention, dots_theirs = update_attention(
        core_ref, other_ref, attention_state, theirs, sum_do[1], matrix_step, own
    )
    dots = jnp.sum(dots_own + dots_theirs, axis=2)
    row_sums = jnp.stack([dots[0] + dots[1] + dots[2], dots[3], jnp.sum(dots_up + dots_gate, axis=(0, 2))])
    sum_gains = row_sums / gains.astype(low).astype(wide)
    return (
        output.reshape(micro_count, slot, width),
        input_grad.reshape(micro_count, slot, width),
        *new_attention,
        *new_in,
        *new_out,
        *update(gains, gains_momentum, gains_average, sum_gains, gain_rate * scale_rows),
    )


def solution(mesh):
    rows_split = P(None, ("fsdp", "dp"), None)
    middle_split = P(None, "fsdp", None)
    first_split = P("fsdp", None)
    gains_split = P(None, "fsdp")
    in_specs = (
        (rows_split, rows_split, P(None, ("fsdp", "dp")))
        + (middle_split,) * 6
        + (first_split,) * 3
        + (gains_split,) * 3
    )
    out_specs = (
        (rows_split, rows_split)
        + (middle_split,) * 6
        + (first_split,) * 3
        + (gains_split,) * 3
    )
    return jax.shard_map(
        on_device, mesh=mesh, in_specs=in_specs, out_specs=out_specs, check_vma=False
    )
```

```python
import functools
import math

import jax
import jax.numpy as jnp
from jax import lax
from jax.experimental import pallas as pl
from jax.experimental.pallas import tpu as pltpu
from jax.sharding import PartitionSpec as P

HEAD_DIM = 128
PAIR = 2 * HEAD_DIM

lower_bound = 0.9
momentum_decay = 0.9
average_decay = 0.7
weight_decay = 0.0005
matrix_rate = 0.03
gain_rate = 0.1
low = jnp.bfloat16
wide = jnp.float32
TILE_F = 256
VMEM_BYTES = 60 * 1024 * 1024


def mm(left, right):
    return jnp.dot(left, right, preferred_element_type=wide)


def mm_nt(left, right):
    return lax.dot_general(left, right, (((1,), (1,)), ((), ())), preferred_element_type=wide)


def mm_tn(left, right):
    return lax.dot_general(left, right, (((0,), (0,)), ((), ())), preferred_element_type=wide)


def sigmoid(u):
    return 0.5 * jnp.tanh(0.5 * u) + 0.5


def whole(shape):
    return pl.BlockSpec(shape, lambda *_: (0,) * len(shape), pipeline_mode=pl.Buffered(1))


def split_sum(ones_matrix, tensor):
    high = tensor.astype(low)
    rest = (tensor - high.astype(wide)).astype(low)
    return mm(ones_matrix, high) + mm(ones_matrix, rest)


def triangle(length, lower):
    rows = lax.broadcasted_iota(jnp.int32, (length, length), 0)
    columns = lax.broadcasted_iota(jnp.int32, (length, length), 1)
    kept = rows >= columns if lower else rows <= columns
    return kept.astype(wide).astype(low)


def decay_parts(f_pre, lower_ones):
    share = sigmoid(f_pre)
    gate = lower_bound + (1.0 - lower_bound) * share
    keys_in = (1.0 - lower_bound) * (1.0 - share)
    cumulative = split_sum(lower_ones, jnp.log(gate))
    middle_row = cumulative.shape[0] // 2
    cumulative = cumulative - cumulative[middle_row : middle_row + 1, :]
    return share, gate, keys_in, cumulative


def first_norm(x_ref, gain_row):
    rows = x_ref[...].astype(wide)
    scale = lax.rsqrt(jnp.mean(rows * rows, axis=-1, keepdims=True) + 1e-06)
    return rows * scale, scale


def lanes_of(half, size):
    return pl.ds(pl.multiple_of(half * size, size), size)


def mixer_forward_first_kernel(
    slot, half_ref, x_ref, w_ref, columns_ref, on_ref, q_ref, f_ref, v_ref, o_ref, g_ref, h_s
):
    @pl.when(pl.program_id(0) == 0)
    def _():
        g_ref[...] = columns_ref[...].astype(wide).T[: g_ref.shape[0], :]

    mixer_forward_kernel(
        slot, half_ref, x_ref, w_ref, g_ref, on_ref, q_ref, f_ref, v_ref, o_ref, h_s
    )


def mixer_forward_kernel(
    slot, half_ref, x_ref, w_ref, g_ref, on_ref, q_ref, f_ref, v_ref, o_ref, h_s
):
    @pl.when(pl.program_id(0) == 0)
    def _():
        normed, _ = first_norm(x_ref, None)
        h_s[...] = (normed * g_ref[0:1, :]).astype(low)

    gain_o = g_ref[1:2, lanes_of(half_ref[0] * pl.num_programs(0) + pl.program_id(0), PAIR)]
    pre = mm(h_s[...], w_ref[...])
    q_ref[...] = pre[:, :PAIR]
    f_ref[...] = pre[:, PAIR : 2 * PAIR]
    v_ref[...] = pre[:, 2 * PAIR :].astype(low)
    lower_ones = triangle(slot, True)
    block_rows = lax.broadcasted_iota(jnp.int32, (HEAD_DIM, HEAD_DIM), 0)
    block_columns = lax.broadcasted_iota(jnp.int32, (HEAD_DIM, HEAD_DIM), 1)
    causal = block_rows >= block_columns
    for sequence in range(x_ref.shape[0] // slot):
        rows = slice(sequence * slot, (sequence + 1) * slot)
        q_pre = q_ref[rows, :]
        _, _, keys_in, cumulative = decay_parts(f_ref[rows, :], lower_ones)
        grown = jnp.exp(-cumulative)
        decayed_q = (q_pre * sigmoid(q_pre) * jnp.exp(cumulative)).astype(low)
        grown_k = (keys_in * grown).astype(low)
        values = v_ref[rows, :]
        for head in range(2):
            lanes = slice(head * HEAD_DIM, (head + 1) * HEAD_DIM)
            for block in range(slot // HEAD_DIM):
                start, end = block * HEAD_DIM, (block + 1) * HEAD_DIM
                q_block = decayed_q[start:end, lanes]
                diagonal = mm_nt(q_block, grown_k[start:end, lanes])
                diagonal = jnp.where(causal, diagonal, 0.0).astype(low)
                out = mm(diagonal, values[start:end, lanes])
                if block > 0:
                    scores = mm_nt(q_block, grown_k[:start, lanes]).astype(low)
                    out = out + mm(scores, values[:start, lanes])
                scale = lax.rsqrt(jnp.mean(out * out, axis=-1, keepdims=True) + 1e-05)
                target = slice(sequence * slot + start, sequence * slot + end)
                o_ref[target, lanes] = out.astype(low)
                on_ref[target, lanes] = (out * scale * gain_o[:, lanes]).astype(low)


def mixer_forward_last_kernel(
    slot,
    half_ref,
    x_ref,
    w_ref,
    g_ref,
    before_ref,
    woo_ref,
    wom_ref,
    on_ref,
    q_ref,
    f_ref,
    v_ref,
    o_ref,
    x1_ref,
    h2_ref,
    h2t_ref,
    h1t_ref,
    h_s,
    on_s,
):
    step = pl.program_id(0)
    half = before_ref.shape[1]
    mixer_forward_kernel(
        slot, half_ref, x_ref, w_ref, g_ref, on_ref, q_ref, f_ref, v_ref, o_ref, h_s
    )
    on_s[:, lanes_of(half_ref[0] * pl.num_programs(0) + step, PAIR)] = on_ref[...]

    @pl.when(step == pl.num_programs(0) - 1)
    def _():
        here = lanes_of(half_ref[0], half)
        there = lanes_of(1 - half_ref[0], half)
        on_s[:, there] = before_ref[...]
        h1t_ref[...] = h_s[...].astype(wide).T.astype(low)
        x1_ref[:, here] = x_ref[:, here].astype(wide) + mm(on_s[...], woo_ref[...])
        x1_ref[:, there] = x_ref[:, there].astype(wide) + mm(on_s[...], wom_ref[...])
        x1 = x1_ref[...]
        scale = lax.rsqrt(jnp.mean(x1 * x1, axis=-1, keepdims=True) + 1e-06)
        normed = x1 * scale * g_ref[2:3, :]
        h2_ref[...] = normed.astype(low)
        h2t_ref[...] = normed.T.astype(low)


def mixer_forward(half, rows, weights, slot, ending=None):
    count, width = rows.shape
    pairs = width // PAIR // 2
    by_pair = pl.BlockSpec((count, PAIR), lambda j, _: (0, j))
    struct = jax.ShapeDtypeStruct
    shape = lambda kind: struct((count, width // 2), kind)
    in_specs = [whole(rows.shape), pl.BlockSpec((width, 3 * PAIR), lambda j, _: (0, j))]
    operands = [half, rows, weights]
    out_specs = [by_pair] * 5
    out_shape = [shape(low), shape(wide), shape(wide), shape(low), shape(low)]
    scratch = [pltpu.VMEM((count, width), low)]
    if ending is None:
        kernel = mixer_forward_first_kernel
        last = weights.shape[1] // HEAD_DIM - 1
        in_specs += [pl.BlockSpec((width, HEAD_DIM), lambda j, _: (0, last))]
        operands += [weights]
        out_specs += [whole((8, width))]
        out_shape += [struct((8, width), wide)]
    if ending is not None:
        kernel = mixer_forward_last_kernel
        out_weights = pl.BlockSpec((width, width // 2), lambda j, _: (0, 3))
        in_specs += [whole(ending[0].shape), whole((count, width // 2)), out_weights, out_weights]
        operands += [ending[0], ending[1], weights, ending[2]]
        out_specs += [whole((count, width))] * 2 + [whole((width, count))] * 2
        out_shape += [
            struct((count, width), wide),
            struct((count, width), low),
            struct((width, count), low),
            struct((width, count), low),
        ]
        scratch += [pltpu.VMEM((count, width), low)]
    return pl.pallas_call(
        functools.partial(kernel, slot),
        grid_spec=pltpu.PrefetchScalarGridSpec(
            num_scalar_prefetch=1,
            grid=(pairs,),
            in_specs=in_specs,
            out_specs=out_specs,
            scratch_shapes=scratch,
        ),
        out_shape=out_shape,
        compiler_params=pltpu.CompilerParams(vmem_limit_bytes=VMEM_BYTES),
        cost_estimate=pl.CostEstimate(
            flops=count * width * 4 * width + 10 * count * slot * width,
            bytes_accessed=count * width * 12 + width * width * 4,
            transcendentals=count * width * 3,
        ),
        name="mixer_forward",
    )(*operands)


def store_down(out_ref, tile, owners):
    if owners is None:
        out_ref[...] = tile
        return
    _, stride, down_rows = owners
    block = math.gcd(down_rows, tile.shape[0])
    first = pl.program_id(0) * (tile.shape[0] // block)
    for part in range(tile.shape[0] // block):
        owner = (first + part) // (down_rows // block)
        inside = (first + part) % (down_rows // block)
        start = pl.multiple_of(owner * stride + inside * block, block)
        out_ref[pl.ds(start, block), :] = tile[part * block : (part + 1) * block, :]


def ffn_tile(owners, core_ref, refs, grads, acc_ref, dh_ref, scratch):
    h_ref, ht_ref, e_ref, wm_ref, wu_ref, wdm_ref, wdo_ref = refs
    g_here, g_there, gdm_ref, gdo_ref = grads
    gu_w, down_w, gu_g, down_g = scratch
    half, tile = wdm_ref.shape[1], wm_ref.shape[1]
    mine, other = lanes_of(core_ref[0], half), lanes_of(1 - core_ref[0], half)
    kind, kind_other = lanes_of(core_ref[0], tile), lanes_of(1 - core_ref[0], tile)
    gu_w[:, kind] = wm_ref[...]
    gu_w[:, kind_other] = wu_ref[...]
    down_w[:, mine] = wdm_ref[...]
    down_w[:, other] = wdo_ref[...]
    pre = mm(h_ref[...], gu_w[...])
    a, b = pre[:, :tile], pre[:, tile:]
    share = sigmoid(a)
    swish = a * share
    mid = (swish * b).astype(low)
    d_mid = mm_nt(e_ref[...], down_w[...])
    down_g[...] = mm_tn(mid, e_ref[...]).astype(low)
    d_a = (d_mid * b * (share + swish * (1.0 - share))).astype(low)
    d_b = (d_mid * swish).astype(low)
    d_pre = jnp.concatenate([d_a, d_b], axis=1)
    acc_ref[...] += mm(mid, down_w[...])
    dh_ref[...] += mm_nt(d_pre, gu_w[...])
    gu_g[...] = mm(ht_ref[...], d_pre).astype(low)
    blocks = tile // HEAD_DIM
    for refs_of, block in ((g_here, core_ref[1]), (g_there, 1 - core_ref[1])):
        refs_of[0][...] = gu_g[:, lanes_of(core_ref[0] * blocks + block, HEAD_DIM)]
        refs_of[1][...] = gu_g[:, lanes_of((1 - core_ref[0]) * blocks + block, HEAD_DIM)]
    store_down(gdm_ref, down_g[:, mine], owners)
    store_down(gdo_ref, down_g[:, other], owners)


def ffn_kernel(
    owners,
    core_ref,
    h_ref,
    ht_ref,
    e_ref,
    wm_ref,
    wu_ref,
    wdm_ref,
    wdo_ref,
    x1_ref,
    onm_ref,
    ono_ref,
    wom_ref,
    woo_ref,
    m_ref,
    g_ref,
    gm_here_ref,
    gu_here_ref,
    gm_there_ref,
    gu_there_ref,
    gdm_ref,
    gdo_ref,
    out_ref,
    dh_s,
    don_ref,
    gom_ref,
    goo_ref,
    on_s,
    acc_s,
    *scratch,
):
    @pl.when(pl.program_id(0) == 0)
    def _():
        acc_s[...] = x1_ref[...]
        dh_s[...] = jnp.zeros_like(dh_s)

    grads = ((gm_here_ref, gu_here_ref), (gm_there_ref, gu_there_ref), gdm_ref, gdo_ref)
    refs = (h_ref, ht_ref, e_ref, wm_ref, wu_ref, wdm_ref, wdo_ref)
    ffn_tile(owners, core_ref, refs, grads, acc_s, dh_s, scratch)

    @pl.when(pl.program_id(0) == pl.num_programs(0) - 1)
    def _():
        half = onm_ref.shape[1]
        mine = lanes_of(core_ref[0], half)
        other = lanes_of(1 - core_ref[0], half)
        out_ref[...] = (acc_s[...] * m_ref[...]).astype(low)
        x1 = x1_ref[...]
        scale = lax.rsqrt(jnp.mean(x1 * x1, axis=-1, keepdims=True) + 1e-06)
        normed = x1 * scale
        d_h2 = dh_s[...]
        scaled = d_h2 * g_ref[2:3, :]
        d_x1 = e_ref[...].astype(wide) + scale * (
            scaled - normed * jnp.mean(scaled * normed, axis=-1, keepdims=True)
        )
        dh_s[...] = d_x1
        on_s[...] = d_x1.astype(low)
        d_mixed = mm_nt(on_s[:, mine], wom_ref[...]) + mm_nt(on_s[:, other], woo_ref[...])
        don_ref[...] = d_mixed.astype(low)
        for columns, g_down_ref, g_ref_o in ((mine, gdm_ref, gom_ref), (other, gdo_ref, goo_ref)):
            d_1 = on_s[:, columns]
            for which, on_ref in ((core_ref[0], onm_ref), (1 - core_ref[0], ono_ref)):
                grad_o = mm_tn(on_ref[...], d_1).astype(low)
                if owners is None:
                    g_ref_o[pl.ds(pl.multiple_of(which * half, half), half), :] = grad_o
                    continue
                count, stride, down_rows = owners
                rows = stride - down_rows
                for part in range(half // rows):
                    owner = which * (count // 2) + part
                    start = pl.multiple_of(owner * stride + down_rows, math.gcd(stride, down_rows))
                    g_down_ref[pl.ds(start, rows), :] = grad_o[part * rows : (part + 1) * rows, :]


def ffn(core, h2, h2t, errors, w_gu, w_d, x1, mixed, w_a, mask, gains8, owners):
    count, width = h2.shape
    half = width // 2
    hidden = w_gu[0].shape[1]
    full = whole((count, width))
    half_full = whole((count, half))
    square = whole((width, half))
    in_tile = pl.BlockSpec((width, TILE_F), lambda j, _: (0, j))
    out_tile = pl.BlockSpec((TILE_F, half), lambda j, _: (j, 0))
    out_weights = pl.BlockSpec((width, half), lambda j, _: (0, 3), pipeline_mode=pl.Buffered(1))
    down_spec, down_shape, out_spec, out_shape = out_tile, (hidden, half), square, (width, half)
    if owners is not None:
        down_shape, out_shape = (owners[0] * owners[1], half), (16, half)
        down_spec, out_spec = whole(down_shape), whole(out_shape)
    struct = jax.ShapeDtypeStruct
    return pl.pallas_call(
        functools.partial(ffn_kernel, owners),
        grid_spec=pltpu.PrefetchScalarGridSpec(
            num_scalar_prefetch=1,
            grid=(hidden // TILE_F,),
            in_specs=[full, whole(h2t.shape), full, in_tile, in_tile, out_tile, out_tile]
            + [full, half_full, half_full, out_weights, out_weights]
            + [whole((count, 1)), whole((8, width))],
            out_specs=[pl.BlockSpec((width, HEAD_DIM), lambda j, _: (0, j))] * 4
            + [down_spec, down_spec]
            + [full, full, full, out_spec, out_spec],
            scratch_shapes=[
                pltpu.VMEM((count, width), low),
                pltpu.VMEM((count, width), wide),
                pltpu.VMEM((width, 2 * TILE_F), low),
                pltpu.VMEM((TILE_F, width), low),
                pltpu.VMEM((width, 2 * TILE_F), low),
                pltpu.VMEM((TILE_F, width), low),
            ],
        ),
        out_shape=[struct((width, hidden // 2), low)] * 4
        + [struct(down_shape, low)] * 2
        + [
            struct((count, width), low),
            struct((count, width), wide),
            struct((count, width), low),
            struct(out_shape, low),
            struct(out_shape, low),
        ],
        compiler_params=pltpu.CompilerParams(vmem_limit_bytes=VMEM_BYTES),
        cost_estimate=pl.CostEstimate(
            flops=16 * count * width * hidden,
            bytes_accessed=count * width * 20 + width * hidden * 12,
            transcendentals=count * hidden,
        ),
        name="ffn",
    )(core, h2, h2t, errors, *w_gu, *w_d, x1, *mixed, *w_a, mask, gains8)


def mixer_backward_kernel(
    slot,
    per_half,
    first,
    half_ref,
    ht_ref,
    g_ref,
    q_ref,
    f_ref,
    v_ref,
    o_ref,
    don_ref,
    *outs,
):
    grad_ref, dpre_ref = outs[-2:]
    gain_o = g_ref[1:2, lanes_of(half_ref[0] * per_half + first + pl.program_id(0), PAIR)]
    lower_ones = triangle(slot, True)
    upper_ones = triangle(slot, False)
    block_rows = lax.broadcasted_iota(jnp.int32, (HEAD_DIM, HEAD_DIM), 0)
    block_columns = lax.broadcasted_iota(jnp.int32, (HEAD_DIM, HEAD_DIM), 1)
    causal = block_rows >= block_columns
    causal_t = block_rows <= block_columns
    blocks = slot // HEAD_DIM
    for sequence in range(q_ref.shape[0] // slot):
        rows = slice(sequence * slot, (sequence + 1) * slot)
        d_on = don_ref[rows, :].astype(wide)
        out = o_ref[rows, :].astype(wide)
        d_out_parts = []
        for head in range(2):
            lanes = slice(head * HEAD_DIM, (head + 1) * HEAD_DIM)
            out_h, d_on_h = out[:, lanes], d_on[:, lanes]
            scale = lax.rsqrt(jnp.mean(out_h * out_h, axis=-1, keepdims=True) + 1e-05)
            normed = out_h * scale
            scaled = d_on_h * gain_o[:, lanes]
            inner = jnp.mean(scaled * normed, axis=-1, keepdims=True)
            d_out_parts.append((scale * (scaled - normed * inner)).astype(low))

        q_pre = q_ref[rows, :]
        share, gate, keys_in, cumulative = decay_parts(f_ref[rows, :], lower_ones)
        grown = jnp.exp(-cumulative)
        shrunk = jnp.exp(cumulative)
        q_share = sigmoid(q_pre)
        decayed_q = (q_pre * q_share * shrunk).astype(low)
        grown_k = (keys_in * grown).astype(low)
        values = v_ref[rows, :]
        dq_parts, dk_parts, dv_parts = [], [], []
        for head in range(2):
            lanes = slice(head * HEAD_DIM, (head + 1) * HEAD_DIM)
            q_h, k_h, v_h = decayed_q[:, lanes], grown_k[:, lanes], values[:, lanes]
            d_out = d_out_parts[head]
            dq_blocks, dk_blocks, dv_blocks = [], [], []
            for block in range(blocks):
                start, end = block * HEAD_DIM, (block + 1) * HEAD_DIM
                here = slice(start, end)
                d_scores = mm_nt(d_out[here], v_h[here])
                d_scores = jnp.where(causal, d_scores, 0.0).astype(low)
                d_q = mm(d_scores, k_h[here])
                if block > 0:
                    before = slice(0, start)
                    d_scores = mm_nt(d_out[here], v_h[before]).astype(low)
                    d_q = d_q + mm(d_scores, k_h[before])
                dq_blocks.append(d_q)
                scores = jnp.where(causal_t, mm_nt(k_h[here], q_h[here]), 0.0).astype(low)
                d_scores = jnp.where(causal_t, mm_nt(v_h[here], d_out[here]), 0.0).astype(low)
                d_v = mm(scores, d_out[here])
                d_k = mm(d_scores, q_h[here])
                if block < blocks - 1:
                    after = slice(end, slot)
                    scores = mm_nt(k_h[here], q_h[after]).astype(low)
                    d_scores = mm_nt(v_h[here], d_out[after]).astype(low)
                    d_v = d_v + mm(scores, d_out[after])
                    d_k = d_k + mm(d_scores, q_h[after])
                dk_blocks.append(d_k)
                dv_blocks.append(d_v)
            dq_parts.append(jnp.concatenate(dq_blocks, axis=0))
            dk_parts.append(jnp.concatenate(dk_blocks, axis=0))
            dv_parts.append(jnp.concatenate(dv_blocks, axis=0))
        d_decayed = jnp.concatenate(dq_parts, axis=1)
        d_grown = jnp.concatenate(dk_parts, axis=1)
        d_value = jnp.concatenate(dv_parts, axis=1)
        d_cumulative = decayed_q.astype(wide) * d_decayed - grown_k.astype(wide) * d_grown
        d_log = split_sum(upper_ones, d_cumulative)
        d_query = d_decayed * shrunk
        d_key = d_grown * grown
        d_q_pre = d_query * q_share * (1.0 + q_pre * (1.0 - q_share))
        d_f_pre = (1.0 - lower_bound) * (d_log / gate - d_key) * share * (1.0 - share)
        dpre_ref[rows, :PAIR] = d_q_pre.astype(low)
        dpre_ref[rows, PAIR : 2 * PAIR] = d_f_pre.astype(low)
        dpre_ref[rows, 2 * PAIR :] = d_value.astype(low)

    grad = mm(ht_ref[...], dpre_ref[...]).astype(low)
    grad_ref[...] = grad.reshape(grad_ref.shape)


def mixer_backward(half, h1t, gains8, kept, d_mixed, slot, shard, pairs=(0, 1), before=()):
    width, count = h1t.shape
    per_half = width // PAIR // 2
    first = pairs[0]
    by_pair = pl.BlockSpec((count, PAIR), lambda j, _: (0, first + j))
    from_whole = pl.BlockSpec((count, PAIR), lambda j, half: (0, half[0] * per_half + first + j))
    struct = jax.ShapeDtypeStruct
    return pl.pallas_call(
        functools.partial(mixer_backward_kernel, slot, per_half, first),
        grid_spec=pltpu.PrefetchScalarGridSpec(
            num_scalar_prefetch=1,
            grid=(len(pairs),),
            in_specs=[whole((width, count)), whole(gains8.shape)]
            + [by_pair] * 4
            + [from_whole]
            + [pl.BlockSpec(memory_space=pl.ANY)] * len(before),
            out_specs=[
                pl.BlockSpec(
                    (width // shard, 1, shard, 3 * PAIR), lambda j, _: (0, first + j, 0, 0)
                ),
                pl.BlockSpec((count, 3 * PAIR), lambda j, _: (0, first + j)),
            ],
        ),
        out_shape=[
            struct((width // shard, per_half, shard, 3 * PAIR), low),
            struct((count, per_half * 3 * PAIR), low),
        ],
        input_output_aliases={8 + k: k for k in range(len(before))},
        compiler_params=pltpu.CompilerParams(vmem_limit_bytes=VMEM_BYTES),
        cost_estimate=pl.CostEstimate(
            flops=len(pairs) * (count * width * 6 * PAIR + 20 * count * slot * PAIR),
            bytes_accessed=len(pairs) * (count * width * 5 + width * PAIR * 6),
            transcendentals=len(pairs) * count * PAIR * 6,
        ),
        name="mixer_backward",
    )(half, h1t, gains8, *kept, d_mixed, *before)


def input_gradient_rows_kernel(
    x_ref, g_ref, dm_ref, do_ref, wm_ref, wo_ref, dx1_ref, dx_ref
):
    d_h1 = mm_nt(dm_ref[...], wm_ref[...]) + mm_nt(do_ref[...], wo_ref[...])
    normed, scale = first_norm(x_ref, None)
    scaled = d_h1 * g_ref[0:1, :]
    dx_ref[...] = dx1_ref[...] + scale * (
        scaled - normed * jnp.mean(scaled * normed, axis=-1, keepdims=True)
    )


def input_gradient(rows, gains8, d_pre, weights, d_x1):
    count, width = rows.shape
    block = count // 2
    columns = d_pre[0].shape[1]
    by_rows = lambda columns: pl.BlockSpec((block, columns), lambda j: (j, 0))
    weight_spec = pl.BlockSpec((width, columns), lambda j: (0, 0), pipeline_mode=pl.Buffered(1))
    return pl.pallas_call(
        input_gradient_rows_kernel,
        grid=(count // block,),
        in_specs=[by_rows(width), whole(gains8.shape)]
        + [by_rows(columns)] * 2
        + [weight_spec] * 2
        + [by_rows(width)],
        out_specs=by_rows(width),
        out_shape=jax.ShapeDtypeStruct((count, width), wide),
        compiler_params=pltpu.CompilerParams(vmem_limit_bytes=VMEM_BYTES),
        cost_estimate=pl.CostEstimate(
            flops=6 * count * width * width,
            bytes_accessed=count * width * 16 + width * width * 6,
            transcendentals=0,
        ),
        name="input_gradient",
    )(rows, gains8, *d_pre, *weights, d_x1)


def update(weight, momentum, average, gradient, step_rate):
    new_momentum = momentum_decay * momentum + gradient
    direction = gradient + momentum_decay * new_momentum + weight_decay * weight
    new_weight = weight - step_rate * direction
    new_average = average_decay * average + (1.0 - average_decay) * new_weight
    return (new_momentum, new_average, new_weight)


def update_kernel(pick, step_rate, sum_count, core_ref, w_ref, m_ref, a_ref, *refs):
    sums, outs, dots_ref = refs[:sum_count], refs[-4:-1], refs[-1]
    weight = w_ref[...]
    gradient = pick(core_ref[0], *[s[...] for s in sums]).astype(wide).reshape(weight.shape)
    results = update(weight, m_ref[...], a_ref[...], gradient, step_rate)
    for out, result in zip(outs, results):
        out[...] = result
    product = weight.astype(low).astype(wide) * gradient
    total = product[..., :HEAD_DIM]
    for start in range(HEAD_DIM, product.shape[-1], HEAD_DIM):
        total = total + product[..., start : start + HEAD_DIM]
    dots_ref[...] = total.reshape(dots_ref.shape)


def update_call(
    core, state, sums, grid, state_spec, sum_specs, pick, step_rate, name, before=()
):
    struct = jax.ShapeDtypeStruct(state[0].shape, wide)
    size = math.prod(state[0].shape)
    rows = state_spec.block_shape[-2]
    steps = math.prod(grid)
    tail = grid[1:]

    def dots_index(*indices):
        place = indices[0]
        for length, index in zip(tail, indices[1:]):
            place = place * length + index
        return (place, 0, 0)

    return pl.pallas_call(
        functools.partial(update_kernel, pick, step_rate, len(sums)),
        grid_spec=pltpu.PrefetchScalarGridSpec(
            num_scalar_prefetch=1,
            grid=grid,
            in_specs=[state_spec] * 3
            + sum_specs
            + [pl.BlockSpec(memory_space=pl.ANY)] * len(before),
            out_specs=[state_spec] * 3 + [pl.BlockSpec((1, rows, HEAD_DIM), dots_index)],
        ),
        out_shape=[struct] * 3 + [jax.ShapeDtypeStruct((steps, rows, HEAD_DIM), wide)],
        input_output_aliases={4 + len(sums) + k: k for k in range(len(before))},
        compiler_params=pltpu.CompilerParams(vmem_limit_bytes=VMEM_BYTES),
        cost_estimate=pl.CostEstimate(flops=12 * size, bytes_accessed=26 * size, transcendentals=0),
        name=name,
    )(core, *state, *sums, *before)


def update_attention(core, half_ref, state, qfv, out, step_rate, before):
    _, shard, width = state[0].shape
    down_rows = out.shape[0] - shard

    def pick(core_index, proj, last):
        gradient = last[down_rows:].astype(wide)
        for kind in range(3):
            parts = [proj[pair * shard :, kind * PAIR :][:shard, :PAIR] for pair in range(2)]
            chosen = jnp.concatenate(parts, axis=1).astype(wide)
            gradient = jnp.where(pl.program_id(0) == kind, chosen, gradient)
        return gradient

    return update_call(
        half_ref,
        state,
        (qfv, out),
        (4,),
        pl.BlockSpec((1, shard, width // 2), lambda kind, half: (kind, 0, half[0])),
        [whole(qfv.shape), whole(out.shape)],
        pick,
        step_rate,
        "update_attention",
        before,
    )


def update_ffn_in(kind_ref, state, totals, step_rate, before):
    _, shard, hidden = state[0].shape

    def pick(_, even, odd):
        blocks = []
        for start in range(0, hidden // 2, HEAD_DIM):
            blocks += [even[:, start : start + HEAD_DIM], odd[:, start : start + HEAD_DIM]]
        return jnp.concatenate(blocks, axis=1)

    return update_call(
        kind_ref,
        state,
        totals,
        (1,),
        pl.BlockSpec((1, shard, hidden), lambda j, kind: (kind[0], 0, 0)),
        [whole(total.shape) for total in totals],
        pick,
        step_rate,
        "update_ffn_in",
        before,
    )


def update_ffn_out(core, state, sums, step_rate):
    shard, width = state[0].shape

    def pick(core_index, mine, other):
        own = pl.program_id(0) == core_index
        return jnp.where(own, mine[:shard].astype(wide), other[:shard].astype(wide))

    return update_call(
        core,
        state,
        sums,
        (2,),
        pl.BlockSpec((shard, width // 2), lambda j, _: (0, j)),
        [whole(total.shape) for total in sums],
        pick,
        step_rate,
        "update_ffn_out",
    )


def pack_kernel(core_ref, w_ref, g_ref, out_ref):
    pairs = w_ref.shape[2] // PAIR
    for pair in range(pairs):
        for kind in range(3):
            start = (pair * 3 + kind) * PAIR
            piece = w_ref[kind, :, pair * PAIR : (pair + 1) * PAIR]
            out_ref[:, start : start + PAIR] = piece.astype(low)
    start = 3 * pairs * PAIR
    out_ref[:, start : start + pairs * PAIR] = w_ref[3].astype(low)
    start += pairs * PAIR
    out_ref[:, start:] = g_ref[...].astype(low)


def pack_attention(core, weights, gains):
    _, shard, width = weights.shape
    half = width // 2
    gain_columns = jnp.pad(gains.T, ((0, 0), (0, HEAD_DIM - 3)))
    columns = 4 * half + HEAD_DIM
    return pl.pallas_call(
        pack_kernel,
        grid_spec=pltpu.PrefetchScalarGridSpec(
            num_scalar_prefetch=1,
            grid=(1,),
            in_specs=[
                pl.BlockSpec((4, shard, half), lambda j, core: (0, 0, core[0])),
                whole((shard, HEAD_DIM)),
            ],
            out_specs=whole((shard, columns)),
        ),
        out_shape=jax.ShapeDtypeStruct((shard, columns), low),
        name="pack_attention",
    )(core, weights, gain_columns)


RING = 8


def ring_place(index):
    return jnp.where(index % 2 == 0, index // 2, RING - 1 - index // 2)


def ring_member(place):
    place = place % RING
    return jnp.where(place < RING // 2, 2 * place, 2 * RING - 1 - 2 * place)


CYCLE = (0, 2, 4, 6, 7, 5, 3, 1)


def ring_next(tensor):
    replicas = lax.axis_size("dp")
    pairs = []
    for place_of, member in enumerate(CYCLE):
        for replica in range(replicas):
            target = CYCLE[(place_of + (1 if replica % 2 == 0 else -1)) % RING]
            pairs.append((member * replicas + replica, target * replicas + replica))
    return lax.ppermute(tensor, ("fsdp", "dp"), pairs)


def ring_shift(tensor, way):
    pairs = [(member, CYCLE[(at + way) % RING]) for at, member in enumerate(CYCLE)]
    return lax.ppermute(tensor, "fsdp", pairs)


def core_swap(tensor):
    return lax.ppermute(tensor, "dp", [(d, d ^ 1) for d in range(lax.axis_size("dp"))])


def column_swap(tensor):
    return lax.ppermute(tensor, "dp", [(d, d ^ 2) for d in range(lax.axis_size("dp"))])


def pack_all_kernel(core_ref, column_ref, w_ref, up_ref, down_ref, g_ref, out_ref):
    shard = w_ref.shape[1]
    half = w_ref.shape[2]
    for pair in range(half // PAIR):
        for kind in range(3):
            start = (pair * 3 + kind) * PAIR
            piece = w_ref[kind, :, pair * PAIR : (pair + 1) * PAIR]
            out_ref[:, start : start + PAIR] = piece.astype(low)
    out_ref[:, 3 * half : 4 * half] = w_ref[3].astype(low)
    start = 4 * half
    rows = lax.broadcasted_iota(jnp.int32, (HEAD_DIM, shard), 0)
    gains = jnp.where(rows == 0, g_ref[0:1, :], jnp.where(rows == 1, g_ref[1:2, :], g_ref[2:3, :]))
    out_ref[:, start : start + HEAD_DIM] = jnp.where(rows < 3, gains, 0.0).T.astype(low)
    start += HEAD_DIM
    out_ref[:, start : start + up_ref.shape[2]] = up_ref[0].astype(low)
    start += up_ref.shape[2]
    for first, count in down_parts(down_ref.shape[0], shard):
        out_ref[:count, start : start + half] = down_ref[first : first + count, :].astype(low)
        if count < shard:
            out_ref[count:, start : start + half] = jnp.zeros((shard - count, half), low)
        start += half


def down_parts(down_rows, shard):
    return [(start, min(shard, down_rows - start)) for start in range(0, down_rows, shard)]


def pack_all(core, column, weights, up, down, gains):
    _, shard, width = weights.shape
    half = width // 2
    parts = len(down_parts(down.shape[0], shard))
    columns = 4 * half + HEAD_DIM + up.shape[2] // 2 + parts * half
    return pl.pallas_call(
        pack_all_kernel,
        grid_spec=pltpu.PrefetchScalarGridSpec(
            num_scalar_prefetch=2,
            grid=(1,),
            in_specs=[
                pl.BlockSpec((4, shard, half), lambda j, core, column: (0, 0, core[0])),
                pl.BlockSpec(
                    (1, shard, up.shape[2] // 2), lambda j, core, column: (core[0], 0, column[0])
                ),
                pl.BlockSpec((down.shape[0], half), lambda j, core, column: (0, core[0])),
                whole(gains.shape),
            ],
            out_specs=whole((shard, columns)),
        ),
        out_shape=jax.ShapeDtypeStruct((shard, columns), low),
        compiler_params=pltpu.CompilerParams(vmem_limit_bytes=VMEM_BYTES),
        name="pack_all",
    )(core, column, weights, up, down, gains)


def place_kernel(which, kept, shapes, origin_ref, column_ref, *refs):
    pieces, outs, semaphores = refs[: len(which)], refs[-1 - len(kept) : -1], refs[-1]
    targets = dict(zip(kept, outs))
    shard, first, up_columns, down_rows, half = shapes
    copies = []

    def copy(source, target):
        copies.append(pltpu.make_async_copy(source, target, semaphores.at[len(copies)]))

    for piece, (origin, across) in zip(pieces, which):
        owner = origin_ref[origin]
        rows = pl.ds(pl.multiple_of(owner * shard, 16), shard)
        if across:
            copy(piece, targets[1].at[rows, lanes_of(1 - column_ref[0], up_columns)])
            continue
        copy(piece.at[:, pl.ds(0, first)], targets[0].at[rows, :])
        own = targets[1].at[rows, lanes_of(column_ref[0], up_columns)]
        copy(piece.at[:, pl.ds(first, up_columns)], own)
        lane = first + up_columns
        for start, count in down_parts(down_rows, shard):
            target = pl.ds(pl.multiple_of(owner * down_rows + start, 16), count)
            copy(piece.at[pl.ds(0, count), pl.ds(lane, half)], targets[2].at[target, :])
            lane += half
    for one in copies:
        one.start()
    for one in copies:
        one.wait()


def place(origins, column, which, pieces, arrays, kept, shapes):
    anywhere = pl.BlockSpec(memory_space=pl.ANY)
    shard, first, up_columns, down_rows, half = shapes
    kinds = [(RING * shard, first), (RING * shard, 2 * up_columns), (RING * down_rows, half)]
    held = [] if arrays is None else list(arrays)
    size = sum(math.prod(piece.shape) for piece in pieces)
    before = 2 + len(pieces)
    return pl.pallas_call(
        functools.partial(place_kernel, which, kept, shapes),
        grid_spec=pltpu.PrefetchScalarGridSpec(
            num_scalar_prefetch=2,
            grid=(1,),
            in_specs=[whole(piece.shape) for piece in pieces] + [anywhere] * len(held),
            out_specs=[anywhere] * len(kept),
            scratch_shapes=[pltpu.SemaphoreType.DMA((8 * len(pieces),))],
        ),
        out_shape=[jax.ShapeDtypeStruct(kinds[k], pieces[0].dtype) for k in kept],
        input_output_aliases={before + k: k for k in range(len(held))},
        compiler_params=pltpu.CompilerParams(vmem_limit_bytes=VMEM_BYTES),
        cost_estimate=pl.CostEstimate(flops=0, bytes_accessed=8 * size, transcendentals=0),
        name="place",
    )(origins, column, *pieces, *held)


def after(tensor, *others):
    return lax.optimization_barrier((tensor, *others))[0]


def core_way():
    return 1 - 2 * (lax.axis_index("dp") % 2)


def ring_origins():
    steps = jnp.array((0, -1, -2, -3, -4, 1, 2, 3), jnp.int32)
    return ring_member(ring_place(lax.axis_index("fsdp")) + steps + RING).astype(jnp.int32)


class RingSumOverColumns:
    def __init__(self, here, there, *others):
        self.here = here
        place = ring_place(lax.axis_index("fsdp"))
        rows = here[0].shape[0] // RING
        self.rows = rows
        self.starts = [
            ring_member(place - core_way() * (s + 1) + 2 * RING) * rows for s in range(RING)
        ]
        self.there = [after(there[0], *others), there[1]] if others else there
        self.sent, self.came, self.totals = [], [], []

    def cross(self, *others):
        start = self.starts[len(self.came)]
        parts = [lax.dynamic_slice_in_dim(array, start, self.rows, 0) for array in self.there]
        sent = (parts[0].astype(wide) + parts[1].astype(wide)).astype(low)
        self.sent.append(after(sent, *others) if others else sent)
        self.came.append(column_swap(self.sent[-1]))

    def term(self):
        start = self.starts[len(self.totals)]
        parts = [lax.dynamic_slice_in_dim(array, start, self.rows, 0) for array in self.here]
        parts.append(self.came[len(self.totals)])
        return parts[0].astype(wide) + parts[1].astype(wide) + parts[2].astype(wide)

    def begin(self, *others):
        self.came[0] = after(self.came[0], *others) if others else self.came[0]
        self.totals.append(self.term().astype(low))

    def step(self, arriving=()):
        total = self.totals[-1]
        ahead = self.came[len(self.totals)]
        moved = ring_next(after(total, ahead))
        moved = after(moved, *arriving) if arriving else moved
        self.totals.append((moved.astype(wide) + self.term()).astype(low))

    def last(self):
        return self.totals[-1]


class RingSum:
    def __init__(self, mine, arrived):
        self.mine, self.arrived = mine, arrived
        place = ring_place(lax.axis_index("fsdp"))
        self.owners = [ring_member(place - core_way() * (s + 1) + 2 * RING) for s in range(RING)]
        self.totals = []

    def term(self):
        parts = []
        for own, arrived in zip(self.mine, self.arrived):
            rows = own.shape[0] // RING
            start = self.owners[len(self.totals)] * rows
            part = lax.dynamic_slice_in_dim(own, start, rows, 0).astype(wide)
            parts.append(part + lax.dynamic_slice_in_dim(arrived, start, rows, 0).astype(wide))
        return parts[0] if len(parts) == 1 else jnp.concatenate(parts, axis=0)

    def begin(self, *others):
        if others:
            self.mine = [after(self.mine[0], *others), *self.mine[1:]]
        self.totals.append(self.term().astype(low))

    def step(self, *before, arriving=()):
        total = self.totals[-1]
        moved = ring_next(after(total, *before) if before else total)
        moved = after(moved, *arriving) if arriving else moved
        self.totals.append((moved.astype(wide) + self.term().astype(wide)).astype(low))

    def last(self):
        return self.totals[-1]


def gather_rows(shard):
    mine = lax.all_gather(shard, "fsdp", axis=0, tiled=True)
    return mine, core_swap(mine)


def core_sum(mine, other):
    return (mine.astype(wide) + core_swap(other).astype(wide)).astype(low)


def scatter_rows(both):
    return lax.psum_scatter(both, "fsdp", scatter_dimension=0, tiled=True)


def over_columns(total):
    total = (total.astype(wide) + column_swap(total).astype(wide)).astype(low)
    return total, core_swap(total)


def on_device(
    inputs,
    cotangent,
    lengths,
    attention_weights,
    attention_momentum,
    attention_average,
    ffn_inputs,
    ffn_inputs_momentum,
    ffn_inputs_average,
    ffn_output,
    ffn_output_momentum,
    ffn_output_average,
    gains,
    gains_momentum,
    gains_average,
):
    micro_count, slot, width = inputs.shape
    hidden = ffn_inputs.shape[2]
    shard, down_rows = ffn_inputs.shape[1], ffn_output.shape[0]
    fsdp_size = lax.axis_size("fsdp")
    replicas = lax.axis_size("dp")
    ringed = fsdp_size == RING
    core = lax.axis_index("dp") % 2
    column = lax.axis_index("dp") // 2
    count = micro_count * slot
    half = width // 2
    core_ref = core.astype(jnp.int32).reshape(1)
    other_ref = 1 - core_ref
    column_ref = column.astype(jnp.int32).reshape(1)
    is_first = core == 0

    rows = inputs.reshape(count, width)
    positions = jnp.arange(slot, dtype=jnp.int32)
    valid = (positions[None, :] < lengths).astype(wide).reshape(count, 1)
    errors = (cotangent.reshape(count, width).astype(wide) * valid).astype(low)

    if ringed:
        origins = ring_origins()
        first = 4 * half + HEAD_DIM
        shapes = (shard, first, hidden // 2, down_rows, half)
        packed = pack_all(
            core_ref, column_ref, attention_weights, ffn_inputs, ffn_output, gains
        )
        wholes, there, which_there = None, [], []
        here, which = [packed], [(0, False)]
        for step in range(1, 6):
            if step <= 3:
                onward = [ring_shift(here[0], 1), ring_shift(here[-1], -1)]
            elif step == 4:
                onward = [ring_next(jnp.where(is_first, *here))]
            across = [column_swap(piece[:, first : first + hidden // 2]) for piece in here]
            wholes = place(
                origins, column_ref, which + which_there, here + there, wholes, (0, 1, 2), shapes
            )
            if step == 5:
                break
            extra = [errors, valid] if step == 2 else []
            tied = list(lax.optimization_barrier((*onward, *across, *wholes, *extra)))
            here, rest = tied[: len(onward)], tied[len(onward) :]
            there, wholes = rest[: len(across)], rest[len(across) : len(across) + 3]
            which_there = [(origin, True) for origin, _ in which]
            which = [(origin, False) for origin in [step, step + 4][: len(onward)]]
        w_a = (wholes[0], core_swap(wholes[0]))
    else:
        w_a = gather_rows(pack_attention(core_ref, attention_weights, gains))
        w_gu = gather_rows(
            lax.dynamic_index_in_dim(ffn_inputs, core, 0, keepdims=False).astype(low)
        )
        w_d = gather_rows(lax.dynamic_slice_in_dim(ffn_output, core * half, half, 1).astype(low))
    mixed_mine, *kept_mine, gains8 = mixer_forward(core_ref, rows, w_a[0], slot)
    if ringed:
        (across,) = lax.optimization_barrier((*across, mixed_mine, w_a[1]))[:1]
        (w_gu_mine,) = place(origins, column_ref, [(4, True)], [across], [wholes[1]], (1,), shapes)
        wholes = [wholes[0], w_gu_mine, wholes[2]]
        rows = after(rows, *wholes[1:])
        w_gu, w_d = [(array, core_swap(array)) for array in wholes[1:]]
    mixed_other, *rest = mixer_forward(
        other_ref, rows, w_a[1], slot, (gains8, mixed_mine, w_a[0])
    )
    kept_other, (x1, h2, h2t, h1t) = rest[:4], rest[4:]
    owners = (fsdp_size, down_rows + shard, down_rows) if ringed else None
    places = jnp.concatenate([core_ref, column_ref])
    *grad_gu, gd_mine, gd_other, output, d_x1, d_mixed, go_mine, go_other = ffn(
        places, h2, h2t, errors, w_gu, w_d, x1, (mixed_mine, mixed_other), w_a, valid, gains8, owners
    )

    gm_here, gu_here, gm_there, gu_there = grad_gu
    there_gu, here_gu = [gm_there, core_swap(gu_there)], [gm_here, core_swap(gu_here)]
    if ringed:
        mine_do, arrived_do = [gd_mine], [core_swap(gd_other)]
    else:
        mine_do, arrived_do = [gd_mine, go_mine], [core_swap(gd_other), core_swap(go_other)]
    by_owner = (fsdp_size * 2 * shard, 3 * PAIR)
    grads_other = mixer_backward(
        other_ref, h1t, gains8, kept_other, d_mixed, slot, shard, (0,)
    )
    if ringed:
        sum_gu = RingSumOverColumns(here_gu, there_gu, grads_other[1])
        sum_gu.cross()
        sum_gu.cross()
    grad_other, dpre_other = mixer_backward(
        other_ref,
        after(h1t, *sum_gu.sent) if ringed else h1t,
        gains8,
        kept_other,
        d_mixed,
        slot,
        shard,
        (1,),
        grads_other,
    )
    arrived_qfv = [core_swap(grad_other.reshape(by_owner))]
    if ringed:
        sum_do = RingSum(mine_do, arrived_do)
        sum_do.begin(dpre_other)
        sum_gu.begin(dpre_other)
        h1t = after(h1t, sum_gu.last(), sum_do.last())
    grad_mine, dpre_mine = mixer_backward(core_ref, h1t, gains8, kept_mine, d_mixed, slot, shard)
    mine_qfv = [grad_mine.reshape(by_owner)]

    def finish_input(*others):
        late = after(dpre_mine, *others) if others else dpre_mine
        return input_gradient(rows, gains8, (late, dpre_other), w_a, d_x1)

    if ringed:
        sum_qfv = RingSum(mine_qfv, arrived_qfv)
        sum_qfv.begin()
        for step in range(1, RING):
            beside = (dpre_mine,) if step == 1 else ()
            if step < RING - 1:
                sum_gu.cross()
            sum_do.step(*([input_grad] if step == 5 else []), arriving=beside)
            sum_gu.step(arriving=beside)
            if step < RING - 1:
                sum_qfv.step()
            if step == 3:
                input_grad = finish_input(sum_qfv.last())
        total_gu, total_do = sum_gu.last(), sum_do.last()
    else:
        both = [
            [
                [(own.astype(wide) + came.astype(wide)).astype(low)]
                for own, came in (here_gu, there_gu)
            ],
            [
                (own.astype(wide) + came.astype(wide)).astype(low)
                for own, came in zip(mine_do, arrived_do)
            ],
            [(mine_qfv[0].astype(wide) + arrived_qfv[0].astype(wide)).astype(low)],
        ]
        ((here,), (there,)), both_do, both_qfv = both
        here = (here.astype(wide) + column_swap(there).astype(wide)).astype(low)
        total_gu = scatter_rows(here)
        total_do = jnp.concatenate([scatter_rows(part) for part in both_do], axis=0)
        total_qfv = scatter_rows(both_qfv[0])
        input_grad = finish_input()
    scale_rows = 1.0 / math.sqrt(count * fsdp_size * replicas)
    matrix_step = matrix_rate * scale_rows
    attention_state = (attention_weights, attention_momentum, attention_average)
    ffn_in_state = (ffn_inputs, ffn_inputs_momentum, ffn_inputs_average)
    ffn_out_state = (ffn_output, ffn_output_momentum, ffn_output_average)
    sum_do = over_columns(total_do)
    there = column_swap(total_gu)
    even = jnp.where(column == 0, total_gu, there)
    odd = jnp.where(column == 0, there, total_gu)
    sum_gu = (even, odd), (core_swap(even), core_swap(odd))
    *new_out, _ = update_ffn_out(core_ref, ffn_out_state, sum_do, matrix_step)
    *new_in, dots_up = update_ffn_in(core_ref, ffn_in_state, sum_gu[0], matrix_step, ())
    *new_in, dots_gate = update_ffn_in(other_ref, ffn_in_state, sum_gu[1], matrix_step, new_in)
    if ringed:
        sum_qfv.step()
        total_qfv = sum_qfv.last()
    there = after(column_swap(total_qfv), new_in[0], new_out[0])
    sum_qfv = (total_qfv.astype(wide) + there.astype(wide)).astype(low)
    *own, dots_own = update_attention(
        core_ref, core_ref, attention_state, sum_qfv, sum_do[0], matrix_step, ()
    )
    theirs = after(core_swap(sum_qfv), own[0])
    *new_attention, dots_theirs = update_attention(
        core_ref, other_ref, attention_state, theirs, sum_do[1], matrix_step, own
    )
    dots = jnp.sum(dots_own + dots_theirs, axis=2)
    row_sums = jnp.stack([dots[0] + dots[1] + dots[2], dots[3], jnp.sum(dots_up + dots_gate, axis=(0, 2))])
    sum_gains = row_sums / gains.astype(low).astype(wide)
    return (
        output.reshape(micro_count, slot, width),
        input_grad.reshape(micro_count, slot, width),
        *new_attention,
        *new_in,
        *new_out,
        *update(gains, gains_momentum, gains_average, sum_gains, gain_rate * scale_rows),
    )


def solution(mesh):
    rows_split = P(None, ("fsdp", "dp"), None)
    middle_split = P(None, "fsdp", None)
    first_split = P("fsdp", None)
    gains_split = P(None, "fsdp")
    in_specs = (
        (rows_split, rows_split, P(None, ("fsdp", "dp")))
        + (middle_split,) * 6
        + (first_split,) * 3
        + (gains_split,) * 3
    )
    out_specs = (
        (rows_split, rows_split)
        + (middle_split,) * 6
        + (first_split,) * 3
        + (gains_split,) * 3
    )
    return jax.shard_map(
        on_device, mesh=mesh, in_specs=in_specs, out_specs=out_specs, check_vma=False
    )
```

```python
import functools
import math

import jax
import jax.numpy as jnp
from jax import lax
from jax.experimental import pallas as pl
from jax.experimental.pallas import tpu as pltpu
from jax.sharding import PartitionSpec as P

HEAD_DIM = 128
PAIR = 2 * HEAD_DIM

lower_bound = 0.9
momentum_decay = 0.9
average_decay = 0.7
weight_decay = 0.0005
matrix_rate = 0.03
gain_rate = 0.1
low = jnp.bfloat16
wide = jnp.float32
TILE_F = 256
VMEM_BYTES = 60 * 1024 * 1024


def mm(left, right):
    return jnp.dot(left, right, preferred_element_type=wide)


def mm_nt(left, right):
    return lax.dot_general(left, right, (((1,), (1,)), ((), ())), preferred_element_type=wide)


def mm_tn(left, right):
    return lax.dot_general(left, right, (((0,), (0,)), ((), ())), preferred_element_type=wide)


def sigmoid(u):
    return 0.5 * jnp.tanh(0.5 * u) + 0.5


def whole(shape):
    return pl.BlockSpec(shape, lambda *_: (0,) * len(shape), pipeline_mode=pl.Buffered(1))


def split_sum(ones_matrix, tensor):
    high = tensor.astype(low)
    rest = (tensor - high.astype(wide)).astype(low)
    return mm(ones_matrix, high) + mm(ones_matrix, rest)


def triangle(length, lower):
    rows = lax.broadcasted_iota(jnp.int32, (length, length), 0)
    columns = lax.broadcasted_iota(jnp.int32, (length, length), 1)
    kept = rows >= columns if lower else rows <= columns
    return kept.astype(wide).astype(low)


def decay_parts(f_pre, lower_ones):
    share = sigmoid(f_pre)
    gate = lower_bound + (1.0 - lower_bound) * share
    keys_in = (1.0 - lower_bound) * (1.0 - share)
    cumulative = split_sum(lower_ones, jnp.log(gate))
    middle_row = cumulative.shape[0] // 2
    cumulative = cumulative - cumulative[middle_row : middle_row + 1, :]
    return share, gate, keys_in, cumulative


def first_norm(x_ref, gain_row):
    rows = x_ref[...].astype(wide)
    scale = lax.rsqrt(jnp.mean(rows * rows, axis=-1, keepdims=True) + 1e-06)
    return rows * scale, scale


def lanes_of(half, size):
    return pl.ds(pl.multiple_of(half * size, size), size)


def mixer_forward_first_kernel(
    slot, half_ref, x_ref, w_ref, columns_ref, on_ref, q_ref, f_ref, v_ref, o_ref, g_ref, h_s
):
    @pl.when(pl.program_id(0) == 0)
    def _():
        g_ref[...] = columns_ref[...].astype(wide).T[: g_ref.shape[0], :]

    mixer_forward_kernel(
        slot, half_ref, x_ref, w_ref, g_ref, on_ref, q_ref, f_ref, v_ref, o_ref, h_s
    )


def mixer_forward_kernel(
    slot, half_ref, x_ref, w_ref, g_ref, on_ref, q_ref, f_ref, v_ref, o_ref, h_s
):
    @pl.when(pl.program_id(0) == 0)
    def _():
        normed, _ = first_norm(x_ref, None)
        h_s[...] = (normed * g_ref[0:1, :]).astype(low)

    gain_o = g_ref[1:2, lanes_of(half_ref[0] * pl.num_programs(0) + pl.program_id(0), PAIR)]
    pre = mm(h_s[...], w_ref[...])
    q_ref[...] = pre[:, :PAIR]
    f_ref[...] = pre[:, PAIR : 2 * PAIR]
    v_ref[...] = pre[:, 2 * PAIR :].astype(low)
    lower_ones = triangle(slot, True)
    block_rows = lax.broadcasted_iota(jnp.int32, (HEAD_DIM, HEAD_DIM), 0)
    block_columns = lax.broadcasted_iota(jnp.int32, (HEAD_DIM, HEAD_DIM), 1)
    causal = block_rows >= block_columns
    for sequence in range(x_ref.shape[0] // slot):
        rows = slice(sequence * slot, (sequence + 1) * slot)
        q_pre = q_ref[rows, :]
        _, _, keys_in, cumulative = decay_parts(f_ref[rows, :], lower_ones)
        grown = jnp.exp(-cumulative)
        decayed_q = (q_pre * sigmoid(q_pre) * jnp.exp(cumulative)).astype(low)
        grown_k = (keys_in * grown).astype(low)
        values = v_ref[rows, :]
        for head in range(2):
            lanes = slice(head * HEAD_DIM, (head + 1) * HEAD_DIM)
            for block in range(slot // HEAD_DIM):
                start, end = block * HEAD_DIM, (block + 1) * HEAD_DIM
                q_block = decayed_q[start:end, lanes]
                diagonal = mm_nt(q_block, grown_k[start:end, lanes])
                diagonal = jnp.where(causal, diagonal, 0.0).astype(low)
                out = mm(diagonal, values[start:end, lanes])
                if block > 0:
                    scores = mm_nt(q_block, grown_k[:start, lanes]).astype(low)
                    out = out + mm(scores, values[:start, lanes])
                scale = lax.rsqrt(jnp.mean(out * out, axis=-1, keepdims=True) + 1e-05)
                target = slice(sequence * slot + start, sequence * slot + end)
                o_ref[target, lanes] = out.astype(low)
                on_ref[target, lanes] = (out * scale * gain_o[:, lanes]).astype(low)


def mixer_forward_last_kernel(
    slot,
    half_ref,
    x_ref,
    w_ref,
    g_ref,
    before_ref,
    woo_ref,
    wom_ref,
    on_ref,
    q_ref,
    f_ref,
    v_ref,
    o_ref,
    x1_ref,
    h2_ref,
    h2t_ref,
    h1t_ref,
    h_s,
    on_s,
):
    step = pl.program_id(0)
    half = before_ref.shape[1]
    mixer_forward_kernel(
        slot, half_ref, x_ref, w_ref, g_ref, on_ref, q_ref, f_ref, v_ref, o_ref, h_s
    )
    on_s[:, lanes_of(half_ref[0] * pl.num_programs(0) + step, PAIR)] = on_ref[...]

    @pl.when(step == pl.num_programs(0) - 1)
    def _():
        here = lanes_of(half_ref[0], half)
        there = lanes_of(1 - half_ref[0], half)
        on_s[:, there] = before_ref[...]
        h1t_ref[...] = h_s[...].astype(wide).T.astype(low)
        x1_ref[:, here] = x_ref[:, here].astype(wide) + mm(on_s[...], woo_ref[...])
        x1_ref[:, there] = x_ref[:, there].astype(wide) + mm(on_s[...], wom_ref[...])
        x1 = x1_ref[...]
        scale = lax.rsqrt(jnp.mean(x1 * x1, axis=-1, keepdims=True) + 1e-06)
        normed = x1 * scale * g_ref[2:3, :]
        h2_ref[...] = normed.astype(low)
        h2t_ref[...] = normed.T.astype(low)


def mixer_forward(half, rows, weights, slot, ending=None):
    count, width = rows.shape
    pairs = width // PAIR // 2
    by_pair = pl.BlockSpec((count, PAIR), lambda j, _: (0, j))
    struct = jax.ShapeDtypeStruct
    shape = lambda kind: struct((count, width // 2), kind)
    in_specs = [whole(rows.shape), pl.BlockSpec((width, 3 * PAIR), lambda j, _: (0, j))]
    operands = [half, rows, weights]
    out_specs = [by_pair] * 5
    out_shape = [shape(low), shape(wide), shape(wide), shape(low), shape(low)]
    scratch = [pltpu.VMEM((count, width), low)]
    if ending is None:
        kernel = mixer_forward_first_kernel
        last = weights.shape[1] // HEAD_DIM - 1
        in_specs += [pl.BlockSpec((width, HEAD_DIM), lambda j, _: (0, last))]
        operands += [weights]
        out_specs += [whole((8, width))]
        out_shape += [struct((8, width), wide)]
    if ending is not None:
        kernel = mixer_forward_last_kernel
        out_weights = pl.BlockSpec((width, width // 2), lambda j, _: (0, 3))
        in_specs += [whole(ending[0].shape), whole((count, width // 2)), out_weights, out_weights]
        operands += [ending[0], ending[1], weights, ending[2]]
        out_specs += [whole((count, width))] * 2 + [whole((width, count))] * 2
        out_shape += [
            struct((count, width), wide),
            struct((count, width), low),
            struct((width, count), low),
            struct((width, count), low),
        ]
        scratch += [pltpu.VMEM((count, width), low)]
    return pl.pallas_call(
        functools.partial(kernel, slot),
        grid_spec=pltpu.PrefetchScalarGridSpec(
            num_scalar_prefetch=1,
            grid=(pairs,),
            in_specs=in_specs,
            out_specs=out_specs,
            scratch_shapes=scratch,
        ),
        out_shape=out_shape,
        compiler_params=pltpu.CompilerParams(vmem_limit_bytes=VMEM_BYTES),
        cost_estimate=pl.CostEstimate(
            flops=count * width * 4 * width + 10 * count * slot * width,
            bytes_accessed=count * width * 12 + width * width * 4,
            transcendentals=count * width * 3,
        ),
        name="mixer_forward",
    )(*operands)


def store_down(out_ref, tile, owners):
    if owners is None:
        out_ref[...] = tile
        return
    _, stride, down_rows = owners
    block = math.gcd(down_rows, tile.shape[0])
    first = pl.program_id(0) * (tile.shape[0] // block)
    for part in range(tile.shape[0] // block):
        owner = (first + part) // (down_rows // block)
        inside = (first + part) % (down_rows // block)
        start = pl.multiple_of(owner * stride + inside * block, block)
        out_ref[pl.ds(start, block), :] = tile[part * block : (part + 1) * block, :]


def ffn_tile(owners, core_ref, refs, grads, acc_ref, dh_ref, scratch):
    h_ref, ht_ref, e_ref, wm_ref, wu_ref, wdm_ref, wdo_ref = refs
    gm_ref, gu_ref, gdm_ref, gdo_ref = grads
    gu_w, down_w, gu_g, down_g = scratch
    half, tile = wdm_ref.shape[1], wm_ref.shape[1]
    mine, other = lanes_of(core_ref[0], half), lanes_of(1 - core_ref[0], half)
    kind, kind_other = lanes_of(core_ref[0], tile), lanes_of(1 - core_ref[0], tile)
    gu_w[:, kind] = wm_ref[...]
    gu_w[:, kind_other] = wu_ref[...]
    down_w[:, mine] = wdm_ref[...]
    down_w[:, other] = wdo_ref[...]
    pre = mm(h_ref[...], gu_w[...])
    a, b = pre[:, :tile], pre[:, tile:]
    share = sigmoid(a)
    swish = a * share
    mid = (swish * b).astype(low)
    d_mid = mm_nt(e_ref[...], down_w[...])
    down_g[...] = mm_tn(mid, e_ref[...]).astype(low)
    d_a = (d_mid * b * (share + swish * (1.0 - share))).astype(low)
    d_b = (d_mid * swish).astype(low)
    d_pre = jnp.concatenate([d_a, d_b], axis=1)
    acc_ref[...] += mm(mid, down_w[...])
    dh_ref[...] += mm_nt(d_pre, gu_w[...])
    gu_g[...] = mm(ht_ref[...], d_pre).astype(low)
    blocks = tile // HEAD_DIM
    for side, block in enumerate((core_ref[1], 1 - core_ref[1])):
        gm_ref[side] = gu_g[:, lanes_of(core_ref[0] * blocks + block, HEAD_DIM)]
        gu_ref[side] = gu_g[:, lanes_of((1 - core_ref[0]) * blocks + block, HEAD_DIM)]
    store_down(gdm_ref, down_g[:, mine], owners)
    store_down(gdo_ref, down_g[:, other], owners)


def ffn_kernel(
    owners,
    core_ref,
    h_ref,
    ht_ref,
    e_ref,
    wm_ref,
    wu_ref,
    wdm_ref,
    wdo_ref,
    x1_ref,
    onm_ref,
    ono_ref,
    wom_ref,
    woo_ref,
    m_ref,
    g_ref,
    gm_ref,
    gu_ref,
    gdm_ref,
    gdo_ref,
    out_ref,
    dh_s,
    don_ref,
    gom_ref,
    goo_ref,
    on_s,
    acc_s,
    *scratch,
):
    @pl.when(pl.program_id(0) == 0)
    def _():
        acc_s[...] = x1_ref[...]
        dh_s[...] = jnp.zeros_like(dh_s)

    grads = (gm_ref, gu_ref, gdm_ref, gdo_ref)
    refs = (h_ref, ht_ref, e_ref, wm_ref, wu_ref, wdm_ref, wdo_ref)
    ffn_tile(owners, core_ref, refs, grads, acc_s, dh_s, scratch)

    @pl.when(pl.program_id(0) == pl.num_programs(0) - 1)
    def _():
        half = onm_ref.shape[1]
        mine = lanes_of(core_ref[0], half)
        other = lanes_of(1 - core_ref[0], half)
        out_ref[...] = (acc_s[...] * m_ref[...]).astype(low)
        x1 = x1_ref[...]
        scale = lax.rsqrt(jnp.mean(x1 * x1, axis=-1, keepdims=True) + 1e-06)
        normed = x1 * scale
        d_h2 = dh_s[...]
        scaled = d_h2 * g_ref[2:3, :]
        d_x1 = e_ref[...].astype(wide) + scale * (
            scaled - normed * jnp.mean(scaled * normed, axis=-1, keepdims=True)
        )
        dh_s[...] = d_x1
        on_s[...] = d_x1.astype(low)
        d_mixed = mm_nt(on_s[:, mine], wom_ref[...]) + mm_nt(on_s[:, other], woo_ref[...])
        don_ref[...] = d_mixed.astype(low)
        for columns, g_down_ref, g_ref_o in ((mine, gdm_ref, gom_ref), (other, gdo_ref, goo_ref)):
            d_1 = on_s[:, columns]
            for which, on_ref in ((core_ref[0], onm_ref), (1 - core_ref[0], ono_ref)):
                grad_o = mm_tn(on_ref[...], d_1).astype(low)
                if owners is None:
                    g_ref_o[pl.ds(pl.multiple_of(which * half, half), half), :] = grad_o
                    continue
                count, stride, down_rows = owners
                rows = stride - down_rows
                for part in range(half // rows):
                    owner = which * (count // 2) + part
                    start = pl.multiple_of(owner * stride + down_rows, math.gcd(stride, down_rows))
                    g_down_ref[pl.ds(start, rows), :] = grad_o[part * rows : (part + 1) * rows, :]


def ffn(core, h2, h2t, errors, w_gu, w_d, x1, mixed, w_a, mask, gains8, owners):
    count, width = h2.shape
    half = width // 2
    hidden = w_gu[0].shape[1]
    full = whole((count, width))
    half_full = whole((count, half))
    square = whole((width, half))
    in_tile = pl.BlockSpec((width, TILE_F), lambda j, _: (0, j))
    out_tile = pl.BlockSpec((TILE_F, half), lambda j, _: (j, 0))
    out_weights = pl.BlockSpec((width, half), lambda j, _: (0, 3), pipeline_mode=pl.Buffered(1))
    down_spec, down_shape, out_spec, out_shape = out_tile, (hidden, half), square, (width, half)
    if owners is not None:
        down_shape, out_shape = (owners[0] * owners[1], half), (16, half)
        down_spec, out_spec = whole(down_shape), whole(out_shape)
    struct = jax.ShapeDtypeStruct
    return pl.pallas_call(
        functools.partial(ffn_kernel, owners),
        grid_spec=pltpu.PrefetchScalarGridSpec(
            num_scalar_prefetch=1,
            grid=(hidden // TILE_F,),
            in_specs=[full, whole(h2t.shape), full, in_tile, in_tile, out_tile, out_tile]
            + [full, half_full, half_full, out_weights, out_weights]
            + [whole((count, 1)), whole((8, width))],
            out_specs=[pl.BlockSpec((2, width, HEAD_DIM), lambda j, _: (0, 0, j))] * 2
            + [down_spec, down_spec]
            + [full, full, full, out_spec, out_spec],
            scratch_shapes=[
                pltpu.VMEM((count, width), low),
                pltpu.VMEM((count, width), wide),
                pltpu.VMEM((width, 2 * TILE_F), low),
                pltpu.VMEM((TILE_F, width), low),
                pltpu.VMEM((width, 2 * TILE_F), low),
                pltpu.VMEM((TILE_F, width), low),
            ],
        ),
        out_shape=[struct((2, width, hidden // 2), low)] * 2
        + [struct(down_shape, low)] * 2
        + [
            struct((count, width), low),
            struct((count, width), wide),
            struct((count, width), low),
            struct(out_shape, low),
            struct(out_shape, low),
        ],
        compiler_params=pltpu.CompilerParams(vmem_limit_bytes=VMEM_BYTES),
        cost_estimate=pl.CostEstimate(
            flops=16 * count * width * hidden,
            bytes_accessed=count * width * 20 + width * hidden * 12,
            transcendentals=count * hidden,
        ),
        name="ffn",
    )(core, h2, h2t, errors, *w_gu, *w_d, x1, *mixed, *w_a, mask, gains8)


def mixer_backward_kernel(
    slot,
    per_half,
    first,
    half_ref,
    ht_ref,
    g_ref,
    q_ref,
    f_ref,
    v_ref,
    o_ref,
    don_ref,
    *outs,
):
    grad_ref, dpre_ref = outs[-2:]
    gain_o = g_ref[1:2, lanes_of(half_ref[0] * per_half + first + pl.program_id(0), PAIR)]
    lower_ones = triangle(slot, True)
    upper_ones = triangle(slot, False)
    block_rows = lax.broadcasted_iota(jnp.int32, (HEAD_DIM, HEAD_DIM), 0)
    block_columns = lax.broadcasted_iota(jnp.int32, (HEAD_DIM, HEAD_DIM), 1)
    causal = block_rows >= block_columns
    causal_t = block_rows <= block_columns
    blocks = slot // HEAD_DIM
    for sequence in range(q_ref.shape[0] // slot):
        rows = slice(sequence * slot, (sequence + 1) * slot)
        d_on = don_ref[rows, :].astype(wide)
        out = o_ref[rows, :].astype(wide)
        d_out_parts = []
        for head in range(2):
            lanes = slice(head * HEAD_DIM, (head + 1) * HEAD_DIM)
            out_h, d_on_h = out[:, lanes], d_on[:, lanes]
            scale = lax.rsqrt(jnp.mean(out_h * out_h, axis=-1, keepdims=True) + 1e-05)
            normed = out_h * scale
            scaled = d_on_h * gain_o[:, lanes]
            inner = jnp.mean(scaled * normed, axis=-1, keepdims=True)
            d_out_parts.append((scale * (scaled - normed * inner)).astype(low))

        q_pre = q_ref[rows, :]
        share, gate, keys_in, cumulative = decay_parts(f_ref[rows, :], lower_ones)
        grown = jnp.exp(-cumulative)
        shrunk = jnp.exp(cumulative)
        q_share = sigmoid(q_pre)
        decayed_q = (q_pre * q_share * shrunk).astype(low)
        grown_k = (keys_in * grown).astype(low)
        values = v_ref[rows, :]
        dq_parts, dk_parts, dv_parts = [], [], []
        for head in range(2):
            lanes = slice(head * HEAD_DIM, (head + 1) * HEAD_DIM)
            q_h, k_h, v_h = decayed_q[:, lanes], grown_k[:, lanes], values[:, lanes]
            d_out = d_out_parts[head]
            dq_blocks, dk_blocks, dv_blocks = [], [], []
            for block in range(blocks):
                start, end = block * HEAD_DIM, (block + 1) * HEAD_DIM
                here = slice(start, end)
                d_scores = mm_nt(d_out[here], v_h[here])
                d_scores = jnp.where(causal, d_scores, 0.0).astype(low)
                d_q = mm(d_scores, k_h[here])
                if block > 0:
                    before = slice(0, start)
                    d_scores = mm_nt(d_out[here], v_h[before]).astype(low)
                    d_q = d_q + mm(d_scores, k_h[before])
                dq_blocks.append(d_q)
                scores = jnp.where(causal_t, mm_nt(k_h[here], q_h[here]), 0.0).astype(low)
                d_scores = jnp.where(causal_t, mm_nt(v_h[here], d_out[here]), 0.0).astype(low)
                d_v = mm(scores, d_out[here])
                d_k = mm(d_scores, q_h[here])
                if block < blocks - 1:
                    after = slice(end, slot)
                    scores = mm_nt(k_h[here], q_h[after]).astype(low)
                    d_scores = mm_nt(v_h[here], d_out[after]).astype(low)
                    d_v = d_v + mm(scores, d_out[after])
                    d_k = d_k + mm(d_scores, q_h[after])
                dk_blocks.append(d_k)
                dv_blocks.append(d_v)
            dq_parts.append(jnp.concatenate(dq_blocks, axis=0))
            dk_parts.append(jnp.concatenate(dk_blocks, axis=0))
            dv_parts.append(jnp.concatenate(dv_blocks, axis=0))
        d_decayed = jnp.concatenate(dq_parts, axis=1)
        d_grown = jnp.concatenate(dk_parts, axis=1)
        d_value = jnp.concatenate(dv_parts, axis=1)
        d_cumulative = decayed_q.astype(wide) * d_decayed - grown_k.astype(wide) * d_grown
        d_log = split_sum(upper_ones, d_cumulative)
        d_query = d_decayed * shrunk
        d_key = d_grown * grown
        d_q_pre = d_query * q_share * (1.0 + q_pre * (1.0 - q_share))
        d_f_pre = (1.0 - lower_bound) * (d_log / gate - d_key) * share * (1.0 - share)
        dpre_ref[rows, :PAIR] = d_q_pre.astype(low)
        dpre_ref[rows, PAIR : 2 * PAIR] = d_f_pre.astype(low)
        dpre_ref[rows, 2 * PAIR :] = d_value.astype(low)

    grad = mm(ht_ref[...], dpre_ref[...]).astype(low)
    grad_ref[...] = grad.reshape(grad_ref.shape)


def mixer_backward(half, h1t, gains8, kept, d_mixed, slot, shard, pairs=(0, 1), before=()):
    width, count = h1t.shape
    per_half = width // PAIR // 2
    first = pairs[0]
    by_pair = pl.BlockSpec((count, PAIR), lambda j, _: (0, first + j))
    from_whole = pl.BlockSpec((count, PAIR), lambda j, half: (0, half[0] * per_half + first + j))
    struct = jax.ShapeDtypeStruct
    return pl.pallas_call(
        functools.partial(mixer_backward_kernel, slot, per_half, first),
        grid_spec=pltpu.PrefetchScalarGridSpec(
            num_scalar_prefetch=1,
            grid=(len(pairs),),
            in_specs=[whole((width, count)), whole(gains8.shape)]
            + [by_pair] * 4
            + [from_whole]
            + [pl.BlockSpec(memory_space=pl.ANY)] * len(before),
            out_specs=[
                pl.BlockSpec(
                    (width // shard, 1, shard, 3 * PAIR), lambda j, _: (0, first + j, 0, 0)
                ),
                pl.BlockSpec((count, 3 * PAIR), lambda j, _: (0, first + j)),
            ],
        ),
        out_shape=[
            struct((width // shard, per_half, shard, 3 * PAIR), low),
            struct((count, per_half * 3 * PAIR), low),
        ],
        input_output_aliases={8 + k: k for k in range(len(before))},
        compiler_params=pltpu.CompilerParams(vmem_limit_bytes=VMEM_BYTES),
        cost_estimate=pl.CostEstimate(
            flops=len(pairs) * (count * width * 6 * PAIR + 20 * count * slot * PAIR),
            bytes_accessed=len(pairs) * (count * width * 5 + width * PAIR * 6),
            transcendentals=len(pairs) * count * PAIR * 6,
        ),
        name="mixer_backward",
    )(half, h1t, gains8, *kept, d_mixed, *before)


def input_gradient_rows_kernel(
    x_ref, g_ref, dm_ref, do_ref, wm_ref, wo_ref, dx1_ref, dx_ref
):
    d_h1 = mm_nt(dm_ref[...], wm_ref[...]) + mm_nt(do_ref[...], wo_ref[...])
    normed, scale = first_norm(x_ref, None)
    scaled = d_h1 * g_ref[0:1, :]
    dx_ref[...] = dx1_ref[...] + scale * (
        scaled - normed * jnp.mean(scaled * normed, axis=-1, keepdims=True)
    )


def input_gradient(rows, gains8, d_pre, weights, d_x1):
    count, width = rows.shape
    block = count // 2
    columns = d_pre[0].shape[1]
    by_rows = lambda columns: pl.BlockSpec((block, columns), lambda j: (j, 0))
    weight_spec = pl.BlockSpec((width, columns), lambda j: (0, 0), pipeline_mode=pl.Buffered(1))
    return pl.pallas_call(
        input_gradient_rows_kernel,
        grid=(count // block,),
        in_specs=[by_rows(width), whole(gains8.shape)]
        + [by_rows(columns)] * 2
        + [weight_spec] * 2
        + [by_rows(width)],
        out_specs=by_rows(width),
        out_shape=jax.ShapeDtypeStruct((count, width), wide),
        compiler_params=pltpu.CompilerParams(vmem_limit_bytes=VMEM_BYTES),
        cost_estimate=pl.CostEstimate(
            flops=6 * count * width * width,
            bytes_accessed=count * width * 16 + width * width * 6,
            transcendentals=0,
        ),
        name="input_gradient",
    )(rows, gains8, *d_pre, *weights, d_x1)


def update(weight, momentum, average, gradient, step_rate):
    new_momentum = momentum_decay * momentum + gradient
    direction = gradient + momentum_decay * new_momentum + weight_decay * weight
    new_weight = weight - step_rate * direction
    new_average = average_decay * average + (1.0 - average_decay) * new_weight
    return (new_momentum, new_average, new_weight)


def update_kernel(pick, step_rate, sum_count, core_ref, w_ref, m_ref, a_ref, *refs):
    sums, outs, dots_ref = refs[:sum_count], refs[-4:-1], refs[-1]
    weight = w_ref[...]
    gradient = pick(core_ref[0], *[s[...] for s in sums]).astype(wide).reshape(weight.shape)
    results = update(weight, m_ref[...], a_ref[...], gradient, step_rate)
    for out, result in zip(outs, results):
        out[...] = result
    product = weight.astype(low).astype(wide) * gradient
    total = product[..., :HEAD_DIM]
    for start in range(HEAD_DIM, product.shape[-1], HEAD_DIM):
        total = total + product[..., start : start + HEAD_DIM]
    dots_ref[...] = total.reshape(dots_ref.shape)


def update_call(
    core, state, sums, grid, state_spec, sum_specs, pick, step_rate, name, before=()
):
    struct = jax.ShapeDtypeStruct(state[0].shape, wide)
    size = math.prod(state[0].shape)
    rows = state_spec.block_shape[-2]
    steps = math.prod(grid)
    tail = grid[1:]

    def dots_index(*indices):
        place = indices[0]
        for length, index in zip(tail, indices[1:]):
            place = place * length + index
        return (place, 0, 0)

    return pl.pallas_call(
        functools.partial(update_kernel, pick, step_rate, len(sums)),
        grid_spec=pltpu.PrefetchScalarGridSpec(
            num_scalar_prefetch=1,
            grid=grid,
            in_specs=[state_spec] * 3
            + sum_specs
            + [pl.BlockSpec(memory_space=pl.ANY)] * len(before),
            out_specs=[state_spec] * 3 + [pl.BlockSpec((1, rows, HEAD_DIM), dots_index)],
        ),
        out_shape=[struct] * 3 + [jax.ShapeDtypeStruct((steps, rows, HEAD_DIM), wide)],
        input_output_aliases={4 + len(sums) + k: k for k in range(len(before))},
        compiler_params=pltpu.CompilerParams(vmem_limit_bytes=VMEM_BYTES),
        cost_estimate=pl.CostEstimate(flops=12 * size, bytes_accessed=26 * size, transcendentals=0),
        name=name,
    )(core, *state, *sums, *before)


def update_attention(core, half_ref, state, qfv, out, step_rate, before):
    _, shard, width = state[0].shape
    down_rows = out.shape[0] - shard

    def pick(core_index, proj, last):
        gradient = last[down_rows:].astype(wide)
        for kind in range(3):
            parts = [proj[pair * shard :, kind * PAIR :][:shard, :PAIR] for pair in range(2)]
            chosen = jnp.concatenate(parts, axis=1).astype(wide)
            gradient = jnp.where(pl.program_id(0) == kind, chosen, gradient)
        return gradient

    return update_call(
        half_ref,
        state,
        (qfv, out),
        (4,),
        pl.BlockSpec((1, shard, width // 2), lambda kind, half: (kind, 0, half[0])),
        [whole(qfv.shape), whole(out.shape)],
        pick,
        step_rate,
        "update_attention",
        before,
    )


def update_ffn_in(kind_ref, state, totals, step_rate, before):
    _, shard, hidden = state[0].shape

    def pick(_, even, odd):
        blocks = []
        for start in range(0, hidden // 2, HEAD_DIM):
            blocks += [even[:, start : start + HEAD_DIM], odd[:, start : start + HEAD_DIM]]
        return jnp.concatenate(blocks, axis=1)

    return update_call(
        kind_ref,
        state,
        totals,
        (1,),
        pl.BlockSpec((1, shard, hidden), lambda j, kind: (kind[0], 0, 0)),
        [whole(total.shape) for total in totals],
        pick,
        step_rate,
        "update_ffn_in",
        before,
    )


def update_ffn_out(core, state, sums, step_rate):
    shard, width = state[0].shape

    def pick(core_index, mine, other):
        own = pl.program_id(0) == core_index
        return jnp.where(own, mine[:shard].astype(wide), other[:shard].astype(wide))

    return update_call(
        core,
        state,
        sums,
        (2,),
        pl.BlockSpec((shard, width // 2), lambda j, _: (0, j)),
        [whole(total.shape) for total in sums],
        pick,
        step_rate,
        "update_ffn_out",
    )


def pack_kernel(core_ref, w_ref, g_ref, out_ref):
    pairs = w_ref.shape[2] // PAIR
    for pair in range(pairs):
        for kind in range(3):
            start = (pair * 3 + kind) * PAIR
            piece = w_ref[kind, :, pair * PAIR : (pair + 1) * PAIR]
            out_ref[:, start : start + PAIR] = piece.astype(low)
    start = 3 * pairs * PAIR
    out_ref[:, start : start + pairs * PAIR] = w_ref[3].astype(low)
    start += pairs * PAIR
    out_ref[:, start:] = g_ref[...].astype(low)


def pack_attention(core, weights, gains):
    _, shard, width = weights.shape
    half = width // 2
    gain_columns = jnp.pad(gains.T, ((0, 0), (0, HEAD_DIM - 3)))
    columns = 4 * half + HEAD_DIM
    return pl.pallas_call(
        pack_kernel,
        grid_spec=pltpu.PrefetchScalarGridSpec(
            num_scalar_prefetch=1,
            grid=(1,),
            in_specs=[
                pl.BlockSpec((4, shard, half), lambda j, core: (0, 0, core[0])),
                whole((shard, HEAD_DIM)),
            ],
            out_specs=whole((shard, columns)),
        ),
        out_shape=jax.ShapeDtypeStruct((shard, columns), low),
        name="pack_attention",
    )(core, weights, gain_columns)


RING = 8


def ring_place(index):
    return jnp.where(index % 2 == 0, index // 2, RING - 1 - index // 2)


def ring_member(place):
    place = place % RING
    return jnp.where(place < RING // 2, 2 * place, 2 * RING - 1 - 2 * place)


CYCLE = (0, 2, 4, 6, 7, 5, 3, 1)


def ring_next(tensor):
    replicas = lax.axis_size("dp")
    pairs = []
    for place_of, member in enumerate(CYCLE):
        for replica in range(replicas):
            target = CYCLE[(place_of + (1 if replica % 2 == 0 else -1)) % RING]
            pairs.append((member * replicas + replica, target * replicas + replica))
    return lax.ppermute(tensor, ("fsdp", "dp"), pairs)


def ring_shift(tensor, way):
    pairs = [(member, CYCLE[(at + way) % RING]) for at, member in enumerate(CYCLE)]
    return lax.ppermute(tensor, "fsdp", pairs)


def core_swap(tensor):
    return lax.ppermute(tensor, "dp", [(d, d ^ 1) for d in range(lax.axis_size("dp"))])


def column_swap(tensor):
    return lax.ppermute(tensor, "dp", [(d, d ^ 2) for d in range(lax.axis_size("dp"))])


def pack_all_kernel(core_ref, column_ref, w_ref, up_ref, down_ref, g_ref, out_ref):
    shard = w_ref.shape[1]
    half = w_ref.shape[2]
    for pair in range(half // PAIR):
        for kind in range(3):
            start = (pair * 3 + kind) * PAIR
            piece = w_ref[kind, :, pair * PAIR : (pair + 1) * PAIR]
            out_ref[:, start : start + PAIR] = piece.astype(low)
    out_ref[:, 3 * half : 4 * half] = w_ref[3].astype(low)
    start = 4 * half
    rows = lax.broadcasted_iota(jnp.int32, (HEAD_DIM, shard), 0)
    gains = jnp.where(rows == 0, g_ref[0:1, :], jnp.where(rows == 1, g_ref[1:2, :], g_ref[2:3, :]))
    out_ref[:, start : start + HEAD_DIM] = jnp.where(rows < 3, gains, 0.0).T.astype(low)
    start += HEAD_DIM
    out_ref[:, start : start + up_ref.shape[2]] = up_ref[0].astype(low)
    start += up_ref.shape[2]
    for first, count in down_parts(down_ref.shape[0], shard):
        out_ref[:count, start : start + half] = down_ref[first : first + count, :].astype(low)
        if count < shard:
            out_ref[count:, start : start + half] = jnp.zeros((shard - count, half), low)
        start += half


def down_parts(down_rows, shard):
    return [(start, min(shard, down_rows - start)) for start in range(0, down_rows, shard)]


def pack_all(core, column, weights, up, down, gains):
    _, shard, width = weights.shape
    half = width // 2
    parts = len(down_parts(down.shape[0], shard))
    columns = 4 * half + HEAD_DIM + up.shape[2] // 2 + parts * half
    return pl.pallas_call(
        pack_all_kernel,
        grid_spec=pltpu.PrefetchScalarGridSpec(
            num_scalar_prefetch=2,
            grid=(1,),
            in_specs=[
                pl.BlockSpec((4, shard, half), lambda j, core, column: (0, 0, core[0])),
                pl.BlockSpec(
                    (1, shard, up.shape[2] // 2), lambda j, core, column: (core[0], 0, column[0])
                ),
                pl.BlockSpec((down.shape[0], half), lambda j, core, column: (0, core[0])),
                whole(gains.shape),
            ],
            out_specs=whole((shard, columns)),
        ),
        out_shape=jax.ShapeDtypeStruct((shard, columns), low),
        compiler_params=pltpu.CompilerParams(vmem_limit_bytes=VMEM_BYTES),
        name="pack_all",
    )(core, column, weights, up, down, gains)


def place_kernel(which, kept, shapes, origin_ref, column_ref, *refs):
    pieces, outs, semaphores = refs[: len(which)], refs[-1 - len(kept) : -1], refs[-1]
    targets = dict(zip(kept, outs))
    shard, first, up_columns, down_rows, half = shapes
    copies = []

    def copy(source, target):
        copies.append(pltpu.make_async_copy(source, target, semaphores.at[len(copies)]))

    for piece, (origin, across) in zip(pieces, which):
        owner = origin_ref[origin]
        rows = pl.ds(pl.multiple_of(owner * shard, 16), shard)
        if across:
            copy(piece, targets[1].at[rows, lanes_of(1 - column_ref[0], up_columns)])
            continue
        copy(piece.at[:, pl.ds(0, first)], targets[0].at[rows, :])
        own = targets[1].at[rows, lanes_of(column_ref[0], up_columns)]
        copy(piece.at[:, pl.ds(first, up_columns)], own)
        lane = first + up_columns
        for start, count in down_parts(down_rows, shard):
            target = pl.ds(pl.multiple_of(owner * down_rows + start, 16), count)
            copy(piece.at[pl.ds(0, count), pl.ds(lane, half)], targets[2].at[target, :])
            lane += half
    for one in copies:
        one.start()
    for one in copies:
        one.wait()


def place(origins, column, which, pieces, arrays, kept, shapes):
    anywhere = pl.BlockSpec(memory_space=pl.ANY)
    shard, first, up_columns, down_rows, half = shapes
    kinds = [(RING * shard, first), (RING * shard, 2 * up_columns), (RING * down_rows, half)]
    held = [] if arrays is None else list(arrays)
    size = sum(math.prod(piece.shape) for piece in pieces)
    before = 2 + len(pieces)
    return pl.pallas_call(
        functools.partial(place_kernel, which, kept, shapes),
        grid_spec=pltpu.PrefetchScalarGridSpec(
            num_scalar_prefetch=2,
            grid=(1,),
            in_specs=[whole(piece.shape) for piece in pieces] + [anywhere] * len(held),
            out_specs=[anywhere] * len(kept),
            scratch_shapes=[pltpu.SemaphoreType.DMA((8 * len(pieces),))],
        ),
        out_shape=[jax.ShapeDtypeStruct(kinds[k], pieces[0].dtype) for k in kept],
        input_output_aliases={before + k: k for k in range(len(held))},
        compiler_params=pltpu.CompilerParams(vmem_limit_bytes=VMEM_BYTES),
        cost_estimate=pl.CostEstimate(flops=0, bytes_accessed=8 * size, transcendentals=0),
        name="place",
    )(origins, column, *pieces, *held)


def after(tensor, *others):
    return lax.optimization_barrier((tensor, *others))[0]


def core_way():
    return 1 - 2 * (lax.axis_index("dp") % 2)


def ring_origins():
    steps = jnp.array((0, -1, -2, -3, -4, 1, 2, 3), jnp.int32)
    return ring_member(ring_place(lax.axis_index("fsdp")) + steps + RING).astype(jnp.int32)


class RingSumOverColumns:
    def __init__(self, mine, arrived):
        self.arrays = (mine, arrived)
        place = ring_place(lax.axis_index("fsdp"))
        self.rows = mine.shape[1] // RING
        self.starts = [
            ring_member(place - core_way() * (s + 1) + 2 * RING) * self.rows for s in range(RING)
        ]
        self.sent, self.came, self.totals = [], [], []

    def part(self, side, step):
        shape = (1, self.rows, self.arrays[0].shape[2])
        parts = [
            lax.dynamic_slice(array, (side, self.starts[step], 0), shape)[0]
            for array in self.arrays
        ]
        return parts[0].astype(wide) + parts[1].astype(wide)

    def cross(self):
        self.sent.append(self.part(1, len(self.sent)).astype(low))
        self.came.append(column_swap(self.sent[-1]))

    def term(self):
        step = len(self.totals)
        return self.part(0, step) + self.came[step].astype(wide)

    def begin(self, *others):
        self.came[0] = after(self.came[0], *others) if others else self.came[0]
        self.totals.append(self.term().astype(low))

    def step(self, arriving=()):
        total, ahead = self.totals[-1], self.came[len(self.totals)]
        moved = ring_next(after(total, ahead) if len(self.totals) > 1 else total)
        moved = after(moved, *arriving) if arriving else moved
        self.totals.append((moved.astype(wide) + self.term()).astype(low))

    def last(self):
        return self.totals[-1]


class RingSum:
    def __init__(self, mine, arrived):
        self.mine, self.arrived = mine, arrived
        place = ring_place(lax.axis_index("fsdp"))
        self.owners = [ring_member(place - core_way() * (s + 1) + 2 * RING) for s in range(RING)]
        self.totals = []

    def term(self):
        parts = []
        for own, arrived in zip(self.mine, self.arrived):
            rows = own.shape[0] // RING
            start = self.owners[len(self.totals)] * rows
            part = lax.dynamic_slice_in_dim(own, start, rows, 0).astype(wide)
            parts.append(part + lax.dynamic_slice_in_dim(arrived, start, rows, 0).astype(wide))
        return parts[0] if len(parts) == 1 else jnp.concatenate(parts, axis=0)

    def begin(self, *others):
        if others:
            self.mine = [after(self.mine[0], *others), *self.mine[1:]]
        self.totals.append(self.term().astype(low))

    def step(self, *before, arriving=()):
        total = self.totals[-1]
        moved = ring_next(after(total, *before) if before else total)
        moved = after(moved, *arriving) if arriving else moved
        self.totals.append((moved.astype(wide) + self.term().astype(wide)).astype(low))

    def last(self):
        return self.totals[-1]


def gather_rows(shard):
    mine = lax.all_gather(shard, "fsdp", axis=0, tiled=True)
    return mine, core_swap(mine)


def core_sum(mine, other):
    return (mine.astype(wide) + core_swap(other).astype(wide)).astype(low)


def scatter_rows(both):
    return lax.psum_scatter(both, "fsdp", scatter_dimension=0, tiled=True)


def over_columns(total):
    total = (total.astype(wide) + column_swap(total).astype(wide)).astype(low)
    return total, core_swap(total)


def on_device(
    inputs,
    cotangent,
    lengths,
    attention_weights,
    attention_momentum,
    attention_average,
    ffn_inputs,
    ffn_inputs_momentum,
    ffn_inputs_average,
    ffn_output,
    ffn_output_momentum,
    ffn_output_average,
    gains,
    gains_momentum,
    gains_average,
):
    micro_count, slot, width = inputs.shape
    hidden = ffn_inputs.shape[2]
    shard, down_rows = ffn_inputs.shape[1], ffn_output.shape[0]
    fsdp_size = lax.axis_size("fsdp")
    replicas = lax.axis_size("dp")
    ringed = fsdp_size == RING
    core = lax.axis_index("dp") % 2
    column = lax.axis_index("dp") // 2
    count = micro_count * slot
    half = width // 2
    core_ref = core.astype(jnp.int32).reshape(1)
    other_ref = 1 - core_ref
    column_ref = column.astype(jnp.int32).reshape(1)
    is_first = core == 0

    rows = inputs.reshape(count, width)
    positions = jnp.arange(slot, dtype=jnp.int32)
    valid = (positions[None, :] < lengths).astype(wide).reshape(count, 1)
    errors = (cotangent.reshape(count, width).astype(wide) * valid).astype(low)

    if ringed:
        origins = ring_origins()
        first = 4 * half + HEAD_DIM
        shapes = (shard, first, hidden // 2, down_rows, half)
        packed = pack_all(
            core_ref, column_ref, attention_weights, ffn_inputs, ffn_output, gains
        )
        wholes, there, which_there = None, [], []
        here, which = [packed], [(0, False)]
        for step in range(1, 6):
            if step <= 3:
                onward = [ring_shift(here[0], 1), ring_shift(here[-1], -1)]
            elif step == 4:
                onward = [ring_next(jnp.where(is_first, *here))]
            across = [column_swap(piece[:, first : first + hidden // 2]) for piece in here]
            wholes = place(
                origins, column_ref, which + which_there, here + there, wholes, (0, 1, 2), shapes
            )
            if step == 5:
                break
            extra = [errors, valid] if step == 2 else []
            tied = list(lax.optimization_barrier((*onward, *across, *wholes, *extra)))
            here, rest = tied[: len(onward)], tied[len(onward) :]
            there, wholes = rest[: len(across)], rest[len(across) : len(across) + 3]
            which_there = [(origin, True) for origin, _ in which]
            which = [(origin, False) for origin in [step, step + 4][: len(onward)]]
        w_a = (wholes[0], core_swap(wholes[0]))
    else:
        w_a = gather_rows(pack_attention(core_ref, attention_weights, gains))
        w_gu = gather_rows(
            lax.dynamic_index_in_dim(ffn_inputs, core, 0, keepdims=False).astype(low)
        )
        w_d = gather_rows(lax.dynamic_slice_in_dim(ffn_output, core * half, half, 1).astype(low))
    mixed_mine, *kept_mine, gains8 = mixer_forward(core_ref, rows, w_a[0], slot)
    if ringed:
        (across,) = lax.optimization_barrier((*across, mixed_mine, w_a[1]))[:1]
        (w_gu_mine,) = place(origins, column_ref, [(4, True)], [across], [wholes[1]], (1,), shapes)
        wholes = [wholes[0], w_gu_mine, wholes[2]]
        rows = after(rows, *wholes[1:])
        w_gu, w_d = [(array, core_swap(array)) for array in wholes[1:]]
    mixed_other, *rest = mixer_forward(
        other_ref, rows, w_a[1], slot, (gains8, mixed_mine, w_a[0])
    )
    kept_other, (x1, h2, h2t, h1t) = rest[:4], rest[4:]
    owners = (fsdp_size, down_rows + shard, down_rows) if ringed else None
    places = jnp.concatenate([core_ref, column_ref])
    *grad_gu, gd_mine, gd_other, output, d_x1, d_mixed, go_mine, go_other = ffn(
        places, h2, h2t, errors, w_gu, w_d, x1, (mixed_mine, mixed_other), w_a, valid, gains8, owners
    )

    gm, gu = grad_gu
    arrived_gu = core_swap(gu)
    if ringed:
        mine_do, arrived_do = [gd_mine], [core_swap(gd_other)]
    else:
        mine_do, arrived_do = [gd_mine, go_mine], [core_swap(gd_other), core_swap(go_other)]
    by_owner = (fsdp_size * 2 * shard, 3 * PAIR)
    d_pre = []
    for call in range(4):
        from_half, kept = (other_ref, kept_other) if call < 2 else (core_ref, kept_mine)
        if ringed and call == 1:
            sum_gu = RingSumOverColumns(after(gm, d_pre[0]), arrived_gu)
            sum_gu.cross()
            sum_gu.cross()
            h1t = after(h1t, *sum_gu.sent)
        elif ringed and call > 1:
            sum_gu.cross()
            ahead = [sum_gu.came[2]] if call == 3 else []
            h1t = after(h1t, sum_gu.last(), sum_do.last(), sum_gu.sent[-1], *ahead)
        grads = mixer_backward(
            from_half,
            h1t,
            gains8,
            kept,
            d_mixed,
            slot,
            shard,
            (call % 2,),
            grads if call % 2 else (),
        )
        d_pre.append(grads[1])
        if call == 1:
            grad_other = grads[0]
            if ringed:
                sum_do = RingSum(mine_do, arrived_do)
                sum_do.begin(d_pre[-1])
                sum_gu.begin(d_pre[-1])
                grad_other = after(grad_other, sum_gu.last(), sum_do.last())
            arrived_qfv = [core_swap(grad_other.reshape(by_owner))]
        elif ringed and call > 1:
            sum_do.step(arriving=(d_pre[-1],))
            sum_gu.step(arriving=(d_pre[-1],))
    mine_qfv = [grads[0].reshape(by_owner)]

    def finish_input(*others):
        late = after(d_pre[3], *others) if others else d_pre[3]
        return input_gradient(rows, gains8, (late, d_pre[1]), w_a, d_x1)

    if ringed:
        sum_qfv = RingSum(mine_qfv, arrived_qfv)
        sum_qfv.begin()
        input_grad = None
        for step in range(1, RING - 1):
            if len(sum_gu.came) < RING:
                sum_gu.cross()
            if len(sum_gu.totals) < RING:
                sum_do.step(*{1: [sum_gu.last()], 4: [input_grad]}.get(step, []))
                sum_gu.step()
            sum_qfv.step()
            if step == 2:
                input_grad = finish_input(sum_qfv.last())
        total_gu, total_do = sum_gu.last(), sum_do.last()
    else:
        both = (gm.astype(wide) + arrived_gu.astype(wide)).astype(low)
        here = (both[0].astype(wide) + column_swap(both[1]).astype(wide)).astype(low)
        total_gu = scatter_rows(here)
        total_do = jnp.concatenate(
            [
                scatter_rows((own.astype(wide) + came.astype(wide)).astype(low))
                for own, came in zip(mine_do, arrived_do)
            ],
            axis=0,
        )
        total_qfv = scatter_rows(
            (mine_qfv[0].astype(wide) + arrived_qfv[0].astype(wide)).astype(low)
        )
        input_grad = finish_input()
    scale_rows = 1.0 / math.sqrt(count * fsdp_size * replicas)
    matrix_step = matrix_rate * scale_rows
    attention_state = (attention_weights, attention_momentum, attention_average)
    ffn_in_state = (ffn_inputs, ffn_inputs_momentum, ffn_inputs_average)
    ffn_out_state = (ffn_output, ffn_output_momentum, ffn_output_average)
    sum_do = over_columns(total_do)
    there = column_swap(total_gu)
    even = jnp.where(column == 0, total_gu, there)
    odd = jnp.where(column == 0, there, total_gu)
    sum_gu = (even, odd), (core_swap(even), core_swap(odd))
    *new_out, _ = update_ffn_out(core_ref, ffn_out_state, sum_do, matrix_step)
    *new_in, dots_up = update_ffn_in(core_ref, ffn_in_state, sum_gu[0], matrix_step, ())
    *new_in, dots_gate = update_ffn_in(other_ref, ffn_in_state, sum_gu[1], matrix_step, new_in)
    if ringed:
        sum_qfv.step(arriving=(new_out[0],))
        total_qfv = sum_qfv.last()
    there = after(column_swap(total_qfv), new_in[0])
    sum_qfv = (total_qfv.astype(wide) + there.astype(wide)).astype(low)
    *own, dots_own = update_attention(
        core_ref, core_ref, attention_state, sum_qfv, sum_do[0], matrix_step, ()
    )
    theirs = after(core_swap(sum_qfv), own[0])
    *new_attention, dots_theirs = update_attention(
        core_ref, other_ref, attention_state, theirs, sum_do[1], matrix_step, own
    )
    dots = jnp.sum(dots_own + dots_theirs, axis=2)
    row_sums = jnp.stack([dots[0] + dots[1] + dots[2], dots[3], jnp.sum(dots_up + dots_gate, axis=(0, 2))])
    sum_gains = row_sums / gains.astype(low).astype(wide)
    return (
        output.reshape(micro_count, slot, width),
        input_grad.reshape(micro_count, slot, width),
        *new_attention,
        *new_in,
        *new_out,
        *update(gains, gains_momentum, gains_average, sum_gains, gain_rate * scale_rows),
    )


def solution(mesh):
    rows_split = P(None, ("fsdp", "dp"), None)
    middle_split = P(None, "fsdp", None)
    first_split = P("fsdp", None)
    gains_split = P(None, "fsdp")
    in_specs = (
        (rows_split, rows_split, P(None, ("fsdp", "dp")))
        + (middle_split,) * 6
        + (first_split,) * 3
        + (gains_split,) * 3
    )
    out_specs = (
        (rows_split, rows_split)
        + (middle_split,) * 6
        + (first_split,) * 3
        + (gains_split,) * 3
    )
    return jax.shard_map(
        on_device, mesh=mesh, in_specs=in_specs, out_specs=out_specs, check_vma=False
    )
```

```python
import functools
import math

import jax
import jax.numpy as jnp
from jax import lax
from jax.experimental import pallas as pl
from jax.experimental.pallas import tpu as pltpu
from jax.sharding import PartitionSpec as P

HEAD_DIM = 128
PAIR = 2 * HEAD_DIM

lower_bound = 0.9
momentum_decay = 0.9
average_decay = 0.7
weight_decay = 0.0005
matrix_rate = 0.03
gain_rate = 0.1
low = jnp.bfloat16
wide = jnp.float32
TILE_F = 256
ROWS = 256
VMEM_BYTES = 60 * 1024 * 1024


def mm(left, right):
    return jnp.dot(left, right, preferred_element_type=wide)


def mm_nt(left, right):
    return lax.dot_general(left, right, (((1,), (1,)), ((), ())), preferred_element_type=wide)


def mm_tn(left, right):
    return lax.dot_general(left, right, (((0,), (0,)), ((), ())), preferred_element_type=wide)


def sigmoid(u):
    return 0.5 * jnp.tanh(0.5 * u) + 0.5


def whole(shape):
    return pl.BlockSpec(shape, lambda *_: (0,) * len(shape), pipeline_mode=pl.Buffered(1))


def split_sum(ones_matrix, tensor):
    high = tensor.astype(low)
    rest = (tensor - high.astype(wide)).astype(low)
    return mm(ones_matrix, high) + mm(ones_matrix, rest)


def causal_mask(length, lower):
    rows = lax.broadcasted_iota(jnp.int32, (length, length), 0)
    columns = lax.broadcasted_iota(jnp.int32, (length, length), 1)
    return rows >= columns if lower else rows <= columns


def triangle(length, lower):
    return causal_mask(length, lower).astype(wide).astype(low)


def decay_parts(f_pre, lower_ones):
    share = sigmoid(f_pre)
    gate = lower_bound + (1.0 - lower_bound) * share
    keys_in = (1.0 - lower_bound) * (1.0 - share)
    cumulative = split_sum(lower_ones, jnp.log(gate))
    middle_row = cumulative.shape[0] // 2
    cumulative = cumulative - cumulative[middle_row : middle_row + 1, :]
    return share, gate, keys_in, cumulative


def first_norm(x_ref, gain_row):
    rows = x_ref[...].astype(wide)
    scale = lax.rsqrt(jnp.mean(rows * rows, axis=-1, keepdims=True) + 1e-06)
    return rows * scale, scale


def lanes_of(half, size):
    return pl.ds(pl.multiple_of(half * size, size), size)


def mixer_forward_first_kernel(
    slot, half_ref, x_ref, w_ref, columns_ref, on_ref, q_ref, f_ref, v_ref, o_ref, g_ref, h_s
):
    @pl.when(pl.program_id(0) == 0)
    def _():
        g_ref[...] = columns_ref[...].astype(wide).T[: g_ref.shape[0], :]

    mixer_forward_kernel(
        slot, half_ref, x_ref, w_ref, g_ref, on_ref, q_ref, f_ref, v_ref, o_ref, h_s
    )


def mixer_forward_kernel(
    slot, half_ref, x_ref, w_ref, g_ref, on_ref, q_ref, f_ref, v_ref, o_ref, h_s
):
    @pl.when(pl.program_id(0) == 0)
    def _():
        normed, _ = first_norm(x_ref, None)
        h_s[...] = (normed * g_ref[0:1, :]).astype(low)

    gain_o = g_ref[1:2, lanes_of(half_ref[0] * pl.num_programs(0) + pl.program_id(0), PAIR)]
    pre = mm(h_s[...], w_ref[...])
    q_ref[...] = pre[:, :PAIR]
    f_ref[...] = pre[:, PAIR : 2 * PAIR]
    v_ref[...] = pre[:, 2 * PAIR :].astype(low)
    lower_ones = triangle(slot, True)
    causal = causal_mask(slot, True)
    for sequence in range(x_ref.shape[0] // slot):
        rows = slice(sequence * slot, (sequence + 1) * slot)
        q_pre = q_ref[rows, :]
        _, _, keys_in, cumulative = decay_parts(f_ref[rows, :], lower_ones)
        grown = jnp.exp(-cumulative)
        decayed_q = (q_pre * sigmoid(q_pre) * jnp.exp(cumulative)).astype(low)
        grown_k = (keys_in * grown).astype(low)
        values = v_ref[rows, :]
        for head in range(2):
            lanes = slice(head * HEAD_DIM, (head + 1) * HEAD_DIM)
            scores = mm_nt(decayed_q[:, lanes], grown_k[:, lanes])
            out = mm(jnp.where(causal, scores, 0.0).astype(low), values[:, lanes])
            scale = lax.rsqrt(jnp.mean(out * out, axis=-1, keepdims=True) + 1e-05)
            o_ref[rows, lanes] = out.astype(low)
            on_ref[rows, lanes] = (out * scale * gain_o[:, lanes]).astype(low)


def mixer_forward_last_kernel(
    slot,
    half_ref,
    x_ref,
    w_ref,
    g_ref,
    before_ref,
    woo_ref,
    wom_ref,
    on_ref,
    q_ref,
    f_ref,
    v_ref,
    o_ref,
    x1_ref,
    h2_ref,
    h2t_ref,
    h1t_ref,
    h_s,
    on_s,
):
    step = pl.program_id(0)
    half = before_ref.shape[1]
    mixer_forward_kernel(
        slot, half_ref, x_ref, w_ref, g_ref, on_ref, q_ref, f_ref, v_ref, o_ref, h_s
    )
    on_s[:, lanes_of(half_ref[0] * pl.num_programs(0) + step, PAIR)] = on_ref[...]

    @pl.when(step == pl.num_programs(0) - 1)
    def _():
        here = lanes_of(half_ref[0], half)
        there = lanes_of(1 - half_ref[0], half)
        on_s[:, there] = before_ref[...]
        h1t_ref[...] = h_s[...].astype(wide).T.astype(low)
        x1_ref[:, here] = x_ref[:, here].astype(wide) + mm(on_s[...], woo_ref[...])
        x1_ref[:, there] = x_ref[:, there].astype(wide) + mm(on_s[...], wom_ref[...])
        x1 = x1_ref[...]
        scale = lax.rsqrt(jnp.mean(x1 * x1, axis=-1, keepdims=True) + 1e-06)
        normed = x1 * scale * g_ref[2:3, :]
        h2_ref[...] = normed.astype(low)
        h2t_ref[...] = normed.T.astype(low)


def mixer_forward(half, rows, weights, slot, ending=None):
    count, width = rows.shape
    pairs = width // PAIR // 2
    by_pair = pl.BlockSpec((count, PAIR), lambda j, _: (0, j))
    struct = jax.ShapeDtypeStruct
    shape = lambda kind: struct((count, width // 2), kind)
    in_specs = [whole(rows.shape), pl.BlockSpec((width, 3 * PAIR), lambda j, _: (0, j))]
    operands = [half, rows, weights]
    out_specs = [by_pair] * 5
    out_shape = [shape(low), shape(wide), shape(wide), shape(low), shape(low)]
    scratch = [pltpu.VMEM((count, width), low)]
    if ending is None:
        kernel = mixer_forward_first_kernel
        last = weights.shape[1] // HEAD_DIM - 1
        in_specs += [pl.BlockSpec((width, HEAD_DIM), lambda j, _: (0, last))]
        operands += [weights]
        out_specs += [whole((8, width))]
        out_shape += [struct((8, width), wide)]
    if ending is not None:
        kernel = mixer_forward_last_kernel
        out_weights = pl.BlockSpec((width, width // 2), lambda j, _: (0, 3))
        in_specs += [whole(ending[0].shape), whole((count, width // 2)), out_weights, out_weights]
        operands += [ending[0], ending[1], weights, ending[2]]
        out_specs += [whole((count, width))] * 2 + [whole((width, count))] * 2
        out_shape += [
            struct((count, width), wide),
            struct((count, width), low),
            struct((width, count), low),
            struct((width, count), low),
        ]
        scratch += [pltpu.VMEM((count, width), low)]
    return pl.pallas_call(
        functools.partial(kernel, slot),
        grid_spec=pltpu.PrefetchScalarGridSpec(
            num_scalar_prefetch=1,
            grid=(pairs,),
            in_specs=in_specs,
            out_specs=out_specs,
            scratch_shapes=scratch,
        ),
        out_shape=out_shape,
        compiler_params=pltpu.CompilerParams(vmem_limit_bytes=VMEM_BYTES),
        cost_estimate=pl.CostEstimate(
            flops=count * width * 4 * width + 10 * count * slot * width,
            bytes_accessed=count * width * 12 + width * width * 4,
            transcendentals=count * width * 3,
        ),
        name="mixer_forward",
    )(*operands)


def store_down(out_ref, tile, owners):
    if owners is None:
        out_ref[...] = tile
        return
    _, stride, down_rows = owners
    block = math.gcd(down_rows, tile.shape[0])
    first = pl.program_id(0) * (tile.shape[0] // block)
    for part in range(tile.shape[0] // block):
        owner = (first + part) // (down_rows // block)
        inside = (first + part) % (down_rows // block)
        start = pl.multiple_of(owner * stride + inside * block, block)
        out_ref[pl.ds(start, block), :] = tile[part * block : (part + 1) * block, :]


def ffn_tile(owners, core_ref, refs, grads, acc_ref, dh_ref, scratch):
    h_ref, ht_ref, e_ref, wm_ref, wu_ref, wdm_ref, wdo_ref = refs
    gm_ref, gu_ref, gdm_ref, gdo_ref = grads
    gu_w, down_w, gu_g, down_g, mid_s, d_pre_s = scratch
    half, tile = wdm_ref.shape[1], wm_ref.shape[1]
    mine, other = lanes_of(core_ref[0], half), lanes_of(1 - core_ref[0], half)
    kind, kind_other = lanes_of(core_ref[0], tile), lanes_of(1 - core_ref[0], tile)
    gu_w[:, kind] = wm_ref[...]
    gu_w[:, kind_other] = wu_ref[...]
    down_w[:, mine] = wdm_ref[...]
    down_w[:, other] = wdo_ref[...]
    count = h_ref.shape[0]
    for start in range(0, count, ROWS):
        rows = slice(start, start + ROWS)
        pre = mm(h_ref[rows, :], gu_w[...])
        d_mid = mm_nt(e_ref[rows, :], down_w[...])
        a, b = pre[:, :tile], pre[:, tile:]
        share = sigmoid(a)
        swish = a * share
        mid_s[rows, :] = (swish * b).astype(low)
        d_pre_s[rows, :tile] = (d_mid * b * (share + swish * (1.0 - share))).astype(low)
        d_pre_s[rows, tile:] = (d_mid * swish).astype(low)
    down_g[...] = mm_tn(mid_s[...], e_ref[...]).astype(low)
    acc_ref[...] += mm(mid_s[...], down_w[...])
    dh_ref[...] += mm_nt(d_pre_s[...], gu_w[...])
    gu_g[...] = mm(ht_ref[...], d_pre_s[...]).astype(low)
    blocks = tile // HEAD_DIM
    for side, block in enumerate((core_ref[1], 1 - core_ref[1])):
        gm_ref[side] = gu_g[:, lanes_of(core_ref[0] * blocks + block, HEAD_DIM)]
        gu_ref[side] = gu_g[:, lanes_of((1 - core_ref[0]) * blocks + block, HEAD_DIM)]
    store_down(gdm_ref, down_g[:, mine], owners)
    store_down(gdo_ref, down_g[:, other], owners)


def ffn_kernel(
    owners,
    core_ref,
    h_ref,
    ht_ref,
    e_ref,
    wm_ref,
    wu_ref,
    wdm_ref,
    wdo_ref,
    x1_ref,
    onm_ref,
    ono_ref,
    wom_ref,
    woo_ref,
    m_ref,
    g_ref,
    gm_ref,
    gu_ref,
    gdm_ref,
    gdo_ref,
    out_ref,
    dh_s,
    don_ref,
    gom_ref,
    goo_ref,
    on_s,
    acc_s,
    *scratch,
):
    @pl.when(pl.program_id(0) == 0)
    def _():
        acc_s[...] = x1_ref[...]
        dh_s[...] = jnp.zeros_like(dh_s)

    grads = (gm_ref, gu_ref, gdm_ref, gdo_ref)
    refs = (h_ref, ht_ref, e_ref, wm_ref, wu_ref, wdm_ref, wdo_ref)
    ffn_tile(owners, core_ref, refs, grads, acc_s, dh_s, scratch)

    @pl.when(pl.program_id(0) == pl.num_programs(0) - 1)
    def _():
        half = onm_ref.shape[1]
        mine = lanes_of(core_ref[0], half)
        other = lanes_of(1 - core_ref[0], half)
        out_ref[...] = (acc_s[...] * m_ref[...]).astype(low)
        x1 = x1_ref[...]
        scale = lax.rsqrt(jnp.mean(x1 * x1, axis=-1, keepdims=True) + 1e-06)
        normed = x1 * scale
        d_h2 = dh_s[...]
        scaled = d_h2 * g_ref[2:3, :]
        d_x1 = e_ref[...].astype(wide) + scale * (
            scaled - normed * jnp.mean(scaled * normed, axis=-1, keepdims=True)
        )
        dh_s[...] = d_x1
        on_s[...] = d_x1.astype(low)
        d_mixed = mm_nt(on_s[:, mine], wom_ref[...]) + mm_nt(on_s[:, other], woo_ref[...])
        don_ref[...] = d_mixed.astype(low)
        for columns, g_down_ref, g_ref_o in ((mine, gdm_ref, gom_ref), (other, gdo_ref, goo_ref)):
            d_1 = on_s[:, columns]
            for which, on_ref in ((core_ref[0], onm_ref), (1 - core_ref[0], ono_ref)):
                grad_o = mm_tn(on_ref[...], d_1).astype(low)
                if owners is None:
                    g_ref_o[pl.ds(pl.multiple_of(which * half, half), half), :] = grad_o
                    continue
                count, stride, down_rows = owners
                rows = stride - down_rows
                for part in range(half // rows):
                    owner = which * (count // 2) + part
                    start = pl.multiple_of(owner * stride + down_rows, math.gcd(stride, down_rows))
                    g_down_ref[pl.ds(start, rows), :] = grad_o[part * rows : (part + 1) * rows, :]


def ffn(core, h2, h2t, errors, w_gu, w_d, x1, mixed, w_a, mask, gains8, owners):
    count, width = h2.shape
    half = width // 2
    hidden = w_gu[0].shape[1]
    full = whole((count, width))
    half_full = whole((count, half))
    square = whole((width, half))
    in_tile = pl.BlockSpec((width, TILE_F), lambda j, _: (0, j))
    out_tile = pl.BlockSpec((TILE_F, half), lambda j, _: (j, 0))
    out_weights = pl.BlockSpec((width, half), lambda j, _: (0, 3), pipeline_mode=pl.Buffered(1))
    down_spec, down_shape, out_spec, out_shape = out_tile, (hidden, half), square, (width, half)
    if owners is not None:
        down_shape, out_shape = (owners[0] * owners[1], half), (16, half)
        down_spec, out_spec = whole(down_shape), whole(out_shape)
    struct = jax.ShapeDtypeStruct
    return pl.pallas_call(
        functools.partial(ffn_kernel, owners),
        grid_spec=pltpu.PrefetchScalarGridSpec(
            num_scalar_prefetch=1,
            grid=(hidden // TILE_F,),
            in_specs=[full, whole(h2t.shape), full, in_tile, in_tile, out_tile, out_tile]
            + [full, half_full, half_full, out_weights, out_weights]
            + [whole((count, 1)), whole((8, width))],
            out_specs=[pl.BlockSpec((2, width, HEAD_DIM), lambda j, _: (0, 0, j))] * 2
            + [down_spec, down_spec]
            + [full, full, full, out_spec, out_spec],
            scratch_shapes=[
                pltpu.VMEM((count, width), low),
                pltpu.VMEM((count, width), wide),
                pltpu.VMEM((width, 2 * TILE_F), low),
                pltpu.VMEM((TILE_F, width), low),
                pltpu.VMEM((width, 2 * TILE_F), low),
                pltpu.VMEM((TILE_F, width), low),
                pltpu.VMEM((count, TILE_F), low),
                pltpu.VMEM((count, 2 * TILE_F), low),
            ],
        ),
        out_shape=[struct((2, width, hidden // 2), low)] * 2
        + [struct(down_shape, low)] * 2
        + [
            struct((count, width), low),
            struct((count, width), wide),
            struct((count, width), low),
            struct(out_shape, low),
            struct(out_shape, low),
        ],
        compiler_params=pltpu.CompilerParams(vmem_limit_bytes=VMEM_BYTES),
        cost_estimate=pl.CostEstimate(
            flops=16 * count * width * hidden,
            bytes_accessed=count * width * 20 + width * hidden * 12,
            transcendentals=count * hidden,
        ),
        name="ffn",
    )(core, h2, h2t, errors, *w_gu, *w_d, x1, *mixed, *w_a, mask, gains8)


def mixer_backward_kernel(
    slot,
    per_half,
    first,
    half_ref,
    ht_ref,
    g_ref,
    q_ref,
    f_ref,
    v_ref,
    o_ref,
    don_ref,
    *outs,
):
    grad_ref, dpre_ref = outs[-2:]
    gain_o = g_ref[1:2, lanes_of(half_ref[0] * per_half + first + pl.program_id(0), PAIR)]
    lower_ones = triangle(slot, True)
    upper_ones = triangle(slot, False)
    causal_t = causal_mask(slot, False)
    for sequence in range(q_ref.shape[0] // slot):
        rows = slice(sequence * slot, (sequence + 1) * slot)
        d_on = don_ref[rows, :].astype(wide)
        out = o_ref[rows, :].astype(wide)
        d_out_parts = []
        for head in range(2):
            lanes = slice(head * HEAD_DIM, (head + 1) * HEAD_DIM)
            out_h, d_on_h = out[:, lanes], d_on[:, lanes]
            scale = lax.rsqrt(jnp.mean(out_h * out_h, axis=-1, keepdims=True) + 1e-05)
            normed = out_h * scale
            scaled = d_on_h * gain_o[:, lanes]
            inner = jnp.mean(scaled * normed, axis=-1, keepdims=True)
            d_out_parts.append((scale * (scaled - normed * inner)).astype(low))

        q_pre = q_ref[rows, :]
        share, gate, keys_in, cumulative = decay_parts(f_ref[rows, :], lower_ones)
        grown = jnp.exp(-cumulative)
        shrunk = jnp.exp(cumulative)
        q_share = sigmoid(q_pre)
        decayed_q = (q_pre * q_share * shrunk).astype(low)
        grown_k = (keys_in * grown).astype(low)
        values = v_ref[rows, :]
        dq_parts, dk_parts, dv_parts = [], [], []
        for head in range(2):
            lanes = slice(head * HEAD_DIM, (head + 1) * HEAD_DIM)
            q_h, k_h, v_h = decayed_q[:, lanes], grown_k[:, lanes], values[:, lanes]
            d_out = d_out_parts[head]
            scores = jnp.where(causal_t, mm_nt(k_h, q_h), 0.0).astype(low)
            d_scores = jnp.where(causal_t, mm_nt(v_h, d_out), 0.0).astype(low)
            dv_parts.append(mm(scores, d_out))
            dk_parts.append(mm(d_scores, q_h))
            dq_parts.append(mm_tn(d_scores, k_h))
        d_decayed = jnp.concatenate(dq_parts, axis=1)
        d_grown = jnp.concatenate(dk_parts, axis=1)
        d_value = jnp.concatenate(dv_parts, axis=1)
        d_cumulative = decayed_q.astype(wide) * d_decayed - grown_k.astype(wide) * d_grown
        d_log = split_sum(upper_ones, d_cumulative)
        d_query = d_decayed * shrunk
        d_key = d_grown * grown
        d_q_pre = d_query * q_share * (1.0 + q_pre * (1.0 - q_share))
        d_f_pre = (1.0 - lower_bound) * (d_log / gate - d_key) * share * (1.0 - share)
        dpre_ref[rows, :PAIR] = d_q_pre.astype(low)
        dpre_ref[rows, PAIR : 2 * PAIR] = d_f_pre.astype(low)
        dpre_ref[rows, 2 * PAIR :] = d_value.astype(low)

    grad = mm(ht_ref[...], dpre_ref[...]).astype(low)
    grad_ref[...] = grad.reshape(grad_ref.shape)


def mixer_backward(half, h1t, gains8, kept, d_mixed, slot, shard, pairs=(0, 1), before=()):
    width, count = h1t.shape
    per_half = width // PAIR // 2
    first = pairs[0]
    by_pair = pl.BlockSpec((count, PAIR), lambda j, _: (0, first + j))
    from_whole = pl.BlockSpec((count, PAIR), lambda j, half: (0, half[0] * per_half + first + j))
    struct = jax.ShapeDtypeStruct
    return pl.pallas_call(
        functools.partial(mixer_backward_kernel, slot, per_half, first),
        grid_spec=pltpu.PrefetchScalarGridSpec(
            num_scalar_prefetch=1,
            grid=(len(pairs),),
            in_specs=[whole((width, count)), whole(gains8.shape)]
            + [by_pair] * 4
            + [from_whole]
            + [pl.BlockSpec(memory_space=pl.ANY)] * len(before),
            out_specs=[
                pl.BlockSpec(
                    (width // shard, 1, shard, 3 * PAIR), lambda j, _: (0, first + j, 0, 0)
                ),
                pl.BlockSpec((count, 3 * PAIR), lambda j, _: (0, first + j)),
            ],
        ),
        out_shape=[
            struct((width // shard, per_half, shard, 3 * PAIR), low),
            struct((count, per_half * 3 * PAIR), low),
        ],
        input_output_aliases={8 + k: k for k in range(len(before))},
        compiler_params=pltpu.CompilerParams(vmem_limit_bytes=VMEM_BYTES),
        cost_estimate=pl.CostEstimate(
            flops=len(pairs) * (count * width * 6 * PAIR + 20 * count * slot * PAIR),
            bytes_accessed=len(pairs) * (count * width * 5 + width * PAIR * 6),
            transcendentals=len(pairs) * count * PAIR * 6,
        ),
        name="mixer_backward",
    )(half, h1t, gains8, *kept, d_mixed, *before)


def input_gradient_rows_kernel(
    x_ref, g_ref, dm_ref, do_ref, wm_ref, wo_ref, dx1_ref, dx_ref
):
    d_h1 = mm_nt(dm_ref[...], wm_ref[...]) + mm_nt(do_ref[...], wo_ref[...])
    normed, scale = first_norm(x_ref, None)
    scaled = d_h1 * g_ref[0:1, :]
    dx_ref[...] = dx1_ref[...] + scale * (
        scaled - normed * jnp.mean(scaled * normed, axis=-1, keepdims=True)
    )


def input_gradient(rows, gains8, d_pre, weights, d_x1):
    count, width = rows.shape
    block = count // 2
    columns = d_pre[0].shape[1]
    by_rows = lambda columns: pl.BlockSpec((block, columns), lambda j: (j, 0))
    weight_spec = pl.BlockSpec((width, columns), lambda j: (0, 0), pipeline_mode=pl.Buffered(1))
    return pl.pallas_call(
        input_gradient_rows_kernel,
        grid=(count // block,),
        in_specs=[by_rows(width), whole(gains8.shape)]
        + [by_rows(columns)] * 2
        + [weight_spec] * 2
        + [by_rows(width)],
        out_specs=by_rows(width),
        out_shape=jax.ShapeDtypeStruct((count, width), wide),
        compiler_params=pltpu.CompilerParams(vmem_limit_bytes=VMEM_BYTES),
        cost_estimate=pl.CostEstimate(
            flops=6 * count * width * width,
            bytes_accessed=count * width * 16 + width * width * 6,
            transcendentals=0,
        ),
        name="input_gradient",
    )(rows, gains8, *d_pre, *weights, d_x1)


def update(weight, momentum, average, gradient, step_rate):
    new_momentum = momentum_decay * momentum + gradient
    direction = gradient + momentum_decay * new_momentum + weight_decay * weight
    new_weight = weight - step_rate * direction
    new_average = average_decay * average + (1.0 - average_decay) * new_weight
    return (new_momentum, new_average, new_weight)


def update_kernel(pick, step_rate, sum_count, core_ref, w_ref, m_ref, a_ref, *refs):
    sums, outs, dots_ref = refs[:sum_count], refs[-4:-1], refs[-1]
    weight = w_ref[...]
    gradient = pick(core_ref[0], *[s[...] for s in sums]).astype(wide).reshape(weight.shape)
    results = update(weight, m_ref[...], a_ref[...], gradient, step_rate)
    for out, result in zip(outs, results):
        out[...] = result
    product = weight.astype(low).astype(wide) * gradient
    total = product[..., :HEAD_DIM]
    for start in range(HEAD_DIM, product.shape[-1], HEAD_DIM):
        total = total + product[..., start : start + HEAD_DIM]
    dots_ref[...] = total.reshape(dots_ref.shape)


def update_call(
    core, state, sums, grid, state_spec, sum_specs, pick, step_rate, name, before=()
):
    struct = jax.ShapeDtypeStruct(state[0].shape, wide)
    size = math.prod(state[0].shape)
    rows = state_spec.block_shape[-2]
    steps = math.prod(grid)
    tail = grid[1:]

    def dots_index(*indices):
        place = indices[0]
        for length, index in zip(tail, indices[1:]):
            place = place * length + index
        return (place, 0, 0)

    return pl.pallas_call(
        functools.partial(update_kernel, pick, step_rate, len(sums)),
        grid_spec=pltpu.PrefetchScalarGridSpec(
            num_scalar_prefetch=1,
            grid=grid,
            in_specs=[state_spec] * 3
            + sum_specs
            + [pl.BlockSpec(memory_space=pl.ANY)] * len(before),
            out_specs=[state_spec] * 3 + [pl.BlockSpec((1, rows, HEAD_DIM), dots_index)],
        ),
        out_shape=[struct] * 3 + [jax.ShapeDtypeStruct((steps, rows, HEAD_DIM), wide)],
        input_output_aliases={4 + len(sums) + k: k for k in range(len(before))},
        compiler_params=pltpu.CompilerParams(vmem_limit_bytes=VMEM_BYTES),
        cost_estimate=pl.CostEstimate(flops=12 * size, bytes_accessed=26 * size, transcendentals=0),
        name=name,
    )(core, *state, *sums, *before)


def update_attention(core, half_ref, state, qfv, out, step_rate, before):
    _, shard, width = state[0].shape
    down_rows = out.shape[0] - shard

    def pick(core_index, proj, last):
        gradient = last[down_rows:].astype(wide)
        for kind in range(3):
            parts = [proj[pair * shard :, kind * PAIR :][:shard, :PAIR] for pair in range(2)]
            chosen = jnp.concatenate(parts, axis=1).astype(wide)
            gradient = jnp.where(pl.program_id(0) == kind, chosen, gradient)
        return gradient

    return update_call(
        half_ref,
        state,
        (qfv, out),
        (4,),
        pl.BlockSpec((1, shard, width // 2), lambda kind, half: (kind, 0, half[0])),
        [whole(qfv.shape), whole(out.shape)],
        pick,
        step_rate,
        "update_attention",
        before,
    )


def update_ffn_in(kind_ref, state, totals, step_rate, before):
    _, shard, hidden = state[0].shape

    def pick(_, even, odd):
        blocks = []
        for start in range(0, hidden // 2, HEAD_DIM):
            blocks += [even[:, start : start + HEAD_DIM], odd[:, start : start + HEAD_DIM]]
        return jnp.concatenate(blocks, axis=1)

    return update_call(
        kind_ref,
        state,
        totals,
        (1,),
        pl.BlockSpec((1, shard, hidden), lambda j, kind: (kind[0], 0, 0)),
        [whole(total.shape) for total in totals],
        pick,
        step_rate,
        "update_ffn_in",
        before,
    )


def update_ffn_out(core, state, sums, step_rate):
    shard, width = state[0].shape

    def pick(core_index, mine, other):
        own = pl.program_id(0) == core_index
        return jnp.where(own, mine[:shard].astype(wide), other[:shard].astype(wide))

    return update_call(
        core,
        state,
        sums,
        (2,),
        pl.BlockSpec((shard, width // 2), lambda j, _: (0, j)),
        [whole(total.shape) for total in sums],
        pick,
        step_rate,
        "update_ffn_out",
    )


def pack_kernel(core_ref, w_ref, g_ref, out_ref):
    pairs = w_ref.shape[2] // PAIR
    for pair in range(pairs):
        for kind in range(3):
            start = (pair * 3 + kind) * PAIR
            piece = w_ref[kind, :, pair * PAIR : (pair + 1) * PAIR]
            out_ref[:, start : start + PAIR] = piece.astype(low)
    start = 3 * pairs * PAIR
    out_ref[:, start : start + pairs * PAIR] = w_ref[3].astype(low)
    start += pairs * PAIR
    out_ref[:, start:] = g_ref[...].astype(low)


def pack_attention(core, weights, gains):
    _, shard, width = weights.shape
    half = width // 2
    gain_columns = jnp.pad(gains.T, ((0, 0), (0, HEAD_DIM - 3)))
    columns = 4 * half + HEAD_DIM
    return pl.pallas_call(
        pack_kernel,
        grid_spec=pltpu.PrefetchScalarGridSpec(
            num_scalar_prefetch=1,
            grid=(1,),
            in_specs=[
                pl.BlockSpec((4, shard, half), lambda j, core: (0, 0, core[0])),
                whole((shard, HEAD_DIM)),
            ],
            out_specs=whole((shard, columns)),
        ),
        out_shape=jax.ShapeDtypeStruct((shard, columns), low),
        name="pack_attention",
    )(core, weights, gain_columns)


RING = 8


def ring_place(index):
    return jnp.where(index % 2 == 0, index // 2, RING - 1 - index // 2)


def ring_member(place):
    place = place % RING
    return jnp.where(place < RING // 2, 2 * place, 2 * RING - 1 - 2 * place)


CYCLE = (0, 2, 4, 6, 7, 5, 3, 1)


def ring_next(tensor):
    replicas = lax.axis_size("dp")
    pairs = []
    for place_of, member in enumerate(CYCLE):
        for replica in range(replicas):
            target = CYCLE[(place_of + (1 if replica % 2 == 0 else -1)) % RING]
            pairs.append((member * replicas + replica, target * replicas + replica))
    return lax.ppermute(tensor, ("fsdp", "dp"), pairs)


def ring_shift(tensor, way):
    pairs = [(member, CYCLE[(at + way) % RING]) for at, member in enumerate(CYCLE)]
    return lax.ppermute(tensor, "fsdp", pairs)


def core_swap(tensor):
    return lax.ppermute(tensor, "dp", [(d, d ^ 1) for d in range(lax.axis_size("dp"))])


def column_swap(tensor):
    return lax.ppermute(tensor, "dp", [(d, d ^ 2) for d in range(lax.axis_size("dp"))])


def pack_all_kernel(core_ref, column_ref, w_ref, up_ref, down_ref, g_ref, out_ref):
    shard = w_ref.shape[1]
    half = w_ref.shape[2]
    for pair in range(half // PAIR):
        for kind in range(3):
            start = (pair * 3 + kind) * PAIR
            piece = w_ref[kind, :, pair * PAIR : (pair + 1) * PAIR]
            out_ref[:, start : start + PAIR] = piece.astype(low)
    out_ref[:, 3 * half : 4 * half] = w_ref[3].astype(low)
    start = 4 * half
    rows = lax.broadcasted_iota(jnp.int32, (HEAD_DIM, shard), 0)
    gains = jnp.where(rows == 0, g_ref[0:1, :], jnp.where(rows == 1, g_ref[1:2, :], g_ref[2:3, :]))
    out_ref[:, start : start + HEAD_DIM] = jnp.where(rows < 3, gains, 0.0).T.astype(low)
    start += HEAD_DIM
    out_ref[:, start : start + up_ref.shape[2]] = up_ref[0].astype(low)
    start += up_ref.shape[2]
    for first, count in down_parts(down_ref.shape[0], shard):
        out_ref[:count, start : start + half] = down_ref[first : first + count, :].astype(low)
        if count < shard:
            out_ref[count:, start : start + half] = jnp.zeros((shard - count, half), low)
        start += half


def down_parts(down_rows, shard):
    return [(start, min(shard, down_rows - start)) for start in range(0, down_rows, shard)]


def pack_all(core, column, weights, up, down, gains):
    _, shard, width = weights.shape
    half = width // 2
    parts = len(down_parts(down.shape[0], shard))
    columns = 4 * half + HEAD_DIM + up.shape[2] // 2 + parts * half
    return pl.pallas_call(
        pack_all_kernel,
        grid_spec=pltpu.PrefetchScalarGridSpec(
            num_scalar_prefetch=2,
            grid=(1,),
            in_specs=[
                pl.BlockSpec((4, shard, half), lambda j, core, column: (0, 0, core[0])),
                pl.BlockSpec(
                    (1, shard, up.shape[2] // 2), lambda j, core, column: (core[0], 0, column[0])
                ),
                pl.BlockSpec((down.shape[0], half), lambda j, core, column: (0, core[0])),
                whole(gains.shape),
            ],
            out_specs=whole((shard, columns)),
        ),
        out_shape=jax.ShapeDtypeStruct((shard, columns), low),
        compiler_params=pltpu.CompilerParams(vmem_limit_bytes=VMEM_BYTES),
        name="pack_all",
    )(core, column, weights, up, down, gains)


def place_kernel(which, kept, shapes, origin_ref, column_ref, *refs):
    pieces, outs, semaphores = refs[: len(which)], refs[-1 - len(kept) : -1], refs[-1]
    targets = dict(zip(kept, outs))
    shard, first, up_columns, down_rows, half = shapes
    copies = []

    def copy(source, target):
        copies.append(pltpu.make_async_copy(source, target, semaphores.at[len(copies)]))

    for piece, (origin, across) in zip(pieces, which):
        owner = origin_ref[origin]
        rows = pl.ds(pl.multiple_of(owner * shard, 16), shard)
        if across:
            copy(piece, targets[1].at[rows, lanes_of(1 - column_ref[0], up_columns)])
            continue
        copy(piece.at[:, pl.ds(0, first)], targets[0].at[rows, :])
        own = targets[1].at[rows, lanes_of(column_ref[0], up_columns)]
        copy(piece.at[:, pl.ds(first, up_columns)], own)
        lane = first + up_columns
        for start, count in down_parts(down_rows, shard):
            target = pl.ds(pl.multiple_of(owner * down_rows + start, 16), count)
            copy(piece.at[pl.ds(0, count), pl.ds(lane, half)], targets[2].at[target, :])
            lane += half
    for one in copies:
        one.start()
    for one in copies:
        one.wait()


def place(origins, column, which, pieces, arrays, kept, shapes):
    anywhere = pl.BlockSpec(memory_space=pl.ANY)
    shard, first, up_columns, down_rows, half = shapes
    kinds = [(RING * shard, first), (RING * shard, 2 * up_columns), (RING * down_rows, half)]
    held = [] if arrays is None else list(arrays)
    size = sum(math.prod(piece.shape) for piece in pieces)
    before = 2 + len(pieces)
    return pl.pallas_call(
        functools.partial(place_kernel, which, kept, shapes),
        grid_spec=pltpu.PrefetchScalarGridSpec(
            num_scalar_prefetch=2,
            grid=(1,),
            in_specs=[whole(piece.shape) for piece in pieces] + [anywhere] * len(held),
            out_specs=[anywhere] * len(kept),
            scratch_shapes=[pltpu.SemaphoreType.DMA((8 * len(pieces),))],
        ),
        out_shape=[jax.ShapeDtypeStruct(kinds[k], pieces[0].dtype) for k in kept],
        input_output_aliases={before + k: k for k in range(len(held))},
        compiler_params=pltpu.CompilerParams(vmem_limit_bytes=VMEM_BYTES),
        cost_estimate=pl.CostEstimate(flops=0, bytes_accessed=8 * size, transcendentals=0),
        name="place",
    )(origins, column, *pieces, *held)


def after(tensor, *others):
    return lax.optimization_barrier((tensor, *others))[0]


def core_way():
    return 1 - 2 * (lax.axis_index("dp") % 2)


def ring_origins():
    steps = jnp.array((0, -1, -2, -3, -4, 1, 2, 3), jnp.int32)
    return ring_member(ring_place(lax.axis_index("fsdp")) + steps + RING).astype(jnp.int32)


class RingSumOverColumns:
    def __init__(self, mine, arrived):
        self.arrays = (mine, arrived)
        place = ring_place(lax.axis_index("fsdp"))
        self.rows = mine.shape[1] // RING
        self.starts = [
            ring_member(place - core_way() * (s + 1) + 2 * RING) * self.rows for s in range(RING)
        ]
        self.sent, self.came, self.totals = [], [], []

    def part(self, side, step):
        shape = (1, self.rows, self.arrays[0].shape[2])
        parts = [
            lax.dynamic_slice(array, (side, self.starts[step], 0), shape)[0]
            for array in self.arrays
        ]
        return parts[0].astype(wide) + parts[1].astype(wide)

    def cross(self):
        self.sent.append(self.part(1, len(self.sent)).astype(low))
        self.came.append(column_swap(self.sent[-1]))

    def term(self):
        step = len(self.totals)
        return self.part(0, step) + self.came[step].astype(wide)

    def begin(self, *others):
        self.came[0] = after(self.came[0], *others) if others else self.came[0]
        self.totals.append(self.term().astype(low))

    def step(self, arriving=()):
        total, ahead = self.totals[-1], self.came[len(self.totals)]
        moved = ring_next(after(total, ahead) if len(self.totals) > 1 else total)
        moved = after(moved, *arriving) if arriving else moved
        self.totals.append((moved.astype(wide) + self.term()).astype(low))

    def last(self):
        return self.totals[-1]


class RingSum:
    def __init__(self, mine, arrived):
        self.mine, self.arrived = mine, arrived
        place = ring_place(lax.axis_index("fsdp"))
        self.owners = [ring_member(place - core_way() * (s + 1) + 2 * RING) for s in range(RING)]
        self.totals = []

    def term(self):
        parts = []
        for own, arrived in zip(self.mine, self.arrived):
            rows = own.shape[0] // RING
            start = self.owners[len(self.totals)] * rows
            part = lax.dynamic_slice_in_dim(own, start, rows, 0).astype(wide)
            parts.append(part + lax.dynamic_slice_in_dim(arrived, start, rows, 0).astype(wide))
        return parts[0] if len(parts) == 1 else jnp.concatenate(parts, axis=0)

    def begin(self, *others):
        if others:
            self.mine = [after(self.mine[0], *others), *self.mine[1:]]
        self.totals.append(self.term().astype(low))

    def step(self, *before, arriving=()):
        total = self.totals[-1]
        moved = ring_next(after(total, *before) if before else total)
        moved = after(moved, *arriving) if arriving else moved
        self.totals.append((moved.astype(wide) + self.term().astype(wide)).astype(low))

    def last(self):
        return self.totals[-1]


def gather_rows(shard):
    mine = lax.all_gather(shard, "fsdp", axis=0, tiled=True)
    return mine, core_swap(mine)


def core_sum(mine, other):
    return (mine.astype(wide) + core_swap(other).astype(wide)).astype(low)


def scatter_rows(both):
    return lax.psum_scatter(both, "fsdp", scatter_dimension=0, tiled=True)


def over_columns(total):
    total = (total.astype(wide) + column_swap(total).astype(wide)).astype(low)
    return total, core_swap(total)


def on_device(
    inputs,
    cotangent,
    lengths,
    attention_weights,
    attention_momentum,
    attention_average,
    ffn_inputs,
    ffn_inputs_momentum,
    ffn_inputs_average,
    ffn_output,
    ffn_output_momentum,
    ffn_output_average,
    gains,
    gains_momentum,
    gains_average,
):
    micro_count, slot, width = inputs.shape
    hidden = ffn_inputs.shape[2]
    shard, down_rows = ffn_inputs.shape[1], ffn_output.shape[0]
    fsdp_size = lax.axis_size("fsdp")
    replicas = lax.axis_size("dp")
    ringed = fsdp_size == RING
    core = lax.axis_index("dp") % 2
    column = lax.axis_index("dp") // 2
    count = micro_count * slot
    half = width // 2
    core_ref = core.astype(jnp.int32).reshape(1)
    other_ref = 1 - core_ref
    column_ref = column.astype(jnp.int32).reshape(1)
    is_first = core == 0

    rows = inputs.reshape(count, width)
    positions = jnp.arange(slot, dtype=jnp.int32)
    valid = (positions[None, :] < lengths).astype(wide).reshape(count, 1)
    errors = (cotangent.reshape(count, width).astype(wide) * valid).astype(low)

    if ringed:
        origins = ring_origins()
        first = 4 * half + HEAD_DIM
        shapes = (shard, first, hidden // 2, down_rows, half)
        packed = pack_all(
            core_ref, column_ref, attention_weights, ffn_inputs, ffn_output, gains
        )
        wholes, there, which_there = None, [], []
        here, which = [packed], [(0, False)]
        for step in range(1, 6):
            if step <= 3:
                onward = [ring_shift(here[0], 1), ring_shift(here[-1], -1)]
            elif step == 4:
                onward = [ring_next(jnp.where(is_first, *here))]
            across = [column_swap(piece[:, first : first + hidden // 2]) for piece in here]
            wholes = place(
                origins, column_ref, which + which_there, here + there, wholes, (0, 1, 2), shapes
            )
            if step == 5:
                break
            extra = [errors, valid] if step == 2 else []
            tied = list(lax.optimization_barrier((*onward, *across, *wholes, *extra)))
            here, rest = tied[: len(onward)], tied[len(onward) :]
            there, wholes = rest[: len(across)], rest[len(across) : len(across) + 3]
            which_there = [(origin, True) for origin, _ in which]
            which = [(origin, False) for origin in [step, step + 4][: len(onward)]]
        w_a = (wholes[0], core_swap(wholes[0]))
    else:
        w_a = gather_rows(pack_attention(core_ref, attention_weights, gains))
        w_gu = gather_rows(
            lax.dynamic_index_in_dim(ffn_inputs, core, 0, keepdims=False).astype(low)
        )
        w_d = gather_rows(lax.dynamic_slice_in_dim(ffn_output, core * half, half, 1).astype(low))
    mixed_mine, *kept_mine, gains8 = mixer_forward(core_ref, rows, w_a[0], slot)
    if ringed:
        (across,) = lax.optimization_barrier((*across, mixed_mine, w_a[1]))[:1]
        (w_gu_mine,) = place(origins, column_ref, [(4, True)], [across], [wholes[1]], (1,), shapes)
        wholes = [wholes[0], w_gu_mine, wholes[2]]
        rows = after(rows, *wholes[1:])
        w_gu, w_d = [(array, core_swap(array)) for array in wholes[1:]]
    mixed_other, *rest = mixer_forward(
        other_ref, rows, w_a[1], slot, (gains8, mixed_mine, w_a[0])
    )
    kept_other, (x1, h2, h2t, h1t) = rest[:4], rest[4:]
    owners = (fsdp_size, down_rows + shard, down_rows) if ringed else None
    places = jnp.concatenate([core_ref, column_ref])
    *grad_gu, gd_mine, gd_other, output, d_x1, d_mixed, go_mine, go_other = ffn(
        places, h2, h2t, errors, w_gu, w_d, x1, (mixed_mine, mixed_other), w_a, valid, gains8, owners
    )

    gm, gu = grad_gu
    arrived_gu = core_swap(gu)
    if ringed:
        mine_do, arrived_do = [gd_mine], [core_swap(gd_other)]
    else:
        mine_do, arrived_do = [gd_mine, go_mine], [core_swap(gd_other), core_swap(go_other)]
    by_owner = (fsdp_size * 2 * shard, 3 * PAIR)
    d_pre = []
    for call in range(4):
        from_half, kept = (other_ref, kept_other) if call < 2 else (core_ref, kept_mine)
        if ringed and call == 1:
            sum_gu = RingSumOverColumns(after(gm, d_pre[0]), arrived_gu)
            sum_gu.cross()
            sum_gu.cross()
            h1t = after(h1t, *sum_gu.sent)
        elif ringed and call > 1:
            sum_gu.cross()
            ahead = [sum_gu.came[2]] if call == 3 else []
            h1t = after(h1t, sum_gu.last(), sum_do.last(), sum_gu.sent[-1], *ahead)
        grads = mixer_backward(
            from_half,
            h1t,
            gains8,
            kept,
            d_mixed,
            slot,
            shard,
            (call % 2,),
            grads if call % 2 else (),
        )
        d_pre.append(grads[1])
        if call == 1:
            grad_other = grads[0]
            if ringed:
                sum_do = RingSum(mine_do, arrived_do)
                sum_do.begin(d_pre[-1])
                sum_gu.begin(d_pre[-1])
                grad_other = after(grad_other, sum_gu.last(), sum_do.last())
            arrived_qfv = [core_swap(grad_other.reshape(by_owner))]
        elif ringed and call > 1:
            sum_do.step(arriving=(d_pre[-1],))
            sum_gu.step(arriving=(d_pre[-1],))
    mine_qfv = [grads[0].reshape(by_owner)]

    def finish_input(*others):
        late = after(d_pre[3], *others) if others else d_pre[3]
        return input_gradient(rows, gains8, (late, d_pre[1]), w_a, d_x1)

    if ringed:
        sum_qfv = RingSum(mine_qfv, arrived_qfv)
        sum_qfv.begin()
        input_grad = None
        for step in range(1, RING - 1):
            if len(sum_gu.came) < RING:
                sum_gu.cross()
            if len(sum_gu.totals) < RING:
                first = [sum_gu.last(), sum_qfv.last()]
                sum_do.step(*{1: first, 4: [input_grad]}.get(step, []))
                sum_gu.step()
            sum_qfv.step()
            if step == 2:
                input_grad = finish_input(sum_qfv.last())
        total_gu, total_do = sum_gu.last(), sum_do.last()
    else:
        both = (gm.astype(wide) + arrived_gu.astype(wide)).astype(low)
        here = (both[0].astype(wide) + column_swap(both[1]).astype(wide)).astype(low)
        total_gu = scatter_rows(here)
        total_do = jnp.concatenate(
            [
                scatter_rows((own.astype(wide) + came.astype(wide)).astype(low))
                for own, came in zip(mine_do, arrived_do)
            ],
            axis=0,
        )
        total_qfv = scatter_rows(
            (mine_qfv[0].astype(wide) + arrived_qfv[0].astype(wide)).astype(low)
        )
        input_grad = finish_input()
    scale_rows = 1.0 / math.sqrt(count * fsdp_size * replicas)
    matrix_step = matrix_rate * scale_rows
    attention_state = (attention_weights, attention_momentum, attention_average)
    ffn_in_state = (ffn_inputs, ffn_inputs_momentum, ffn_inputs_average)
    ffn_out_state = (ffn_output, ffn_output_momentum, ffn_output_average)
    sum_do = over_columns(total_do)
    there = column_swap(total_gu)
    even = jnp.where(column == 0, total_gu, there)
    odd = jnp.where(column == 0, there, total_gu)
    sum_gu = (even, odd), (core_swap(even), core_swap(odd))
    *new_out, _ = update_ffn_out(core_ref, ffn_out_state, sum_do, matrix_step)
    *new_in, dots_up = update_ffn_in(core_ref, ffn_in_state, sum_gu[0], matrix_step, ())
    *new_in, dots_gate = update_ffn_in(other_ref, ffn_in_state, sum_gu[1], matrix_step, new_in)
    if ringed:
        sum_qfv.step(arriving=(new_out[0],))
        total_qfv = sum_qfv.last()
    there = after(column_swap(total_qfv), new_in[0])
    sum_qfv = (total_qfv.astype(wide) + there.astype(wide)).astype(low)
    *own, dots_own = update_attention(
        core_ref, core_ref, attention_state, sum_qfv, sum_do[0], matrix_step, ()
    )
    theirs = after(core_swap(sum_qfv), own[0])
    *new_attention, dots_theirs = update_attention(
        core_ref, other_ref, attention_state, theirs, sum_do[1], matrix_step, own
    )
    dots = jnp.sum(dots_own + dots_theirs, axis=2)
    row_sums = jnp.stack([dots[0] + dots[1] + dots[2], dots[3], jnp.sum(dots_up + dots_gate, axis=(0, 2))])
    sum_gains = row_sums / gains.astype(low).astype(wide)
    return (
        output.reshape(micro_count, slot, width),
        input_grad.reshape(micro_count, slot, width),
        *new_attention,
        *new_in,
        *new_out,
        *update(gains, gains_momentum, gains_average, sum_gains, gain_rate * scale_rows),
    )


def solution(mesh):
    rows_split = P(None, ("fsdp", "dp"), None)
    middle_split = P(None, "fsdp", None)
    first_split = P("fsdp", None)
    gains_split = P(None, "fsdp")
    in_specs = (
        (rows_split, rows_split, P(None, ("fsdp", "dp")))
        + (middle_split,) * 6
        + (first_split,) * 3
        + (gains_split,) * 3
    )
    out_specs = (
        (rows_split, rows_split)
        + (middle_split,) * 6
        + (first_split,) * 3
        + (gains_split,) * 3
    )
    return jax.shard_map(
        on_device, mesh=mesh, in_specs=in_specs, out_specs=out_specs, check_vma=False
    )
```

```python
import functools
import math

import jax
import jax.numpy as jnp
from jax import lax
from jax.experimental import pallas as pl
from jax.experimental.pallas import tpu as pltpu
from jax.sharding import PartitionSpec as P

HEAD_DIM = 128
PAIR = 2 * HEAD_DIM
GAIN_ROWS = 16

lower_bound = 0.9
momentum_decay = 0.9
average_decay = 0.7
weight_decay = 0.0005
matrix_rate = 0.03
gain_rate = 0.1
low = jnp.bfloat16
wide = jnp.float32
TILE_F = 256
VMEM_BYTES = 60 * 1024 * 1024


def mm(left, right):
    return jnp.dot(left, right, preferred_element_type=wide)


def mm_nt(left, right):
    return lax.dot_general(left, right, (((1,), (1,)), ((), ())), preferred_element_type=wide)


def mm_tn(left, right):
    return lax.dot_general(left, right, (((0,), (0,)), ((), ())), preferred_element_type=wide)


def sigmoid(u):
    return 0.5 * jnp.tanh(0.5 * u) + 0.5


def whole(shape):
    return pl.BlockSpec(shape, lambda *_: (0,) * len(shape), pipeline_mode=pl.Buffered(1))


def split_sum(ones_matrix, tensor):
    high = tensor.astype(low)
    rest = (tensor - high.astype(wide)).astype(low)
    return mm(ones_matrix, high) + mm(ones_matrix, rest)


def causal_mask(length, lower):
    rows = lax.broadcasted_iota(jnp.int32, (length, length), 0)
    columns = lax.broadcasted_iota(jnp.int32, (length, length), 1)
    return rows >= columns if lower else rows <= columns


def triangle(length, lower):
    return causal_mask(length, lower).astype(wide).astype(low)


def decay_parts(f_pre, lower_ones):
    share = sigmoid(f_pre)
    gate = lower_bound + (1.0 - lower_bound) * share
    keys_in = (1.0 - lower_bound) * (1.0 - share)
    cumulative = split_sum(lower_ones, jnp.log(gate))
    middle_row = cumulative.shape[0] // 2
    cumulative = cumulative - cumulative[middle_row : middle_row + 1, :]
    return share, gate, keys_in, cumulative


def first_norm(x_ref, gain_row):
    rows = x_ref[...].astype(wide)
    scale = lax.rsqrt(jnp.mean(rows * rows, axis=-1, keepdims=True) + 1e-06)
    return rows * scale, scale


def lanes_of(half, size):
    return pl.ds(pl.multiple_of(half * size, size), size)


def mixer_forward_first_kernel(
    slot, half_ref, x_ref, w_ref, gains_ref, on_ref, q_ref, f_ref, v_ref, o_ref, g_ref, h_s
):
    @pl.when(pl.program_id(0) == 0)
    def _():
        g_ref[...] = gains_ref[...].astype(wide)[: g_ref.shape[0], :]

    mixer_forward_kernel(
        slot, half_ref, x_ref, w_ref, g_ref, on_ref, q_ref, f_ref, v_ref, o_ref, h_s
    )


def mixer_forward_kernel(
    slot, half_ref, x_ref, w_ref, g_ref, on_ref, q_ref, f_ref, v_ref, o_ref, h_s
):
    @pl.when(pl.program_id(0) == 0)
    def _():
        normed, _ = first_norm(x_ref, None)
        h_s[...] = (normed * g_ref[0:1, :]).astype(low)

    gain_o = g_ref[1:2, lanes_of(half_ref[0] * pl.num_programs(0) + pl.program_id(0), PAIR)]
    pre = mm(h_s[...], w_ref[...])
    q_ref[...] = pre[:, :PAIR]
    f_ref[...] = pre[:, PAIR : 2 * PAIR]
    v_ref[...] = pre[:, 2 * PAIR :].astype(low)
    lower_ones = triangle(slot, True)
    causal = causal_mask(slot, True)
    for sequence in range(x_ref.shape[0] // slot):
        rows = slice(sequence * slot, (sequence + 1) * slot)
        q_pre = q_ref[rows, :]
        _, _, keys_in, cumulative = decay_parts(f_ref[rows, :], lower_ones)
        grown = jnp.exp(-cumulative)
        decayed_q = (q_pre * sigmoid(q_pre) * jnp.exp(cumulative)).astype(low)
        grown_k = (keys_in * grown).astype(low)
        values = v_ref[rows, :]
        for head in range(2):
            lanes = slice(head * HEAD_DIM, (head + 1) * HEAD_DIM)
            scores = mm_nt(decayed_q[:, lanes], grown_k[:, lanes])
            out = mm(jnp.where(causal, scores, 0.0).astype(low), values[:, lanes])
            scale = lax.rsqrt(jnp.mean(out * out, axis=-1, keepdims=True) + 1e-05)
            o_ref[rows, lanes] = out.astype(low)
            on_ref[rows, lanes] = (out * scale * gain_o[:, lanes]).astype(low)


def mixer_forward_last_kernel(
    slot,
    half_ref,
    x_ref,
    w_ref,
    g_ref,
    before_ref,
    woo_ref,
    wom_ref,
    on_ref,
    q_ref,
    f_ref,
    v_ref,
    o_ref,
    x1_ref,
    h2_ref,
    h2t_ref,
    h1t_ref,
    h_s,
    on_s,
):
    step = pl.program_id(0)
    half = before_ref.shape[1]
    mixer_forward_kernel(
        slot, half_ref, x_ref, w_ref, g_ref, on_ref, q_ref, f_ref, v_ref, o_ref, h_s
    )
    on_s[:, lanes_of(half_ref[0] * pl.num_programs(0) + step, PAIR)] = on_ref[...]

    @pl.when(step == pl.num_programs(0) - 1)
    def _():
        here = lanes_of(half_ref[0], half)
        there = lanes_of(1 - half_ref[0], half)
        on_s[:, there] = before_ref[...]
        h1t_ref[...] = h_s[...].astype(wide).T.astype(low)
        x1_ref[:, here] = x_ref[:, here].astype(wide) + mm(on_s[...], woo_ref[...])
        x1_ref[:, there] = x_ref[:, there].astype(wide) + mm(on_s[...], wom_ref[...])
        x1 = x1_ref[...]
        scale = lax.rsqrt(jnp.mean(x1 * x1, axis=-1, keepdims=True) + 1e-06)
        normed = x1 * scale * g_ref[2:3, :]
        h2_ref[...] = normed.astype(low)
        h2t_ref[...] = normed.T.astype(low)


def mixer_forward(half, rows, weights, slot, gains=None, ending=None):
    count, width = rows.shape
    pairs = width // PAIR // 2
    by_pair = pl.BlockSpec((count, PAIR), lambda j, _: (0, j))
    struct = jax.ShapeDtypeStruct
    shape = lambda kind: struct((count, width // 2), kind)
    in_specs = [whole(rows.shape), pl.BlockSpec((width, 3 * PAIR), lambda j, _: (0, j))]
    operands = [half, rows, weights]
    out_specs = [by_pair] * 5
    out_shape = [shape(low), shape(wide), shape(wide), shape(low), shape(low)]
    scratch = [pltpu.VMEM((count, width), low)]
    if ending is None:
        kernel = mixer_forward_first_kernel
        in_specs += [whole(gains.shape)]
        operands += [gains]
        out_specs += [whole((8, width))]
        out_shape += [struct((8, width), wide)]
    if ending is not None:
        kernel = mixer_forward_last_kernel
        out_weights = pl.BlockSpec((width, width // 2), lambda j, _: (0, 3))
        in_specs += [whole(ending[0].shape), whole((count, width // 2)), out_weights, out_weights]
        operands += [ending[0], ending[1], weights, ending[2]]
        out_specs += [whole((count, width))] * 2 + [whole((width, count))] * 2
        out_shape += [
            struct((count, width), wide),
            struct((count, width), low),
            struct((width, count), low),
            struct((width, count), low),
        ]
        scratch += [pltpu.VMEM((count, width), low)]
    return pl.pallas_call(
        functools.partial(kernel, slot),
        grid_spec=pltpu.PrefetchScalarGridSpec(
            num_scalar_prefetch=1,
            grid=(pairs,),
            in_specs=in_specs,
            out_specs=out_specs,
            scratch_shapes=scratch,
        ),
        out_shape=out_shape,
        compiler_params=pltpu.CompilerParams(vmem_limit_bytes=VMEM_BYTES),
        cost_estimate=pl.CostEstimate(
            flops=count * width * 4 * width + 10 * count * slot * width,
            bytes_accessed=count * width * 12 + width * width * 4,
            transcendentals=count * width * 3,
        ),
        name="mixer_forward",
    )(*operands)


def store_down(out_ref, tile, owners):
    if owners is None:
        out_ref[...] = tile
        return
    _, stride, down_rows = owners
    block = math.gcd(down_rows, tile.shape[0])
    first = (pl.program_id(0) - 1) * (tile.shape[0] // block)
    for part in range(tile.shape[0] // block):
        owner = (first + part) // (down_rows // block)
        inside = (first + part) % (down_rows // block)
        start = pl.multiple_of(owner * stride + inside * block, block)
        out_ref[pl.ds(start, block), :] = tile[part * block : (part + 1) * block, :]


def ffn_ahead(core_ref, h_ref, wm_ref, wu_ref, gu_w, pre_s, slot):
    tile = wm_ref.shape[1]
    gu_w[slot, :, lanes_of(core_ref[0], tile)] = wm_ref[...]
    gu_w[slot, :, lanes_of(1 - core_ref[0], tile)] = wu_ref[...]
    pre_s[slot] = mm(h_ref[...], gu_w[slot])


def ffn_tile(owners, core_ref, refs, grads, acc_ref, dh_ref, scratch):
    h_ref, ht_ref, e_ref, wm_ref, wu_ref, wdm_ref, wdo_ref = refs
    gm_ref, gu_ref, gdm_ref, gdo_ref = grads
    gu_w, down_w, gu_g, down_g, pre_s = scratch
    half, tile = wdm_ref.shape[1], wm_ref.shape[1]
    mine, other = lanes_of(core_ref[0], half), lanes_of(1 - core_ref[0], half)
    now = lax.rem(pl.program_id(0) + 1, 2)
    down_w[:, mine] = wdm_ref[...]
    down_w[:, other] = wdo_ref[...]
    d_mid = mm_nt(e_ref[...], down_w[...])
    a, b = pre_s[now, :, :tile], pre_s[now, :, tile:]
    ffn_ahead(core_ref, h_ref, wm_ref, wu_ref, gu_w, pre_s, 1 - now)
    share = sigmoid(a)
    swish = a * share
    mid = (swish * b).astype(low)
    down_g[...] = mm_tn(mid, e_ref[...]).astype(low)
    d_a = (d_mid * b * (share + swish * (1.0 - share))).astype(low)
    d_b = (d_mid * swish).astype(low)
    d_pre = jnp.concatenate([d_a, d_b], axis=1)
    acc_ref[...] += mm(mid, down_w[...])
    dh_ref[...] += mm_nt(d_pre, gu_w[now])
    gu_g[...] = mm(ht_ref[...], d_pre).astype(low)
    blocks = tile // HEAD_DIM
    for side, block in enumerate((core_ref[1], 1 - core_ref[1])):
        gm_ref[side] = gu_g[:, lanes_of(core_ref[0] * blocks + block, HEAD_DIM)]
        gu_ref[side] = gu_g[:, lanes_of((1 - core_ref[0]) * blocks + block, HEAD_DIM)]
    store_down(gdm_ref, down_g[:, mine], owners)
    store_down(gdo_ref, down_g[:, other], owners)


def ffn_kernel(
    owners,
    core_ref,
    h_ref,
    ht_ref,
    e_ref,
    wm_ref,
    wu_ref,
    wdm_ref,
    wdo_ref,
    x1_ref,
    onm_ref,
    ono_ref,
    wom_ref,
    woo_ref,
    m_ref,
    g_ref,
    gm_ref,
    gu_ref,
    gdm_ref,
    gdo_ref,
    out_ref,
    dh_s,
    don_ref,
    gom_ref,
    goo_ref,
    on_s,
    acc_s,
    *scratch,
):
    @pl.when(pl.program_id(0) == 0)
    def _():
        acc_s[...] = x1_ref[...]
        dh_s[...] = jnp.zeros_like(dh_s)
        ffn_ahead(core_ref, h_ref, wm_ref, wu_ref, scratch[0], scratch[-1], 0)

    grads = (gm_ref, gu_ref, gdm_ref, gdo_ref)
    refs = (h_ref, ht_ref, e_ref, wm_ref, wu_ref, wdm_ref, wdo_ref)

    @pl.when(pl.program_id(0) > 0)
    def _():
        ffn_tile(owners, core_ref, refs, grads, acc_s, dh_s, scratch)

    @pl.when(pl.program_id(0) == pl.num_programs(0) - 1)
    def _():
        half = onm_ref.shape[1]
        mine = lanes_of(core_ref[0], half)
        other = lanes_of(1 - core_ref[0], half)
        positions = lax.broadcasted_iota(jnp.int32, (out_ref.shape[0] // m_ref.shape[0], 1), 0)
        for sequence in range(m_ref.shape[0]):
            rows = slice(sequence * positions.shape[0], (sequence + 1) * positions.shape[0])
            valid = (positions < m_ref[sequence]).astype(wide)
            out_ref[rows, :] = (acc_s[rows, :] * valid).astype(low)
        x1 = x1_ref[...]
        scale = lax.rsqrt(jnp.mean(x1 * x1, axis=-1, keepdims=True) + 1e-06)
        normed = x1 * scale
        d_h2 = dh_s[...]
        scaled = d_h2 * g_ref[2:3, :]
        d_x1 = e_ref[...].astype(wide) + scale * (
            scaled - normed * jnp.mean(scaled * normed, axis=-1, keepdims=True)
        )
        dh_s[...] = d_x1
        on_s[...] = d_x1.astype(low)
        d_mixed = mm_nt(on_s[:, mine], wom_ref[...]) + mm_nt(on_s[:, other], woo_ref[...])
        don_ref[...] = d_mixed.astype(low)
        for columns, g_down_ref, g_ref_o in ((mine, gdm_ref, gom_ref), (other, gdo_ref, goo_ref)):
            d_1 = on_s[:, columns]
            for which, on_ref in ((core_ref[0], onm_ref), (1 - core_ref[0], ono_ref)):
                grad_o = mm_tn(on_ref[...], d_1).astype(low)
                if owners is None:
                    g_ref_o[pl.ds(pl.multiple_of(which * half, half), half), :] = grad_o
                    continue
                count, stride, down_rows = owners
                rows = stride - down_rows
                for part in range(half // rows):
                    owner = which * (count // 2) + part
                    start = pl.multiple_of(owner * stride + down_rows, math.gcd(stride, down_rows))
                    g_down_ref[pl.ds(start, rows), :] = grad_o[part * rows : (part + 1) * rows, :]


def ffn(core, h2, h2t, errors, w_gu, w_d, x1, mixed, w_a, lengths, gains8, owners):
    count, width = h2.shape
    half = width // 2
    hidden = w_gu[0].shape[1]
    full = whole((count, width))
    half_full = whole((count, half))
    square = whole((width, half))
    tiles = hidden // TILE_F
    ahead = lambda j: jnp.minimum(j, tiles - 1)
    behind = lambda j: jnp.maximum(j - 1, 0)
    in_tile = pl.BlockSpec((width, TILE_F), lambda j, _: (0, ahead(j)))
    out_tile = pl.BlockSpec((TILE_F, half), lambda j, _: (behind(j), 0))
    out_weights = pl.BlockSpec((width, half), lambda j, _: (0, 3), pipeline_mode=pl.Buffered(1))
    down_spec, down_shape, out_spec, out_shape = out_tile, (hidden, half), square, (width, half)
    if owners is not None:
        down_shape, out_shape = (owners[0] * owners[1], half), (16, half)
        down_spec, out_spec = whole(down_shape), whole(out_shape)
    struct = jax.ShapeDtypeStruct
    return pl.pallas_call(
        functools.partial(ffn_kernel, owners),
        grid_spec=pltpu.PrefetchScalarGridSpec(
            num_scalar_prefetch=1,
            grid=(tiles + 1,),
            in_specs=[full, whole(h2t.shape), full, in_tile, in_tile, out_tile, out_tile]
            + [full, half_full, half_full, out_weights, out_weights]
            + [pl.BlockSpec(memory_space=pltpu.SMEM), whole((8, width))],
            out_specs=[pl.BlockSpec((2, width, HEAD_DIM), lambda j, _: (0, 0, behind(j)))] * 2
            + [down_spec, down_spec]
            + [full, full, full, out_spec, out_spec],
            scratch_shapes=[
                pltpu.VMEM((count, width), low),
                pltpu.VMEM((count, width), wide),
                pltpu.VMEM((2, width, 2 * TILE_F), low),
                pltpu.VMEM((TILE_F, width), low),
                pltpu.VMEM((width, 2 * TILE_F), low),
                pltpu.VMEM((TILE_F, width), low),
                pltpu.VMEM((2, count, 2 * TILE_F), wide),
            ],
        ),
        out_shape=[struct((2, width, hidden // 2), low)] * 2
        + [struct(down_shape, low)] * 2
        + [
            struct((count, width), low),
            struct((count, width), wide),
            struct((count, width), low),
            struct(out_shape, low),
            struct(out_shape, low),
        ],
        compiler_params=pltpu.CompilerParams(vmem_limit_bytes=VMEM_BYTES),
        cost_estimate=pl.CostEstimate(
            flops=16 * count * width * hidden,
            bytes_accessed=count * width * 20 + width * hidden * 12,
            transcendentals=count * hidden,
        ),
        name="ffn",
    )(core, h2, h2t, errors, *w_gu, *w_d, x1, *mixed, *w_a, lengths, gains8)


def mixer_backward_kernel(
    slot,
    per_half,
    first,
    half_ref,
    ht_ref,
    g_ref,
    q_ref,
    f_ref,
    v_ref,
    o_ref,
    don_ref,
    *outs,
):
    grad_ref, dpre_ref = outs[-2:]
    gain_o = g_ref[1:2, lanes_of(half_ref[0] * per_half + first + pl.program_id(0), PAIR)]
    lower_ones = triangle(slot, True)
    upper_ones = triangle(slot, False)
    causal_t = causal_mask(slot, False)
    for sequence in range(q_ref.shape[0] // slot):
        rows = slice(sequence * slot, (sequence + 1) * slot)
        d_on = don_ref[rows, :].astype(wide)
        out = o_ref[rows, :].astype(wide)
        d_out_parts = []
        for head in range(2):
            lanes = slice(head * HEAD_DIM, (head + 1) * HEAD_DIM)
            out_h, d_on_h = out[:, lanes], d_on[:, lanes]
            scale = lax.rsqrt(jnp.mean(out_h * out_h, axis=-1, keepdims=True) + 1e-05)
            normed = out_h * scale
            scaled = d_on_h * gain_o[:, lanes]
            inner = jnp.mean(scaled * normed, axis=-1, keepdims=True)
            d_out_parts.append((scale * (scaled - normed * inner)).astype(low))

        q_pre = q_ref[rows, :]
        share, gate, keys_in, cumulative = decay_parts(f_ref[rows, :], lower_ones)
        grown = jnp.exp(-cumulative)
        shrunk = jnp.exp(cumulative)
        q_share = sigmoid(q_pre)
        decayed_q = (q_pre * q_share * shrunk).astype(low)
        grown_k = (keys_in * grown).astype(low)
        values = v_ref[rows, :]
        dq_parts, dk_parts, dv_parts = [], [], []
        for head in range(2):
            lanes = slice(head * HEAD_DIM, (head + 1) * HEAD_DIM)
            q_h, k_h, v_h = decayed_q[:, lanes], grown_k[:, lanes], values[:, lanes]
            d_out = d_out_parts[head]
            scores = jnp.where(causal_t, mm_nt(k_h, q_h), 0.0).astype(low)
            d_scores = jnp.where(causal_t, mm_nt(v_h, d_out), 0.0).astype(low)
            dv_parts.append(mm(scores, d_out))
            dk_parts.append(mm(d_scores, q_h))
            dq_parts.append(mm_tn(d_scores, k_h))
        d_decayed = jnp.concatenate(dq_parts, axis=1)
        d_grown = jnp.concatenate(dk_parts, axis=1)
        d_value = jnp.concatenate(dv_parts, axis=1)
        d_cumulative = decayed_q.astype(wide) * d_decayed - grown_k.astype(wide) * d_grown
        d_log = split_sum(upper_ones, d_cumulative)
        d_query = d_decayed * shrunk
        d_key = d_grown * grown
        d_q_pre = d_query * q_share * (1.0 + q_pre * (1.0 - q_share))
        d_f_pre = (1.0 - lower_bound) * (d_log / gate - d_key) * share * (1.0 - share)
        dpre_ref[rows, :PAIR] = d_q_pre.astype(low)
        dpre_ref[rows, PAIR : 2 * PAIR] = d_f_pre.astype(low)
        dpre_ref[rows, 2 * PAIR :] = d_value.astype(low)

    grad = mm(ht_ref[...], dpre_ref[...]).astype(low)
    grad_ref[...] = grad.reshape(grad_ref.shape)


def mixer_backward(half, h1t, gains8, kept, d_mixed, slot, shard, pairs=(0, 1), before=()):
    width, count = h1t.shape
    per_half = width // PAIR // 2
    first = pairs[0]
    by_pair = pl.BlockSpec((count, PAIR), lambda j, _: (0, first + j))
    from_whole = pl.BlockSpec((count, PAIR), lambda j, half: (0, half[0] * per_half + first + j))
    struct = jax.ShapeDtypeStruct
    return pl.pallas_call(
        functools.partial(mixer_backward_kernel, slot, per_half, first),
        grid_spec=pltpu.PrefetchScalarGridSpec(
            num_scalar_prefetch=1,
            grid=(len(pairs),),
            in_specs=[whole((width, count)), whole(gains8.shape)]
            + [by_pair] * 4
            + [from_whole]
            + [pl.BlockSpec(memory_space=pl.ANY)] * len(before),
            out_specs=[
                pl.BlockSpec(
                    (width // shard, 1, shard, 3 * PAIR), lambda j, _: (0, first + j, 0, 0)
                ),
                pl.BlockSpec((count, 3 * PAIR), lambda j, _: (0, first + j)),
            ],
        ),
        out_shape=[
            struct((width // shard, per_half, shard, 3 * PAIR), low),
            struct((count, per_half * 3 * PAIR), low),
        ],
        input_output_aliases={8 + k: k for k in range(len(before))},
        compiler_params=pltpu.CompilerParams(vmem_limit_bytes=VMEM_BYTES),
        cost_estimate=pl.CostEstimate(
            flops=len(pairs) * (count * width * 6 * PAIR + 20 * count * slot * PAIR),
            bytes_accessed=len(pairs) * (count * width * 5 + width * PAIR * 6),
            transcendentals=len(pairs) * count * PAIR * 6,
        ),
        name="mixer_backward",
    )(half, h1t, gains8, *kept, d_mixed, *before)


def input_gradient_rows_kernel(
    x_ref, g_ref, dm_ref, do_ref, wm_ref, wo_ref, dx1_ref, dx_ref
):
    d_h1 = mm_nt(dm_ref[...], wm_ref[...]) + mm_nt(do_ref[...], wo_ref[...])
    normed, scale = first_norm(x_ref, None)
    scaled = d_h1 * g_ref[0:1, :]
    dx_ref[...] = dx1_ref[...] + scale * (
        scaled - normed * jnp.mean(scaled * normed, axis=-1, keepdims=True)
    )


def input_gradient(rows, gains8, d_pre, weights, d_x1):
    count, width = rows.shape
    block = count // 2
    columns = d_pre[0].shape[1]
    by_rows = lambda columns: pl.BlockSpec((block, columns), lambda j: (j, 0))
    weight_spec = pl.BlockSpec((width, columns), lambda j: (0, 0), pipeline_mode=pl.Buffered(1))
    return pl.pallas_call(
        input_gradient_rows_kernel,
        grid=(count // block,),
        in_specs=[by_rows(width), whole(gains8.shape)]
        + [by_rows(columns)] * 2
        + [weight_spec] * 2
        + [by_rows(width)],
        out_specs=by_rows(width),
        out_shape=jax.ShapeDtypeStruct((count, width), wide),
        compiler_params=pltpu.CompilerParams(vmem_limit_bytes=VMEM_BYTES),
        cost_estimate=pl.CostEstimate(
            flops=6 * count * width * width,
            bytes_accessed=count * width * 16 + width * width * 6,
            transcendentals=0,
        ),
        name="input_gradient",
    )(rows, gains8, *d_pre, *weights, d_x1)


def update(weight, momentum, average, gradient, step_rate):
    new_momentum = momentum_decay * momentum + gradient
    direction = gradient + momentum_decay * new_momentum + weight_decay * weight
    new_weight = weight - step_rate * direction
    new_average = average_decay * average + (1.0 - average_decay) * new_weight
    return (new_momentum, new_average, new_weight)


def update_kernel(pick, step_rate, sum_count, core_ref, w_ref, m_ref, a_ref, *refs):
    sums, outs, dots_ref = refs[:sum_count], refs[-4:-1], refs[-1]
    weight = w_ref[...]
    gradient = pick(core_ref[0], *[s[...] for s in sums]).astype(wide).reshape(weight.shape)
    results = update(weight, m_ref[...], a_ref[...], gradient, step_rate)
    for out, result in zip(outs, results):
        out[...] = result
    product = weight.astype(low).astype(wide) * gradient
    total = product[..., :HEAD_DIM]
    for start in range(HEAD_DIM, product.shape[-1], HEAD_DIM):
        total = total + product[..., start : start + HEAD_DIM]
    dots_ref[...] = total.reshape(dots_ref.shape)


def update_call(
    core, state, sums, grid, state_spec, sum_specs, pick, step_rate, name, before=()
):
    struct = jax.ShapeDtypeStruct(state[0].shape, wide)
    size = math.prod(state[0].shape)
    rows = state_spec.block_shape[-2]
    steps = math.prod(grid)
    tail = grid[1:]

    def dots_index(*indices):
        place = indices[0]
        for length, index in zip(tail, indices[1:]):
            place = place * length + index
        return (place, 0, 0)

    return pl.pallas_call(
        functools.partial(update_kernel, pick, step_rate, len(sums)),
        grid_spec=pltpu.PrefetchScalarGridSpec(
            num_scalar_prefetch=1,
            grid=grid,
            in_specs=[state_spec] * 3
            + sum_specs
            + [pl.BlockSpec(memory_space=pl.ANY)] * len(before),
            out_specs=[state_spec] * 3 + [pl.BlockSpec((1, rows, HEAD_DIM), dots_index)],
        ),
        out_shape=[struct] * 3 + [jax.ShapeDtypeStruct((steps, rows, HEAD_DIM), wide)],
        input_output_aliases={4 + len(sums) + k: k for k in range(len(before))},
        compiler_params=pltpu.CompilerParams(vmem_limit_bytes=VMEM_BYTES),
        cost_estimate=pl.CostEstimate(flops=12 * size, bytes_accessed=26 * size, transcendentals=0),
        name=name,
    )(core, *state, *sums, *before)


def update_attention(core, half_ref, state, qfv, out, step_rate, before):
    _, shard, width = state[0].shape
    down_rows = out.shape[0] - shard

    def pick(core_index, proj, last):
        gradient = last[down_rows:].astype(wide)
        for kind in range(3):
            parts = [proj[pair * shard :, kind * PAIR :][:shard, :PAIR] for pair in range(2)]
            chosen = jnp.concatenate(parts, axis=1).astype(wide)
            gradient = jnp.where(pl.program_id(0) == kind, chosen, gradient)
        return gradient

    return update_call(
        half_ref,
        state,
        (qfv, out),
        (4,),
        pl.BlockSpec((1, shard, width // 2), lambda kind, half: (kind, 0, half[0])),
        [whole(qfv.shape), whole(out.shape)],
        pick,
        step_rate,
        "update_attention",
        before,
    )


def update_ffn_in(kind_ref, state, totals, step_rate, before):
    _, shard, hidden = state[0].shape
    block = shard // 2

    def pick(_, even, odd):
        blocks = []
        for start in range(0, hidden // 2, HEAD_DIM):
            blocks += [even[:, start : start + HEAD_DIM], odd[:, start : start + HEAD_DIM]]
        return jnp.concatenate(blocks, axis=1)

    return update_call(
        kind_ref,
        state,
        totals,
        (2,),
        pl.BlockSpec((1, block, hidden), lambda j, kind: (kind[0], j, 0)),
        [pl.BlockSpec((block, hidden // 2), lambda j, _: (j, 0))] * 2,
        pick,
        step_rate,
        "update_ffn_in",
        before,
    )


def update_ffn_out(core, state, sums, step_rate):
    shard, width = state[0].shape

    def pick(core_index, mine, other):
        own = pl.program_id(0) == core_index
        return jnp.where(own, mine[:shard].astype(wide), other[:shard].astype(wide))

    return update_call(
        core,
        state,
        sums,
        (2,),
        pl.BlockSpec((shard, width // 2), lambda j, _: (0, j)),
        [whole(total.shape) for total in sums],
        pick,
        step_rate,
        "update_ffn_out",
    )


def pack_kernel(core_ref, w_ref, out_ref):
    half = w_ref.shape[2]
    for pair in range(half // PAIR):
        for kind in range(3):
            start = (pair * 3 + kind) * PAIR
            piece = w_ref[kind, :, pair * PAIR : (pair + 1) * PAIR]
            out_ref[:, start : start + PAIR] = piece.astype(low)
    out_ref[:, 3 * half : 4 * half] = w_ref[3].astype(low)


def pack_attention(core, weights):
    _, shard, width = weights.shape
    half = width // 2
    return pl.pallas_call(
        pack_kernel,
        grid_spec=pltpu.PrefetchScalarGridSpec(
            num_scalar_prefetch=1,
            grid=(1,),
            in_specs=[pl.BlockSpec((4, shard, half), lambda j, core: (0, 0, core[0]))],
            out_specs=whole((shard, 4 * half)),
        ),
        out_shape=jax.ShapeDtypeStruct((shard, 4 * half), low),
        name="pack_attention",
    )(core, weights)


RING = 8


def ring_place(index):
    return jnp.where(index % 2 == 0, index // 2, RING - 1 - index // 2)


def ring_member(place):
    place = place % RING
    return jnp.where(place < RING // 2, 2 * place, 2 * RING - 1 - 2 * place)


CYCLE = (0, 2, 4, 6, 7, 5, 3, 1)


def ring_next(tensor):
    replicas = lax.axis_size("dp")
    pairs = []
    for place_of, member in enumerate(CYCLE):
        for replica in range(replicas):
            target = CYCLE[(place_of + (1 if replica % 2 == 0 else -1)) % RING]
            pairs.append((member * replicas + replica, target * replicas + replica))
    return lax.ppermute(tensor, ("fsdp", "dp"), pairs)


def ring_shift(tensor, way):
    pairs = [(member, CYCLE[(at + way) % RING]) for at, member in enumerate(CYCLE)]
    return lax.ppermute(tensor, "fsdp", pairs)


def core_swap(tensor):
    return lax.ppermute(tensor, "dp", [(d, d ^ 1) for d in range(lax.axis_size("dp"))])


def column_swap(tensor):
    return lax.ppermute(tensor, "dp", [(d, d ^ 2) for d in range(lax.axis_size("dp"))])


def pack_all_kernel(core_ref, column_ref, w_ref, up_ref, down_ref, g_ref, out_ref):
    shard = w_ref.shape[1]
    half = w_ref.shape[2]
    for pair in range(half // PAIR):
        for kind in range(3):
            start = (pair * 3 + kind) * PAIR
            piece = w_ref[kind, :, pair * PAIR : (pair + 1) * PAIR]
            out_ref[:, start : start + PAIR] = piece.astype(low)
    out_ref[:, 3 * half : 4 * half] = w_ref[3].astype(low)
    start = 4 * half
    out_ref[:, start : start + up_ref.shape[2]] = up_ref[0].astype(low)
    start += up_ref.shape[2]
    for first, count in down_parts(down_ref.shape[0], shard):
        out_ref[:count, start : start + half] = down_ref[first : first + count, :].astype(low)
        if count < shard:
            out_ref[count:, start : start + half] = jnp.zeros((shard - count, half), low)
            rows = lax.broadcasted_iota(jnp.int32, (GAIN_ROWS, g_ref.shape[1]), 0)
            gains = jnp.where(rows == 1, g_ref[1:2, :], g_ref[2:3, :])
            gains = jnp.where(rows == 0, g_ref[0:1, :], gains)
            gains = jnp.where(rows < 3, gains, 0.0).astype(low)
            out_ref[count : count + GAIN_ROWS, start : start + g_ref.shape[1]] = gains
        start += half


def down_parts(down_rows, shard):
    return [(start, min(shard, down_rows - start)) for start in range(0, down_rows, shard)]


def pack_all(core, column, weights, up, down, gains):
    _, shard, width = weights.shape
    half = width // 2
    parts = len(down_parts(down.shape[0], shard))
    columns = 4 * half + up.shape[2] // 2 + parts * half
    return pl.pallas_call(
        pack_all_kernel,
        grid_spec=pltpu.PrefetchScalarGridSpec(
            num_scalar_prefetch=2,
            grid=(1,),
            in_specs=[
                pl.BlockSpec((4, shard, half), lambda j, core, column: (0, 0, core[0])),
                pl.BlockSpec(
                    (1, shard, up.shape[2] // 2), lambda j, core, column: (core[0], 0, column[0])
                ),
                pl.BlockSpec((down.shape[0], half), lambda j, core, column: (0, core[0])),
                whole(gains.shape),
            ],
            out_specs=whole((shard, columns)),
        ),
        out_shape=jax.ShapeDtypeStruct((shard, columns), low),
        compiler_params=pltpu.CompilerParams(vmem_limit_bytes=VMEM_BYTES),
        name="pack_all",
    )(core, column, weights, up, down, gains)


def place_kernel(which, kept, shapes, origin_ref, column_ref, *refs):
    pieces, outs, semaphores = refs[: len(which)], refs[-1 - len(kept) : -1], refs[-1]
    targets = dict(zip(kept, outs))
    shard, first, up_columns, down_rows, half = shapes
    copies = []

    def copy(source, target):
        copies.append(pltpu.make_async_copy(source, target, semaphores.at[len(copies)]))

    for piece, (origin, across) in zip(pieces, which):
        owner = origin_ref[origin]
        rows = pl.ds(pl.multiple_of(owner * shard, 16), shard)
        if across:
            copy(piece, targets[1].at[rows, lanes_of(1 - column_ref[0], up_columns)])
            continue
        copy(piece.at[:, pl.ds(0, first)], targets[0].at[rows, :])
        own = targets[1].at[rows, lanes_of(column_ref[0], up_columns)]
        copy(piece.at[:, pl.ds(first, up_columns)], own)
        lane = first + up_columns
        for start, count in down_parts(down_rows, shard):
            target = pl.ds(pl.multiple_of(owner * down_rows + start, 16), count)
            copy(piece.at[pl.ds(0, count), pl.ds(lane, half)], targets[2].at[target, :])
            if count < shard:
                source = piece.at[pl.ds(count, GAIN_ROWS), pl.ds(lane, shard)]
                copy(source, targets[3].at[:, lanes_of(owner, shard)])
            lane += half
    for one in copies:
        one.start()
    for one in copies:
        one.wait()


def place(origins, column, which, pieces, arrays, kept, shapes):
    anywhere = pl.BlockSpec(memory_space=pl.ANY)
    shard, first, up_columns, down_rows, half = shapes
    kinds = [(RING * shard, first), (RING * shard, 2 * up_columns), (RING * down_rows, half)]
    kinds.append((GAIN_ROWS, RING * shard))
    held = [] if arrays is None else list(arrays)
    size = sum(math.prod(piece.shape) for piece in pieces)
    before = 2 + len(pieces)
    return pl.pallas_call(
        functools.partial(place_kernel, which, kept, shapes),
        grid_spec=pltpu.PrefetchScalarGridSpec(
            num_scalar_prefetch=2,
            grid=(1,),
            in_specs=[whole(piece.shape) for piece in pieces] + [anywhere] * len(held),
            out_specs=[anywhere] * len(kept),
            scratch_shapes=[pltpu.SemaphoreType.DMA((8 * len(pieces),))],
        ),
        out_shape=[jax.ShapeDtypeStruct(kinds[k], pieces[0].dtype) for k in kept],
        input_output_aliases={before + k: k for k in range(len(held))},
        compiler_params=pltpu.CompilerParams(vmem_limit_bytes=VMEM_BYTES),
        cost_estimate=pl.CostEstimate(flops=0, bytes_accessed=8 * size, transcendentals=0),
        name="place",
    )(origins, column, *pieces, *held)


def after(tensor, *others):
    return lax.optimization_barrier((tensor, *others))[0]


def core_way():
    return 1 - 2 * (lax.axis_index("dp") % 2)


def ring_origins():
    steps = jnp.array((0, -1, -2, -3, -4, 1, 2, 3), jnp.int32)
    return ring_member(ring_place(lax.axis_index("fsdp")) + steps + RING).astype(jnp.int32)


class RingSumOverColumns:
    def __init__(self, mine, arrived):
        self.arrays = (mine, arrived)
        place = ring_place(lax.axis_index("fsdp"))
        self.rows = mine.shape[1] // RING
        self.starts = [
            ring_member(place - core_way() * (s + 1) + 2 * RING) * self.rows for s in range(RING)
        ]
        self.sent, self.came, self.totals = [], [], []

    def part(self, side, step):
        shape = (1, self.rows, self.arrays[0].shape[2])
        parts = [
            lax.dynamic_slice(array, (side, self.starts[step], 0), shape)[0]
            for array in self.arrays
        ]
        return parts[0].astype(wide) + parts[1].astype(wide)

    def cross(self):
        self.sent.append(self.part(1, len(self.sent)).astype(low))
        self.came.append(column_swap(self.sent[-1]))

    def term(self):
        step = len(self.totals)
        return self.part(0, step) + self.came[step].astype(wide)

    def begin(self, *others):
        self.came[0] = after(self.came[0], *others) if others else self.came[0]
        self.totals.append(self.term().astype(low))

    def step(self, arriving=()):
        total, ahead = self.totals[-1], self.came[len(self.totals)]
        moved = ring_next(after(total, ahead) if len(self.totals) > 1 else total)
        moved = after(moved, *arriving) if arriving else moved
        self.totals.append((moved.astype(wide) + self.term()).astype(low))

    def last(self):
        return self.totals[-1]


class RingSum:
    def __init__(self, mine, arrived):
        self.mine, self.arrived = mine, arrived
        place = ring_place(lax.axis_index("fsdp"))
        self.owners = [ring_member(place - core_way() * (s + 1) + 2 * RING) for s in range(RING)]
        self.totals = []

    def term(self):
        parts = []
        for own, arrived in zip(self.mine, self.arrived):
            rows = own.shape[0] // RING
            start = self.owners[len(self.totals)] * rows
            part = lax.dynamic_slice_in_dim(own, start, rows, 0).astype(wide)
            parts.append(part + lax.dynamic_slice_in_dim(arrived, start, rows, 0).astype(wide))
        return parts[0] if len(parts) == 1 else jnp.concatenate(parts, axis=0)

    def begin(self, *others):
        if others:
            self.mine = [after(self.mine[0], *others), *self.mine[1:]]
        self.totals.append(self.term().astype(low))

    def step(self, *before, arriving=()):
        total = self.totals[-1]
        moved = ring_next(after(total, *before) if before else total)
        moved = after(moved, *arriving) if arriving else moved
        self.totals.append((moved.astype(wide) + self.term().astype(wide)).astype(low))

    def last(self):
        return self.totals[-1]


def gather_rows(shard):
    mine = lax.all_gather(shard, "fsdp", axis=0, tiled=True)
    return mine, core_swap(mine)


def core_sum(mine, other):
    return (mine.astype(wide) + core_swap(other).astype(wide)).astype(low)


def scatter_rows(both):
    return lax.psum_scatter(both, "fsdp", scatter_dimension=0, tiled=True)


def over_columns(total):
    total = (total.astype(wide) + column_swap(total).astype(wide)).astype(low)
    return total, core_swap(total)


def on_device(
    inputs,
    cotangent,
    lengths,
    attention_weights,
    attention_momentum,
    attention_average,
    ffn_inputs,
    ffn_inputs_momentum,
    ffn_inputs_average,
    ffn_output,
    ffn_output_momentum,
    ffn_output_average,
    gains,
    gains_momentum,
    gains_average,
):
    micro_count, slot, width = inputs.shape
    hidden = ffn_inputs.shape[2]
    shard, down_rows = ffn_inputs.shape[1], ffn_output.shape[0]
    fsdp_size = lax.axis_size("fsdp")
    replicas = lax.axis_size("dp")
    ringed = fsdp_size == RING
    core = lax.axis_index("dp") % 2
    column = lax.axis_index("dp") // 2
    count = micro_count * slot
    half = width // 2
    core_ref = core.astype(jnp.int32).reshape(1)
    other_ref = 1 - core_ref
    column_ref = column.astype(jnp.int32).reshape(1)
    is_first = core == 0

    rows = inputs.reshape(count, width)
    positions = jnp.arange(slot, dtype=jnp.int32)
    valid = (positions[None, :] < lengths).astype(wide).reshape(count, 1)
    errors = (cotangent.reshape(count, width).astype(wide) * valid).astype(low)

    if ringed:
        origins = ring_origins()
        first = 4 * half
        shapes = (shard, first, hidden // 2, down_rows, half)
        packed = pack_all(
            core_ref, column_ref, attention_weights, ffn_inputs, ffn_output, gains
        )
        wholes, there, which_there = None, [], []
        here, which = [packed], [(0, False)]
        for step in range(1, 6):
            if step <= 3:
                onward = [ring_shift(here[0], 1), ring_shift(here[-1], -1)]
            elif step == 4:
                onward = [ring_next(jnp.where(is_first, *here))]
            across = [column_swap(piece[:, first : first + hidden // 2]) for piece in here]
            wholes = place(
                origins, column_ref, which + which_there, here + there, wholes, (0, 1, 2, 3), shapes
            )
            if step == 5:
                break
            extra = [errors] if step == 2 else []
            tied = list(lax.optimization_barrier((*onward, *across, *wholes, *extra)))
            here, rest = tied[: len(onward)], tied[len(onward) :]
            there, wholes = rest[: len(across)], rest[len(across) : len(across) + 4]
            which_there = [(origin, True) for origin, _ in which]
            which = [(origin, False) for origin in [step, step + 4][: len(onward)]]
        w_a, gain_rows = (wholes[0], core_swap(wholes[0])), wholes[3]
    else:
        w_a = gather_rows(pack_attention(core_ref, attention_weights))
        gain_rows = lax.all_gather(gains.astype(low), "fsdp", axis=1, tiled=True)
        gain_rows = jnp.pad(gain_rows, ((0, GAIN_ROWS - 3), (0, 0)))
        w_gu = gather_rows(
            lax.dynamic_index_in_dim(ffn_inputs, core, 0, keepdims=False).astype(low)
        )
        w_d = gather_rows(lax.dynamic_slice_in_dim(ffn_output, core * half, half, 1).astype(low))
    mixed_mine, *kept_mine, gains8 = mixer_forward(core_ref, rows, w_a[0], slot, gain_rows)
    if ringed:
        (across,) = lax.optimization_barrier((*across, mixed_mine, w_a[1]))[:1]
        (w_gu_mine,) = place(origins, column_ref, [(4, True)], [across], [wholes[1]], (1,), shapes)
        wholes = [wholes[0], w_gu_mine, wholes[2], wholes[3]]
        rows = after(rows, *wholes[1:3])
        w_gu, w_d = [(array, core_swap(array)) for array in wholes[1:3]]
    mixed_other, *rest = mixer_forward(
        other_ref, rows, w_a[1], slot, None, (gains8, mixed_mine, w_a[0])
    )
    kept_other, (x1, h2, h2t, h1t) = rest[:4], rest[4:]
    owners = (fsdp_size, down_rows + shard, down_rows) if ringed else None
    places = jnp.concatenate([core_ref, column_ref])
    *grad_gu, gd_mine, gd_other, output, d_x1, d_mixed, go_mine, go_other = ffn(
        places, h2, h2t, errors, w_gu, w_d, x1, (mixed_mine, mixed_other), w_a, lengths[:, 0], gains8, owners
    )

    gm, gu = grad_gu
    arrived_gu = core_swap(gu)
    if ringed:
        mine_do, arrived_do = [gd_mine], [core_swap(gd_other)]
    else:
        mine_do, arrived_do = [gd_mine, go_mine], [core_swap(gd_other), core_swap(go_other)]
    by_owner = (fsdp_size * 2 * shard, 3 * PAIR)
    d_pre = []
    for call in range(4):
        from_half, kept = (other_ref, kept_other) if call < 2 else (core_ref, kept_mine)
        if ringed and call == 1:
            sum_gu = RingSumOverColumns(after(gm, d_pre[0]), arrived_gu)
            sum_gu.cross()
            sum_gu.cross()
            h1t = after(h1t, *sum_gu.sent)
        elif ringed and call > 1:
            sum_gu.cross()
            ahead = [sum_gu.came[2]] if call == 3 else []
            h1t = after(h1t, sum_gu.last(), sum_do.last(), sum_gu.sent[-1], *ahead)
        grads = mixer_backward(
            from_half,
            h1t,
            gains8,
            kept,
            d_mixed,
            slot,
            shard,
            (call % 2,),
            grads if call % 2 else (),
        )
        d_pre.append(grads[1])
        if call == 1:
            grad_other = grads[0]
            if ringed:
                sum_do = RingSum(mine_do, arrived_do)
                sum_do.begin(d_pre[-1])
                sum_gu.begin(d_pre[-1])
                grad_other = after(grad_other, sum_gu.last(), sum_do.last())
            arrived_qfv = [core_swap(grad_other.reshape(by_owner))]
        elif ringed and call > 1:
            sum_do.step(arriving=(d_pre[-1],))
            sum_gu.step(arriving=(d_pre[-1],))
    mine_qfv = [grads[0].reshape(by_owner)]

    def finish_input(*others):
        late = after(d_pre[3], *others) if others else d_pre[3]
        return input_gradient(rows, gains8, (late, d_pre[1]), w_a, d_x1)

    if ringed:
        sum_qfv = RingSum(mine_qfv, arrived_qfv)
        sum_qfv.begin()
        input_grad = None
        for step in range(1, RING - 1):
            if len(sum_gu.came) < RING:
                sum_gu.cross()
            if len(sum_gu.totals) < RING:
                first = [sum_gu.last(), sum_qfv.last()]
                sum_do.step(*{1: first, 4: [input_grad]}.get(step, []))
                sum_gu.step()
            sum_qfv.step()
            if step == 2:
                input_grad = finish_input(sum_qfv.last())
        total_gu, total_do = sum_gu.last(), sum_do.last()
    else:
        both = (gm.astype(wide) + arrived_gu.astype(wide)).astype(low)
        here = (both[0].astype(wide) + column_swap(both[1]).astype(wide)).astype(low)
        total_gu = scatter_rows(here)
        total_do = jnp.concatenate(
            [
                scatter_rows((own.astype(wide) + came.astype(wide)).astype(low))
                for own, came in zip(mine_do, arrived_do)
            ],
            axis=0,
        )
        total_qfv = scatter_rows(
            (mine_qfv[0].astype(wide) + arrived_qfv[0].astype(wide)).astype(low)
        )
        input_grad = finish_input()
    scale_rows = 1.0 / math.sqrt(count * fsdp_size * replicas)
    matrix_step = matrix_rate * scale_rows
    attention_state = (attention_weights, attention_momentum, attention_average)
    ffn_in_state = (ffn_inputs, ffn_inputs_momentum, ffn_inputs_average)
    ffn_out_state = (ffn_output, ffn_output_momentum, ffn_output_average)
    sum_do = over_columns(total_do)
    there = column_swap(total_gu)
    even = jnp.where(column == 0, total_gu, there)
    odd = jnp.where(column == 0, there, total_gu)
    sum_gu = (even, odd), (core_swap(even), core_swap(odd))
    *new_out, _ = update_ffn_out(core_ref, ffn_out_state, sum_do, matrix_step)
    *new_in, dots_up = update_ffn_in(core_ref, ffn_in_state, sum_gu[0], matrix_step, ())
    *new_in, dots_gate = update_ffn_in(other_ref, ffn_in_state, sum_gu[1], matrix_step, new_in)
    if ringed:
        sum_qfv.step(arriving=(new_out[0],))
        total_qfv = sum_qfv.last()
    there = after(column_swap(total_qfv), new_in[0])
    sum_qfv = (total_qfv.astype(wide) + there.astype(wide)).astype(low)
    *own, dots_own = update_attention(
        core_ref, core_ref, attention_state, sum_qfv, sum_do[0], matrix_step, ()
    )
    theirs = after(core_swap(sum_qfv), own[0])
    *new_attention, dots_theirs = update_attention(
        core_ref, other_ref, attention_state, theirs, sum_do[1], matrix_step, own
    )
    dots = jnp.sum(dots_own + dots_theirs, axis=2)
    row_sums = jnp.stack([dots[0] + dots[1] + dots[2], dots[3], jnp.sum(dots_up + dots_gate, axis=2).reshape(-1)])
    sum_gains = row_sums / gains.astype(low).astype(wide)
    return (
        output.reshape(micro_count, slot, width),
        input_grad.reshape(micro_count, slot, width),
        *new_attention,
        *new_in,
        *new_out,
        *update(gains, gains_momentum, gains_average, sum_gains, gain_rate * scale_rows),
    )


def solution(mesh):
    rows_split = P(None, ("fsdp", "dp"), None)
    middle_split = P(None, "fsdp", None)
    first_split = P("fsdp", None)
    gains_split = P(None, "fsdp")
    in_specs = (
        (rows_split, rows_split, P(None, ("fsdp", "dp")))
        + (middle_split,) * 6
        + (first_split,) * 3
        + (gains_split,) * 3
    )
    out_specs = (
        (rows_split, rows_split)
        + (middle_split,) * 6
        + (first_split,) * 3
        + (gains_split,) * 3
    )
    return jax.shard_map(
        on_device, mesh=mesh, in_specs=in_specs, out_specs=out_specs, check_vma=False
    )
```

```python
import functools
import math

import jax
import jax.numpy as jnp
from jax import lax
from jax.experimental import pallas as pl
from jax.experimental.pallas import tpu as pltpu
from jax.sharding import PartitionSpec as P

HEAD_DIM = 128
PAIR = 2 * HEAD_DIM
GAIN_ROWS = 16

lower_bound = 0.9
momentum_decay = 0.9
average_decay = 0.7
weight_decay = 0.0005
matrix_rate = 0.03
gain_rate = 0.1
low = jnp.bfloat16
wide = jnp.float32
TILE_F = 256
VMEM_BYTES = 60 * 1024 * 1024


def mm(left, right):
    return jnp.dot(left, right, preferred_element_type=wide)


def mm_nt(left, right):
    return lax.dot_general(left, right, (((1,), (1,)), ((), ())), preferred_element_type=wide)


def mm_tn(left, right):
    return lax.dot_general(left, right, (((0,), (0,)), ((), ())), preferred_element_type=wide)


def sigmoid(u):
    return 0.5 * jnp.tanh(0.5 * u) + 0.5


def whole(shape):
    return pl.BlockSpec(shape, lambda *_: (0,) * len(shape), pipeline_mode=pl.Buffered(1))


def split_sum(ones_matrix, tensor):
    high = tensor.astype(low)
    rest = (tensor - high.astype(wide)).astype(low)
    return mm(ones_matrix, high) + mm(ones_matrix, rest)


def causal_mask(length, lower):
    rows = lax.broadcasted_iota(jnp.int32, (length, length), 0)
    columns = lax.broadcasted_iota(jnp.int32, (length, length), 1)
    return rows >= columns if lower else rows <= columns


def triangle(length, lower):
    return causal_mask(length, lower).astype(wide).astype(low)


def decay_parts(f_pre, lower_ones):
    share = sigmoid(f_pre)
    gate = lower_bound + (1.0 - lower_bound) * share
    keys_in = (1.0 - lower_bound) * (1.0 - share)
    cumulative = split_sum(lower_ones, jnp.log(gate))
    middle_row = cumulative.shape[0] // 2
    cumulative = cumulative - cumulative[middle_row : middle_row + 1, :]
    return share, gate, keys_in, cumulative


def first_norm(x_ref, gain_row):
    rows = x_ref[...].astype(wide)
    scale = lax.rsqrt(jnp.mean(rows * rows, axis=-1, keepdims=True) + 1e-06)
    return rows * scale, scale


def lanes_of(half, size):
    return pl.ds(pl.multiple_of(half * size, size), size)


def mixer_forward_first_kernel(
    slot, half_ref, x_ref, w_ref, gains_ref, on_ref, q_ref, f_ref, v_ref, o_ref, g_ref, h_s
):
    @pl.when(pl.program_id(0) == 0)
    def _():
        g_ref[...] = gains_ref[...].astype(wide)[: g_ref.shape[0], :]

    mixer_forward_kernel(
        slot, half_ref, x_ref, w_ref, g_ref, on_ref, q_ref, f_ref, v_ref, o_ref, h_s
    )


def mixer_forward_kernel(
    slot, half_ref, x_ref, w_ref, g_ref, on_ref, q_ref, f_ref, v_ref, o_ref, h_s
):
    @pl.when(pl.program_id(0) == 0)
    def _():
        normed, _ = first_norm(x_ref, None)
        h_s[...] = (normed * g_ref[0:1, :]).astype(low)

    gain_o = g_ref[1:2, lanes_of(half_ref[0] * pl.num_programs(0) + pl.program_id(0), PAIR)]
    pre = mm(h_s[...], w_ref[...])
    q_ref[...] = pre[:, :PAIR]
    f_ref[...] = pre[:, PAIR : 2 * PAIR]
    v_ref[...] = pre[:, 2 * PAIR :].astype(low)
    lower_ones = triangle(slot, True)
    causal = causal_mask(slot, True)
    for sequence in range(x_ref.shape[0] // slot):
        rows = slice(sequence * slot, (sequence + 1) * slot)
        q_pre = q_ref[rows, :]
        _, _, keys_in, cumulative = decay_parts(f_ref[rows, :], lower_ones)
        grown = jnp.exp(-cumulative)
        decayed_q = (q_pre * sigmoid(q_pre) * jnp.exp(cumulative)).astype(low)
        grown_k = (keys_in * grown).astype(low)
        values = v_ref[rows, :]
        for head in range(2):
            lanes = slice(head * HEAD_DIM, (head + 1) * HEAD_DIM)
            scores = mm_nt(decayed_q[:, lanes], grown_k[:, lanes])
            out = mm(jnp.where(causal, scores, 0.0).astype(low), values[:, lanes])
            scale = lax.rsqrt(jnp.mean(out * out, axis=-1, keepdims=True) + 1e-05)
            o_ref[rows, lanes] = out.astype(low)
            on_ref[rows, lanes] = (out * scale * gain_o[:, lanes]).astype(low)


def mixer_forward_last_kernel(
    slot,
    half_ref,
    x_ref,
    w_ref,
    g_ref,
    before_ref,
    woo_ref,
    wom_ref,
    on_ref,
    q_ref,
    f_ref,
    v_ref,
    o_ref,
    x1_ref,
    h2_ref,
    h2t_ref,
    h1t_ref,
    h_s,
    on_s,
):
    step = pl.program_id(0)
    half = before_ref.shape[1]
    mixer_forward_kernel(
        slot, half_ref, x_ref, w_ref, g_ref, on_ref, q_ref, f_ref, v_ref, o_ref, h_s
    )
    on_s[:, lanes_of(half_ref[0] * pl.num_programs(0) + step, PAIR)] = on_ref[...]

    @pl.when(step == pl.num_programs(0) - 1)
    def _():
        here = lanes_of(half_ref[0], half)
        there = lanes_of(1 - half_ref[0], half)
        on_s[:, there] = before_ref[...]
        h1t_ref[...] = h_s[...].astype(wide).T.astype(low)
        x1_ref[:, here] = x_ref[:, here].astype(wide) + mm(on_s[...], woo_ref[...])
        x1_ref[:, there] = x_ref[:, there].astype(wide) + mm(on_s[...], wom_ref[...])
        x1 = x1_ref[...]
        scale = lax.rsqrt(jnp.mean(x1 * x1, axis=-1, keepdims=True) + 1e-06)
        normed = x1 * scale * g_ref[2:3, :]
        h2_ref[...] = normed.astype(low)
        h2t_ref[...] = normed.T.astype(low)


def mixer_forward(half, rows, weights, slot, gains=None, ending=None):
    count, width = rows.shape
    pairs = width // PAIR // 2
    by_pair = pl.BlockSpec((count, PAIR), lambda j, _: (0, j))
    struct = jax.ShapeDtypeStruct
    shape = lambda kind: struct((count, width // 2), kind)
    in_specs = [whole(rows.shape), pl.BlockSpec((width, 3 * PAIR), lambda j, _: (0, j))]
    operands = [half, rows, weights]
    out_specs = [by_pair] * 5
    out_shape = [shape(low), shape(wide), shape(wide), shape(low), shape(low)]
    scratch = [pltpu.VMEM((count, width), low)]
    if ending is None:
        kernel = mixer_forward_first_kernel
        in_specs += [whole(gains.shape)]
        operands += [gains]
        out_specs += [whole((8, width))]
        out_shape += [struct((8, width), wide)]
    if ending is not None:
        kernel = mixer_forward_last_kernel
        out_weights = pl.BlockSpec((width, width // 2), lambda j, _: (0, 3))
        in_specs += [whole(ending[0].shape), whole((count, width // 2)), out_weights, out_weights]
        operands += [ending[0], ending[1], weights, ending[2]]
        out_specs += [whole((count, width))] * 2 + [whole((width, count))] * 2
        out_shape += [
            struct((count, width), wide),
            struct((count, width), low),
            struct((width, count), low),
            struct((width, count), low),
        ]
        scratch += [pltpu.VMEM((count, width), low)]
    return pl.pallas_call(
        functools.partial(kernel, slot),
        grid_spec=pltpu.PrefetchScalarGridSpec(
            num_scalar_prefetch=1,
            grid=(pairs,),
            in_specs=in_specs,
            out_specs=out_specs,
            scratch_shapes=scratch,
        ),
        out_shape=out_shape,
        compiler_params=pltpu.CompilerParams(vmem_limit_bytes=VMEM_BYTES),
        cost_estimate=pl.CostEstimate(
            flops=count * width * 4 * width + 10 * count * slot * width,
            bytes_accessed=count * width * 12 + width * width * 4,
            transcendentals=count * width * 3,
        ),
        name="mixer_forward",
    )(*operands)


def store_down(out_ref, tile, owners):
    _, stride, down_rows = owners
    block = math.gcd(down_rows, tile.shape[0])
    first = pl.program_id(0) * (tile.shape[0] // block)
    for part in range(tile.shape[0] // block):
        owner = (first + part) // (down_rows // block)
        inside = (first + part) % (down_rows // block)
        start = pl.multiple_of(owner * stride + inside * block, block)
        out_ref[pl.ds(start, block), :] = tile[part * block : (part + 1) * block, :]


def ffn_kernel(
    owners,
    core_ref,
    h_ref,
    ht_ref,
    e_ref,
    wm_ref,
    wu_ref,
    wdm_ref,
    wdo_ref,
    x1_hbm,
    onm_hbm,
    ono_hbm,
    wom_hbm,
    woo_hbm,
    m_ref,
    g_ref,
    gm_ref,
    gu_ref,
    gdm_hbm,
    gdo_hbm,
    out_hbm,
    dx1_hbm,
    don_hbm,
    *scratch,
):
    gu_w, gu_g, down_g, down_w, mid_s, dh_s, on_s, x1_s, wo_s, out_s, gdm_s, gdo_s = scratch[:12]
    in_semaphores, out_semaphores, down_semaphores = scratch[12:]
    step, last = pl.program_id(0), pl.num_programs(0) - 1
    half, tile = wdm_ref.shape[1], wm_ref.shape[1]
    mine, other = lanes_of(core_ref[0], half), lanes_of(1 - core_ref[0], half)
    kind, kind_other = lanes_of(core_ref[0], tile), lanes_of(1 - core_ref[0], tile)
    count, stride, down_rows = owners

    width = on_s.shape[1]
    sources = (
        (x1_hbm, x1_s),
        (onm_hbm, on_s.at[:, mine]),
        (ono_hbm, on_s.at[:, other]),
        (wom_hbm.at[:, pl.ds(3 * half, half)], wo_s.at[:, mine]),
        (woo_hbm.at[:, pl.ds(3 * half, half)], wo_s.at[:, other]),
    )
    fetches = [
        pltpu.make_async_copy(source, target, in_semaphores.at[number])
        for number, (source, target) in enumerate(sources)
    ]

    def down_copies(owner):
        rows = pl.ds(pl.multiple_of(owner * stride, math.gcd(stride, 32)), down_rows)
        return [
            pltpu.make_async_copy(held.at[rows, :], out.at[rows, :], down_semaphores.at[side, owner])
            for side, (held, out) in enumerate(((gdm_s, gdm_hbm), (gdo_s, gdo_hbm)))
        ]

    @pl.when(step == 0)
    def _():
        dh_s[...] = jnp.zeros_like(dh_s)
        for fetch in fetches:
            fetch.start()

    gu_w[:, kind] = wm_ref[...]
    gu_w[:, kind_other] = wu_ref[...]
    hidden_rows = pl.ds(pl.multiple_of(step * tile, tile), tile)
    down_w[hidden_rows, mine] = wdm_ref[...]
    down_w[hidden_rows, other] = wdo_ref[...]
    pre = mm(h_ref[...], gu_w[...])
    a, b = pre[:, :tile], pre[:, tile:]
    share = sigmoid(a)
    swish = a * share
    mid = (swish * b).astype(low)
    mid_s[:, lanes_of(step, tile)] = mid
    d_mid = mm_nt(e_ref[...], down_w[hidden_rows, :])
    down_g[...] = mm_tn(mid, e_ref[...]).astype(low)
    d_a = (d_mid * b * (share + swish * (1.0 - share))).astype(low)
    d_b = (d_mid * swish).astype(low)
    d_pre = jnp.concatenate([d_a, d_b], axis=1)
    dh_s[...] += mm_nt(d_pre, gu_w[...])
    gu_g[...] = mm(ht_ref[...], d_pre).astype(low)
    blocks = tile // HEAD_DIM
    for side, block in enumerate((core_ref[1], 1 - core_ref[1])):
        gm_ref[side] = gu_g[:, lanes_of(core_ref[0] * blocks + block, HEAD_DIM)]
        gu_ref[side] = gu_g[:, lanes_of((1 - core_ref[0]) * blocks + block, HEAD_DIM)]
    store_down(gdm_s, down_g[:, mine], owners)
    store_down(gdo_s, down_g[:, other], owners)

    done = (step + 1) * tile // down_rows

    @pl.when(done > step * tile // down_rows)
    def _():
        for copy in down_copies(done - 1):
            copy.start()

    @pl.when(step == last)
    def _():
        for fetch in fetches:
            fetch.wait()
        x1 = x1_s[...]
        x2 = x1 + mm(mid_s[...], down_w[...])
        positions = lax.broadcasted_iota(jnp.int32, (out_s.shape[0] // m_ref.shape[0], 1), 0)
        for sequence in range(m_ref.shape[0]):
            rows = slice(sequence * positions.shape[0], (sequence + 1) * positions.shape[0])
            valid = (positions < m_ref[sequence]).astype(wide)
            out_s[rows, :] = (x2[rows, :] * valid).astype(low)
        leaving = [pltpu.make_async_copy(out_s, out_hbm, out_semaphores.at[0])]
        leaving[-1].start()
        scale = lax.rsqrt(jnp.mean(x1 * x1, axis=-1, keepdims=True) + 1e-06)
        normed = x1 * scale
        scaled = dh_s[...] * g_ref[2:3, :]
        d_x1 = e_ref[...].astype(wide) + scale * (
            scaled - normed * jnp.mean(scaled * normed, axis=-1, keepdims=True)
        )
        dh_s[...] = d_x1
        leaving.append(pltpu.make_async_copy(dh_s, dx1_hbm, out_semaphores.at[1]))
        leaving[-1].start()
        d_1 = mid_s.at[:, pl.ds(0, width)]
        d_1[...] = d_x1.astype(low)
        d_mixed = mid_s.at[:, pl.ds(width, width)]
        d_mixed[...] = mm_nt(d_1[...], wo_s[...]).astype(low)
        leaving.append(pltpu.make_async_copy(d_mixed, don_hbm, out_semaphores.at[2]))
        leaving[-1].start()
        rows = stride - down_rows
        grad_o = mm_tn(on_s[...], d_1[...]).astype(low)
        down_w[pl.ds(0, width), :] = grad_o
        for columns, held, out in ((mine, gdm_s, gdm_hbm), (other, gdo_s, gdo_hbm)):
            for owner in range(count):
                target = slice(owner * stride + down_rows, (owner + 1) * stride)
                held[target, :] = down_w[owner * rows : (owner + 1) * rows, columns]
                copy = pltpu.make_async_copy(
                    held.at[target, :], out.at[target, :], out_semaphores.at[len(leaving)]
                )
                copy.start()
                leaving.append(copy)
        for owner in range(count):
            leaving += down_copies(owner)
        for copy in leaving:
            copy.wait()


def ffn(core, h2, h2t, errors, w_gu, w_d, x1, mixed, w_a, lengths, gains8, owners):
    count, width = h2.shape
    half = width // 2
    hidden = w_gu[0].shape[1]
    full = whole((count, width))
    in_tile = pl.BlockSpec((width, TILE_F), lambda j, _: (0, j))
    out_tile = pl.BlockSpec((TILE_F, half), lambda j, _: (j, 0))
    grad_tile = pl.BlockSpec((2, width, HEAD_DIM), lambda j, _: (0, 0, j))
    anywhere = pl.BlockSpec(memory_space=pl.ANY)
    down_shape = (owners[0] * owners[1], half)
    struct = jax.ShapeDtypeStruct
    vmem = pltpu.VMEM
    return pl.pallas_call(
        functools.partial(ffn_kernel, owners),
        grid_spec=pltpu.PrefetchScalarGridSpec(
            num_scalar_prefetch=1,
            grid=(hidden // TILE_F,),
            in_specs=[full, whole(h2t.shape), full, in_tile, in_tile, out_tile, out_tile]
            + [anywhere] * 5
            + [pl.BlockSpec(memory_space=pltpu.SMEM), whole((8, width))],
            out_specs=[grad_tile, grad_tile] + [anywhere] * 5,
            scratch_shapes=[
                vmem((width, 2 * TILE_F), low),
                vmem((width, 2 * TILE_F), low),
                vmem((TILE_F, width), low),
                vmem((hidden, width), low),
                vmem((count, hidden), low),
                vmem((count, width), wide),
                vmem((count, width), low),
                vmem((count, width), wide),
                vmem((width, width), low),
                vmem((count, width), low),
                vmem(down_shape, low),
                vmem(down_shape, low),
                pltpu.SemaphoreType.DMA((5,)),
                pltpu.SemaphoreType.DMA((3 + 2 * owners[0],)),
                pltpu.SemaphoreType.DMA((2, owners[0])),
            ],
        ),
        out_shape=[struct((2, width, hidden // 2), low)] * 2
        + [struct(down_shape, low)] * 2
        + [
            struct((count, width), low),
            struct((count, width), wide),
            struct((count, width), low),
        ],
        compiler_params=pltpu.CompilerParams(vmem_limit_bytes=VMEM_BYTES),
        cost_estimate=pl.CostEstimate(
            flops=18 * count * width * hidden,
            bytes_accessed=count * width * 20 + width * hidden * 12,
            transcendentals=count * hidden,
        ),
        name="ffn",
    )(core, h2, h2t, errors, *w_gu, *w_d, x1, *mixed, *w_a, lengths, gains8)


def mixer_backward_kernel(
    slot,
    per_half,
    first,
    half_ref,
    ht_ref,
    g_ref,
    q_ref,
    f_ref,
    v_ref,
    o_ref,
    don_ref,
    *outs,
):
    grad_ref, dpre_ref = outs[-2:]
    gain_o = g_ref[1:2, lanes_of(half_ref[0] * per_half + first + pl.program_id(0), PAIR)]
    lower_ones = triangle(slot, True)
    upper_ones = triangle(slot, False)
    causal_t = causal_mask(slot, False)
    for sequence in range(q_ref.shape[0] // slot):
        rows = slice(sequence * slot, (sequence + 1) * slot)
        d_on = don_ref[rows, :].astype(wide)
        out = o_ref[rows, :].astype(wide)
        d_out_parts = []
        for head in range(2):
            lanes = slice(head * HEAD_DIM, (head + 1) * HEAD_DIM)
            out_h, d_on_h = out[:, lanes], d_on[:, lanes]
            scale = lax.rsqrt(jnp.mean(out_h * out_h, axis=-1, keepdims=True) + 1e-05)
            normed = out_h * scale
            scaled = d_on_h * gain_o[:, lanes]
            inner = jnp.mean(scaled * normed, axis=-1, keepdims=True)
            d_out_parts.append((scale * (scaled - normed * inner)).astype(low))

        q_pre = q_ref[rows, :]
        share, gate, keys_in, cumulative = decay_parts(f_ref[rows, :], lower_ones)
        grown = jnp.exp(-cumulative)
        shrunk = jnp.exp(cumulative)
        q_share = sigmoid(q_pre)
        decayed_q = (q_pre * q_share * shrunk).astype(low)
        grown_k = (keys_in * grown).astype(low)
        values = v_ref[rows, :]
        dq_parts, dk_parts, dv_parts = [], [], []
        for head in range(2):
            lanes = slice(head * HEAD_DIM, (head + 1) * HEAD_DIM)
            q_h, k_h, v_h = decayed_q[:, lanes], grown_k[:, lanes], values[:, lanes]
            d_out = d_out_parts[head]
            scores = jnp.where(causal_t, mm_nt(k_h, q_h), 0.0).astype(low)
            d_scores = jnp.where(causal_t, mm_nt(v_h, d_out), 0.0).astype(low)
            dv_parts.append(mm(scores, d_out))
            dk_parts.append(mm(d_scores, q_h))
            dq_parts.append(mm_tn(d_scores, k_h))
        d_decayed = jnp.concatenate(dq_parts, axis=1)
        d_grown = jnp.concatenate(dk_parts, axis=1)
        d_value = jnp.concatenate(dv_parts, axis=1)
        d_cumulative = decayed_q.astype(wide) * d_decayed - grown_k.astype(wide) * d_grown
        d_log = split_sum(upper_ones, d_cumulative)
        d_query = d_decayed * shrunk
        d_key = d_grown * grown
        d_q_pre = d_query * q_share * (1.0 + q_pre * (1.0 - q_share))
        d_f_pre = (1.0 - lower_bound) * (d_log / gate - d_key) * share * (1.0 - share)
        dpre_ref[rows, :PAIR] = d_q_pre.astype(low)
        dpre_ref[rows, PAIR : 2 * PAIR] = d_f_pre.astype(low)
        dpre_ref[rows, 2 * PAIR :] = d_value.astype(low)

    grad = mm(ht_ref[...], dpre_ref[...]).astype(low)
    grad_ref[...] = grad.reshape(grad_ref.shape)


def mixer_backward(half, h1t, gains8, kept, d_mixed, slot, shard, pairs=(0, 1), before=()):
    width, count = h1t.shape
    per_half = width // PAIR // 2
    first = pairs[0]
    by_pair = pl.BlockSpec((count, PAIR), lambda j, _: (0, first + j))
    from_whole = pl.BlockSpec((count, PAIR), lambda j, half: (0, half[0] * per_half + first + j))
    struct = jax.ShapeDtypeStruct
    return pl.pallas_call(
        functools.partial(mixer_backward_kernel, slot, per_half, first),
        grid_spec=pltpu.PrefetchScalarGridSpec(
            num_scalar_prefetch=1,
            grid=(len(pairs),),
            in_specs=[whole((width, count)), whole(gains8.shape)]
            + [by_pair] * 4
            + [from_whole]
            + [pl.BlockSpec(memory_space=pl.ANY)] * len(before),
            out_specs=[
                pl.BlockSpec(
                    (width // shard, 1, shard, 3 * PAIR), lambda j, _: (0, first + j, 0, 0)
                ),
                pl.BlockSpec((count, 3 * PAIR), lambda j, _: (0, first + j)),
            ],
        ),
        out_shape=[
            struct((width // shard, per_half, shard, 3 * PAIR), low),
            struct((count, per_half * 3 * PAIR), low),
        ],
        input_output_aliases={8 + k: k for k in range(len(before))},
        compiler_params=pltpu.CompilerParams(vmem_limit_bytes=VMEM_BYTES),
        cost_estimate=pl.CostEstimate(
            flops=len(pairs) * (count * width * 6 * PAIR + 20 * count * slot * PAIR),
            bytes_accessed=len(pairs) * (count * width * 5 + width * PAIR * 6),
            transcendentals=len(pairs) * count * PAIR * 6,
        ),
        name="mixer_backward",
    )(half, h1t, gains8, *kept, d_mixed, *before)


def input_gradient_rows_kernel(
    x_ref, g_ref, dm_ref, do_ref, wm_ref, wo_ref, dx1_ref, dx_ref
):
    d_h1 = mm_nt(dm_ref[...], wm_ref[...]) + mm_nt(do_ref[...], wo_ref[...])
    normed, scale = first_norm(x_ref, None)
    scaled = d_h1 * g_ref[0:1, :]
    dx_ref[...] = dx1_ref[...] + scale * (
        scaled - normed * jnp.mean(scaled * normed, axis=-1, keepdims=True)
    )


def input_gradient(rows, gains8, d_pre, weights, d_x1):
    count, width = rows.shape
    block = count // 2
    columns = d_pre[0].shape[1]
    by_rows = lambda columns: pl.BlockSpec((block, columns), lambda j: (j, 0))
    weight_spec = pl.BlockSpec((width, columns), lambda j: (0, 0), pipeline_mode=pl.Buffered(1))
    return pl.pallas_call(
        input_gradient_rows_kernel,
        grid=(count // block,),
        in_specs=[by_rows(width), whole(gains8.shape)]
        + [by_rows(columns)] * 2
        + [weight_spec] * 2
        + [by_rows(width)],
        out_specs=by_rows(width),
        out_shape=jax.ShapeDtypeStruct((count, width), wide),
        compiler_params=pltpu.CompilerParams(vmem_limit_bytes=VMEM_BYTES),
        cost_estimate=pl.CostEstimate(
            flops=6 * count * width * width,
            bytes_accessed=count * width * 16 + width * width * 6,
            transcendentals=0,
        ),
        name="input_gradient",
    )(rows, gains8, *d_pre, *weights, d_x1)


def update(weight, momentum, average, gradient, step_rate):
    new_momentum = momentum_decay * momentum + gradient
    direction = gradient + momentum_decay * new_momentum + weight_decay * weight
    new_weight = weight - step_rate * direction
    new_average = average_decay * average + (1.0 - average_decay) * new_weight
    return (new_momentum, new_average, new_weight)


def update_kernel(pick, step_rate, sum_count, core_ref, w_ref, m_ref, a_ref, *refs):
    sums, outs, dots_ref = refs[:sum_count], refs[-4:-1], refs[-1]
    weight = w_ref[...]
    gradient = pick(core_ref[0], *[s[...] for s in sums]).astype(wide).reshape(weight.shape)
    results = update(weight, m_ref[...], a_ref[...], gradient, step_rate)
    for out, result in zip(outs, results):
        out[...] = result
    product = weight.astype(low).astype(wide) * gradient
    total = product[..., :HEAD_DIM]
    for start in range(HEAD_DIM, product.shape[-1], HEAD_DIM):
        total = total + product[..., start : start + HEAD_DIM]
    dots_ref[...] = total.reshape(dots_ref.shape)


def update_call(
    core, state, sums, grid, state_spec, sum_specs, pick, step_rate, name, before=()
):
    struct = jax.ShapeDtypeStruct(state[0].shape, wide)
    size = math.prod(state[0].shape)
    rows = state_spec.block_shape[-2]
    steps = math.prod(grid)
    tail = grid[1:]

    def dots_index(*indices):
        place = indices[0]
        for length, index in zip(tail, indices[1:]):
            place = place * length + index
        return (place, 0, 0)

    return pl.pallas_call(
        functools.partial(update_kernel, pick, step_rate, len(sums)),
        grid_spec=pltpu.PrefetchScalarGridSpec(
            num_scalar_prefetch=1,
            grid=grid,
            in_specs=[state_spec] * 3
            + sum_specs
            + [pl.BlockSpec(memory_space=pl.ANY)] * len(before),
            out_specs=[state_spec] * 3 + [pl.BlockSpec((1, rows, HEAD_DIM), dots_index)],
        ),
        out_shape=[struct] * 3 + [jax.ShapeDtypeStruct((steps, rows, HEAD_DIM), wide)],
        input_output_aliases={4 + len(sums) + k: k for k in range(len(before))},
        compiler_params=pltpu.CompilerParams(vmem_limit_bytes=VMEM_BYTES),
        cost_estimate=pl.CostEstimate(flops=12 * size, bytes_accessed=26 * size, transcendentals=0),
        name=name,
    )(core, *state, *sums, *before)


def update_attention(core, half_ref, state, qfv, out, step_rate, before):
    _, shard, width = state[0].shape
    down_rows = out.shape[0] - shard

    def pick(core_index, proj, last):
        gradient = last[down_rows:].astype(wide)
        for kind in range(3):
            parts = [proj[pair * shard :, kind * PAIR :][:shard, :PAIR] for pair in range(2)]
            chosen = jnp.concatenate(parts, axis=1).astype(wide)
            gradient = jnp.where(pl.program_id(0) == kind, chosen, gradient)
        return gradient

    return update_call(
        half_ref,
        state,
        (qfv, out),
        (4,),
        pl.BlockSpec((1, shard, width // 2), lambda kind, half: (kind, 0, half[0])),
        [whole(qfv.shape), whole(out.shape)],
        pick,
        step_rate,
        "update_attention",
        before,
    )


def update_ffn_in(kind_ref, state, totals, step_rate, before):
    _, shard, hidden = state[0].shape
    block = shard // 2

    def pick(_, even, odd):
        blocks = []
        for start in range(0, hidden // 2, HEAD_DIM):
            blocks += [even[:, start : start + HEAD_DIM], odd[:, start : start + HEAD_DIM]]
        return jnp.concatenate(blocks, axis=1)

    return update_call(
        kind_ref,
        state,
        totals,
        (2,),
        pl.BlockSpec((1, block, hidden), lambda j, kind: (kind[0], j, 0)),
        [pl.BlockSpec((block, hidden // 2), lambda j, _: (j, 0))] * 2,
        pick,
        step_rate,
        "update_ffn_in",
        before,
    )


def update_ffn_out(core, state, sums, step_rate):
    shard, width = state[0].shape

    def pick(core_index, mine, other):
        own = pl.program_id(0) == core_index
        return jnp.where(own, mine[:shard].astype(wide), other[:shard].astype(wide))

    return update_call(
        core,
        state,
        sums,
        (2,),
        pl.BlockSpec((shard, width // 2), lambda j, _: (0, j)),
        [whole(total.shape) for total in sums],
        pick,
        step_rate,
        "update_ffn_out",
    )


def pack_kernel(core_ref, w_ref, out_ref):
    half = w_ref.shape[2]
    for pair in range(half // PAIR):
        for kind in range(3):
            start = (pair * 3 + kind) * PAIR
            piece = w_ref[kind, :, pair * PAIR : (pair + 1) * PAIR]
            out_ref[:, start : start + PAIR] = piece.astype(low)
    out_ref[:, 3 * half : 4 * half] = w_ref[3].astype(low)


def pack_attention(core, weights):
    _, shard, width = weights.shape
    half = width // 2
    return pl.pallas_call(
        pack_kernel,
        grid_spec=pltpu.PrefetchScalarGridSpec(
            num_scalar_prefetch=1,
            grid=(1,),
            in_specs=[pl.BlockSpec((4, shard, half), lambda j, core: (0, 0, core[0]))],
            out_specs=whole((shard, 4 * half)),
        ),
        out_shape=jax.ShapeDtypeStruct((shard, 4 * half), low),
        name="pack_attention",
    )(core, weights)


RING = 8


def ring_place(index):
    return jnp.where(index % 2 == 0, index // 2, RING - 1 - index // 2)


def ring_member(place):
    place = place % RING
    return jnp.where(place < RING // 2, 2 * place, 2 * RING - 1 - 2 * place)


CYCLE = (0, 2, 4, 6, 7, 5, 3, 1)


def ring_next(tensor):
    replicas = lax.axis_size("dp")
    pairs = []
    for place_of, member in enumerate(CYCLE):
        for replica in range(replicas):
            target = CYCLE[(place_of + (1 if replica % 2 == 0 else -1)) % RING]
            pairs.append((member * replicas + replica, target * replicas + replica))
    return lax.ppermute(tensor, ("fsdp", "dp"), pairs)


def ring_shift(tensor, way):
    pairs = [(member, CYCLE[(at + way) % RING]) for at, member in enumerate(CYCLE)]
    return lax.ppermute(tensor, "fsdp", pairs)


def core_swap(tensor):
    return lax.ppermute(tensor, "dp", [(d, d ^ 1) for d in range(lax.axis_size("dp"))])


def column_swap(tensor):
    return lax.ppermute(tensor, "dp", [(d, d ^ 2) for d in range(lax.axis_size("dp"))])


def pack_all_kernel(core_ref, column_ref, w_ref, up_ref, down_ref, g_ref, out_ref):
    shard = w_ref.shape[1]
    half = w_ref.shape[2]
    for pair in range(half // PAIR):
        for kind in range(3):
            start = (pair * 3 + kind) * PAIR
            piece = w_ref[kind, :, pair * PAIR : (pair + 1) * PAIR]
            out_ref[:, start : start + PAIR] = piece.astype(low)
    out_ref[:, 3 * half : 4 * half] = w_ref[3].astype(low)
    start = 4 * half
    out_ref[:, start : start + up_ref.shape[2]] = up_ref[0].astype(low)
    start += up_ref.shape[2]
    for first, count in down_parts(down_ref.shape[0], shard):
        out_ref[:count, start : start + half] = down_ref[first : first + count, :].astype(low)
        if count < shard:
            out_ref[count:, start : start + half] = jnp.zeros((shard - count, half), low)
            rows = lax.broadcasted_iota(jnp.int32, (GAIN_ROWS, g_ref.shape[1]), 0)
            gains = jnp.where(rows == 1, g_ref[1:2, :], g_ref[2:3, :])
            gains = jnp.where(rows == 0, g_ref[0:1, :], gains)
            gains = jnp.where(rows < 3, gains, 0.0).astype(low)
            out_ref[count : count + GAIN_ROWS, start : start + g_ref.shape[1]] = gains
        start += half


def down_parts(down_rows, shard):
    return [(start, min(shard, down_rows - start)) for start in range(0, down_rows, shard)]


def pack_all(core, column, weights, up, down, gains):
    _, shard, width = weights.shape
    half = width // 2
    parts = len(down_parts(down.shape[0], shard))
    columns = 4 * half + up.shape[2] // 2 + parts * half
    return pl.pallas_call(
        pack_all_kernel,
        grid_spec=pltpu.PrefetchScalarGridSpec(
            num_scalar_prefetch=2,
            grid=(1,),
            in_specs=[
                pl.BlockSpec((4, shard, half), lambda j, core, column: (0, 0, core[0])),
                pl.BlockSpec(
                    (1, shard, up.shape[2] // 2), lambda j, core, column: (core[0], 0, column[0])
                ),
                pl.BlockSpec((down.shape[0], half), lambda j, core, column: (0, core[0])),
                whole(gains.shape),
            ],
            out_specs=whole((shard, columns)),
        ),
        out_shape=jax.ShapeDtypeStruct((shard, columns), low),
        compiler_params=pltpu.CompilerParams(vmem_limit_bytes=VMEM_BYTES),
        name="pack_all",
    )(core, column, weights, up, down, gains)


def place_kernel(which, kept, shapes, origin_ref, column_ref, *refs):
    pieces, outs, semaphores = refs[: len(which)], refs[-1 - len(kept) : -1], refs[-1]
    targets = dict(zip(kept, outs))
    shard, first, up_columns, down_rows, half = shapes
    copies = []

    def copy(source, target):
        copies.append(pltpu.make_async_copy(source, target, semaphores.at[len(copies)]))

    for piece, (origin, across) in zip(pieces, which):
        owner = origin_ref[origin]
        rows = pl.ds(pl.multiple_of(owner * shard, 16), shard)
        if across:
            copy(piece, targets[1].at[rows, lanes_of(1 - column_ref[0], up_columns)])
            continue
        copy(piece.at[:, pl.ds(0, first)], targets[0].at[rows, :])
        own = targets[1].at[rows, lanes_of(column_ref[0], up_columns)]
        copy(piece.at[:, pl.ds(first, up_columns)], own)
        lane = first + up_columns
        for start, count in down_parts(down_rows, shard):
            target = pl.ds(pl.multiple_of(owner * down_rows + start, 16), count)
            copy(piece.at[pl.ds(0, count), pl.ds(lane, half)], targets[2].at[target, :])
            if count < shard:
                source = piece.at[pl.ds(count, GAIN_ROWS), pl.ds(lane, shard)]
                copy(source, targets[3].at[:, lanes_of(owner, shard)])
            lane += half
    for one in copies:
        one.start()
    for one in copies:
        one.wait()


def place(origins, column, which, pieces, arrays, kept, shapes):
    anywhere = pl.BlockSpec(memory_space=pl.ANY)
    shard, first, up_columns, down_rows, half = shapes
    kinds = [(RING * shard, first), (RING * shard, 2 * up_columns), (RING * down_rows, half)]
    kinds.append((GAIN_ROWS, RING * shard))
    held = [] if arrays is None else list(arrays)
    size = sum(math.prod(piece.shape) for piece in pieces)
    before = 2 + len(pieces)
    return pl.pallas_call(
        functools.partial(place_kernel, which, kept, shapes),
        grid_spec=pltpu.PrefetchScalarGridSpec(
            num_scalar_prefetch=2,
            grid=(1,),
            in_specs=[whole(piece.shape) for piece in pieces] + [anywhere] * len(held),
            out_specs=[anywhere] * len(kept),
            scratch_shapes=[pltpu.SemaphoreType.DMA((8 * len(pieces),))],
        ),
        out_shape=[jax.ShapeDtypeStruct(kinds[k], pieces[0].dtype) for k in kept],
        input_output_aliases={before + k: k for k in range(len(held))},
        compiler_params=pltpu.CompilerParams(vmem_limit_bytes=VMEM_BYTES),
        cost_estimate=pl.CostEstimate(flops=0, bytes_accessed=8 * size, transcendentals=0),
        name="place",
    )(origins, column, *pieces, *held)


def after(tensor, *others):
    return lax.optimization_barrier((tensor, *others))[0]


def core_way():
    return 1 - 2 * (lax.axis_index("dp") % 2)


def ring_origins():
    steps = jnp.array((0, -1, -2, -3, -4, 1, 2, 3), jnp.int32)
    return ring_member(ring_place(lax.axis_index("fsdp")) + steps + RING).astype(jnp.int32)


class RingSumOverColumns:
    def __init__(self, mine, arrived):
        self.arrays = (mine, arrived)
        place = ring_place(lax.axis_index("fsdp"))
        self.rows = mine.shape[1] // RING
        self.starts = [
            ring_member(place - core_way() * (s + 1) + 2 * RING) * self.rows for s in range(RING)
        ]
        self.sent, self.came, self.totals = [], [], []

    def part(self, side, step):
        shape = (1, self.rows, self.arrays[0].shape[2])
        parts = [
            lax.dynamic_slice(array, (side, self.starts[step], 0), shape)[0]
            for array in self.arrays
        ]
        return parts[0].astype(wide) + parts[1].astype(wide)

    def cross(self):
        self.sent.append(self.part(1, len(self.sent)).astype(low))
        self.came.append(column_swap(self.sent[-1]))

    def term(self):
        step = len(self.totals)
        return self.part(0, step) + self.came[step].astype(wide)

    def begin(self, *others):
        self.came[0] = after(self.came[0], *others) if others else self.came[0]
        self.totals.append(self.term().astype(low))

    def step(self, arriving=()):
        total, ahead = self.totals[-1], self.came[len(self.totals)]
        moved = ring_next(after(total, ahead) if len(self.totals) > 1 else total)
        moved = after(moved, *arriving) if arriving else moved
        self.totals.append((moved.astype(wide) + self.term()).astype(low))

    def last(self):
        return self.totals[-1]


class RingSum:
    def __init__(self, mine, arrived):
        self.mine, self.arrived = mine, arrived
        place = ring_place(lax.axis_index("fsdp"))
        self.owners = [ring_member(place - core_way() * (s + 1) + 2 * RING) for s in range(RING)]
        self.totals = []

    def term(self):
        parts = []
        for own, arrived in zip(self.mine, self.arrived):
            rows = own.shape[0] // RING
            start = self.owners[len(self.totals)] * rows
            part = lax.dynamic_slice_in_dim(own, start, rows, 0).astype(wide)
            parts.append(part + lax.dynamic_slice_in_dim(arrived, start, rows, 0).astype(wide))
        return parts[0] if len(parts) == 1 else jnp.concatenate(parts, axis=0)

    def begin(self, *others):
        if others:
            self.mine = [after(self.mine[0], *others), *self.mine[1:]]
        self.totals.append(self.term().astype(low))

    def step(self, *before, arriving=()):
        total = self.totals[-1]
        moved = ring_next(after(total, *before) if before else total)
        moved = after(moved, *arriving) if arriving else moved
        self.totals.append((moved.astype(wide) + self.term().astype(wide)).astype(low))

    def last(self):
        return self.totals[-1]


def gather_rows(shard):
    mine = lax.all_gather(shard, "fsdp", axis=0, tiled=True)
    return mine, core_swap(mine)


def core_sum(mine, other):
    return (mine.astype(wide) + core_swap(other).astype(wide)).astype(low)


def scatter_rows(both):
    return lax.psum_scatter(both, "fsdp", scatter_dimension=0, tiled=True)


def over_columns(total):
    total = (total.astype(wide) + column_swap(total).astype(wide)).astype(low)
    return total, core_swap(total)


def on_device(
    inputs,
    cotangent,
    lengths,
    attention_weights,
    attention_momentum,
    attention_average,
    ffn_inputs,
    ffn_inputs_momentum,
    ffn_inputs_average,
    ffn_output,
    ffn_output_momentum,
    ffn_output_average,
    gains,
    gains_momentum,
    gains_average,
):
    micro_count, slot, width = inputs.shape
    hidden = ffn_inputs.shape[2]
    shard, down_rows = ffn_inputs.shape[1], ffn_output.shape[0]
    fsdp_size = lax.axis_size("fsdp")
    replicas = lax.axis_size("dp")
    ringed = fsdp_size == RING
    core = lax.axis_index("dp") % 2
    column = lax.axis_index("dp") // 2
    count = micro_count * slot
    half = width // 2
    core_ref = core.astype(jnp.int32).reshape(1)
    other_ref = 1 - core_ref
    column_ref = column.astype(jnp.int32).reshape(1)
    is_first = core == 0

    rows = inputs.reshape(count, width)
    positions = jnp.arange(slot, dtype=jnp.int32)
    valid = (positions[None, :] < lengths).astype(wide).reshape(count, 1)
    errors = (cotangent.reshape(count, width).astype(wide) * valid).astype(low)

    if ringed:
        origins = ring_origins()
        first = 4 * half
        shapes = (shard, first, hidden // 2, down_rows, half)
        packed = pack_all(
            core_ref, column_ref, attention_weights, ffn_inputs, ffn_output, gains
        )
        wholes, there, which_there = None, [], []
        here, which = [packed], [(0, False)]
        for step in range(1, 6):
            if step <= 3:
                onward = [ring_shift(here[0], 1), ring_shift(here[-1], -1)]
            elif step == 4:
                onward = [ring_next(jnp.where(is_first, *here))]
            across = [column_swap(piece[:, first : first + hidden // 2]) for piece in here]
            wholes = place(
                origins, column_ref, which + which_there, here + there, wholes, (0, 1, 2, 3), shapes
            )
            if step == 5:
                break
            extra = [errors] if step == 2 else []
            tied = list(lax.optimization_barrier((*onward, *across, *wholes, *extra)))
            here, rest = tied[: len(onward)], tied[len(onward) :]
            there, wholes = rest[: len(across)], rest[len(across) : len(across) + 4]
            which_there = [(origin, True) for origin, _ in which]
            which = [(origin, False) for origin in [step, step + 4][: len(onward)]]
        w_a, gain_rows = (wholes[0], core_swap(wholes[0])), wholes[3]
    else:
        w_a = gather_rows(pack_attention(core_ref, attention_weights))
        gain_rows = lax.all_gather(gains.astype(low), "fsdp", axis=1, tiled=True)
        gain_rows = jnp.pad(gain_rows, ((0, GAIN_ROWS - 3), (0, 0)))
        w_gu = gather_rows(
            lax.dynamic_index_in_dim(ffn_inputs, core, 0, keepdims=False).astype(low)
        )
        w_d = gather_rows(lax.dynamic_slice_in_dim(ffn_output, core * half, half, 1).astype(low))
    mixed_mine, *kept_mine, gains8 = mixer_forward(core_ref, rows, w_a[0], slot, gain_rows)
    if ringed:
        (across,) = lax.optimization_barrier((*across, mixed_mine, w_a[1]))[:1]
        (w_gu_mine,) = place(origins, column_ref, [(4, True)], [across], [wholes[1]], (1,), shapes)
        wholes = [wholes[0], w_gu_mine, wholes[2], wholes[3]]
        rows = after(rows, *wholes[1:3])
        w_gu, w_d = [(array, core_swap(array)) for array in wholes[1:3]]
    mixed_other, *rest = mixer_forward(
        other_ref, rows, w_a[1], slot, None, (gains8, mixed_mine, w_a[0])
    )
    kept_other, (x1, h2, h2t, h1t) = rest[:4], rest[4:]
    owners = (RING, down_rows + shard, down_rows)
    if not ringed:
        owners = (1, hidden + width, hidden)
    places = jnp.concatenate([core_ref, column_ref])
    *grad_gu, gd_mine, gd_other, output, d_x1, d_mixed = ffn(
        places, h2, h2t, errors, w_gu, w_d, x1, (mixed_mine, mixed_other), w_a, lengths[:, 0], gains8, owners
    )

    gm, gu = grad_gu
    arrived_gu = core_swap(gu)
    mine_do, arrived_do = [gd_mine], [core_swap(gd_other)]
    by_owner = (fsdp_size * 2 * shard, 3 * PAIR)
    d_pre = []
    for call in range(4):
        from_half, kept = (other_ref, kept_other) if call < 2 else (core_ref, kept_mine)
        if ringed and call == 1:
            sum_gu = RingSumOverColumns(after(gm, d_pre[0]), arrived_gu)
            sum_gu.cross()
            sum_gu.cross()
            h1t = after(h1t, *sum_gu.sent)
        elif ringed and call > 1:
            sum_gu.cross()
            ahead = [sum_gu.came[2]] if call == 3 else []
            h1t = after(h1t, sum_gu.last(), sum_do.last(), sum_gu.sent[-1], *ahead)
        grads = mixer_backward(
            from_half,
            h1t,
            gains8,
            kept,
            d_mixed,
            slot,
            shard,
            (call % 2,),
            grads if call % 2 else (),
        )
        d_pre.append(grads[1])
        if call == 1:
            grad_other = grads[0]
            if ringed:
                sum_do = RingSum(mine_do, arrived_do)
                sum_do.begin(d_pre[-1])
                sum_gu.begin(d_pre[-1])
                grad_other = after(grad_other, sum_gu.last(), sum_do.last())
            arrived_qfv = [core_swap(grad_other.reshape(by_owner))]
        elif ringed and call > 1:
            sum_do.step(arriving=(d_pre[-1],))
            sum_gu.step(arriving=(d_pre[-1],))
    mine_qfv = [grads[0].reshape(by_owner)]

    def finish_input(*others):
        late = after(d_pre[3], *others) if others else d_pre[3]
        return input_gradient(rows, gains8, (late, d_pre[1]), w_a, d_x1)

    if ringed:
        sum_qfv = RingSum(mine_qfv, arrived_qfv)
        sum_qfv.begin()
        input_grad = None
        for step in range(1, RING - 1):
            if len(sum_gu.came) < RING:
                sum_gu.cross()
            if len(sum_gu.totals) < RING:
                first = [sum_gu.last(), sum_qfv.last()]
                sum_do.step(*{1: first, 4: [input_grad]}.get(step, []))
                sum_gu.step()
            sum_qfv.step()
            if step == 2:
                input_grad = finish_input(sum_qfv.last())
        total_gu, total_do = sum_gu.last(), sum_do.last()
    else:
        both = (gm.astype(wide) + arrived_gu.astype(wide)).astype(low)
        here = (both[0].astype(wide) + column_swap(both[1]).astype(wide)).astype(low)
        total_gu = scatter_rows(here)
        both = (gd_mine.astype(wide) + arrived_do[0].astype(wide)).astype(low)
        total_do = jnp.concatenate(
            [scatter_rows(both[:hidden]), scatter_rows(both[hidden:])], axis=0
        )
        total_qfv = scatter_rows(
            (mine_qfv[0].astype(wide) + arrived_qfv[0].astype(wide)).astype(low)
        )
        input_grad = finish_input()
    scale_rows = 1.0 / math.sqrt(count * fsdp_size * replicas)
    matrix_step = matrix_rate * scale_rows
    attention_state = (attention_weights, attention_momentum, attention_average)
    ffn_in_state = (ffn_inputs, ffn_inputs_momentum, ffn_inputs_average)
    ffn_out_state = (ffn_output, ffn_output_momentum, ffn_output_average)
    sum_do = over_columns(total_do)
    there = column_swap(total_gu)
    even = jnp.where(column == 0, total_gu, there)
    odd = jnp.where(column == 0, there, total_gu)
    sum_gu = (even, odd), (core_swap(even), core_swap(odd))
    *new_out, _ = update_ffn_out(core_ref, ffn_out_state, sum_do, matrix_step)
    *new_in, dots_up = update_ffn_in(core_ref, ffn_in_state, sum_gu[0], matrix_step, ())
    *new_in, dots_gate = update_ffn_in(other_ref, ffn_in_state, sum_gu[1], matrix_step, new_in)
    if ringed:
        sum_qfv.step(arriving=(new_out[0],))
        total_qfv = sum_qfv.last()
    there = after(column_swap(total_qfv), new_in[0])
    sum_qfv = (total_qfv.astype(wide) + there.astype(wide)).astype(low)
    *own, dots_own = update_attention(
        core_ref, core_ref, attention_state, sum_qfv, sum_do[0], matrix_step, ()
    )
    theirs = after(core_swap(sum_qfv), own[0])
    *new_attention, dots_theirs = update_attention(
        core_ref, other_ref, attention_state, theirs, sum_do[1], matrix_step, own
    )
    dots = jnp.sum(dots_own + dots_theirs, axis=2)
    row_sums = jnp.stack([dots[0] + dots[1] + dots[2], dots[3], jnp.sum(dots_up + dots_gate, axis=2).reshape(-1)])
    sum_gains = row_sums / gains.astype(low).astype(wide)
    return (
        output.reshape(micro_count, slot, width),
        input_grad.reshape(micro_count, slot, width),
        *new_attention,
        *new_in,
        *new_out,
        *update(gains, gains_momentum, gains_average, sum_gains, gain_rate * scale_rows),
    )


def solution(mesh):
    rows_split = P(None, ("fsdp", "dp"), None)
    middle_split = P(None, "fsdp", None)
    first_split = P("fsdp", None)
    gains_split = P(None, "fsdp")
    in_specs = (
        (rows_split, rows_split, P(None, ("fsdp", "dp")))
        + (middle_split,) * 6
        + (first_split,) * 3
        + (gains_split,) * 3
    )
    out_specs = (
        (rows_split, rows_split)
        + (middle_split,) * 6
        + (first_split,) * 3
        + (gains_split,) * 3
    )
    return jax.shard_map(
        on_device, mesh=mesh, in_specs=in_specs, out_specs=out_specs, check_vma=False
    )
```

```python
import functools
import math

import jax
import jax.numpy as jnp
from jax import lax
from jax.experimental import pallas as pl
from jax.experimental.pallas import tpu as pltpu
from jax.sharding import PartitionSpec as P

HEAD_DIM = 128
PAIR = 2 * HEAD_DIM
GAIN_ROWS = 16

lower_bound = 0.9
momentum_decay = 0.9
average_decay = 0.7
weight_decay = 0.0005
matrix_rate = 0.03
gain_rate = 0.1
low = jnp.bfloat16
wide = jnp.float32
TILE_F = 256
VMEM_BYTES = 60 * 1024 * 1024


def mm(left, right):
    return jnp.dot(left, right, preferred_element_type=wide)


def mm_nt(left, right):
    return lax.dot_general(left, right, (((1,), (1,)), ((), ())), preferred_element_type=wide)


def mm_tn(left, right):
    return lax.dot_general(left, right, (((0,), (0,)), ((), ())), preferred_element_type=wide)


def sigmoid(u):
    return 0.5 * jnp.tanh(0.5 * u) + 0.5


def whole(shape):
    return pl.BlockSpec(shape, lambda *_: (0,) * len(shape), pipeline_mode=pl.Buffered(1))


def split_sum(ones_matrix, tensor):
    high = tensor.astype(low)
    rest = (tensor - high.astype(wide)).astype(low)
    return mm(ones_matrix, high) + mm(ones_matrix, rest)


def causal_mask(length, lower):
    rows = lax.broadcasted_iota(jnp.int32, (length, length), 0)
    columns = lax.broadcasted_iota(jnp.int32, (length, length), 1)
    return rows >= columns if lower else rows <= columns


def triangle(length, lower):
    return causal_mask(length, lower).astype(wide).astype(low)


def decay_parts(f_pre, lower_ones):
    share = sigmoid(f_pre)
    gate = lower_bound + (1.0 - lower_bound) * share
    keys_in = (1.0 - lower_bound) * (1.0 - share)
    cumulative = split_sum(lower_ones, jnp.log(gate))
    middle_row = cumulative.shape[0] // 2
    cumulative = cumulative - cumulative[middle_row : middle_row + 1, :]
    return share, gate, keys_in, cumulative


def first_norm(x_ref, gain_row):
    rows = x_ref[...].astype(wide)
    scale = lax.rsqrt(jnp.mean(rows * rows, axis=-1, keepdims=True) + 1e-06)
    return rows * scale, scale


def lanes_of(half, size):
    return pl.ds(pl.multiple_of(half * size, size), size)


def mixer_forward_first_kernel(
    slot, half_ref, x_ref, w_ref, gains_ref, on_ref, q_ref, f_ref, v_ref, o_ref, g_ref, h_s
):
    @pl.when(pl.program_id(0) == 0)
    def _():
        g_ref[...] = gains_ref[...].astype(wide)[: g_ref.shape[0], :]

    mixer_forward_kernel(
        slot, half_ref, x_ref, w_ref, g_ref, on_ref, q_ref, f_ref, v_ref, o_ref, h_s
    )


def mixer_forward_kernel(
    slot, half_ref, x_ref, w_ref, g_ref, on_ref, q_ref, f_ref, v_ref, o_ref, h_s
):
    @pl.when(pl.program_id(0) == 0)
    def _():
        normed, _ = first_norm(x_ref, None)
        h_s[...] = (normed * g_ref[0:1, :]).astype(low)

    gain_o = g_ref[1:2, lanes_of(half_ref[0] * pl.num_programs(0) + pl.program_id(0), PAIR)]
    pre = mm(h_s[...], w_ref[...])
    q_ref[...] = pre[:, :PAIR]
    f_ref[...] = pre[:, PAIR : 2 * PAIR]
    v_ref[...] = pre[:, 2 * PAIR :].astype(low)
    lower_ones = triangle(slot, True)
    causal = causal_mask(slot, True)
    for sequence in range(x_ref.shape[0] // slot):
        rows = slice(sequence * slot, (sequence + 1) * slot)
        q_pre = q_ref[rows, :]
        _, _, keys_in, cumulative = decay_parts(f_ref[rows, :], lower_ones)
        grown = jnp.exp(-cumulative)
        decayed_q = (q_pre * sigmoid(q_pre) * jnp.exp(cumulative)).astype(low)
        grown_k = (keys_in * grown).astype(low)
        values = v_ref[rows, :]
        for head in range(2):
            lanes = slice(head * HEAD_DIM, (head + 1) * HEAD_DIM)
            scores = mm_nt(decayed_q[:, lanes], grown_k[:, lanes])
            out = mm(jnp.where(causal, scores, 0.0).astype(low), values[:, lanes])
            scale = lax.rsqrt(jnp.mean(out * out, axis=-1, keepdims=True) + 1e-05)
            o_ref[rows, lanes] = out.astype(low)
            on_ref[rows, lanes] = (out * scale * gain_o[:, lanes]).astype(low)


def mixer_forward_last_kernel(
    slot,
    half_ref,
    x_ref,
    w_ref,
    g_ref,
    before_ref,
    woo_ref,
    wom_ref,
    on_ref,
    q_ref,
    f_ref,
    v_ref,
    o_ref,
    x1_ref,
    h2_ref,
    h2t_ref,
    h1t_ref,
    h_s,
    on_s,
):
    step = pl.program_id(0)
    half = before_ref.shape[1]
    mixer_forward_kernel(
        slot, half_ref, x_ref, w_ref, g_ref, on_ref, q_ref, f_ref, v_ref, o_ref, h_s
    )
    on_s[:, lanes_of(half_ref[0] * pl.num_programs(0) + step, PAIR)] = on_ref[...]

    @pl.when(step == pl.num_programs(0) - 1)
    def _():
        here = lanes_of(half_ref[0], half)
        there = lanes_of(1 - half_ref[0], half)
        on_s[:, there] = before_ref[...]
        h1t_ref[...] = h_s[...].astype(wide).T.astype(low)
        x1_ref[:, here] = x_ref[:, here].astype(wide) + mm(on_s[...], woo_ref[...])
        x1_ref[:, there] = x_ref[:, there].astype(wide) + mm(on_s[...], wom_ref[...])
        x1 = x1_ref[...]
        scale = lax.rsqrt(jnp.mean(x1 * x1, axis=-1, keepdims=True) + 1e-06)
        normed = x1 * scale * g_ref[2:3, :]
        h2_ref[...] = normed.astype(low)
        h2t_ref[...] = normed.T.astype(low)


def mixer_forward(half, rows, weights, slot, gains=None, ending=None):
    count, width = rows.shape
    pairs = width // PAIR // 2
    by_pair = pl.BlockSpec((count, PAIR), lambda j, _: (0, j))
    struct = jax.ShapeDtypeStruct
    shape = lambda kind: struct((count, width // 2), kind)
    in_specs = [whole(rows.shape), pl.BlockSpec((width, 3 * PAIR), lambda j, _: (0, j))]
    operands = [half, rows, weights]
    out_specs = [by_pair] * 5
    out_shape = [shape(low), shape(wide), shape(wide), shape(low), shape(low)]
    scratch = [pltpu.VMEM((count, width), low)]
    if ending is None:
        kernel = mixer_forward_first_kernel
        in_specs += [whole(gains.shape)]
        operands += [gains]
        out_specs += [whole((8, width))]
        out_shape += [struct((8, width), wide)]
    if ending is not None:
        kernel = mixer_forward_last_kernel
        out_weights = pl.BlockSpec((width, width // 2), lambda j, _: (0, 3))
        in_specs += [whole(ending[0].shape), whole((count, width // 2)), out_weights, out_weights]
        operands += [ending[0], ending[1], weights, ending[2]]
        out_specs += [whole((count, width))] * 2 + [whole((width, count))] * 2
        out_shape += [
            struct((count, width), wide),
            struct((count, width), low),
            struct((width, count), low),
            struct((width, count), low),
        ]
        scratch += [pltpu.VMEM((count, width), low)]
    return pl.pallas_call(
        functools.partial(kernel, slot),
        grid_spec=pltpu.PrefetchScalarGridSpec(
            num_scalar_prefetch=1,
            grid=(pairs,),
            in_specs=in_specs,
            out_specs=out_specs,
            scratch_shapes=scratch,
        ),
        out_shape=out_shape,
        compiler_params=pltpu.CompilerParams(vmem_limit_bytes=VMEM_BYTES),
        cost_estimate=pl.CostEstimate(
            flops=count * width * 4 * width + 10 * count * slot * width,
            bytes_accessed=count * width * 12 + width * width * 4,
            transcendentals=count * width * 3,
        ),
        name="mixer_forward",
    )(*operands)


def store_down(out_ref, tile, owners):
    _, stride, down_rows = owners
    block = math.gcd(down_rows, tile.shape[0])
    first = pl.program_id(0) * (tile.shape[0] // block)
    for part in range(tile.shape[0] // block):
        owner = (first + part) // (down_rows // block)
        inside = (first + part) % (down_rows // block)
        start = pl.multiple_of(owner * stride + inside * block, block)
        out_ref[pl.ds(start, block), :] = tile[part * block : (part + 1) * block, :]


def ffn_kernel(
    owners,
    core_ref,
    h_ref,
    ht_ref,
    e_ref,
    wm_ref,
    wu_ref,
    wdm_ref,
    wdo_ref,
    x1_hbm,
    onm_hbm,
    ono_hbm,
    wom_hbm,
    woo_hbm,
    m_ref,
    g_ref,
    gm_ref,
    gu_ref,
    gdm_hbm,
    gdo_hbm,
    out_hbm,
    dx1_hbm,
    don_hbm,
    *scratch,
):
    gu_w, gu_g, down_g, down_w, mid_s, dh_s, on_s, x1_s, wo_s, out_s, gdm_s, gdo_s = scratch[:12]
    pre_s, in_semaphores, out_semaphores, down_semaphores = scratch[12:]
    step, last = pl.program_id(0), pl.num_programs(0) - 1
    half, tile = wdm_ref.shape[1], wm_ref.shape[1]
    mine, other = lanes_of(core_ref[0], half), lanes_of(1 - core_ref[0], half)
    kind, kind_other = lanes_of(core_ref[0], tile), lanes_of(1 - core_ref[0], tile)
    count, stride, down_rows = owners
    turn = lax.rem(step, 2)
    now = pl.ds(pl.multiple_of(turn * 2 * tile, 2 * tile), 2 * tile)
    now_mine = lanes_of(2 * turn + core_ref[0], tile)
    now_other = lanes_of(2 * turn + 1 - core_ref[0], tile)

    width = on_s.shape[1]
    sources = (
        (x1_hbm, x1_s),
        (onm_hbm, on_s.at[:, mine]),
        (ono_hbm, on_s.at[:, other]),
        (wom_hbm.at[:, pl.ds(3 * half, half)], wo_s.at[:, mine]),
        (woo_hbm.at[:, pl.ds(3 * half, half)], wo_s.at[:, other]),
    )
    fetches = [
        pltpu.make_async_copy(source, target, in_semaphores.at[number])
        for number, (source, target) in enumerate(sources)
    ]

    def down_copies(owner):
        rows = pl.ds(pl.multiple_of(owner * stride, math.gcd(stride, 32)), down_rows)
        return [
            pltpu.make_async_copy(held.at[rows, :], out.at[rows, :], down_semaphores.at[side, owner])
            for side, (held, out) in enumerate(((gdm_s, gdm_hbm), (gdo_s, gdo_hbm)))
        ]

    @pl.when(step == 0)
    def _():
        dh_s[...] = jnp.zeros_like(dh_s)
        for fetch in fetches:
            fetch.start()

    gu_w[:, now_mine] = wm_ref[...]
    gu_w[:, now_other] = wu_ref[...]
    hidden_rows = pl.ds(pl.multiple_of(step * tile, tile), tile)
    down_w[hidden_rows, mine] = wdm_ref[...]
    down_w[hidden_rows, other] = wdo_ref[...]
    pre = mm(h_ref[...], gu_w[:, now])
    a, b = pre[:, :tile], pre[:, tile:]
    share = sigmoid(a)
    swish = a * share
    mid = (swish * b).astype(low)
    mid_s[:, lanes_of(step, tile)] = mid
    d_mid = mm_nt(e_ref[...], down_w[hidden_rows, :])
    down_g[...] = mm_tn(mid, e_ref[...]).astype(low)
    d_a = (d_mid * b * (share + swish * (1.0 - share))).astype(low)
    d_b = (d_mid * swish).astype(low)
    d_pre = jnp.concatenate([d_a, d_b], axis=1)
    pre_s[:, now] = d_pre
    gu_g[...] = mm(ht_ref[...], d_pre).astype(low)
    blocks = tile // HEAD_DIM
    for side, block in enumerate((core_ref[1], 1 - core_ref[1])):
        gm_ref[side] = gu_g[:, lanes_of(core_ref[0] * blocks + block, HEAD_DIM)]
        gu_ref[side] = gu_g[:, lanes_of((1 - core_ref[0]) * blocks + block, HEAD_DIM)]
    store_down(gdm_s, down_g[:, mine], owners)
    store_down(gdo_s, down_g[:, other], owners)

    @pl.when(turn == 1)
    def _():
        dh_s[...] += mm_nt(pre_s[...], gu_w[...])

    done = (step + 1) * tile // down_rows

    @pl.when(done > step * tile // down_rows)
    def _():
        for copy in down_copies(done - 1):
            copy.start()

    @pl.when(step == last)
    def _():
        for fetch in fetches:
            fetch.wait()
        x1 = x1_s[...]
        x2 = x1 + mm(mid_s[...], down_w[...])
        positions = lax.broadcasted_iota(jnp.int32, (out_s.shape[0] // m_ref.shape[0], 1), 0)
        for sequence in range(m_ref.shape[0]):
            rows = slice(sequence * positions.shape[0], (sequence + 1) * positions.shape[0])
            valid = (positions < m_ref[sequence]).astype(wide)
            out_s[rows, :] = (x2[rows, :] * valid).astype(low)
        leaving = [pltpu.make_async_copy(out_s, out_hbm, out_semaphores.at[0])]
        leaving[-1].start()
        scale = lax.rsqrt(jnp.mean(x1 * x1, axis=-1, keepdims=True) + 1e-06)
        normed = x1 * scale
        d_h2 = dh_s[...]
        if (mid_s.shape[1] // tile) % 2:
            d_h2 = d_h2 + mm_nt(pre_s[:, : 2 * tile], gu_w[:, : 2 * tile])
        scaled = d_h2 * g_ref[2:3, :]
        d_x1 = e_ref[...].astype(wide) + scale * (
            scaled - normed * jnp.mean(scaled * normed, axis=-1, keepdims=True)
        )
        dh_s[...] = d_x1
        leaving.append(pltpu.make_async_copy(dh_s, dx1_hbm, out_semaphores.at[1]))
        leaving[-1].start()
        d_1 = mid_s.at[:, pl.ds(0, width)]
        d_1[...] = d_x1.astype(low)
        d_mixed = mid_s.at[:, pl.ds(width, width)]
        d_mixed[...] = mm_nt(d_1[...], wo_s[...]).astype(low)
        leaving.append(pltpu.make_async_copy(d_mixed, don_hbm, out_semaphores.at[2]))
        leaving[-1].start()
        rows = stride - down_rows
        grad_o = mm_tn(on_s[...], d_1[...]).astype(low)
        down_w[pl.ds(0, width), :] = grad_o
        for columns, held, out in ((mine, gdm_s, gdm_hbm), (other, gdo_s, gdo_hbm)):
            for owner in range(count):
                target = slice(owner * stride + down_rows, (owner + 1) * stride)
                held[target, :] = down_w[owner * rows : (owner + 1) * rows, columns]
                copy = pltpu.make_async_copy(
                    held.at[target, :], out.at[target, :], out_semaphores.at[len(leaving)]
                )
                copy.start()
                leaving.append(copy)
        for owner in range(count):
            leaving += down_copies(owner)
        for copy in leaving:
            copy.wait()


def ffn(core, h2, h2t, errors, w_gu, w_d, x1, mixed, w_a, lengths, gains8, owners):
    count, width = h2.shape
    half = width // 2
    hidden = w_gu[0].shape[1]
    full = whole((count, width))
    in_tile = pl.BlockSpec((width, TILE_F), lambda j, _: (0, j))
    out_tile = pl.BlockSpec((TILE_F, half), lambda j, _: (j, 0))
    grad_tile = pl.BlockSpec((2, width, HEAD_DIM), lambda j, _: (0, 0, j))
    anywhere = pl.BlockSpec(memory_space=pl.ANY)
    down_shape = (owners[0] * owners[1], half)
    struct = jax.ShapeDtypeStruct
    vmem = pltpu.VMEM
    return pl.pallas_call(
        functools.partial(ffn_kernel, owners),
        grid_spec=pltpu.PrefetchScalarGridSpec(
            num_scalar_prefetch=1,
            grid=(hidden // TILE_F,),
            in_specs=[full, whole(h2t.shape), full, in_tile, in_tile, out_tile, out_tile]
            + [anywhere] * 5
            + [pl.BlockSpec(memory_space=pltpu.SMEM), whole((8, width))],
            out_specs=[grad_tile, grad_tile] + [anywhere] * 5,
            scratch_shapes=[
                vmem((width, 4 * TILE_F), low),
                vmem((width, 2 * TILE_F), low),
                vmem((TILE_F, width), low),
                vmem((hidden, width), low),
                vmem((count, hidden), low),
                vmem((count, width), wide),
                vmem((count, width), low),
                vmem((count, width), wide),
                vmem((width, width), low),
                vmem((count, width), low),
                vmem(down_shape, low),
                vmem(down_shape, low),
                vmem((count, 4 * TILE_F), low),
                pltpu.SemaphoreType.DMA((5,)),
                pltpu.SemaphoreType.DMA((3 + 2 * owners[0],)),
                pltpu.SemaphoreType.DMA((2, owners[0])),
            ],
        ),
        out_shape=[struct((2, width, hidden // 2), low)] * 2
        + [struct(down_shape, low)] * 2
        + [
            struct((count, width), low),
            struct((count, width), wide),
            struct((count, width), low),
        ],
        compiler_params=pltpu.CompilerParams(vmem_limit_bytes=VMEM_BYTES),
        cost_estimate=pl.CostEstimate(
            flops=18 * count * width * hidden,
            bytes_accessed=count * width * 20 + width * hidden * 12,
            transcendentals=count * hidden,
        ),
        name="ffn",
    )(core, h2, h2t, errors, *w_gu, *w_d, x1, *mixed, *w_a, lengths, gains8)


def mixer_backward_kernel(
    slot,
    per_half,
    first,
    half_ref,
    ht_ref,
    g_ref,
    q_ref,
    f_ref,
    v_ref,
    o_ref,
    don_ref,
    *outs,
):
    grad_ref, dpre_ref = outs[-2:]
    gain_o = g_ref[1:2, lanes_of(half_ref[0] * per_half + first + pl.program_id(0), PAIR)]
    lower_ones = triangle(slot, True)
    upper_ones = triangle(slot, False)
    causal_t = causal_mask(slot, False)
    for sequence in range(q_ref.shape[0] // slot):
        rows = slice(sequence * slot, (sequence + 1) * slot)
        d_on = don_ref[rows, :].astype(wide)
        out = o_ref[rows, :].astype(wide)
        d_out_parts = []
        for head in range(2):
            lanes = slice(head * HEAD_DIM, (head + 1) * HEAD_DIM)
            out_h, d_on_h = out[:, lanes], d_on[:, lanes]
            scale = lax.rsqrt(jnp.mean(out_h * out_h, axis=-1, keepdims=True) + 1e-05)
            normed = out_h * scale
            scaled = d_on_h * gain_o[:, lanes]
            inner = jnp.mean(scaled * normed, axis=-1, keepdims=True)
            d_out_parts.append((scale * (scaled - normed * inner)).astype(low))

        q_pre = q_ref[rows, :]
        share, gate, keys_in, cumulative = decay_parts(f_ref[rows, :], lower_ones)
        grown = jnp.exp(-cumulative)
        shrunk = jnp.exp(cumulative)
        q_share = sigmoid(q_pre)
        decayed_q = (q_pre * q_share * shrunk).astype(low)
        grown_k = (keys_in * grown).astype(low)
        values = v_ref[rows, :]
        dq_parts, dk_parts, dv_parts = [], [], []
        for head in range(2):
            lanes = slice(head * HEAD_DIM, (head + 1) * HEAD_DIM)
            q_h, k_h, v_h = decayed_q[:, lanes], grown_k[:, lanes], values[:, lanes]
            d_out = d_out_parts[head]
            scores = jnp.where(causal_t, mm_nt(k_h, q_h), 0.0).astype(low)
            d_scores = jnp.where(causal_t, mm_nt(v_h, d_out), 0.0).astype(low)
            dv_parts.append(mm(scores, d_out))
            dk_parts.append(mm(d_scores, q_h))
            dq_parts.append(mm_tn(d_scores, k_h))
        d_decayed = jnp.concatenate(dq_parts, axis=1)
        d_grown = jnp.concatenate(dk_parts, axis=1)
        d_value = jnp.concatenate(dv_parts, axis=1)
        d_cumulative = decayed_q.astype(wide) * d_decayed - grown_k.astype(wide) * d_grown
        d_log = split_sum(upper_ones, d_cumulative)
        d_query = d_decayed * shrunk
        d_key = d_grown * grown
        d_q_pre = d_query * q_share * (1.0 + q_pre * (1.0 - q_share))
        d_f_pre = (1.0 - lower_bound) * (d_log / gate - d_key) * share * (1.0 - share)
        dpre_ref[rows, :PAIR] = d_q_pre.astype(low)
        dpre_ref[rows, PAIR : 2 * PAIR] = d_f_pre.astype(low)
        dpre_ref[rows, 2 * PAIR :] = d_value.astype(low)

    grad = mm(ht_ref[...], dpre_ref[...]).astype(low)
    grad_ref[...] = grad.reshape(grad_ref.shape)


def mixer_backward(half, h1t, gains8, kept, d_mixed, slot, shard, pairs=(0, 1), before=()):
    width, count = h1t.shape
    per_half = width // PAIR // 2
    first = pairs[0]
    by_pair = pl.BlockSpec((count, PAIR), lambda j, _: (0, first + j))
    from_whole = pl.BlockSpec((count, PAIR), lambda j, half: (0, half[0] * per_half + first + j))
    struct = jax.ShapeDtypeStruct
    return pl.pallas_call(
        functools.partial(mixer_backward_kernel, slot, per_half, first),
        grid_spec=pltpu.PrefetchScalarGridSpec(
            num_scalar_prefetch=1,
            grid=(len(pairs),),
            in_specs=[whole((width, count)), whole(gains8.shape)]
            + [by_pair] * 4
            + [from_whole]
            + [pl.BlockSpec(memory_space=pl.ANY)] * len(before),
            out_specs=[
                pl.BlockSpec(
                    (width // shard, 1, shard, 3 * PAIR), lambda j, _: (0, first + j, 0, 0)
                ),
                pl.BlockSpec((count, 3 * PAIR), lambda j, _: (0, first + j)),
            ],
        ),
        out_shape=[
            struct((width // shard, per_half, shard, 3 * PAIR), low),
            struct((count, per_half * 3 * PAIR), low),
        ],
        input_output_aliases={8 + k: k for k in range(len(before))},
        compiler_params=pltpu.CompilerParams(vmem_limit_bytes=VMEM_BYTES),
        cost_estimate=pl.CostEstimate(
            flops=len(pairs) * (count * width * 6 * PAIR + 20 * count * slot * PAIR),
            bytes_accessed=len(pairs) * (count * width * 5 + width * PAIR * 6),
            transcendentals=len(pairs) * count * PAIR * 6,
        ),
        name="mixer_backward",
    )(half, h1t, gains8, *kept, d_mixed, *before)


def input_gradient_rows_kernel(
    x_ref, g_ref, dm_ref, do_ref, wm_ref, wo_ref, dx1_ref, dx_ref
):
    d_h1 = mm_nt(dm_ref[...], wm_ref[...]) + mm_nt(do_ref[...], wo_ref[...])
    normed, scale = first_norm(x_ref, None)
    scaled = d_h1 * g_ref[0:1, :]
    dx_ref[...] = dx1_ref[...] + scale * (
        scaled - normed * jnp.mean(scaled * normed, axis=-1, keepdims=True)
    )


def input_gradient(rows, gains8, d_pre, weights, d_x1):
    count, width = rows.shape
    block = count // 2
    columns = d_pre[0].shape[1]
    by_rows = lambda columns: pl.BlockSpec((block, columns), lambda j: (j, 0))
    weight_spec = pl.BlockSpec((width, columns), lambda j: (0, 0), pipeline_mode=pl.Buffered(1))
    return pl.pallas_call(
        input_gradient_rows_kernel,
        grid=(count // block,),
        in_specs=[by_rows(width), whole(gains8.shape)]
        + [by_rows(columns)] * 2
        + [weight_spec] * 2
        + [by_rows(width)],
        out_specs=by_rows(width),
        out_shape=jax.ShapeDtypeStruct((count, width), wide),
        compiler_params=pltpu.CompilerParams(vmem_limit_bytes=VMEM_BYTES),
        cost_estimate=pl.CostEstimate(
            flops=6 * count * width * width,
            bytes_accessed=count * width * 16 + width * width * 6,
            transcendentals=0,
        ),
        name="input_gradient",
    )(rows, gains8, *d_pre, *weights, d_x1)


def update(weight, momentum, average, gradient, step_rate):
    new_momentum = momentum_decay * momentum + gradient
    direction = gradient + momentum_decay * new_momentum + weight_decay * weight
    new_weight = weight - step_rate * direction
    new_average = average_decay * average + (1.0 - average_decay) * new_weight
    return (new_momentum, new_average, new_weight)


def update_kernel(pick, step_rate, sum_count, core_ref, w_ref, m_ref, a_ref, *refs):
    sums, outs, dots_ref = refs[:sum_count], refs[-4:-1], refs[-1]
    weight = w_ref[...]
    gradient = pick(core_ref[0], *[s[...] for s in sums]).astype(wide).reshape(weight.shape)
    results = update(weight, m_ref[...], a_ref[...], gradient, step_rate)
    for out, result in zip(outs, results):
        out[...] = result
    product = weight.astype(low).astype(wide) * gradient
    total = product[..., :HEAD_DIM]
    for start in range(HEAD_DIM, product.shape[-1], HEAD_DIM):
        total = total + product[..., start : start + HEAD_DIM]
    dots_ref[...] = total.reshape(dots_ref.shape)


def update_call(
    core, state, sums, grid, state_spec, sum_specs, pick, step_rate, name, before=()
):
    struct = jax.ShapeDtypeStruct(state[0].shape, wide)
    size = math.prod(state[0].shape)
    rows = state_spec.block_shape[-2]
    steps = math.prod(grid)
    tail = grid[1:]

    def dots_index(*indices):
        place = indices[0]
        for length, index in zip(tail, indices[1:]):
            place = place * length + index
        return (place, 0, 0)

    return pl.pallas_call(
        functools.partial(update_kernel, pick, step_rate, len(sums)),
        grid_spec=pltpu.PrefetchScalarGridSpec(
            num_scalar_prefetch=1,
            grid=grid,
            in_specs=[state_spec] * 3
            + sum_specs
            + [pl.BlockSpec(memory_space=pl.ANY)] * len(before),
            out_specs=[state_spec] * 3 + [pl.BlockSpec((1, rows, HEAD_DIM), dots_index)],
        ),
        out_shape=[struct] * 3 + [jax.ShapeDtypeStruct((steps, rows, HEAD_DIM), wide)],
        input_output_aliases={4 + len(sums) + k: k for k in range(len(before))},
        compiler_params=pltpu.CompilerParams(vmem_limit_bytes=VMEM_BYTES),
        cost_estimate=pl.CostEstimate(flops=12 * size, bytes_accessed=26 * size, transcendentals=0),
        name=name,
    )(core, *state, *sums, *before)


def update_attention_kernel(
    pick, step_rate, gain_step, core_ref, w_ref, m_ref, a_ref, qfv_ref, out_ref, *refs
):
    if gain_step is None:
        update_kernel(pick, step_rate, 2, core_ref, w_ref, m_ref, a_ref, qfv_ref, out_ref, *refs)
        return
    *held, dots_s = refs
    own_dots, up_dots, gate_dots, g_ref, gm_ref, ga_ref = held[:6]
    outs, gain_outs = held[-6:-3], held[-3:]
    kind = pl.program_id(0)
    dots = dots_s.at[kind]
    update_kernel(
        pick, step_rate, 2, core_ref, w_ref, m_ref, a_ref, qfv_ref, out_ref, *outs, dots
    )

    @pl.when(kind == pl.num_programs(0) - 1)
    def _():
        shard = dots_s.shape[1]
        sums = [own_dots[k] + dots_s[k] for k in range(4)]
        two = (up_dots[...] + gate_dots[...]).reshape(shard, HEAD_DIM)
        columns = [
            jnp.sum(total, axis=1, keepdims=True) for total in (sums[0] + sums[1] + sums[2], sums[3], two)
        ]
        lanes = lax.broadcasted_iota(jnp.int32, (shard, HEAD_DIM), 1)
        table = jnp.where(lanes == 1, columns[1], columns[2])
        table = jnp.where(lanes == 0, columns[0], table)
        gain = g_ref[...]
        gradient = table.T[:3, :] / gain.astype(low).astype(wide)
        results = update(gain, gm_ref[...], ga_ref[...], gradient, gain_step)
        for out, result in zip(gain_outs, results):
            out[...] = result


def update_attention(half_ref, state, qfv, out, step_rate, gains=None):
    _, shard, width = state[0].shape
    down_rows = out.shape[0] - shard

    def pick(core_index, proj, last):
        gradient = last[down_rows:].astype(wide)
        for kind in range(3):
            parts = [proj[pair * shard :, kind * PAIR :][:shard, :PAIR] for pair in range(2)]
            chosen = jnp.concatenate(parts, axis=1).astype(wide)
            gradient = jnp.where(pl.program_id(0) == kind, chosen, gradient)
        return gradient

    struct = jax.ShapeDtypeStruct
    state_spec = pl.BlockSpec((1, shard, width // 2), lambda kind, half: (kind, 0, half[0]))
    in_specs = [state_spec] * 3 + [whole(qfv.shape), whole(out.shape)]
    out_specs = [state_spec] * 3
    out_shape = [struct(state[0].shape, wide)] * 3
    operands = [half_ref, *state, qfv, out]
    aliases, scratch, gain_step = {}, [], None
    if gains is None:
        out_specs += [pl.BlockSpec((1, shard, HEAD_DIM), lambda kind, half: (kind, 0, 0))]
        out_shape += [struct((4, shard, HEAD_DIM), wide)]
    else:
        before, dots, gain_state, gain_step = gains
        in_specs += [whole(part.shape) for part in (*dots, *gain_state)]
        operands += [*dots, *gain_state]
        aliases = {len(operands) + k: k for k in range(3)}
        in_specs += [pl.BlockSpec(memory_space=pl.ANY)] * 3
        operands += list(before)
        out_specs += [whole(gain_state[0].shape)] * 3
        out_shape += [struct(gain_state[0].shape, wide)] * 3
        scratch = [pltpu.VMEM((4, shard, HEAD_DIM), wide)]
    size = math.prod(state[0].shape) // 2
    return pl.pallas_call(
        functools.partial(update_attention_kernel, pick, step_rate, gain_step),
        grid_spec=pltpu.PrefetchScalarGridSpec(
            num_scalar_prefetch=1,
            grid=(4,),
            in_specs=in_specs,
            out_specs=out_specs,
            scratch_shapes=scratch,
        ),
        out_shape=out_shape,
        input_output_aliases=aliases,
        compiler_params=pltpu.CompilerParams(vmem_limit_bytes=VMEM_BYTES),
        cost_estimate=pl.CostEstimate(flops=12 * size, bytes_accessed=26 * size, transcendentals=0),
        name="update_attention",
    )(*operands)


def update_ffn_in(kind_ref, state, totals, step_rate, before):
    _, shard, hidden = state[0].shape
    block = shard // 2

    def pick(_, even, odd):
        blocks = []
        for start in range(0, hidden // 2, HEAD_DIM):
            blocks += [even[:, start : start + HEAD_DIM], odd[:, start : start + HEAD_DIM]]
        return jnp.concatenate(blocks, axis=1)

    return update_call(
        kind_ref,
        state,
        totals,
        (2,),
        pl.BlockSpec((1, block, hidden), lambda j, kind: (kind[0], j, 0)),
        [pl.BlockSpec((block, hidden // 2), lambda j, _: (j, 0))] * 2,
        pick,
        step_rate,
        "update_ffn_in",
        before,
    )


def update_ffn_out(core, state, sums, step_rate):
    shard, width = state[0].shape

    def pick(core_index, mine, other):
        own = pl.program_id(0) == core_index
        return jnp.where(own, mine[:shard].astype(wide), other[:shard].astype(wide))

    return update_call(
        core,
        state,
        sums,
        (2,),
        pl.BlockSpec((shard, width // 2), lambda j, _: (0, j)),
        [whole(total.shape) for total in sums],
        pick,
        step_rate,
        "update_ffn_out",
    )


def pack_kernel(core_ref, w_ref, out_ref):
    half = w_ref.shape[2]
    for pair in range(half // PAIR):
        for kind in range(3):
            start = (pair * 3 + kind) * PAIR
            piece = w_ref[kind, :, pair * PAIR : (pair + 1) * PAIR]
            out_ref[:, start : start + PAIR] = piece.astype(low)
    out_ref[:, 3 * half : 4 * half] = w_ref[3].astype(low)


def pack_attention(core, weights):
    _, shard, width = weights.shape
    half = width // 2
    return pl.pallas_call(
        pack_kernel,
        grid_spec=pltpu.PrefetchScalarGridSpec(
            num_scalar_prefetch=1,
            grid=(1,),
            in_specs=[pl.BlockSpec((4, shard, half), lambda j, core: (0, 0, core[0]))],
            out_specs=whole((shard, 4 * half)),
        ),
        out_shape=jax.ShapeDtypeStruct((shard, 4 * half), low),
        name="pack_attention",
    )(core, weights)


RING = 8


def ring_place(index):
    return jnp.where(index % 2 == 0, index // 2, RING - 1 - index // 2)


def ring_member(place):
    place = place % RING
    return jnp.where(place < RING // 2, 2 * place, 2 * RING - 1 - 2 * place)


CYCLE = (0, 2, 4, 6, 7, 5, 3, 1)


def ring_next(tensor):
    replicas = lax.axis_size("dp")
    pairs = []
    for place_of, member in enumerate(CYCLE):
        for replica in range(replicas):
            target = CYCLE[(place_of + (1 if replica % 2 == 0 else -1)) % RING]
            pairs.append((member * replicas + replica, target * replicas + replica))
    return lax.ppermute(tensor, ("fsdp", "dp"), pairs)


def ring_shift(tensor, way):
    pairs = [(member, CYCLE[(at + way) % RING]) for at, member in enumerate(CYCLE)]
    return lax.ppermute(tensor, "fsdp", pairs)


def core_swap(tensor):
    return lax.ppermute(tensor, "dp", [(d, d ^ 1) for d in range(lax.axis_size("dp"))])


def column_swap(tensor):
    return lax.ppermute(tensor, "dp", [(d, d ^ 2) for d in range(lax.axis_size("dp"))])


def pack_all_kernel(
    core_ref, column_ref, w_ref, up_ref, other_ref, down_ref, g_ref, out_ref, across_ref
):
    across_ref[...] = other_ref[0].astype(low)
    shard = w_ref.shape[1]
    half = w_ref.shape[2]
    for pair in range(half // PAIR):
        for kind in range(3):
            start = (pair * 3 + kind) * PAIR
            piece = w_ref[kind, :, pair * PAIR : (pair + 1) * PAIR]
            out_ref[:, start : start + PAIR] = piece.astype(low)
    out_ref[:, 3 * half : 4 * half] = w_ref[3].astype(low)
    start = 4 * half
    out_ref[:, start : start + up_ref.shape[2]] = up_ref[0].astype(low)
    start += up_ref.shape[2]
    for first, count in down_parts(down_ref.shape[0], shard):
        out_ref[:count, start : start + half] = down_ref[first : first + count, :].astype(low)
        if count < shard:
            out_ref[count:, start : start + half] = jnp.zeros((shard - count, half), low)
            rows = lax.broadcasted_iota(jnp.int32, (GAIN_ROWS, g_ref.shape[1]), 0)
            gains = jnp.where(rows == 1, g_ref[1:2, :], g_ref[2:3, :])
            gains = jnp.where(rows == 0, g_ref[0:1, :], gains)
            gains = jnp.where(rows < 3, gains, 0.0).astype(low)
            out_ref[count : count + GAIN_ROWS, start : start + g_ref.shape[1]] = gains
        start += half


def down_parts(down_rows, shard):
    return [(start, min(shard, down_rows - start)) for start in range(0, down_rows, shard)]


def pack_all(core, column, weights, up, down, gains):
    _, shard, width = weights.shape
    half = width // 2
    parts = len(down_parts(down.shape[0], shard))
    columns = 4 * half + up.shape[2] // 2 + parts * half
    return pl.pallas_call(
        pack_all_kernel,
        grid_spec=pltpu.PrefetchScalarGridSpec(
            num_scalar_prefetch=2,
            grid=(1,),
            in_specs=[
                pl.BlockSpec((4, shard, half), lambda j, core, column: (0, 0, core[0])),
                pl.BlockSpec(
                    (1, shard, up.shape[2] // 2), lambda j, core, column: (core[0], 0, column[0])
                ),
                pl.BlockSpec(
                    (1, shard, up.shape[2] // 2),
                    lambda j, core, column: (core[0], 0, 1 - column[0]),
                ),
                pl.BlockSpec((down.shape[0], half), lambda j, core, column: (0, core[0])),
                whole(gains.shape),
            ],
            out_specs=[whole((shard, columns)), whole((shard, up.shape[2] // 2))],
        ),
        out_shape=[
            jax.ShapeDtypeStruct((shard, columns), low),
            jax.ShapeDtypeStruct((shard, up.shape[2] // 2), low),
        ],
        compiler_params=pltpu.CompilerParams(vmem_limit_bytes=VMEM_BYTES),
        name="pack_all",
    )(core, column, weights, up, up, down, gains)


def place_kernel(which, kept, shapes, origin_ref, column_ref, *refs):
    pieces, outs, semaphores = refs[: len(which)], refs[-1 - len(kept) : -1], refs[-1]
    targets = dict(zip(kept, outs))
    shard, first, up_columns, down_rows, half = shapes
    copies = []

    def copy(source, target):
        copies.append(pltpu.make_async_copy(source, target, semaphores.at[len(copies)]))

    for piece, (origin, across) in zip(pieces, which):
        owner = origin_ref[origin]
        rows = pl.ds(pl.multiple_of(owner * shard, 16), shard)
        if across:
            copy(piece, targets[1].at[rows, lanes_of(1 - column_ref[0], up_columns)])
            continue
        copy(piece.at[:, pl.ds(0, first)], targets[0].at[rows, :])
        own = targets[1].at[rows, lanes_of(column_ref[0], up_columns)]
        copy(piece.at[:, pl.ds(first, up_columns)], own)
        lane = first + up_columns
        for start, count in down_parts(down_rows, shard):
            target = pl.ds(pl.multiple_of(owner * down_rows + start, 16), count)
            copy(piece.at[pl.ds(0, count), pl.ds(lane, half)], targets[2].at[target, :])
            if count < shard:
                source = piece.at[pl.ds(count, GAIN_ROWS), pl.ds(lane, shard)]
                copy(source, targets[3].at[:, lanes_of(owner, shard)])
            lane += half
    for one in copies:
        one.start()
    for one in copies:
        one.wait()


def place(origins, column, which, pieces, arrays, kept, shapes):
    anywhere = pl.BlockSpec(memory_space=pl.ANY)
    shard, first, up_columns, down_rows, half = shapes
    kinds = [(RING * shard, first), (RING * shard, 2 * up_columns), (RING * down_rows, half)]
    kinds.append((GAIN_ROWS, RING * shard))
    held = [] if arrays is None else list(arrays)
    size = sum(math.prod(piece.shape) for piece in pieces)
    before = 2 + len(pieces)
    return pl.pallas_call(
        functools.partial(place_kernel, which, kept, shapes),
        grid_spec=pltpu.PrefetchScalarGridSpec(
            num_scalar_prefetch=2,
            grid=(1,),
            in_specs=[whole(piece.shape) for piece in pieces] + [anywhere] * len(held),
            out_specs=[anywhere] * len(kept),
            scratch_shapes=[pltpu.SemaphoreType.DMA((8 * len(pieces),))],
        ),
        out_shape=[jax.ShapeDtypeStruct(kinds[k], pieces[0].dtype) for k in kept],
        input_output_aliases={before + k: k for k in range(len(held))},
        compiler_params=pltpu.CompilerParams(vmem_limit_bytes=VMEM_BYTES),
        cost_estimate=pl.CostEstimate(flops=0, bytes_accessed=8 * size, transcendentals=0),
        name="place",
    )(origins, column, *pieces, *held)


def after(tensor, *others):
    return lax.optimization_barrier((tensor, *others))[0]


def core_way():
    return 1 - 2 * (lax.axis_index("dp") % 2)


def ring_origins():
    steps = jnp.array((0, -1, -2, -3, -4, 1, 2, 3), jnp.int32)
    return ring_member(ring_place(lax.axis_index("fsdp")) + steps + RING).astype(jnp.int32)


class RingSumOverColumns:
    def __init__(self, mine, arrived):
        self.arrays = (mine, arrived)
        place = ring_place(lax.axis_index("fsdp"))
        self.rows = mine.shape[1] // RING
        self.starts = [
            ring_member(place - core_way() * (s + 1) + 2 * RING) * self.rows for s in range(RING)
        ]
        self.sent, self.came, self.totals = [], [], []

    def part(self, side, step):
        shape = (1, self.rows, self.arrays[0].shape[2])
        parts = [
            lax.dynamic_slice(array, (side, self.starts[step], 0), shape)[0]
            for array in self.arrays
        ]
        return parts[0].astype(wide) + parts[1].astype(wide)

    def cross(self):
        self.sent.append(self.part(1, len(self.sent)).astype(low))
        self.came.append(column_swap(self.sent[-1]))

    def term(self):
        step = len(self.totals)
        return self.part(0, step) + self.came[step].astype(wide)

    def begin(self, *others):
        self.came[0] = after(self.came[0], *others) if others else self.came[0]
        self.totals.append(self.term().astype(low))

    def step(self, arriving=()):
        total, ahead = self.totals[-1], self.came[len(self.totals)]
        moved = ring_next(after(total, ahead) if len(self.totals) > 1 else total)
        moved = after(moved, *arriving) if arriving else moved
        self.totals.append((moved.astype(wide) + self.term()).astype(low))

    def last(self):
        return self.totals[-1]


class RingSum:
    def __init__(self, mine, arrived):
        self.mine, self.arrived = mine, arrived
        place = ring_place(lax.axis_index("fsdp"))
        self.owners = [ring_member(place - core_way() * (s + 1) + 2 * RING) for s in range(RING)]
        self.totals = []

    def term(self):
        parts = []
        for own, arrived in zip(self.mine, self.arrived):
            rows = own.shape[0] // RING
            start = self.owners[len(self.totals)] * rows
            part = lax.dynamic_slice_in_dim(own, start, rows, 0).astype(wide)
            parts.append(part + lax.dynamic_slice_in_dim(arrived, start, rows, 0).astype(wide))
        return parts[0] if len(parts) == 1 else jnp.concatenate(parts, axis=0)

    def begin(self, *others):
        if others:
            self.mine = [after(self.mine[0], *others), *self.mine[1:]]
        self.totals.append(self.term().astype(low))

    def step(self, *before, arriving=()):
        total = self.totals[-1]
        moved = ring_next(after(total, *before) if before else total)
        moved = after(moved, *arriving) if arriving else moved
        self.totals.append((moved.astype(wide) + self.term().astype(wide)).astype(low))

    def last(self):
        return self.totals[-1]


def gather_rows(shard):
    mine = lax.all_gather(shard, "fsdp", axis=0, tiled=True)
    return mine, core_swap(mine)


def core_sum(mine, other):
    return (mine.astype(wide) + core_swap(other).astype(wide)).astype(low)


def scatter_rows(both):
    return lax.psum_scatter(both, "fsdp", scatter_dimension=0, tiled=True)


def over_columns(total):
    total = (total.astype(wide) + column_swap(total).astype(wide)).astype(low)
    return total, core_swap(total)


def on_device(
    inputs,
    cotangent,
    lengths,
    attention_weights,
    attention_momentum,
    attention_average,
    ffn_inputs,
    ffn_inputs_momentum,
    ffn_inputs_average,
    ffn_output,
    ffn_output_momentum,
    ffn_output_average,
    gains,
    gains_momentum,
    gains_average,
):
    micro_count, slot, width = inputs.shape
    hidden = ffn_inputs.shape[2]
    shard, down_rows = ffn_inputs.shape[1], ffn_output.shape[0]
    fsdp_size = lax.axis_size("fsdp")
    replicas = lax.axis_size("dp")
    ringed = fsdp_size == RING
    core = lax.axis_index("dp") % 2
    column = lax.axis_index("dp") // 2
    count = micro_count * slot
    half = width // 2
    core_ref = core.astype(jnp.int32).reshape(1)
    other_ref = 1 - core_ref
    column_ref = column.astype(jnp.int32).reshape(1)
    is_first = core == 0

    rows = inputs.reshape(count, width)
    positions = jnp.arange(slot, dtype=jnp.int32)
    valid = (positions[None, :] < lengths).astype(wide).reshape(count, 1)
    errors = (cotangent.reshape(count, width).astype(wide) * valid).astype(low)

    if ringed:
        origins = ring_origins()
        first = 4 * half
        shapes = (shard, first, hidden // 2, down_rows, half)
        packed, own_across = pack_all(
            core_ref, column_ref, attention_weights, ffn_inputs, ffn_output, gains
        )
        wholes, there, which_there = None, [own_across], [(0, True)]
        here, which = [packed], [(0, False)]
        for step in range(1, 6):
            if step <= 3:
                onward = [ring_shift(here[0], 1), ring_shift(here[-1], -1)]
            elif step == 4:
                onward = [ring_next(jnp.where(is_first, *here))]
            across = []
            if step > 1:
                across = [column_swap(piece[:, first : first + hidden // 2]) for piece in here]
            wholes = place(
                origins, column_ref, which + which_there, here + there, wholes, (0, 1, 2, 3), shapes
            )
            if step == 5:
                break
            extra = [errors] if step == 2 else []
            tied = list(lax.optimization_barrier((*onward, *across, *wholes, *extra)))
            here, rest = tied[: len(onward)], tied[len(onward) :]
            there, wholes = rest[: len(across)], rest[len(across) : len(across) + 4]
            which_there = [(origin, True) for origin, _ in which] if across else []
            which = [(origin, False) for origin in [step, step + 4][: len(onward)]]
        w_a, gain_rows = (wholes[0], core_swap(wholes[0])), wholes[3]
    else:
        w_a = gather_rows(pack_attention(core_ref, attention_weights))
        gain_rows = lax.all_gather(gains.astype(low), "fsdp", axis=1, tiled=True)
        gain_rows = jnp.pad(gain_rows, ((0, GAIN_ROWS - 3), (0, 0)))
        w_gu = gather_rows(
            lax.dynamic_index_in_dim(ffn_inputs, core, 0, keepdims=False).astype(low)
        )
        w_d = gather_rows(lax.dynamic_slice_in_dim(ffn_output, core * half, half, 1).astype(low))
    mixed_mine, *kept_mine, gains8 = mixer_forward(core_ref, rows, w_a[0], slot, gain_rows)
    if ringed:
        (across,) = lax.optimization_barrier((*across, mixed_mine, w_a[1]))[:1]
        (w_gu_mine,) = place(origins, column_ref, [(4, True)], [across], [wholes[1]], (1,), shapes)
        wholes = [wholes[0], w_gu_mine, wholes[2], wholes[3]]
        rows = after(rows, *wholes[1:3])
        w_gu, w_d = [(array, core_swap(array)) for array in wholes[1:3]]
    mixed_other, *rest = mixer_forward(
        other_ref, rows, w_a[1], slot, None, (gains8, mixed_mine, w_a[0])
    )
    kept_other, (x1, h2, h2t, h1t) = rest[:4], rest[4:]
    owners = (RING, down_rows + shard, down_rows)
    if not ringed:
        owners = (1, hidden + width, hidden)
    places = jnp.concatenate([core_ref, column_ref])
    *grad_gu, gd_mine, gd_other, output, d_x1, d_mixed = ffn(
        places, h2, h2t, errors, w_gu, w_d, x1, (mixed_mine, mixed_other), w_a, lengths[:, 0], gains8, owners
    )

    gm, gu = grad_gu
    arrived_gu = core_swap(gu)
    mine_do, arrived_do = [gd_mine], [core_swap(gd_other)]
    by_owner = (fsdp_size * 2 * shard, 3 * PAIR)
    d_pre = []
    for call in range(4):
        from_half, kept = (other_ref, kept_other) if call < 2 else (core_ref, kept_mine)
        if ringed and call == 1:
            sum_gu = RingSumOverColumns(after(gm, d_pre[0]), arrived_gu)
            sum_gu.cross()
            sum_gu.cross()
            h1t = after(h1t, *sum_gu.sent)
        elif ringed and call > 1:
            sum_gu.cross()
            ahead = [sum_gu.came[2]] if call == 3 else []
            h1t = after(h1t, sum_gu.last(), sum_do.last(), sum_gu.sent[-1], *ahead)
        grads = mixer_backward(
            from_half,
            h1t,
            gains8,
            kept,
            d_mixed,
            slot,
            shard,
            (call % 2,),
            grads if call % 2 else (),
        )
        d_pre.append(grads[1])
        if call == 1:
            grad_other = grads[0]
            if ringed:
                sum_do = RingSum(mine_do, arrived_do)
                sum_do.begin(d_pre[-1])
                sum_gu.begin(d_pre[-1])
                grad_other = after(grad_other, sum_gu.last(), sum_do.last())
            arrived_qfv = [core_swap(grad_other.reshape(by_owner))]
        elif ringed and call > 1:
            sum_do.step(arriving=(d_pre[-1],))
            sum_gu.step(arriving=(d_pre[-1],))
    mine_qfv = [grads[0].reshape(by_owner)]

    def finish_input(*others):
        late = after(d_pre[3], *others) if others else d_pre[3]
        return input_gradient(rows, gains8, (late, d_pre[1]), w_a, d_x1)

    if ringed:
        sum_qfv = RingSum(mine_qfv, arrived_qfv)
        sum_qfv.begin()
        input_grad = None
        for step in range(1, RING - 1):
            if len(sum_gu.came) < RING:
                sum_gu.cross()
            if len(sum_gu.totals) < RING:
                first = [sum_gu.last(), sum_qfv.last()]
                sum_do.step(*{1: first, 4: [input_grad]}.get(step, []))
                sum_gu.step()
            sum_qfv.step()
            if step == 2:
                input_grad = finish_input(sum_qfv.last())
        total_gu, total_do = sum_gu.last(), sum_do.last()
    else:
        both = (gm.astype(wide) + arrived_gu.astype(wide)).astype(low)
        here = (both[0].astype(wide) + column_swap(both[1]).astype(wide)).astype(low)
        total_gu = scatter_rows(here)
        both = (gd_mine.astype(wide) + arrived_do[0].astype(wide)).astype(low)
        total_do = jnp.concatenate(
            [scatter_rows(both[:hidden]), scatter_rows(both[hidden:])], axis=0
        )
        total_qfv = scatter_rows(
            (mine_qfv[0].astype(wide) + arrived_qfv[0].astype(wide)).astype(low)
        )
        input_grad = finish_input()
    scale_rows = 1.0 / math.sqrt(count * fsdp_size * replicas)
    matrix_step = matrix_rate * scale_rows
    attention_state = (attention_weights, attention_momentum, attention_average)
    ffn_in_state = (ffn_inputs, ffn_inputs_momentum, ffn_inputs_average)
    ffn_out_state = (ffn_output, ffn_output_momentum, ffn_output_average)
    sum_do = over_columns(total_do)
    there = column_swap(total_gu)
    even = jnp.where(column == 0, total_gu, there)
    odd = jnp.where(column == 0, there, total_gu)
    sum_gu = (even, odd), (core_swap(even), core_swap(odd))
    *new_out, _ = update_ffn_out(core_ref, ffn_out_state, sum_do, matrix_step)
    *new_in, dots_up = update_ffn_in(core_ref, ffn_in_state, sum_gu[0], matrix_step, ())
    *new_in, dots_gate = update_ffn_in(other_ref, ffn_in_state, sum_gu[1], matrix_step, new_in)
    if ringed:
        sum_qfv.step(arriving=(new_out[0],))
        total_qfv = sum_qfv.last()
    there = after(column_swap(total_qfv), new_in[0])
    sum_qfv = (total_qfv.astype(wide) + there.astype(wide)).astype(low)
    *own, dots_own = update_attention(
        core_ref, attention_state, sum_qfv, sum_do[0], matrix_step
    )
    theirs = after(core_swap(sum_qfv), own[0])
    gain_state = (gains, gains_momentum, gains_average)
    *new_attention, gains_m, gains_a, gains_w = update_attention(
        other_ref,
        attention_state,
        theirs,
        sum_do[1],
        matrix_step,
        (own, (dots_own, dots_up, dots_gate), gain_state, gain_rate * scale_rows),
    )
    return (
        output.reshape(micro_count, slot, width),
        input_grad.reshape(micro_count, slot, width),
        *new_attention,
        *new_in,
        *new_out,
        gains_m,
        gains_a,
        gains_w,
    )


def solution(mesh):
    rows_split = P(None, ("fsdp", "dp"), None)
    middle_split = P(None, "fsdp", None)
    first_split = P("fsdp", None)
    gains_split = P(None, "fsdp")
    in_specs = (
        (rows_split, rows_split, P(None, ("fsdp", "dp")))
        + (middle_split,) * 6
        + (first_split,) * 3
        + (gains_split,) * 3
    )
    out_specs = (
        (rows_split, rows_split)
        + (middle_split,) * 6
        + (first_split,) * 3
        + (gains_split,) * 3
    )
    return jax.shard_map(
        on_device, mesh=mesh, in_specs=in_specs, out_specs=out_specs, check_vma=False
    )
```

```python
import functools
import math

import jax
import jax.numpy as jnp
from jax import lax
from jax.experimental import pallas as pl
from jax.experimental.pallas import tpu as pltpu
from jax.sharding import PartitionSpec as P

HEAD_DIM = 128
PAIR = 2 * HEAD_DIM
GAIN_ROWS = 16

lower_bound = 0.9
momentum_decay = 0.9
average_decay = 0.7
weight_decay = 0.0005
matrix_rate = 0.03
gain_rate = 0.1
low = jnp.bfloat16
wide = jnp.float32
TILE_F = 256
VMEM_BYTES = 60 * 1024 * 1024


def mm(left, right):
    return jnp.dot(left, right, preferred_element_type=wide)


def mm_nt(left, right):
    return lax.dot_general(left, right, (((1,), (1,)), ((), ())), preferred_element_type=wide)


def mm_tn(left, right):
    return lax.dot_general(left, right, (((0,), (0,)), ((), ())), preferred_element_type=wide)


def sigmoid(u):
    return 0.5 * jnp.tanh(0.5 * u) + 0.5


def whole(shape):
    return pl.BlockSpec(shape, lambda *_: (0,) * len(shape), pipeline_mode=pl.Buffered(1))


def split_sum(ones_matrix, tensor):
    high = tensor.astype(low)
    rest = (tensor - high.astype(wide)).astype(low)
    return mm(ones_matrix, high) + mm(ones_matrix, rest)


def causal_mask(length, lower):
    rows = lax.broadcasted_iota(jnp.int32, (length, length), 0)
    columns = lax.broadcasted_iota(jnp.int32, (length, length), 1)
    return rows >= columns if lower else rows <= columns


def triangle(length, lower):
    return causal_mask(length, lower).astype(wide).astype(low)


def decay_parts(f_pre, lower_ones):
    share = sigmoid(f_pre)
    gate = lower_bound + (1.0 - lower_bound) * share
    keys_in = (1.0 - lower_bound) * (1.0 - share)
    cumulative = split_sum(lower_ones, jnp.log(gate))
    middle_row = cumulative.shape[0] // 2
    cumulative = cumulative - cumulative[middle_row : middle_row + 1, :]
    return share, gate, keys_in, cumulative


def first_norm(x_ref, gain_row):
    rows = x_ref[...].astype(wide)
    scale = lax.rsqrt(jnp.mean(rows * rows, axis=-1, keepdims=True) + 1e-06)
    return rows * scale, scale


def lanes_of(half, size):
    return pl.ds(pl.multiple_of(half * size, size), size)


def mixer_forward_first_kernel(
    slot, half_ref, x_ref, w_ref, gains_ref, on_ref, q_ref, f_ref, v_ref, o_ref, g_ref, h_s
):
    @pl.when(pl.program_id(0) == 0)
    def _():
        g_ref[...] = gains_ref[...].astype(wide)[: g_ref.shape[0], :]

    mixer_forward_kernel(
        slot, half_ref, x_ref, w_ref, g_ref, on_ref, q_ref, f_ref, v_ref, o_ref, h_s
    )


def mixer_forward_kernel(
    slot, half_ref, x_ref, w_ref, g_ref, on_ref, q_ref, f_ref, v_ref, o_ref, h_s
):
    @pl.when(pl.program_id(0) == 0)
    def _():
        normed, _ = first_norm(x_ref, None)
        h_s[...] = (normed * g_ref[0:1, :]).astype(low)

    gain_o = g_ref[1:2, lanes_of(half_ref[0] * pl.num_programs(0) + pl.program_id(0), PAIR)]
    pre = mm(h_s[...], w_ref[...])
    q_ref[...] = pre[:, :PAIR]
    f_ref[...] = pre[:, PAIR : 2 * PAIR]
    v_ref[...] = pre[:, 2 * PAIR :].astype(low)
    lower_ones = triangle(slot, True)
    causal = causal_mask(slot, True)
    for sequence in range(x_ref.shape[0] // slot):
        rows = slice(sequence * slot, (sequence + 1) * slot)
        q_pre = q_ref[rows, :]
        _, _, keys_in, cumulative = decay_parts(f_ref[rows, :], lower_ones)
        grown = jnp.exp(-cumulative)
        decayed_q = (q_pre * sigmoid(q_pre) * jnp.exp(cumulative)).astype(low)
        grown_k = (keys_in * grown).astype(low)
        values = v_ref[rows, :]
        for head in range(2):
            lanes = slice(head * HEAD_DIM, (head + 1) * HEAD_DIM)
            scores = mm_nt(decayed_q[:, lanes], grown_k[:, lanes])
            out = mm(jnp.where(causal, scores, 0.0).astype(low), values[:, lanes])
            scale = lax.rsqrt(jnp.mean(out * out, axis=-1, keepdims=True) + 1e-05)
            o_ref[rows, lanes] = out.astype(low)
            on_ref[rows, lanes] = (out * scale * gain_o[:, lanes]).astype(low)


def mixer_forward_last_kernel(
    slot,
    half_ref,
    x_ref,
    w_ref,
    g_ref,
    before_ref,
    woo_ref,
    wom_ref,
    on_ref,
    q_ref,
    f_ref,
    v_ref,
    o_ref,
    x1_ref,
    h2_ref,
    h2t_ref,
    h1t_ref,
    h_s,
    on_s,
):
    step = pl.program_id(0)
    half = before_ref.shape[1]
    mixer_forward_kernel(
        slot, half_ref, x_ref, w_ref, g_ref, on_ref, q_ref, f_ref, v_ref, o_ref, h_s
    )
    on_s[:, lanes_of(half_ref[0] * pl.num_programs(0) + step, PAIR)] = on_ref[...]

    @pl.when(step == pl.num_programs(0) - 1)
    def _():
        here = lanes_of(half_ref[0], half)
        there = lanes_of(1 - half_ref[0], half)
        on_s[:, there] = before_ref[...]
        h1t_ref[...] = h_s[...].T
        x1_ref[:, here] = x_ref[:, here].astype(wide) + mm(on_s[...], woo_ref[...])
        x1_ref[:, there] = x_ref[:, there].astype(wide) + mm(on_s[...], wom_ref[...])
        x1 = x1_ref[...]
        scale = lax.rsqrt(jnp.mean(x1 * x1, axis=-1, keepdims=True) + 1e-06)
        normed = x1 * scale * g_ref[2:3, :]
        h2_ref[...] = normed.astype(low)
        h2t_ref[...] = h2_ref[...].T


def mixer_forward(half, rows, weights, slot, gains=None, ending=None):
    count, width = rows.shape
    pairs = width // PAIR // 2
    by_pair = pl.BlockSpec((count, PAIR), lambda j, _: (0, j))
    struct = jax.ShapeDtypeStruct
    shape = lambda kind: struct((count, width // 2), kind)
    in_specs = [whole(rows.shape), pl.BlockSpec((width, 3 * PAIR), lambda j, _: (0, j))]
    operands = [half, rows, weights]
    out_specs = [by_pair] * 5
    out_shape = [shape(low), shape(wide), shape(wide), shape(low), shape(low)]
    scratch = [pltpu.VMEM((count, width), low)]
    if ending is None:
        kernel = mixer_forward_first_kernel
        in_specs += [whole(gains.shape)]
        operands += [gains]
        out_specs += [whole((8, width))]
        out_shape += [struct((8, width), wide)]
    if ending is not None:
        kernel = mixer_forward_last_kernel
        out_weights = pl.BlockSpec((width, width // 2), lambda j, _: (0, 3))
        in_specs += [whole(ending[0].shape), whole((count, width // 2)), out_weights, out_weights]
        operands += [ending[0], ending[1], weights, ending[2]]
        out_specs += [whole((count, width))] * 2 + [whole((width, count))] * 2
        out_shape += [
            struct((count, width), wide),
            struct((count, width), low),
            struct((width, count), low),
            struct((width, count), low),
        ]
        scratch += [pltpu.VMEM((count, width), low)]
    return pl.pallas_call(
        functools.partial(kernel, slot),
        grid_spec=pltpu.PrefetchScalarGridSpec(
            num_scalar_prefetch=1,
            grid=(pairs,),
            in_specs=in_specs,
            out_specs=out_specs,
            scratch_shapes=scratch,
        ),
        out_shape=out_shape,
        compiler_params=pltpu.CompilerParams(vmem_limit_bytes=VMEM_BYTES),
        cost_estimate=pl.CostEstimate(
            flops=count * width * 4 * width + 10 * count * slot * width,
            bytes_accessed=count * width * 12 + width * width * 4,
            transcendentals=count * width * 3,
        ),
        name="mixer_forward",
    )(*operands)


def store_down(out_ref, tile, owners):
    _, stride, down_rows = owners
    block = math.gcd(down_rows, tile.shape[0])
    first = pl.program_id(0) * (tile.shape[0] // block)
    for part in range(tile.shape[0] // block):
        owner = (first + part) // (down_rows // block)
        inside = (first + part) % (down_rows // block)
        start = pl.multiple_of(owner * stride + inside * block, block)
        out_ref[pl.ds(start, block), :] = tile[part * block : (part + 1) * block, :]


def ffn_kernel(
    owners,
    core_ref,
    h_ref,
    ht_ref,
    e_ref,
    wm_ref,
    wu_ref,
    wdm_ref,
    wdo_ref,
    x1_hbm,
    onm_hbm,
    ono_hbm,
    wom_hbm,
    woo_hbm,
    m_ref,
    g_ref,
    gm_ref,
    gu_ref,
    gdm_hbm,
    gdo_hbm,
    out_hbm,
    dx1_hbm,
    don_hbm,
    *scratch,
):
    gu_w, gu_g, down_g, down_w, mid_s, dh_s, on_s, x1_s, wo_s, out_s, gdm_s, gdo_s = scratch[:12]
    in_semaphores, out_semaphores, down_semaphores = scratch[12:]
    step, last = pl.program_id(0), pl.num_programs(0) - 1
    half, tile = wdm_ref.shape[1], wm_ref.shape[1]
    mine, other = lanes_of(core_ref[0], half), lanes_of(1 - core_ref[0], half)
    kind, kind_other = lanes_of(core_ref[0], tile), lanes_of(1 - core_ref[0], tile)
    count, stride, down_rows = owners

    width = on_s.shape[1]
    sources = (
        (x1_hbm, x1_s),
        (onm_hbm, on_s.at[:, mine]),
        (ono_hbm, on_s.at[:, other]),
        (wom_hbm.at[:, pl.ds(3 * half, half)], wo_s.at[:, mine]),
        (woo_hbm.at[:, pl.ds(3 * half, half)], wo_s.at[:, other]),
    )
    fetches = [
        pltpu.make_async_copy(source, target, in_semaphores.at[number])
        for number, (source, target) in enumerate(sources)
    ]

    def down_copies(owner):
        rows = pl.ds(pl.multiple_of(owner * stride, math.gcd(stride, 32)), down_rows)
        return [
            pltpu.make_async_copy(held.at[rows, :], out.at[rows, :], down_semaphores.at[side, owner])
            for side, (held, out) in enumerate(((gdm_s, gdm_hbm), (gdo_s, gdo_hbm)))
        ]

    @pl.when(step == 0)
    def _():
        dh_s[...] = jnp.zeros_like(dh_s)
        for fetch in fetches:
            fetch.start()

    gu_w[:, kind] = wm_ref[...]
    gu_w[:, kind_other] = wu_ref[...]
    hidden_rows = pl.ds(pl.multiple_of(step * tile, tile), tile)
    down_w[hidden_rows, mine] = wdm_ref[...]
    down_w[hidden_rows, other] = wdo_ref[...]
    pre = mm(h_ref[...], gu_w[...])
    a, b = pre[:, :tile], pre[:, tile:]
    share = sigmoid(a)
    swish = a * share
    mid = (swish * b).astype(low)
    mid_s[:, lanes_of(step, tile)] = mid
    d_mid = mm_nt(e_ref[...], down_w[hidden_rows, :])
    down_g[...] = mm_tn(mid, e_ref[...]).astype(low)
    d_a = (d_mid * b * (share + swish * (1.0 - share))).astype(low)
    d_b = (d_mid * swish).astype(low)
    d_pre = jnp.concatenate([d_a, d_b], axis=1)
    dh_s[...] += mm_nt(d_pre, gu_w[...])
    gu_g[...] = mm(ht_ref[...], d_pre).astype(low)
    blocks = tile // HEAD_DIM
    for side, block in enumerate((core_ref[1], 1 - core_ref[1])):
        gm_ref[side] = gu_g[:, lanes_of(core_ref[0] * blocks + block, HEAD_DIM)]
        gu_ref[side] = gu_g[:, lanes_of((1 - core_ref[0]) * blocks + block, HEAD_DIM)]
    store_down(gdm_s, down_g[:, mine], owners)
    store_down(gdo_s, down_g[:, other], owners)

    done = (step + 1) * tile // down_rows

    @pl.when(done > step * tile // down_rows)
    def _():
        for copy in down_copies(done - 1):
            copy.start()

    @pl.when(step == last)
    def _():
        for fetch in fetches:
            fetch.wait()
        x1 = x1_s[...]
        x2 = x1 + mm(mid_s[...], down_w[...])
        positions = lax.broadcasted_iota(jnp.int32, (out_s.shape[0] // m_ref.shape[0], 1), 0)
        for sequence in range(m_ref.shape[0]):
            rows = slice(sequence * positions.shape[0], (sequence + 1) * positions.shape[0])
            valid = (positions < m_ref[sequence]).astype(wide)
            out_s[rows, :] = (x2[rows, :] * valid).astype(low)
        leaving = [pltpu.make_async_copy(out_s, out_hbm, out_semaphores.at[0])]
        leaving[-1].start()
        scale = lax.rsqrt(jnp.mean(x1 * x1, axis=-1, keepdims=True) + 1e-06)
        normed = x1 * scale
        scaled = dh_s[...] * g_ref[2:3, :]
        d_x1 = e_ref[...].astype(wide) + scale * (
            scaled - normed * jnp.mean(scaled * normed, axis=-1, keepdims=True)
        )
        dh_s[...] = d_x1
        leaving.append(pltpu.make_async_copy(dh_s, dx1_hbm, out_semaphores.at[1]))
        leaving[-1].start()
        d_1 = mid_s.at[:, pl.ds(0, width)]
        d_1[...] = d_x1.astype(low)
        d_mixed = mid_s.at[:, pl.ds(width, width)]
        d_mixed[...] = mm_nt(d_1[...], wo_s[...]).astype(low)
        leaving.append(pltpu.make_async_copy(d_mixed, don_hbm, out_semaphores.at[2]))
        leaving[-1].start()
        rows = stride - down_rows
        grad_o = mm_tn(on_s[...], d_1[...]).astype(low)
        down_w[pl.ds(0, width), :] = grad_o
        for columns, held, out in ((mine, gdm_s, gdm_hbm), (other, gdo_s, gdo_hbm)):
            for owner in range(count):
                target = slice(owner * stride + down_rows, (owner + 1) * stride)
                held[target, :] = down_w[owner * rows : (owner + 1) * rows, columns]
                copy = pltpu.make_async_copy(
                    held.at[target, :], out.at[target, :], out_semaphores.at[len(leaving)]
                )
                copy.start()
                leaving.append(copy)
        for owner in range(count):
            leaving += down_copies(owner)
        for copy in leaving:
            copy.wait()


def ffn(core, h2, h2t, errors, w_gu, w_d, x1, mixed, w_a, lengths, gains8, owners):
    count, width = h2.shape
    half = width // 2
    hidden = w_gu[0].shape[1]
    full = whole((count, width))
    in_tile = pl.BlockSpec((width, TILE_F), lambda j, _: (0, j))
    out_tile = pl.BlockSpec((TILE_F, half), lambda j, _: (j, 0))
    grad_tile = pl.BlockSpec((2, width, HEAD_DIM), lambda j, _: (0, 0, j))
    anywhere = pl.BlockSpec(memory_space=pl.ANY)
    down_shape = (owners[0] * owners[1], half)
    struct = jax.ShapeDtypeStruct
    vmem = pltpu.VMEM
    return pl.pallas_call(
        functools.partial(ffn_kernel, owners),
        grid_spec=pltpu.PrefetchScalarGridSpec(
            num_scalar_prefetch=1,
            grid=(hidden // TILE_F,),
            in_specs=[full, whole(h2t.shape), full, in_tile, in_tile, out_tile, out_tile]
            + [anywhere] * 5
            + [pl.BlockSpec(memory_space=pltpu.SMEM), whole((8, width))],
            out_specs=[grad_tile, grad_tile] + [anywhere] * 5,
            scratch_shapes=[
                vmem((width, 2 * TILE_F), low),
                vmem((width, 2 * TILE_F), low),
                vmem((TILE_F, width), low),
                vmem((hidden, width), low),
                vmem((count, hidden), low),
                vmem((count, width), wide),
                vmem((count, width), low),
                vmem((count, width), wide),
                vmem((width, width), low),
                vmem((count, width), low),
                vmem(down_shape, low),
                vmem(down_shape, low),
                pltpu.SemaphoreType.DMA((5,)),
                pltpu.SemaphoreType.DMA((3 + 2 * owners[0],)),
                pltpu.SemaphoreType.DMA((2, owners[0])),
            ],
        ),
        out_shape=[struct((2, width, hidden // 2), low)] * 2
        + [struct(down_shape, low)] * 2
        + [
            struct((count, width), low),
            struct((count, width), wide),
            struct((count, width), low),
        ],
        compiler_params=pltpu.CompilerParams(vmem_limit_bytes=VMEM_BYTES),
        cost_estimate=pl.CostEstimate(
            flops=18 * count * width * hidden,
            bytes_accessed=count * width * 20 + width * hidden * 12,
            transcendentals=count * hidden,
        ),
        name="ffn",
    )(core, h2, h2t, errors, *w_gu, *w_d, x1, *mixed, *w_a, lengths, gains8)


def mixer_backward_kernel(
    slot,
    per_half,
    first,
    half_ref,
    ht_ref,
    g_ref,
    q_ref,
    f_ref,
    v_ref,
    o_ref,
    don_ref,
    *outs,
):
    grad_ref, dpre_ref = outs[-2:]
    gain_o = g_ref[1:2, lanes_of(half_ref[0] * per_half + first + pl.program_id(0), PAIR)]
    lower_ones = triangle(slot, True)
    upper_ones = triangle(slot, False)
    causal_t = causal_mask(slot, False)
    for sequence in range(q_ref.shape[0] // slot):
        rows = slice(sequence * slot, (sequence + 1) * slot)
        d_on = don_ref[rows, :].astype(wide)
        out = o_ref[rows, :].astype(wide)
        d_out_parts = []
        for head in range(2):
            lanes = slice(head * HEAD_DIM, (head + 1) * HEAD_DIM)
            out_h, d_on_h = out[:, lanes], d_on[:, lanes]
            scale = lax.rsqrt(jnp.mean(out_h * out_h, axis=-1, keepdims=True) + 1e-05)
            normed = out_h * scale
            scaled = d_on_h * gain_o[:, lanes]
            inner = jnp.mean(scaled * normed, axis=-1, keepdims=True)
            d_out_parts.append((scale * (scaled - normed * inner)).astype(low))

        q_pre = q_ref[rows, :]
        share, gate, keys_in, cumulative = decay_parts(f_ref[rows, :], lower_ones)
        grown = jnp.exp(-cumulative)
        shrunk = jnp.exp(cumulative)
        q_share = sigmoid(q_pre)
        decayed_q = (q_pre * q_share * shrunk).astype(low)
        grown_k = (keys_in * grown).astype(low)
        values = v_ref[rows, :]
        dq_parts, dk_parts, dv_parts = [], [], []
        for head in range(2):
            lanes = slice(head * HEAD_DIM, (head + 1) * HEAD_DIM)
            q_h, k_h, v_h = decayed_q[:, lanes], grown_k[:, lanes], values[:, lanes]
            d_out = d_out_parts[head]
            scores = jnp.where(causal_t, mm_nt(k_h, q_h), 0.0).astype(low)
            d_scores = jnp.where(causal_t, mm_nt(v_h, d_out), 0.0).astype(low)
            dv_parts.append(mm(scores, d_out))
            dk_parts.append(mm(d_scores, q_h))
            dq_parts.append(mm_tn(d_scores, k_h))
        d_decayed = jnp.concatenate(dq_parts, axis=1)
        d_grown = jnp.concatenate(dk_parts, axis=1)
        d_value = jnp.concatenate(dv_parts, axis=1)
        d_cumulative = decayed_q.astype(wide) * d_decayed - grown_k.astype(wide) * d_grown
        d_log = split_sum(upper_ones, d_cumulative)
        d_query = d_decayed * shrunk
        d_key = d_grown * grown
        d_q_pre = d_query * q_share * (1.0 + q_pre * (1.0 - q_share))
        d_f_pre = (1.0 - lower_bound) * (d_log / gate - d_key) * share * (1.0 - share)
        dpre_ref[rows, :PAIR] = d_q_pre.astype(low)
        dpre_ref[rows, PAIR : 2 * PAIR] = d_f_pre.astype(low)
        dpre_ref[rows, 2 * PAIR :] = d_value.astype(low)

    grad = mm(ht_ref[...], dpre_ref[...]).astype(low)
    grad_ref[...] = grad.reshape(grad_ref.shape)


def mixer_backward(half, h1t, gains8, kept, d_mixed, slot, shard, pairs=(0, 1), before=()):
    width, count = h1t.shape
    per_half = width // PAIR // 2
    first = pairs[0]
    by_pair = pl.BlockSpec((count, PAIR), lambda j, _: (0, first + j))
    from_whole = pl.BlockSpec((count, PAIR), lambda j, half: (0, half[0] * per_half + first + j))
    struct = jax.ShapeDtypeStruct
    return pl.pallas_call(
        functools.partial(mixer_backward_kernel, slot, per_half, first),
        grid_spec=pltpu.PrefetchScalarGridSpec(
            num_scalar_prefetch=1,
            grid=(len(pairs),),
            in_specs=[whole((width, count)), whole(gains8.shape)]
            + [by_pair] * 4
            + [from_whole]
            + [pl.BlockSpec(memory_space=pl.ANY)] * len(before),
            out_specs=[
                pl.BlockSpec(
                    (width // shard, 1, shard, 3 * PAIR), lambda j, _: (0, first + j, 0, 0)
                ),
                pl.BlockSpec((count, 3 * PAIR), lambda j, _: (0, first + j)),
            ],
        ),
        out_shape=[
            struct((width // shard, per_half, shard, 3 * PAIR), low),
            struct((count, per_half * 3 * PAIR), low),
        ],
        input_output_aliases={8 + k: k for k in range(len(before))},
        compiler_params=pltpu.CompilerParams(vmem_limit_bytes=VMEM_BYTES),
        cost_estimate=pl.CostEstimate(
            flops=len(pairs) * (count * width * 6 * PAIR + 20 * count * slot * PAIR),
            bytes_accessed=len(pairs) * (count * width * 5 + width * PAIR * 6),
            transcendentals=len(pairs) * count * PAIR * 6,
        ),
        name="mixer_backward",
    )(half, h1t, gains8, *kept, d_mixed, *before)


def input_gradient_rows_kernel(
    x_ref, g_ref, dm_ref, do_ref, wm_ref, wo_ref, dx1_ref, dx_ref
):
    d_h1 = mm_nt(dm_ref[...], wm_ref[...]) + mm_nt(do_ref[...], wo_ref[...])
    normed, scale = first_norm(x_ref, None)
    scaled = d_h1 * g_ref[0:1, :]
    dx_ref[...] = dx1_ref[...] + scale * (
        scaled - normed * jnp.mean(scaled * normed, axis=-1, keepdims=True)
    )


def input_gradient(rows, gains8, d_pre, weights, d_x1):
    count, width = rows.shape
    block = count // 2
    columns = d_pre[0].shape[1]
    by_rows = lambda columns: pl.BlockSpec((block, columns), lambda j: (j, 0))
    weight_spec = pl.BlockSpec((width, columns), lambda j: (0, 0), pipeline_mode=pl.Buffered(1))
    return pl.pallas_call(
        input_gradient_rows_kernel,
        grid=(count // block,),
        in_specs=[by_rows(width), whole(gains8.shape)]
        + [by_rows(columns)] * 2
        + [weight_spec] * 2
        + [by_rows(width)],
        out_specs=by_rows(width),
        out_shape=jax.ShapeDtypeStruct((count, width), wide),
        compiler_params=pltpu.CompilerParams(vmem_limit_bytes=VMEM_BYTES),
        cost_estimate=pl.CostEstimate(
            flops=6 * count * width * width,
            bytes_accessed=count * width * 16 + width * width * 6,
            transcendentals=0,
        ),
        name="input_gradient",
    )(rows, gains8, *d_pre, *weights, d_x1)


def update(weight, momentum, average, gradient, step_rate):
    new_momentum = momentum_decay * momentum + gradient
    direction = gradient + momentum_decay * new_momentum + weight_decay * weight
    new_weight = weight - step_rate * direction
    new_average = average_decay * average + (1.0 - average_decay) * new_weight
    return (new_momentum, new_average, new_weight)


def update_kernel(pick, step_rate, sum_count, core_ref, w_ref, m_ref, a_ref, *refs):
    sums, outs, dots_ref = refs[:sum_count], refs[-4:-1], refs[-1]
    weight = w_ref[...]
    gradient = pick(core_ref[0], *[s[...] for s in sums]).astype(wide).reshape(weight.shape)
    results = update(weight, m_ref[...], a_ref[...], gradient, step_rate)
    for out, result in zip(outs, results):
        out[...] = result
    product = weight.astype(low).astype(wide) * gradient
    total = product[..., :HEAD_DIM]
    for start in range(HEAD_DIM, product.shape[-1], HEAD_DIM):
        total = total + product[..., start : start + HEAD_DIM]
    dots_ref[...] = total.reshape(dots_ref.shape)


def update_call(
    core, state, sums, grid, state_spec, sum_specs, pick, step_rate, name, before=()
):
    struct = jax.ShapeDtypeStruct(state[0].shape, wide)
    size = math.prod(state[0].shape)
    rows = state_spec.block_shape[-2]
    steps = math.prod(grid)
    tail = grid[1:]

    def dots_index(*indices):
        place = indices[0]
        for length, index in zip(tail, indices[1:]):
            place = place * length + index
        return (place, 0, 0)

    return pl.pallas_call(
        functools.partial(update_kernel, pick, step_rate, len(sums)),
        grid_spec=pltpu.PrefetchScalarGridSpec(
            num_scalar_prefetch=1,
            grid=grid,
            in_specs=[state_spec] * 3
            + sum_specs
            + [pl.BlockSpec(memory_space=pl.ANY)] * len(before),
            out_specs=[state_spec] * 3 + [pl.BlockSpec((1, rows, HEAD_DIM), dots_index)],
        ),
        out_shape=[struct] * 3 + [jax.ShapeDtypeStruct((steps, rows, HEAD_DIM), wide)],
        input_output_aliases={4 + len(sums) + k: k for k in range(len(before))},
        compiler_params=pltpu.CompilerParams(vmem_limit_bytes=VMEM_BYTES),
        cost_estimate=pl.CostEstimate(flops=12 * size, bytes_accessed=26 * size, transcendentals=0),
        name=name,
    )(core, *state, *sums, *before)


def update_attention_kernel(
    pick, step_rate, gain_step, core_ref, w_ref, m_ref, a_ref, qfv_ref, out_ref, *refs
):
    if gain_step is None:
        update_kernel(pick, step_rate, 2, core_ref, w_ref, m_ref, a_ref, qfv_ref, out_ref, *refs)
        return
    *held, dots_s = refs
    own_dots, up_dots, gate_dots, g_ref, gm_ref, ga_ref = held[:6]
    outs, gain_outs = held[-6:-3], held[-3:]
    kind = pl.program_id(0)
    dots = dots_s.at[kind]
    update_kernel(
        pick, step_rate, 2, core_ref, w_ref, m_ref, a_ref, qfv_ref, out_ref, *outs, dots
    )

    @pl.when(kind == pl.num_programs(0) - 1)
    def _():
        shard = dots_s.shape[1]
        sums = [own_dots[k] + dots_s[k] for k in range(4)]
        two = (up_dots[...] + gate_dots[...]).reshape(shard, HEAD_DIM)
        columns = [
            jnp.sum(total, axis=1, keepdims=True) for total in (sums[0] + sums[1] + sums[2], sums[3], two)
        ]
        lanes = lax.broadcasted_iota(jnp.int32, (shard, HEAD_DIM), 1)
        table = jnp.where(lanes == 1, columns[1], columns[2])
        table = jnp.where(lanes == 0, columns[0], table)
        gain = g_ref[...]
        gradient = table.T[:3, :] / gain.astype(low).astype(wide)
        results = update(gain, gm_ref[...], ga_ref[...], gradient, gain_step)
        for out, result in zip(gain_outs, results):
            out[...] = result


def update_attention(half_ref, state, qfv, out, step_rate, gains=None):
    _, shard, width = state[0].shape
    down_rows = out.shape[0] - shard

    def pick(core_index, proj, last):
        gradient = last[down_rows:].astype(wide)
        for kind in range(3):
            parts = [proj[pair * shard :, kind * PAIR :][:shard, :PAIR] for pair in range(2)]
            chosen = jnp.concatenate(parts, axis=1).astype(wide)
            gradient = jnp.where(pl.program_id(0) == kind, chosen, gradient)
        return gradient

    struct = jax.ShapeDtypeStruct
    state_spec = pl.BlockSpec((1, shard, width // 2), lambda kind, half: (kind, 0, half[0]))
    in_specs = [state_spec] * 3 + [whole(qfv.shape), whole(out.shape)]
    out_specs = [state_spec] * 3
    out_shape = [struct(state[0].shape, wide)] * 3
    operands = [half_ref, *state, qfv, out]
    aliases, scratch, gain_step = {}, [], None
    if gains is None:
        out_specs += [pl.BlockSpec((1, shard, HEAD_DIM), lambda kind, half: (kind, 0, 0))]
        out_shape += [struct((4, shard, HEAD_DIM), wide)]
    else:
        before, dots, gain_state, gain_step = gains
        in_specs += [whole(part.shape) for part in (*dots, *gain_state)]
        operands += [*dots, *gain_state]
        aliases = {len(operands) + k: k for k in range(3)}
        in_specs += [pl.BlockSpec(memory_space=pl.ANY)] * 3
        operands += list(before)
        out_specs += [whole(gain_state[0].shape)] * 3
        out_shape += [struct(gain_state[0].shape, wide)] * 3
        scratch = [pltpu.VMEM((4, shard, HEAD_DIM), wide)]
    size = math.prod(state[0].shape) // 2
    return pl.pallas_call(
        functools.partial(update_attention_kernel, pick, step_rate, gain_step),
        grid_spec=pltpu.PrefetchScalarGridSpec(
            num_scalar_prefetch=1,
            grid=(4,),
            in_specs=in_specs,
            out_specs=out_specs,
            scratch_shapes=scratch,
        ),
        out_shape=out_shape,
        input_output_aliases=aliases,
        compiler_params=pltpu.CompilerParams(vmem_limit_bytes=VMEM_BYTES),
        cost_estimate=pl.CostEstimate(flops=12 * size, bytes_accessed=26 * size, transcendentals=0),
        name="update_attention",
    )(*operands)


def update_ffn_in(kind_ref, state, totals, step_rate, before):
    _, shard, hidden = state[0].shape
    block = shard // 2

    def pick(_, even, odd):
        blocks = []
        for start in range(0, hidden // 2, HEAD_DIM):
            blocks += [even[:, start : start + HEAD_DIM], odd[:, start : start + HEAD_DIM]]
        return jnp.concatenate(blocks, axis=1)

    return update_call(
        kind_ref,
        state,
        totals,
        (2,),
        pl.BlockSpec((1, block, hidden), lambda j, kind: (kind[0], j, 0)),
        [pl.BlockSpec((block, hidden // 2), lambda j, _: (j, 0))] * 2,
        pick,
        step_rate,
        "update_ffn_in",
        before,
    )


def update_ffn_out(core, state, sums, step_rate):
    shard, width = state[0].shape

    def pick(core_index, mine, other):
        own = pl.program_id(0) == core_index
        return jnp.where(own, mine[:shard].astype(wide), other[:shard].astype(wide))

    return update_call(
        core,
        state,
        sums,
        (2,),
        pl.BlockSpec((shard, width // 2), lambda j, _: (0, j)),
        [whole(total.shape) for total in sums],
        pick,
        step_rate,
        "update_ffn_out",
    )


def pack_kernel(core_ref, w_ref, out_ref):
    half = w_ref.shape[2]
    for pair in range(half // PAIR):
        for kind in range(3):
            start = (pair * 3 + kind) * PAIR
            piece = w_ref[kind, :, pair * PAIR : (pair + 1) * PAIR]
            out_ref[:, start : start + PAIR] = piece.astype(low)
    out_ref[:, 3 * half : 4 * half] = w_ref[3].astype(low)


def pack_attention(core, weights):
    _, shard, width = weights.shape
    half = width // 2
    return pl.pallas_call(
        pack_kernel,
        grid_spec=pltpu.PrefetchScalarGridSpec(
            num_scalar_prefetch=1,
            grid=(1,),
            in_specs=[pl.BlockSpec((4, shard, half), lambda j, core: (0, 0, core[0]))],
            out_specs=whole((shard, 4 * half)),
        ),
        out_shape=jax.ShapeDtypeStruct((shard, 4 * half), low),
        name="pack_attention",
    )(core, weights)


RING = 8


def ring_place(index):
    return jnp.where(index % 2 == 0, index // 2, RING - 1 - index // 2)


def ring_member(place):
    place = place % RING
    return jnp.where(place < RING // 2, 2 * place, 2 * RING - 1 - 2 * place)


CYCLE = (0, 2, 4, 6, 7, 5, 3, 1)


def ring_next(tensor):
    replicas = lax.axis_size("dp")
    pairs = []
    for place_of, member in enumerate(CYCLE):
        for replica in range(replicas):
            target = CYCLE[(place_of + (1 if replica % 2 == 0 else -1)) % RING]
            pairs.append((member * replicas + replica, target * replicas + replica))
    return lax.ppermute(tensor, ("fsdp", "dp"), pairs)


def ring_shift(tensor, way):
    pairs = [(member, CYCLE[(at + way) % RING]) for at, member in enumerate(CYCLE)]
    return lax.ppermute(tensor, "fsdp", pairs)


def core_swap(tensor):
    return lax.ppermute(tensor, "dp", [(d, d ^ 1) for d in range(lax.axis_size("dp"))])


def column_swap(tensor):
    return lax.ppermute(tensor, "dp", [(d, d ^ 2) for d in range(lax.axis_size("dp"))])


def pack_all_kernel(
    core_ref, column_ref, w_ref, up_ref, other_ref, down_ref, g_ref, out_ref, across_ref
):
    across_ref[...] = other_ref[0].astype(low)
    shard = w_ref.shape[1]
    half = w_ref.shape[2]
    for pair in range(half // PAIR):
        for kind in range(3):
            start = (pair * 3 + kind) * PAIR
            piece = w_ref[kind, :, pair * PAIR : (pair + 1) * PAIR]
            out_ref[:, start : start + PAIR] = piece.astype(low)
    out_ref[:, 3 * half : 4 * half] = w_ref[3].astype(low)
    start = 4 * half
    out_ref[:, start : start + up_ref.shape[2]] = up_ref[0].astype(low)
    start += up_ref.shape[2]
    for first, count in down_parts(down_ref.shape[0], shard):
        out_ref[:count, start : start + half] = down_ref[first : first + count, :].astype(low)
        if count < shard:
            out_ref[count:, start : start + half] = jnp.zeros((shard - count, half), low)
            rows = lax.broadcasted_iota(jnp.int32, (GAIN_ROWS, g_ref.shape[1]), 0)
            gains = jnp.where(rows == 1, g_ref[1:2, :], g_ref[2:3, :])
            gains = jnp.where(rows == 0, g_ref[0:1, :], gains)
            gains = jnp.where(rows < 3, gains, 0.0).astype(low)
            out_ref[count : count + GAIN_ROWS, start : start + g_ref.shape[1]] = gains
        start += half


def down_parts(down_rows, shard):
    return [(start, min(shard, down_rows - start)) for start in range(0, down_rows, shard)]


def pack_all(core, column, weights, up, down, gains):
    _, shard, width = weights.shape
    half = width // 2
    parts = len(down_parts(down.shape[0], shard))
    columns = 4 * half + up.shape[2] // 2 + parts * half
    return pl.pallas_call(
        pack_all_kernel,
        grid_spec=pltpu.PrefetchScalarGridSpec(
            num_scalar_prefetch=2,
            grid=(1,),
            in_specs=[
                pl.BlockSpec((4, shard, half), lambda j, core, column: (0, 0, core[0])),
                pl.BlockSpec(
                    (1, shard, up.shape[2] // 2), lambda j, core, column: (core[0], 0, column[0])
                ),
                pl.BlockSpec(
                    (1, shard, up.shape[2] // 2),
                    lambda j, core, column: (core[0], 0, 1 - column[0]),
                ),
                pl.BlockSpec((down.shape[0], half), lambda j, core, column: (0, core[0])),
                whole(gains.shape),
            ],
            out_specs=[whole((shard, columns)), whole((shard, up.shape[2] // 2))],
        ),
        out_shape=[
            jax.ShapeDtypeStruct((shard, columns), low),
            jax.ShapeDtypeStruct((shard, up.shape[2] // 2), low),
        ],
        compiler_params=pltpu.CompilerParams(vmem_limit_bytes=VMEM_BYTES),
        name="pack_all",
    )(core, column, weights, up, up, down, gains)


def place_kernel(which, kept, shapes, origin_ref, column_ref, *refs):
    pieces, outs, semaphores = refs[: len(which)], refs[-1 - len(kept) : -1], refs[-1]
    targets = dict(zip(kept, outs))
    shard, first, up_columns, down_rows, half = shapes
    copies = []

    def copy(source, target):
        copies.append(pltpu.make_async_copy(source, target, semaphores.at[len(copies)]))

    for piece, (origin, across) in zip(pieces, which):
        owner = origin_ref[origin]
        rows = pl.ds(pl.multiple_of(owner * shard, 16), shard)
        if across:
            copy(piece, targets[1].at[rows, lanes_of(1 - column_ref[0], up_columns)])
            continue
        copy(piece.at[:, pl.ds(0, first)], targets[0].at[rows, :])
        own = targets[1].at[rows, lanes_of(column_ref[0], up_columns)]
        copy(piece.at[:, pl.ds(first, up_columns)], own)
        lane = first + up_columns
        for start, count in down_parts(down_rows, shard):
            target = pl.ds(pl.multiple_of(owner * down_rows + start, 16), count)
            copy(piece.at[pl.ds(0, count), pl.ds(lane, half)], targets[2].at[target, :])
            if count < shard:
                source = piece.at[pl.ds(count, GAIN_ROWS), pl.ds(lane, shard)]
                copy(source, targets[3].at[:, lanes_of(owner, shard)])
            lane += half
    for one in copies:
        one.start()
    for one in copies:
        one.wait()


def place(origins, column, which, pieces, arrays, kept, shapes):
    anywhere = pl.BlockSpec(memory_space=pl.ANY)
    shard, first, up_columns, down_rows, half = shapes
    kinds = [(RING * shard, first), (RING * shard, 2 * up_columns), (RING * down_rows, half)]
    kinds.append((GAIN_ROWS, RING * shard))
    held = [] if arrays is None else list(arrays)
    size = sum(math.prod(piece.shape) for piece in pieces)
    before = 2 + len(pieces)
    return pl.pallas_call(
        functools.partial(place_kernel, which, kept, shapes),
        grid_spec=pltpu.PrefetchScalarGridSpec(
            num_scalar_prefetch=2,
            grid=(1,),
            in_specs=[whole(piece.shape) for piece in pieces] + [anywhere] * len(held),
            out_specs=[anywhere] * len(kept),
            scratch_shapes=[pltpu.SemaphoreType.DMA((8 * len(pieces),))],
        ),
        out_shape=[jax.ShapeDtypeStruct(kinds[k], pieces[0].dtype) for k in kept],
        input_output_aliases={before + k: k for k in range(len(held))},
        compiler_params=pltpu.CompilerParams(vmem_limit_bytes=VMEM_BYTES),
        cost_estimate=pl.CostEstimate(flops=0, bytes_accessed=8 * size, transcendentals=0),
        name="place",
    )(origins, column, *pieces, *held)


def after(tensor, *others):
    return lax.optimization_barrier((tensor, *others))[0]


def core_way():
    return 1 - 2 * (lax.axis_index("dp") % 2)


def ring_origins():
    steps = jnp.array((0, -1, -2, -3, -4, 1, 2, 3), jnp.int32)
    return ring_member(ring_place(lax.axis_index("fsdp")) + steps + RING).astype(jnp.int32)


class RingSumOverColumns:
    def __init__(self, mine, arrived):
        self.arrays = (mine, arrived)
        place = ring_place(lax.axis_index("fsdp"))
        self.rows = mine.shape[1] // RING
        self.starts = [
            ring_member(place - core_way() * (s + 1) + 2 * RING) * self.rows for s in range(RING)
        ]
        self.sent, self.came, self.totals = [], [], []

    def part(self, side, step, *others):
        shape = (1, self.rows, self.arrays[0].shape[2])
        first = after(self.arrays[0], *others) if others else self.arrays[0]
        parts = [
            lax.dynamic_slice(array, (side, self.starts[step], 0), shape)[0]
            for array in (first, self.arrays[1])
        ]
        return parts[0].astype(wide) + parts[1].astype(wide)

    def cross(self, *others):
        self.sent.append(self.part(1, len(self.sent), *others).astype(low))
        self.came.append(column_swap(self.sent[-1]))

    def term(self):
        step = len(self.totals)
        return self.part(0, step) + self.came[step].astype(wide)

    def begin(self, *others):
        self.came[0] = after(self.came[0], *others) if others else self.came[0]
        self.totals.append(self.term().astype(low))

    def step(self, *before, arriving=()):
        total, ahead = self.totals[-1], self.came[len(self.totals)]
        moved = ring_next(after(total, ahead, *before) if len(self.totals) > 1 else total)
        moved = after(moved, *arriving) if arriving else moved
        self.totals.append((moved.astype(wide) + self.term()).astype(low))

    def last(self):
        return self.totals[-1]


class RingSum:
    def __init__(self, mine, arrived):
        self.mine, self.arrived = mine, arrived
        place = ring_place(lax.axis_index("fsdp"))
        self.owners = [ring_member(place - core_way() * (s + 1) + 2 * RING) for s in range(RING)]
        self.totals = []

    def term(self):
        parts = []
        for own, arrived in zip(self.mine, self.arrived):
            rows = own.shape[0] // RING
            start = self.owners[len(self.totals)] * rows
            part = lax.dynamic_slice_in_dim(own, start, rows, 0).astype(wide)
            parts.append(part + lax.dynamic_slice_in_dim(arrived, start, rows, 0).astype(wide))
        return parts[0] if len(parts) == 1 else jnp.concatenate(parts, axis=0)

    def begin(self, *others):
        if others:
            self.mine = [after(self.mine[0], *others), *self.mine[1:]]
        self.totals.append(self.term().astype(low))

    def step(self, *before, arriving=()):
        total = self.totals[-1]
        moved = ring_next(after(total, *before) if before else total)
        moved = after(moved, *arriving) if arriving else moved
        self.totals.append((moved.astype(wide) + self.term().astype(wide)).astype(low))

    def last(self):
        return self.totals[-1]


def gather_rows(shard):
    mine = lax.all_gather(shard, "fsdp", axis=0, tiled=True)
    return mine, core_swap(mine)


def core_sum(mine, other):
    return (mine.astype(wide) + core_swap(other).astype(wide)).astype(low)


def scatter_rows(both):
    return lax.psum_scatter(both, "fsdp", scatter_dimension=0, tiled=True)


def over_columns(total):
    total = (total.astype(wide) + column_swap(total).astype(wide)).astype(low)
    return total, core_swap(total)


def on_device(
    inputs,
    cotangent,
    lengths,
    attention_weights,
    attention_momentum,
    attention_average,
    ffn_inputs,
    ffn_inputs_momentum,
    ffn_inputs_average,
    ffn_output,
    ffn_output_momentum,
    ffn_output_average,
    gains,
    gains_momentum,
    gains_average,
):
    micro_count, slot, width = inputs.shape
    hidden = ffn_inputs.shape[2]
    shard, down_rows = ffn_inputs.shape[1], ffn_output.shape[0]
    fsdp_size = lax.axis_size("fsdp")
    replicas = lax.axis_size("dp")
    ringed = fsdp_size == RING
    core = lax.axis_index("dp") % 2
    column = lax.axis_index("dp") // 2
    count = micro_count * slot
    half = width // 2
    core_ref = core.astype(jnp.int32).reshape(1)
    other_ref = 1 - core_ref
    column_ref = column.astype(jnp.int32).reshape(1)
    is_first = core == 0

    rows = inputs.reshape(count, width)
    positions = jnp.arange(slot, dtype=jnp.int32)
    valid = (positions[None, :] < lengths).astype(wide).reshape(count, 1)
    errors = (cotangent.reshape(count, width).astype(wide) * valid).astype(low)

    if ringed:
        origins = ring_origins()
        first = 4 * half
        shapes = (shard, first, hidden // 2, down_rows, half)
        packed, own_across = pack_all(
            core_ref, column_ref, attention_weights, ffn_inputs, ffn_output, gains
        )
        wholes, there, which_there = None, [own_across], [(0, True)]
        here, which = [packed], [(0, False)]
        for step in range(1, 6):
            if step <= 3:
                onward = [ring_shift(here[0], 1), ring_shift(here[-1], -1)]
            elif step == 4:
                onward = [ring_next(jnp.where(is_first, *here))]
            across = []
            if step > 1:
                across = [column_swap(piece[:, first : first + hidden // 2]) for piece in here]
            wholes = place(
                origins, column_ref, which + which_there, here + there, wholes, (0, 1, 2, 3), shapes
            )
            if step == 5:
                break
            extra = [errors] if step == 2 else []
            tied = list(lax.optimization_barrier((*onward, *across, *wholes, *extra)))
            here, rest = tied[: len(onward)], tied[len(onward) :]
            there, wholes = rest[: len(across)], rest[len(across) : len(across) + 4]
            which_there = [(origin, True) for origin, _ in which] if across else []
            which = [(origin, False) for origin in [step, step + 4][: len(onward)]]
        w_a, gain_rows = (wholes[0], core_swap(wholes[0])), wholes[3]
    else:
        w_a = gather_rows(pack_attention(core_ref, attention_weights))
        gain_rows = lax.all_gather(gains.astype(low), "fsdp", axis=1, tiled=True)
        gain_rows = jnp.pad(gain_rows, ((0, GAIN_ROWS - 3), (0, 0)))
        w_gu = gather_rows(
            lax.dynamic_index_in_dim(ffn_inputs, core, 0, keepdims=False).astype(low)
        )
        w_d = gather_rows(lax.dynamic_slice_in_dim(ffn_output, core * half, half, 1).astype(low))
    mixed_mine, *kept_mine, gains8 = mixer_forward(core_ref, rows, w_a[0], slot, gain_rows)
    if ringed:
        (across,) = lax.optimization_barrier((*across, mixed_mine, w_a[1]))[:1]
        (w_gu_mine,) = place(origins, column_ref, [(4, True)], [across], [wholes[1]], (1,), shapes)
        wholes = [wholes[0], w_gu_mine, wholes[2], wholes[3]]
        rows = after(rows, *wholes[1:3])
        w_gu, w_d = [(array, core_swap(array)) for array in wholes[1:3]]
    mixed_other, *rest = mixer_forward(
        other_ref, rows, w_a[1], slot, None, (gains8, mixed_mine, w_a[0])
    )
    kept_other, (x1, h2, h2t, h1t) = rest[:4], rest[4:]
    owners = (RING, down_rows + shard, down_rows)
    if not ringed:
        owners = (1, hidden + width, hidden)
    places = jnp.concatenate([core_ref, column_ref])
    *grad_gu, gd_mine, gd_other, output, d_x1, d_mixed = ffn(
        places, h2, h2t, errors, w_gu, w_d, x1, (mixed_mine, mixed_other), w_a, lengths[:, 0], gains8, owners
    )

    gm, gu = grad_gu
    arrived_gu = core_swap(gu)
    mine_do, arrived_do = [gd_mine], [core_swap(gd_other)]
    by_owner = (fsdp_size * 2 * shard, 3 * PAIR)
    d_pre = []
    for call in range(4):
        from_half, kept = (other_ref, kept_other) if call < 2 else (core_ref, kept_mine)
        if ringed and call == 1:
            sum_gu = RingSumOverColumns(after(gm, d_pre[0]), arrived_gu)
            sum_gu.cross()
            sum_gu.cross()
            h1t = after(h1t, *sum_gu.sent)
        elif ringed and call > 1:
            sum_gu.cross(d_pre[-1])
            ahead = [sum_gu.came[2]] if call == 3 else []
            h1t = after(h1t, sum_gu.last(), sum_do.last(), sum_gu.sent[-1], *ahead)
        grads = mixer_backward(
            from_half,
            h1t,
            gains8,
            kept,
            d_mixed,
            slot,
            shard,
            (call % 2,),
            grads if call % 2 else (),
        )
        d_pre.append(grads[1])
        if call == 1:
            grad_other = grads[0]
            if ringed:
                sum_do = RingSum(mine_do, arrived_do)
                sum_do.begin(d_pre[-1])
                sum_gu.begin(d_pre[-1])
                grad_other = after(grad_other, sum_gu.last(), sum_do.last())
            arrived_qfv = [core_swap(grad_other.reshape(by_owner))]
        elif ringed and call > 1:
            sum_do.step(arriving=(d_pre[-1],))
            sum_gu.step(arriving=(d_pre[-1],))
    mine_qfv = [grads[0].reshape(by_owner)]

    def finish_input(*others):
        late = after(d_pre[3], *others) if others else d_pre[3]
        return input_gradient(rows, gains8, (late, d_pre[1]), w_a, d_x1)

    if ringed:
        sum_qfv = RingSum(mine_qfv, arrived_qfv)
        sum_qfv.begin()
        input_grad = None
        for step in range(1, RING - 1):
            if len(sum_gu.came) < RING:
                sum_gu.cross(sum_gu.last())
            if len(sum_gu.totals) < RING:
                first = [sum_gu.last(), sum_qfv.last()]
                done = [sum_qfv.last(), *([sum_do.last()] if step == 1 else [])]
                sum_do.step(*{1: first, 4: [input_grad]}.get(step, []))
                sum_gu.step(*done)
            sum_qfv.step()
            if step == 2:
                input_grad = finish_input(sum_qfv.last())
        total_gu, total_do = sum_gu.last(), sum_do.last()
    else:
        both = (gm.astype(wide) + arrived_gu.astype(wide)).astype(low)
        here = (both[0].astype(wide) + column_swap(both[1]).astype(wide)).astype(low)
        total_gu = scatter_rows(here)
        both = (gd_mine.astype(wide) + arrived_do[0].astype(wide)).astype(low)
        total_do = jnp.concatenate(
            [scatter_rows(both[:hidden]), scatter_rows(both[hidden:])], axis=0
        )
        total_qfv = scatter_rows(
            (mine_qfv[0].astype(wide) + arrived_qfv[0].astype(wide)).astype(low)
        )
        input_grad = finish_input()
    scale_rows = 1.0 / math.sqrt(count * fsdp_size * replicas)
    matrix_step = matrix_rate * scale_rows
    attention_state = (attention_weights, attention_momentum, attention_average)
    ffn_in_state = (ffn_inputs, ffn_inputs_momentum, ffn_inputs_average)
    ffn_out_state = (ffn_output, ffn_output_momentum, ffn_output_average)
    sum_do = over_columns(total_do)
    there = column_swap(total_gu)
    even = jnp.where(column == 0, total_gu, there)
    odd = jnp.where(column == 0, there, total_gu)
    sum_gu = (even, odd), (core_swap(even), core_swap(odd))
    *new_out, _ = update_ffn_out(core_ref, ffn_out_state, sum_do, matrix_step)
    *new_in, dots_up = update_ffn_in(core_ref, ffn_in_state, sum_gu[0], matrix_step, ())
    *new_in, dots_gate = update_ffn_in(other_ref, ffn_in_state, sum_gu[1], matrix_step, new_in)
    if ringed:
        sum_qfv.step(arriving=(new_out[0],))
        total_qfv = sum_qfv.last()
    there = after(column_swap(total_qfv), new_in[0])
    sum_qfv = (total_qfv.astype(wide) + there.astype(wide)).astype(low)
    *own, dots_own = update_attention(
        core_ref, attention_state, sum_qfv, sum_do[0], matrix_step
    )
    theirs = after(core_swap(sum_qfv), own[0])
    gain_state = (gains, gains_momentum, gains_average)
    *new_attention, gains_m, gains_a, gains_w = update_attention(
        other_ref,
        attention_state,
        theirs,
        sum_do[1],
        matrix_step,
        (own, (dots_own, dots_up, dots_gate), gain_state, gain_rate * scale_rows),
    )
    return (
        output.reshape(micro_count, slot, width),
        input_grad.reshape(micro_count, slot, width),
        *new_attention,
        *new_in,
        *new_out,
        gains_m,
        gains_a,
        gains_w,
    )


def solution(mesh):
    rows_split = P(None, ("fsdp", "dp"), None)
    middle_split = P(None, "fsdp", None)
    first_split = P("fsdp", None)
    gains_split = P(None, "fsdp")
    in_specs = (
        (rows_split, rows_split, P(None, ("fsdp", "dp")))
        + (middle_split,) * 6
        + (first_split,) * 3
        + (gains_split,) * 3
    )
    out_specs = (
        (rows_split, rows_split)
        + (middle_split,) * 6
        + (first_split,) * 3
        + (gains_split,) * 3
    )
    return jax.shard_map(
        on_device, mesh=mesh, in_specs=in_specs, out_specs=out_specs, check_vma=False
    )
```

```python
import functools
import math

import jax
import jax.numpy as jnp
from jax import lax
from jax.experimental import pallas as pl
from jax.experimental.pallas import tpu as pltpu
from jax.sharding import PartitionSpec as P

HEAD_DIM = 128
PAIR = 2 * HEAD_DIM
GAIN_ROWS = 16

lower_bound = 0.9
momentum_decay = 0.9
average_decay = 0.7
weight_decay = 0.0005
matrix_rate = 0.03
gain_rate = 0.1
low = jnp.bfloat16
wide = jnp.float32
TILE_F = 256
VMEM_BYTES = 60 * 1024 * 1024


def mm(left, right):
    return jnp.dot(left, right, preferred_element_type=wide)


def mm_nt(left, right):
    return lax.dot_general(left, right, (((1,), (1,)), ((), ())), preferred_element_type=wide)


def mm_tn(left, right):
    return lax.dot_general(left, right, (((0,), (0,)), ((), ())), preferred_element_type=wide)


def sigmoid(u):
    return 0.5 * jnp.tanh(0.5 * u) + 0.5


def whole(shape):
    return pl.BlockSpec(shape, lambda *_: (0,) * len(shape), pipeline_mode=pl.Buffered(1))


def split_sum(ones_matrix, tensor):
    high = tensor.astype(low)
    rest = (tensor - high.astype(wide)).astype(low)
    return mm(ones_matrix, high) + mm(ones_matrix, rest)


def causal_mask(length, lower):
    rows = lax.broadcasted_iota(jnp.int32, (length, length), 0)
    columns = lax.broadcasted_iota(jnp.int32, (length, length), 1)
    return rows >= columns if lower else rows <= columns


def triangle(length, lower):
    return causal_mask(length, lower).astype(wide).astype(low)


def decay_parts(f_pre, lower_ones):
    share = sigmoid(f_pre)
    gate = lower_bound + (1.0 - lower_bound) * share
    keys_in = (1.0 - lower_bound) * (1.0 - share)
    cumulative = split_sum(lower_ones, jnp.log(gate))
    middle_row = cumulative.shape[0] // 2
    cumulative = cumulative - cumulative[middle_row : middle_row + 1, :]
    return share, gate, keys_in, cumulative


def first_norm(x_ref, gain_row):
    rows = x_ref[...].astype(wide)
    scale = lax.rsqrt(jnp.mean(rows * rows, axis=-1, keepdims=True) + 1e-06)
    return rows * scale, scale


def lanes_of(half, size):
    return pl.ds(pl.multiple_of(half * size, size), size)


def mixer_forward_first_kernel(
    slot, half_ref, x_ref, w_ref, gains_ref, on_ref, q_ref, f_ref, v_ref, o_ref, g_ref, h_s
):
    @pl.when(pl.program_id(0) == 0)
    def _():
        g_ref[...] = gains_ref[...].astype(wide)[: g_ref.shape[0], :]

    mixer_forward_kernel(
        slot, half_ref, x_ref, w_ref, g_ref, on_ref, q_ref, f_ref, v_ref, o_ref, h_s
    )


def mixer_forward_kernel(
    slot, half_ref, x_ref, w_ref, g_ref, on_ref, q_ref, f_ref, v_ref, o_ref, h_s
):
    @pl.when(pl.program_id(0) == 0)
    def _():
        normed, _ = first_norm(x_ref, None)
        h_s[...] = (normed * g_ref[0:1, :]).astype(low)

    gain_o = g_ref[1:2, lanes_of(half_ref[0] * pl.num_programs(0) + pl.program_id(0), PAIR)]
    pre = mm(h_s[...], w_ref[...])
    q_ref[...] = pre[:, :PAIR]
    f_ref[...] = pre[:, PAIR : 2 * PAIR]
    v_ref[...] = pre[:, 2 * PAIR :].astype(low)
    lower_ones = triangle(slot, True)
    causal = causal_mask(slot, True)
    for sequence in range(x_ref.shape[0] // slot):
        rows = slice(sequence * slot, (sequence + 1) * slot)
        q_pre = q_ref[rows, :]
        _, _, keys_in, cumulative = decay_parts(f_ref[rows, :], lower_ones)
        grown = jnp.exp(-cumulative)
        decayed_q = (q_pre * sigmoid(q_pre) * jnp.exp(cumulative)).astype(low)
        grown_k = (keys_in * grown).astype(low)
        values = v_ref[rows, :]
        for head in range(2):
            lanes = slice(head * HEAD_DIM, (head + 1) * HEAD_DIM)
            scores = mm_nt(decayed_q[:, lanes], grown_k[:, lanes])
            out = mm(jnp.where(causal, scores, 0.0).astype(low), values[:, lanes])
            scale = lax.rsqrt(jnp.mean(out * out, axis=-1, keepdims=True) + 1e-05)
            o_ref[rows, lanes] = out.astype(low)
            on_ref[rows, lanes] = (out * scale * gain_o[:, lanes]).astype(low)


def mixer_forward_last_kernel(
    slot,
    half_ref,
    x_ref,
    w_ref,
    g_ref,
    before_ref,
    woo_ref,
    wom_ref,
    on_ref,
    q_ref,
    f_ref,
    v_ref,
    o_ref,
    x1_ref,
    h2_ref,
    h2t_ref,
    h1t_ref,
    h_s,
    on_s,
):
    step = pl.program_id(0)
    half = before_ref.shape[1]
    mixer_forward_kernel(
        slot, half_ref, x_ref, w_ref, g_ref, on_ref, q_ref, f_ref, v_ref, o_ref, h_s
    )
    on_s[:, lanes_of(half_ref[0] * pl.num_programs(0) + step, PAIR)] = on_ref[...]

    @pl.when(step == pl.num_programs(0) - 1)
    def _():
        here = lanes_of(half_ref[0], half)
        there = lanes_of(1 - half_ref[0], half)
        on_s[:, there] = before_ref[...]
        h1t_ref[...] = h_s[...].astype(wide).T.astype(low)
        x1_ref[:, here] = x_ref[:, here].astype(wide) + mm(on_s[...], woo_ref[...])
        x1_ref[:, there] = x_ref[:, there].astype(wide) + mm(on_s[...], wom_ref[...])
        x1 = x1_ref[...]
        scale = lax.rsqrt(jnp.mean(x1 * x1, axis=-1, keepdims=True) + 1e-06)
        normed = x1 * scale * g_ref[2:3, :]
        h2_ref[...] = normed.astype(low)
        h2t_ref[...] = normed.T.astype(low)


def mixer_forward(half, rows, weights, slot, gains=None, ending=None):
    count, width = rows.shape
    pairs = width // PAIR // 2
    by_pair = pl.BlockSpec((count, PAIR), lambda j, _: (0, j))
    struct = jax.ShapeDtypeStruct
    shape = lambda kind: struct((count, width // 2), kind)
    in_specs = [whole(rows.shape), pl.BlockSpec((width, 3 * PAIR), lambda j, _: (0, j))]
    operands = [half, rows, weights]
    out_specs = [by_pair] * 5
    out_shape = [shape(low), shape(wide), shape(wide), shape(low), shape(low)]
    scratch = [pltpu.VMEM((count, width), low)]
    if ending is None:
        kernel = mixer_forward_first_kernel
        in_specs += [whole(gains.shape)]
        operands += [gains]
        out_specs += [whole((8, width))]
        out_shape += [struct((8, width), wide)]
    if ending is not None:
        kernel = mixer_forward_last_kernel
        out_weights = pl.BlockSpec((width, width // 2), lambda j, _: (0, 3))
        in_specs += [whole(ending[0].shape), whole((count, width // 2)), out_weights, out_weights]
        operands += [ending[0], ending[1], weights, ending[2]]
        out_specs += [whole((count, width))] * 2 + [whole((width, count))] * 2
        out_shape += [
            struct((count, width), wide),
            struct((count, width), low),
            struct((width, count), low),
            struct((width, count), low),
        ]
        scratch += [pltpu.VMEM((count, width), low)]
    return pl.pallas_call(
        functools.partial(kernel, slot),
        grid_spec=pltpu.PrefetchScalarGridSpec(
            num_scalar_prefetch=1,
            grid=(pairs,),
            in_specs=in_specs,
            out_specs=out_specs,
            scratch_shapes=scratch,
        ),
        out_shape=out_shape,
        compiler_params=pltpu.CompilerParams(vmem_limit_bytes=VMEM_BYTES),
        cost_estimate=pl.CostEstimate(
            flops=count * width * 4 * width + 10 * count * slot * width,
            bytes_accessed=count * width * 12 + width * width * 4,
            transcendentals=count * width * 3,
        ),
        name="mixer_forward",
    )(*operands)


def store_down(out_ref, tile, owners):
    _, stride, down_rows = owners
    block = math.gcd(down_rows, tile.shape[0])
    first = pl.program_id(0) * (tile.shape[0] // block)
    for part in range(tile.shape[0] // block):
        owner = (first + part) // (down_rows // block)
        inside = (first + part) % (down_rows // block)
        start = pl.multiple_of(owner * stride + inside * block, block)
        out_ref[pl.ds(start, block), :] = tile[part * block : (part + 1) * block, :]


def ffn_kernel(
    owners,
    core_ref,
    h_ref,
    ht_ref,
    e_ref,
    wm_ref,
    wu_ref,
    wdm_ref,
    wdo_ref,
    x1_hbm,
    onm_hbm,
    ono_hbm,
    wom_hbm,
    woo_hbm,
    m_ref,
    g_ref,
    gm_ref,
    gu_ref,
    gdm_hbm,
    gdo_hbm,
    out_hbm,
    dx1_hbm,
    don_hbm,
    *scratch,
):
    gu_w, gu_g, down_g, down_w, mid_s, dh_s, on_s, x1_s, wo_s, out_s, gdm_s, gdo_s = scratch[:12]
    in_semaphores, out_semaphores, down_semaphores = scratch[12:]
    step, last = pl.program_id(0), pl.num_programs(0) - 1
    half, tile = wdm_ref.shape[1], wm_ref.shape[1]
    mine, other = lanes_of(core_ref[0], half), lanes_of(1 - core_ref[0], half)
    kind, kind_other = lanes_of(core_ref[0], tile), lanes_of(1 - core_ref[0], tile)
    count, stride, down_rows = owners

    width = on_s.shape[1]
    sources = (
        (x1_hbm, x1_s),
        (onm_hbm, on_s.at[:, mine]),
        (ono_hbm, on_s.at[:, other]),
        (wom_hbm.at[:, pl.ds(3 * half, half)], wo_s.at[:, mine]),
        (woo_hbm.at[:, pl.ds(3 * half, half)], wo_s.at[:, other]),
    )
    fetches = [
        pltpu.make_async_copy(source, target, in_semaphores.at[number])
        for number, (source, target) in enumerate(sources)
    ]

    def down_copies(owner):
        rows = pl.ds(pl.multiple_of(owner * stride, math.gcd(stride, 32)), down_rows)
        return [
            pltpu.make_async_copy(held.at[rows, :], out.at[rows, :], down_semaphores.at[side, owner])
            for side, (held, out) in enumerate(((gdm_s, gdm_hbm), (gdo_s, gdo_hbm)))
        ]

    @pl.when(step == 0)
    def _():
        dh_s[...] = jnp.zeros_like(dh_s)
        for fetch in fetches:
            fetch.start()

    gu_w[:, kind] = wm_ref[...]
    gu_w[:, kind_other] = wu_ref[...]
    hidden_rows = pl.ds(pl.multiple_of(step * tile, tile), tile)
    down_w[hidden_rows, mine] = wdm_ref[...]
    down_w[hidden_rows, other] = wdo_ref[...]
    pre = mm(h_ref[...], gu_w[...])
    a, b = pre[:, :tile], pre[:, tile:]
    share = sigmoid(a)
    swish = a * share
    mid = (swish * b).astype(low)
    mid_s[:, lanes_of(step, tile)] = mid
    d_mid = mm_nt(e_ref[...], down_w[hidden_rows, :])
    down_g[...] = mm_tn(mid, e_ref[...]).astype(low)
    d_a = (d_mid * b * (share + swish * (1.0 - share))).astype(low)
    d_b = (d_mid * swish).astype(low)
    d_pre = jnp.concatenate([d_a, d_b], axis=1)
    dh_s[...] += mm_nt(d_pre, gu_w[...])
    gu_g[...] = mm(ht_ref[...], d_pre).astype(low)
    blocks = tile // HEAD_DIM
    for side, block in enumerate((core_ref[1], 1 - core_ref[1])):
        gm_ref[side] = gu_g[:, lanes_of(core_ref[0] * blocks + block, HEAD_DIM)]
        gu_ref[side] = gu_g[:, lanes_of((1 - core_ref[0]) * blocks + block, HEAD_DIM)]
    store_down(gdm_s, down_g[:, mine], owners)
    store_down(gdo_s, down_g[:, other], owners)

    done = (step + 1) * tile // down_rows

    @pl.when(done > step * tile // down_rows)
    def _():
        for copy in down_copies(done - 1):
            copy.start()

    @pl.when(step == last)
    def _():
        for fetch in fetches:
            fetch.wait()
        x1 = x1_s[...]
        x2 = x1 + mm(mid_s[...], down_w[...])
        positions = lax.broadcasted_iota(jnp.int32, (out_s.shape[0] // m_ref.shape[0], 1), 0)
        for sequence in range(m_ref.shape[0]):
            rows = slice(sequence * positions.shape[0], (sequence + 1) * positions.shape[0])
            valid = (positions < m_ref[sequence]).astype(wide)
            out_s[rows, :] = (x2[rows, :] * valid).astype(low)
        leaving = [pltpu.make_async_copy(out_s, out_hbm, out_semaphores.at[0])]
        leaving[-1].start()
        scale = lax.rsqrt(jnp.mean(x1 * x1, axis=-1, keepdims=True) + 1e-06)
        normed = x1 * scale
        scaled = dh_s[...] * g_ref[2:3, :]
        d_x1 = e_ref[...].astype(wide) + scale * (
            scaled - normed * jnp.mean(scaled * normed, axis=-1, keepdims=True)
        )
        dh_s[...] = d_x1
        leaving.append(pltpu.make_async_copy(dh_s, dx1_hbm, out_semaphores.at[1]))
        leaving[-1].start()
        d_1 = mid_s.at[:, pl.ds(0, width)]
        d_1[...] = d_x1.astype(low)
        d_mixed = mid_s.at[:, pl.ds(width, width)]
        d_mixed[...] = mm_nt(d_1[...], wo_s[...]).astype(low)
        leaving.append(pltpu.make_async_copy(d_mixed, don_hbm, out_semaphores.at[2]))
        leaving[-1].start()
        rows = stride - down_rows
        grad_o = mm_tn(on_s[...], d_1[...]).astype(low)
        down_w[pl.ds(0, width), :] = grad_o
        for columns, held, out in ((mine, gdm_s, gdm_hbm), (other, gdo_s, gdo_hbm)):
            for owner in range(count):
                target = slice(owner * stride + down_rows, (owner + 1) * stride)
                held[target, :] = down_w[owner * rows : (owner + 1) * rows, columns]
                copy = pltpu.make_async_copy(
                    held.at[target, :], out.at[target, :], out_semaphores.at[len(leaving)]
                )
                copy.start()
                leaving.append(copy)
        for owner in range(count):
            leaving += down_copies(owner)
        for copy in leaving:
            copy.wait()


def ffn(core, h2, h2t, errors, w_gu, w_d, x1, mixed, w_a, lengths, gains8, owners):
    count, width = h2.shape
    half = width // 2
    hidden = w_gu[0].shape[1]
    full = whole((count, width))
    in_tile = pl.BlockSpec((width, TILE_F), lambda j, _: (0, j))
    out_tile = pl.BlockSpec((TILE_F, half), lambda j, _: (j, 0))
    grad_tile = pl.BlockSpec((2, width, HEAD_DIM), lambda j, _: (0, 0, j))
    anywhere = pl.BlockSpec(memory_space=pl.ANY)
    down_shape = (owners[0] * owners[1], half)
    struct = jax.ShapeDtypeStruct
    vmem = pltpu.VMEM
    return pl.pallas_call(
        functools.partial(ffn_kernel, owners),
        grid_spec=pltpu.PrefetchScalarGridSpec(
            num_scalar_prefetch=1,
            grid=(hidden // TILE_F,),
            in_specs=[full, whole(h2t.shape), full, in_tile, in_tile, out_tile, out_tile]
            + [anywhere] * 5
            + [pl.BlockSpec(memory_space=pltpu.SMEM), whole((8, width))],
            out_specs=[grad_tile, grad_tile] + [anywhere] * 5,
            scratch_shapes=[
                vmem((width, 2 * TILE_F), low),
                vmem((width, 2 * TILE_F), low),
                vmem((TILE_F, width), low),
                vmem((hidden, width), low),
                vmem((count, hidden), low),
                vmem((count, width), wide),
                vmem((count, width), low),
                vmem((count, width), wide),
                vmem((width, width), low),
                vmem((count, width), low),
                vmem(down_shape, low),
                vmem(down_shape, low),
                pltpu.SemaphoreType.DMA((5,)),
                pltpu.SemaphoreType.DMA((3 + 2 * owners[0],)),
                pltpu.SemaphoreType.DMA((2, owners[0])),
            ],
        ),
        out_shape=[struct((2, width, hidden // 2), low)] * 2
        + [struct(down_shape, low)] * 2
        + [
            struct((count, width), low),
            struct((count, width), wide),
            struct((count, width), low),
        ],
        compiler_params=pltpu.CompilerParams(vmem_limit_bytes=VMEM_BYTES),
        cost_estimate=pl.CostEstimate(
            flops=18 * count * width * hidden,
            bytes_accessed=count * width * 20 + width * hidden * 12,
            transcendentals=count * hidden,
        ),
        name="ffn",
    )(core, h2, h2t, errors, *w_gu, *w_d, x1, *mixed, *w_a, lengths, gains8)


def mixer_backward_kernel(
    slot,
    per_half,
    first,
    half_ref,
    ht_ref,
    g_ref,
    q_ref,
    f_ref,
    v_ref,
    o_ref,
    don_ref,
    *outs,
):
    grad_ref, dpre_ref = outs[-2:]
    gain_o = g_ref[1:2, lanes_of(half_ref[0] * per_half + first + pl.program_id(0), PAIR)]
    lower_ones = triangle(slot, True)
    upper_ones = triangle(slot, False)
    causal_t = causal_mask(slot, False)
    for sequence in range(q_ref.shape[0] // slot):
        rows = slice(sequence * slot, (sequence + 1) * slot)
        d_on = don_ref[rows, :].astype(wide)
        out = o_ref[rows, :].astype(wide)
        d_out_parts = []
        for head in range(2):
            lanes = slice(head * HEAD_DIM, (head + 1) * HEAD_DIM)
            out_h, d_on_h = out[:, lanes], d_on[:, lanes]
            scale = lax.rsqrt(jnp.mean(out_h * out_h, axis=-1, keepdims=True) + 1e-05)
            normed = out_h * scale
            scaled = d_on_h * gain_o[:, lanes]
            inner = jnp.mean(scaled * normed, axis=-1, keepdims=True)
            d_out_parts.append((scale * (scaled - normed * inner)).astype(low))

        q_pre = q_ref[rows, :]
        share, gate, keys_in, cumulative = decay_parts(f_ref[rows, :], lower_ones)
        grown = jnp.exp(-cumulative)
        shrunk = jnp.exp(cumulative)
        q_share = sigmoid(q_pre)
        decayed_q = (q_pre * q_share * shrunk).astype(low)
        grown_k = (keys_in * grown).astype(low)
        values = v_ref[rows, :]
        dq_parts, dk_parts, dv_parts = [], [], []
        for head in range(2):
            lanes = slice(head * HEAD_DIM, (head + 1) * HEAD_DIM)
            q_h, k_h, v_h = decayed_q[:, lanes], grown_k[:, lanes], values[:, lanes]
            d_out = d_out_parts[head]
            scores = jnp.where(causal_t, mm_nt(k_h, q_h), 0.0).astype(low)
            d_scores = jnp.where(causal_t, mm_nt(v_h, d_out), 0.0).astype(low)
            dv_parts.append(mm(scores, d_out))
            dk_parts.append(mm(d_scores, q_h))
            dq_parts.append(mm_tn(d_scores, k_h))
        d_decayed = jnp.concatenate(dq_parts, axis=1)
        d_grown = jnp.concatenate(dk_parts, axis=1)
        d_value = jnp.concatenate(dv_parts, axis=1)
        d_cumulative = decayed_q.astype(wide) * d_decayed - grown_k.astype(wide) * d_grown
        d_log = split_sum(upper_ones, d_cumulative)
        d_query = d_decayed * shrunk
        d_key = d_grown * grown
        d_q_pre = d_query * q_share * (1.0 + q_pre * (1.0 - q_share))
        d_f_pre = (1.0 - lower_bound) * (d_log / gate - d_key) * share * (1.0 - share)
        dpre_ref[rows, :PAIR] = d_q_pre.astype(low)
        dpre_ref[rows, PAIR : 2 * PAIR] = d_f_pre.astype(low)
        dpre_ref[rows, 2 * PAIR :] = d_value.astype(low)

    grad = mm(ht_ref[...], dpre_ref[...]).astype(low)
    grad_ref[...] = grad.reshape(grad_ref.shape)


def mixer_backward(half, h1t, gains8, kept, d_mixed, slot, shard, pairs=(0, 1), before=()):
    width, count = h1t.shape
    per_half = width // PAIR // 2
    first = pairs[0]
    by_pair = pl.BlockSpec((count, PAIR), lambda j, _: (0, first + j))
    from_whole = pl.BlockSpec((count, PAIR), lambda j, half: (0, half[0] * per_half + first + j))
    struct = jax.ShapeDtypeStruct
    return pl.pallas_call(
        functools.partial(mixer_backward_kernel, slot, per_half, first),
        grid_spec=pltpu.PrefetchScalarGridSpec(
            num_scalar_prefetch=1,
            grid=(len(pairs),),
            in_specs=[whole((width, count)), whole(gains8.shape)]
            + [by_pair] * 4
            + [from_whole]
            + [pl.BlockSpec(memory_space=pl.ANY)] * len(before),
            out_specs=[
                pl.BlockSpec(
                    (width // shard, 1, shard, 3 * PAIR), lambda j, _: (0, first + j, 0, 0)
                ),
                pl.BlockSpec((count, 3 * PAIR), lambda j, _: (0, first + j)),
            ],
        ),
        out_shape=[
            struct((width // shard, per_half, shard, 3 * PAIR), low),
            struct((count, per_half * 3 * PAIR), low),
        ],
        input_output_aliases={8 + k: k for k in range(len(before))},
        compiler_params=pltpu.CompilerParams(vmem_limit_bytes=VMEM_BYTES),
        cost_estimate=pl.CostEstimate(
            flops=len(pairs) * (count * width * 6 * PAIR + 20 * count * slot * PAIR),
            bytes_accessed=len(pairs) * (count * width * 5 + width * PAIR * 6),
            transcendentals=len(pairs) * count * PAIR * 6,
        ),
        name="mixer_backward",
    )(half, h1t, gains8, *kept, d_mixed, *before)


def input_gradient_rows_kernel(
    x_ref, g_ref, dm_ref, do_ref, wm_ref, wo_ref, dx1_ref, dx_ref
):
    d_h1 = mm_nt(dm_ref[...], wm_ref[...]) + mm_nt(do_ref[...], wo_ref[...])
    normed, scale = first_norm(x_ref, None)
    scaled = d_h1 * g_ref[0:1, :]
    dx_ref[...] = dx1_ref[...] + scale * (
        scaled - normed * jnp.mean(scaled * normed, axis=-1, keepdims=True)
    )


def input_gradient(rows, gains8, d_pre, weights, d_x1):
    count, width = rows.shape
    block = count // 2
    columns = d_pre[0].shape[1]
    by_rows = lambda columns: pl.BlockSpec((block, columns), lambda j: (j, 0))
    weight_spec = pl.BlockSpec((width, columns), lambda j: (0, 0), pipeline_mode=pl.Buffered(1))
    return pl.pallas_call(
        input_gradient_rows_kernel,
        grid=(count // block,),
        in_specs=[by_rows(width), whole(gains8.shape)]
        + [by_rows(columns)] * 2
        + [weight_spec] * 2
        + [by_rows(width)],
        out_specs=by_rows(width),
        out_shape=jax.ShapeDtypeStruct((count, width), wide),
        compiler_params=pltpu.CompilerParams(vmem_limit_bytes=VMEM_BYTES),
        cost_estimate=pl.CostEstimate(
            flops=6 * count * width * width,
            bytes_accessed=count * width * 16 + width * width * 6,
            transcendentals=0,
        ),
        name="input_gradient",
    )(rows, gains8, *d_pre, *weights, d_x1)


def update(weight, momentum, average, gradient, step_rate):
    new_momentum = momentum_decay * momentum + gradient
    direction = gradient + momentum_decay * new_momentum + weight_decay * weight
    new_weight = weight - step_rate * direction
    new_average = average_decay * average + (1.0 - average_decay) * new_weight
    return (new_momentum, new_average, new_weight)


def update_kernel(pick, step_rate, sum_count, core_ref, w_ref, m_ref, a_ref, *refs):
    sums, outs, dots_ref = refs[:sum_count], refs[-4:-1], refs[-1]
    weight = w_ref[...]
    gradient = pick(core_ref[0], *[s[...] for s in sums]).astype(wide).reshape(weight.shape)
    results = update(weight, m_ref[...], a_ref[...], gradient, step_rate)
    for out, result in zip(outs, results):
        out[...] = result
    product = weight.astype(low).astype(wide) * gradient
    total = product[..., :HEAD_DIM]
    for start in range(HEAD_DIM, product.shape[-1], HEAD_DIM):
        total = total + product[..., start : start + HEAD_DIM]
    dots_ref[...] = total.reshape(dots_ref.shape)


def update_call(
    core, state, sums, grid, state_spec, sum_specs, pick, step_rate, name, before=()
):
    struct = jax.ShapeDtypeStruct(state[0].shape, wide)
    size = math.prod(state[0].shape)
    rows = state_spec.block_shape[-2]
    steps = math.prod(grid)
    tail = grid[1:]

    def dots_index(*indices):
        place = indices[0]
        for length, index in zip(tail, indices[1:]):
            place = place * length + index
        return (place, 0, 0)

    return pl.pallas_call(
        functools.partial(update_kernel, pick, step_rate, len(sums)),
        grid_spec=pltpu.PrefetchScalarGridSpec(
            num_scalar_prefetch=1,
            grid=grid,
            in_specs=[state_spec] * 3
            + sum_specs
            + [pl.BlockSpec(memory_space=pl.ANY)] * len(before),
            out_specs=[state_spec] * 3 + [pl.BlockSpec((1, rows, HEAD_DIM), dots_index)],
        ),
        out_shape=[struct] * 3 + [jax.ShapeDtypeStruct((steps, rows, HEAD_DIM), wide)],
        input_output_aliases={4 + len(sums) + k: k for k in range(len(before))},
        compiler_params=pltpu.CompilerParams(vmem_limit_bytes=VMEM_BYTES),
        cost_estimate=pl.CostEstimate(flops=12 * size, bytes_accessed=26 * size, transcendentals=0),
        name=name,
    )(core, *state, *sums, *before)


def update_attention_kernel(
    pick, step_rate, gain_step, core_ref, w_ref, m_ref, a_ref, qfv_ref, out_ref, *refs
):
    if gain_step is None:
        update_kernel(pick, step_rate, 2, core_ref, w_ref, m_ref, a_ref, qfv_ref, out_ref, *refs)
        return
    *held, dots_s = refs
    own_dots, up_dots, gate_dots, g_ref, gm_ref, ga_ref = held[:6]
    outs, gain_outs = held[-6:-3], held[-3:]
    kind = pl.program_id(0)
    dots = dots_s.at[kind]
    update_kernel(
        pick, step_rate, 2, core_ref, w_ref, m_ref, a_ref, qfv_ref, out_ref, *outs, dots
    )

    @pl.when(kind == pl.num_programs(0) - 1)
    def _():
        shard = dots_s.shape[1]
        sums = [own_dots[k] + dots_s[k] for k in range(4)]
        two = (up_dots[...] + gate_dots[...]).reshape(shard, HEAD_DIM)
        columns = [
            jnp.sum(total, axis=1, keepdims=True) for total in (sums[0] + sums[1] + sums[2], sums[3], two)
        ]
        lanes = lax.broadcasted_iota(jnp.int32, (shard, HEAD_DIM), 1)
        table = jnp.where(lanes == 1, columns[1], columns[2])
        table = jnp.where(lanes == 0, columns[0], table)
        gain = g_ref[...]
        gradient = table.T[:3, :] / gain.astype(low).astype(wide)
        results = update(gain, gm_ref[...], ga_ref[...], gradient, gain_step)
        for out, result in zip(gain_outs, results):
            out[...] = result


def update_attention(half_ref, state, qfv, out, step_rate, gains=None):
    _, shard, width = state[0].shape
    down_rows = out.shape[0] - shard

    def pick(core_index, proj, last):
        gradient = last[down_rows:].astype(wide)
        for kind in range(3):
            parts = [proj[pair * shard :, kind * PAIR :][:shard, :PAIR] for pair in range(2)]
            chosen = jnp.concatenate(parts, axis=1).astype(wide)
            gradient = jnp.where(pl.program_id(0) == kind, chosen, gradient)
        return gradient

    struct = jax.ShapeDtypeStruct
    state_spec = pl.BlockSpec((1, shard, width // 2), lambda kind, half: (kind, 0, half[0]))
    in_specs = [state_spec] * 3 + [whole(qfv.shape), whole(out.shape)]
    out_specs = [state_spec] * 3
    out_shape = [struct(state[0].shape, wide)] * 3
    operands = [half_ref, *state, qfv, out]
    aliases, scratch, gain_step = {}, [], None
    if gains is None:
        out_specs += [pl.BlockSpec((1, shard, HEAD_DIM), lambda kind, half: (kind, 0, 0))]
        out_shape += [struct((4, shard, HEAD_DIM), wide)]
    else:
        before, dots, gain_state, gain_step = gains
        in_specs += [whole(part.shape) for part in (*dots, *gain_state)]
        operands += [*dots, *gain_state]
        aliases = {len(operands) + k: k for k in range(3)}
        in_specs += [pl.BlockSpec(memory_space=pl.ANY)] * 3
        operands += list(before)
        out_specs += [whole(gain_state[0].shape)] * 3
        out_shape += [struct(gain_state[0].shape, wide)] * 3
        scratch = [pltpu.VMEM((4, shard, HEAD_DIM), wide)]
    size = math.prod(state[0].shape) // 2
    return pl.pallas_call(
        functools.partial(update_attention_kernel, pick, step_rate, gain_step),
        grid_spec=pltpu.PrefetchScalarGridSpec(
            num_scalar_prefetch=1,
            grid=(4,),
            in_specs=in_specs,
            out_specs=out_specs,
            scratch_shapes=scratch,
        ),
        out_shape=out_shape,
        input_output_aliases=aliases,
        compiler_params=pltpu.CompilerParams(vmem_limit_bytes=VMEM_BYTES),
        cost_estimate=pl.CostEstimate(flops=12 * size, bytes_accessed=26 * size, transcendentals=0),
        name="update_attention",
    )(*operands)


def update_ffn_in(kind_ref, state, totals, step_rate, before):
    _, shard, hidden = state[0].shape
    block = shard // 2

    def pick(_, even, odd):
        blocks = []
        for start in range(0, hidden // 2, HEAD_DIM):
            blocks += [even[:, start : start + HEAD_DIM], odd[:, start : start + HEAD_DIM]]
        return jnp.concatenate(blocks, axis=1)

    return update_call(
        kind_ref,
        state,
        totals,
        (2,),
        pl.BlockSpec((1, block, hidden), lambda j, kind: (kind[0], j, 0)),
        [pl.BlockSpec((block, hidden // 2), lambda j, _: (j, 0))] * 2,
        pick,
        step_rate,
        "update_ffn_in",
        before,
    )


def update_ffn_out(core, state, sums, step_rate):
    shard, width = state[0].shape

    def pick(core_index, mine, other):
        own = pl.program_id(0) == core_index
        return jnp.where(own, mine[:shard].astype(wide), other[:shard].astype(wide))

    return update_call(
        core,
        state,
        sums,
        (2,),
        pl.BlockSpec((shard, width // 2), lambda j, _: (0, j)),
        [whole(total.shape) for total in sums],
        pick,
        step_rate,
        "update_ffn_out",
    )


def pack_kernel(core_ref, w_ref, out_ref):
    half = w_ref.shape[2]
    for pair in range(half // PAIR):
        for kind in range(3):
            start = (pair * 3 + kind) * PAIR
            piece = w_ref[kind, :, pair * PAIR : (pair + 1) * PAIR]
            out_ref[:, start : start + PAIR] = piece.astype(low)
    out_ref[:, 3 * half : 4 * half] = w_ref[3].astype(low)


def pack_attention(core, weights):
    _, shard, width = weights.shape
    half = width // 2
    return pl.pallas_call(
        pack_kernel,
        grid_spec=pltpu.PrefetchScalarGridSpec(
            num_scalar_prefetch=1,
            grid=(1,),
            in_specs=[pl.BlockSpec((4, shard, half), lambda j, core: (0, 0, core[0]))],
            out_specs=whole((shard, 4 * half)),
        ),
        out_shape=jax.ShapeDtypeStruct((shard, 4 * half), low),
        name="pack_attention",
    )(core, weights)


RING = 8


def ring_place(index):
    return jnp.where(index % 2 == 0, index // 2, RING - 1 - index // 2)


def ring_member(place):
    place = place % RING
    return jnp.where(place < RING // 2, 2 * place, 2 * RING - 1 - 2 * place)


CYCLE = (0, 2, 4, 6, 7, 5, 3, 1)


def ring_next(tensor):
    replicas = lax.axis_size("dp")
    pairs = []
    for place_of, member in enumerate(CYCLE):
        for replica in range(replicas):
            target = CYCLE[(place_of + (1 if replica % 2 == 0 else -1)) % RING]
            pairs.append((member * replicas + replica, target * replicas + replica))
    return lax.ppermute(tensor, ("fsdp", "dp"), pairs)


def ring_shift(tensor, way):
    pairs = [(member, CYCLE[(at + way) % RING]) for at, member in enumerate(CYCLE)]
    return lax.ppermute(tensor, "fsdp", pairs)


def core_swap(tensor):
    return lax.ppermute(tensor, "dp", [(d, d ^ 1) for d in range(lax.axis_size("dp"))])


def column_swap(tensor):
    return lax.ppermute(tensor, "dp", [(d, d ^ 2) for d in range(lax.axis_size("dp"))])


def pack_all_kernel(
    core_ref, column_ref, w_ref, up_ref, other_ref, down_ref, g_ref, out_ref, across_ref
):
    across_ref[...] = other_ref[0].astype(low)
    shard = w_ref.shape[1]
    half = w_ref.shape[2]
    for pair in range(half // PAIR):
        for kind in range(3):
            start = (pair * 3 + kind) * PAIR
            piece = w_ref[kind, :, pair * PAIR : (pair + 1) * PAIR]
            out_ref[:, start : start + PAIR] = piece.astype(low)
    out_ref[:, 3 * half : 4 * half] = w_ref[3].astype(low)
    start = 4 * half
    out_ref[:, start : start + up_ref.shape[2]] = up_ref[0].astype(low)
    start += up_ref.shape[2]
    for first, count in down_parts(down_ref.shape[0], shard):
        out_ref[:count, start : start + half] = down_ref[first : first + count, :].astype(low)
        if count < shard:
            out_ref[count:, start : start + half] = jnp.zeros((shard - count, half), low)
            rows = lax.broadcasted_iota(jnp.int32, (GAIN_ROWS, g_ref.shape[1]), 0)
            gains = jnp.where(rows == 1, g_ref[1:2, :], g_ref[2:3, :])
            gains = jnp.where(rows == 0, g_ref[0:1, :], gains)
            gains = jnp.where(rows < 3, gains, 0.0).astype(low)
            out_ref[count : count + GAIN_ROWS, start : start + g_ref.shape[1]] = gains
        start += half


def down_parts(down_rows, shard):
    return [(start, min(shard, down_rows - start)) for start in range(0, down_rows, shard)]


def pack_all(core, column, weights, up, down, gains):
    _, shard, width = weights.shape
    half = width // 2
    parts = len(down_parts(down.shape[0], shard))
    columns = 4 * half + up.shape[2] // 2 + parts * half
    return pl.pallas_call(
        pack_all_kernel,
        grid_spec=pltpu.PrefetchScalarGridSpec(
            num_scalar_prefetch=2,
            grid=(1,),
            in_specs=[
                pl.BlockSpec((4, shard, half), lambda j, core, column: (0, 0, core[0])),
                pl.BlockSpec(
                    (1, shard, up.shape[2] // 2), lambda j, core, column: (core[0], 0, column[0])
                ),
                pl.BlockSpec(
                    (1, shard, up.shape[2] // 2),
                    lambda j, core, column: (core[0], 0, 1 - column[0]),
                ),
                pl.BlockSpec((down.shape[0], half), lambda j, core, column: (0, core[0])),
                whole(gains.shape),
            ],
            out_specs=[whole((shard, columns)), whole((shard, up.shape[2] // 2))],
        ),
        out_shape=[
            jax.ShapeDtypeStruct((shard, columns), low),
            jax.ShapeDtypeStruct((shard, up.shape[2] // 2), low),
        ],
        compiler_params=pltpu.CompilerParams(vmem_limit_bytes=VMEM_BYTES),
        name="pack_all",
    )(core, column, weights, up, up, down, gains)


def place_kernel(which, kept, shapes, origin_ref, column_ref, *refs):
    pieces, outs, semaphores = refs[: len(which)], refs[-1 - len(kept) : -1], refs[-1]
    targets = dict(zip(kept, outs))
    shard, first, up_columns, down_rows, half = shapes
    copies = []

    def copy(source, target):
        copies.append(pltpu.make_async_copy(source, target, semaphores.at[len(copies)]))

    for piece, (origin, across) in zip(pieces, which):
        owner = origin_ref[origin]
        rows = pl.ds(pl.multiple_of(owner * shard, 16), shard)
        if across:
            copy(piece, targets[1].at[rows, lanes_of(1 - column_ref[0], up_columns)])
            continue
        copy(piece.at[:, pl.ds(0, first)], targets[0].at[rows, :])
        own = targets[1].at[rows, lanes_of(column_ref[0], up_columns)]
        copy(piece.at[:, pl.ds(first, up_columns)], own)
        lane = first + up_columns
        for start, count in down_parts(down_rows, shard):
            target = pl.ds(pl.multiple_of(owner * down_rows + start, 16), count)
            copy(piece.at[pl.ds(0, count), pl.ds(lane, half)], targets[2].at[target, :])
            if count < shard:
                source = piece.at[pl.ds(count, GAIN_ROWS), pl.ds(lane, shard)]
                copy(source, targets[3].at[:, lanes_of(owner, shard)])
            lane += half
    for one in copies:
        one.start()
    for one in copies:
        one.wait()


def place(origins, column, which, pieces, arrays, kept, shapes):
    anywhere = pl.BlockSpec(memory_space=pl.ANY)
    shard, first, up_columns, down_rows, half = shapes
    kinds = [(RING * shard, first), (RING * shard, 2 * up_columns), (RING * down_rows, half)]
    kinds.append((GAIN_ROWS, RING * shard))
    held = [] if arrays is None else list(arrays)
    size = sum(math.prod(piece.shape) for piece in pieces)
    before = 2 + len(pieces)
    return pl.pallas_call(
        functools.partial(place_kernel, which, kept, shapes),
        grid_spec=pltpu.PrefetchScalarGridSpec(
            num_scalar_prefetch=2,
            grid=(1,),
            in_specs=[whole(piece.shape) for piece in pieces] + [anywhere] * len(held),
            out_specs=[anywhere] * len(kept),
            scratch_shapes=[pltpu.SemaphoreType.DMA((8 * len(pieces),))],
        ),
        out_shape=[jax.ShapeDtypeStruct(kinds[k], pieces[0].dtype) for k in kept],
        input_output_aliases={before + k: k for k in range(len(held))},
        compiler_params=pltpu.CompilerParams(vmem_limit_bytes=VMEM_BYTES),
        cost_estimate=pl.CostEstimate(flops=0, bytes_accessed=8 * size, transcendentals=0),
        name="place",
    )(origins, column, *pieces, *held)


def after(tensor, *others):
    return lax.optimization_barrier((tensor, *others))[0]


def core_way():
    return 1 - 2 * (lax.axis_index("dp") % 2)


def ring_origins():
    steps = jnp.array((0, -1, -2, -3, -4, 1, 2, 3), jnp.int32)
    return ring_member(ring_place(lax.axis_index("fsdp")) + steps + RING).astype(jnp.int32)


class RingSumOverColumns:
    def __init__(self, mine, arrived):
        self.arrays = (mine, arrived)
        place = ring_place(lax.axis_index("fsdp"))
        self.rows = mine.shape[1] // RING
        self.starts = [
            ring_member(place - core_way() * (s + 1) + 2 * RING) * self.rows for s in range(RING)
        ]
        self.sent, self.came, self.totals = [], [], []

    def part(self, side, step):
        shape = (1, self.rows, self.arrays[0].shape[2])
        parts = [
            lax.dynamic_slice(array, (side, self.starts[step], 0), shape)[0]
            for array in self.arrays
        ]
        return parts[0].astype(wide) + parts[1].astype(wide)

    def cross(self):
        self.sent.append(self.part(1, len(self.sent)).astype(low))
        self.came.append(column_swap(self.sent[-1]))

    def term(self):
        step = len(self.totals)
        return self.part(0, step) + self.came[step].astype(wide)

    def begin(self, *others):
        self.came[0] = after(self.came[0], *others) if others else self.came[0]
        self.totals.append(self.term().astype(low))

    def step(self, arriving=()):
        total, ahead = self.totals[-1], self.came[len(self.totals)]
        moved = ring_next(after(total, ahead) if len(self.totals) > 1 else total)
        moved = after(moved, *arriving) if arriving else moved
        self.totals.append((moved.astype(wide) + self.term()).astype(low))

    def last(self):
        return self.totals[-1]


class RingSum:
    def __init__(self, mine, arrived):
        self.mine, self.arrived = mine, arrived
        place = ring_place(lax.axis_index("fsdp"))
        self.owners = [ring_member(place - core_way() * (s + 1) + 2 * RING) for s in range(RING)]
        self.totals = []

    def term(self):
        parts = []
        for own, arrived in zip(self.mine, self.arrived):
            rows = own.shape[0] // RING
            start = self.owners[len(self.totals)] * rows
            part = lax.dynamic_slice_in_dim(own, start, rows, 0).astype(wide)
            parts.append(part + lax.dynamic_slice_in_dim(arrived, start, rows, 0).astype(wide))
        return parts[0] if len(parts) == 1 else jnp.concatenate(parts, axis=0)

    def begin(self, *others):
        if others:
            self.mine = [after(self.mine[0], *others), *self.mine[1:]]
        self.totals.append(self.term().astype(low))

    def step(self, *before, arriving=()):
        total = self.totals[-1]
        moved = ring_next(after(total, *before) if before else total)
        moved = after(moved, *arriving) if arriving else moved
        self.totals.append((moved.astype(wide) + self.term().astype(wide)).astype(low))

    def last(self):
        return self.totals[-1]


def gather_rows(shard):
    mine = lax.all_gather(shard, "fsdp", axis=0, tiled=True)
    return mine, core_swap(mine)


def core_sum(mine, other):
    return (mine.astype(wide) + core_swap(other).astype(wide)).astype(low)


def scatter_rows(both):
    return lax.psum_scatter(both, "fsdp", scatter_dimension=0, tiled=True)


def over_columns(total):
    total = (total.astype(wide) + column_swap(total).astype(wide)).astype(low)
    return total, core_swap(total)


def on_device(
    inputs,
    cotangent,
    lengths,
    attention_weights,
    attention_momentum,
    attention_average,
    ffn_inputs,
    ffn_inputs_momentum,
    ffn_inputs_average,
    ffn_output,
    ffn_output_momentum,
    ffn_output_average,
    gains,
    gains_momentum,
    gains_average,
):
    micro_count, slot, width = inputs.shape
    hidden = ffn_inputs.shape[2]
    shard, down_rows = ffn_inputs.shape[1], ffn_output.shape[0]
    fsdp_size = lax.axis_size("fsdp")
    replicas = lax.axis_size("dp")
    ringed = fsdp_size == RING
    core = lax.axis_index("dp") % 2
    column = lax.axis_index("dp") // 2
    count = micro_count * slot
    half = width // 2
    core_ref = core.astype(jnp.int32).reshape(1)
    other_ref = 1 - core_ref
    column_ref = column.astype(jnp.int32).reshape(1)
    is_first = core == 0

    rows = inputs.reshape(count, width)
    positions = jnp.arange(slot, dtype=jnp.int32)
    valid = (positions[None, :] < lengths).astype(wide).reshape(count, 1)
    errors = (cotangent.reshape(count, width).astype(wide) * valid).astype(low)

    if ringed:
        origins = ring_origins()
        first = 4 * half
        shapes = (shard, first, hidden // 2, down_rows, half)
        packed, own_across = pack_all(
            core_ref, column_ref, attention_weights, ffn_inputs, ffn_output, gains
        )
        wholes, there, which_there = None, [own_across], [(0, True)]
        here, which = [packed], [(0, False)]
        for step in range(1, 6):
            if step <= 3:
                onward = [ring_shift(here[0], 1), ring_shift(here[-1], -1)]
            elif step == 4:
                onward = [ring_next(jnp.where(is_first, *here))]
            across = []
            if step > 1:
                across = [column_swap(piece[:, first : first + hidden // 2]) for piece in here]
            wholes = place(
                origins, column_ref, which + which_there, here + there, wholes, (0, 1, 2, 3), shapes
            )
            if step == 5:
                break
            extra = [errors] if step == 2 else []
            tied = list(lax.optimization_barrier((*onward, *across, *wholes, *extra)))
            here, rest = tied[: len(onward)], tied[len(onward) :]
            there, wholes = rest[: len(across)], rest[len(across) : len(across) + 4]
            which_there = [(origin, True) for origin, _ in which] if across else []
            which = [(origin, False) for origin in [step, step + 4][: len(onward)]]
        w_a, gain_rows = (wholes[0], core_swap(wholes[0])), wholes[3]
    else:
        w_a = gather_rows(pack_attention(core_ref, attention_weights))
        gain_rows = lax.all_gather(gains.astype(low), "fsdp", axis=1, tiled=True)
        gain_rows = jnp.pad(gain_rows, ((0, GAIN_ROWS - 3), (0, 0)))
        w_gu = gather_rows(
            lax.dynamic_index_in_dim(ffn_inputs, core, 0, keepdims=False).astype(low)
        )
        w_d = gather_rows(lax.dynamic_slice_in_dim(ffn_output, core * half, half, 1).astype(low))
    mixed_mine, *kept_mine, gains8 = mixer_forward(core_ref, rows, w_a[0], slot, gain_rows)
    if ringed:
        (across,) = lax.optimization_barrier((*across, mixed_mine, w_a[1]))[:1]
        (w_gu_mine,) = place(origins, column_ref, [(4, True)], [across], [wholes[1]], (1,), shapes)
        wholes = [wholes[0], w_gu_mine, wholes[2], wholes[3]]
        rows = after(rows, *wholes[1:3])
        w_gu, w_d = [(array, core_swap(array)) for array in wholes[1:3]]
    mixed_other, *rest = mixer_forward(
        other_ref, rows, w_a[1], slot, None, (gains8, mixed_mine, w_a[0])
    )
    kept_other, (x1, h2, h2t, h1t) = rest[:4], rest[4:]
    owners = (RING, down_rows + shard, down_rows)
    if not ringed:
        owners = (1, hidden + width, hidden)
    places = jnp.concatenate([core_ref, column_ref])
    *grad_gu, gd_mine, gd_other, output, d_x1, d_mixed = ffn(
        places, h2, h2t, errors, w_gu, w_d, x1, (mixed_mine, mixed_other), w_a, lengths[:, 0], gains8, owners
    )

    gm, gu = grad_gu
    arrived_gu = core_swap(gu)
    mine_do, arrived_do = [gd_mine], [core_swap(gd_other)]
    by_owner = (fsdp_size * 2 * shard, 3 * PAIR)
    d_pre = []
    for call in range(4):
        from_half, kept = (other_ref, kept_other) if call < 2 else (core_ref, kept_mine)
        if ringed and call == 1:
            sum_gu = RingSumOverColumns(after(gm, d_pre[0]), arrived_gu)
            sum_gu.cross()
            sum_gu.cross()
            h1t = after(h1t, *sum_gu.sent)
        elif ringed and call > 1:
            sum_gu.cross()
            ahead = [sum_gu.came[2]] if call == 3 else []
            h1t = after(h1t, sum_gu.last(), sum_do.last(), sum_gu.sent[-1], *ahead)
        grads = mixer_backward(
            from_half,
            h1t,
            gains8,
            kept,
            d_mixed,
            slot,
            shard,
            (call % 2,),
            grads if call % 2 else (),
        )
        d_pre.append(grads[1])
        if call == 1:
            grad_other = grads[0]
            if ringed:
                sum_do = RingSum(mine_do, arrived_do)
                sum_do.begin(d_pre[-1])
                sum_gu.begin(d_pre[-1])
                grad_other = after(grad_other, sum_gu.last(), sum_do.last())
            arrived_qfv = [core_swap(grad_other.reshape(by_owner))]
        elif ringed and call > 1:
            sum_do.step(arriving=(d_pre[-1],))
            sum_gu.step(arriving=(d_pre[-1],))
    mine_qfv = [grads[0].reshape(by_owner)]

    def finish_input(*others):
        late = after(d_pre[3], *others) if others else d_pre[3]
        return input_gradient(rows, gains8, (late, d_pre[1]), w_a, d_x1)

    if ringed:
        sum_qfv = RingSum(mine_qfv, arrived_qfv)
        sum_qfv.begin()
        input_grad = None
        for step in range(1, RING - 1):
            if len(sum_gu.came) < RING:
                sum_gu.cross()
            if len(sum_gu.totals) < RING:
                first = [sum_gu.last(), sum_qfv.last()]
                sum_do.step(*{1: first, 4: [input_grad]}.get(step, []))
                sum_gu.step()
            sum_qfv.step()
            if step == 2:
                input_grad = finish_input(sum_qfv.last(), sum_gu.came[5])
        total_gu, total_do = sum_gu.last(), sum_do.last()
    else:
        both = (gm.astype(wide) + arrived_gu.astype(wide)).astype(low)
        here = (both[0].astype(wide) + column_swap(both[1]).astype(wide)).astype(low)
        total_gu = scatter_rows(here)
        both = (gd_mine.astype(wide) + arrived_do[0].astype(wide)).astype(low)
        total_do = jnp.concatenate(
            [scatter_rows(both[:hidden]), scatter_rows(both[hidden:])], axis=0
        )
        total_qfv = scatter_rows(
            (mine_qfv[0].astype(wide) + arrived_qfv[0].astype(wide)).astype(low)
        )
        input_grad = finish_input()
    scale_rows = 1.0 / math.sqrt(count * fsdp_size * replicas)
    matrix_step = matrix_rate * scale_rows
    attention_state = (attention_weights, attention_momentum, attention_average)
    ffn_in_state = (ffn_inputs, ffn_inputs_momentum, ffn_inputs_average)
    ffn_out_state = (ffn_output, ffn_output_momentum, ffn_output_average)
    sum_do = over_columns(total_do)
    there = column_swap(total_gu)
    even = jnp.where(column == 0, total_gu, there)
    odd = jnp.where(column == 0, there, total_gu)
    sum_gu = (even, odd), (core_swap(even), core_swap(odd))
    *new_out, _ = update_ffn_out(core_ref, ffn_out_state, sum_do, matrix_step)
    *new_in, dots_up = update_ffn_in(core_ref, ffn_in_state, sum_gu[0], matrix_step, ())
    *new_in, dots_gate = update_ffn_in(other_ref, ffn_in_state, sum_gu[1], matrix_step, new_in)
    if ringed:
        sum_qfv.step(arriving=(new_out[0],))
        total_qfv = sum_qfv.last()
    there = after(column_swap(total_qfv), new_in[0])
    sum_qfv = (total_qfv.astype(wide) + there.astype(wide)).astype(low)
    *own, dots_own = update_attention(
        core_ref, attention_state, sum_qfv, sum_do[0], matrix_step
    )
    theirs = after(core_swap(sum_qfv), own[0])
    gain_state = (gains, gains_momentum, gains_average)
    *new_attention, gains_m, gains_a, gains_w = update_attention(
        other_ref,
        attention_state,
        theirs,
        sum_do[1],
        matrix_step,
        (own, (dots_own, dots_up, dots_gate), gain_state, gain_rate * scale_rows),
    )
    return (
        output.reshape(micro_count, slot, width),
        input_grad.reshape(micro_count, slot, width),
        *new_attention,
        *new_in,
        *new_out,
        gains_m,
        gains_a,
        gains_w,
    )


def solution(mesh):
    rows_split = P(None, ("fsdp", "dp"), None)
    middle_split = P(None, "fsdp", None)
    first_split = P("fsdp", None)
    gains_split = P(None, "fsdp")
    in_specs = (
        (rows_split, rows_split, P(None, ("fsdp", "dp")))
        + (middle_split,) * 6
        + (first_split,) * 3
        + (gains_split,) * 3
    )
    out_specs = (
        (rows_split, rows_split)
        + (middle_split,) * 6
        + (first_split,) * 3
        + (gains_split,) * 3
    )
    return jax.shard_map(
        on_device, mesh=mesh, in_specs=in_specs, out_specs=out_specs, check_vma=False
    )
```

```python
import functools
import math

import jax
import jax.numpy as jnp
from jax import lax
from jax.experimental import pallas as pl
from jax.experimental.pallas import tpu as pltpu
from jax.sharding import PartitionSpec as P

HEAD_DIM = 128
PAIR = 2 * HEAD_DIM
GAIN_ROWS = 16

lower_bound = 0.9
momentum_decay = 0.9
average_decay = 0.7
weight_decay = 0.0005
matrix_rate = 0.03
gain_rate = 0.1
low = jnp.bfloat16
wide = jnp.float32
TILE_F = 256
VMEM_BYTES = 60 * 1024 * 1024


def mm(left, right):
    return jnp.dot(left, right, preferred_element_type=wide)


def mm_nt(left, right):
    return lax.dot_general(left, right, (((1,), (1,)), ((), ())), preferred_element_type=wide)


def mm_tn(left, right):
    return lax.dot_general(left, right, (((0,), (0,)), ((), ())), preferred_element_type=wide)


def sigmoid(u):
    return 0.5 * jnp.tanh(0.5 * u) + 0.5


def whole(shape):
    return pl.BlockSpec(shape, lambda *_: (0,) * len(shape), pipeline_mode=pl.Buffered(1))


def split_sum(ones_matrix, tensor):
    high = tensor.astype(low)
    rest = (tensor - high.astype(wide)).astype(low)
    return mm(ones_matrix, high) + mm(ones_matrix, rest)


def causal_mask(length, lower):
    rows = lax.broadcasted_iota(jnp.int32, (length, length), 0)
    columns = lax.broadcasted_iota(jnp.int32, (length, length), 1)
    return rows >= columns if lower else rows <= columns


def triangle(length, lower):
    return causal_mask(length, lower).astype(wide).astype(low)


def decay_parts(f_pre, lower_ones):
    share = sigmoid(f_pre)
    gate = lower_bound + (1.0 - lower_bound) * share
    keys_in = (1.0 - lower_bound) * (1.0 - share)
    cumulative = split_sum(lower_ones, jnp.log(gate))
    middle_row = cumulative.shape[0] // 2
    cumulative = cumulative - cumulative[middle_row : middle_row + 1, :]
    return share, gate, keys_in, cumulative


def first_norm(x_ref, gain_row):
    rows = x_ref[...].astype(wide)
    scale = lax.rsqrt(jnp.mean(rows * rows, axis=-1, keepdims=True) + 1e-06)
    return rows * scale, scale


def lanes_of(half, size):
    return pl.ds(pl.multiple_of(half * size, size), size)


def mixer_forward_first_kernel(
    slot, half_ref, x_ref, w_ref, gains_ref, on_ref, q_ref, f_ref, v_ref, o_ref, g_ref, h_s
):
    @pl.when(pl.program_id(0) == 0)
    def _():
        g_ref[...] = gains_ref[...].astype(wide)[: g_ref.shape[0], :]

    mixer_forward_kernel(
        slot, half_ref, x_ref, w_ref, g_ref, on_ref, q_ref, f_ref, v_ref, o_ref, h_s
    )


def mixer_forward_kernel(
    slot, half_ref, x_ref, w_ref, g_ref, on_ref, q_ref, f_ref, v_ref, o_ref, h_s
):
    @pl.when(pl.program_id(0) == 0)
    def _():
        normed, _ = first_norm(x_ref, None)
        h_s[...] = (normed * g_ref[0:1, :]).astype(low)

    gain_o = g_ref[1:2, lanes_of(half_ref[0] * pl.num_programs(0) + pl.program_id(0), PAIR)]
    pre = mm(h_s[...], w_ref[...])
    q_ref[...] = pre[:, :PAIR]
    f_ref[...] = pre[:, PAIR : 2 * PAIR]
    v_ref[...] = pre[:, 2 * PAIR :].astype(low)
    lower_ones = triangle(slot, True)
    causal = causal_mask(slot, True)
    for sequence in range(x_ref.shape[0] // slot):
        rows = slice(sequence * slot, (sequence + 1) * slot)
        q_pre = q_ref[rows, :]
        _, _, keys_in, cumulative = decay_parts(f_ref[rows, :], lower_ones)
        grown = jnp.exp(-cumulative)
        decayed_q = (q_pre * sigmoid(q_pre) * jnp.exp(cumulative)).astype(low)
        grown_k = (keys_in * grown).astype(low)
        values = v_ref[rows, :]
        for head in range(2):
            lanes = slice(head * HEAD_DIM, (head + 1) * HEAD_DIM)
            scores = mm_nt(decayed_q[:, lanes], grown_k[:, lanes])
            out = mm(jnp.where(causal, scores, 0.0).astype(low), values[:, lanes])
            scale = lax.rsqrt(jnp.mean(out * out, axis=-1, keepdims=True) + 1e-05)
            o_ref[rows, lanes] = out.astype(low)
            on_ref[rows, lanes] = (out * scale * gain_o[:, lanes]).astype(low)


def mixer_forward_last_kernel(
    slot,
    half_ref,
    x_ref,
    w_ref,
    g_ref,
    before_hbm,
    woo_hbm,
    wom_hbm,
    on_ref,
    q_ref,
    f_ref,
    v_ref,
    o_ref,
    x1_hbm,
    h2_ref,
    h2t_ref,
    h_s,
    on_s,
    x1_s,
    wo_s,
    semaphores,
):
    step = pl.program_id(0)
    half = before_hbm.shape[1]
    here, there = lanes_of(half_ref[0], half), lanes_of(1 - half_ref[0], half)
    sources = (
        (before_hbm, on_s.at[:, there]),
        (woo_hbm.at[:, pl.ds(3 * half, half)], wo_s.at[:, here]),
        (wom_hbm.at[:, pl.ds(3 * half, half)], wo_s.at[:, there]),
    )
    fetches = [
        pltpu.make_async_copy(source, target, semaphores.at[number])
        for number, (source, target) in enumerate(sources)
    ]

    @pl.when(step == 0)
    def _():
        for fetch in fetches:
            fetch.start()

    mixer_forward_kernel(
        slot, half_ref, x_ref, w_ref, g_ref, on_ref, q_ref, f_ref, v_ref, o_ref, h_s
    )
    on_s[:, lanes_of(half_ref[0] * pl.num_programs(0) + step, PAIR)] = on_ref[...]

    @pl.when(step == pl.num_programs(0) - 1)
    def _():
        for fetch in fetches:
            fetch.wait()
        x1 = x_ref[...].astype(wide) + mm(on_s[...], wo_s[...])
        x1_s[...] = x1
        leaving = pltpu.make_async_copy(x1_s, x1_hbm, semaphores.at[3])
        leaving.start()
        scale = lax.rsqrt(jnp.mean(x1 * x1, axis=-1, keepdims=True) + 1e-06)
        normed = x1 * scale * g_ref[2:3, :]
        h2_ref[...] = normed.astype(low)
        h2t_ref[...] = normed.T.astype(low)
        leaving.wait()


def norm_rows_kernel(x_ref, out_ref):
    normed, _ = first_norm(x_ref, None)
    out_ref[...] = normed.T.astype(low)


def norm_rows(rows):
    count, width = rows.shape
    return pl.pallas_call(
        norm_rows_kernel,
        in_specs=[pl.BlockSpec(memory_space=pltpu.VMEM)],
        out_specs=pl.BlockSpec(memory_space=pltpu.VMEM),
        out_shape=jax.ShapeDtypeStruct((width, count), low),
        compiler_params=pltpu.CompilerParams(vmem_limit_bytes=VMEM_BYTES),
        name="norm_rows",
    )(rows)


def mixer_forward(half, rows, weights, slot, gains=None, ending=None):
    count, width = rows.shape
    pairs = width // PAIR // 2
    by_pair = pl.BlockSpec((count, PAIR), lambda j, _: (0, j))
    struct = jax.ShapeDtypeStruct
    shape = lambda kind: struct((count, width // 2), kind)
    in_specs = [whole(rows.shape), pl.BlockSpec((width, 3 * PAIR), lambda j, _: (0, j))]
    operands = [half, rows, weights]
    out_specs = [by_pair] * 5
    out_shape = [shape(low), shape(wide), shape(wide), shape(low), shape(low)]
    scratch = [pltpu.VMEM((count, width), low)]
    if ending is None:
        kernel = mixer_forward_first_kernel
        in_specs += [whole(gains.shape)]
        operands += [gains]
        out_specs += [whole((8, width))]
        out_shape += [struct((8, width), wide)]
    if ending is not None:
        kernel = mixer_forward_last_kernel
        anywhere = pl.BlockSpec(memory_space=pl.ANY)
        in_specs += [whole(ending[0].shape), anywhere, anywhere, anywhere]
        operands += [ending[0], ending[1], weights, ending[2]]
        out_specs += [anywhere, whole((count, width)), whole((width, count))]
        out_shape += [
            struct((count, width), wide),
            struct((count, width), low),
            struct((width, count), low),
        ]
        scratch += [
            pltpu.VMEM((count, width), low),
            pltpu.VMEM((count, width), wide),
            pltpu.VMEM((width, width), low),
            pltpu.SemaphoreType.DMA((4,)),
        ]
    return pl.pallas_call(
        functools.partial(kernel, slot),
        grid_spec=pltpu.PrefetchScalarGridSpec(
            num_scalar_prefetch=1,
            grid=(pairs,),
            in_specs=in_specs,
            out_specs=out_specs,
            scratch_shapes=scratch,
        ),
        out_shape=out_shape,
        compiler_params=pltpu.CompilerParams(vmem_limit_bytes=VMEM_BYTES),
        cost_estimate=pl.CostEstimate(
            flops=count * width * 4 * width + 10 * count * slot * width,
            bytes_accessed=count * width * 12 + width * width * 4,
            transcendentals=count * width * 3,
        ),
        name="mixer_forward",
    )(*operands)


def store_down(out_ref, tile, owners):
    _, stride, down_rows = owners
    block = math.gcd(down_rows, tile.shape[0])
    first = pl.program_id(0) * (tile.shape[0] // block)
    for part in range(tile.shape[0] // block):
        owner = (first + part) // (down_rows // block)
        inside = (first + part) % (down_rows // block)
        start = pl.multiple_of(owner * stride + inside * block, block)
        out_ref[pl.ds(start, block), :] = tile[part * block : (part + 1) * block, :]


def ffn_kernel(
    owners,
    core_ref,
    h_ref,
    ht_ref,
    e_ref,
    wm_ref,
    wu_ref,
    wdm_ref,
    wdo_ref,
    x1_hbm,
    onm_hbm,
    ono_hbm,
    wom_hbm,
    woo_hbm,
    m_ref,
    g_ref,
    gm_ref,
    gu_ref,
    gdm_hbm,
    gdo_hbm,
    out_hbm,
    dx1_hbm,
    don_hbm,
    *scratch,
):
    gu_w, gu_g, down_g, down_w, mid_s, dh_s, on_s, x1_s, wo_s, out_s, gdm_s, gdo_s = scratch[:12]
    in_semaphores, out_semaphores, down_semaphores = scratch[12:]
    step, last = pl.program_id(0), pl.num_programs(0) - 1
    half, tile = wdm_ref.shape[1], wm_ref.shape[1]
    mine, other = lanes_of(core_ref[0], half), lanes_of(1 - core_ref[0], half)
    kind, kind_other = lanes_of(core_ref[0], tile), lanes_of(1 - core_ref[0], tile)
    count, stride, down_rows = owners

    width = on_s.shape[1]
    sources = (
        (x1_hbm, x1_s),
        (onm_hbm, on_s.at[:, mine]),
        (ono_hbm, on_s.at[:, other]),
        (wom_hbm.at[:, pl.ds(3 * half, half)], wo_s.at[:, mine]),
        (woo_hbm.at[:, pl.ds(3 * half, half)], wo_s.at[:, other]),
    )
    fetches = [
        pltpu.make_async_copy(source, target, in_semaphores.at[number])
        for number, (source, target) in enumerate(sources)
    ]

    def down_copies(owner):
        rows = pl.ds(pl.multiple_of(owner * stride, math.gcd(stride, 32)), down_rows)
        return [
            pltpu.make_async_copy(held.at[rows, :], out.at[rows, :], down_semaphores.at[side, owner])
            for side, (held, out) in enumerate(((gdm_s, gdm_hbm), (gdo_s, gdo_hbm)))
        ]

    @pl.when(step == 0)
    def _():
        dh_s[...] = jnp.zeros_like(dh_s)
        for fetch in fetches:
            fetch.start()

    gu_w[:, kind] = wm_ref[...]
    gu_w[:, kind_other] = wu_ref[...]
    hidden_rows = pl.ds(pl.multiple_of(step * tile, tile), tile)
    down_w[hidden_rows, mine] = wdm_ref[...]
    down_w[hidden_rows, other] = wdo_ref[...]
    pre = mm(h_ref[...], gu_w[...])
    a, b = pre[:, :tile], pre[:, tile:]
    share = sigmoid(a)
    swish = a * share
    mid = (swish * b).astype(low)
    mid_s[:, lanes_of(step, tile)] = mid
    d_mid = mm_nt(e_ref[...], down_w[hidden_rows, :])
    down_g[...] = mm_tn(mid, e_ref[...]).astype(low)
    d_a = (d_mid * b * (share + swish * (1.0 - share))).astype(low)
    d_b = (d_mid * swish).astype(low)
    d_pre = jnp.concatenate([d_a, d_b], axis=1)
    dh_s[...] += mm_nt(d_pre, gu_w[...])
    gu_g[...] = mm(ht_ref[...], d_pre).astype(low)
    blocks = tile // HEAD_DIM
    for side, block in enumerate((core_ref[1], 1 - core_ref[1])):
        gm_ref[side] = gu_g[:, lanes_of(core_ref[0] * blocks + block, HEAD_DIM)]
        gu_ref[side] = gu_g[:, lanes_of((1 - core_ref[0]) * blocks + block, HEAD_DIM)]
    store_down(gdm_s, down_g[:, mine], owners)
    store_down(gdo_s, down_g[:, other], owners)

    done = (step + 1) * tile // down_rows

    @pl.when(done > step * tile // down_rows)
    def _():
        for copy in down_copies(done - 1):
            copy.start()

    @pl.when(step == last)
    def _():
        for fetch in fetches:
            fetch.wait()
        x1 = x1_s[...]
        x2 = x1 + mm(mid_s[...], down_w[...])
        positions = lax.broadcasted_iota(jnp.int32, (out_s.shape[0] // m_ref.shape[0], 1), 0)
        for sequence in range(m_ref.shape[0]):
            rows = slice(sequence * positions.shape[0], (sequence + 1) * positions.shape[0])
            valid = (positions < m_ref[sequence]).astype(wide)
            out_s[rows, :] = (x2[rows, :] * valid).astype(low)
        leaving = [pltpu.make_async_copy(out_s, out_hbm, out_semaphores.at[0])]
        leaving[-1].start()
        scale = lax.rsqrt(jnp.mean(x1 * x1, axis=-1, keepdims=True) + 1e-06)
        normed = x1 * scale
        scaled = dh_s[...] * g_ref[2:3, :]
        d_x1 = e_ref[...].astype(wide) + scale * (
            scaled - normed * jnp.mean(scaled * normed, axis=-1, keepdims=True)
        )
        dh_s[...] = d_x1
        leaving.append(pltpu.make_async_copy(dh_s, dx1_hbm, out_semaphores.at[1]))
        leaving[-1].start()
        d_1 = mid_s.at[:, pl.ds(0, width)]
        d_1[...] = d_x1.astype(low)
        d_mixed = mid_s.at[:, pl.ds(width, width)]
        d_mixed[...] = mm_nt(d_1[...], wo_s[...]).astype(low)
        leaving.append(pltpu.make_async_copy(d_mixed, don_hbm, out_semaphores.at[2]))
        leaving[-1].start()
        rows = stride - down_rows
        grad_o = mm_tn(on_s[...], d_1[...]).astype(low)
        down_w[pl.ds(0, width), :] = grad_o
        for columns, held, out in ((mine, gdm_s, gdm_hbm), (other, gdo_s, gdo_hbm)):
            for owner in range(count):
                target = slice(owner * stride + down_rows, (owner + 1) * stride)
                held[target, :] = down_w[owner * rows : (owner + 1) * rows, columns]
                copy = pltpu.make_async_copy(
                    held.at[target, :], out.at[target, :], out_semaphores.at[len(leaving)]
                )
                copy.start()
                leaving.append(copy)
        for owner in range(count):
            leaving += down_copies(owner)
        for copy in leaving:
            copy.wait()


def ffn(core, h2, h2t, errors, w_gu, w_d, x1, mixed, w_a, lengths, gains8, owners):
    count, width = h2.shape
    half = width // 2
    hidden = w_gu[0].shape[1]
    full = whole((count, width))
    in_tile = pl.BlockSpec((width, TILE_F), lambda j, _: (0, j))
    out_tile = pl.BlockSpec((TILE_F, half), lambda j, _: (j, 0))
    grad_tile = pl.BlockSpec((2, width, HEAD_DIM), lambda j, _: (0, 0, j))
    anywhere = pl.BlockSpec(memory_space=pl.ANY)
    down_shape = (owners[0] * owners[1], half)
    struct = jax.ShapeDtypeStruct
    vmem = pltpu.VMEM
    return pl.pallas_call(
        functools.partial(ffn_kernel, owners),
        grid_spec=pltpu.PrefetchScalarGridSpec(
            num_scalar_prefetch=1,
            grid=(hidden // TILE_F,),
            in_specs=[full, whole(h2t.shape), full, in_tile, in_tile, out_tile, out_tile]
            + [anywhere] * 5
            + [pl.BlockSpec(memory_space=pltpu.SMEM), whole((8, width))],
            out_specs=[grad_tile, grad_tile] + [anywhere] * 5,
            scratch_shapes=[
                vmem((width, 2 * TILE_F), low),
                vmem((width, 2 * TILE_F), low),
                vmem((TILE_F, width), low),
                vmem((hidden, width), low),
                vmem((count, hidden), low),
                vmem((count, width), wide),
                vmem((count, width), low),
                vmem((count, width), wide),
                vmem((width, width), low),
                vmem((count, width), low),
                vmem(down_shape, low),
                vmem(down_shape, low),
                pltpu.SemaphoreType.DMA((5,)),
                pltpu.SemaphoreType.DMA((3 + 2 * owners[0],)),
                pltpu.SemaphoreType.DMA((2, owners[0])),
            ],
        ),
        out_shape=[struct((2, width, hidden // 2), low)] * 2
        + [struct(down_shape, low)] * 2
        + [
            struct((count, width), low),
            struct((count, width), wide),
            struct((count, width), low),
        ],
        compiler_params=pltpu.CompilerParams(vmem_limit_bytes=VMEM_BYTES),
        cost_estimate=pl.CostEstimate(
            flops=18 * count * width * hidden,
            bytes_accessed=count * width * 20 + width * hidden * 12,
            transcendentals=count * hidden,
        ),
        name="ffn",
    )(core, h2, h2t, errors, *w_gu, *w_d, x1, *mixed, *w_a, lengths, gains8)


def mixer_backward_kernel(
    slot,
    per_half,
    first,
    half_ref,
    nt_hbm,
    g_ref,
    q_ref,
    f_ref,
    v_ref,
    o_ref,
    don_ref,
    *outs,
):
    grad_ref, dpre_hbm, nt_s, dpre_ref, semaphores = outs[-5:]
    fetch = pltpu.make_async_copy(nt_hbm, nt_s, semaphores.at[0])
    fetch.start()
    gain_o = g_ref[1:2, lanes_of(half_ref[0] * per_half + first + pl.program_id(0), PAIR)]
    lower_ones = triangle(slot, True)
    upper_ones = triangle(slot, False)
    causal_t = causal_mask(slot, False)
    for sequence in range(q_ref.shape[0] // slot):
        rows = slice(sequence * slot, (sequence + 1) * slot)
        d_on = don_ref[rows, :].astype(wide)
        out = o_ref[rows, :].astype(wide)
        d_out_parts = []
        for head in range(2):
            lanes = slice(head * HEAD_DIM, (head + 1) * HEAD_DIM)
            out_h, d_on_h = out[:, lanes], d_on[:, lanes]
            scale = lax.rsqrt(jnp.mean(out_h * out_h, axis=-1, keepdims=True) + 1e-05)
            normed = out_h * scale
            scaled = d_on_h * gain_o[:, lanes]
            inner = jnp.mean(scaled * normed, axis=-1, keepdims=True)
            d_out_parts.append((scale * (scaled - normed * inner)).astype(low))

        q_pre = q_ref[rows, :]
        share, gate, keys_in, cumulative = decay_parts(f_ref[rows, :], lower_ones)
        grown = jnp.exp(-cumulative)
        shrunk = jnp.exp(cumulative)
        q_share = sigmoid(q_pre)
        decayed_q = (q_pre * q_share * shrunk).astype(low)
        grown_k = (keys_in * grown).astype(low)
        values = v_ref[rows, :]
        dq_parts, dk_parts, dv_parts = [], [], []
        for head in range(2):
            lanes = slice(head * HEAD_DIM, (head + 1) * HEAD_DIM)
            q_h, k_h, v_h = decayed_q[:, lanes], grown_k[:, lanes], values[:, lanes]
            d_out = d_out_parts[head]
            scores = jnp.where(causal_t, mm_nt(k_h, q_h), 0.0).astype(low)
            d_scores = jnp.where(causal_t, mm_nt(v_h, d_out), 0.0).astype(low)
            dv_parts.append(mm(scores, d_out))
            dk_parts.append(mm(d_scores, q_h))
            dq_parts.append(mm_tn(d_scores, k_h))
        d_decayed = jnp.concatenate(dq_parts, axis=1)
        d_grown = jnp.concatenate(dk_parts, axis=1)
        d_value = jnp.concatenate(dv_parts, axis=1)
        d_cumulative = decayed_q.astype(wide) * d_decayed - grown_k.astype(wide) * d_grown
        d_log = split_sum(upper_ones, d_cumulative)
        d_query = d_decayed * shrunk
        d_key = d_grown * grown
        d_q_pre = d_query * q_share * (1.0 + q_pre * (1.0 - q_share))
        d_f_pre = (1.0 - lower_bound) * (d_log / gate - d_key) * share * (1.0 - share)
        dpre_ref[rows, :PAIR] = d_q_pre.astype(low)
        dpre_ref[rows, PAIR : 2 * PAIR] = d_f_pre.astype(low)
        dpre_ref[rows, 2 * PAIR :] = d_value.astype(low)

    columns = pl.ds(first * 3 * PAIR, 3 * PAIR)
    leaving = pltpu.make_async_copy(dpre_ref, dpre_hbm.at[:, columns], semaphores.at[1])
    leaving.start()
    fetch.wait()
    gain_column = g_ref[...].T[:, 0:1]
    grad = (mm(nt_s[...], dpre_ref[...]) * gain_column).astype(low)
    grad_ref[...] = grad.reshape(grad_ref.shape)
    leaving.wait()


def mixer_backward(half, n1t, gains8, kept, d_mixed, slot, shard, pairs=(0, 1), before=()):
    width, count = n1t.shape
    per_half = width // PAIR // 2
    first = pairs[0]
    by_pair = pl.BlockSpec((count, PAIR), lambda j, _: (0, first + j))
    from_whole = pl.BlockSpec((count, PAIR), lambda j, half: (0, half[0] * per_half + first + j))
    struct = jax.ShapeDtypeStruct
    return pl.pallas_call(
        functools.partial(mixer_backward_kernel, slot, per_half, first),
        grid_spec=pltpu.PrefetchScalarGridSpec(
            num_scalar_prefetch=1,
            grid=(len(pairs),),
            in_specs=[pl.BlockSpec(memory_space=pl.ANY), whole(gains8.shape)]
            + [by_pair] * 4
            + [from_whole]
            + [pl.BlockSpec(memory_space=pl.ANY)] * len(before),
            out_specs=[
                pl.BlockSpec(
                    (width // shard, 1, shard, 3 * PAIR), lambda j, _: (0, first + j, 0, 0)
                ),
                pl.BlockSpec(memory_space=pl.ANY),
            ],
            scratch_shapes=[
                pltpu.VMEM((width, count), low),
                pltpu.VMEM((count, 3 * PAIR), low),
                pltpu.SemaphoreType.DMA((2,)),
            ],
        ),
        out_shape=[
            struct((width // shard, per_half, shard, 3 * PAIR), low),
            struct((count, per_half * 3 * PAIR), low),
        ],
        input_output_aliases={8 + k: k for k in range(len(before))},
        compiler_params=pltpu.CompilerParams(vmem_limit_bytes=VMEM_BYTES),
        cost_estimate=pl.CostEstimate(
            flops=len(pairs) * (count * width * 6 * PAIR + 20 * count * slot * PAIR),
            bytes_accessed=len(pairs) * (count * width * 5 + width * PAIR * 6),
            transcendentals=len(pairs) * count * PAIR * 6,
        ),
        name="mixer_backward",
    )(half, n1t, gains8, *kept, d_mixed, *before)


def input_gradient_rows_kernel(
    x_ref, g_ref, dm_ref, do_ref, wm_ref, wo_ref, dx1_ref, dx_ref
):
    d_h1 = mm_nt(dm_ref[...], wm_ref[...]) + mm_nt(do_ref[...], wo_ref[...])
    normed, scale = first_norm(x_ref, None)
    scaled = d_h1 * g_ref[0:1, :]
    dx_ref[...] = dx1_ref[...] + scale * (
        scaled - normed * jnp.mean(scaled * normed, axis=-1, keepdims=True)
    )


def input_gradient(rows, gains8, d_pre, weights, d_x1):
    count, width = rows.shape
    block = count // 2
    columns = d_pre[0].shape[1]
    by_rows = lambda columns: pl.BlockSpec((block, columns), lambda j: (j, 0))
    weight_spec = pl.BlockSpec((width, columns), lambda j: (0, 0), pipeline_mode=pl.Buffered(1))
    return pl.pallas_call(
        input_gradient_rows_kernel,
        grid=(count // block,),
        in_specs=[by_rows(width), whole(gains8.shape)]
        + [by_rows(columns)] * 2
        + [weight_spec] * 2
        + [by_rows(width)],
        out_specs=by_rows(width),
        out_shape=jax.ShapeDtypeStruct((count, width), wide),
        compiler_params=pltpu.CompilerParams(vmem_limit_bytes=VMEM_BYTES),
        cost_estimate=pl.CostEstimate(
            flops=6 * count * width * width,
            bytes_accessed=count * width * 16 + width * width * 6,
            transcendentals=0,
        ),
        name="input_gradient",
    )(rows, gains8, *d_pre, *weights, d_x1)


def update(weight, momentum, average, gradient, step_rate):
    new_momentum = momentum_decay * momentum + gradient
    direction = gradient + momentum_decay * new_momentum + weight_decay * weight
    new_weight = weight - step_rate * direction
    new_average = average_decay * average + (1.0 - average_decay) * new_weight
    return (new_momentum, new_average, new_weight)


def update_kernel(pick, step_rate, sum_count, core_ref, w_ref, m_ref, a_ref, *refs):
    sums, outs, dots_ref = refs[:sum_count], refs[-4:-1], refs[-1]
    weight = w_ref[...]
    gradient = pick(core_ref[0], *[s[...] for s in sums]).astype(wide).reshape(weight.shape)
    results = update(weight, m_ref[...], a_ref[...], gradient, step_rate)
    for out, result in zip(outs, results):
        out[...] = result
    product = weight.astype(low).astype(wide) * gradient
    total = product[..., :HEAD_DIM]
    for start in range(HEAD_DIM, product.shape[-1], HEAD_DIM):
        total = total + product[..., start : start + HEAD_DIM]
    dots_ref[...] = total.reshape(dots_ref.shape)


def update_call(
    core, state, sums, grid, state_spec, sum_specs, pick, step_rate, name, before=()
):
    struct = jax.ShapeDtypeStruct(state[0].shape, wide)
    size = math.prod(state[0].shape)
    rows = state_spec.block_shape[-2]
    steps = math.prod(grid)
    tail = grid[1:]

    def dots_index(*indices):
        place = indices[0]
        for length, index in zip(tail, indices[1:]):
            place = place * length + index
        return (place, 0, 0)

    return pl.pallas_call(
        functools.partial(update_kernel, pick, step_rate, len(sums)),
        grid_spec=pltpu.PrefetchScalarGridSpec(
            num_scalar_prefetch=1,
            grid=grid,
            in_specs=[state_spec] * 3
            + sum_specs
            + [pl.BlockSpec(memory_space=pl.ANY)] * len(before),
            out_specs=[state_spec] * 3 + [pl.BlockSpec((1, rows, HEAD_DIM), dots_index)],
        ),
        out_shape=[struct] * 3 + [jax.ShapeDtypeStruct((steps, rows, HEAD_DIM), wide)],
        input_output_aliases={4 + len(sums) + k: k for k in range(len(before))},
        compiler_params=pltpu.CompilerParams(vmem_limit_bytes=VMEM_BYTES),
        cost_estimate=pl.CostEstimate(flops=12 * size, bytes_accessed=26 * size, transcendentals=0),
        name=name,
    )(core, *state, *sums, *before)


def update_attention_kernel(
    pick, step_rate, gain_step, core_ref, w_ref, m_ref, a_ref, qfv_ref, out_ref, *refs
):
    if gain_step is None:
        update_kernel(pick, step_rate, 2, core_ref, w_ref, m_ref, a_ref, qfv_ref, out_ref, *refs)
        return
    *held, dots_s = refs
    own_dots, up_dots, gate_dots, g_ref, gm_ref, ga_ref = held[:6]
    outs, gain_outs = held[-6:-3], held[-3:]
    kind = pl.program_id(0)
    dots = dots_s.at[kind]
    update_kernel(
        pick, step_rate, 2, core_ref, w_ref, m_ref, a_ref, qfv_ref, out_ref, *outs, dots
    )

    @pl.when(kind == pl.num_programs(0) - 1)
    def _():
        shard = dots_s.shape[1]
        sums = [own_dots[k] + dots_s[k] for k in range(4)]
        two = (up_dots[...] + gate_dots[...]).reshape(shard, HEAD_DIM)
        columns = [
            jnp.sum(total, axis=1, keepdims=True) for total in (sums[0] + sums[1] + sums[2], sums[3], two)
        ]
        lanes = lax.broadcasted_iota(jnp.int32, (shard, HEAD_DIM), 1)
        table = jnp.where(lanes == 1, columns[1], columns[2])
        table = jnp.where(lanes == 0, columns[0], table)
        gain = g_ref[...]
        gradient = table.T[:3, :] / gain.astype(low).astype(wide)
        results = update(gain, gm_ref[...], ga_ref[...], gradient, gain_step)
        for out, result in zip(gain_outs, results):
            out[...] = result


def update_attention(half_ref, state, qfv, out, step_rate, gains=None):
    _, shard, width = state[0].shape
    down_rows = out.shape[0] - shard

    def pick(core_index, proj, last):
        gradient = last[down_rows:].astype(wide)
        for kind in range(3):
            parts = [proj[pair * shard :, kind * PAIR :][:shard, :PAIR] for pair in range(2)]
            chosen = jnp.concatenate(parts, axis=1).astype(wide)
            gradient = jnp.where(pl.program_id(0) == kind, chosen, gradient)
        return gradient

    struct = jax.ShapeDtypeStruct
    state_spec = pl.BlockSpec((1, shard, width // 2), lambda kind, half: (kind, 0, half[0]))
    in_specs = [state_spec] * 3 + [whole(qfv.shape), whole(out.shape)]
    out_specs = [state_spec] * 3
    out_shape = [struct(state[0].shape, wide)] * 3
    operands = [half_ref, *state, qfv, out]
    aliases, scratch, gain_step = {}, [], None
    if gains is None:
        out_specs += [pl.BlockSpec((1, shard, HEAD_DIM), lambda kind, half: (kind, 0, 0))]
        out_shape += [struct((4, shard, HEAD_DIM), wide)]
    else:
        before, dots, gain_state, gain_step = gains
        in_specs += [whole(part.shape) for part in (*dots, *gain_state)]
        operands += [*dots, *gain_state]
        aliases = {len(operands) + k: k for k in range(3)}
        in_specs += [pl.BlockSpec(memory_space=pl.ANY)] * 3
        operands += list(before)
        out_specs += [whole(gain_state[0].shape)] * 3
        out_shape += [struct(gain_state[0].shape, wide)] * 3
        scratch = [pltpu.VMEM((4, shard, HEAD_DIM), wide)]
    size = math.prod(state[0].shape) // 2
    return pl.pallas_call(
        functools.partial(update_attention_kernel, pick, step_rate, gain_step),
        grid_spec=pltpu.PrefetchScalarGridSpec(
            num_scalar_prefetch=1,
            grid=(4,),
            in_specs=in_specs,
            out_specs=out_specs,
            scratch_shapes=scratch,
        ),
        out_shape=out_shape,
        input_output_aliases=aliases,
        compiler_params=pltpu.CompilerParams(vmem_limit_bytes=VMEM_BYTES),
        cost_estimate=pl.CostEstimate(flops=12 * size, bytes_accessed=26 * size, transcendentals=0),
        name="update_attention",
    )(*operands)


def update_ffn_in(kind_ref, state, totals, step_rate, before):
    _, shard, hidden = state[0].shape
    block = shard // 2

    def pick(_, even, odd):
        blocks = []
        for start in range(0, hidden // 2, HEAD_DIM):
            blocks += [even[:, start : start + HEAD_DIM], odd[:, start : start + HEAD_DIM]]
        return jnp.concatenate(blocks, axis=1)

    return update_call(
        kind_ref,
        state,
        totals,
        (2,),
        pl.BlockSpec((1, block, hidden), lambda j, kind: (kind[0], j, 0)),
        [pl.BlockSpec((block, hidden // 2), lambda j, _: (j, 0))] * 2,
        pick,
        step_rate,
        "update_ffn_in",
        before,
    )


def update_ffn_out(core, state, sums, step_rate):
    shard, width = state[0].shape

    def pick(core_index, mine, other):
        own = pl.program_id(0) == core_index
        return jnp.where(own, mine[:shard].astype(wide), other[:shard].astype(wide))

    return update_call(
        core,
        state,
        sums,
        (2,),
        pl.BlockSpec((shard, width // 2), lambda j, _: (0, j)),
        [whole(total.shape) for total in sums],
        pick,
        step_rate,
        "update_ffn_out",
    )


def pack_kernel(core_ref, w_ref, out_ref):
    half = w_ref.shape[2]
    for pair in range(half // PAIR):
        for kind in range(3):
            start = (pair * 3 + kind) * PAIR
            piece = w_ref[kind, :, pair * PAIR : (pair + 1) * PAIR]
            out_ref[:, start : start + PAIR] = piece.astype(low)
    out_ref[:, 3 * half : 4 * half] = w_ref[3].astype(low)


def pack_attention(core, weights):
    _, shard, width = weights.shape
    half = width // 2
    return pl.pallas_call(
        pack_kernel,
        grid_spec=pltpu.PrefetchScalarGridSpec(
            num_scalar_prefetch=1,
            grid=(1,),
            in_specs=[pl.BlockSpec((4, shard, half), lambda j, core: (0, 0, core[0]))],
            out_specs=whole((shard, 4 * half)),
        ),
        out_shape=jax.ShapeDtypeStruct((shard, 4 * half), low),
        name="pack_attention",
    )(core, weights)


RING = 8


def ring_place(index):
    return jnp.where(index % 2 == 0, index // 2, RING - 1 - index // 2)


def ring_member(place):
    place = place % RING
    return jnp.where(place < RING // 2, 2 * place, 2 * RING - 1 - 2 * place)


CYCLE = (0, 2, 4, 6, 7, 5, 3, 1)


def ring_next(tensor):
    replicas = lax.axis_size("dp")
    pairs = []
    for place_of, member in enumerate(CYCLE):
        for replica in range(replicas):
            target = CYCLE[(place_of + (1 if replica % 2 == 0 else -1)) % RING]
            pairs.append((member * replicas + replica, target * replicas + replica))
    return lax.ppermute(tensor, ("fsdp", "dp"), pairs)


def ring_shift(tensor, way):
    pairs = [(member, CYCLE[(at + way) % RING]) for at, member in enumerate(CYCLE)]
    return lax.ppermute(tensor, "fsdp", pairs)


def core_swap(tensor):
    return lax.ppermute(tensor, "dp", [(d, d ^ 1) for d in range(lax.axis_size("dp"))])


def column_swap(tensor):
    return lax.ppermute(tensor, "dp", [(d, d ^ 2) for d in range(lax.axis_size("dp"))])


def pack_all_kernel(
    core_ref, column_ref, w_ref, up_ref, other_ref, down_ref, g_ref, out_ref, across_ref
):
    across_ref[...] = other_ref[0].astype(low)
    shard = w_ref.shape[1]
    half = w_ref.shape[2]
    for pair in range(half // PAIR):
        for kind in range(3):
            start = (pair * 3 + kind) * PAIR
            piece = w_ref[kind, :, pair * PAIR : (pair + 1) * PAIR]
            out_ref[:, start : start + PAIR] = piece.astype(low)
    out_ref[:, 3 * half : 4 * half] = w_ref[3].astype(low)
    start = 4 * half
    out_ref[:, start : start + up_ref.shape[2]] = up_ref[0].astype(low)
    start += up_ref.shape[2]
    for first, count in down_parts(down_ref.shape[0], shard):
        out_ref[:count, start : start + half] = down_ref[first : first + count, :].astype(low)
        if count < shard:
            out_ref[count:, start : start + half] = jnp.zeros((shard - count, half), low)
            rows = lax.broadcasted_iota(jnp.int32, (GAIN_ROWS, g_ref.shape[1]), 0)
            gains = jnp.where(rows == 1, g_ref[1:2, :], g_ref[2:3, :])
            gains = jnp.where(rows == 0, g_ref[0:1, :], gains)
            gains = jnp.where(rows < 3, gains, 0.0).astype(low)
            out_ref[count : count + GAIN_ROWS, start : start + g_ref.shape[1]] = gains
        start += half


def down_parts(down_rows, shard):
    return [(start, min(shard, down_rows - start)) for start in range(0, down_rows, shard)]


def pack_all(core, column, weights, up, down, gains):
    _, shard, width = weights.shape
    half = width // 2
    parts = len(down_parts(down.shape[0], shard))
    columns = 4 * half + up.shape[2] // 2 + parts * half
    return pl.pallas_call(
        pack_all_kernel,
        grid_spec=pltpu.PrefetchScalarGridSpec(
            num_scalar_prefetch=2,
            grid=(1,),
            in_specs=[
                pl.BlockSpec((4, shard, half), lambda j, core, column: (0, 0, core[0])),
                pl.BlockSpec(
                    (1, shard, up.shape[2] // 2), lambda j, core, column: (core[0], 0, column[0])
                ),
                pl.BlockSpec(
                    (1, shard, up.shape[2] // 2),
                    lambda j, core, column: (core[0], 0, 1 - column[0]),
                ),
                pl.BlockSpec((down.shape[0], half), lambda j, core, column: (0, core[0])),
                whole(gains.shape),
            ],
            out_specs=[whole((shard, columns)), whole((shard, up.shape[2] // 2))],
        ),
        out_shape=[
            jax.ShapeDtypeStruct((shard, columns), low),
            jax.ShapeDtypeStruct((shard, up.shape[2] // 2), low),
        ],
        compiler_params=pltpu.CompilerParams(vmem_limit_bytes=VMEM_BYTES),
        name="pack_all",
    )(core, column, weights, up, up, down, gains)


def place_kernel(which, kept, shapes, origin_ref, column_ref, *refs):
    pieces, outs, semaphores = refs[: len(which)], refs[-1 - len(kept) : -1], refs[-1]
    targets = dict(zip(kept, outs))
    shard, first, up_columns, down_rows, half = shapes
    copies = []

    def copy(source, target):
        copies.append(pltpu.make_async_copy(source, target, semaphores.at[len(copies)]))

    for piece, (origin, across) in zip(pieces, which):
        owner = origin_ref[origin]
        rows = pl.ds(pl.multiple_of(owner * shard, 16), shard)
        if across:
            copy(piece, targets[1].at[rows, lanes_of(1 - column_ref[0], up_columns)])
            continue
        copy(piece.at[:, pl.ds(0, first)], targets[0].at[rows, :])
        own = targets[1].at[rows, lanes_of(column_ref[0], up_columns)]
        copy(piece.at[:, pl.ds(first, up_columns)], own)
        lane = first + up_columns
        for start, count in down_parts(down_rows, shard):
            target = pl.ds(pl.multiple_of(owner * down_rows + start, 16), count)
            copy(piece.at[pl.ds(0, count), pl.ds(lane, half)], targets[2].at[target, :])
            if count < shard:
                source = piece.at[pl.ds(count, GAIN_ROWS), pl.ds(lane, shard)]
                copy(source, targets[3].at[:, lanes_of(owner, shard)])
            lane += half
    for one in copies:
        one.start()
    for one in copies:
        one.wait()


def place(origins, column, which, pieces, arrays, kept, shapes):
    anywhere = pl.BlockSpec(memory_space=pl.ANY)
    shard, first, up_columns, down_rows, half = shapes
    kinds = [(RING * shard, first), (RING * shard, 2 * up_columns), (RING * down_rows, half)]
    kinds.append((GAIN_ROWS, RING * shard))
    held = [] if arrays is None else list(arrays)
    size = sum(math.prod(piece.shape) for piece in pieces)
    before = 2 + len(pieces)
    return pl.pallas_call(
        functools.partial(place_kernel, which, kept, shapes),
        grid_spec=pltpu.PrefetchScalarGridSpec(
            num_scalar_prefetch=2,
            grid=(1,),
            in_specs=[whole(piece.shape) for piece in pieces] + [anywhere] * len(held),
            out_specs=[anywhere] * len(kept),
            scratch_shapes=[pltpu.SemaphoreType.DMA((8 * len(pieces),))],
        ),
        out_shape=[jax.ShapeDtypeStruct(kinds[k], pieces[0].dtype) for k in kept],
        input_output_aliases={before + k: k for k in range(len(held))},
        compiler_params=pltpu.CompilerParams(vmem_limit_bytes=VMEM_BYTES),
        cost_estimate=pl.CostEstimate(flops=0, bytes_accessed=8 * size, transcendentals=0),
        name="place",
    )(origins, column, *pieces, *held)


def after(tensor, *others):
    return lax.optimization_barrier((tensor, *others))[0]


def core_way():
    return 1 - 2 * (lax.axis_index("dp") % 2)


def ring_origins():
    steps = jnp.array((0, -1, -2, -3, -4, 1, 2, 3), jnp.int32)
    return ring_member(ring_place(lax.axis_index("fsdp")) + steps + RING).astype(jnp.int32)


class RingSumOverColumns:
    def __init__(self, mine, arrived):
        self.arrays = (mine, arrived)
        place = ring_place(lax.axis_index("fsdp"))
        self.rows = mine.shape[1] // RING
        self.starts = [
            ring_member(place - core_way() * (s + 1) + 2 * RING) * self.rows for s in range(RING)
        ]
        self.sent, self.came, self.totals = [], [], []

    def part(self, side, step):
        shape = (1, self.rows, self.arrays[0].shape[2])
        parts = [
            lax.dynamic_slice(array, (side, self.starts[step], 0), shape)[0]
            for array in self.arrays
        ]
        return parts[0].astype(wide) + parts[1].astype(wide)

    def cross(self):
        self.sent.append(self.part(1, len(self.sent)).astype(low))
        self.came.append(column_swap(self.sent[-1]))

    def term(self):
        step = len(self.totals)
        return self.part(0, step) + self.came[step].astype(wide)

    def begin(self, *others):
        self.came[0] = after(self.came[0], *others) if others else self.came[0]
        self.totals.append(self.term().astype(low))

    def step(self, arriving=()):
        total, ahead = self.totals[-1], self.came[len(self.totals)]
        moved = ring_next(after(total, ahead) if len(self.totals) > 1 else total)
        moved = after(moved, *arriving) if arriving else moved
        self.totals.append((moved.astype(wide) + self.term()).astype(low))

    def last(self):
        return self.totals[-1]


class RingSum:
    def __init__(self, mine, arrived):
        self.mine, self.arrived = mine, arrived
        place = ring_place(lax.axis_index("fsdp"))
        self.owners = [ring_member(place - core_way() * (s + 1) + 2 * RING) for s in range(RING)]
        self.totals = []

    def term(self):
        parts = []
        for own, arrived in zip(self.mine, self.arrived):
            rows = own.shape[0] // RING
            start = self.owners[len(self.totals)] * rows
            part = lax.dynamic_slice_in_dim(own, start, rows, 0).astype(wide)
            parts.append(part + lax.dynamic_slice_in_dim(arrived, start, rows, 0).astype(wide))
        return parts[0] if len(parts) == 1 else jnp.concatenate(parts, axis=0)

    def begin(self, *others):
        if others:
            self.mine = [after(self.mine[0], *others), *self.mine[1:]]
        self.totals.append(self.term().astype(low))

    def step(self, *before, arriving=()):
        total = self.totals[-1]
        moved = ring_next(after(total, *before) if before else total)
        moved = after(moved, *arriving) if arriving else moved
        self.totals.append((moved.astype(wide) + self.term().astype(wide)).astype(low))

    def last(self):
        return self.totals[-1]


def gather_rows(shard):
    mine = lax.all_gather(shard, "fsdp", axis=0, tiled=True)
    return mine, core_swap(mine)


def core_sum(mine, other):
    return (mine.astype(wide) + core_swap(other).astype(wide)).astype(low)


def scatter_rows(both):
    return lax.psum_scatter(both, "fsdp", scatter_dimension=0, tiled=True)


def over_columns(total):
    total = (total.astype(wide) + column_swap(total).astype(wide)).astype(low)
    return total, core_swap(total)


def on_device(
    inputs,
    cotangent,
    lengths,
    attention_weights,
    attention_momentum,
    attention_average,
    ffn_inputs,
    ffn_inputs_momentum,
    ffn_inputs_average,
    ffn_output,
    ffn_output_momentum,
    ffn_output_average,
    gains,
    gains_momentum,
    gains_average,
):
    micro_count, slot, width = inputs.shape
    hidden = ffn_inputs.shape[2]
    shard, down_rows = ffn_inputs.shape[1], ffn_output.shape[0]
    fsdp_size = lax.axis_size("fsdp")
    replicas = lax.axis_size("dp")
    ringed = fsdp_size == RING
    core = lax.axis_index("dp") % 2
    column = lax.axis_index("dp") // 2
    count = micro_count * slot
    half = width // 2
    core_ref = core.astype(jnp.int32).reshape(1)
    other_ref = 1 - core_ref
    column_ref = column.astype(jnp.int32).reshape(1)
    is_first = core == 0

    rows = inputs.reshape(count, width)
    n1t = norm_rows(rows)
    positions = jnp.arange(slot, dtype=jnp.int32)
    valid = (positions[None, :] < lengths).astype(wide).reshape(count, 1)
    errors = (cotangent.reshape(count, width).astype(wide) * valid).astype(low)

    if ringed:
        origins = ring_origins()
        first = 4 * half
        shapes = (shard, first, hidden // 2, down_rows, half)
        packed, own_across = pack_all(
            core_ref, column_ref, attention_weights, ffn_inputs, ffn_output, gains
        )
        wholes, there, which_there = None, [own_across], [(0, True)]
        here, which = [packed], [(0, False)]
        for step in range(1, 6):
            if step <= 3:
                onward = [ring_shift(here[0], 1), ring_shift(here[-1], -1)]
            elif step == 4:
                onward = [ring_next(jnp.where(is_first, *here))]
            across = []
            if step > 1:
                across = [column_swap(piece[:, first : first + hidden // 2]) for piece in here]
            wholes = place(
                origins, column_ref, which + which_there, here + there, wholes, (0, 1, 2, 3), shapes
            )
            if step == 5:
                break
            extra = [errors, n1t] if step == 2 else []
            tied = list(lax.optimization_barrier((*onward, *across, *wholes, *extra)))
            here, rest = tied[: len(onward)], tied[len(onward) :]
            there, wholes = rest[: len(across)], rest[len(across) : len(across) + 4]
            which_there = [(origin, True) for origin, _ in which] if across else []
            which = [(origin, False) for origin in [step, step + 4][: len(onward)]]
        w_a, gain_rows = (wholes[0], core_swap(wholes[0])), wholes[3]
    else:
        w_a = gather_rows(pack_attention(core_ref, attention_weights))
        gain_rows = lax.all_gather(gains.astype(low), "fsdp", axis=1, tiled=True)
        gain_rows = jnp.pad(gain_rows, ((0, GAIN_ROWS - 3), (0, 0)))
        w_gu = gather_rows(
            lax.dynamic_index_in_dim(ffn_inputs, core, 0, keepdims=False).astype(low)
        )
        w_d = gather_rows(lax.dynamic_slice_in_dim(ffn_output, core * half, half, 1).astype(low))
    mixed_mine, *kept_mine, gains8 = mixer_forward(core_ref, rows, w_a[0], slot, gain_rows)
    if ringed:
        (across,) = lax.optimization_barrier((*across, mixed_mine, w_a[1]))[:1]
        (w_gu_mine,) = place(origins, column_ref, [(4, True)], [across], [wholes[1]], (1,), shapes)
        wholes = [wholes[0], w_gu_mine, wholes[2], wholes[3]]
        rows = after(rows, *wholes[1:3])
        w_gu, w_d = [(array, core_swap(array)) for array in wholes[1:3]]
    mixed_other, *rest = mixer_forward(
        other_ref, rows, w_a[1], slot, None, (gains8, mixed_mine, w_a[0])
    )
    kept_other, (x1, h2, h2t) = rest[:4], rest[4:]
    owners = (RING, down_rows + shard, down_rows)
    if not ringed:
        owners = (1, hidden + width, hidden)
    places = jnp.concatenate([core_ref, column_ref])
    *grad_gu, gd_mine, gd_other, output, d_x1, d_mixed = ffn(
        places, h2, h2t, errors, w_gu, w_d, x1, (mixed_mine, mixed_other), w_a, lengths[:, 0], gains8, owners
    )

    gm, gu = grad_gu
    arrived_gu = core_swap(gu)
    mine_do, arrived_do = [gd_mine], [core_swap(gd_other)]
    by_owner = (fsdp_size * 2 * shard, 3 * PAIR)
    d_pre = []
    for call in range(4):
        from_half, kept = (other_ref, kept_other) if call < 2 else (core_ref, kept_mine)
        if ringed and call == 1:
            sum_gu = RingSumOverColumns(after(gm, d_pre[0]), arrived_gu)
            sum_gu.cross()
            sum_gu.cross()
            n1t = after(n1t, *sum_gu.sent)
        elif ringed and call > 1:
            sum_gu.cross()
            ahead = [sum_gu.came[2]] if call == 3 else []
            n1t = after(n1t, sum_gu.last(), sum_do.last(), sum_gu.sent[-1], *ahead)
        grads = mixer_backward(
            from_half,
            n1t,
            gains8,
            kept,
            d_mixed,
            slot,
            shard,
            (call % 2,),
            grads if call % 2 else (),
        )
        d_pre.append(grads[1])
        if call == 1:
            grad_other = grads[0]
            if ringed:
                sum_do = RingSum(mine_do, arrived_do)
                sum_do.begin(d_pre[-1])
                sum_gu.begin(d_pre[-1])
                grad_other = after(grad_other, sum_gu.last(), sum_do.last())
            arrived_qfv = [core_swap(grad_other.reshape(by_owner))]
        elif ringed and call > 1:
            sum_do.step(arriving=(d_pre[-1],))
            sum_gu.step(arriving=(d_pre[-1],))
    mine_qfv = [grads[0].reshape(by_owner)]

    def finish_input(*others):
        late = after(d_pre[3], *others) if others else d_pre[3]
        return input_gradient(rows, gains8, (late, d_pre[1]), w_a, d_x1)

    if ringed:
        sum_qfv = RingSum(mine_qfv, arrived_qfv)
        sum_qfv.begin()
        input_grad = None
        for step in range(1, RING - 1):
            if len(sum_gu.came) < RING:
                sum_gu.cross()
            if len(sum_gu.totals) < RING:
                first = [sum_gu.last(), sum_qfv.last()]
                sum_do.step(*{1: first, 4: [input_grad]}.get(step, []))
                sum_gu.step()
            sum_qfv.step()
            if step == 2:
                input_grad = finish_input(sum_qfv.last(), sum_gu.came[5])
        total_gu, total_do = sum_gu.last(), sum_do.last()
    else:
        both = (gm.astype(wide) + arrived_gu.astype(wide)).astype(low)
        here = (both[0].astype(wide) + column_swap(both[1]).astype(wide)).astype(low)
        total_gu = scatter_rows(here)
        both = (gd_mine.astype(wide) + arrived_do[0].astype(wide)).astype(low)
        total_do = jnp.concatenate(
            [scatter_rows(both[:hidden]), scatter_rows(both[hidden:])], axis=0
        )
        total_qfv = scatter_rows(
            (mine_qfv[0].astype(wide) + arrived_qfv[0].astype(wide)).astype(low)
        )
        input_grad = finish_input()
    scale_rows = 1.0 / math.sqrt(count * fsdp_size * replicas)
    matrix_step = matrix_rate * scale_rows
    attention_state = (attention_weights, attention_momentum, attention_average)
    ffn_in_state = (ffn_inputs, ffn_inputs_momentum, ffn_inputs_average)
    ffn_out_state = (ffn_output, ffn_output_momentum, ffn_output_average)
    sum_do = over_columns(total_do)
    there = column_swap(total_gu)
    even = jnp.where(column == 0, total_gu, there)
    odd = jnp.where(column == 0, there, total_gu)
    sum_gu = (even, odd), (core_swap(even), core_swap(odd))
    *new_out, _ = update_ffn_out(core_ref, ffn_out_state, sum_do, matrix_step)
    *new_in, dots_up = update_ffn_in(core_ref, ffn_in_state, sum_gu[0], matrix_step, ())
    *new_in, dots_gate = update_ffn_in(other_ref, ffn_in_state, sum_gu[1], matrix_step, new_in)
    if ringed:
        sum_qfv.step(arriving=(new_out[0],))
        total_qfv = sum_qfv.last()
    there = after(column_swap(total_qfv), new_in[0])
    sum_qfv = (total_qfv.astype(wide) + there.astype(wide)).astype(low)
    *own, dots_own = update_attention(
        core_ref, attention_state, sum_qfv, sum_do[0], matrix_step
    )
    theirs = after(core_swap(sum_qfv), own[0])
    gain_state = (gains, gains_momentum, gains_average)
    *new_attention, gains_m, gains_a, gains_w = update_attention(
        other_ref,
        attention_state,
        theirs,
        sum_do[1],
        matrix_step,
        (own, (dots_own, dots_up, dots_gate), gain_state, gain_rate * scale_rows),
    )
    return (
        output.reshape(micro_count, slot, width),
        input_grad.reshape(micro_count, slot, width),
        *new_attention,
        *new_in,
        *new_out,
        gains_m,
        gains_a,
        gains_w,
    )


def solution(mesh):
    rows_split = P(None, ("fsdp", "dp"), None)
    middle_split = P(None, "fsdp", None)
    first_split = P("fsdp", None)
    gains_split = P(None, "fsdp")
    in_specs = (
        (rows_split, rows_split, P(None, ("fsdp", "dp")))
        + (middle_split,) * 6
        + (first_split,) * 3
        + (gains_split,) * 3
    )
    out_specs = (
        (rows_split, rows_split)
        + (middle_split,) * 6
        + (first_split,) * 3
        + (gains_split,) * 3
    )
    return jax.shard_map(
        on_device, mesh=mesh, in_specs=in_specs, out_specs=out_specs, check_vma=False
    )
```

```python
import functools
import math

import jax
import jax.numpy as jnp
from jax import lax
from jax.experimental import pallas as pl
from jax.experimental.pallas import tpu as pltpu
from jax.sharding import PartitionSpec as P

HEAD_DIM = 128
PAIR = 2 * HEAD_DIM
GAIN_ROWS = 16

lower_bound = 0.9
momentum_decay = 0.9
average_decay = 0.7
weight_decay = 0.0005
matrix_rate = 0.03
gain_rate = 0.1
low = jnp.bfloat16
wide = jnp.float32
TILE_F = 256
VMEM_BYTES = 60 * 1024 * 1024


def mm(left, right):
    return jnp.dot(left, right, preferred_element_type=wide)


def mm_nt(left, right):
    return lax.dot_general(left, right, (((1,), (1,)), ((), ())), preferred_element_type=wide)


def mm_tn(left, right):
    return lax.dot_general(left, right, (((0,), (0,)), ((), ())), preferred_element_type=wide)


def sigmoid(u):
    return 0.5 * jnp.tanh(0.5 * u) + 0.5


def whole(shape):
    return pl.BlockSpec(shape, lambda *_: (0,) * len(shape), pipeline_mode=pl.Buffered(1))


def split_sum(ones_matrix, tensor):
    high = tensor.astype(low)
    rest = (tensor - high.astype(wide)).astype(low)
    return mm(ones_matrix, high) + mm(ones_matrix, rest)


def causal_mask(length, lower):
    rows = lax.broadcasted_iota(jnp.int32, (length, length), 0)
    columns = lax.broadcasted_iota(jnp.int32, (length, length), 1)
    return rows >= columns if lower else rows <= columns


def triangle(length, lower):
    return causal_mask(length, lower).astype(wide).astype(low)


def decay_parts(f_pre, lower_ones):
    share = sigmoid(f_pre)
    gate = lower_bound + (1.0 - lower_bound) * share
    keys_in = (1.0 - lower_bound) * (1.0 - share)
    cumulative = split_sum(lower_ones, jnp.log(gate))
    middle_row = cumulative.shape[0] // 2
    cumulative = cumulative - cumulative[middle_row : middle_row + 1, :]
    return share, gate, keys_in, cumulative


def first_norm(x_ref, gain_row):
    rows = x_ref[...].astype(wide)
    scale = lax.rsqrt(jnp.mean(rows * rows, axis=-1, keepdims=True) + 1e-06)
    return rows * scale, scale


def lanes_of(half, size):
    return pl.ds(pl.multiple_of(half * size, size), size)


def mixer_forward_first_kernel(
    slot, half_ref, x_ref, w_ref, gains_ref, on_ref, q_ref, f_ref, v_ref, o_ref, g_ref, h_s
):
    @pl.when(pl.program_id(0) == 0)
    def _():
        g_ref[...] = gains_ref[...].astype(wide)[: g_ref.shape[0], :]

    mixer_forward_kernel(
        slot, half_ref, x_ref, w_ref, g_ref, on_ref, q_ref, f_ref, v_ref, o_ref, h_s
    )


def mixer_forward_kernel(
    slot, half_ref, x_ref, w_ref, g_ref, on_ref, q_ref, f_ref, v_ref, o_ref, h_s
):
    @pl.when(pl.program_id(0) == 0)
    def _():
        normed, _ = first_norm(x_ref, None)
        h_s[...] = (normed * g_ref[0:1, :]).astype(low)

    gain_o = g_ref[1:2, lanes_of(half_ref[0] * pl.num_programs(0) + pl.program_id(0), PAIR)]
    pre = mm(h_s[...], w_ref[...])
    q_ref[...] = pre[:, :PAIR]
    f_ref[...] = pre[:, PAIR : 2 * PAIR]
    v_ref[...] = pre[:, 2 * PAIR :].astype(low)
    lower_ones = triangle(slot, True)
    causal = causal_mask(slot, True)
    for sequence in range(x_ref.shape[0] // slot):
        rows = slice(sequence * slot, (sequence + 1) * slot)
        q_pre = q_ref[rows, :]
        _, _, keys_in, cumulative = decay_parts(f_ref[rows, :], lower_ones)
        grown = jnp.exp(-cumulative)
        decayed_q = (q_pre * sigmoid(q_pre) * jnp.exp(cumulative)).astype(low)
        grown_k = (keys_in * grown).astype(low)
        values = v_ref[rows, :]
        for head in range(2):
            lanes = slice(head * HEAD_DIM, (head + 1) * HEAD_DIM)
            scores = mm_nt(decayed_q[:, lanes], grown_k[:, lanes])
            out = mm(jnp.where(causal, scores, 0.0).astype(low), values[:, lanes])
            scale = lax.rsqrt(jnp.mean(out * out, axis=-1, keepdims=True) + 1e-05)
            o_ref[rows, lanes] = out.astype(low)
            on_ref[rows, lanes] = (out * scale * gain_o[:, lanes]).astype(low)


def mixer_forward_last_kernel(
    slot,
    half_ref,
    x_ref,
    w_ref,
    g_ref,
    before_hbm,
    woo_hbm,
    wom_hbm,
    on_ref,
    q_ref,
    f_ref,
    v_ref,
    o_ref,
    x1_hbm,
    h2_ref,
    h2t_ref,
    h_s,
    on_s,
    x1_s,
    wo_s,
    semaphores,
):
    step = pl.program_id(0)
    half = before_hbm.shape[1]
    here, there = lanes_of(half_ref[0], half), lanes_of(1 - half_ref[0], half)
    sources = (
        (before_hbm, on_s.at[:, there]),
        (woo_hbm.at[:, pl.ds(3 * half, half)], wo_s.at[:, here]),
        (wom_hbm.at[:, pl.ds(3 * half, half)], wo_s.at[:, there]),
    )
    fetches = [
        pltpu.make_async_copy(source, target, semaphores.at[number])
        for number, (source, target) in enumerate(sources)
    ]

    @pl.when(step == 0)
    def _():
        for fetch in fetches:
            fetch.start()

    mixer_forward_kernel(
        slot, half_ref, x_ref, w_ref, g_ref, on_ref, q_ref, f_ref, v_ref, o_ref, h_s
    )
    on_s[:, lanes_of(half_ref[0] * pl.num_programs(0) + step, PAIR)] = on_ref[...]

    @pl.when(step == pl.num_programs(0) - 1)
    def _():
        for fetch in fetches:
            fetch.wait()
        x1 = x_ref[...].astype(wide) + mm(on_s[...], wo_s[...])
        x1_s[...] = x1
        leaving = pltpu.make_async_copy(x1_s, x1_hbm, semaphores.at[3])
        leaving.start()
        scale = lax.rsqrt(jnp.mean(x1 * x1, axis=-1, keepdims=True) + 1e-06)
        normed = x1 * scale * g_ref[2:3, :]
        h2_ref[...] = normed.astype(low)
        h2t_ref[...] = normed.T.astype(low)
        leaving.wait()


def norm_rows_kernel(x_ref, out_ref):
    normed, _ = first_norm(x_ref, None)
    out_ref[...] = normed.T.astype(low)


def norm_rows(rows):
    count, width = rows.shape
    return pl.pallas_call(
        norm_rows_kernel,
        in_specs=[pl.BlockSpec(memory_space=pltpu.VMEM)],
        out_specs=pl.BlockSpec(memory_space=pltpu.VMEM),
        out_shape=jax.ShapeDtypeStruct((width, count), low),
        compiler_params=pltpu.CompilerParams(vmem_limit_bytes=VMEM_BYTES),
        name="norm_rows",
    )(rows)


def mixer_forward(half, rows, weights, slot, gains=None, ending=None):
    count, width = rows.shape
    pairs = width // PAIR // 2
    by_pair = pl.BlockSpec((count, PAIR), lambda j, _: (0, j))
    struct = jax.ShapeDtypeStruct
    shape = lambda kind: struct((count, width // 2), kind)
    in_specs = [whole(rows.shape), pl.BlockSpec((width, 3 * PAIR), lambda j, _: (0, j))]
    operands = [half, rows, weights]
    out_specs = [by_pair] * 5
    out_shape = [shape(low), shape(wide), shape(wide), shape(low), shape(low)]
    scratch = [pltpu.VMEM((count, width), low)]
    if ending is None:
        kernel = mixer_forward_first_kernel
        in_specs += [whole(gains.shape)]
        operands += [gains]
        out_specs += [whole((8, width))]
        out_shape += [struct((8, width), wide)]
    if ending is not None:
        kernel = mixer_forward_last_kernel
        anywhere = pl.BlockSpec(memory_space=pl.ANY)
        in_specs += [whole(ending[0].shape), anywhere, anywhere, anywhere]
        operands += [ending[0], ending[1], weights, ending[2]]
        out_specs += [anywhere, whole((count, width)), whole((width, count))]
        out_shape += [
            struct((count, width), wide),
            struct((count, width), low),
            struct((width, count), low),
        ]
        scratch += [
            pltpu.VMEM((count, width), low),
            pltpu.VMEM((count, width), wide),
            pltpu.VMEM((width, width), low),
            pltpu.SemaphoreType.DMA((4,)),
        ]
    return pl.pallas_call(
        functools.partial(kernel, slot),
        grid_spec=pltpu.PrefetchScalarGridSpec(
            num_scalar_prefetch=1,
            grid=(pairs,),
            in_specs=in_specs,
            out_specs=out_specs,
            scratch_shapes=scratch,
        ),
        out_shape=out_shape,
        compiler_params=pltpu.CompilerParams(vmem_limit_bytes=VMEM_BYTES),
        cost_estimate=pl.CostEstimate(
            flops=count * width * 4 * width + 10 * count * slot * width,
            bytes_accessed=count * width * 12 + width * width * 4,
            transcendentals=count * width * 3,
        ),
        name="mixer_forward",
    )(*operands)


def store_down(out_ref, tile, owners):
    _, stride, down_rows = owners
    block = math.gcd(down_rows, tile.shape[0])
    first = pl.program_id(0) * (tile.shape[0] // block)
    for part in range(tile.shape[0] // block):
        owner = (first + part) // (down_rows // block)
        inside = (first + part) % (down_rows // block)
        start = pl.multiple_of(owner * stride + inside * block, block)
        out_ref[pl.ds(start, block), :] = tile[part * block : (part + 1) * block, :]


def ffn_kernel(
    owners,
    core_ref,
    h_ref,
    ht_ref,
    e_ref,
    wm_ref,
    wu_ref,
    wdm_ref,
    wdo_ref,
    x1_hbm,
    onm_hbm,
    ono_hbm,
    wom_hbm,
    woo_hbm,
    m_ref,
    g_ref,
    gm_ref,
    gu_ref,
    gdm_hbm,
    gdo_hbm,
    out_hbm,
    dx1_hbm,
    don_hbm,
    *scratch,
):
    gu_w, gu_g, down_g, down_w, mid_s, dh_s, on_s, x1_s, wo_s, out_s, gdm_s, gdo_s = scratch[:12]
    in_semaphores, out_semaphores, down_semaphores = scratch[12:]
    step, last = pl.program_id(0), pl.num_programs(0) - 1
    half, tile = wdm_ref.shape[1], wm_ref.shape[1]
    mine, other = lanes_of(core_ref[0], half), lanes_of(1 - core_ref[0], half)
    kind, kind_other = lanes_of(core_ref[0], tile), lanes_of(1 - core_ref[0], tile)
    count, stride, down_rows = owners

    width = on_s.shape[1]
    sources = (
        (x1_hbm, x1_s),
        (onm_hbm, on_s.at[:, mine]),
        (ono_hbm, on_s.at[:, other]),
        (wom_hbm.at[:, pl.ds(3 * half, half)], wo_s.at[:, mine]),
        (woo_hbm.at[:, pl.ds(3 * half, half)], wo_s.at[:, other]),
    )
    fetches = [
        pltpu.make_async_copy(source, target, in_semaphores.at[number])
        for number, (source, target) in enumerate(sources)
    ]

    def down_copies(owner):
        rows = pl.ds(pl.multiple_of(owner * stride, math.gcd(stride, 32)), down_rows)
        return [
            pltpu.make_async_copy(held.at[rows, :], out.at[rows, :], down_semaphores.at[side, owner])
            for side, (held, out) in enumerate(((gdm_s, gdm_hbm), (gdo_s, gdo_hbm)))
        ]

    @pl.when(step == 0)
    def _():
        dh_s[...] = jnp.zeros_like(dh_s)
        for fetch in fetches:
            fetch.start()

    gu_w[:, kind] = wm_ref[...]
    gu_w[:, kind_other] = wu_ref[...]
    hidden_rows = pl.ds(pl.multiple_of(step * tile, tile), tile)
    down_w[hidden_rows, mine] = wdm_ref[...]
    down_w[hidden_rows, other] = wdo_ref[...]
    pre = mm(h_ref[...], gu_w[...])
    a, b = pre[:, :tile], pre[:, tile:]
    share = sigmoid(a)
    swish = a * share
    mid = (swish * b).astype(low)
    mid_s[:, lanes_of(step, tile)] = mid
    d_mid = mm_nt(e_ref[...], down_w[hidden_rows, :])
    down_g[...] = mm_tn(mid, e_ref[...]).astype(low)
    d_a = (d_mid * b * (share + swish * (1.0 - share))).astype(low)
    d_b = (d_mid * swish).astype(low)
    d_pre = jnp.concatenate([d_a, d_b], axis=1)
    dh_s[...] += mm_nt(d_pre, gu_w[...])
    gu_g[...] = mm(ht_ref[...], d_pre).astype(low)
    blocks = tile // HEAD_DIM
    for side, block in enumerate((core_ref[1], 1 - core_ref[1])):
        gm_ref[side] = gu_g[:, lanes_of(core_ref[0] * blocks + block, HEAD_DIM)]
        gu_ref[side] = gu_g[:, lanes_of((1 - core_ref[0]) * blocks + block, HEAD_DIM)]
    store_down(gdm_s, down_g[:, mine], owners)
    store_down(gdo_s, down_g[:, other], owners)

    done = (step + 1) * tile // down_rows

    @pl.when(done > step * tile // down_rows)
    def _():
        for copy in down_copies(done - 1):
            copy.start()

    @pl.when(step == last)
    def _():
        for fetch in fetches:
            fetch.wait()
        x1 = x1_s[...]
        x2 = x1 + mm(mid_s[...], down_w[...])
        positions = lax.broadcasted_iota(jnp.int32, (out_s.shape[0] // m_ref.shape[0], 1), 0)
        for sequence in range(m_ref.shape[0]):
            rows = slice(sequence * positions.shape[0], (sequence + 1) * positions.shape[0])
            valid = (positions < m_ref[sequence]).astype(wide)
            out_s[rows, :] = (x2[rows, :] * valid).astype(low)
        leaving = [pltpu.make_async_copy(out_s, out_hbm, out_semaphores.at[0])]
        leaving[-1].start()
        scale = lax.rsqrt(jnp.mean(x1 * x1, axis=-1, keepdims=True) + 1e-06)
        normed = x1 * scale
        scaled = dh_s[...] * g_ref[2:3, :]
        d_x1 = e_ref[...].astype(wide) + scale * (
            scaled - normed * jnp.mean(scaled * normed, axis=-1, keepdims=True)
        )
        dh_s[...] = d_x1
        leaving.append(pltpu.make_async_copy(dh_s, dx1_hbm, out_semaphores.at[1]))
        leaving[-1].start()
        d_1 = mid_s.at[:, pl.ds(0, width)]
        d_1[...] = d_x1.astype(low)
        d_mixed = mid_s.at[:, pl.ds(width, width)]
        d_mixed[...] = mm_nt(d_1[...], wo_s[...]).astype(low)
        leaving.append(pltpu.make_async_copy(d_mixed, don_hbm, out_semaphores.at[2]))
        leaving[-1].start()
        rows = stride - down_rows
        grad_o = mm_tn(on_s[...], d_1[...]).astype(low)
        down_w[pl.ds(0, width), :] = grad_o
        for columns, held, out in ((mine, gdm_s, gdm_hbm), (other, gdo_s, gdo_hbm)):
            for owner in range(count):
                target = slice(owner * stride + down_rows, (owner + 1) * stride)
                held[target, :] = down_w[owner * rows : (owner + 1) * rows, columns]
                copy = pltpu.make_async_copy(
                    held.at[target, :], out.at[target, :], out_semaphores.at[len(leaving)]
                )
                copy.start()
                leaving.append(copy)
        for owner in range(count):
            leaving += down_copies(owner)
        for copy in leaving:
            copy.wait()


def ffn(core, h2, h2t, errors, w_gu, w_d, x1, mixed, w_a, lengths, gains8, owners):
    count, width = h2.shape
    half = width // 2
    hidden = w_gu[0].shape[1]
    full = whole((count, width))
    in_tile = pl.BlockSpec((width, TILE_F), lambda j, _: (0, j))
    out_tile = pl.BlockSpec((TILE_F, half), lambda j, _: (j, 0))
    grad_tile = pl.BlockSpec((2, width, HEAD_DIM), lambda j, _: (0, 0, j))
    anywhere = pl.BlockSpec(memory_space=pl.ANY)
    down_shape = (owners[0] * owners[1], half)
    struct = jax.ShapeDtypeStruct
    vmem = pltpu.VMEM
    return pl.pallas_call(
        functools.partial(ffn_kernel, owners),
        grid_spec=pltpu.PrefetchScalarGridSpec(
            num_scalar_prefetch=1,
            grid=(hidden // TILE_F,),
            in_specs=[full, whole(h2t.shape), full, in_tile, in_tile, out_tile, out_tile]
            + [anywhere] * 5
            + [pl.BlockSpec(memory_space=pltpu.SMEM), whole((8, width))],
            out_specs=[grad_tile, grad_tile] + [anywhere] * 5,
            scratch_shapes=[
                vmem((width, 2 * TILE_F), low),
                vmem((width, 2 * TILE_F), low),
                vmem((TILE_F, width), low),
                vmem((hidden, width), low),
                vmem((count, hidden), low),
                vmem((count, width), wide),
                vmem((count, width), low),
                vmem((count, width), wide),
                vmem((width, width), low),
                vmem((count, width), low),
                vmem(down_shape, low),
                vmem(down_shape, low),
                pltpu.SemaphoreType.DMA((5,)),
                pltpu.SemaphoreType.DMA((3 + 2 * owners[0],)),
                pltpu.SemaphoreType.DMA((2, owners[0])),
            ],
        ),
        out_shape=[struct((2, width, hidden // 2), low)] * 2
        + [struct(down_shape, low)] * 2
        + [
            struct((count, width), low),
            struct((count, width), wide),
            struct((count, width), low),
        ],
        compiler_params=pltpu.CompilerParams(vmem_limit_bytes=VMEM_BYTES),
        cost_estimate=pl.CostEstimate(
            flops=18 * count * width * hidden,
            bytes_accessed=count * width * 20 + width * hidden * 12,
            transcendentals=count * hidden,
        ),
        name="ffn",
    )(core, h2, h2t, errors, *w_gu, *w_d, x1, *mixed, *w_a, lengths, gains8)


def mixer_backward_kernel(
    slot,
    per_half,
    first,
    half_ref,
    nt_hbm,
    g_ref,
    q_ref,
    f_ref,
    v_ref,
    o_ref,
    don_ref,
    *outs,
):
    grad_ref, dpre_hbm, nt_s, dpre_ref, semaphores = outs[-5:]
    fetch = pltpu.make_async_copy(nt_hbm, nt_s, semaphores.at[0])
    fetch.start()
    gain_o = g_ref[1:2, lanes_of(half_ref[0] * per_half + first + pl.program_id(0), PAIR)]
    lower_ones = triangle(slot, True)
    upper_ones = triangle(slot, False)
    causal_t = causal_mask(slot, False)
    for sequence in range(q_ref.shape[0] // slot):
        rows = slice(sequence * slot, (sequence + 1) * slot)
        d_on = don_ref[rows, :].astype(wide)
        out = o_ref[rows, :].astype(wide)
        d_out_parts = []
        for head in range(2):
            lanes = slice(head * HEAD_DIM, (head + 1) * HEAD_DIM)
            out_h, d_on_h = out[:, lanes], d_on[:, lanes]
            scale = lax.rsqrt(jnp.mean(out_h * out_h, axis=-1, keepdims=True) + 1e-05)
            normed = out_h * scale
            scaled = d_on_h * gain_o[:, lanes]
            inner = jnp.mean(scaled * normed, axis=-1, keepdims=True)
            d_out_parts.append((scale * (scaled - normed * inner)).astype(low))

        q_pre = q_ref[rows, :]
        share, gate, keys_in, cumulative = decay_parts(f_ref[rows, :], lower_ones)
        grown = jnp.exp(-cumulative)
        shrunk = jnp.exp(cumulative)
        q_share = sigmoid(q_pre)
        decayed_q = (q_pre * q_share * shrunk).astype(low)
        grown_k = (keys_in * grown).astype(low)
        values = v_ref[rows, :]
        dq_parts, dk_parts, dv_parts = [], [], []
        for head in range(2):
            lanes = slice(head * HEAD_DIM, (head + 1) * HEAD_DIM)
            q_h, k_h, v_h = decayed_q[:, lanes], grown_k[:, lanes], values[:, lanes]
            d_out = d_out_parts[head]
            scores = jnp.where(causal_t, mm_nt(k_h, q_h), 0.0).astype(low)
            d_scores = jnp.where(causal_t, mm_nt(v_h, d_out), 0.0).astype(low)
            dv_parts.append(mm(scores, d_out))
            dk_parts.append(mm(d_scores, q_h))
            dq_parts.append(mm_tn(d_scores, k_h))
        d_decayed = jnp.concatenate(dq_parts, axis=1)
        d_grown = jnp.concatenate(dk_parts, axis=1)
        d_value = jnp.concatenate(dv_parts, axis=1)
        d_cumulative = decayed_q.astype(wide) * d_decayed - grown_k.astype(wide) * d_grown
        d_log = split_sum(upper_ones, d_cumulative)
        d_query = d_decayed * shrunk
        d_key = d_grown * grown
        d_q_pre = d_query * q_share * (1.0 + q_pre * (1.0 - q_share))
        d_f_pre = (1.0 - lower_bound) * (d_log / gate - d_key) * share * (1.0 - share)
        dpre_ref[rows, :PAIR] = d_q_pre.astype(low)
        dpre_ref[rows, PAIR : 2 * PAIR] = d_f_pre.astype(low)
        dpre_ref[rows, 2 * PAIR :] = d_value.astype(low)

    columns = pl.ds(first * 3 * PAIR, 3 * PAIR)
    leaving = pltpu.make_async_copy(dpre_ref, dpre_hbm.at[:, columns], semaphores.at[1])
    leaving.start()
    fetch.wait()
    gain_column = g_ref[...].T[:, 0:1]
    grad = (mm(nt_s[...], dpre_ref[...]) * gain_column).astype(low)
    grad_ref[...] = grad.reshape(grad_ref.shape)
    leaving.wait()


def mixer_backward(half, n1t, gains8, kept, d_mixed, slot, shard, pairs=(0, 1), before=()):
    width, count = n1t.shape
    per_half = width // PAIR // 2
    first = pairs[0]
    by_pair = pl.BlockSpec((count, PAIR), lambda j, _: (0, first + j))
    from_whole = pl.BlockSpec((count, PAIR), lambda j, half: (0, half[0] * per_half + first + j))
    struct = jax.ShapeDtypeStruct
    return pl.pallas_call(
        functools.partial(mixer_backward_kernel, slot, per_half, first),
        grid_spec=pltpu.PrefetchScalarGridSpec(
            num_scalar_prefetch=1,
            grid=(len(pairs),),
            in_specs=[pl.BlockSpec(memory_space=pl.ANY), whole(gains8.shape)]
            + [by_pair] * 4
            + [from_whole]
            + [pl.BlockSpec(memory_space=pl.ANY)] * len(before),
            out_specs=[
                pl.BlockSpec(
                    (width // shard, 1, shard, 3 * PAIR), lambda j, _: (0, first + j, 0, 0)
                ),
                pl.BlockSpec(memory_space=pl.ANY),
            ],
            scratch_shapes=[
                pltpu.VMEM((width, count), low),
                pltpu.VMEM((count, 3 * PAIR), low),
                pltpu.SemaphoreType.DMA((2,)),
            ],
        ),
        out_shape=[
            struct((width // shard, per_half, shard, 3 * PAIR), low),
            struct((count, per_half * 3 * PAIR), low),
        ],
        input_output_aliases={8 + k: k for k in range(len(before))},
        compiler_params=pltpu.CompilerParams(vmem_limit_bytes=VMEM_BYTES),
        cost_estimate=pl.CostEstimate(
            flops=len(pairs) * (count * width * 6 * PAIR + 20 * count * slot * PAIR),
            bytes_accessed=len(pairs) * (count * width * 5 + width * PAIR * 6),
            transcendentals=len(pairs) * count * PAIR * 6,
        ),
        name="mixer_backward",
    )(half, n1t, gains8, *kept, d_mixed, *before)


def input_gradient_rows_kernel(
    x_ref, g_ref, dm_ref, do_ref, wm_ref, wo_ref, dx1_ref, dx_ref
):
    d_h1 = mm_nt(dm_ref[...], wm_ref[...]) + mm_nt(do_ref[...], wo_ref[...])
    normed, scale = first_norm(x_ref, None)
    scaled = d_h1 * g_ref[0:1, :]
    dx_ref[...] = dx1_ref[...] + scale * (
        scaled - normed * jnp.mean(scaled * normed, axis=-1, keepdims=True)
    )


def input_gradient(rows, gains8, d_pre, weights, d_x1):
    count, width = rows.shape
    block = count // 2
    columns = d_pre[0].shape[1]
    by_rows = lambda columns: pl.BlockSpec((block, columns), lambda j: (j, 0))
    weight_spec = pl.BlockSpec((width, columns), lambda j: (0, 0), pipeline_mode=pl.Buffered(1))
    return pl.pallas_call(
        input_gradient_rows_kernel,
        grid=(count // block,),
        in_specs=[by_rows(width), whole(gains8.shape)]
        + [by_rows(columns)] * 2
        + [weight_spec] * 2
        + [by_rows(width)],
        out_specs=by_rows(width),
        out_shape=jax.ShapeDtypeStruct((count, width), wide),
        compiler_params=pltpu.CompilerParams(vmem_limit_bytes=VMEM_BYTES),
        cost_estimate=pl.CostEstimate(
            flops=6 * count * width * width,
            bytes_accessed=count * width * 16 + width * width * 6,
            transcendentals=0,
        ),
        name="input_gradient",
    )(rows, gains8, *d_pre, *weights, d_x1)


def update(weight, momentum, average, gradient, step_rate):
    new_momentum = momentum_decay * momentum + gradient
    direction = gradient + momentum_decay * new_momentum + weight_decay * weight
    new_weight = weight - step_rate * direction
    new_average = average_decay * average + (1.0 - average_decay) * new_weight
    return (new_momentum, new_average, new_weight)


def update_kernel(pick, step_rate, sum_count, core_ref, w_ref, m_ref, a_ref, *refs):
    sums, outs, dots_ref = refs[:sum_count], refs[-4:-1], refs[-1]
    weight = w_ref[...]
    gradient = pick(core_ref[0], *[s[...] for s in sums]).astype(wide).reshape(weight.shape)
    results = update(weight, m_ref[...], a_ref[...], gradient, step_rate)
    for out, result in zip(outs, results):
        out[...] = result
    product = weight.astype(low).astype(wide) * gradient
    total = product[..., :HEAD_DIM]
    for start in range(HEAD_DIM, product.shape[-1], HEAD_DIM):
        total = total + product[..., start : start + HEAD_DIM]
    dots_ref[...] = total.reshape(dots_ref.shape)


def update_call(
    core, state, sums, grid, state_spec, sum_specs, pick, step_rate, name, before=()
):
    struct = jax.ShapeDtypeStruct(state[0].shape, wide)
    size = math.prod(state[0].shape)
    rows = state_spec.block_shape[-2]
    steps = math.prod(grid)
    tail = grid[1:]

    def dots_index(*indices):
        place = indices[0]
        for length, index in zip(tail, indices[1:]):
            place = place * length + index
        return (place, 0, 0)

    return pl.pallas_call(
        functools.partial(update_kernel, pick, step_rate, len(sums)),
        grid_spec=pltpu.PrefetchScalarGridSpec(
            num_scalar_prefetch=1,
            grid=grid,
            in_specs=[state_spec] * 3
            + sum_specs
            + [pl.BlockSpec(memory_space=pl.ANY)] * len(before),
            out_specs=[state_spec] * 3 + [pl.BlockSpec((1, rows, HEAD_DIM), dots_index)],
        ),
        out_shape=[struct] * 3 + [jax.ShapeDtypeStruct((steps, rows, HEAD_DIM), wide)],
        input_output_aliases={4 + len(sums) + k: k for k in range(len(before))},
        compiler_params=pltpu.CompilerParams(vmem_limit_bytes=VMEM_BYTES),
        cost_estimate=pl.CostEstimate(flops=12 * size, bytes_accessed=26 * size, transcendentals=0),
        name=name,
    )(core, *state, *sums, *before)


def update_attention_kernel(
    pick, step_rate, gain_step, core_ref, w_ref, m_ref, a_ref, qfv_ref, out_ref, *refs
):
    if gain_step is None:
        update_kernel(pick, step_rate, 2, core_ref, w_ref, m_ref, a_ref, qfv_ref, out_ref, *refs)
        return
    *held, dots_s = refs
    own_dots, up_dots, gate_dots, g_ref, gm_ref, ga_ref = held[:6]
    outs, gain_outs = held[-6:-3], held[-3:]
    kind = pl.program_id(0)
    dots = dots_s.at[kind]
    update_kernel(
        pick, step_rate, 2, core_ref, w_ref, m_ref, a_ref, qfv_ref, out_ref, *outs, dots
    )

    @pl.when(kind == pl.num_programs(0) - 1)
    def _():
        shard = dots_s.shape[1]
        sums = [own_dots[k] + dots_s[k] for k in range(4)]
        two = (up_dots[...] + gate_dots[...]).reshape(shard, HEAD_DIM)
        columns = [
            jnp.sum(total, axis=1, keepdims=True) for total in (sums[0] + sums[1] + sums[2], sums[3], two)
        ]
        lanes = lax.broadcasted_iota(jnp.int32, (shard, HEAD_DIM), 1)
        table = jnp.where(lanes == 1, columns[1], columns[2])
        table = jnp.where(lanes == 0, columns[0], table)
        gain = g_ref[...]
        gradient = table.T[:3, :] / gain.astype(low).astype(wide)
        results = update(gain, gm_ref[...], ga_ref[...], gradient, gain_step)
        for out, result in zip(gain_outs, results):
            out[...] = result


def update_attention(half_ref, state, qfv, out, step_rate, gains=None):
    _, shard, width = state[0].shape
    down_rows = out.shape[0] - shard

    def pick(core_index, proj, last):
        gradient = last[down_rows:].astype(wide)
        for kind in range(3):
            parts = [proj[pair * shard :, kind * PAIR :][:shard, :PAIR] for pair in range(2)]
            chosen = jnp.concatenate(parts, axis=1).astype(wide)
            gradient = jnp.where(pl.program_id(0) == kind, chosen, gradient)
        return gradient

    struct = jax.ShapeDtypeStruct
    state_spec = pl.BlockSpec((1, shard, width // 2), lambda kind, half: (kind, 0, half[0]))
    in_specs = [state_spec] * 3 + [whole(qfv.shape), whole(out.shape)]
    out_specs = [state_spec] * 3
    out_shape = [struct(state[0].shape, wide)] * 3
    operands = [half_ref, *state, qfv, out]
    aliases, scratch, gain_step = {}, [], None
    if gains is None:
        out_specs += [pl.BlockSpec((1, shard, HEAD_DIM), lambda kind, half: (kind, 0, 0))]
        out_shape += [struct((4, shard, HEAD_DIM), wide)]
    else:
        before, dots, gain_state, gain_step = gains
        in_specs += [whole(part.shape) for part in (*dots, *gain_state)]
        operands += [*dots, *gain_state]
        aliases = {len(operands) + k: k for k in range(3)}
        in_specs += [pl.BlockSpec(memory_space=pl.ANY)] * 3
        operands += list(before)
        out_specs += [whole(gain_state[0].shape)] * 3
        out_shape += [struct(gain_state[0].shape, wide)] * 3
        scratch = [pltpu.VMEM((4, shard, HEAD_DIM), wide)]
    size = math.prod(state[0].shape) // 2
    return pl.pallas_call(
        functools.partial(update_attention_kernel, pick, step_rate, gain_step),
        grid_spec=pltpu.PrefetchScalarGridSpec(
            num_scalar_prefetch=1,
            grid=(4,),
            in_specs=in_specs,
            out_specs=out_specs,
            scratch_shapes=scratch,
        ),
        out_shape=out_shape,
        input_output_aliases=aliases,
        compiler_params=pltpu.CompilerParams(vmem_limit_bytes=VMEM_BYTES),
        cost_estimate=pl.CostEstimate(flops=12 * size, bytes_accessed=26 * size, transcendentals=0),
        name="update_attention",
    )(*operands)


def update_ffn_in(kind_ref, state, totals, step_rate, before):
    _, shard, hidden = state[0].shape
    block = shard // 2

    def pick(_, even, odd):
        blocks = []
        for start in range(0, hidden // 2, HEAD_DIM):
            blocks += [even[:, start : start + HEAD_DIM], odd[:, start : start + HEAD_DIM]]
        return jnp.concatenate(blocks, axis=1)

    return update_call(
        kind_ref,
        state,
        totals,
        (2,),
        pl.BlockSpec((1, block, hidden), lambda j, kind: (kind[0], j, 0)),
        [pl.BlockSpec((block, hidden // 2), lambda j, _: (j, 0))] * 2,
        pick,
        step_rate,
        "update_ffn_in",
        before,
    )


def update_ffn_out(core, state, sums, step_rate):
    shard, width = state[0].shape

    def pick(core_index, mine, other):
        own = pl.program_id(0) == core_index
        return jnp.where(own, mine[:shard].astype(wide), other[:shard].astype(wide))

    return update_call(
        core,
        state,
        sums,
        (2,),
        pl.BlockSpec((shard, width // 2), lambda j, _: (0, j)),
        [whole(total.shape) for total in sums],
        pick,
        step_rate,
        "update_ffn_out",
    )


def pack_kernel(core_ref, w_ref, out_ref):
    half = w_ref.shape[2]
    for pair in range(half // PAIR):
        for kind in range(3):
            start = (pair * 3 + kind) * PAIR
            piece = w_ref[kind, :, pair * PAIR : (pair + 1) * PAIR]
            out_ref[:, start : start + PAIR] = piece.astype(low)
    out_ref[:, 3 * half : 4 * half] = w_ref[3].astype(low)


def pack_attention(core, weights):
    _, shard, width = weights.shape
    half = width // 2
    return pl.pallas_call(
        pack_kernel,
        grid_spec=pltpu.PrefetchScalarGridSpec(
            num_scalar_prefetch=1,
            grid=(1,),
            in_specs=[pl.BlockSpec((4, shard, half), lambda j, core: (0, 0, core[0]))],
            out_specs=whole((shard, 4 * half)),
        ),
        out_shape=jax.ShapeDtypeStruct((shard, 4 * half), low),
        name="pack_attention",
    )(core, weights)


RING = 8


def ring_place(index):
    return jnp.where(index % 2 == 0, index // 2, RING - 1 - index // 2)


def ring_member(place):
    place = place % RING
    return jnp.where(place < RING // 2, 2 * place, 2 * RING - 1 - 2 * place)


CYCLE = (0, 2, 4, 6, 7, 5, 3, 1)


def ring_next(tensor):
    replicas = lax.axis_size("dp")
    pairs = []
    for place_of, member in enumerate(CYCLE):
        for replica in range(replicas):
            target = CYCLE[(place_of + (1 if replica % 2 == 0 else -1)) % RING]
            pairs.append((member * replicas + replica, target * replicas + replica))
    return lax.ppermute(tensor, ("fsdp", "dp"), pairs)


def ring_shift(tensor, way):
    pairs = [(member, CYCLE[(at + way) % RING]) for at, member in enumerate(CYCLE)]
    return lax.ppermute(tensor, "fsdp", pairs)


def core_swap(tensor):
    return lax.ppermute(tensor, "dp", [(d, d ^ 1) for d in range(lax.axis_size("dp"))])


def column_swap(tensor):
    return lax.ppermute(tensor, "dp", [(d, d ^ 2) for d in range(lax.axis_size("dp"))])


def pack_all_kernel(
    core_ref, column_ref, w_ref, up_ref, other_ref, down_ref, g_ref, out_ref, across_ref
):
    across_ref[...] = other_ref[0].astype(low)
    shard = w_ref.shape[1]
    half = w_ref.shape[2]
    for pair in range(half // PAIR):
        for kind in range(3):
            start = (pair * 3 + kind) * PAIR
            piece = w_ref[kind, :, pair * PAIR : (pair + 1) * PAIR]
            out_ref[:, start : start + PAIR] = piece.astype(low)
    out_ref[:, 3 * half : 4 * half] = w_ref[3].astype(low)
    start = 4 * half
    out_ref[:, start : start + up_ref.shape[2]] = up_ref[0].astype(low)
    start += up_ref.shape[2]
    for first, count in down_parts(down_ref.shape[0], shard):
        out_ref[:count, start : start + half] = down_ref[first : first + count, :].astype(low)
        if count < shard:
            out_ref[count:, start : start + half] = jnp.zeros((shard - count, half), low)
            rows = lax.broadcasted_iota(jnp.int32, (GAIN_ROWS, g_ref.shape[1]), 0)
            gains = jnp.where(rows == 1, g_ref[1:2, :], g_ref[2:3, :])
            gains = jnp.where(rows == 0, g_ref[0:1, :], gains)
            gains = jnp.where(rows < 3, gains, 0.0).astype(low)
            out_ref[count : count + GAIN_ROWS, start : start + g_ref.shape[1]] = gains
        start += half


def down_parts(down_rows, shard):
    return [(start, min(shard, down_rows - start)) for start in range(0, down_rows, shard)]


def pack_all(core, column, weights, up, down, gains):
    _, shard, width = weights.shape
    half = width // 2
    parts = len(down_parts(down.shape[0], shard))
    columns = 4 * half + up.shape[2] // 2 + parts * half
    return pl.pallas_call(
        pack_all_kernel,
        grid_spec=pltpu.PrefetchScalarGridSpec(
            num_scalar_prefetch=2,
            grid=(1,),
            in_specs=[
                pl.BlockSpec((4, shard, half), lambda j, core, column: (0, 0, core[0])),
                pl.BlockSpec(
                    (1, shard, up.shape[2] // 2), lambda j, core, column: (core[0], 0, column[0])
                ),
                pl.BlockSpec(
                    (1, shard, up.shape[2] // 2),
                    lambda j, core, column: (core[0], 0, 1 - column[0]),
                ),
                pl.BlockSpec((down.shape[0], half), lambda j, core, column: (0, core[0])),
                whole(gains.shape),
            ],
            out_specs=[whole((shard, columns)), whole((shard, up.shape[2] // 2))],
        ),
        out_shape=[
            jax.ShapeDtypeStruct((shard, columns), low),
            jax.ShapeDtypeStruct((shard, up.shape[2] // 2), low),
        ],
        compiler_params=pltpu.CompilerParams(vmem_limit_bytes=VMEM_BYTES),
        name="pack_all",
    )(core, column, weights, up, up, down, gains)


def place_kernel(which, kept, shapes, origin_ref, column_ref, *refs):
    pieces, outs, semaphores = refs[: len(which)], refs[-1 - len(kept) : -1], refs[-1]
    targets = dict(zip(kept, outs))
    shard, first, up_columns, down_rows, half = shapes
    copies = []

    def copy(source, target):
        copies.append(pltpu.make_async_copy(source, target, semaphores.at[len(copies)]))

    for piece, (origin, across) in zip(pieces, which):
        owner = origin_ref[origin]
        rows = pl.ds(pl.multiple_of(owner * shard, 16), shard)
        if across:
            copy(piece, targets[1].at[rows, lanes_of(1 - column_ref[0], up_columns)])
            continue
        copy(piece.at[:, pl.ds(0, first)], targets[0].at[rows, :])
        own = targets[1].at[rows, lanes_of(column_ref[0], up_columns)]
        copy(piece.at[:, pl.ds(first, up_columns)], own)
        lane = first + up_columns
        for start, count in down_parts(down_rows, shard):
            target = pl.ds(pl.multiple_of(owner * down_rows + start, 16), count)
            copy(piece.at[pl.ds(0, count), pl.ds(lane, half)], targets[2].at[target, :])
            if count < shard:
                source = piece.at[pl.ds(count, GAIN_ROWS), pl.ds(lane, shard)]
                copy(source, targets[3].at[:, lanes_of(owner, shard)])
            lane += half
    for one in copies:
        one.start()
    for one in copies:
        one.wait()


def place(origins, column, which, pieces, arrays, kept, shapes):
    anywhere = pl.BlockSpec(memory_space=pl.ANY)
    shard, first, up_columns, down_rows, half = shapes
    kinds = [(RING * shard, first), (RING * shard, 2 * up_columns), (RING * down_rows, half)]
    kinds.append((GAIN_ROWS, RING * shard))
    held = [] if arrays is None else list(arrays)
    size = sum(math.prod(piece.shape) for piece in pieces)
    before = 2 + len(pieces)
    return pl.pallas_call(
        functools.partial(place_kernel, which, kept, shapes),
        grid_spec=pltpu.PrefetchScalarGridSpec(
            num_scalar_prefetch=2,
            grid=(1,),
            in_specs=[whole(piece.shape) for piece in pieces] + [anywhere] * len(held),
            out_specs=[anywhere] * len(kept),
            scratch_shapes=[pltpu.SemaphoreType.DMA((8 * len(pieces),))],
        ),
        out_shape=[jax.ShapeDtypeStruct(kinds[k], pieces[0].dtype) for k in kept],
        input_output_aliases={before + k: k for k in range(len(held))},
        compiler_params=pltpu.CompilerParams(vmem_limit_bytes=VMEM_BYTES),
        cost_estimate=pl.CostEstimate(flops=0, bytes_accessed=8 * size, transcendentals=0),
        name="place",
    )(origins, column, *pieces, *held)


def after(tensor, *others):
    return lax.optimization_barrier((tensor, *others))[0]


def core_way():
    return 1 - 2 * (lax.axis_index("dp") % 2)


def ring_origins():
    steps = jnp.array((0, -1, -2, -3, -4, 1, 2, 3), jnp.int32)
    return ring_member(ring_place(lax.axis_index("fsdp")) + steps + RING).astype(jnp.int32)


class RingSumOverColumns:
    def __init__(self, mine, arrived):
        self.arrays = (mine, arrived)
        place = ring_place(lax.axis_index("fsdp"))
        self.rows = mine.shape[1] // RING
        self.starts = [
            ring_member(place - core_way() * (s + 1) + 2 * RING) * self.rows for s in range(RING)
        ]
        self.sent, self.came, self.totals = [], [], []

    def part(self, side, step):
        shape = (1, self.rows, self.arrays[0].shape[2])
        parts = [
            lax.dynamic_slice(array, (side, self.starts[step], 0), shape)[0]
            for array in self.arrays
        ]
        return parts[0].astype(wide) + parts[1].astype(wide)

    def cross(self):
        self.sent.append(self.part(1, len(self.sent)).astype(low))
        self.came.append(column_swap(self.sent[-1]))

    def term(self):
        step = len(self.totals)
        return self.part(0, step) + self.came[step].astype(wide)

    def begin(self, *others):
        self.came[0] = after(self.came[0], *others) if others else self.came[0]
        self.totals.append(self.term().astype(low))

    def step(self, arriving=()):
        total, ahead = self.totals[-1], self.came[len(self.totals)]
        moved = ring_next(after(total, ahead) if len(self.totals) > 1 else total)
        moved = after(moved, *arriving) if arriving else moved
        self.totals.append((moved.astype(wide) + self.term()).astype(low))

    def last(self):
        return self.totals[-1]


class RingSum:
    def __init__(self, mine, arrived):
        self.mine, self.arrived = mine, arrived
        place = ring_place(lax.axis_index("fsdp"))
        self.owners = [ring_member(place - core_way() * (s + 1) + 2 * RING) for s in range(RING)]
        self.totals = []

    def term(self):
        parts = []
        for own, arrived in zip(self.mine, self.arrived):
            rows = own.shape[0] // RING
            start = self.owners[len(self.totals)] * rows
            part = lax.dynamic_slice_in_dim(own, start, rows, 0).astype(wide)
            parts.append(part + lax.dynamic_slice_in_dim(arrived, start, rows, 0).astype(wide))
        return parts[0] if len(parts) == 1 else jnp.concatenate(parts, axis=0)

    def begin(self, *others):
        if others:
            self.mine = [after(self.mine[0], *others), *self.mine[1:]]
        self.totals.append(self.term().astype(low))

    def step(self, *before, arriving=()):
        total = self.totals[-1]
        moved = ring_next(after(total, *before) if before else total)
        moved = after(moved, *arriving) if arriving else moved
        self.totals.append((moved.astype(wide) + self.term().astype(wide)).astype(low))

    def last(self):
        return self.totals[-1]


def gather_rows(shard):
    mine = lax.all_gather(shard, "fsdp", axis=0, tiled=True)
    return mine, core_swap(mine)


def core_sum(mine, other):
    return (mine.astype(wide) + core_swap(other).astype(wide)).astype(low)


def scatter_rows(both):
    return lax.psum_scatter(both, "fsdp", scatter_dimension=0, tiled=True)


def over_columns(total):
    total = (total.astype(wide) + column_swap(total).astype(wide)).astype(low)
    return total, core_swap(total)


def on_device(
    inputs,
    cotangent,
    lengths,
    attention_weights,
    attention_momentum,
    attention_average,
    ffn_inputs,
    ffn_inputs_momentum,
    ffn_inputs_average,
    ffn_output,
    ffn_output_momentum,
    ffn_output_average,
    gains,
    gains_momentum,
    gains_average,
):
    micro_count, slot, width = inputs.shape
    hidden = ffn_inputs.shape[2]
    shard, down_rows = ffn_inputs.shape[1], ffn_output.shape[0]
    fsdp_size = lax.axis_size("fsdp")
    replicas = lax.axis_size("dp")
    ringed = fsdp_size == RING
    core = lax.axis_index("dp") % 2
    column = lax.axis_index("dp") // 2
    count = micro_count * slot
    half = width // 2
    core_ref = core.astype(jnp.int32).reshape(1)
    other_ref = 1 - core_ref
    column_ref = column.astype(jnp.int32).reshape(1)
    is_first = core == 0

    rows = inputs.reshape(count, width)
    n1t = norm_rows(rows)
    positions = jnp.arange(slot, dtype=jnp.int32)
    valid = (positions[None, :] < lengths).astype(wide).reshape(count, 1)
    errors = (cotangent.reshape(count, width).astype(wide) * valid).astype(low)

    if ringed:
        origins = ring_origins()
        first = 4 * half
        shapes = (shard, first, hidden // 2, down_rows, half)
        packed, own_across = pack_all(
            core_ref, column_ref, attention_weights, ffn_inputs, ffn_output, gains
        )
        wholes, there, which_there = None, [own_across], [(0, True)]
        here, which = [packed], [(0, False)]
        for step in range(1, 6):
            if step <= 3:
                onward = [ring_shift(here[0], 1), ring_shift(here[-1], -1)]
            elif step == 4:
                onward = [ring_next(jnp.where(is_first, *here))]
            across = []
            if step > 1:
                across = [column_swap(piece[:, first : first + hidden // 2]) for piece in here]
            wholes = place(
                origins, column_ref, which + which_there, here + there, wholes, (0, 1, 2, 3), shapes
            )
            if step == 5:
                break
            extra = [errors, n1t] if step == 2 else []
            tied = list(lax.optimization_barrier((*onward, *across, *wholes, *extra)))
            here, rest = tied[: len(onward)], tied[len(onward) :]
            there, wholes = rest[: len(across)], rest[len(across) : len(across) + 4]
            which_there = [(origin, True) for origin, _ in which] if across else []
            which = [(origin, False) for origin in [step, step + 4][: len(onward)]]
        w_a, gain_rows = (wholes[0], core_swap(wholes[0])), wholes[3]
    else:
        w_a = gather_rows(pack_attention(core_ref, attention_weights))
        gain_rows = lax.all_gather(gains.astype(low), "fsdp", axis=1, tiled=True)
        gain_rows = jnp.pad(gain_rows, ((0, GAIN_ROWS - 3), (0, 0)))
        w_gu = gather_rows(
            lax.dynamic_index_in_dim(ffn_inputs, core, 0, keepdims=False).astype(low)
        )
        w_d = gather_rows(lax.dynamic_slice_in_dim(ffn_output, core * half, half, 1).astype(low))
    mixed_mine, *kept_mine, gains8 = mixer_forward(core_ref, rows, w_a[0], slot, gain_rows)
    if ringed:
        (across,) = lax.optimization_barrier((*across, mixed_mine, w_a[1]))[:1]
        (w_gu_mine,) = place(origins, column_ref, [(4, True)], [across], [wholes[1]], (1,), shapes)
        wholes = [wholes[0], w_gu_mine, wholes[2], wholes[3]]
        rows = after(rows, *wholes[1:3])
        w_gu, w_d = [(array, core_swap(array)) for array in wholes[1:3]]
    mixed_other, *rest = mixer_forward(
        other_ref, rows, w_a[1], slot, None, (gains8, mixed_mine, w_a[0])
    )
    kept_other, (x1, h2, h2t) = rest[:4], rest[4:]
    owners = (RING, down_rows + shard, down_rows)
    if not ringed:
        owners = (1, hidden + width, hidden)
    places = jnp.concatenate([core_ref, column_ref])
    *grad_gu, gd_mine, gd_other, output, d_x1, d_mixed = ffn(
        places, h2, h2t, errors, w_gu, w_d, x1, (mixed_mine, mixed_other), w_a, lengths[:, 0], gains8, owners
    )

    gm, gu = grad_gu
    arrived_gu = core_swap(gu)
    mine_do, arrived_do = [gd_mine], [core_swap(gd_other)]
    by_owner = (fsdp_size * 2 * shard, 3 * PAIR)
    d_pre = []
    for call in range(4):
        from_half, kept = (other_ref, kept_other) if call < 2 else (core_ref, kept_mine)
        if ringed and call == 1:
            sum_gu = RingSumOverColumns(after(gm, d_pre[0]), arrived_gu)
            sum_gu.cross()
            sum_gu.cross()
            n1t = after(n1t, *sum_gu.sent)
        elif ringed and call > 1:
            sum_gu.cross()
            ahead = [sum_gu.came[2]] if call == 3 else []
            n1t = after(n1t, sum_gu.last(), sum_do.last(), sum_gu.sent[-1], *ahead)
        grads = mixer_backward(
            from_half,
            n1t,
            gains8,
            kept,
            d_mixed,
            slot,
            shard,
            (call % 2,),
            grads if call % 2 else (),
        )
        d_pre.append(grads[1])
        if call == 1:
            grad_other = grads[0]
            if ringed:
                sum_do = RingSum(mine_do, arrived_do)
                sum_do.begin(d_pre[-1])
                sum_gu.begin(d_pre[-1])
                grad_other = after(grad_other, sum_gu.last(), sum_do.last())
            arrived_qfv = [core_swap(grad_other.reshape(by_owner))]
        elif ringed and call > 1:
            gate = d_pre[-1]
            if call == 3:
                sum_qfv = RingSum([grads[0].reshape(by_owner)], arrived_qfv)
                sum_qfv.begin()
                gate = sum_qfv.last()
            sum_do.step(arriving=(gate,))
            sum_gu.step(arriving=(gate,))
    mine_qfv = [grads[0].reshape(by_owner)]

    def finish_input(*others):
        late = after(d_pre[3], *others) if others else d_pre[3]
        return input_gradient(rows, gains8, (late, d_pre[1]), w_a, d_x1)

    if ringed:
        input_grad = None
        for step in range(1, RING - 1):
            if len(sum_gu.came) < RING:
                sum_gu.cross()
            if len(sum_gu.totals) < RING:
                first = [sum_gu.last(), sum_qfv.last()]
                sum_do.step(*{1: first, 4: [input_grad]}.get(step, []))
                sum_gu.step()
            sum_qfv.step()
            if step == 2:
                input_grad = finish_input(sum_qfv.last(), sum_gu.came[5])
        total_gu, total_do = sum_gu.last(), sum_do.last()
    else:
        both = (gm.astype(wide) + arrived_gu.astype(wide)).astype(low)
        here = (both[0].astype(wide) + column_swap(both[1]).astype(wide)).astype(low)
        total_gu = scatter_rows(here)
        both = (gd_mine.astype(wide) + arrived_do[0].astype(wide)).astype(low)
        total_do = jnp.concatenate(
            [scatter_rows(both[:hidden]), scatter_rows(both[hidden:])], axis=0
        )
        total_qfv = scatter_rows(
            (mine_qfv[0].astype(wide) + arrived_qfv[0].astype(wide)).astype(low)
        )
        input_grad = finish_input()
    scale_rows = 1.0 / math.sqrt(count * fsdp_size * replicas)
    matrix_step = matrix_rate * scale_rows
    attention_state = (attention_weights, attention_momentum, attention_average)
    ffn_in_state = (ffn_inputs, ffn_inputs_momentum, ffn_inputs_average)
    ffn_out_state = (ffn_output, ffn_output_momentum, ffn_output_average)
    sum_do = over_columns(total_do)
    there = column_swap(total_gu)
    even = jnp.where(column == 0, total_gu, there)
    odd = jnp.where(column == 0, there, total_gu)
    sum_gu = (even, odd), (core_swap(even), core_swap(odd))
    *new_out, _ = update_ffn_out(core_ref, ffn_out_state, sum_do, matrix_step)
    *new_in, dots_up = update_ffn_in(core_ref, ffn_in_state, sum_gu[0], matrix_step, ())
    *new_in, dots_gate = update_ffn_in(other_ref, ffn_in_state, sum_gu[1], matrix_step, new_in)
    if ringed:
        sum_qfv.step(arriving=(new_out[0],))
        total_qfv = sum_qfv.last()
    there = after(column_swap(total_qfv), new_in[0])
    sum_qfv = (total_qfv.astype(wide) + there.astype(wide)).astype(low)
    *own, dots_own = update_attention(
        core_ref, attention_state, sum_qfv, sum_do[0], matrix_step
    )
    theirs = after(core_swap(sum_qfv), own[0])
    gain_state = (gains, gains_momentum, gains_average)
    *new_attention, gains_m, gains_a, gains_w = update_attention(
        other_ref,
        attention_state,
        theirs,
        sum_do[1],
        matrix_step,
        (own, (dots_own, dots_up, dots_gate), gain_state, gain_rate * scale_rows),
    )
    return (
        output.reshape(micro_count, slot, width),
        input_grad.reshape(micro_count, slot, width),
        *new_attention,
        *new_in,
        *new_out,
        gains_m,
        gains_a,
        gains_w,
    )


def solution(mesh):
    rows_split = P(None, ("fsdp", "dp"), None)
    middle_split = P(None, "fsdp", None)
    first_split = P("fsdp", None)
    gains_split = P(None, "fsdp")
    in_specs = (
        (rows_split, rows_split, P(None, ("fsdp", "dp")))
        + (middle_split,) * 6
        + (first_split,) * 3
        + (gains_split,) * 3
    )
    out_specs = (
        (rows_split, rows_split)
        + (middle_split,) * 6
        + (first_split,) * 3
        + (gains_split,) * 3
    )
    return jax.shard_map(
        on_device, mesh=mesh, in_specs=in_specs, out_specs=out_specs, check_vma=False
    )
```

```python
import functools
import math

import jax
import jax.numpy as jnp
from jax import lax
from jax.experimental import pallas as pl
from jax.experimental.pallas import tpu as pltpu
from jax.sharding import PartitionSpec as P

HEAD_DIM = 128
PAIR = 2 * HEAD_DIM
GAIN_ROWS = 16

lower_bound = 0.9
momentum_decay = 0.9
average_decay = 0.7
weight_decay = 0.0005
matrix_rate = 0.03
gain_rate = 0.1
low = jnp.bfloat16
wide = jnp.float32
TILE_F = 256
VMEM_BYTES = 60 * 1024 * 1024


def mm(left, right):
    return jnp.dot(left, right, preferred_element_type=wide)


def mm_nt(left, right):
    return lax.dot_general(left, right, (((1,), (1,)), ((), ())), preferred_element_type=wide)


def mm_tn(left, right):
    return lax.dot_general(left, right, (((0,), (0,)), ((), ())), preferred_element_type=wide)


def sigmoid(u):
    return 0.5 * jnp.tanh(0.5 * u) + 0.5


def whole(shape):
    return pl.BlockSpec(shape, lambda *_: (0,) * len(shape), pipeline_mode=pl.Buffered(1))


def split_sum(ones_matrix, tensor):
    high = tensor.astype(low)
    rest = (tensor - high.astype(wide)).astype(low)
    return mm(ones_matrix, high) + mm(ones_matrix, rest)


def causal_mask(length, lower):
    rows = lax.broadcasted_iota(jnp.int32, (length, length), 0)
    columns = lax.broadcasted_iota(jnp.int32, (length, length), 1)
    return rows >= columns if lower else rows <= columns


def triangle(length, lower):
    return causal_mask(length, lower).astype(wide).astype(low)


def decay_parts(f_pre, lower_ones):
    share = sigmoid(f_pre)
    gate = lower_bound + (1.0 - lower_bound) * share
    keys_in = (1.0 - lower_bound) * (1.0 - share)
    cumulative = split_sum(lower_ones, jnp.log(gate))
    middle_row = cumulative.shape[0] // 2
    cumulative = cumulative - cumulative[middle_row : middle_row + 1, :]
    return share, gate, keys_in, cumulative


def first_norm(x_ref, gain_row):
    rows = x_ref[...].astype(wide)
    scale = lax.rsqrt(jnp.mean(rows * rows, axis=-1, keepdims=True) + 1e-06)
    return rows * scale, scale


def lanes_of(half, size):
    return pl.ds(pl.multiple_of(half * size, size), size)


def mixer_forward_first_kernel(
    slot, half_ref, x_ref, w_ref, gains_ref, on_ref, q_ref, f_ref, v_ref, o_ref, g_ref, h_s
):
    @pl.when(pl.program_id(0) == 0)
    def _():
        g_ref[...] = gains_ref[...].astype(wide)[: g_ref.shape[0], :]

    mixer_forward_kernel(
        slot, half_ref, x_ref, w_ref, g_ref, on_ref, q_ref, f_ref, v_ref, o_ref, h_s
    )


def mixer_forward_kernel(
    slot, half_ref, x_ref, w_ref, g_ref, on_ref, q_ref, f_ref, v_ref, o_ref, h_s
):
    @pl.when(pl.program_id(0) == 0)
    def _():
        normed, _ = first_norm(x_ref, None)
        h_s[...] = (normed * g_ref[0:1, :]).astype(low)

    gain_o = g_ref[1:2, lanes_of(half_ref[0] * pl.num_programs(0) + pl.program_id(0), PAIR)]
    pre = mm(h_s[...], w_ref[...])
    q_ref[...] = pre[:, :PAIR]
    f_ref[...] = pre[:, PAIR : 2 * PAIR]
    v_ref[...] = pre[:, 2 * PAIR :].astype(low)
    lower_ones = triangle(slot, True)
    causal = causal_mask(slot, True)
    for sequence in range(x_ref.shape[0] // slot):
        rows = slice(sequence * slot, (sequence + 1) * slot)
        q_pre = q_ref[rows, :]
        _, _, keys_in, cumulative = decay_parts(f_ref[rows, :], lower_ones)
        grown = jnp.exp(-cumulative)
        decayed_q = (q_pre * sigmoid(q_pre) * jnp.exp(cumulative)).astype(low)
        grown_k = (keys_in * grown).astype(low)
        values = v_ref[rows, :]
        for head in range(2):
            lanes = slice(head * HEAD_DIM, (head + 1) * HEAD_DIM)
            scores = mm_nt(decayed_q[:, lanes], grown_k[:, lanes])
            out = mm(jnp.where(causal, scores, 0.0).astype(low), values[:, lanes])
            scale = lax.rsqrt(jnp.mean(out * out, axis=-1, keepdims=True) + 1e-05)
            o_ref[rows, lanes] = out.astype(low)
            on_ref[rows, lanes] = (out * scale * gain_o[:, lanes]).astype(low)


def mixer_forward_last_kernel(
    slot,
    half_ref,
    x_ref,
    w_ref,
    g_ref,
    before_hbm,
    woo_hbm,
    wom_hbm,
    on_ref,
    q_ref,
    f_ref,
    v_ref,
    o_ref,
    x1_hbm,
    h2_ref,
    h2t_ref,
    h_s,
    on_s,
    x1_s,
    wo_s,
    semaphores,
):
    step = pl.program_id(0)
    half = before_hbm.shape[1]
    here, there = lanes_of(half_ref[0], half), lanes_of(1 - half_ref[0], half)
    sources = (
        (before_hbm, on_s.at[:, there]),
        (woo_hbm.at[:, pl.ds(3 * half, half)], wo_s.at[:, here]),
        (wom_hbm.at[:, pl.ds(3 * half, half)], wo_s.at[:, there]),
    )
    fetches = [
        pltpu.make_async_copy(source, target, semaphores.at[number])
        for number, (source, target) in enumerate(sources)
    ]

    @pl.when(step == 0)
    def _():
        for fetch in fetches:
            fetch.start()

    mixer_forward_kernel(
        slot, half_ref, x_ref, w_ref, g_ref, on_ref, q_ref, f_ref, v_ref, o_ref, h_s
    )
    on_s[:, lanes_of(half_ref[0] * pl.num_programs(0) + step, PAIR)] = on_ref[...]

    @pl.when(step == pl.num_programs(0) - 1)
    def _():
        for fetch in fetches:
            fetch.wait()
        x1 = x_ref[...].astype(wide) + mm(on_s[...], wo_s[...])
        x1_s[...] = x1
        leaving = pltpu.make_async_copy(x1_s, x1_hbm, semaphores.at[3])
        leaving.start()
        scale = lax.rsqrt(jnp.mean(x1 * x1, axis=-1, keepdims=True) + 1e-06)
        normed = x1 * scale * g_ref[2:3, :]
        h2_ref[...] = normed.astype(low)
        h2t_ref[...] = normed.T.astype(low)
        leaving.wait()


def norm_rows_kernel(x_ref, out_ref):
    normed, _ = first_norm(x_ref, None)
    out_ref[...] = normed.T.astype(low)


def norm_rows(rows):
    count, width = rows.shape
    return pl.pallas_call(
        norm_rows_kernel,
        in_specs=[pl.BlockSpec(memory_space=pltpu.VMEM)],
        out_specs=pl.BlockSpec(memory_space=pltpu.VMEM),
        out_shape=jax.ShapeDtypeStruct((width, count), low),
        compiler_params=pltpu.CompilerParams(vmem_limit_bytes=VMEM_BYTES),
        name="norm_rows",
    )(rows)


def mixer_forward(half, rows, weights, slot, gains=None, ending=None):
    count, width = rows.shape
    pairs = width // PAIR // 2
    by_pair = pl.BlockSpec((count, PAIR), lambda j, _: (0, j))
    struct = jax.ShapeDtypeStruct
    shape = lambda kind: struct((count, width // 2), kind)
    in_specs = [whole(rows.shape), pl.BlockSpec((width, 3 * PAIR), lambda j, _: (0, j))]
    operands = [half, rows, weights]
    out_specs = [by_pair] * 5
    out_shape = [shape(low), shape(wide), shape(wide), shape(low), shape(low)]
    scratch = [pltpu.VMEM((count, width), low)]
    if ending is None:
        kernel = mixer_forward_first_kernel
        in_specs += [whole(gains.shape)]
        operands += [gains]
        out_specs += [whole((8, width))]
        out_shape += [struct((8, width), wide)]
    if ending is not None:
        kernel = mixer_forward_last_kernel
        anywhere = pl.BlockSpec(memory_space=pl.ANY)
        in_specs += [whole(ending[0].shape), anywhere, anywhere, anywhere]
        operands += [ending[0], ending[1], weights, ending[2]]
        out_specs += [anywhere, whole((count, width)), whole((width, count))]
        out_shape += [
            struct((count, width), wide),
            struct((count, width), low),
            struct((width, count), low),
        ]
        scratch += [
            pltpu.VMEM((count, width), low),
            pltpu.VMEM((count, width), wide),
            pltpu.VMEM((width, width), low),
            pltpu.SemaphoreType.DMA((4,)),
        ]
    return pl.pallas_call(
        functools.partial(kernel, slot),
        grid_spec=pltpu.PrefetchScalarGridSpec(
            num_scalar_prefetch=1,
            grid=(pairs,),
            in_specs=in_specs,
            out_specs=out_specs,
            scratch_shapes=scratch,
        ),
        out_shape=out_shape,
        compiler_params=pltpu.CompilerParams(vmem_limit_bytes=VMEM_BYTES),
        cost_estimate=pl.CostEstimate(
            flops=count * width * 4 * width + 10 * count * slot * width,
            bytes_accessed=count * width * 12 + width * width * 4,
            transcendentals=count * width * 3,
        ),
        name="mixer_forward",
    )(*operands)


def store_down(out_ref, tile, owners):
    _, stride, down_rows = owners
    block = math.gcd(down_rows, tile.shape[0])
    first = pl.program_id(0) * (tile.shape[0] // block)
    for part in range(tile.shape[0] // block):
        owner = (first + part) // (down_rows // block)
        inside = (first + part) % (down_rows // block)
        start = pl.multiple_of(owner * stride + inside * block, block)
        out_ref[pl.ds(start, block), :] = tile[part * block : (part + 1) * block, :]


def ffn_kernel(
    owners,
    core_ref,
    h_ref,
    ht_ref,
    e_ref,
    wm_ref,
    wu_ref,
    wdm_ref,
    wdo_ref,
    x1_hbm,
    onm_hbm,
    ono_hbm,
    wom_hbm,
    woo_hbm,
    m_ref,
    g_ref,
    gm_ref,
    gu_ref,
    gdm_hbm,
    gdo_hbm,
    out_hbm,
    dx1_hbm,
    don_hbm,
    *scratch,
):
    gu_w, gu_g, down_g, down_w, mid_s, dh_s, on_s, x1_s, wo_s, out_s, gdm_s, gdo_s = scratch[:12]
    in_semaphores, out_semaphores, down_semaphores = scratch[12:]
    step, last = pl.program_id(0), pl.num_programs(0) - 1
    half, tile = wdm_ref.shape[1], wm_ref.shape[1]
    mine, other = lanes_of(core_ref[0], half), lanes_of(1 - core_ref[0], half)
    kind, kind_other = lanes_of(core_ref[0], tile), lanes_of(1 - core_ref[0], tile)
    count, stride, down_rows = owners

    width = on_s.shape[1]
    sources = (
        (x1_hbm, x1_s),
        (onm_hbm, on_s.at[:, mine]),
        (ono_hbm, on_s.at[:, other]),
        (wom_hbm.at[:, pl.ds(3 * half, half)], wo_s.at[:, mine]),
        (woo_hbm.at[:, pl.ds(3 * half, half)], wo_s.at[:, other]),
    )
    fetches = [
        pltpu.make_async_copy(source, target, in_semaphores.at[number])
        for number, (source, target) in enumerate(sources)
    ]

    def down_copies(owner):
        rows = pl.ds(pl.multiple_of(owner * stride, math.gcd(stride, 32)), down_rows)
        return [
            pltpu.make_async_copy(held.at[rows, :], out.at[rows, :], down_semaphores.at[side, owner])
            for side, (held, out) in enumerate(((gdm_s, gdm_hbm), (gdo_s, gdo_hbm)))
        ]

    @pl.when(step == 0)
    def _():
        dh_s[...] = jnp.zeros_like(dh_s)
        for fetch in fetches:
            fetch.start()

    gu_w[:, kind] = wm_ref[...]
    gu_w[:, kind_other] = wu_ref[...]
    hidden_rows = pl.ds(pl.multiple_of(step * tile, tile), tile)
    down_w[hidden_rows, mine] = wdm_ref[...]
    down_w[hidden_rows, other] = wdo_ref[...]
    pre = mm(h_ref[...], gu_w[...])
    a, b = pre[:, :tile], pre[:, tile:]
    share = sigmoid(a)
    swish = a * share
    mid = (swish * b).astype(low)
    mid_s[:, lanes_of(step, tile)] = mid
    d_mid = mm_nt(e_ref[...], down_w[hidden_rows, :])
    down_g[...] = mm_tn(mid, e_ref[...]).astype(low)
    d_a = (d_mid * b * (share + swish * (1.0 - share))).astype(low)
    d_b = (d_mid * swish).astype(low)
    d_pre = jnp.concatenate([d_a, d_b], axis=1)
    dh_s[...] += mm_nt(d_pre, gu_w[...])
    gu_g[...] = mm(ht_ref[...], d_pre).astype(low)
    blocks = tile // HEAD_DIM
    for side, block in enumerate((core_ref[1], 1 - core_ref[1])):
        gm_ref[side] = gu_g[:, lanes_of(core_ref[0] * blocks + block, HEAD_DIM)]
        gu_ref[side] = gu_g[:, lanes_of((1 - core_ref[0]) * blocks + block, HEAD_DIM)]
    store_down(gdm_s, down_g[:, mine], owners)
    store_down(gdo_s, down_g[:, other], owners)

    done = (step + 1) * tile // down_rows

    @pl.when(done > step * tile // down_rows)
    def _():
        for copy in down_copies(done - 1):
            copy.start()

    @pl.when(step == last)
    def _():
        for fetch in fetches:
            fetch.wait()
        x1 = x1_s[...]
        x2 = x1 + mm(mid_s[...], down_w[...])
        positions = lax.broadcasted_iota(jnp.int32, (out_s.shape[0] // m_ref.shape[0], 1), 0)
        for sequence in range(m_ref.shape[0]):
            rows = slice(sequence * positions.shape[0], (sequence + 1) * positions.shape[0])
            valid = (positions < m_ref[sequence]).astype(wide)
            out_s[rows, :] = (x2[rows, :] * valid).astype(low)
        leaving = [pltpu.make_async_copy(out_s, out_hbm, out_semaphores.at[0])]
        leaving[-1].start()
        scale = lax.rsqrt(jnp.mean(x1 * x1, axis=-1, keepdims=True) + 1e-06)
        normed = x1 * scale
        scaled = dh_s[...] * g_ref[2:3, :]
        d_x1 = e_ref[...].astype(wide) + scale * (
            scaled - normed * jnp.mean(scaled * normed, axis=-1, keepdims=True)
        )
        dh_s[...] = d_x1
        leaving.append(pltpu.make_async_copy(dh_s, dx1_hbm, out_semaphores.at[1]))
        leaving[-1].start()
        d_1 = mid_s.at[:, pl.ds(0, width)]
        d_1[...] = d_x1.astype(low)
        d_mixed = mid_s.at[:, pl.ds(width, width)]
        d_mixed[...] = mm_nt(d_1[...], wo_s[...]).astype(low)
        leaving.append(pltpu.make_async_copy(d_mixed, don_hbm, out_semaphores.at[2]))
        leaving[-1].start()
        rows = stride - down_rows
        grad_o = mm_tn(on_s[...], d_1[...]).astype(low)
        down_w[pl.ds(0, width), :] = grad_o
        for columns, held, out in ((mine, gdm_s, gdm_hbm), (other, gdo_s, gdo_hbm)):
            for owner in range(count):
                target = slice(owner * stride + down_rows, (owner + 1) * stride)
                held[target, :] = down_w[owner * rows : (owner + 1) * rows, columns]
                copy = pltpu.make_async_copy(
                    held.at[target, :], out.at[target, :], out_semaphores.at[len(leaving)]
                )
                copy.start()
                leaving.append(copy)
        for owner in range(count):
            leaving += down_copies(owner)
        for copy in leaving:
            copy.wait()


def ffn(core, h2, h2t, errors, w_gu, w_d, x1, mixed, w_a, lengths, gains8, owners):
    count, width = h2.shape
    half = width // 2
    hidden = w_gu[0].shape[1]
    full = whole((count, width))
    in_tile = pl.BlockSpec((width, TILE_F), lambda j, _: (0, j))
    out_tile = pl.BlockSpec((TILE_F, half), lambda j, _: (j, 0))
    grad_tile = pl.BlockSpec((2, width, HEAD_DIM), lambda j, _: (0, 0, j))
    anywhere = pl.BlockSpec(memory_space=pl.ANY)
    down_shape = (owners[0] * owners[1], half)
    struct = jax.ShapeDtypeStruct
    vmem = pltpu.VMEM
    return pl.pallas_call(
        functools.partial(ffn_kernel, owners),
        grid_spec=pltpu.PrefetchScalarGridSpec(
            num_scalar_prefetch=1,
            grid=(hidden // TILE_F,),
            in_specs=[full, whole(h2t.shape), full, in_tile, in_tile, out_tile, out_tile]
            + [anywhere] * 5
            + [pl.BlockSpec(memory_space=pltpu.SMEM), whole((8, width))],
            out_specs=[grad_tile, grad_tile] + [anywhere] * 5,
            scratch_shapes=[
                vmem((width, 2 * TILE_F), low),
                vmem((width, 2 * TILE_F), low),
                vmem((TILE_F, width), low),
                vmem((hidden, width), low),
                vmem((count, hidden), low),
                vmem((count, width), wide),
                vmem((count, width), low),
                vmem((count, width), wide),
                vmem((width, width), low),
                vmem((count, width), low),
                vmem(down_shape, low),
                vmem(down_shape, low),
                pltpu.SemaphoreType.DMA((5,)),
                pltpu.SemaphoreType.DMA((3 + 2 * owners[0],)),
                pltpu.SemaphoreType.DMA((2, owners[0])),
            ],
        ),
        out_shape=[struct((2, width, hidden // 2), low)] * 2
        + [struct(down_shape, low)] * 2
        + [
            struct((count, width), low),
            struct((count, width), wide),
            struct((count, width), low),
        ],
        compiler_params=pltpu.CompilerParams(vmem_limit_bytes=VMEM_BYTES),
        cost_estimate=pl.CostEstimate(
            flops=18 * count * width * hidden,
            bytes_accessed=count * width * 20 + width * hidden * 12,
            transcendentals=count * hidden,
        ),
        name="ffn",
    )(core, h2, h2t, errors, *w_gu, *w_d, x1, *mixed, *w_a, lengths, gains8)


def mixer_backward_kernel(
    slot,
    per_half,
    first,
    half_ref,
    nt_hbm,
    g_ref,
    q_ref,
    f_ref,
    v_ref,
    o_ref,
    don_ref,
    *outs,
):
    grad_ref, dpre_hbm, nt_s, dpre_ref, semaphores = outs[-5:]
    fetch = pltpu.make_async_copy(nt_hbm, nt_s, semaphores.at[0])
    fetch.start()
    gain_o = g_ref[1:2, lanes_of(half_ref[0] * per_half + first + pl.program_id(0), PAIR)]
    lower_ones = triangle(slot, True)
    upper_ones = triangle(slot, False)
    causal_t = causal_mask(slot, False)
    for sequence in range(q_ref.shape[0] // slot):
        rows = slice(sequence * slot, (sequence + 1) * slot)
        d_on = don_ref[rows, :].astype(wide)
        out = o_ref[rows, :].astype(wide)
        d_out_parts = []
        for head in range(2):
            lanes = slice(head * HEAD_DIM, (head + 1) * HEAD_DIM)
            out_h, d_on_h = out[:, lanes], d_on[:, lanes]
            scale = lax.rsqrt(jnp.mean(out_h * out_h, axis=-1, keepdims=True) + 1e-05)
            normed = out_h * scale
            scaled = d_on_h * gain_o[:, lanes]
            inner = jnp.mean(scaled * normed, axis=-1, keepdims=True)
            d_out_parts.append((scale * (scaled - normed * inner)).astype(low))

        q_pre = q_ref[rows, :]
        share, gate, keys_in, cumulative = decay_parts(f_ref[rows, :], lower_ones)
        grown = jnp.exp(-cumulative)
        shrunk = jnp.exp(cumulative)
        q_share = sigmoid(q_pre)
        decayed_q = (q_pre * q_share * shrunk).astype(low)
        grown_k = (keys_in * grown).astype(low)
        values = v_ref[rows, :]
        dq_parts, dk_parts, dv_parts = [], [], []
        for head in range(2):
            lanes = slice(head * HEAD_DIM, (head + 1) * HEAD_DIM)
            q_h, k_h, v_h = decayed_q[:, lanes], grown_k[:, lanes], values[:, lanes]
            d_out = d_out_parts[head]
            scores = jnp.where(causal_t, mm_nt(k_h, q_h), 0.0).astype(low)
            d_scores = jnp.where(causal_t, mm_nt(v_h, d_out), 0.0).astype(low)
            dv_parts.append(mm(scores, d_out))
            dk_parts.append(mm(d_scores, q_h))
            dq_parts.append(mm_tn(d_scores, k_h))
        d_decayed = jnp.concatenate(dq_parts, axis=1)
        d_grown = jnp.concatenate(dk_parts, axis=1)
        d_value = jnp.concatenate(dv_parts, axis=1)
        d_cumulative = decayed_q.astype(wide) * d_decayed - grown_k.astype(wide) * d_grown
        d_log = split_sum(upper_ones, d_cumulative)
        d_query = d_decayed * shrunk
        d_key = d_grown * grown
        d_q_pre = d_query * q_share * (1.0 + q_pre * (1.0 - q_share))
        d_f_pre = (1.0 - lower_bound) * (d_log / gate - d_key) * share * (1.0 - share)
        dpre_ref[rows, :PAIR] = d_q_pre.astype(low)
        dpre_ref[rows, PAIR : 2 * PAIR] = d_f_pre.astype(low)
        dpre_ref[rows, 2 * PAIR :] = d_value.astype(low)

    columns = pl.ds(first * 3 * PAIR, 3 * PAIR)
    leaving = pltpu.make_async_copy(dpre_ref, dpre_hbm.at[:, columns], semaphores.at[1])
    leaving.start()
    fetch.wait()
    gain_column = g_ref[...].T[:, 0:1]
    grad = (mm(nt_s[...], dpre_ref[...]) * gain_column).astype(low)
    grad_ref[...] = grad.reshape(grad_ref.shape)
    leaving.wait()


def mixer_backward(half, n1t, gains8, kept, d_mixed, slot, shard, pairs=(0, 1), before=()):
    width, count = n1t.shape
    per_half = width // PAIR // 2
    first = pairs[0]
    by_pair = pl.BlockSpec((count, PAIR), lambda j, _: (0, first + j))
    from_whole = pl.BlockSpec((count, PAIR), lambda j, half: (0, half[0] * per_half + first + j))
    struct = jax.ShapeDtypeStruct
    return pl.pallas_call(
        functools.partial(mixer_backward_kernel, slot, per_half, first),
        grid_spec=pltpu.PrefetchScalarGridSpec(
            num_scalar_prefetch=1,
            grid=(len(pairs),),
            in_specs=[pl.BlockSpec(memory_space=pl.ANY), whole(gains8.shape)]
            + [by_pair] * 4
            + [from_whole]
            + [pl.BlockSpec(memory_space=pl.ANY)] * len(before),
            out_specs=[
                pl.BlockSpec(
                    (width // shard, 1, shard, 3 * PAIR), lambda j, _: (0, first + j, 0, 0)
                ),
                pl.BlockSpec(memory_space=pl.ANY),
            ],
            scratch_shapes=[
                pltpu.VMEM((width, count), low),
                pltpu.VMEM((count, 3 * PAIR), low),
                pltpu.SemaphoreType.DMA((2,)),
            ],
        ),
        out_shape=[
            struct((width // shard, per_half, shard, 3 * PAIR), low),
            struct((count, per_half * 3 * PAIR), low),
        ],
        input_output_aliases={8 + k: k for k in range(len(before))},
        compiler_params=pltpu.CompilerParams(vmem_limit_bytes=VMEM_BYTES),
        cost_estimate=pl.CostEstimate(
            flops=len(pairs) * (count * width * 6 * PAIR + 20 * count * slot * PAIR),
            bytes_accessed=len(pairs) * (count * width * 5 + width * PAIR * 6),
            transcendentals=len(pairs) * count * PAIR * 6,
        ),
        name="mixer_backward",
    )(half, n1t, gains8, *kept, d_mixed, *before)


def input_gradient_rows_kernel(
    x_ref, g_ref, dm_ref, do_ref, wm_ref, wo_ref, dx1_ref, dx_ref
):
    d_h1 = mm_nt(dm_ref[...], wm_ref[...]) + mm_nt(do_ref[...], wo_ref[...])
    normed, scale = first_norm(x_ref, None)
    scaled = d_h1 * g_ref[0:1, :]
    dx_ref[...] = dx1_ref[...] + scale * (
        scaled - normed * jnp.mean(scaled * normed, axis=-1, keepdims=True)
    )


def input_gradient(rows, gains8, d_pre, weights, d_x1):
    count, width = rows.shape
    block = count // 2
    columns = d_pre[0].shape[1]
    by_rows = lambda columns: pl.BlockSpec((block, columns), lambda j: (j, 0))
    weight_spec = pl.BlockSpec((width, columns), lambda j: (0, 0), pipeline_mode=pl.Buffered(1))
    return pl.pallas_call(
        input_gradient_rows_kernel,
        grid=(count // block,),
        in_specs=[by_rows(width), whole(gains8.shape)]
        + [by_rows(columns)] * 2
        + [weight_spec] * 2
        + [by_rows(width)],
        out_specs=by_rows(width),
        out_shape=jax.ShapeDtypeStruct((count, width), wide),
        compiler_params=pltpu.CompilerParams(vmem_limit_bytes=VMEM_BYTES),
        cost_estimate=pl.CostEstimate(
            flops=6 * count * width * width,
            bytes_accessed=count * width * 16 + width * width * 6,
            transcendentals=0,
        ),
        name="input_gradient",
    )(rows, gains8, *d_pre, *weights, d_x1)


def update(weight, momentum, average, gradient, step_rate):
    new_momentum = momentum_decay * momentum + gradient
    direction = gradient + momentum_decay * new_momentum + weight_decay * weight
    new_weight = weight - step_rate * direction
    new_average = average_decay * average + (1.0 - average_decay) * new_weight
    return (new_momentum, new_average, new_weight)


def update_kernel(pick, step_rate, sum_count, core_ref, w_ref, m_ref, a_ref, *refs):
    sums, outs, dots_ref = refs[:sum_count], refs[-4:-1], refs[-1]
    weight = w_ref[...]
    gradient = pick(core_ref[0], *[s[...] for s in sums]).astype(wide).reshape(weight.shape)
    results = update(weight, m_ref[...], a_ref[...], gradient, step_rate)
    for out, result in zip(outs, results):
        out[...] = result
    product = weight.astype(low).astype(wide) * gradient
    total = product[..., :HEAD_DIM]
    for start in range(HEAD_DIM, product.shape[-1], HEAD_DIM):
        total = total + product[..., start : start + HEAD_DIM]
    dots_ref[...] = total.reshape(dots_ref.shape)


def update_call(
    core, state, sums, grid, state_spec, sum_specs, pick, step_rate, name, before=()
):
    struct = jax.ShapeDtypeStruct(state[0].shape, wide)
    size = math.prod(state[0].shape)
    rows = state_spec.block_shape[-2]
    steps = math.prod(grid)
    tail = grid[1:]

    def dots_index(*indices):
        place = indices[0]
        for length, index in zip(tail, indices[1:]):
            place = place * length + index
        return (place, 0, 0)

    return pl.pallas_call(
        functools.partial(update_kernel, pick, step_rate, len(sums)),
        grid_spec=pltpu.PrefetchScalarGridSpec(
            num_scalar_prefetch=1,
            grid=grid,
            in_specs=[state_spec] * 3
            + sum_specs
            + [pl.BlockSpec(memory_space=pl.ANY)] * len(before),
            out_specs=[state_spec] * 3 + [pl.BlockSpec((1, rows, HEAD_DIM), dots_index)],
        ),
        out_shape=[struct] * 3 + [jax.ShapeDtypeStruct((steps, rows, HEAD_DIM), wide)],
        input_output_aliases={4 + len(sums) + k: k for k in range(len(before))},
        compiler_params=pltpu.CompilerParams(vmem_limit_bytes=VMEM_BYTES),
        cost_estimate=pl.CostEstimate(flops=12 * size, bytes_accessed=26 * size, transcendentals=0),
        name=name,
    )(core, *state, *sums, *before)


def update_attention_kernel(
    pick, step_rate, gain_step, core_ref, w_ref, m_ref, a_ref, qfv_ref, out_ref, *refs
):
    if gain_step is None:
        update_kernel(pick, step_rate, 2, core_ref, w_ref, m_ref, a_ref, qfv_ref, out_ref, *refs)
        return
    *held, dots_s = refs
    own_dots, up_dots, gate_dots, g_ref, gm_ref, ga_ref = held[:6]
    outs, gain_outs = held[-6:-3], held[-3:]
    kind = pl.program_id(0)
    dots = dots_s.at[kind]
    update_kernel(
        pick, step_rate, 2, core_ref, w_ref, m_ref, a_ref, qfv_ref, out_ref, *outs, dots
    )

    @pl.when(kind == pl.num_programs(0) - 1)
    def _():
        shard = dots_s.shape[1]
        sums = [own_dots[k] + dots_s[k] for k in range(4)]
        two = (up_dots[...] + gate_dots[...]).reshape(shard, HEAD_DIM)
        columns = [
            jnp.sum(total, axis=1, keepdims=True) for total in (sums[0] + sums[1] + sums[2], sums[3], two)
        ]
        lanes = lax.broadcasted_iota(jnp.int32, (shard, HEAD_DIM), 1)
        table = jnp.where(lanes == 1, columns[1], columns[2])
        table = jnp.where(lanes == 0, columns[0], table)
        gain = g_ref[...]
        gradient = table.T[:3, :] / gain.astype(low).astype(wide)
        results = update(gain, gm_ref[...], ga_ref[...], gradient, gain_step)
        for out, result in zip(gain_outs, results):
            out[...] = result


def update_attention(half_ref, state, qfv, out, step_rate, gains=None):
    _, shard, width = state[0].shape
    down_rows = out.shape[0] - shard

    def pick(core_index, proj, last):
        gradient = last[down_rows:].astype(wide)
        for kind in range(3):
            parts = [proj[pair * shard :, kind * PAIR :][:shard, :PAIR] for pair in range(2)]
            chosen = jnp.concatenate(parts, axis=1).astype(wide)
            gradient = jnp.where(pl.program_id(0) == kind, chosen, gradient)
        return gradient

    struct = jax.ShapeDtypeStruct
    state_spec = pl.BlockSpec((1, shard, width // 2), lambda kind, half: (kind, 0, half[0]))
    in_specs = [state_spec] * 3 + [whole(qfv.shape), whole(out.shape)]
    out_specs = [state_spec] * 3
    out_shape = [struct(state[0].shape, wide)] * 3
    operands = [half_ref, *state, qfv, out]
    aliases, scratch, gain_step = {}, [], None
    if gains is None:
        out_specs += [pl.BlockSpec((1, shard, HEAD_DIM), lambda kind, half: (kind, 0, 0))]
        out_shape += [struct((4, shard, HEAD_DIM), wide)]
    else:
        before, dots, gain_state, gain_step = gains
        in_specs += [whole(part.shape) for part in (*dots, *gain_state)]
        operands += [*dots, *gain_state]
        aliases = {len(operands) + k: k for k in range(3)}
        in_specs += [pl.BlockSpec(memory_space=pl.ANY)] * 3
        operands += list(before)
        out_specs += [whole(gain_state[0].shape)] * 3
        out_shape += [struct(gain_state[0].shape, wide)] * 3
        scratch = [pltpu.VMEM((4, shard, HEAD_DIM), wide)]
    size = math.prod(state[0].shape) // 2
    return pl.pallas_call(
        functools.partial(update_attention_kernel, pick, step_rate, gain_step),
        grid_spec=pltpu.PrefetchScalarGridSpec(
            num_scalar_prefetch=1,
            grid=(4,),
            in_specs=in_specs,
            out_specs=out_specs,
            scratch_shapes=scratch,
        ),
        out_shape=out_shape,
        input_output_aliases=aliases,
        compiler_params=pltpu.CompilerParams(vmem_limit_bytes=VMEM_BYTES),
        cost_estimate=pl.CostEstimate(flops=12 * size, bytes_accessed=26 * size, transcendentals=0),
        name="update_attention",
    )(*operands)


def update_ffn_in(kind_ref, state, totals, step_rate, before):
    _, shard, hidden = state[0].shape
    blocks_of = 4 if shard % 64 == 0 else 2
    block = shard // blocks_of

    def pick(_, even, odd):
        blocks = []
        for start in range(0, hidden // 2, HEAD_DIM):
            blocks += [even[:, start : start + HEAD_DIM], odd[:, start : start + HEAD_DIM]]
        return jnp.concatenate(blocks, axis=1)

    return update_call(
        kind_ref,
        state,
        totals,
        (blocks_of,),
        pl.BlockSpec((1, block, hidden), lambda j, kind: (kind[0], j, 0)),
        [pl.BlockSpec((block, hidden // 2), lambda j, _: (j, 0))] * 2,
        pick,
        step_rate,
        "update_ffn_in",
        before,
    )


def update_ffn_out(core, state, sums, step_rate):
    shard, width = state[0].shape
    half = width // 2
    block = shard // 2 if shard % 32 == 0 else shard

    def pick(core_index, mine, other):
        own = pl.program_id(0) == core_index
        return jnp.where(own, mine.astype(wide), other.astype(wide))

    sum_spec = pl.BlockSpec((block, half), lambda j, r, _: (r, 0))
    return update_call(
        core,
        state,
        sums,
        (2, shard // block),
        pl.BlockSpec((block, half), lambda j, r, _: (r, j)),
        [sum_spec, sum_spec],
        pick,
        step_rate,
        "update_ffn_out",
    )


def pack_kernel(core_ref, w_ref, out_ref):
    half = w_ref.shape[2]
    for pair in range(half // PAIR):
        for kind in range(3):
            start = (pair * 3 + kind) * PAIR
            piece = w_ref[kind, :, pair * PAIR : (pair + 1) * PAIR]
            out_ref[:, start : start + PAIR] = piece.astype(low)
    out_ref[:, 3 * half : 4 * half] = w_ref[3].astype(low)


def pack_attention(core, weights):
    _, shard, width = weights.shape
    half = width // 2
    return pl.pallas_call(
        pack_kernel,
        grid_spec=pltpu.PrefetchScalarGridSpec(
            num_scalar_prefetch=1,
            grid=(1,),
            in_specs=[pl.BlockSpec((4, shard, half), lambda j, core: (0, 0, core[0]))],
            out_specs=whole((shard, 4 * half)),
        ),
        out_shape=jax.ShapeDtypeStruct((shard, 4 * half), low),
        name="pack_attention",
    )(core, weights)


RING = 8


def ring_place(index):
    return jnp.where(index % 2 == 0, index // 2, RING - 1 - index // 2)


def ring_member(place):
    place = place % RING
    return jnp.where(place < RING // 2, 2 * place, 2 * RING - 1 - 2 * place)


CYCLE = (0, 2, 4, 6, 7, 5, 3, 1)


def ring_next(tensor):
    replicas = lax.axis_size("dp")
    pairs = []
    for place_of, member in enumerate(CYCLE):
        for replica in range(replicas):
            target = CYCLE[(place_of + (1 if replica % 2 == 0 else -1)) % RING]
            pairs.append((member * replicas + replica, target * replicas + replica))
    return lax.ppermute(tensor, ("fsdp", "dp"), pairs)


def ring_shift(tensor, way):
    pairs = [(member, CYCLE[(at + way) % RING]) for at, member in enumerate(CYCLE)]
    return lax.ppermute(tensor, "fsdp", pairs)


def core_swap(tensor):
    return lax.ppermute(tensor, "dp", [(d, d ^ 1) for d in range(lax.axis_size("dp"))])


def column_swap(tensor):
    return lax.ppermute(tensor, "dp", [(d, d ^ 2) for d in range(lax.axis_size("dp"))])


def pack_all_kernel(
    core_ref, column_ref, w_ref, up_ref, other_ref, down_ref, g_ref, out_ref, across_ref
):
    across_ref[...] = other_ref[0].astype(low)
    shard = w_ref.shape[1]
    half = w_ref.shape[2]
    for pair in range(half // PAIR):
        for kind in range(3):
            start = (pair * 3 + kind) * PAIR
            piece = w_ref[kind, :, pair * PAIR : (pair + 1) * PAIR]
            out_ref[:, start : start + PAIR] = piece.astype(low)
    out_ref[:, 3 * half : 4 * half] = w_ref[3].astype(low)
    start = 4 * half
    out_ref[:, start : start + up_ref.shape[2]] = up_ref[0].astype(low)
    start += up_ref.shape[2]
    for first, count in down_parts(down_ref.shape[0], shard):
        out_ref[:count, start : start + half] = down_ref[first : first + count, :].astype(low)
        if count < shard:
            out_ref[count:, start : start + half] = jnp.zeros((shard - count, half), low)
            rows = lax.broadcasted_iota(jnp.int32, (GAIN_ROWS, g_ref.shape[1]), 0)
            gains = jnp.where(rows == 1, g_ref[1:2, :], g_ref[2:3, :])
            gains = jnp.where(rows == 0, g_ref[0:1, :], gains)
            gains = jnp.where(rows < 3, gains, 0.0).astype(low)
            out_ref[count : count + GAIN_ROWS, start : start + g_ref.shape[1]] = gains
        start += half


def down_parts(down_rows, shard):
    return [(start, min(shard, down_rows - start)) for start in range(0, down_rows, shard)]


def pack_all(core, column, weights, up, down, gains):
    _, shard, width = weights.shape
    half = width // 2
    parts = len(down_parts(down.shape[0], shard))
    columns = 4 * half + up.shape[2] // 2 + parts * half
    return pl.pallas_call(
        pack_all_kernel,
        grid_spec=pltpu.PrefetchScalarGridSpec(
            num_scalar_prefetch=2,
            grid=(1,),
            in_specs=[
                pl.BlockSpec((4, shard, half), lambda j, core, column: (0, 0, core[0])),
                pl.BlockSpec(
                    (1, shard, up.shape[2] // 2), lambda j, core, column: (core[0], 0, column[0])
                ),
                pl.BlockSpec(
                    (1, shard, up.shape[2] // 2),
                    lambda j, core, column: (core[0], 0, 1 - column[0]),
                ),
                pl.BlockSpec((down.shape[0], half), lambda j, core, column: (0, core[0])),
                whole(gains.shape),
            ],
            out_specs=[whole((shard, columns)), whole((shard, up.shape[2] // 2))],
        ),
        out_shape=[
            jax.ShapeDtypeStruct((shard, columns), low),
            jax.ShapeDtypeStruct((shard, up.shape[2] // 2), low),
        ],
        compiler_params=pltpu.CompilerParams(vmem_limit_bytes=VMEM_BYTES),
        name="pack_all",
    )(core, column, weights, up, up, down, gains)


def place_kernel(which, kept, shapes, origin_ref, column_ref, *refs):
    pieces, outs, semaphores = refs[: len(which)], refs[-1 - len(kept) : -1], refs[-1]
    targets = dict(zip(kept, outs))
    shard, first, up_columns, down_rows, half = shapes
    copies = []

    def copy(source, target):
        copies.append(pltpu.make_async_copy(source, target, semaphores.at[len(copies)]))

    for piece, (origin, across) in zip(pieces, which):
        owner = origin_ref[origin]
        rows = pl.ds(pl.multiple_of(owner * shard, 16), shard)
        if across:
            copy(piece, targets[1].at[rows, lanes_of(1 - column_ref[0], up_columns)])
            continue
        copy(piece.at[:, pl.ds(0, first)], targets[0].at[rows, :])
        own = targets[1].at[rows, lanes_of(column_ref[0], up_columns)]
        copy(piece.at[:, pl.ds(first, up_columns)], own)
        lane = first + up_columns
        for start, count in down_parts(down_rows, shard):
            target = pl.ds(pl.multiple_of(owner * down_rows + start, 16), count)
            copy(piece.at[pl.ds(0, count), pl.ds(lane, half)], targets[2].at[target, :])
            if count < shard:
                source = piece.at[pl.ds(count, GAIN_ROWS), pl.ds(lane, shard)]
                copy(source, targets[3].at[:, lanes_of(owner, shard)])
            lane += half
    for one in copies:
        one.start()
    for one in copies:
        one.wait()


def place(origins, column, which, pieces, arrays, kept, shapes):
    anywhere = pl.BlockSpec(memory_space=pl.ANY)
    shard, first, up_columns, down_rows, half = shapes
    kinds = [(RING * shard, first), (RING * shard, 2 * up_columns), (RING * down_rows, half)]
    kinds.append((GAIN_ROWS, RING * shard))
    held = [] if arrays is None else list(arrays)
    size = sum(math.prod(piece.shape) for piece in pieces)
    before = 2 + len(pieces)
    return pl.pallas_call(
        functools.partial(place_kernel, which, kept, shapes),
        grid_spec=pltpu.PrefetchScalarGridSpec(
            num_scalar_prefetch=2,
            grid=(1,),
            in_specs=[whole(piece.shape) for piece in pieces] + [anywhere] * len(held),
            out_specs=[anywhere] * len(kept),
            scratch_shapes=[pltpu.SemaphoreType.DMA((8 * len(pieces),))],
        ),
        out_shape=[jax.ShapeDtypeStruct(kinds[k], pieces[0].dtype) for k in kept],
        input_output_aliases={before + k: k for k in range(len(held))},
        compiler_params=pltpu.CompilerParams(vmem_limit_bytes=VMEM_BYTES),
        cost_estimate=pl.CostEstimate(flops=0, bytes_accessed=8 * size, transcendentals=0),
        name="place",
    )(origins, column, *pieces, *held)


def after(tensor, *others):
    return lax.optimization_barrier((tensor, *others))[0]


def core_way():
    return 1 - 2 * (lax.axis_index("dp") % 2)


def ring_origins():
    steps = jnp.array((0, -1, -2, -3, -4, 1, 2, 3), jnp.int32)
    return ring_member(ring_place(lax.axis_index("fsdp")) + steps + RING).astype(jnp.int32)


class RingSumOverColumns:
    def __init__(self, mine, arrived):
        self.arrays = (mine, arrived)
        place = ring_place(lax.axis_index("fsdp"))
        self.rows = mine.shape[1] // RING
        self.starts = [
            ring_member(place - core_way() * (s + 1) + 2 * RING) * self.rows for s in range(RING)
        ]
        self.sent, self.came, self.totals = [], [], []

    def part(self, side, step):
        shape = (1, self.rows, self.arrays[0].shape[2])
        parts = [
            lax.dynamic_slice(array, (side, self.starts[step], 0), shape)[0]
            for array in self.arrays
        ]
        return parts[0].astype(wide) + parts[1].astype(wide)

    def cross(self):
        self.sent.append(self.part(1, len(self.sent)).astype(low))
        self.came.append(column_swap(self.sent[-1]))

    def term(self):
        step = len(self.totals)
        return self.part(0, step) + self.came[step].astype(wide)

    def begin(self, *others):
        self.came[0] = after(self.came[0], *others) if others else self.came[0]
        self.totals.append(self.term().astype(low))

    def step(self, arriving=()):
        total, ahead = self.totals[-1], self.came[len(self.totals)]
        moved = ring_next(after(total, ahead) if len(self.totals) > 1 else total)
        moved = after(moved, *arriving) if arriving else moved
        self.totals.append((moved.astype(wide) + self.term()).astype(low))

    def last(self):
        return self.totals[-1]


class RingSum:
    def __init__(self, mine, arrived):
        self.mine, self.arrived = mine, arrived
        place = ring_place(lax.axis_index("fsdp"))
        self.owners = [ring_member(place - core_way() * (s + 1) + 2 * RING) for s in range(RING)]
        self.totals = []

    def term(self):
        parts = []
        for own, arrived in zip(self.mine, self.arrived):
            rows = own.shape[0] // RING
            start = self.owners[len(self.totals)] * rows
            part = lax.dynamic_slice_in_dim(own, start, rows, 0).astype(wide)
            parts.append(part + lax.dynamic_slice_in_dim(arrived, start, rows, 0).astype(wide))
        return parts[0] if len(parts) == 1 else jnp.concatenate(parts, axis=0)

    def begin(self, *others):
        if others:
            self.mine = [after(self.mine[0], *others), *self.mine[1:]]
        self.totals.append(self.term().astype(low))

    def step(self, *before, arriving=()):
        total = self.totals[-1]
        moved = ring_next(after(total, *before) if before else total)
        moved = after(moved, *arriving) if arriving else moved
        self.totals.append((moved.astype(wide) + self.term().astype(wide)).astype(low))

    def last(self):
        return self.totals[-1]


def gather_rows(shard):
    mine = lax.all_gather(shard, "fsdp", axis=0, tiled=True)
    return mine, core_swap(mine)


def core_sum(mine, other):
    return (mine.astype(wide) + core_swap(other).astype(wide)).astype(low)


def scatter_rows(both):
    return lax.psum_scatter(both, "fsdp", scatter_dimension=0, tiled=True)


def over_columns(total):
    total = (total.astype(wide) + column_swap(total).astype(wide)).astype(low)
    return total, core_swap(total)


def on_device(
    inputs,
    cotangent,
    lengths,
    attention_weights,
    attention_momentum,
    attention_average,
    ffn_inputs,
    ffn_inputs_momentum,
    ffn_inputs_average,
    ffn_output,
    ffn_output_momentum,
    ffn_output_average,
    gains,
    gains_momentum,
    gains_average,
):
    micro_count, slot, width = inputs.shape
    hidden = ffn_inputs.shape[2]
    shard, down_rows = ffn_inputs.shape[1], ffn_output.shape[0]
    fsdp_size = lax.axis_size("fsdp")
    replicas = lax.axis_size("dp")
    ringed = fsdp_size == RING
    core = lax.axis_index("dp") % 2
    column = lax.axis_index("dp") // 2
    count = micro_count * slot
    half = width // 2
    core_ref = core.astype(jnp.int32).reshape(1)
    other_ref = 1 - core_ref
    column_ref = column.astype(jnp.int32).reshape(1)
    is_first = core == 0

    rows = inputs.reshape(count, width)
    n1t = norm_rows(rows)
    positions = jnp.arange(slot, dtype=jnp.int32)
    valid = (positions[None, :] < lengths).astype(wide).reshape(count, 1)
    errors = (cotangent.reshape(count, width).astype(wide) * valid).astype(low)

    if ringed:
        origins = ring_origins()
        first = 4 * half
        shapes = (shard, first, hidden // 2, down_rows, half)
        packed, own_across = pack_all(
            core_ref, column_ref, attention_weights, ffn_inputs, ffn_output, gains
        )
        wholes, there, which_there = None, [own_across], [(0, True)]
        here, which = [packed], [(0, False)]
        for step in range(1, 6):
            if step <= 3:
                onward = [ring_shift(here[0], 1), ring_shift(here[-1], -1)]
            elif step == 4:
                onward = [ring_next(jnp.where(is_first, *here))]
            across = []
            if step > 1:
                across = [column_swap(piece[:, first : first + hidden // 2]) for piece in here]
            wholes = place(
                origins, column_ref, which + which_there, here + there, wholes, (0, 1, 2, 3), shapes
            )
            if step == 5:
                break
            extra = [errors, n1t] if step == 2 else []
            tied = list(lax.optimization_barrier((*onward, *across, *wholes, *extra)))
            here, rest = tied[: len(onward)], tied[len(onward) :]
            there, wholes = rest[: len(across)], rest[len(across) : len(across) + 4]
            which_there = [(origin, True) for origin, _ in which] if across else []
            which = [(origin, False) for origin in [step, step + 4][: len(onward)]]
        w_a, gain_rows = (wholes[0], core_swap(wholes[0])), wholes[3]
    else:
        w_a = gather_rows(pack_attention(core_ref, attention_weights))
        gain_rows = lax.all_gather(gains.astype(low), "fsdp", axis=1, tiled=True)
        gain_rows = jnp.pad(gain_rows, ((0, GAIN_ROWS - 3), (0, 0)))
        w_gu = gather_rows(
            lax.dynamic_index_in_dim(ffn_inputs, core, 0, keepdims=False).astype(low)
        )
        w_d = gather_rows(lax.dynamic_slice_in_dim(ffn_output, core * half, half, 1).astype(low))
    mixed_mine, *kept_mine, gains8 = mixer_forward(core_ref, rows, w_a[0], slot, gain_rows)
    if ringed:
        (across,) = lax.optimization_barrier((*across, mixed_mine, w_a[1]))[:1]
        (w_gu_mine,) = place(origins, column_ref, [(4, True)], [across], [wholes[1]], (1,), shapes)
        wholes = [wholes[0], w_gu_mine, wholes[2], wholes[3]]
        rows = after(rows, *wholes[1:3])
        w_gu, w_d = [(array, core_swap(array)) for array in wholes[1:3]]
    mixed_other, *rest = mixer_forward(
        other_ref, rows, w_a[1], slot, None, (gains8, mixed_mine, w_a[0])
    )
    kept_other, (x1, h2, h2t) = rest[:4], rest[4:]
    owners = (RING, down_rows + shard, down_rows)
    if not ringed:
        owners = (1, hidden + width, hidden)
    places = jnp.concatenate([core_ref, column_ref])
    *grad_gu, gd_mine, gd_other, output, d_x1, d_mixed = ffn(
        places, h2, h2t, errors, w_gu, w_d, x1, (mixed_mine, mixed_other), w_a, lengths[:, 0], gains8, owners
    )

    gm, gu = grad_gu
    arrived_gu = core_swap(gu)
    mine_do, arrived_do = [gd_mine], [core_swap(gd_other)]
    by_owner = (fsdp_size * 2 * shard, 3 * PAIR)
    d_pre = []
    for call in range(4):
        from_half, kept = (other_ref, kept_other) if call < 2 else (core_ref, kept_mine)
        if ringed and call == 1:
            sum_gu = RingSumOverColumns(after(gm, d_pre[0]), arrived_gu)
            sum_gu.cross()
            sum_gu.cross()
            n1t = after(n1t, *sum_gu.sent)
        elif ringed and call > 1:
            sum_gu.cross()
            ahead = [sum_gu.came[2]] if call == 3 else []
            n1t = after(n1t, sum_gu.last(), sum_do.last(), sum_gu.sent[-1], *ahead)
        grads = mixer_backward(
            from_half,
            n1t,
            gains8,
            kept,
            d_mixed,
            slot,
            shard,
            (call % 2,),
            grads if call % 2 else (),
        )
        d_pre.append(grads[1])
        if call == 1:
            grad_other = grads[0]
            if ringed:
                sum_do = RingSum(mine_do, arrived_do)
                sum_do.begin(d_pre[-1])
                sum_gu.begin(d_pre[-1])
                grad_other = after(grad_other, sum_gu.last(), sum_do.last())
            arrived_qfv = [core_swap(grad_other.reshape(by_owner))]
        elif ringed and call > 1:
            gate = d_pre[-1]
            if call == 3:
                sum_qfv = RingSum([grads[0].reshape(by_owner)], arrived_qfv)
                sum_qfv.begin()
                gate = sum_qfv.last()
            sum_do.step(arriving=(gate,))
            sum_gu.step(arriving=(gate,))
    mine_qfv = [grads[0].reshape(by_owner)]

    def finish_input(*others):
        late = after(d_pre[3], *others) if others else d_pre[3]
        return input_gradient(rows, gains8, (late, d_pre[1]), w_a, d_x1)

    if ringed:
        input_grad = None
        for step in range(1, RING - 1):
            if len(sum_gu.came) < RING:
                sum_gu.cross()
            if len(sum_gu.totals) < RING:
                first = [sum_gu.last(), sum_qfv.last()]
                sum_do.step(*{1: first, 4: [input_grad]}.get(step, []))
                sum_gu.step()
            sum_qfv.step()
            if step == 2:
                input_grad = finish_input(sum_qfv.last(), sum_gu.came[5])
        total_gu, total_do = sum_gu.last(), sum_do.last()
    else:
        both = (gm.astype(wide) + arrived_gu.astype(wide)).astype(low)
        here = (both[0].astype(wide) + column_swap(both[1]).astype(wide)).astype(low)
        total_gu = scatter_rows(here)
        both = (gd_mine.astype(wide) + arrived_do[0].astype(wide)).astype(low)
        total_do = jnp.concatenate(
            [scatter_rows(both[:hidden]), scatter_rows(both[hidden:])], axis=0
        )
        total_qfv = scatter_rows(
            (mine_qfv[0].astype(wide) + arrived_qfv[0].astype(wide)).astype(low)
        )
        input_grad = finish_input()
    scale_rows = 1.0 / math.sqrt(count * fsdp_size * replicas)
    matrix_step = matrix_rate * scale_rows
    attention_state = (attention_weights, attention_momentum, attention_average)
    ffn_in_state = (ffn_inputs, ffn_inputs_momentum, ffn_inputs_average)
    ffn_out_state = (ffn_output, ffn_output_momentum, ffn_output_average)
    sum_do = over_columns(total_do)
    there = column_swap(total_gu)
    even = jnp.where(column == 0, total_gu, there)
    odd = jnp.where(column == 0, there, total_gu)
    sum_gu = (even, odd), (core_swap(even), core_swap(odd))
    *new_out, _ = update_ffn_out(core_ref, ffn_out_state, sum_do, matrix_step)
    *new_in, dots_up = update_ffn_in(core_ref, ffn_in_state, sum_gu[0], matrix_step, ())
    *new_in, dots_gate = update_ffn_in(other_ref, ffn_in_state, sum_gu[1], matrix_step, new_in)
    if ringed:
        sum_qfv.step(arriving=(new_out[0],))
        total_qfv = sum_qfv.last()
    there = after(column_swap(total_qfv), new_in[0])
    sum_qfv = (total_qfv.astype(wide) + there.astype(wide)).astype(low)
    *own, dots_own = update_attention(
        core_ref, attention_state, sum_qfv, sum_do[0], matrix_step
    )
    theirs = after(core_swap(sum_qfv), own[0])
    gain_state = (gains, gains_momentum, gains_average)
    *new_attention, gains_m, gains_a, gains_w = update_attention(
        other_ref,
        attention_state,
        theirs,
        sum_do[1],
        matrix_step,
        (own, (dots_own, dots_up, dots_gate), gain_state, gain_rate * scale_rows),
    )
    return (
        output.reshape(micro_count, slot, width),
        input_grad.reshape(micro_count, slot, width),
        *new_attention,
        *new_in,
        *new_out,
        gains_m,
        gains_a,
        gains_w,
    )


def solution(mesh):
    rows_split = P(None, ("fsdp", "dp"), None)
    middle_split = P(None, "fsdp", None)
    first_split = P("fsdp", None)
    gains_split = P(None, "fsdp")
    in_specs = (
        (rows_split, rows_split, P(None, ("fsdp", "dp")))
        + (middle_split,) * 6
        + (first_split,) * 3
        + (gains_split,) * 3
    )
    out_specs = (
        (rows_split, rows_split)
        + (middle_split,) * 6
        + (first_split,) * 3
        + (gains_split,) * 3
    )
    return jax.shard_map(
        on_device, mesh=mesh, in_specs=in_specs, out_specs=out_specs, check_vma=False
    )
```

```python
import functools
import math

import jax
import jax.numpy as jnp
from jax import lax
from jax.experimental import pallas as pl
from jax.experimental.pallas import tpu as pltpu
from jax.sharding import PartitionSpec as P

HEAD_DIM = 128
PAIR = 2 * HEAD_DIM
GAIN_ROWS = 16

lower_bound = 0.9
momentum_decay = 0.9
average_decay = 0.7
weight_decay = 0.0005
matrix_rate = 0.03
gain_rate = 0.1
low = jnp.bfloat16
wide = jnp.float32
TILE_F = 256
VMEM_BYTES = 60 * 1024 * 1024


def mm(left, right):
    return jnp.dot(left, right, preferred_element_type=wide)


def mm_nt(left, right):
    return lax.dot_general(left, right, (((1,), (1,)), ((), ())), preferred_element_type=wide)


def mm_tn(left, right):
    return lax.dot_general(left, right, (((0,), (0,)), ((), ())), preferred_element_type=wide)


def sigmoid(u):
    return 0.5 * jnp.tanh(0.5 * u) + 0.5


def whole(shape):
    return pl.BlockSpec(shape, lambda *_: (0,) * len(shape), pipeline_mode=pl.Buffered(1))


def split_sum(ones_matrix, tensor):
    high = tensor.astype(low)
    rest = (tensor - high.astype(wide)).astype(low)
    return mm(ones_matrix, high) + mm(ones_matrix, rest)


def causal_mask(length, lower):
    rows = lax.broadcasted_iota(jnp.int32, (length, length), 0)
    columns = lax.broadcasted_iota(jnp.int32, (length, length), 1)
    return rows >= columns if lower else rows <= columns


def triangle(length, lower):
    return causal_mask(length, lower).astype(wide).astype(low)


def decay_parts(f_pre, lower_ones):
    share = sigmoid(f_pre)
    gate = lower_bound + (1.0 - lower_bound) * share
    keys_in = (1.0 - lower_bound) * (1.0 - share)
    cumulative = split_sum(lower_ones, jnp.log(gate))
    middle_row = cumulative.shape[0] // 2
    cumulative = cumulative - cumulative[middle_row : middle_row + 1, :]
    return share, gate, keys_in, cumulative


def first_norm(x_ref, gain_row):
    rows = x_ref[...].astype(wide)
    scale = lax.rsqrt(jnp.mean(rows * rows, axis=-1, keepdims=True) + 1e-06)
    return rows * scale, scale


def lanes_of(half, size):
    return pl.ds(pl.multiple_of(half * size, size), size)


def mixer_forward_first_kernel(
    slot, half_ref, x_ref, w_ref, gains_ref, on_ref, q_ref, f_ref, v_ref, o_ref, g_ref, h_s
):
    @pl.when(pl.program_id(0) == 0)
    def _():
        g_ref[...] = gains_ref[...].astype(wide)[: g_ref.shape[0], :]

    mixer_forward_kernel(
        slot, half_ref, x_ref, w_ref, g_ref, on_ref, q_ref, f_ref, v_ref, o_ref, h_s
    )


def mixer_forward_kernel(
    slot, half_ref, x_ref, w_ref, g_ref, on_ref, q_ref, f_ref, v_ref, o_ref, h_s
):
    @pl.when(pl.program_id(0) == 0)
    def _():
        normed, _ = first_norm(x_ref, None)
        h_s[...] = (normed * g_ref[0:1, :]).astype(low)

    gain_o = g_ref[1:2, lanes_of(half_ref[0] * pl.num_programs(0) + pl.program_id(0), PAIR)]
    pre = mm(h_s[...], w_ref[...])
    q_ref[...] = pre[:, :PAIR]
    f_ref[...] = pre[:, PAIR : 2 * PAIR]
    v_ref[...] = pre[:, 2 * PAIR :].astype(low)
    lower_ones = triangle(slot, True)
    causal = causal_mask(slot, True)
    for sequence in range(x_ref.shape[0] // slot):
        rows = slice(sequence * slot, (sequence + 1) * slot)
        q_pre = q_ref[rows, :]
        _, _, keys_in, cumulative = decay_parts(f_ref[rows, :], lower_ones)
        grown = jnp.exp(-cumulative)
        decayed_q = (q_pre * sigmoid(q_pre) * jnp.exp(cumulative)).astype(low)
        grown_k = (keys_in * grown).astype(low)
        values = v_ref[rows, :]
        for head in range(2):
            lanes = slice(head * HEAD_DIM, (head + 1) * HEAD_DIM)
            scores = mm_nt(decayed_q[:, lanes], grown_k[:, lanes])
            out = mm(jnp.where(causal, scores, 0.0).astype(low), values[:, lanes])
            scale = lax.rsqrt(jnp.mean(out * out, axis=-1, keepdims=True) + 1e-05)
            o_ref[rows, lanes] = out.astype(low)
            on_ref[rows, lanes] = (out * scale * gain_o[:, lanes]).astype(low)


def mixer_forward_last_kernel(
    slot,
    half_ref,
    x_ref,
    w_ref,
    g_ref,
    before_hbm,
    woo_hbm,
    wom_hbm,
    on_ref,
    q_ref,
    f_ref,
    v_ref,
    o_ref,
    x1_hbm,
    h2_ref,
    h2t_ref,
    h_s,
    on_s,
    x1_s,
    wo_s,
    semaphores,
):
    step = pl.program_id(0)
    half = before_hbm.shape[1]
    here, there = lanes_of(half_ref[0], half), lanes_of(1 - half_ref[0], half)
    sources = (
        (before_hbm, on_s.at[:, there]),
        (woo_hbm.at[:, pl.ds(3 * half, half)], wo_s.at[:, here]),
        (wom_hbm.at[:, pl.ds(3 * half, half)], wo_s.at[:, there]),
    )
    fetches = [
        pltpu.make_async_copy(source, target, semaphores.at[number])
        for number, (source, target) in enumerate(sources)
    ]

    @pl.when(step == 0)
    def _():
        for fetch in fetches:
            fetch.start()

    mixer_forward_kernel(
        slot, half_ref, x_ref, w_ref, g_ref, on_ref, q_ref, f_ref, v_ref, o_ref, h_s
    )
    on_s[:, lanes_of(half_ref[0] * pl.num_programs(0) + step, PAIR)] = on_ref[...]

    @pl.when(step == pl.num_programs(0) - 1)
    def _():
        for fetch in fetches:
            fetch.wait()
        x1 = x_ref[...].astype(wide) + mm(on_s[...], wo_s[...])
        x1_s[...] = x1
        leaving = pltpu.make_async_copy(x1_s, x1_hbm, semaphores.at[3])
        leaving.start()
        scale = lax.rsqrt(jnp.mean(x1 * x1, axis=-1, keepdims=True) + 1e-06)
        normed = x1 * scale * g_ref[2:3, :]
        h2_ref[...] = normed.astype(low)
        h2t_ref[...] = normed.T.astype(low)
        leaving.wait()


def norm_rows_kernel(x_ref, out_ref):
    normed, _ = first_norm(x_ref, None)
    out_ref[...] = normed.T.astype(low)


def norm_rows(rows):
    count, width = rows.shape
    return pl.pallas_call(
        norm_rows_kernel,
        in_specs=[pl.BlockSpec(memory_space=pltpu.VMEM)],
        out_specs=pl.BlockSpec(memory_space=pltpu.VMEM),
        out_shape=jax.ShapeDtypeStruct((width, count), low),
        compiler_params=pltpu.CompilerParams(vmem_limit_bytes=VMEM_BYTES),
        name="norm_rows",
    )(rows)


def mixer_forward(half, rows, weights, slot, gains=None, ending=None):
    count, width = rows.shape
    pairs = width // PAIR // 2
    by_pair = pl.BlockSpec((count, PAIR), lambda j, _: (0, j))
    struct = jax.ShapeDtypeStruct
    shape = lambda kind: struct((count, width // 2), kind)
    in_specs = [whole(rows.shape), pl.BlockSpec((width, 3 * PAIR), lambda j, _: (0, j))]
    operands = [half, rows, weights]
    out_specs = [by_pair] * 5
    out_shape = [shape(low), shape(wide), shape(wide), shape(low), shape(low)]
    scratch = [pltpu.VMEM((count, width), low)]
    if ending is None:
        kernel = mixer_forward_first_kernel
        in_specs += [whole(gains.shape)]
        operands += [gains]
        out_specs += [whole((8, width))]
        out_shape += [struct((8, width), wide)]
    if ending is not None:
        kernel = mixer_forward_last_kernel
        anywhere = pl.BlockSpec(memory_space=pl.ANY)
        in_specs += [whole(ending[0].shape), anywhere, anywhere, anywhere]
        operands += [ending[0], ending[1], weights, ending[2]]
        out_specs += [anywhere, whole((count, width)), whole((width, count))]
        out_shape += [
            struct((count, width), wide),
            struct((count, width), low),
            struct((width, count), low),
        ]
        scratch += [
            pltpu.VMEM((count, width), low),
            pltpu.VMEM((count, width), wide),
            pltpu.VMEM((width, width), low),
            pltpu.SemaphoreType.DMA((4,)),
        ]
    return pl.pallas_call(
        functools.partial(kernel, slot),
        grid_spec=pltpu.PrefetchScalarGridSpec(
            num_scalar_prefetch=1,
            grid=(pairs,),
            in_specs=in_specs,
            out_specs=out_specs,
            scratch_shapes=scratch,
        ),
        out_shape=out_shape,
        compiler_params=pltpu.CompilerParams(vmem_limit_bytes=VMEM_BYTES),
        cost_estimate=pl.CostEstimate(
            flops=count * width * 4 * width + 10 * count * slot * width,
            bytes_accessed=count * width * 12 + width * width * 4,
            transcendentals=count * width * 3,
        ),
        name="mixer_forward",
    )(*operands)


def store_down(out_ref, tile, owners):
    _, stride, down_rows = owners
    block = math.gcd(down_rows, tile.shape[0])
    first = pl.program_id(0) * (tile.shape[0] // block)
    for part in range(tile.shape[0] // block):
        owner = (first + part) // (down_rows // block)
        inside = (first + part) % (down_rows // block)
        start = pl.multiple_of(owner * stride + inside * block, block)
        out_ref[pl.ds(start, block), :] = tile[part * block : (part + 1) * block, :]


def ffn_kernel(
    owners,
    core_ref,
    h_ref,
    ht_ref,
    e_ref,
    wm_ref,
    wu_ref,
    wdm_ref,
    wdo_ref,
    x1_hbm,
    onm_hbm,
    ono_hbm,
    wom_hbm,
    woo_hbm,
    m_ref,
    g_ref,
    gm_ref,
    gu_ref,
    gdm_hbm,
    gdo_hbm,
    out_hbm,
    dx1_hbm,
    don_hbm,
    *scratch,
):
    gu_w, gu_g, down_g, down_w, mid_s, dh_s, on_s, x1_s, wo_s, out_s, gdm_s, gdo_s = scratch[:12]
    in_semaphores, out_semaphores, down_semaphores = scratch[12:]
    step, last = pl.program_id(0), pl.num_programs(0) - 1
    half, tile = wdm_ref.shape[1], wm_ref.shape[1]
    mine, other = lanes_of(core_ref[0], half), lanes_of(1 - core_ref[0], half)
    kind, kind_other = lanes_of(core_ref[0], tile), lanes_of(1 - core_ref[0], tile)
    count, stride, down_rows = owners

    width = on_s.shape[1]
    sources = (
        (x1_hbm, x1_s),
        (onm_hbm, on_s.at[:, mine]),
        (ono_hbm, on_s.at[:, other]),
        (wom_hbm.at[:, pl.ds(3 * half, half)], wo_s.at[:, mine]),
        (woo_hbm.at[:, pl.ds(3 * half, half)], wo_s.at[:, other]),
    )
    fetches = [
        pltpu.make_async_copy(source, target, in_semaphores.at[number])
        for number, (source, target) in enumerate(sources)
    ]

    def down_copies(owner):
        rows = pl.ds(pl.multiple_of(owner * stride, math.gcd(stride, 32)), down_rows)
        return [
            pltpu.make_async_copy(held.at[rows, :], out.at[rows, :], down_semaphores.at[side, owner])
            for side, (held, out) in enumerate(((gdm_s, gdm_hbm), (gdo_s, gdo_hbm)))
        ]

    @pl.when(step == 0)
    def _():
        dh_s[...] = jnp.zeros_like(dh_s)
        for fetch in fetches:
            fetch.start()

    gu_w[:, kind] = wm_ref[...]
    gu_w[:, kind_other] = wu_ref[...]
    hidden_rows = pl.ds(pl.multiple_of(step * tile, tile), tile)
    down_w[hidden_rows, mine] = wdm_ref[...]
    down_w[hidden_rows, other] = wdo_ref[...]
    pre = mm(h_ref[...], gu_w[...])
    a, b = pre[:, :tile], pre[:, tile:]
    share = sigmoid(a)
    swish = a * share
    mid = (swish * b).astype(low)
    mid_s[:, lanes_of(step, tile)] = mid
    d_mid = mm_nt(e_ref[...], down_w[hidden_rows, :])
    down_g[...] = mm_tn(mid, e_ref[...]).astype(low)
    d_a = (d_mid * b * (share + swish * (1.0 - share))).astype(low)
    d_b = (d_mid * swish).astype(low)
    d_pre = jnp.concatenate([d_a, d_b], axis=1)
    dh_s[...] += mm_nt(d_pre, gu_w[...])
    gu_g[...] = mm(ht_ref[...], d_pre).astype(low)
    blocks = tile // HEAD_DIM
    for side, block in enumerate((core_ref[1], 1 - core_ref[1])):
        gm_ref[side] = gu_g[:, lanes_of(core_ref[0] * blocks + block, HEAD_DIM)]
        gu_ref[side] = gu_g[:, lanes_of((1 - core_ref[0]) * blocks + block, HEAD_DIM)]
    store_down(gdm_s, down_g[:, mine], owners)
    store_down(gdo_s, down_g[:, other], owners)

    done = (step + 1) * tile // down_rows

    @pl.when(done > step * tile // down_rows)
    def _():
        for copy in down_copies(done - 1):
            copy.start()

    @pl.when(step == last)
    def _():
        for fetch in fetches:
            fetch.wait()
        x1 = x1_s[...]
        x2 = x1 + mm(mid_s[...], down_w[...])
        positions = lax.broadcasted_iota(jnp.int32, (out_s.shape[0] // m_ref.shape[0], 1), 0)
        for sequence in range(m_ref.shape[0]):
            rows = slice(sequence * positions.shape[0], (sequence + 1) * positions.shape[0])
            valid = (positions < m_ref[sequence]).astype(wide)
            out_s[rows, :] = (x2[rows, :] * valid).astype(low)
        leaving = [pltpu.make_async_copy(out_s, out_hbm, out_semaphores.at[0])]
        leaving[-1].start()
        scale = lax.rsqrt(jnp.mean(x1 * x1, axis=-1, keepdims=True) + 1e-06)
        normed = x1 * scale
        scaled = dh_s[...] * g_ref[2:3, :]
        d_x1 = e_ref[...].astype(wide) + scale * (
            scaled - normed * jnp.mean(scaled * normed, axis=-1, keepdims=True)
        )
        dh_s[...] = d_x1
        leaving.append(pltpu.make_async_copy(dh_s, dx1_hbm, out_semaphores.at[1]))
        leaving[-1].start()
        d_1 = mid_s.at[:, pl.ds(0, width)]
        d_1[...] = d_x1.astype(low)
        d_mixed = mid_s.at[:, pl.ds(width, width)]
        d_mixed[...] = mm_nt(d_1[...], wo_s[...]).astype(low)
        leaving.append(pltpu.make_async_copy(d_mixed, don_hbm, out_semaphores.at[2]))
        leaving[-1].start()
        rows = stride - down_rows
        grad_o = mm_tn(on_s[...], d_1[...]).astype(low)
        down_w[pl.ds(0, width), :] = grad_o
        for columns, held, out in ((mine, gdm_s, gdm_hbm), (other, gdo_s, gdo_hbm)):
            for owner in range(count):
                target = slice(owner * stride + down_rows, (owner + 1) * stride)
                held[target, :] = down_w[owner * rows : (owner + 1) * rows, columns]
                copy = pltpu.make_async_copy(
                    held.at[target, :], out.at[target, :], out_semaphores.at[len(leaving)]
                )
                copy.start()
                leaving.append(copy)
        for owner in range(count):
            leaving += down_copies(owner)
        for copy in leaving:
            copy.wait()


def ffn(core, h2, h2t, errors, w_gu, w_d, x1, mixed, w_a, lengths, gains8, owners):
    count, width = h2.shape
    half = width // 2
    hidden = w_gu[0].shape[1]
    full = whole((count, width))
    in_tile = pl.BlockSpec((width, TILE_F), lambda j, _: (0, j))
    out_tile = pl.BlockSpec((TILE_F, half), lambda j, _: (j, 0))
    grad_tile = pl.BlockSpec((2, width, HEAD_DIM), lambda j, _: (0, 0, j))
    anywhere = pl.BlockSpec(memory_space=pl.ANY)
    down_shape = (owners[0] * owners[1], half)
    struct = jax.ShapeDtypeStruct
    vmem = pltpu.VMEM
    return pl.pallas_call(
        functools.partial(ffn_kernel, owners),
        grid_spec=pltpu.PrefetchScalarGridSpec(
            num_scalar_prefetch=1,
            grid=(hidden // TILE_F,),
            in_specs=[full, whole(h2t.shape), full, in_tile, in_tile, out_tile, out_tile]
            + [anywhere] * 5
            + [pl.BlockSpec(memory_space=pltpu.SMEM), whole((8, width))],
            out_specs=[grad_tile, grad_tile] + [anywhere] * 5,
            scratch_shapes=[
                vmem((width, 2 * TILE_F), low),
                vmem((width, 2 * TILE_F), low),
                vmem((TILE_F, width), low),
                vmem((hidden, width), low),
                vmem((count, hidden), low),
                vmem((count, width), wide),
                vmem((count, width), low),
                vmem((count, width), wide),
                vmem((width, width), low),
                vmem((count, width), low),
                vmem(down_shape, low),
                vmem(down_shape, low),
                pltpu.SemaphoreType.DMA((5,)),
                pltpu.SemaphoreType.DMA((3 + 2 * owners[0],)),
                pltpu.SemaphoreType.DMA((2, owners[0])),
            ],
        ),
        out_shape=[struct((2, width, hidden // 2), low)] * 2
        + [struct(down_shape, low)] * 2
        + [
            struct((count, width), low),
            struct((count, width), wide),
            struct((count, width), low),
        ],
        compiler_params=pltpu.CompilerParams(vmem_limit_bytes=VMEM_BYTES),
        cost_estimate=pl.CostEstimate(
            flops=18 * count * width * hidden,
            bytes_accessed=count * width * 20 + width * hidden * 12,
            transcendentals=count * hidden,
        ),
        name="ffn",
    )(core, h2, h2t, errors, *w_gu, *w_d, x1, *mixed, *w_a, lengths, gains8)


def mixer_backward_kernel(
    slot,
    per_half,
    first,
    half_ref,
    nt_hbm,
    g_ref,
    q_ref,
    f_ref,
    v_ref,
    o_ref,
    don_ref,
    *outs,
):
    grad_ref, dpre_hbm, nt_s, dpre_ref, semaphores = outs[-5:]
    fetch = pltpu.make_async_copy(nt_hbm, nt_s, semaphores.at[0])
    fetch.start()
    gain_o = g_ref[1:2, lanes_of(half_ref[0] * per_half + first + pl.program_id(0), PAIR)]
    lower_ones = triangle(slot, True)
    upper_ones = triangle(slot, False)
    causal_t = causal_mask(slot, False)
    for sequence in range(q_ref.shape[0] // slot):
        rows = slice(sequence * slot, (sequence + 1) * slot)
        d_on = don_ref[rows, :].astype(wide)
        out = o_ref[rows, :].astype(wide)
        d_out_parts = []
        for head in range(2):
            lanes = slice(head * HEAD_DIM, (head + 1) * HEAD_DIM)
            out_h, d_on_h = out[:, lanes], d_on[:, lanes]
            scale = lax.rsqrt(jnp.mean(out_h * out_h, axis=-1, keepdims=True) + 1e-05)
            normed = out_h * scale
            scaled = d_on_h * gain_o[:, lanes]
            inner = jnp.mean(scaled * normed, axis=-1, keepdims=True)
            d_out_parts.append((scale * (scaled - normed * inner)).astype(low))

        q_pre = q_ref[rows, :]
        share, gate, keys_in, cumulative = decay_parts(f_ref[rows, :], lower_ones)
        grown = jnp.exp(-cumulative)
        shrunk = jnp.exp(cumulative)
        q_share = sigmoid(q_pre)
        decayed_q = (q_pre * q_share * shrunk).astype(low)
        grown_k = (keys_in * grown).astype(low)
        values = v_ref[rows, :]
        dq_parts, dk_parts, dv_parts = [], [], []
        for head in range(2):
            lanes = slice(head * HEAD_DIM, (head + 1) * HEAD_DIM)
            q_h, k_h, v_h = decayed_q[:, lanes], grown_k[:, lanes], values[:, lanes]
            d_out = d_out_parts[head]
            scores = jnp.where(causal_t, mm_nt(k_h, q_h), 0.0).astype(low)
            d_scores = jnp.where(causal_t, mm_nt(v_h, d_out), 0.0).astype(low)
            dv_parts.append(mm(scores, d_out))
            dk_parts.append(mm(d_scores, q_h))
            dq_parts.append(mm_tn(d_scores, k_h))
        d_decayed = jnp.concatenate(dq_parts, axis=1)
        d_grown = jnp.concatenate(dk_parts, axis=1)
        d_value = jnp.concatenate(dv_parts, axis=1)
        d_cumulative = decayed_q.astype(wide) * d_decayed - grown_k.astype(wide) * d_grown
        d_log = split_sum(upper_ones, d_cumulative)
        d_query = d_decayed * shrunk
        d_key = d_grown * grown
        d_q_pre = d_query * q_share * (1.0 + q_pre * (1.0 - q_share))
        d_f_pre = (1.0 - lower_bound) * (d_log / gate - d_key) * share * (1.0 - share)
        dpre_ref[rows, :PAIR] = d_q_pre.astype(low)
        dpre_ref[rows, PAIR : 2 * PAIR] = d_f_pre.astype(low)
        dpre_ref[rows, 2 * PAIR :] = d_value.astype(low)

    columns = pl.ds(first * 3 * PAIR, 3 * PAIR)
    leaving = pltpu.make_async_copy(dpre_ref, dpre_hbm.at[:, columns], semaphores.at[1])
    leaving.start()
    fetch.wait()
    gain_column = g_ref[...].T[:, 0:1]
    grad = (mm(nt_s[...], dpre_ref[...]) * gain_column).astype(low)
    grad_ref[...] = grad.reshape(grad_ref.shape)
    leaving.wait()


def mixer_backward(half, n1t, gains8, kept, d_mixed, slot, shard, pairs=(0, 1), before=()):
    width, count = n1t.shape
    per_half = width // PAIR // 2
    first = pairs[0]
    by_pair = pl.BlockSpec((count, PAIR), lambda j, _: (0, first + j))
    from_whole = pl.BlockSpec((count, PAIR), lambda j, half: (0, half[0] * per_half + first + j))
    struct = jax.ShapeDtypeStruct
    return pl.pallas_call(
        functools.partial(mixer_backward_kernel, slot, per_half, first),
        grid_spec=pltpu.PrefetchScalarGridSpec(
            num_scalar_prefetch=1,
            grid=(len(pairs),),
            in_specs=[pl.BlockSpec(memory_space=pl.ANY), whole(gains8.shape)]
            + [by_pair] * 4
            + [from_whole]
            + [pl.BlockSpec(memory_space=pl.ANY)] * len(before),
            out_specs=[
                pl.BlockSpec(
                    (width // shard, 1, shard, 3 * PAIR), lambda j, _: (0, first + j, 0, 0)
                ),
                pl.BlockSpec(memory_space=pl.ANY),
            ],
            scratch_shapes=[
                pltpu.VMEM((width, count), low),
                pltpu.VMEM((count, 3 * PAIR), low),
                pltpu.SemaphoreType.DMA((2,)),
            ],
        ),
        out_shape=[
            struct((width // shard, per_half, shard, 3 * PAIR), low),
            struct((count, per_half * 3 * PAIR), low),
        ],
        input_output_aliases={8 + k: k for k in range(len(before))},
        compiler_params=pltpu.CompilerParams(vmem_limit_bytes=VMEM_BYTES),
        cost_estimate=pl.CostEstimate(
            flops=len(pairs) * (count * width * 6 * PAIR + 20 * count * slot * PAIR),
            bytes_accessed=len(pairs) * (count * width * 5 + width * PAIR * 6),
            transcendentals=len(pairs) * count * PAIR * 6,
        ),
        name="mixer_backward",
    )(half, n1t, gains8, *kept, d_mixed, *before)


def input_gradient_rows_kernel(
    x_ref, g_ref, dm_ref, do_ref, wm_ref, wo_ref, dx1_ref, dx_ref
):
    d_h1 = mm_nt(dm_ref[...], wm_ref[...]) + mm_nt(do_ref[...], wo_ref[...])
    normed, scale = first_norm(x_ref, None)
    scaled = d_h1 * g_ref[0:1, :]
    dx_ref[...] = dx1_ref[...] + scale * (
        scaled - normed * jnp.mean(scaled * normed, axis=-1, keepdims=True)
    )


def input_gradient(rows, gains8, d_pre, weights, d_x1):
    count, width = rows.shape
    block = count // 2
    columns = d_pre[0].shape[1]
    by_rows = lambda columns: pl.BlockSpec((block, columns), lambda j: (j, 0))
    weight_spec = pl.BlockSpec((width, columns), lambda j: (0, 0), pipeline_mode=pl.Buffered(1))
    return pl.pallas_call(
        input_gradient_rows_kernel,
        grid=(count // block,),
        in_specs=[by_rows(width), whole(gains8.shape)]
        + [by_rows(columns)] * 2
        + [weight_spec] * 2
        + [by_rows(width)],
        out_specs=by_rows(width),
        out_shape=jax.ShapeDtypeStruct((count, width), wide),
        compiler_params=pltpu.CompilerParams(vmem_limit_bytes=VMEM_BYTES),
        cost_estimate=pl.CostEstimate(
            flops=6 * count * width * width,
            bytes_accessed=count * width * 16 + width * width * 6,
            transcendentals=0,
        ),
        name="input_gradient",
    )(rows, gains8, *d_pre, *weights, d_x1)


def update(weight, momentum, average, gradient, step_rate):
    new_momentum = momentum_decay * momentum + gradient
    direction = gradient + momentum_decay * new_momentum + weight_decay * weight
    new_weight = weight - step_rate * direction
    new_average = average_decay * average + (1.0 - average_decay) * new_weight
    return (new_momentum, new_average, new_weight)


def update_kernel(pick, step_rate, sum_count, core_ref, w_ref, m_ref, a_ref, *refs):
    sums, outs, dots_ref = refs[:sum_count], refs[-4:-1], refs[-1]
    weight = w_ref[...]
    gradient = pick(core_ref[0], *[s[...] for s in sums]).astype(wide).reshape(weight.shape)
    results = update(weight, m_ref[...], a_ref[...], gradient, step_rate)
    for out, result in zip(outs, results):
        out[...] = result
    product = weight.astype(low).astype(wide) * gradient
    total = product[..., :HEAD_DIM]
    for start in range(HEAD_DIM, product.shape[-1], HEAD_DIM):
        total = total + product[..., start : start + HEAD_DIM]
    dots_ref[...] = total.reshape(dots_ref.shape)


def update_call(
    core, state, sums, grid, state_spec, sum_specs, pick, step_rate, name, before=()
):
    struct = jax.ShapeDtypeStruct(state[0].shape, wide)
    size = math.prod(state[0].shape)
    rows = state_spec.block_shape[-2]
    steps = math.prod(grid)
    tail = grid[1:]

    def dots_index(*indices):
        place = indices[0]
        for length, index in zip(tail, indices[1:]):
            place = place * length + index
        return (place, 0, 0)

    return pl.pallas_call(
        functools.partial(update_kernel, pick, step_rate, len(sums)),
        grid_spec=pltpu.PrefetchScalarGridSpec(
            num_scalar_prefetch=1,
            grid=grid,
            in_specs=[state_spec] * 3
            + sum_specs
            + [pl.BlockSpec(memory_space=pl.ANY)] * len(before),
            out_specs=[state_spec] * 3 + [pl.BlockSpec((1, rows, HEAD_DIM), dots_index)],
        ),
        out_shape=[struct] * 3 + [jax.ShapeDtypeStruct((steps, rows, HEAD_DIM), wide)],
        input_output_aliases={4 + len(sums) + k: k for k in range(len(before))},
        compiler_params=pltpu.CompilerParams(vmem_limit_bytes=VMEM_BYTES),
        cost_estimate=pl.CostEstimate(flops=12 * size, bytes_accessed=26 * size, transcendentals=0),
        name=name,
    )(core, *state, *sums, *before)


def update_attention_kernel(
    pick, step_rate, gain_step, core_ref, w_ref, m_ref, a_ref, qfv_ref, out_ref, *refs
):
    if gain_step is None:
        update_kernel(pick, step_rate, 2, core_ref, w_ref, m_ref, a_ref, qfv_ref, out_ref, *refs)
        return
    *held, dots_s = refs
    own_dots, up_dots, gate_dots, g_ref, gm_ref, ga_ref = held[:6]
    outs, gain_outs = held[-6:-3], held[-3:]
    kind = pl.program_id(0)
    dots = dots_s.at[pl.ds(2 * kind, 2)]
    update_kernel(
        pick, step_rate, 2, core_ref, w_ref, m_ref, a_ref, qfv_ref, out_ref, *outs, dots
    )

    @pl.when(kind == pl.num_programs(0) - 1)
    def _():
        shard = dots_s.shape[1]
        sums = [own_dots[k] + dots_s[k] for k in range(4)]
        two = (up_dots[...] + gate_dots[...]).reshape(shard, HEAD_DIM)
        columns = [
            jnp.sum(total, axis=1, keepdims=True) for total in (sums[0] + sums[1] + sums[2], sums[3], two)
        ]
        lanes = lax.broadcasted_iota(jnp.int32, (shard, HEAD_DIM), 1)
        table = jnp.where(lanes == 1, columns[1], columns[2])
        table = jnp.where(lanes == 0, columns[0], table)
        gain = g_ref[...]
        gradient = table.T[:3, :] / gain.astype(low).astype(wide)
        results = update(gain, gm_ref[...], ga_ref[...], gradient, gain_step)
        for out, result in zip(gain_outs, results):
            out[...] = result


def update_attention(half_ref, state, qfv, out, step_rate, gains=None):
    _, shard, width = state[0].shape
    down_rows = out.shape[0] - shard

    def pick(core_index, proj, last):
        chosen = []
        for kind in range(3):
            parts = [proj[pair * shard :, kind * PAIR :][:shard, :PAIR] for pair in range(2)]
            chosen.append(jnp.concatenate(parts, axis=1).astype(wide))
        chosen.append(last[down_rows:].astype(wide))
        early = pl.program_id(0) == 0
        both = [jnp.where(early, chosen[k], chosen[k + 2]) for k in range(2)]
        return jnp.concatenate(both, axis=0)

    struct = jax.ShapeDtypeStruct
    state_spec = pl.BlockSpec((2, shard, width // 2), lambda kind, half: (kind, 0, half[0]))
    in_specs = [state_spec] * 3 + [whole(qfv.shape), whole(out.shape)]
    out_specs = [state_spec] * 3
    out_shape = [struct(state[0].shape, wide)] * 3
    operands = [half_ref, *state, qfv, out]
    aliases, scratch, gain_step = {}, [], None
    if gains is None:
        out_specs += [pl.BlockSpec((2, shard, HEAD_DIM), lambda kind, half: (kind, 0, 0))]
        out_shape += [struct((4, shard, HEAD_DIM), wide)]
    else:
        before, dots, gain_state, gain_step = gains
        in_specs += [whole(part.shape) for part in (*dots, *gain_state)]
        operands += [*dots, *gain_state]
        aliases = {len(operands) + k: k for k in range(3)}
        in_specs += [pl.BlockSpec(memory_space=pl.ANY)] * 3
        operands += list(before)
        out_specs += [whole(gain_state[0].shape)] * 3
        out_shape += [struct(gain_state[0].shape, wide)] * 3
        scratch = [pltpu.VMEM((4, shard, HEAD_DIM), wide)]
    size = math.prod(state[0].shape) // 2
    return pl.pallas_call(
        functools.partial(update_attention_kernel, pick, step_rate, gain_step),
        grid_spec=pltpu.PrefetchScalarGridSpec(
            num_scalar_prefetch=1,
            grid=(2,),
            in_specs=in_specs,
            out_specs=out_specs,
            scratch_shapes=scratch,
        ),
        out_shape=out_shape,
        input_output_aliases=aliases,
        compiler_params=pltpu.CompilerParams(vmem_limit_bytes=VMEM_BYTES),
        cost_estimate=pl.CostEstimate(flops=12 * size, bytes_accessed=26 * size, transcendentals=0),
        name="update_attention",
    )(*operands)


def update_ffn_in(kind_ref, state, totals, step_rate, before):
    _, shard, hidden = state[0].shape
    block = shard // 2

    def pick(_, even, odd):
        blocks = []
        for start in range(0, hidden // 2, HEAD_DIM):
            blocks += [even[:, start : start + HEAD_DIM], odd[:, start : start + HEAD_DIM]]
        return jnp.concatenate(blocks, axis=1)

    return update_call(
        kind_ref,
        state,
        totals,
        (2,),
        pl.BlockSpec((1, block, hidden), lambda j, kind: (kind[0], j, 0)),
        [pl.BlockSpec((block, hidden // 2), lambda j, _: (j, 0))] * 2,
        pick,
        step_rate,
        "update_ffn_in",
        before,
    )


def update_ffn_out(core, state, sums, step_rate):
    shard, width = state[0].shape

    def pick(core_index, mine, other):
        own = pl.program_id(0) == core_index
        return jnp.where(own, mine[:shard].astype(wide), other[:shard].astype(wide))

    return update_call(
        core,
        state,
        sums,
        (2,),
        pl.BlockSpec((shard, width // 2), lambda j, _: (0, j)),
        [whole(total.shape) for total in sums],
        pick,
        step_rate,
        "update_ffn_out",
    )


def pack_kernel(core_ref, w_ref, out_ref):
    half = w_ref.shape[2]
    for pair in range(half // PAIR):
        for kind in range(3):
            start = (pair * 3 + kind) * PAIR
            piece = w_ref[kind, :, pair * PAIR : (pair + 1) * PAIR]
            out_ref[:, start : start + PAIR] = piece.astype(low)
    out_ref[:, 3 * half : 4 * half] = w_ref[3].astype(low)


def pack_attention(core, weights):
    _, shard, width = weights.shape
    half = width // 2
    return pl.pallas_call(
        pack_kernel,
        grid_spec=pltpu.PrefetchScalarGridSpec(
            num_scalar_prefetch=1,
            grid=(1,),
            in_specs=[pl.BlockSpec((4, shard, half), lambda j, core: (0, 0, core[0]))],
            out_specs=whole((shard, 4 * half)),
        ),
        out_shape=jax.ShapeDtypeStruct((shard, 4 * half), low),
        name="pack_attention",
    )(core, weights)


RING = 8


def ring_place(index):
    return jnp.where(index % 2 == 0, index // 2, RING - 1 - index // 2)


def ring_member(place):
    place = place % RING
    return jnp.where(place < RING // 2, 2 * place, 2 * RING - 1 - 2 * place)


CYCLE = (0, 2, 4, 6, 7, 5, 3, 1)


def ring_next(tensor):
    replicas = lax.axis_size("dp")
    pairs = []
    for place_of, member in enumerate(CYCLE):
        for replica in range(replicas):
            target = CYCLE[(place_of + (1 if replica % 2 == 0 else -1)) % RING]
            pairs.append((member * replicas + replica, target * replicas + replica))
    return lax.ppermute(tensor, ("fsdp", "dp"), pairs)


def ring_shift(tensor, way):
    pairs = [(member, CYCLE[(at + way) % RING]) for at, member in enumerate(CYCLE)]
    return lax.ppermute(tensor, "fsdp", pairs)


def core_swap(tensor):
    return lax.ppermute(tensor, "dp", [(d, d ^ 1) for d in range(lax.axis_size("dp"))])


def column_swap(tensor):
    return lax.ppermute(tensor, "dp", [(d, d ^ 2) for d in range(lax.axis_size("dp"))])


def pack_all_kernel(
    core_ref, column_ref, w_ref, up_ref, other_ref, down_ref, g_ref, out_ref, across_ref
):
    across_ref[...] = other_ref[0].astype(low)
    shard = w_ref.shape[1]
    half = w_ref.shape[2]
    for pair in range(half // PAIR):
        for kind in range(3):
            start = (pair * 3 + kind) * PAIR
            piece = w_ref[kind, :, pair * PAIR : (pair + 1) * PAIR]
            out_ref[:, start : start + PAIR] = piece.astype(low)
    out_ref[:, 3 * half : 4 * half] = w_ref[3].astype(low)
    start = 4 * half
    out_ref[:, start : start + up_ref.shape[2]] = up_ref[0].astype(low)
    start += up_ref.shape[2]
    for first, count in down_parts(down_ref.shape[0], shard):
        out_ref[:count, start : start + half] = down_ref[first : first + count, :].astype(low)
        if count < shard:
            out_ref[count:, start : start + half] = jnp.zeros((shard - count, half), low)
            rows = lax.broadcasted_iota(jnp.int32, (GAIN_ROWS, g_ref.shape[1]), 0)
            gains = jnp.where(rows == 1, g_ref[1:2, :], g_ref[2:3, :])
            gains = jnp.where(rows == 0, g_ref[0:1, :], gains)
            gains = jnp.where(rows < 3, gains, 0.0).astype(low)
            out_ref[count : count + GAIN_ROWS, start : start + g_ref.shape[1]] = gains
        start += half


def down_parts(down_rows, shard):
    return [(start, min(shard, down_rows - start)) for start in range(0, down_rows, shard)]


def pack_all(core, column, weights, up, down, gains):
    _, shard, width = weights.shape
    half = width // 2
    parts = len(down_parts(down.shape[0], shard))
    columns = 4 * half + up.shape[2] // 2 + parts * half
    return pl.pallas_call(
        pack_all_kernel,
        grid_spec=pltpu.PrefetchScalarGridSpec(
            num_scalar_prefetch=2,
            grid=(1,),
            in_specs=[
                pl.BlockSpec((4, shard, half), lambda j, core, column: (0, 0, core[0])),
                pl.BlockSpec(
                    (1, shard, up.shape[2] // 2), lambda j, core, column: (core[0], 0, column[0])
                ),
                pl.BlockSpec(
                    (1, shard, up.shape[2] // 2),
                    lambda j, core, column: (core[0], 0, 1 - column[0]),
                ),
                pl.BlockSpec((down.shape[0], half), lambda j, core, column: (0, core[0])),
                whole(gains.shape),
            ],
            out_specs=[whole((shard, columns)), whole((shard, up.shape[2] // 2))],
        ),
        out_shape=[
            jax.ShapeDtypeStruct((shard, columns), low),
            jax.ShapeDtypeStruct((shard, up.shape[2] // 2), low),
        ],
        compiler_params=pltpu.CompilerParams(vmem_limit_bytes=VMEM_BYTES),
        name="pack_all",
    )(core, column, weights, up, up, down, gains)


def place_kernel(which, kept, shapes, origin_ref, column_ref, *refs):
    pieces, outs, semaphores = refs[: len(which)], refs[-1 - len(kept) : -1], refs[-1]
    targets = dict(zip(kept, outs))
    shard, first, up_columns, down_rows, half = shapes
    copies = []

    def copy(source, target):
        copies.append(pltpu.make_async_copy(source, target, semaphores.at[len(copies)]))

    for piece, (origin, across) in zip(pieces, which):
        owner = origin_ref[origin]
        rows = pl.ds(pl.multiple_of(owner * shard, 16), shard)
        if across:
            copy(piece, targets[1].at[rows, lanes_of(1 - column_ref[0], up_columns)])
            continue
        copy(piece.at[:, pl.ds(0, first)], targets[0].at[rows, :])
        own = targets[1].at[rows, lanes_of(column_ref[0], up_columns)]
        copy(piece.at[:, pl.ds(first, up_columns)], own)
        lane = first + up_columns
        for start, count in down_parts(down_rows, shard):
            target = pl.ds(pl.multiple_of(owner * down_rows + start, 16), count)
            copy(piece.at[pl.ds(0, count), pl.ds(lane, half)], targets[2].at[target, :])
            if count < shard:
                source = piece.at[pl.ds(count, GAIN_ROWS), pl.ds(lane, shard)]
                copy(source, targets[3].at[:, lanes_of(owner, shard)])
            lane += half
    for one in copies:
        one.start()
    for one in copies:
        one.wait()


def place(origins, column, which, pieces, arrays, kept, shapes):
    anywhere = pl.BlockSpec(memory_space=pl.ANY)
    shard, first, up_columns, down_rows, half = shapes
    kinds = [(RING * shard, first), (RING * shard, 2 * up_columns), (RING * down_rows, half)]
    kinds.append((GAIN_ROWS, RING * shard))
    held = [] if arrays is None else list(arrays)
    size = sum(math.prod(piece.shape) for piece in pieces)
    before = 2 + len(pieces)
    return pl.pallas_call(
        functools.partial(place_kernel, which, kept, shapes),
        grid_spec=pltpu.PrefetchScalarGridSpec(
            num_scalar_prefetch=2,
            grid=(1,),
            in_specs=[whole(piece.shape) for piece in pieces] + [anywhere] * len(held),
            out_specs=[anywhere] * len(kept),
            scratch_shapes=[pltpu.SemaphoreType.DMA((8 * len(pieces),))],
        ),
        out_shape=[jax.ShapeDtypeStruct(kinds[k], pieces[0].dtype) for k in kept],
        input_output_aliases={before + k: k for k in range(len(held))},
        compiler_params=pltpu.CompilerParams(vmem_limit_bytes=VMEM_BYTES),
        cost_estimate=pl.CostEstimate(flops=0, bytes_accessed=8 * size, transcendentals=0),
        name="place",
    )(origins, column, *pieces, *held)


def after(tensor, *others):
    return lax.optimization_barrier((tensor, *others))[0]


def core_way():
    return 1 - 2 * (lax.axis_index("dp") % 2)


def ring_origins():
    steps = jnp.array((0, -1, -2, -3, -4, 1, 2, 3), jnp.int32)
    return ring_member(ring_place(lax.axis_index("fsdp")) + steps + RING).astype(jnp.int32)


class RingSumOverColumns:
    def __init__(self, mine, arrived):
        self.arrays = (mine, arrived)
        place = ring_place(lax.axis_index("fsdp"))
        self.rows = mine.shape[1] // RING
        self.starts = [
            ring_member(place - core_way() * (s + 1) + 2 * RING) * self.rows for s in range(RING)
        ]
        self.sent, self.came, self.totals = [], [], []

    def part(self, side, step):
        shape = (1, self.rows, self.arrays[0].shape[2])
        parts = [
            lax.dynamic_slice(array, (side, self.starts[step], 0), shape)[0]
            for array in self.arrays
        ]
        return parts[0].astype(wide) + parts[1].astype(wide)

    def cross(self):
        self.sent.append(self.part(1, len(self.sent)).astype(low))
        self.came.append(column_swap(self.sent[-1]))

    def term(self):
        step = len(self.totals)
        return self.part(0, step) + self.came[step].astype(wide)

    def begin(self, *others):
        self.came[0] = after(self.came[0], *others) if others else self.came[0]
        self.totals.append(self.term().astype(low))

    def step(self, arriving=()):
        total, ahead = self.totals[-1], self.came[len(self.totals)]
        moved = ring_next(after(total, ahead) if len(self.totals) > 1 else total)
        moved = after(moved, *arriving) if arriving else moved
        self.totals.append((moved.astype(wide) + self.term()).astype(low))

    def last(self):
        return self.totals[-1]


class RingSum:
    def __init__(self, mine, arrived):
        self.mine, self.arrived = mine, arrived
        place = ring_place(lax.axis_index("fsdp"))
        self.owners = [ring_member(place - core_way() * (s + 1) + 2 * RING) for s in range(RING)]
        self.totals = []

    def term(self):
        parts = []
        for own, arrived in zip(self.mine, self.arrived):
            rows = own.shape[0] // RING
            start = self.owners[len(self.totals)] * rows
            part = lax.dynamic_slice_in_dim(own, start, rows, 0).astype(wide)
            parts.append(part + lax.dynamic_slice_in_dim(arrived, start, rows, 0).astype(wide))
        return parts[0] if len(parts) == 1 else jnp.concatenate(parts, axis=0)

    def begin(self, *others):
        if others:
            self.mine = [after(self.mine[0], *others), *self.mine[1:]]
        self.totals.append(self.term().astype(low))

    def step(self, *before, arriving=()):
        total = self.totals[-1]
        moved = ring_next(after(total, *before) if before else total)
        moved = after(moved, *arriving) if arriving else moved
        self.totals.append((moved.astype(wide) + self.term().astype(wide)).astype(low))

    def last(self):
        return self.totals[-1]


def gather_rows(shard):
    mine = lax.all_gather(shard, "fsdp", axis=0, tiled=True)
    return mine, core_swap(mine)


def core_sum(mine, other):
    return (mine.astype(wide) + core_swap(other).astype(wide)).astype(low)


def scatter_rows(both):
    return lax.psum_scatter(both, "fsdp", scatter_dimension=0, tiled=True)


def over_columns(total):
    total = (total.astype(wide) + column_swap(total).astype(wide)).astype(low)
    return total, core_swap(total)


def on_device(
    inputs,
    cotangent,
    lengths,
    attention_weights,
    attention_momentum,
    attention_average,
    ffn_inputs,
    ffn_inputs_momentum,
    ffn_inputs_average,
    ffn_output,
    ffn_output_momentum,
    ffn_output_average,
    gains,
    gains_momentum,
    gains_average,
):
    micro_count, slot, width = inputs.shape
    hidden = ffn_inputs.shape[2]
    shard, down_rows = ffn_inputs.shape[1], ffn_output.shape[0]
    fsdp_size = lax.axis_size("fsdp")
    replicas = lax.axis_size("dp")
    ringed = fsdp_size == RING
    core = lax.axis_index("dp") % 2
    column = lax.axis_index("dp") // 2
    count = micro_count * slot
    half = width // 2
    core_ref = core.astype(jnp.int32).reshape(1)
    other_ref = 1 - core_ref
    column_ref = column.astype(jnp.int32).reshape(1)
    is_first = core == 0

    rows = inputs.reshape(count, width)
    n1t = norm_rows(rows)
    positions = jnp.arange(slot, dtype=jnp.int32)
    valid = (positions[None, :] < lengths).astype(wide).reshape(count, 1)
    errors = (cotangent.reshape(count, width).astype(wide) * valid).astype(low)

    if ringed:
        origins = ring_origins()
        first = 4 * half
        shapes = (shard, first, hidden // 2, down_rows, half)
        packed, own_across = pack_all(
            core_ref, column_ref, attention_weights, ffn_inputs, ffn_output, gains
        )
        wholes, there, which_there = None, [own_across], [(0, True)]
        here, which = [packed], [(0, False)]
        for step in range(1, 6):
            if step <= 3:
                onward = [ring_shift(here[0], 1), ring_shift(here[-1], -1)]
            elif step == 4:
                onward = [ring_next(jnp.where(is_first, *here))]
            across = []
            if step > 1:
                across = [column_swap(piece[:, first : first + hidden // 2]) for piece in here]
            wholes = place(
                origins, column_ref, which + which_there, here + there, wholes, (0, 1, 2, 3), shapes
            )
            if step == 5:
                break
            extra = [errors, n1t] if step == 2 else []
            tied = list(lax.optimization_barrier((*onward, *across, *wholes, *extra)))
            here, rest = tied[: len(onward)], tied[len(onward) :]
            there, wholes = rest[: len(across)], rest[len(across) : len(across) + 4]
            which_there = [(origin, True) for origin, _ in which] if across else []
            which = [(origin, False) for origin in [step, step + 4][: len(onward)]]
        w_a, gain_rows = (wholes[0], core_swap(wholes[0])), wholes[3]
    else:
        w_a = gather_rows(pack_attention(core_ref, attention_weights))
        gain_rows = lax.all_gather(gains.astype(low), "fsdp", axis=1, tiled=True)
        gain_rows = jnp.pad(gain_rows, ((0, GAIN_ROWS - 3), (0, 0)))
        w_gu = gather_rows(
            lax.dynamic_index_in_dim(ffn_inputs, core, 0, keepdims=False).astype(low)
        )
        w_d = gather_rows(lax.dynamic_slice_in_dim(ffn_output, core * half, half, 1).astype(low))
    mixed_mine, *kept_mine, gains8 = mixer_forward(core_ref, rows, w_a[0], slot, gain_rows)
    if ringed:
        (across,) = lax.optimization_barrier((*across, mixed_mine, w_a[1]))[:1]
        (w_gu_mine,) = place(origins, column_ref, [(4, True)], [across], [wholes[1]], (1,), shapes)
        wholes = [wholes[0], w_gu_mine, wholes[2], wholes[3]]
        rows = after(rows, *wholes[1:3])
        w_gu, w_d = [(array, core_swap(array)) for array in wholes[1:3]]
    mixed_other, *rest = mixer_forward(
        other_ref, rows, w_a[1], slot, None, (gains8, mixed_mine, w_a[0])
    )
    kept_other, (x1, h2, h2t) = rest[:4], rest[4:]
    owners = (RING, down_rows + shard, down_rows)
    if not ringed:
        owners = (1, hidden + width, hidden)
    places = jnp.concatenate([core_ref, column_ref])
    *grad_gu, gd_mine, gd_other, output, d_x1, d_mixed = ffn(
        places, h2, h2t, errors, w_gu, w_d, x1, (mixed_mine, mixed_other), w_a, lengths[:, 0], gains8, owners
    )

    gm, gu = grad_gu
    arrived_gu = core_swap(gu)
    mine_do, arrived_do = [gd_mine], [core_swap(gd_other)]
    by_owner = (fsdp_size * 2 * shard, 3 * PAIR)
    d_pre = []
    for call in range(4):
        from_half, kept = (other_ref, kept_other) if call < 2 else (core_ref, kept_mine)
        if ringed and call == 1:
            sum_gu = RingSumOverColumns(after(gm, d_pre[0]), arrived_gu)
            sum_gu.cross()
            sum_gu.cross()
            n1t = after(n1t, *sum_gu.sent)
        elif ringed and call > 1:
            sum_gu.cross()
            ahead = [sum_gu.came[2]] if call == 3 else []
            n1t = after(n1t, sum_gu.last(), sum_do.last(), sum_gu.sent[-1], *ahead)
        grads = mixer_backward(
            from_half,
            n1t,
            gains8,
            kept,
            d_mixed,
            slot,
            shard,
            (call % 2,),
            grads if call % 2 else (),
        )
        d_pre.append(grads[1])
        if call == 1:
            grad_other = grads[0]
            if ringed:
                sum_do = RingSum(mine_do, arrived_do)
                sum_do.begin(d_pre[-1])
                sum_gu.begin(d_pre[-1])
                grad_other = after(grad_other, sum_gu.last(), sum_do.last())
            arrived_qfv = [core_swap(grad_other.reshape(by_owner))]
        elif ringed and call > 1:
            gate = d_pre[-1]
            if call == 3:
                sum_qfv = RingSum([grads[0].reshape(by_owner)], arrived_qfv)
                sum_qfv.begin()
                gate = sum_qfv.last()
            sum_do.step(arriving=(gate,))
            sum_gu.step(arriving=(gate,))
    mine_qfv = [grads[0].reshape(by_owner)]

    def finish_input(*others):
        late = after(d_pre[3], *others) if others else d_pre[3]
        return input_gradient(rows, gains8, (late, d_pre[1]), w_a, d_x1)

    if ringed:
        input_grad = None
        for step in range(1, RING - 1):
            if len(sum_gu.came) < RING:
                sum_gu.cross()
            if len(sum_gu.totals) < RING:
                first = [sum_gu.last(), sum_qfv.last()]
                sum_do.step(*{1: first, 4: [input_grad]}.get(step, []))
                sum_gu.step()
            sum_qfv.step()
            if step == 2:
                input_grad = finish_input(sum_qfv.last(), sum_gu.came[5])
        total_gu, total_do = sum_gu.last(), sum_do.last()
    else:
        both = (gm.astype(wide) + arrived_gu.astype(wide)).astype(low)
        here = (both[0].astype(wide) + column_swap(both[1]).astype(wide)).astype(low)
        total_gu = scatter_rows(here)
        both = (gd_mine.astype(wide) + arrived_do[0].astype(wide)).astype(low)
        total_do = jnp.concatenate(
            [scatter_rows(both[:hidden]), scatter_rows(both[hidden:])], axis=0
        )
        total_qfv = scatter_rows(
            (mine_qfv[0].astype(wide) + arrived_qfv[0].astype(wide)).astype(low)
        )
        input_grad = finish_input()
    scale_rows = 1.0 / math.sqrt(count * fsdp_size * replicas)
    matrix_step = matrix_rate * scale_rows
    attention_state = (attention_weights, attention_momentum, attention_average)
    ffn_in_state = (ffn_inputs, ffn_inputs_momentum, ffn_inputs_average)
    ffn_out_state = (ffn_output, ffn_output_momentum, ffn_output_average)
    sum_do = over_columns(total_do)
    there = column_swap(total_gu)
    even = jnp.where(column == 0, total_gu, there)
    odd = jnp.where(column == 0, there, total_gu)
    sum_gu = (even, odd), (core_swap(even), core_swap(odd))
    *new_out, _ = update_ffn_out(core_ref, ffn_out_state, sum_do, matrix_step)
    *new_in, dots_up = update_ffn_in(core_ref, ffn_in_state, sum_gu[0], matrix_step, ())
    *new_in, dots_gate = update_ffn_in(other_ref, ffn_in_state, sum_gu[1], matrix_step, new_in)
    if ringed:
        sum_qfv.step(arriving=(new_out[0],))
        total_qfv = sum_qfv.last()
    there = after(column_swap(total_qfv), new_in[0])
    sum_qfv = (total_qfv.astype(wide) + there.astype(wide)).astype(low)
    *own, dots_own = update_attention(
        core_ref, attention_state, sum_qfv, sum_do[0], matrix_step
    )
    theirs = after(core_swap(sum_qfv), own[0])
    gain_state = (gains, gains_momentum, gains_average)
    *new_attention, gains_m, gains_a, gains_w = update_attention(
        other_ref,
        attention_state,
        theirs,
        sum_do[1],
        matrix_step,
        (own, (dots_own, dots_up, dots_gate), gain_state, gain_rate * scale_rows),
    )
    return (
        output.reshape(micro_count, slot, width),
        input_grad.reshape(micro_count, slot, width),
        *new_attention,
        *new_in,
        *new_out,
        gains_m,
        gains_a,
        gains_w,
    )


def solution(mesh):
    rows_split = P(None, ("fsdp", "dp"), None)
    middle_split = P(None, "fsdp", None)
    first_split = P("fsdp", None)
    gains_split = P(None, "fsdp")
    in_specs = (
        (rows_split, rows_split, P(None, ("fsdp", "dp")))
        + (middle_split,) * 6
        + (first_split,) * 3
        + (gains_split,) * 3
    )
    out_specs = (
        (rows_split, rows_split)
        + (middle_split,) * 6
        + (first_split,) * 3
        + (gains_split,) * 3
    )
    return jax.shard_map(
        on_device, mesh=mesh, in_specs=in_specs, out_specs=out_specs, check_vma=False
    )
```
